32 devices in a mesh: section: 2 (over core), dp: 4 (over z), tensor: 4 (over y, x).
Axes of the slice: x: 2, y: 2, z: 4, core: 2. Of those that a mesh axis runs over, the one named last changes fastest.
Arguments:
- inputs: bfloat16 [2, 1152, 2048], P(None, 'dp'), may hold values from -6 to 6
- cotangent: bfloat16 [2, 1152, 2048], P(None, 'dp'), may hold values from -6 to 6
- seg_ids: int32 [2, 1152], replicated, may hold values from 0 to 8, as said below
- parents: int32 [2, 9], replicated, may hold values from 0 to 4, as said below
- order: int32 [2], replicated, may hold values from 0 to 1, each once
- attn_gain: bfloat16 [2, 2048], P('section', 'dp'), may hold values from 0.5 to 1.5
- w_query: bfloat16 [2, 2048, 2048], P('section', 'dp', 'tensor'), may hold values from -0.125 to 0.125
- w_key: bfloat16 [2, 2048, 1024], P('section', 'dp', 'tensor'), may hold values from -0.125 to 0.125
- w_value: bfloat16 [2, 2048, 1024], P('section', 'dp', 'tensor'), may hold values from -0.125 to 0.125
- w_out: bfloat16 [2, 2048, 2048], P('section', 'tensor', 'dp'), may hold values from -1.5 to 1.5
- q_gain: bfloat16 [2, 128], P('section'), may hold values from 0.25 to 1.75
- k_gain: bfloat16 [2, 128], P('section'), may hold values from 0.25 to 1.75
- mlp_gain: bfloat16 [2, 2048], P('section', 'dp'), may hold values from 0.5 to 1.5
- w_gate: bfloat16 [2, 2048, 6144], P('section', 'dp', 'tensor'), may hold values from -0.125 to 0.125
- w_up: bfloat16 [2, 2048, 6144], P('section', 'dp', 'tensor'), may hold values from -0.125 to 0.125
- w_down: bfloat16 [2, 6144, 2048], P('section', 'tensor', 'dp'), may hold values from -0.078125 to 0.078125
Outputs:
- layer_out: bfloat16 [2, 2, 1152, 2048], P('section', None, 'dp')
- input_grad: bfloat16 [2, 2, 1152, 2048], P('section', None, 'dp')
- grad_attn_gain: float32 [2, 2048], P('section', 'dp')
- grad_w_query: float32 [2, 2048, 2048], P('section', 'dp', 'tensor')
- grad_w_key: float32 [2, 2048, 1024], P('section', 'dp', 'tensor')
- grad_w_value: float32 [2, 2048, 1024], P('section', 'dp', 'tensor')
- grad_w_out: float32 [2, 2048, 2048], P('section', 'tensor', 'dp')
- grad_q_gain: float32 [2, 128], P('section')
- grad_k_gain: float32 [2, 128], P('section')
- grad_mlp_gain: float32 [2, 2048], P('section', 'dp')
- grad_w_gate: float32 [2, 2048, 6144], P('section', 'dp', 'tensor')
- grad_w_up: float32 [2, 2048, 6144], P('section', 'dp', 'tensor')
- grad_w_down: float32 [2, 6144, 2048], P('section', 'tensor', 'dp')
The draws below stay inside these ranges and needn't reach their ends.
Inputs may be any that keep to these rules, and one draw needn't show every extreme that they name: `seg_ids`: in each tree the first 512 places hold segment 0, the trunk; the others hold the branch segments 1 to 4 of 96 tokens each and the leaf segments 5 to 8 of 64 tokens each, each segment contiguous, in any order. `parents`: entry s is the parent segment of segment s: 0 for the trunk and every branch, a branch for every leaf.
All inputs are finite; a program needn't handle non-finite values.
Results may differ from the reference program's by a relative error of at most 0.034.
Values may be sent and summed in bfloat16 or wider, within the bound.
A program may use at most 320 MiB of HBM per device.

```python
import jax
import jax.numpy as jnp
from jax import lax

D = 2048
QH = 16
KH = 8
HD = 128
FF = 6144
TRUNK = 512
BRANCH = 96
LEAF = 64
NB = 4
NL = 4
MICRO = 2
TREE = 1152
SEGS = 9
LAYERS = 2


def draw_seg_ids(key, part):
    key = jax.random.fold_in(key, 11)
    tree_keys = jax.random.split(key, MICRO)
    layouts = jax.vmap(lambda tree_key: jax.random.permutation(tree_key, NB + NL))(tree_keys) + 1
    lengths = jnp.where(layouts <= NB, BRANCH, LEAF)
    segment_ends = TRUNK + jnp.cumsum(lengths, axis=1)
    places = jnp.arange(TREE)
    counted = jnp.sum((places[None, None, :] >= segment_ends[:, :, None]).astype(jnp.int32), axis=1)
    picked = jnp.take_along_axis(layouts, jnp.clip(counted, 0, NB + NL - 1), axis=1)
    return jnp.where(places[None, :] < TRUNK, 0, picked).astype(jnp.int32)


def draw_parents(key, part):
    key = jax.random.fold_in(key, 12)
    leaf_parent = jax.random.randint(key, (MICRO, NL), 1, NB + 1)
    upper_part = jnp.zeros((MICRO, 1 + NB), jnp.int32)
    return jnp.concatenate([upper_part, leaf_parent.astype(jnp.int32)], axis=1)


def shard_levels(rng, shape, pieces, smallest, largest):
    def one(position, parts):
        draws = jax.random.uniform(jax.random.fold_in(jax.random.fold_in(rng, 6), position), (parts,), jnp.float32, smallest / len(pieces), largest / len(pieces))
        return jnp.repeat(jnp.exp(draws), shape[position] // parts).reshape((-1,) + (1,) * (len(shape) - position - 1))

    gain = one(*pieces[0])
    for cut in pieces[1:]:
        gain = gain * one(*cut)
    return gain


def bell_draw(own_key, shape, spread, limit, shards=(), held_as=jnp.bfloat16):
    entries = spread * jax.random.normal(own_key, shape, jnp.float32)
    if shards:
        entries = entries * shard_levels(own_key, shape, shards, -0.22, 0.18)
    return jnp.clip(entries, -limit, limit).astype(held_as)


def setup_inputs(seed: int = 0) -> dict:
    key_list = jax.random.split(jax.random.key(seed), 17)
    return {
        "inputs": bell_draw(key_list[0], (MICRO, TREE, D), 1.0, 6.0, ((1, 4),)),
        "cotangent": bell_draw(key_list[1], (MICRO, TREE, D), 1.0, 6.0, ((1, 4),)),
        "seg_ids": draw_seg_ids(jax.random.fold_in(key_list[16], 71), 0),
        "parents": draw_parents(jax.random.fold_in(key_list[16], 71), 0),
        "order": jax.random.permutation(key_list[4], MICRO).astype(jnp.int32),
        "attn_gain": jnp.clip(1.0 + 0.1 * jax.random.normal(key_list[5], (LAYERS, D), jnp.float32), 0.5, 1.5).astype(jnp.bfloat16),
        "w_query": bell_draw(key_list[6], (LAYERS, D, QH * HD), D ** -0.5, 0.125, ((0, 2), (1, 4), (2, 4))),
        "w_key": bell_draw(key_list[7], (LAYERS, D, KH * HD), D ** -0.5, 0.125, ((0, 2), (1, 4), (2, 4))),
        "w_value": bell_draw(key_list[8], (LAYERS, D, KH * HD), D ** -0.5, 0.125, ((0, 2), (1, 4), (2, 4))),
        "w_out": bell_draw(key_list[9], (LAYERS, QH * HD, D), (QH * HD // 128) ** -0.5, 1.5, ((0, 2), (1, 4), (2, 4))),
        "q_gain": jnp.clip(1.0 + 0.15 * jax.random.normal(key_list[10], (LAYERS, HD), jnp.float32), 0.25, 1.75).astype(jnp.bfloat16),
        "k_gain": jnp.clip(1.0 + 0.15 * jax.random.normal(key_list[11], (LAYERS, HD), jnp.float32), 0.25, 1.75).astype(jnp.bfloat16),
        "mlp_gain": jnp.clip(1.0 + 0.1 * jax.random.normal(key_list[12], (LAYERS, D), jnp.float32), 0.5, 1.5).astype(jnp.bfloat16),
        "w_gate": bell_draw(key_list[13], (LAYERS, D, FF), D ** -0.5, 0.125, ((0, 2), (1, 4), (2, 4))),
        "w_up": bell_draw(key_list[14], (LAYERS, D, FF), D ** -0.5, 0.125, ((0, 2), (1, 4), (2, 4))),
        "w_down": bell_draw(key_list[15], (LAYERS, FF, D), FF ** -0.5, 0.078125, ((0, 2), (1, 4), (2, 4))),
    }


EPSILON = 1e-06
THETA = 1000000.0
MASKED = -1e+30

@jax.custom_vjp
def low(v):
    return lax.optimization_barrier(v.astype(jnp.bfloat16)).astype(jnp.float32)

@jax.custom_vjp
def low_back(v):
    return v

def low_keep(v):
    return (low(v), None)

def low_pass(kept, grad):
    return (grad,)

def back_keep(v):
    return (v, None)

def back_low(kept, grad):
    return (low(grad),)
low.defvjp(low_keep, low_pass)
low_back.defvjp(back_keep, back_low)

def matmul(left, right):
    return jnp.dot(left, right, precision=lax.Precision.HIGHEST)

def rms_scale(values, weight_gain):
    mean_sq = lax.optimization_barrier(jnp.mean(values * values, axis=-1, keepdims=True))
    return values * lax.rsqrt(mean_sq + EPSILON) * weight_gain

def rotate(values, cos_table, sine_table):
    middle_at = values.shape[-1] // 2
    leading = values[..., :middle_at]
    trailing = values[..., middle_at:]
    return jnp.concatenate([leading * cos_table - trailing * sine_table, trailing * cos_table + leading * sine_table], axis=-1)

def rope_tables(positions, head_dim):
    half_steps = jnp.arange(head_dim // 2, dtype=jnp.float32)
    inverse = THETA ** (-2.0 * half_steps / head_dim)
    angles = positions.astype(jnp.float32)[:, None] * inverse[None, :]
    return (jnp.cos(angles)[:, None, :], jnp.sin(angles)[:, None, :])

def tree_layout(seg_row, parent_row):
    labels = jnp.arange(SEGS, dtype=jnp.int32)
    places = jnp.arange(TREE, dtype=jnp.int32)
    member = seg_row[None, :] == labels[:, None]
    starts = lax.optimization_barrier(jnp.min(jnp.where(member, places[None, :], TREE), axis=1))
    depth_base = jnp.where(labels == 0, 0, jnp.where(labels <= NB, TRUNK, TRUNK + BRANCH))
    shifts = (depth_base - starts).astype(jnp.int32)
    positions = places + lax.optimization_barrier(jnp.sum(jnp.where(member, shifts[:, None], 0), axis=0)).astype(jnp.int32)
    grandparent = parent_row[parent_row]
    ancestor = (labels[None, :] == labels[:, None]) | (labels[None, :] == parent_row[:, None]) | (labels[None, :] == grandparent[:, None])
    return (positions, ancestor)

def attend(queries, keys_rep, values_rep, seg_row, ancestor):
    block_rows = TREE // 4
    places = jnp.arange(TREE, dtype=jnp.int32)
    scale_factor = HD ** (-0.5)

    def attend_block(block_start):
        rows_q = lax.dynamic_slice_in_dim(queries, block_start, block_rows, 1)
        row_places = block_start + jnp.arange(block_rows, dtype=jnp.int32)
        row_segs = lax.dynamic_slice_in_dim(seg_row, block_start, block_rows, 0)
        raw_scores = jnp.einsum('hqd,hkd->hqk', rows_q, keys_rep, precision=lax.Precision.HIGHEST) * scale_factor
        raw_scores = low_back(raw_scores)
        reach_table = ancestor[row_segs][:, seg_row]
        same_seg = row_segs[:, None] == seg_row[None, :]
        causal = places[None, :] <= row_places[:, None]
        allowed = reach_table & (jnp.logical_not(same_seg) | causal)
        probs_low = low(jax.nn.softmax(jnp.where(allowed[None], raw_scores, MASKED), axis=-1))
        return jnp.einsum('hqk,hkd->hqd', probs_low, values_rep, precision=lax.Precision.HIGHEST)
    starts = (jnp.arange(4, dtype=jnp.int32) * block_rows).astype(jnp.int32)
    blocks = lax.map(jax.checkpoint(attend_block), starts)
    return blocks.transpose(0, 2, 1, 3).reshape(TREE, QH * HD)

def layer_apply(tree_input, weights, seg_row, parent_row):
    attn_scale, w_query, w_key, w_value, w_out, q_scale, k_scale, mlp_scale, w_gate, w_up, w_down = weights
    positions, ancestor = tree_layout(seg_row, parent_row)
    residual = low_back(tree_input)
    normed = low(rms_scale(residual, attn_scale))
    q_pre = low_back(matmul(normed, w_query))
    k_pre = low_back(matmul(normed, w_key))
    value_low = low_back(low(matmul(normed, w_value)))
    cos_table, sine_table = rope_tables(positions, HD)
    queries = low(rotate(rms_scale(q_pre.reshape(TREE, QH, HD), q_scale), cos_table, sine_table))
    keys_low = low(rotate(rms_scale(k_pre.reshape(TREE, KH, HD), k_scale), cos_table, sine_table))
    group_size = QH // KH
    keys_rep = jnp.repeat(keys_low.transpose(1, 0, 2), group_size, axis=0)
    values_rep = jnp.repeat(value_low.reshape(TREE, KH, HD).transpose(1, 0, 2), group_size, axis=0)
    attended = attend(queries.transpose(1, 0, 2), keys_rep, values_rep, seg_row, ancestor)
    attended = low_back(low(attended))
    attn_out = low_back(matmul(attended, w_out))
    middle = residual + attn_out
    mlp_in = low(rms_scale(middle, mlp_scale))
    gate_pre = low_back(matmul(mlp_in, w_gate))
    up_pre = low_back(matmul(mlp_in, w_up))
    hidden_low = low(jax.nn.silu(gate_pre) * up_pre)
    mlp_out = low_back(matmul(hidden_low, w_down))
    return middle + mlp_out

def reference(inputs, cotangent, seg_ids, parents, order, attn_gain, w_query, w_key, w_value, w_out, q_gain, k_gain, mlp_gain, w_gate, w_up, w_down):
    weights = tuple((weight.astype(jnp.float32) for weight in (attn_gain, w_query, w_key, w_value, w_out, q_gain, k_gain, mlp_gain, w_gate, w_up, w_down)))
    picked = inputs[order].astype(jnp.float32)
    seg_rows_all = seg_ids[order]
    parent_rows = parents[order]
    boundary = jnp.zeros_like(picked)
    layer_saved = jax.checkpoint(layer_apply)

    def forward(picked_in, weight_set, boundary_in):
        section_zero = tuple((weight[0] for weight in weight_set))
        section_one = tuple((weight[1] for weight in weight_set))

        def tree_step(carried, tree_item):
            tree_input, seg_row, parent_row, boundary_part = tree_item
            middle_out = low(layer_saved(tree_input, section_zero, seg_row, parent_row))
            final_out = layer_saved(middle_out + boundary_part, section_one, seg_row, parent_row)
            return (carried, (final_out, middle_out))
        _, (final_outs, middle_outs) = lax.scan(tree_step, jnp.zeros((), jnp.float32), (picked_in, seg_rows_all, parent_rows, boundary_in))
        return (final_outs, middle_outs)
    final_outs, pull_back, middle_outs = jax.vjp(forward, picked, weights, boundary, has_aux=True)
    d_picked, d_weights, d_boundary = pull_back(cotangent.astype(jnp.float32))
    layer_out = jnp.stack([middle_outs, final_outs]).astype(jnp.bfloat16)
    input_grad = jnp.stack([d_picked, d_boundary]).astype(jnp.bfloat16)
    return (layer_out, input_grad, d_weights[0], d_weights[1], d_weights[2], d_weights[3], d_weights[4], d_weights[5], d_weights[6], d_weights[7], d_weights[8], d_weights[9], d_weights[10])
```

```python
from functools import partial

import jax
import jax.numpy as jnp
from jax import lax
from jax.sharding import PartitionSpec as P

HD = 128
TRUNK = 512
BRANCH = 96
NB = 4
TREE = 1152
SEGS = 9


EPSILON = 1e-06
THETA = 1000000.0
MASKED = -1e30
F32 = jnp.float32
BF16 = jnp.bfloat16


def rms_scale(values, weight_gain):
    mean_sq = jnp.mean(values * values, axis=-1, keepdims=True)
    return values * lax.rsqrt(mean_sq + EPSILON) * weight_gain


def rotate(values, cos_table, sine_table):
    middle_at = values.shape[-1] // 2
    leading = values[..., :middle_at]
    trailing = values[..., middle_at:]
    return jnp.concatenate(
        [leading * cos_table - trailing * sine_table, trailing * cos_table + leading * sine_table],
        axis=-1,
    )


def rope_tables(positions, head_dim):
    half_steps = jnp.arange(head_dim // 2, dtype=F32)
    inverse = THETA ** (-2.0 * half_steps / head_dim)
    angles = positions.astype(F32)[:, None] * inverse[None, :]
    return (jnp.cos(angles)[:, None, :], jnp.sin(angles)[:, None, :])


def swiglu(gate_in, up_in):
    return jax.nn.silu(gate_in) * up_in


def embed_heads(q_pre, k_pre, q_scale, k_scale, cos_table, sine_table):
    row_count = q_pre.shape[0]
    queries = rms_scale(q_pre.reshape(row_count, -1, HD), q_scale)
    keys_part = rms_scale(k_pre.reshape(row_count, -1, HD), k_scale)
    return (rotate(queries, cos_table, sine_table), rotate(keys_part, cos_table, sine_table))


def tree_layout(seg_row, parent_row):
    labels = jnp.arange(SEGS, dtype=jnp.int32)
    places = jnp.arange(TREE, dtype=jnp.int32)
    member = seg_row[None, :] == labels[:, None]
    starts = jnp.min(jnp.where(member, places[None, :], TREE), axis=1)
    depth_base = jnp.where(labels == 0, 0, jnp.where(labels <= NB, TRUNK, TRUNK + BRANCH))
    shifts = depth_base - starts
    positions = places + jnp.sum(jnp.where(member, shifts[:, None], 0), axis=0)
    grandparent = jnp.sum(
        jnp.where(parent_row[:, None] == labels[None, :], parent_row[None, :], 0), axis=1
    )
    ancestor = (
        (labels[None, :] == labels[:, None])
        | (labels[None, :] == parent_row[:, None])
        | (labels[None, :] == grandparent[:, None])
    )
    return (positions, member.astype(F32), ancestor.astype(F32))


def path_mask(seg_row, parent_row, row_start, row_count):
    positions, member, ancestor = tree_layout(seg_row, parent_row)
    member_rows = lax.dynamic_slice_in_dim(member, row_start, row_count, 1)
    seg_rows = lax.dynamic_slice_in_dim(seg_row, row_start, row_count, 0)
    reach_table = jnp.dot(jnp.dot(member_rows.T, ancestor), member)
    places = jnp.arange(TREE, dtype=jnp.int32)
    row_places = row_start + jnp.arange(row_count, dtype=jnp.int32)
    same_seg = seg_rows[:, None] == seg_row[None, :]
    causal = places[None, :] <= row_places[:, None]
    allowed = (reach_table > 0.5) & (jnp.logical_not(same_seg) | causal)
    row_positions = lax.dynamic_slice_in_dim(positions, row_start, row_count, 0)
    return (allowed, row_positions)


OUTER = (((0,), (0,)), ((), ()))
INNER = (((1,), (1,)), ((), ()))


def dot(left, right):
    return jnp.dot(left, right, preferred_element_type=F32)


def dot_inner(left, right):
    return lax.dot_general(left, right, INNER, preferred_element_type=F32)


def dot_outer(left, right):
    return lax.dot_general(left, right, OUTER, preferred_element_type=F32)


def exchange(pieces, axis):
    size = lax.axis_size(axis)
    me = lax.axis_index(axis)
    got = jnp.zeros_like(pieces)
    own = lax.dynamic_index_in_dim(pieces, me, 0, keepdims=True)
    got = lax.dynamic_update_slice_in_dim(got, own, me, 0)
    for step in range(1, size):
        other = me ^ step
        piece = lax.dynamic_index_in_dim(pieces, other, 0, keepdims=True)
        arrived = lax.ppermute(piece, axis, [(i, i ^ step) for i in range(size)])
        got = lax.dynamic_update_slice_in_dim(got, arrived, other, 0)
    return got


def masked_scores(query_bf, key_all, allowed):
    row_count = query_bf.shape[0]
    kv_heads = key_all.shape[1] // HD
    grouped = query_bf.reshape(row_count, kv_heads, -1, HD)
    key_heads = key_all.reshape(key_all.shape[0], kv_heads, HD)
    raw_scores = jnp.einsum(
        "rkgd,tkd->kgrt", grouped, key_heads, preferred_element_type=F32
    ) * HD ** (-0.5)
    return (jnp.where(allowed[None, None], raw_scores, MASKED), grouped, key_heads)


def layer_forward(hidden_in, weights, gains, slot):
    attn_scale, q_scale, k_scale, mlp_scale = gains
    w_qkv, w_outt, w_gate, w_up, w_downt, q_width, k_width = weights
    allowed, cos_table, sine_table = slot
    residual = hidden_in.astype(F32)
    normed = rms_scale(residual, attn_scale).astype(BF16)
    qkv = dot(normed, w_qkv)
    q_pre = qkv[:, :q_width]
    k_pre = qkv[:, q_width : q_width + k_width]
    value_bf = qkv[:, q_width + k_width :].astype(BF16)
    queries, keys_rot = embed_heads(q_pre, k_pre, q_scale, k_scale, cos_table, sine_table)
    query_bf = queries.astype(BF16)
    key_bf = keys_rot.reshape(keys_rot.shape[0], -1).astype(BF16)
    kv_all = lax.all_gather(jnp.concatenate([key_bf, value_bf], axis=1), "dp", axis=0, tiled=True)
    key_all = kv_all[:, :k_width]
    value_all = kv_all[:, k_width:]
    scores, grouped, key_heads = masked_scores(query_bf, key_all, allowed)
    row_max = jnp.max(scores, axis=-1, keepdims=True)
    exp_scores = jnp.exp(scores - row_max)
    row_total = jnp.sum(exp_scores, axis=-1, keepdims=True)
    prob_bf = (exp_scores / row_total).astype(BF16)
    log_total = row_max + jnp.log(row_total)
    value_heads = value_all.reshape(value_all.shape[0], -1, HD)
    attended = jnp.einsum("kgrt,tkd->rkgd", prob_bf, value_heads, preferred_element_type=F32)
    attended_bf = attended.reshape(attended.shape[0], -1).astype(BF16)
    attn_partial = dot_inner(attended_bf, w_outt).astype(BF16)
    attn_rows = lax.psum_scatter(attn_partial, "tensor", scatter_dimension=0, tiled=True)
    own_rows = attn_rows.shape[0]
    own_in = lax.dynamic_slice_in_dim(
        hidden_in, lax.axis_index("tensor") * own_rows, own_rows, 0
    ).astype(F32)
    middle = own_in + attn_rows.astype(F32)
    mlp_in = lax.all_gather(
        rms_scale(middle, mlp_scale).astype(BF16), "dp", axis=0, tiled=True
    )
    gate_pre = dot(mlp_in, w_gate)
    upward = dot(mlp_in, w_up)
    hidden_bf = swiglu(gate_pre, upward).astype(BF16)
    mlp_partial = dot_inner(hidden_bf, w_downt).astype(BF16)
    mlp_rows = lax.psum_scatter(mlp_partial, "dp", scatter_dimension=0, tiled=True)
    output_own = (middle + mlp_rows.astype(F32)).astype(BF16)
    output_bf = lax.all_gather(output_own, "tensor", axis=0, tiled=True)
    stored = (
        own_in, normed, q_pre, k_pre, query_bf, key_all, value_all, log_total, attended_bf,
        middle, mlp_in, gate_pre, upward, hidden_bf,
    )
    return (output_bf, stored)


def layer_backward(grad_out, stored, weights, gains, slot):
    attn_scale, q_scale, k_scale, mlp_scale = gains
    w_qkv, w_outt, w_gate, w_up, w_downt, q_width, k_width = weights
    allowed, cos_table, sine_table = slot
    (
        own_in, normed, q_pre, k_pre, query_bf, key_all, value_all, log_total, attended_bf,
        middle, mlp_in, gate_pre, upward, hidden_bf,
    ) = stored
    own_rows = own_in.shape[0]
    own_grad = lax.dynamic_slice_in_dim(
        grad_out, lax.axis_index("tensor") * own_rows, own_rows, 0
    )
    grad_mlp = lax.all_gather(own_grad, "dp", axis=0, tiled=True)
    grad_hidden = dot(grad_mlp, w_downt)
    _, swiglu_pull = jax.vjp(swiglu, gate_pre, upward)
    grad_gate, grad_upward = swiglu_pull(grad_hidden)
    gate_bf = grad_gate.astype(BF16)
    up_bf = grad_upward.astype(BF16)
    mlp_partial = (dot_inner(gate_bf, w_gate) + dot_inner(up_bf, w_up)).astype(BF16)
    mlp_rows = lax.psum_scatter(mlp_partial, "dp", scatter_dimension=0, tiled=True)
    _, mlp_norm_pull = jax.vjp(rms_scale, middle, mlp_scale)
    grad_middle, grad_mlp_scale = mlp_norm_pull(mlp_rows.astype(F32))
    grad_middle = grad_middle + own_grad.astype(F32)
    grad_attn = lax.all_gather(grad_middle.astype(BF16), "tensor", axis=0, tiled=True)
    grad_attended = dot(grad_attn, w_outt).astype(BF16)
    scores, grouped, key_heads = masked_scores(query_bf, key_all, allowed)
    prob_full = jnp.exp(scores - log_total)
    value_heads = value_all.reshape(value_all.shape[0], -1, HD)
    grad_heads = grad_attended.reshape(grouped.shape)
    grad_prob = jnp.einsum(
        "rkgd,tkd->kgrt", grad_heads, value_heads, preferred_element_type=F32
    )
    row_dot = jnp.sum(prob_full * grad_prob, axis=-1, keepdims=True)
    grad_scores = (prob_full * (grad_prob - row_dot)).astype(BF16)
    scale_factor = HD ** (-0.5)
    grad_query = (
        jnp.einsum("kgrt,tkd->rkgd", grad_scores, key_heads, preferred_element_type=F32)
        * scale_factor
    )
    grad_key_all = (
        jnp.einsum("kgrt,rkgd->tkd", grad_scores, grouped, preferred_element_type=F32)
        * scale_factor
    )
    grad_value_all = jnp.einsum(
        "kgrt,rkgd->tkd", prob_full.astype(BF16), grad_heads, preferred_element_type=F32
    )
    tree_rows = grad_key_all.shape[0]
    grad_kv = lax.psum_scatter(
        jnp.concatenate(
            [grad_key_all.reshape(tree_rows, -1), grad_value_all.reshape(tree_rows, -1)], axis=1
        ).astype(BF16),
        "dp",
        scatter_dimension=0,
        tiled=True,
    )
    grad_key = grad_kv[:, :k_width].astype(F32)
    value_grad_bf = grad_kv[:, k_width:]
    row_count = q_pre.shape[0]
    _, embedding_pull = jax.vjp(
        partial(embed_heads, cos_table=cos_table, sine_table=sine_table),
        q_pre, k_pre, q_scale, k_scale,
    )
    grad_q_pre, grad_k_pre, grad_q_scale, grad_k_scale = embedding_pull(
        (grad_query.reshape(row_count, -1, HD), grad_key.reshape(row_count, -1, HD))
    )
    qkv_grad = jnp.concatenate(
        [grad_q_pre.astype(BF16), grad_k_pre.astype(BF16), value_grad_bf], axis=1
    )
    attn_partial = dot_inner(qkv_grad, w_qkv).astype(BF16)
    attn_rows = lax.psum_scatter(attn_partial, "tensor", scatter_dimension=0, tiled=True)
    _, attn_norm_pull = jax.vjp(rms_scale, own_in, attn_scale)
    grad_residual, grad_attn_scale = attn_norm_pull(attn_rows.astype(F32))
    incoming_own = (grad_residual + grad_middle).astype(BF16)
    incoming = lax.all_gather(incoming_own, "tensor", axis=0, tiled=True)
    products = (
        (normed, qkv_grad),
        (grad_attn, attended_bf),
        (mlp_in, gate_bf),
        (mlp_in, up_bf),
        (grad_mlp, hidden_bf),
    )
    return (incoming, products, (grad_q_scale, grad_k_scale, grad_attn_scale, grad_mlp_scale))


def on_device(
    inputs, cotangent, seg_ids, parents, order, attn_gain, w_query, w_key, w_value, w_out,
    q_gain, k_gain, mlp_gain, w_gate, w_up, w_down,
):
    section_index = lax.axis_index("section")
    data_index = lax.axis_index("dp")
    dp_size = lax.axis_size("dp")
    tensor_size = lax.axis_size("tensor")
    micro_count, row_count, depth = inputs.shape
    row_start = data_index * row_count
    first_section = section_index == 0
    q_width = w_query.shape[2]
    k_width = w_key.shape[2]
    own_depth = w_query.shape[1]
    own_units = w_gate.shape[2]
    share = own_units // dp_size

    gains_all = lax.all_gather(
        jnp.concatenate([attn_gain, mlp_gain], axis=0), "dp", axis=1, tiled=True
    ).astype(F32)
    gains = (gains_all[0], q_gain[0].astype(F32), k_gain[0].astype(F32), gains_all[1])

    attn_shard = jnp.concatenate([w_query[0], w_key[0], w_value[0], w_out[0].T], axis=1)
    attn_all = lax.all_gather(attn_shard, "dp", axis=0, tiled=True)
    qkv_width = q_width + 2 * k_width
    w_qkv = attn_all[:, :qkv_width]
    w_outt = attn_all[:, qkv_width:]

    def spread(shard):
        pieces = shard.reshape(own_depth, dp_size, share).transpose(1, 0, 2)
        rows = exchange(pieces, "dp").reshape(depth, share)
        return lax.all_gather(rows, "tensor", axis=1, tiled=True)

    weights = (
        w_qkv, w_outt, spread(w_gate[0]), spread(w_up[0]), spread(w_down[0].T), q_width, k_width,
    )

    def slot_setup(slot_index):
        tree_id = lax.dynamic_index_in_dim(order, slot_index, 0, keepdims=False)
        seg_row = lax.dynamic_index_in_dim(seg_ids, tree_id, 0, keepdims=False)
        parent_row = lax.dynamic_index_in_dim(parents, tree_id, 0, keepdims=False)
        allowed, row_positions = path_mask(seg_row, parent_row, row_start, row_count)
        cos_table, sine_table = rope_tables(row_positions, HD)
        return (tree_id, (allowed, cos_table, sine_table))

    ticks = micro_count + 1
    incoming = jnp.zeros((row_count, depth), BF16)
    outputs, kept, slots = [], [], []
    for tick in range(ticks):
        slot_index = jnp.clip(tick - section_index, 0, micro_count - 1)
        tree_id, slot = slot_setup(slot_index)
        fresh_rows = lax.dynamic_index_in_dim(inputs, tree_id, 0, keepdims=False)
        hidden_in = jnp.where(first_section, fresh_rows, incoming)
        output_bf, stored = layer_forward(hidden_in, weights, gains, slot)
        if tick + 1 < ticks:
            incoming = lax.ppermute(output_bf, "section", [(0, 1)])
        outputs.append(output_bf)
        kept.append(stored)
        slots.append(slot)

    incoming = jnp.zeros((row_count, depth), BF16)
    grads, products, gain_parts = [None] * ticks, [None] * ticks, [None] * ticks
    for step in range(ticks):
        tick = ticks - 1 - step
        slot_index = jnp.clip(tick - section_index, 0, micro_count - 1)
        fresh_rows = lax.dynamic_index_in_dim(cotangent, slot_index, 0, keepdims=False)
        grad_out = jnp.where(first_section, incoming, fresh_rows)
        incoming_out, products[tick], gain_parts[tick] = layer_backward(
            grad_out, kept[tick], weights, gains, slots[tick]
        )
        if tick > 0:
            incoming = lax.ppermute(incoming_out, "section", [(1, 0)])
        grads[tick] = incoming_out

    def of_section(items):
        return [jnp.where(first_section, items[i], items[i + 1]) for i in range(micro_count)]

    layer_out = jnp.stack(of_section(outputs))[None]
    input_grad = jnp.stack(of_section(grads))[None]

    def weight_grad(which):
        left = jnp.concatenate(of_section([p[which][0] for p in products]), axis=0)
        right = jnp.concatenate(of_section([p[which][1] for p in products]), axis=0)
        return dot_outer(left, right).astype(BF16)

    def collect(which):
        whole = weight_grad(which)
        rows = lax.psum_scatter(whole, "tensor", scatter_dimension=1, tiled=True)
        pieces = exchange(rows.reshape(dp_size, own_depth, share), "dp")
        return pieces.transpose(1, 0, 2).reshape(own_depth, own_units).astype(F32)

    grad_down = collect(4).T
    grad_gate = collect(2)
    grad_up = collect(3)
    attn_grad = lax.psum_scatter(
        jnp.concatenate([weight_grad(0), weight_grad(1)], axis=1),
        "dp", scatter_dimension=0, tiled=True,
    ).astype(F32)
    gain_sums = [
        sum(of_section([part[which] for part in gain_parts])) for which in range(4)
    ]
    flat = jnp.concatenate([gain_sums[0], gain_sums[1], gain_sums[2], gain_sums[3]])
    gain_total = lax.psum(flat, ("dp", "tensor"))
    share_width = attn_gain.shape[1]
    attn_gain_grad = lax.dynamic_slice_in_dim(
        gain_total, 2 * HD + data_index * share_width, share_width, 0
    )
    mlp_gain_grad = lax.dynamic_slice_in_dim(
        gain_total, 2 * HD + depth + data_index * share_width, share_width, 0
    )
    return (
        layer_out,
        input_grad,
        attn_gain_grad[None],
        attn_grad[:, :q_width][None],
        attn_grad[:, q_width : q_width + k_width][None],
        attn_grad[:, q_width + k_width : qkv_width][None],
        attn_grad[:, qkv_width:].T[None],
        gain_total[:HD][None],
        gain_total[HD : 2 * HD][None],
        mlp_gain_grad[None],
        grad_gate[None],
        grad_up[None],
        grad_down[None],
    )


def solution(mesh):
    rows = P(None, "dp", None)
    wide = P("section", "dp", "tensor")
    tall = P("section", "tensor", "dp")
    gain = P("section", "dp")
    head_gain = P("section", None)
    slots = P("section", None, "dp", None)
    in_specs = (
        rows, rows, P(), P(), P(), gain, wide, wide, wide, tall, head_gain, head_gain, gain,
        wide, wide, tall,
    )
    out_specs = (
        slots, slots, gain, wide, wide, wide, tall, head_gain, head_gain, gain, wide, wide, tall,
    )
    return jax.shard_map(
        on_device, mesh=mesh, in_specs=in_specs, out_specs=out_specs, check_vma=False
    )
```

```python
from functools import partial

import jax
import jax.numpy as jnp
from jax import lax
from jax.sharding import PartitionSpec as P

HD = 128
TRUNK = 512
BRANCH = 96
NB = 4
TREE = 1152
SEGS = 9


EPSILON = 1e-06
THETA = 1000000.0
MASKED = -1e30
F32 = jnp.float32
BF16 = jnp.bfloat16


def rms_scale(values, weight_gain):
    mean_sq = jnp.mean(values * values, axis=-1, keepdims=True)
    return values * lax.rsqrt(mean_sq + EPSILON) * weight_gain


def rotate(values, cos_table, sine_table):
    middle_at = values.shape[-1] // 2
    leading = values[..., :middle_at]
    trailing = values[..., middle_at:]
    return jnp.concatenate(
        [leading * cos_table - trailing * sine_table, trailing * cos_table + leading * sine_table],
        axis=-1,
    )


def rope_tables(positions, head_dim):
    half_steps = jnp.arange(head_dim // 2, dtype=F32)
    inverse = THETA ** (-2.0 * half_steps / head_dim)
    angles = positions.astype(F32)[:, None] * inverse[None, :]
    return (jnp.cos(angles)[:, None, :], jnp.sin(angles)[:, None, :])


def swiglu(gate_in, up_in):
    return jax.nn.silu(gate_in) * up_in


def embed_heads(q_pre, k_pre, q_scale, k_scale, cos_table, sine_table):
    row_count = q_pre.shape[0]
    queries = rms_scale(q_pre.reshape(row_count, -1, HD), q_scale)
    keys_part = rms_scale(k_pre.reshape(row_count, -1, HD), k_scale)
    return (rotate(queries, cos_table, sine_table), rotate(keys_part, cos_table, sine_table))


def tree_layout(seg_row, parent_row):
    labels = jnp.arange(SEGS, dtype=jnp.int32)
    places = jnp.arange(TREE, dtype=jnp.int32)
    member = seg_row[None, :] == labels[:, None]
    starts = jnp.min(jnp.where(member, places[None, :], TREE), axis=1)
    depth_base = jnp.where(labels == 0, 0, jnp.where(labels <= NB, TRUNK, TRUNK + BRANCH))
    shifts = depth_base - starts
    positions = places + jnp.sum(jnp.where(member, shifts[:, None], 0), axis=0)
    grandparent = jnp.sum(
        jnp.where(parent_row[:, None] == labels[None, :], parent_row[None, :], 0), axis=1
    )
    ancestor = (
        (labels[None, :] == labels[:, None])
        | (labels[None, :] == parent_row[:, None])
        | (labels[None, :] == grandparent[:, None])
    )
    return (positions, member.astype(F32), ancestor.astype(F32))


def path_mask(seg_row, parent_row, row_start, row_count):
    positions, member, ancestor = tree_layout(seg_row, parent_row)
    member_rows = lax.dynamic_slice_in_dim(member, row_start, row_count, 1)
    seg_rows = lax.dynamic_slice_in_dim(seg_row, row_start, row_count, 0)
    reach_table = jnp.dot(jnp.dot(member_rows.T, ancestor), member)
    places = jnp.arange(TREE, dtype=jnp.int32)
    row_places = row_start + jnp.arange(row_count, dtype=jnp.int32)
    same_seg = seg_rows[:, None] == seg_row[None, :]
    causal = places[None, :] <= row_places[:, None]
    allowed = (reach_table > 0.5) & (jnp.logical_not(same_seg) | causal)
    row_positions = lax.dynamic_slice_in_dim(positions, row_start, row_count, 0)
    return (allowed, row_positions)


OUTER = (((0,), (0,)), ((), ()))
INNER = (((1,), (1,)), ((), ()))


def dot(left, right):
    return jnp.dot(left, right, preferred_element_type=F32)


def dot_inner(left, right):
    return lax.dot_general(left, right, INNER, preferred_element_type=F32)


def dot_outer(left, right):
    return lax.dot_general(left, right, OUTER, preferred_element_type=F32)


def exchange(pieces, axis):
    size = lax.axis_size(axis)
    me = lax.axis_index(axis)
    got = jnp.zeros_like(pieces)
    own = lax.dynamic_index_in_dim(pieces, me, 0, keepdims=True)
    got = lax.dynamic_update_slice_in_dim(got, own, me, 0)
    for step in range(1, size):
        other = me ^ step
        piece = lax.dynamic_index_in_dim(pieces, other, 0, keepdims=True)
        arrived = lax.ppermute(piece, axis, [(i, i ^ step) for i in range(size)])
        got = lax.dynamic_update_slice_in_dim(got, arrived, other, 0)
    return got


def masked_scores(query_bf, key_all, allowed):
    raw_scores = jnp.einsum(
        "brgd,btd->bgrt", query_bf, key_all, preferred_element_type=F32
    ) * HD ** (-0.5)
    return jnp.where(allowed[:, None], raw_scores, MASKED)


def gather_kv(own):
    return lax.all_gather(own, "dp", axis=1, tiled=True)


def scatter_kv(whole):
    return lax.psum_scatter(whole, "dp", scatter_dimension=1, tiled=True)


def scatter_attn(whole):
    mine = lax.psum_scatter(whole, "section", scatter_dimension=0, tiled=True)
    return lax.psum_scatter(mine, "tensor", scatter_dimension=1, tiled=True)[0]


def gather_rows(own):
    mine = lax.all_gather(own, "tensor", axis=0, tiled=True)
    return lax.all_gather(mine, "section", axis=0)


def gather_mlp(own):
    mine = lax.all_gather(own, "dp", axis=0, tiled=True)
    return lax.all_gather(mine, "section", axis=0, tiled=True)


def scatter_mlp(whole):
    mine = lax.psum_scatter(whole, "section", scatter_dimension=0, tiled=True)
    return lax.psum_scatter(mine, "dp", scatter_dimension=0, tiled=True)


def embed(q_pre, k_pre, q_scale, k_scale, cos_table, sine_table):
    queries = rms_scale(q_pre, q_scale)
    keys = rms_scale(k_pre, k_scale)
    return (
        rotate(queries, cos_table[:, :, None], sine_table[:, :, None]),
        rotate(keys, cos_table, sine_table),
    )


def layer_forward(hidden_in, own_in, weights, gains, slot):
    attn_scale, mlp_scale, q_scale, k_scale = gains
    w_qkv, w_outt, w_gate, w_up, w_down = weights
    allowed, cos_table, sine_table = slot
    trees, row_count, depth = hidden_in.shape
    q_width = w_outt.shape[1]
    normed = rms_scale(hidden_in.astype(F32), attn_scale).astype(BF16).reshape(-1, depth)
    qkv = dot(normed, w_qkv).reshape(trees, row_count, -1)
    q_pre = qkv[:, :, :q_width].reshape(trees, row_count, -1, HD)
    k_pre = qkv[:, :, q_width : q_width + HD]
    value_bf = qkv[:, :, q_width + HD :].astype(BF16)
    queries, keys_rot = embed(q_pre, k_pre, q_scale, k_scale, cos_table, sine_table)
    query_bf = queries.astype(BF16)
    kv_all = gather_kv(jnp.concatenate([keys_rot.astype(BF16), value_bf], axis=2))
    key_all = kv_all[:, :, :HD]
    value_all = kv_all[:, :, HD:]
    scores = masked_scores(query_bf, key_all, allowed)
    row_max = jnp.max(scores, axis=-1, keepdims=True)
    exp_scores = jnp.exp(scores - row_max)
    row_total = jnp.sum(exp_scores, axis=-1, keepdims=True)
    prob_bf = (exp_scores / row_total).astype(BF16)
    log_total = row_max + jnp.log(row_total)
    attended = jnp.einsum("bgrt,btd->brgd", prob_bf, value_all, preferred_element_type=F32)
    attended_bf = attended.reshape(trees * row_count, -1).astype(BF16)
    attn_partial = dot_inner(attended_bf, w_outt).astype(BF16).reshape(trees, row_count, depth)
    middle = own_in + scatter_attn(attn_partial).astype(F32)
    mlp_in = gather_mlp(rms_scale(middle, mlp_scale).astype(BF16))
    gate_pre = dot_inner(mlp_in, w_gate)
    upward = dot_inner(mlp_in, w_up)
    hidden_bf = swiglu(gate_pre, upward).astype(BF16)
    mlp_rows = scatter_mlp(dot(hidden_bf, w_down).astype(BF16))
    output_own = (middle + mlp_rows.astype(F32)).astype(BF16)
    output_bf = gather_rows(output_own)
    stored = (
        own_in, normed, q_pre, k_pre, query_bf, key_all, value_all, log_total, attended_bf,
        middle, mlp_in, gate_pre, upward, hidden_bf,
    )
    return (output_bf, output_own.astype(F32), stored)


def layer_backward(grad_own, stored, weights, gains, slot, shared_kv):
    attn_scale, mlp_scale, q_scale, k_scale = gains
    w_qkv, w_outt, w_gate, w_up, w_down = weights
    allowed, cos_table, sine_table = slot
    (
        own_in, normed, q_pre, k_pre, query_bf, key_all, value_all, log_total, attended_bf,
        middle, mlp_in, gate_pre, upward, hidden_bf,
    ) = stored
    trees, row_count = query_bf.shape[:2]
    depth = normed.shape[1]
    grad_mlp = gather_mlp(grad_own)
    grad_hidden = dot_inner(grad_mlp, w_down)
    _, swiglu_pull = jax.vjp(swiglu, gate_pre, upward)
    grad_gate, grad_upward = swiglu_pull(grad_hidden)
    gate_bf = grad_gate.astype(BF16)
    up_bf = grad_upward.astype(BF16)
    mlp_rows = scatter_mlp((dot(gate_bf, w_gate) + dot(up_bf, w_up)).astype(BF16))
    _, mlp_norm_pull = jax.vjp(rms_scale, middle, mlp_scale)
    grad_middle, grad_mlp_scale = mlp_norm_pull(mlp_rows.astype(F32))
    grad_middle = grad_middle + grad_own.astype(F32)
    grad_attn = gather_rows(grad_middle.astype(BF16)).reshape(-1, depth)
    grad_heads = dot(grad_attn, w_outt).astype(BF16).reshape(query_bf.shape)
    scores = masked_scores(query_bf, key_all, allowed)
    prob_full = jnp.exp(scores - log_total)
    grad_prob = jnp.einsum("brgd,btd->bgrt", grad_heads, value_all, preferred_element_type=F32)
    row_dot = jnp.sum(prob_full * grad_prob, axis=-1, keepdims=True)
    grad_scores = (prob_full * (grad_prob - row_dot)).astype(BF16)
    scale_factor = HD ** (-0.5)
    grad_query = (
        jnp.einsum("bgrt,btd->brgd", grad_scores, key_all, preferred_element_type=F32)
        * scale_factor
    )
    grad_key_all = (
        jnp.einsum("bgrt,brgd->btd", grad_scores, query_bf, preferred_element_type=F32)
        * scale_factor
    )
    grad_value_all = jnp.einsum(
        "bgrt,brgd->btd", prob_full.astype(BF16), grad_heads, preferred_element_type=F32
    )
    grad_kv = scatter_kv(jnp.concatenate([grad_key_all, grad_value_all], axis=2).astype(BF16))
    if shared_kv:
        total = lax.psum(grad_kv, "section")
        grad_kv = jnp.where(lax.axis_index("section") == 0, total, jnp.zeros_like(total))
    _, embedding_pull = jax.vjp(
        partial(embed, cos_table=cos_table, sine_table=sine_table), q_pre, k_pre, q_scale, k_scale
    )
    grad_q_pre, grad_k_pre, grad_q_scale, grad_k_scale = embedding_pull(
        (grad_query, grad_kv[:, :, :HD].astype(F32))
    )
    qkv_grad = jnp.concatenate(
        [
            grad_q_pre.astype(BF16).reshape(trees, row_count, -1),
            grad_k_pre.astype(BF16),
            grad_kv[:, :, HD:],
        ],
        axis=2,
    ).reshape(trees * row_count, -1)
    attn_partial = dot_inner(qkv_grad, w_qkv).astype(BF16).reshape(trees, row_count, depth)
    attn_rows = scatter_attn(attn_partial)
    _, attn_norm_pull = jax.vjp(rms_scale, own_in, attn_scale)
    grad_residual, grad_attn_scale = attn_norm_pull(attn_rows.astype(F32))
    incoming_own = (grad_residual + grad_middle).astype(BF16)
    incoming = gather_rows(incoming_own)
    products = (
        (normed, qkv_grad),
        (grad_attn, attended_bf),
        (gate_bf, mlp_in),
        (up_bf, mlp_in),
        (hidden_bf, grad_mlp),
    )
    gain_grads = jnp.concatenate([grad_attn_scale, grad_mlp_scale, grad_q_scale, grad_k_scale])
    return (incoming, incoming_own, products, gain_grads)


def swap_cores(mine, other):
    core = lax.axis_index("section")
    arrived = lax.ppermute(other, "section", [(0, 1), (1, 0)])
    return (jnp.where(core == 0, mine, arrived), jnp.where(core == 0, arrived, mine))


def on_device(
    inputs, cotangent, seg_ids, parents, order, attn_gain, w_query, w_key, w_value, w_out,
    q_gain, k_gain, mlp_gain, w_gate, w_up, w_down,
):
    core = lax.axis_index("section")
    data_index = lax.axis_index("dp")
    tensor_index = lax.axis_index("tensor")
    dp_size = lax.axis_size("dp")
    tensor_size = lax.axis_size("tensor")
    trees, row_count, depth = inputs.shape
    own_rows = row_count // tensor_size
    row_start = data_index * row_count
    own_depth = w_query.shape[1]
    q_width = w_query.shape[2] // 2
    shared_kv = w_key.shape[2] == HD
    k_width = HD if shared_kv else w_key.shape[2] // 2
    own_units = w_gate.shape[2]
    share = own_units // (2 * dp_size)

    def pick(stacked, index):
        return lax.dynamic_index_in_dim(stacked, index, 0, keepdims=False)

    gains_own = jnp.concatenate([attn_gain[0], mlp_gain[0], q_gain[0], k_gain[0]])
    gains_all = lax.all_gather(gains_own, ("section", "dp")).astype(F32)
    gains_all = gains_all.reshape(2, dp_size, -1)
    gains = [
        (
            gains_all[layer, :, :own_depth].reshape(depth),
            gains_all[layer, :, own_depth : 2 * own_depth].reshape(depth),
            gains_all[layer, 0, 2 * own_depth : 2 * own_depth + HD],
            gains_all[layer, 0, 2 * own_depth + HD :],
        )
        for layer in range(2)
    ]

    def halves(width, array):
        return [array[:, :width], array[:, array.shape[1] - width :]]

    attn_halves = jnp.stack(
        [
            jnp.concatenate(parts, axis=1)
            for parts in zip(
                halves(q_width, w_query[0]),
                halves(k_width, w_key[0]),
                halves(k_width, w_value[0]),
                halves(q_width, w_out[0].T),
            )
        ]
    )
    attn_shards = swap_cores(pick(attn_halves, core), pick(attn_halves, 1 - core))
    unit_blocks = jnp.stack([w_gate[0].T, w_up[0].T, w_down[0]]).reshape(
        3, 2, dp_size, share, own_depth
    )
    unit_blocks = unit_blocks.transpose(1, 2, 0, 3, 4)
    unit_shards = swap_cores(pick(unit_blocks, core), pick(unit_blocks, 1 - core))

    qkv_width = q_width + 2 * k_width
    weights = []
    for layer in range(2):
        attn_all = lax.all_gather(attn_shards[layer], "dp", axis=0, tiled=True)
        pieces = exchange(unit_shards[layer], "dp")
        pieces = pieces.transpose(1, 2, 0, 3).reshape(3, share, depth)
        mats = [lax.all_gather(pieces[i], "tensor", axis=0, tiled=True) for i in range(3)]
        weights.append((attn_all[:, :qkv_width], attn_all[:, qkv_width:], *mats))

    def slot_setup(slot_index):
        tree_id = pick(order, slot_index)
        allowed, row_positions = path_mask(
            pick(seg_ids, tree_id), pick(parents, tree_id), row_start, row_count
        )
        cos_table, sine_table = rope_tables(row_positions, HD)
        return (pick(inputs, tree_id), allowed, cos_table[:, 0], sine_table[:, 0])

    setups = [slot_setup(i) for i in range(trees)]
    hidden, *slot = (jnp.stack(item) for item in zip(*setups))

    def own_part(whole):
        return lax.dynamic_slice_in_dim(
            pick(whole, core), tensor_index * own_rows, own_rows, 0
        )

    own_in = own_part(hidden).astype(F32)
    outputs, kept = [], []
    for layer in range(2):
        hidden, own_in, stored = layer_forward(hidden, own_in, weights[layer], gains[layer], slot)
        outputs.append(hidden)
        kept.append(stored)

    grad_own = own_part(cotangent)
    grads, weight_grads, gain_grads = [None, None], [None, None], [None, None]
    for layer in (1, 0):
        grads[layer], grad_own, products, gain_grads[layer] = layer_backward(
            grad_own, kept[layer], weights[layer], gains[layer], slot, shared_kv
        )
        whole = [dot_outer(left, right).astype(BF16) for left, right in products]
        attn_grad = lax.psum_scatter(
            jnp.concatenate(whole[:2], axis=1), "dp", scatter_dimension=0, tiled=True
        )
        unit_grad = [
            lax.psum_scatter(item, "tensor", scatter_dimension=0, tiled=True) for item in whole[2:]
        ]
        pieces = jnp.stack(unit_grad).reshape(3, share, dp_size, own_depth).transpose(2, 0, 1, 3)
        weight_grads[layer] = (attn_grad, exchange(pieces, "dp"))

    def bring_home(first, second):
        mine, other = jnp.where(core == 0, first, second), jnp.where(core == 0, second, first)
        arrived = lax.ppermute(other, "section", [(0, 1), (1, 0)])
        return (jnp.where(core == 0, mine, arrived), jnp.where(core == 0, arrived, mine))

    attn_home = bring_home(weight_grads[0][0], weight_grads[1][0])
    unit_home = jnp.stack(bring_home(weight_grads[0][1], weight_grads[1][1]))
    unit_home = unit_home.transpose(2, 0, 1, 3, 4).reshape(3, own_units, own_depth)

    def joined(start, width):
        parts = [half[:, start : start + width] for half in attn_home]
        if shared_kv and start in (q_width, q_width + k_width):
            return parts[0].astype(F32)
        return jnp.concatenate(parts, axis=1).astype(F32)

    gain_total = lax.psum(jnp.stack(gain_grads), ("section", "dp", "tensor"))
    gain_own = pick(gain_total, core)
    share_width = attn_gain.shape[1]
    attn_gain_grad = lax.dynamic_slice_in_dim(gain_own, data_index * share_width, share_width, 0)
    mlp_gain_grad = lax.dynamic_slice_in_dim(
        gain_own, depth + data_index * share_width, share_width, 0
    )
    return (
        jnp.where(core == 0, outputs[0], outputs[1])[None],
        jnp.where(core == 0, grads[0], grads[1])[None],
        attn_gain_grad[None],
        joined(0, q_width)[None],
        joined(q_width, k_width)[None],
        joined(q_width + k_width, k_width)[None],
        joined(qkv_width, q_width).T[None],
        gain_own[2 * depth : 2 * depth + HD][None],
        gain_own[2 * depth + HD :][None],
        mlp_gain_grad[None],
        unit_home[0].T.astype(F32)[None],
        unit_home[1].T.astype(F32)[None],
        unit_home[2].astype(F32)[None],
    )


def solution(mesh):
    rows = P(None, "dp", None)
    wide = P("section", "dp", "tensor")
    tall = P("section", "tensor", "dp")
    gain = P("section", "dp")
    head_gain = P("section", None)
    slots = P("section", None, "dp", None)
    in_specs = (
        rows, rows, P(), P(), P(), gain, wide, wide, wide, tall, head_gain, head_gain, gain,
        wide, wide, tall,
    )
    out_specs = (
        slots, slots, gain, wide, wide, wide, tall, head_gain, head_gain, gain, wide, wide, tall,
    )
    return jax.shard_map(
        on_device, mesh=mesh, in_specs=in_specs, out_specs=out_specs, check_vma=False
    )
```

```python
from functools import partial

import jax
import jax.numpy as jnp
from jax import lax
from jax.experimental import pallas as pl
from jax.experimental.pallas import tpu as pltpu
from jax.sharding import PartitionSpec as P

HD = 128
TRUNK = 512
BRANCH = 96
NB = 4
TREE = 1152
SEGS = 9


EPSILON = 1e-06
THETA = 1000000.0
MASKED = -1e30
F32 = jnp.float32
BF16 = jnp.bfloat16


def rms_scale(values, weight_gain):
    mean_sq = jnp.mean(values * values, axis=-1, keepdims=True)
    return values * lax.rsqrt(mean_sq + EPSILON) * weight_gain


def rotate(values, cos_table, sine_table):
    middle_at = values.shape[-1] // 2
    leading = values[..., :middle_at]
    trailing = values[..., middle_at:]
    return jnp.concatenate(
        [leading * cos_table - trailing * sine_table, trailing * cos_table + leading * sine_table],
        axis=-1,
    )


def rope_tables(positions, head_dim):
    half_steps = jnp.arange(head_dim // 2, dtype=F32)
    inverse = THETA ** (-2.0 * half_steps / head_dim)
    angles = positions.astype(F32)[:, None] * inverse[None, :]
    return (jnp.cos(angles)[:, None, :], jnp.sin(angles)[:, None, :])


def swiglu(gate_in, up_in):
    return jax.nn.silu(gate_in) * up_in


def embed_heads(q_pre, k_pre, q_scale, k_scale, cos_table, sine_table):
    row_count = q_pre.shape[0]
    queries = rms_scale(q_pre.reshape(row_count, -1, HD), q_scale)
    keys_part = rms_scale(k_pre.reshape(row_count, -1, HD), k_scale)
    return (rotate(queries, cos_table, sine_table), rotate(keys_part, cos_table, sine_table))


def tree_layout(seg_row, parent_row):
    labels = jnp.arange(SEGS, dtype=jnp.int32)
    places = jnp.arange(TREE, dtype=jnp.int32)
    member = seg_row[None, :] == labels[:, None]
    starts = jnp.min(jnp.where(member, places[None, :], TREE), axis=1)
    depth_base = jnp.where(labels == 0, 0, jnp.where(labels <= NB, TRUNK, TRUNK + BRANCH))
    shifts = depth_base - starts
    positions = places + jnp.sum(jnp.where(member, shifts[:, None], 0), axis=0)
    grandparent = jnp.sum(
        jnp.where(parent_row[:, None] == labels[None, :], parent_row[None, :], 0), axis=1
    )
    ancestor = (
        (labels[None, :] == labels[:, None])
        | (labels[None, :] == parent_row[:, None])
        | (labels[None, :] == grandparent[:, None])
    )
    return (positions, member.astype(F32), ancestor.astype(F32))


def path_mask(seg_row, parent_row, row_start, row_count):
    positions, member, ancestor = tree_layout(seg_row, parent_row)
    member_rows = lax.dynamic_slice_in_dim(member, row_start, row_count, 1)
    seg_rows = lax.dynamic_slice_in_dim(seg_row, row_start, row_count, 0)
    reach_table = jnp.dot(jnp.dot(member_rows.T, ancestor), member)
    places = jnp.arange(TREE, dtype=jnp.int32)
    row_places = row_start + jnp.arange(row_count, dtype=jnp.int32)
    same_seg = seg_rows[:, None] == seg_row[None, :]
    causal = places[None, :] <= row_places[:, None]
    allowed = (reach_table > 0.5) & (jnp.logical_not(same_seg) | causal)
    row_positions = lax.dynamic_slice_in_dim(positions, row_start, row_count, 0)
    return (allowed, row_positions)


OUTER = (((0,), (0,)), ((), ()))
INNER = (((1,), (1,)), ((), ()))


def dot(left, right):
    return jnp.dot(left, right, preferred_element_type=F32)


def dot_inner(left, right):
    return lax.dot_general(left, right, INNER, preferred_element_type=F32)


def dot_outer(left, right):
    return lax.dot_general(left, right, OUTER, preferred_element_type=F32)


def exchange(pieces, axis):
    size = lax.axis_size(axis)
    me = lax.axis_index(axis)
    got = jnp.zeros_like(pieces)
    own = lax.dynamic_index_in_dim(pieces, me, 0, keepdims=True)
    got = lax.dynamic_update_slice_in_dim(got, own, me, 0)
    for step in range(1, size):
        other = me ^ step
        piece = lax.dynamic_index_in_dim(pieces, other, 0, keepdims=True)
        arrived = lax.ppermute(piece, axis, [(i, i ^ step) for i in range(size)])
        got = lax.dynamic_update_slice_in_dim(got, arrived, other, 0)
    return got


def masked_scores(query_bf, key_all, allowed):
    raw_scores = jnp.einsum(
        "brgd,btd->bgrt", query_bf, key_all, preferred_element_type=F32
    ) * HD ** (-0.5)
    return jnp.where(allowed[:, None], raw_scores, MASKED)


MESH = pl.DeviceIdType.MESH
CHUNK = 256


def greet(axes):
    barrier = pltpu.get_barrier_semaphore()
    count = 0
    for axis in axes:
        size = lax.axis_size(axis)
        me = lax.axis_index(axis)
        for step in range(1, size):
            pl.semaphore_signal(
                barrier, inc=1, device_id={axis: lax.rem(me + step, size)}, device_id_type=MESH
            )
        count += size - 1
    pl.semaphore_wait(barrier, count)


def remote(src, dst, send_sem, recv_sem, device_id):
    return pltpu.make_async_remote_copy(
        src_ref=src, dst_ref=dst, send_sem=send_sem, recv_sem=recv_sem,
        device_id=device_id, device_id_type=MESH,
    )


def kernel_call(kernel, out_shape, scratch, collective_id, cost_us, *args):
    in_vmem = pl.BlockSpec(memory_space=pltpu.VMEM)
    return pl.pallas_call(
        kernel,
        out_shape=out_shape,
        in_specs=[in_vmem] * len(args),
        out_specs=jax.tree.map(lambda _: in_vmem, out_shape),
        scratch_shapes=scratch,
        cost_estimate=pl.CostEstimate(flops=0, bytes_accessed=cost_us * 3_000_000, transcendentals=0),
        compiler_params=pltpu.CompilerParams(
            collective_id=collective_id, has_side_effects=True, vmem_limit_bytes=40 << 20
        ),
    )(*args)


def hub(partial_sums, own_args, body, own_outs, scatter, gathers, collective_id, cost_us):
    trees = 2
    rows, depth = own_args[0].shape
    half = depth // 2
    scatter_size = lax.axis_size(scatter) if scatter else 1
    sizes = [lax.axis_size(axis) for axis in gathers]
    n_args = len(own_args) + (1 if scatter else 0)
    n_outs = len(own_outs) + len(gathers)

    def kernel(*refs):
        args, outs, scratch = refs[:n_args], refs[n_args : n_args + n_outs], refs[n_args + n_outs :]
        own_out_refs, gathered = outs[: len(own_outs)], outs[len(own_outs) :]
        core = lax.axis_index("section")
        sibling = 1 - core
        axes = ["section"] + sorted(set(gathers) | ({scatter} if scatter else set()))

        if scatter:
            terms = args[0]
            args = args[1:]
            to_sib, from_sib, to_peer, from_peer, total_ref = scratch[:5]
            sib_send, sib_recv, peer_send, peer_recv = scratch[5:9]
            scratch = scratch[9:]
            me = lax.axis_index(scatter)

            def packed(tree, place, at):
                low = rows * place // 16 * 16
                high = -(-rows * (place + 1) // 16) * 16
                skip = rows * place - low
                parts = [
                    terms[tree, low:high, pl.ds(side * half + at, CHUNK)].astype(F32)[
                        skip : skip + rows
                    ]
                    for side in range(2)
                ]
                return jnp.concatenate(parts, axis=0)

            def columns(step):
                return pl.multiple_of(step * CHUNK, CHUNK)

            for place in range(scatter_size):
                @pl.loop(0, half // CHUNK)
                def _(step):
                    at = columns(step)
                    to_sib[place, :, pl.ds(at, CHUNK)] = packed(sibling, place, at).astype(BF16)

            greet(axes)
            to_sibling = [
                remote(
                    to_sib.at[place], from_sib.at[place], sib_send.at[place], sib_recv.at[place],
                    {"section": sibling},
                )
                for place in range(scatter_size)
            ]
            for copy in to_sibling:
                copy.start()

            def peer_copy(place, slot):
                return remote(
                    to_peer.at[place], from_peer.at[slot], peer_send.at[place],
                    peer_recv.at[slot], {scatter: place},
                )

            for place in range(scatter_size):
                to_sibling[place].wait_recv()

                @pl.loop(0, half // CHUNK)
                def _(step):
                    at = columns(step)
                    both = packed(core, place, at) + from_sib[place, :, pl.ds(at, CHUNK)].astype(F32)
                    to_peer[place, :, pl.ds(at, CHUNK)] = both.astype(BF16)

                    @pl.when(place == me)
                    def _():
                        total_ref[:, pl.ds(at, CHUNK)] = both

                @pl.when(place != me)
                def _():
                    peer_copy(place, me).start()

            for place in range(scatter_size):
                @pl.when(place != me)
                def _():
                    peer_copy(place, place).wait_recv()
                    total_ref[...] += from_peer[place].astype(F32)

            total = total_ref[...]
            total = jnp.concatenate([total[:rows], total[rows:]], axis=1)
        else:
            greet(axes)
            total = None

        result = body(total, args, own_out_refs)
        piece = jnp.concatenate([result[:, :half], result[:, half:]], axis=0).astype(BF16)
        gather_state = []
        for index, axis in enumerate(gathers):
            board, send, recv, relay_send, relay_recv = scratch[5 * index : 5 * index + 5]
            me_there = lax.axis_index(axis)
            board[core, me_there] = piece

            def spread(place, slot, board=board, send=send, recv=recv, axis=axis):
                return remote(
                    board.at[core, slot], board.at[core, slot], send.at[place], recv.at[slot],
                    {axis: place},
                )

            def relay(tree, slot, board=board, send=relay_send, recv=relay_recv):
                return remote(
                    board.at[tree, slot], board.at[tree, slot], send.at[slot], recv.at[slot],
                    {"section": sibling},
                )

            for place in range(sizes[index]):
                @pl.when(place != me_there)
                def _():
                    spread(place, me_there).start()

            relay(core, me_there).start()
            gather_state.append((board, me_there, spread, relay))

        def unpack(out, board, tree, size):
            @pl.loop(0, half // CHUNK)
            def _(step):
                at = pl.multiple_of(step * CHUNK, CHUNK)
                blocks = [board[tree, place, :, pl.ds(at, CHUNK)].astype(F32) for place in range(size)]
                for side in range(2):
                    whole = jnp.concatenate(
                        [block[side * rows : (side + 1) * rows] for block in blocks], axis=0
                    )
                    out[tree, :, pl.ds(side * half + at, CHUNK)] = whole.astype(BF16)

        for (board, me_there, spread, relay), size in zip(gather_state, sizes):
            for place in range(size):
                @pl.when(place != me_there)
                def _():
                    spread(place, place).wait_recv()
                    relay(core, place).start()

        for (board, me_there, spread, relay), size, out in zip(gather_state, sizes, gathered):
            unpack(out, board, core, size)

        for (board, me_there, spread, relay), size, out in zip(gather_state, sizes, gathered):
            for place in range(size):
                relay(sibling, place).wait_recv()
            unpack(out, board, sibling, size)

        if scatter:
            for place in range(scatter_size):
                to_sibling[place].wait_send()

                @pl.when(place != me)
                def _():
                    peer_copy(place, me).wait_send()

        for (board, me_there, spread, relay), size in zip(gather_state, sizes):
            for place in range(size):
                relay(core, place).wait_send()

                @pl.when(place != me_there)
                def _():
                    spread(place, me_there).wait_send()

    sem = pltpu.SemaphoreType.DMA
    scratch = []
    if scatter:
        boxes = pltpu.VMEM((scatter_size, 2 * rows, half), BF16)
        scratch += [boxes] * 4 + [pltpu.VMEM((2 * rows, half), F32)] + [sem((scatter_size,))] * 4
    for size in sizes:
        scratch += [pltpu.VMEM((trees, size, 2 * rows, half), BF16)] + [sem((size,))] * 4
    out_shape = [jax.ShapeDtypeStruct(shape, F32) for shape in own_outs] + [
        jax.ShapeDtypeStruct((trees, size * rows, depth), BF16) for size in sizes
    ]
    ins = ([partial_sums] if scatter else []) + list(own_args)
    return kernel_call(kernel, out_shape, scratch, collective_id, cost_us, *ins)


def hub_plain(partial_sums, own_args, body, own_outs, scatter, gathers):
    total = None
    if scatter:
        mine = lax.psum_scatter(partial_sums, "section", scatter_dimension=0, tiled=True)
        mine = lax.psum_scatter(mine, scatter, scatter_dimension=1, tiled=True)[0]
        total = mine.astype(F32)

    class Cell:
        def __setitem__(self, _, value):
            self.value = value

    cells = [Cell() for _ in own_outs]
    result = body(total, own_args, cells).astype(BF16)
    gathered = [
        lax.all_gather(lax.all_gather(result, axis, axis=0, tiled=True), "section", axis=0)
        for axis in gathers
    ]
    return [cell.value for cell in cells] + gathered


def gather_kv(own):
    trees, rows, width = own.shape
    if rows % 16:
        return lax.all_gather(own, "dp", axis=1, tiled=True)
    size = lax.axis_size("dp")

    def kernel(own_ref, out_ref, send, recv):
        me = lax.axis_index("dp")
        greet(["dp"])

        def spread(place, slot):
            return remote(
                own_ref, out_ref.at[:, slot], send.at[place], recv.at[slot], {"dp": place}
            )

        for place in range(size):
            @pl.when(place != me)
            def _():
                spread(place, me).start()

        out_ref[:, me] = own_ref[...]
        for place in range(size):
            @pl.when(place != me)
            def _():
                spread(place, place).wait_recv()
                spread(place, me).wait_send()

    shape = jax.ShapeDtypeStruct((trees, size, rows, width), BF16)
    sem = pltpu.SemaphoreType.DMA
    whole = kernel_call(kernel, shape, [sem((size,))] * 2, 1, 30, own)
    return whole.reshape(trees, size * rows, width)


def scatter_kv(whole):
    trees, all_rows, width = whole.shape
    size = lax.axis_size("dp")
    rows = all_rows // size
    if rows % 16:
        return lax.psum_scatter(whole, "dp", scatter_dimension=1, tiled=True)

    def kernel(in_ref, out_ref, boxes, send, recv):
        me = lax.axis_index("dp")
        greet(["dp"])

        def spread(place, slot):
            return remote(
                in_ref.at[:, place], boxes.at[slot], send.at[place], recv.at[slot], {"dp": place}
            )

        for place in range(size):
            @pl.when(place != me)
            def _():
                spread(place, me).start()

        boxes[me] = in_ref[:, me]
        for place in range(size):
            @pl.when(place != me)
            def _():
                spread(place, place).wait_recv()

        total = boxes[0].astype(F32)
        for place in range(1, size):
            total += boxes[place].astype(F32)
        out_ref[...] = total.astype(BF16)
        for place in range(size):
            @pl.when(place != me)
            def _():
                spread(place, me).wait_send()

    shape = jax.ShapeDtypeStruct((trees, rows, width), BF16)
    sem = pltpu.SemaphoreType.DMA
    scratch = [pltpu.VMEM((size, trees, rows, width), BF16), sem((size,)), sem((size,))]
    return kernel_call(
        kernel, shape, scratch, 2, 30, whole.reshape(trees, size, rows, width)
    )


def meet(partial_sums, own_args, body, own_outs, scatter, gathers, collective_id, cost_us):
    rows, depth = own_args[0].shape
    if rows % 8 or depth % (2 * CHUNK):
        return hub_plain(partial_sums, own_args, body, own_outs, scatter, gathers)
    return hub(partial_sums, own_args, body, own_outs, scatter, gathers, collective_id, cost_us)


def norm_body(total, args, outs):
    middle = args[0][...] + total
    outs[0][...] = middle
    mean_sq = jnp.mean(middle * middle, axis=1, keepdims=True)
    return middle * lax.rsqrt(mean_sq + EPSILON) * args[1][...]


def add_body(total, args, outs):
    result = args[0][...] + total
    outs[0][...] = result
    return result


def norm_back_body(total, args, outs):
    values, gain = args[0][...], args[1][...]
    scale = lax.rsqrt(jnp.mean(values * values, axis=1, keepdims=True) + EPSILON)
    unit = values * scale
    outs[1][...] = jnp.sum(total * unit, axis=0, keepdims=True)
    scaled = total * gain
    along = jnp.mean(scaled * unit, axis=1, keepdims=True)
    result = (scaled - unit * along) * scale + args[2][...]
    outs[0][...] = result
    return result


def pass_body(total, args, outs):
    return args[0][...]


def embed(q_pre, k_pre, q_scale, k_scale, cos_table, sine_table):
    queries = rms_scale(q_pre, q_scale)
    keys = rms_scale(k_pre, k_scale)
    return (
        rotate(queries, cos_table[:, :, None], sine_table[:, :, None]),
        rotate(keys, cos_table, sine_table),
    )


def layer_forward(hidden_in, own_in, weights, gains, slot):
    attn_scale, mlp_scale, q_scale, k_scale = gains
    w_qkv, w_outt, w_gate, w_up, w_down = weights
    allowed, cos_table, sine_table = slot
    trees, row_count, depth = hidden_in.shape
    q_width = w_outt.shape[1]
    normed = rms_scale(hidden_in.astype(F32), attn_scale).astype(BF16).reshape(-1, depth)
    qkv = dot(normed, w_qkv).reshape(trees, row_count, -1)
    q_pre = qkv[:, :, :q_width].reshape(trees, row_count, -1, HD)
    k_pre = qkv[:, :, q_width : q_width + HD]
    value_bf = qkv[:, :, q_width + HD :].astype(BF16)
    queries, keys_rot = embed(q_pre, k_pre, q_scale, k_scale, cos_table, sine_table)
    query_bf = queries.astype(BF16)
    kv_all = gather_kv(jnp.concatenate([keys_rot.astype(BF16), value_bf], axis=2))
    key_all = kv_all[:, :, :HD]
    value_all = kv_all[:, :, HD:]
    scores = masked_scores(query_bf, key_all, allowed)
    row_max = jnp.max(scores, axis=-1, keepdims=True)
    exp_scores = jnp.exp(scores - row_max)
    row_total = jnp.sum(exp_scores, axis=-1, keepdims=True)
    prob_bf = (exp_scores / row_total).astype(BF16)
    log_total = row_max + jnp.log(row_total)
    attended = jnp.einsum("bgrt,btd->brgd", prob_bf, value_all, preferred_element_type=F32)
    attended_bf = attended.reshape(trees * row_count, -1).astype(BF16)
    attn_partial = dot_inner(attended_bf, w_outt).astype(BF16).reshape(trees, row_count, depth)
    own_shape = own_in.shape
    middle, mlp_in = meet(
        attn_partial, [own_in, mlp_scale[None]], norm_body, [own_shape], "tensor", ["dp"], 3, 50
    )
    mlp_in = mlp_in.reshape(-1, depth)
    gate_pre = dot_inner(mlp_in, w_gate)
    upward = dot_inner(mlp_in, w_up)
    hidden_bf = swiglu(gate_pre, upward).astype(BF16)
    mlp_partial = dot(hidden_bf, w_down).astype(BF16).reshape(trees, -1, depth)
    output_own, output_bf = meet(
        mlp_partial, [middle], add_body, [own_shape], "dp", ["tensor"], 4, 50
    )
    stored = (
        own_in, normed, q_pre, k_pre, query_bf, key_all, value_all, log_total, attended_bf,
        middle, mlp_in, gate_pre, upward, hidden_bf,
    )
    return (output_bf, output_own.astype(BF16).astype(F32), stored)


def layer_backward(grad_own, grad_mlp, stored, weights, gains, slot, shared_kv, is_first):
    attn_scale, mlp_scale, q_scale, k_scale = gains
    w_qkv, w_outt, w_gate, w_up, w_down = weights
    allowed, cos_table, sine_table = slot
    (
        own_in, normed, q_pre, k_pre, query_bf, key_all, value_all, log_total, attended_bf,
        middle, mlp_in, gate_pre, upward, hidden_bf,
    ) = stored
    trees, row_count = query_bf.shape[:2]
    depth = normed.shape[1]
    grad_hidden = dot_inner(grad_mlp, w_down)
    _, swiglu_pull = jax.vjp(swiglu, gate_pre, upward)
    grad_gate, grad_upward = swiglu_pull(grad_hidden)
    gate_bf = grad_gate.astype(BF16)
    up_bf = grad_upward.astype(BF16)
    mlp_partial = (dot(gate_bf, w_gate) + dot(up_bf, w_up)).astype(BF16)
    own_outs = [own_in.shape, (1, depth)]
    grad_middle, grad_mlp_scale, grad_attn = meet(
        mlp_partial.reshape(trees, -1, depth),
        [middle, mlp_scale[None], grad_own],
        norm_back_body, own_outs, "dp", ["tensor"], 5, 50,
    )
    grad_attn = grad_attn.reshape(-1, depth)
    grad_heads = dot(grad_attn, w_outt).astype(BF16).reshape(query_bf.shape)
    scores = masked_scores(query_bf, key_all, allowed)
    prob_full = jnp.exp(scores - log_total)
    grad_prob = jnp.einsum("brgd,btd->bgrt", grad_heads, value_all, preferred_element_type=F32)
    row_dot = jnp.sum(prob_full * grad_prob, axis=-1, keepdims=True)
    grad_scores = (prob_full * (grad_prob - row_dot)).astype(BF16)
    scale_factor = HD ** (-0.5)
    grad_query = (
        jnp.einsum("bgrt,btd->brgd", grad_scores, key_all, preferred_element_type=F32)
        * scale_factor
    )
    grad_key_all = (
        jnp.einsum("bgrt,brgd->btd", grad_scores, query_bf, preferred_element_type=F32)
        * scale_factor
    )
    grad_value_all = jnp.einsum(
        "bgrt,brgd->btd", prob_full.astype(BF16), grad_heads, preferred_element_type=F32
    )
    grad_kv = scatter_kv(jnp.concatenate([grad_key_all, grad_value_all], axis=2).astype(BF16))
    if shared_kv:
        total = lax.psum(grad_kv, "section")
        grad_kv = jnp.where(lax.axis_index("section") == 0, total, jnp.zeros_like(total))
    _, embedding_pull = jax.vjp(
        partial(embed, cos_table=cos_table, sine_table=sine_table), q_pre, k_pre, q_scale, k_scale
    )
    grad_q_pre, grad_k_pre, grad_q_scale, grad_k_scale = embedding_pull(
        (grad_query, grad_kv[:, :, :HD].astype(F32))
    )
    qkv_grad = jnp.concatenate(
        [
            grad_q_pre.astype(BF16).reshape(trees, row_count, -1),
            grad_k_pre.astype(BF16),
            grad_kv[:, :, HD:],
        ],
        axis=2,
    ).reshape(trees * row_count, -1)
    attn_partial = dot_inner(qkv_grad, w_qkv).astype(BF16).reshape(trees, row_count, depth)
    gathers = ["tensor"] if is_first else ["tensor", "dp"]
    incoming_own, grad_attn_scale, *gathered = meet(
        attn_partial, [own_in, attn_scale[None], grad_middle],
        norm_back_body, own_outs, "tensor", gathers, 6 if is_first else 7, 40,
    )
    products = (
        (normed, qkv_grad),
        (grad_attn, attended_bf),
        (gate_bf, mlp_in),
        (up_bf, mlp_in),
        (hidden_bf, grad_mlp),
    )
    gain_grads = jnp.concatenate(
        [grad_attn_scale[0], grad_mlp_scale[0], grad_q_scale, grad_k_scale]
    )
    return (gathered, incoming_own.astype(BF16).astype(F32), products, gain_grads)


def swap_cores(mine, other):
    core = lax.axis_index("section")
    arrived = lax.ppermute(other, "section", [(0, 1), (1, 0)])
    return (jnp.where(core == 0, mine, arrived), jnp.where(core == 0, arrived, mine))


def on_device(
    inputs, cotangent, seg_ids, parents, order, attn_gain, w_query, w_key, w_value, w_out,
    q_gain, k_gain, mlp_gain, w_gate, w_up, w_down,
):
    core = lax.axis_index("section")
    data_index = lax.axis_index("dp")
    tensor_index = lax.axis_index("tensor")
    dp_size = lax.axis_size("dp")
    tensor_size = lax.axis_size("tensor")
    trees, row_count, depth = inputs.shape
    own_rows = row_count // tensor_size
    row_start = data_index * row_count
    own_depth = w_query.shape[1]
    q_width = w_query.shape[2] // 2
    shared_kv = w_key.shape[2] == HD
    k_width = HD if shared_kv else w_key.shape[2] // 2
    own_units = w_gate.shape[2]
    share = own_units // (2 * dp_size)

    def pick(stacked, index):
        return lax.dynamic_index_in_dim(stacked, index, 0, keepdims=False)

    gains_own = jnp.concatenate([attn_gain[0], mlp_gain[0], q_gain[0], k_gain[0]])
    gains_all = lax.all_gather(gains_own, ("section", "dp")).astype(F32)
    gains_all = gains_all.reshape(2, dp_size, -1)
    gains = [
        (
            gains_all[layer, :, :own_depth].reshape(depth),
            gains_all[layer, :, own_depth : 2 * own_depth].reshape(depth),
            gains_all[layer, 0, 2 * own_depth : 2 * own_depth + HD],
            gains_all[layer, 0, 2 * own_depth + HD :],
        )
        for layer in range(2)
    ]

    def halves(width, array):
        return [array[:, :width], array[:, array.shape[1] - width :]]

    attn_halves = jnp.stack(
        [
            jnp.concatenate(parts, axis=1)
            for parts in zip(
                halves(q_width, w_query[0]),
                halves(k_width, w_key[0]),
                halves(k_width, w_value[0]),
                halves(q_width, w_out[0].T),
            )
        ]
    )
    attn_shards = swap_cores(pick(attn_halves, core), pick(attn_halves, 1 - core))
    unit_blocks = jnp.stack([w_gate[0].T, w_up[0].T, w_down[0]]).reshape(
        3, 2, dp_size, share, own_depth
    )
    unit_blocks = unit_blocks.transpose(1, 2, 0, 3, 4)
    unit_shards = swap_cores(pick(unit_blocks, core), pick(unit_blocks, 1 - core))

    qkv_width = q_width + 2 * k_width
    weights = []
    for layer in range(2):
        attn_all = lax.all_gather(attn_shards[layer], "dp", axis=0, tiled=True)
        pieces = exchange(unit_shards[layer], "dp")
        pieces = pieces.transpose(1, 2, 0, 3).reshape(3, share, depth)
        mats = [lax.all_gather(pieces[i], "tensor", axis=0, tiled=True) for i in range(3)]
        weights.append((attn_all[:, :qkv_width], attn_all[:, qkv_width:], *mats))

    def slot_setup(slot_index):
        tree_id = pick(order, slot_index)
        allowed, row_positions = path_mask(
            pick(seg_ids, tree_id), pick(parents, tree_id), row_start, row_count
        )
        cos_table, sine_table = rope_tables(row_positions, HD)
        return (pick(inputs, tree_id), allowed, cos_table[:, 0], sine_table[:, 0])

    setups = [slot_setup(i) for i in range(trees)]
    hidden, *slot = (jnp.stack(item) for item in zip(*setups))

    def own_part(whole):
        return lax.dynamic_slice_in_dim(
            pick(whole, core), tensor_index * own_rows, own_rows, 0
        )

    own_in = own_part(hidden).astype(F32)
    outputs, kept = [], []
    for layer in range(2):
        hidden, own_in, stored = layer_forward(hidden, own_in, weights[layer], gains[layer], slot)
        outputs.append(hidden)
        kept.append(stored)

    grad_own = own_part(cotangent).astype(F32)
    (grad_mlp,) = meet(None, [grad_own], pass_body, [], None, ["dp"], 8, 30)
    grads, weight_grads, gain_grads = [None, None], [None, None], [None, None]
    for layer in (1, 0):
        gathered, grad_own, products, gain_grads[layer] = layer_backward(
            grad_own, grad_mlp.reshape(-1, depth), kept[layer], weights[layer], gains[layer], slot,
            shared_kv, layer == 0,
        )
        grads[layer], grad_mlp = gathered[0], gathered[-1]
        whole = [dot_outer(left, right).astype(BF16) for left, right in products]
        attn_grad = lax.psum_scatter(
            jnp.concatenate(whole[:2], axis=1), "dp", scatter_dimension=0, tiled=True
        )
        unit_grad = [
            lax.psum_scatter(item, "tensor", scatter_dimension=0, tiled=True) for item in whole[2:]
        ]
        pieces = jnp.stack(unit_grad).reshape(3, share, dp_size, own_depth).transpose(2, 0, 1, 3)
        weight_grads[layer] = (attn_grad, exchange(pieces, "dp"))

    def bring_home(first, second):
        mine, other = jnp.where(core == 0, first, second), jnp.where(core == 0, second, first)
        arrived = lax.ppermute(other, "section", [(0, 1), (1, 0)])
        return (jnp.where(core == 0, mine, arrived), jnp.where(core == 0, arrived, mine))

    attn_home = bring_home(weight_grads[0][0], weight_grads[1][0])
    unit_home = jnp.stack(bring_home(weight_grads[0][1], weight_grads[1][1]))
    unit_home = unit_home.transpose(2, 0, 1, 3, 4).reshape(3, own_units, own_depth)

    def joined(start, width):
        parts = [half[:, start : start + width] for half in attn_home]
        if shared_kv and start in (q_width, q_width + k_width):
            return parts[0].astype(F32)
        return jnp.concatenate(parts, axis=1).astype(F32)

    gain_total = lax.psum(jnp.stack(gain_grads), ("section", "dp", "tensor"))
    gain_own = pick(gain_total, core)
    share_width = attn_gain.shape[1]
    attn_gain_grad = lax.dynamic_slice_in_dim(gain_own, data_index * share_width, share_width, 0)
    mlp_gain_grad = lax.dynamic_slice_in_dim(
        gain_own, depth + data_index * share_width, share_width, 0
    )
    return (
        jnp.where(core == 0, outputs[0], outputs[1])[None],
        jnp.where(core == 0, grads[0], grads[1])[None],
        attn_gain_grad[None],
        joined(0, q_width)[None],
        joined(q_width, k_width)[None],
        joined(q_width + k_width, k_width)[None],
        joined(qkv_width, q_width).T[None],
        gain_own[2 * depth : 2 * depth + HD][None],
        gain_own[2 * depth + HD :][None],
        mlp_gain_grad[None],
        unit_home[0].T.astype(F32)[None],
        unit_home[1].T.astype(F32)[None],
        unit_home[2].astype(F32)[None],
    )


def solution(mesh):
    rows = P(None, "dp", None)
    wide = P("section", "dp", "tensor")
    tall = P("section", "tensor", "dp")
    gain = P("section", "dp")
    head_gain = P("section", None)
    slots = P("section", None, "dp", None)
    in_specs = (
        rows, rows, P(), P(), P(), gain, wide, wide, wide, tall, head_gain, head_gain, gain,
        wide, wide, tall,
    )
    out_specs = (
        slots, slots, gain, wide, wide, wide, tall, head_gain, head_gain, gain, wide, wide, tall,
    )
    return jax.shard_map(
        on_device, mesh=mesh, in_specs=in_specs, out_specs=out_specs, check_vma=False
    )
```

```python
from functools import partial

import jax
import jax.numpy as jnp
from jax import lax
from jax.experimental import pallas as pl
from jax.experimental.pallas import tpu as pltpu
from jax.sharding import PartitionSpec as P

HD = 128
TRUNK = 512
BRANCH = 96
NB = 4
TREE = 1152
SEGS = 9


EPSILON = 1e-06
THETA = 1000000.0
MASKED = -1e30
F32 = jnp.float32
BF16 = jnp.bfloat16


def rms_scale(values, weight_gain):
    mean_sq = jnp.mean(values * values, axis=-1, keepdims=True)
    return values * lax.rsqrt(mean_sq + EPSILON) * weight_gain


def rotate(values, cos_table, sine_table):
    middle_at = values.shape[-1] // 2
    leading = values[..., :middle_at]
    trailing = values[..., middle_at:]
    return jnp.concatenate(
        [leading * cos_table - trailing * sine_table, trailing * cos_table + leading * sine_table],
        axis=-1,
    )


def rope_tables(positions, head_dim):
    half_steps = jnp.arange(head_dim // 2, dtype=F32)
    inverse = THETA ** (-2.0 * half_steps / head_dim)
    angles = positions.astype(F32)[:, None] * inverse[None, :]
    return (jnp.cos(angles)[:, None, :], jnp.sin(angles)[:, None, :])


def swiglu(gate_in, up_in):
    return jax.nn.silu(gate_in) * up_in


def embed_heads(q_pre, k_pre, q_scale, k_scale, cos_table, sine_table):
    row_count = q_pre.shape[0]
    queries = rms_scale(q_pre.reshape(row_count, -1, HD), q_scale)
    keys_part = rms_scale(k_pre.reshape(row_count, -1, HD), k_scale)
    return (rotate(queries, cos_table, sine_table), rotate(keys_part, cos_table, sine_table))


def tree_layout(seg_row, parent_row):
    labels = jnp.arange(SEGS, dtype=jnp.int32)
    places = jnp.arange(TREE, dtype=jnp.int32)
    member = seg_row[None, :] == labels[:, None]
    starts = jnp.min(jnp.where(member, places[None, :], TREE), axis=1)
    depth_base = jnp.where(labels == 0, 0, jnp.where(labels <= NB, TRUNK, TRUNK + BRANCH))
    shifts = depth_base - starts
    positions = places + jnp.sum(jnp.where(member, shifts[:, None], 0), axis=0)
    grandparent = jnp.sum(
        jnp.where(parent_row[:, None] == labels[None, :], parent_row[None, :], 0), axis=1
    )
    ancestor = (
        (labels[None, :] == labels[:, None])
        | (labels[None, :] == parent_row[:, None])
        | (labels[None, :] == grandparent[:, None])
    )
    return (positions, member.astype(F32), ancestor.astype(F32))


def path_mask(seg_row, parent_row, row_start, row_count):
    positions, member, ancestor = tree_layout(seg_row, parent_row)
    member_rows = lax.dynamic_slice_in_dim(member, row_start, row_count, 1)
    seg_rows = lax.dynamic_slice_in_dim(seg_row, row_start, row_count, 0)
    reach_table = jnp.dot(jnp.dot(member_rows.T, ancestor), member)
    places = jnp.arange(TREE, dtype=jnp.int32)
    row_places = row_start + jnp.arange(row_count, dtype=jnp.int32)
    same_seg = seg_rows[:, None] == seg_row[None, :]
    causal = places[None, :] <= row_places[:, None]
    allowed = (reach_table > 0.5) & (jnp.logical_not(same_seg) | causal)
    row_positions = lax.dynamic_slice_in_dim(positions, row_start, row_count, 0)
    return (allowed, row_positions)


OUTER = (((0,), (0,)), ((), ()))
INNER = (((1,), (1,)), ((), ()))


def dot(left, right):
    return jnp.dot(left, right, preferred_element_type=F32)


def dot_inner(left, right):
    return lax.dot_general(left, right, INNER, preferred_element_type=F32)


def dot_outer(left, right):
    return lax.dot_general(left, right, OUTER, preferred_element_type=F32)


def exchange(pieces, axis):
    size = lax.axis_size(axis)
    me = lax.axis_index(axis)
    got = jnp.zeros_like(pieces)
    own = lax.dynamic_index_in_dim(pieces, me, 0, keepdims=True)
    got = lax.dynamic_update_slice_in_dim(got, own, me, 0)
    for step in range(1, size):
        other = me ^ step
        piece = lax.dynamic_index_in_dim(pieces, other, 0, keepdims=True)
        arrived = lax.ppermute(piece, axis, [(i, i ^ step) for i in range(size)])
        got = lax.dynamic_update_slice_in_dim(got, arrived, other, 0)
    return got


def gather_by_permutes(own, axis):
    size = lax.axis_size(axis)
    me = lax.axis_index(axis)
    got = lax.dynamic_update_slice_in_dim(
        jnp.zeros((size,) + own.shape, own.dtype), own[None], me, 0
    )
    for step in range(1, size):
        arrived = lax.ppermute(own, axis, [(i, i ^ step) for i in range(size)])
        got = lax.dynamic_update_slice_in_dim(got, arrived[None], me ^ step, 0)
    return got


def scatter_by_permutes(pieces, axis):
    size = lax.axis_size(axis)
    me = lax.axis_index(axis)
    total = lax.dynamic_index_in_dim(pieces, me, 0, keepdims=False).astype(F32)
    for step in range(1, size):
        piece = lax.dynamic_index_in_dim(pieces, me ^ step, 0, keepdims=False)
        total += lax.ppermute(piece, axis, [(i, i ^ step) for i in range(size)]).astype(F32)
    return total.astype(BF16)


def masked_scores(query_bf, key_all, allowed):
    raw_scores = jnp.einsum(
        "brgd,btd->bgrt", query_bf, key_all, preferred_element_type=F32
    ) * HD ** (-0.5)
    return jnp.where(allowed[:, None], raw_scores, MASKED)


MESH = pl.DeviceIdType.MESH
CHUNK = 256


def greet(axes):
    barrier = pltpu.get_barrier_semaphore()
    count = 0
    for axis in axes:
        size = lax.axis_size(axis)
        me = lax.axis_index(axis)
        for step in range(1, size):
            pl.semaphore_signal(
                barrier, inc=1, device_id={axis: lax.rem(me + step, size)}, device_id_type=MESH
            )
        count += size - 1
    pl.semaphore_wait(barrier, count)


def remote(src, dst, send_sem, recv_sem, device_id):
    return pltpu.make_async_remote_copy(
        src_ref=src, dst_ref=dst, send_sem=send_sem, recv_sem=recv_sem,
        device_id=device_id, device_id_type=MESH,
    )


def kernel_call(kernel, out_shape, scratch, collective_id, cost_us, *args):
    in_vmem = pl.BlockSpec(memory_space=pltpu.VMEM)
    return pl.pallas_call(
        kernel,
        out_shape=out_shape,
        in_specs=[in_vmem] * len(args),
        out_specs=jax.tree.map(lambda _: in_vmem, out_shape),
        scratch_shapes=scratch,
        cost_estimate=pl.CostEstimate(flops=0, bytes_accessed=cost_us * 3_000_000, transcendentals=0),
        compiler_params=pltpu.CompilerParams(
            collective_id=collective_id, has_side_effects=True, vmem_limit_bytes=40 << 20
        ),
    )(*args)


def hub(partial_sums, own_args, body, own_outs, scatter, gathers, collective_id, cost_us):
    trees = 2
    rows, depth = own_args[0].shape
    half = depth // 2
    scatter_size = lax.axis_size(scatter) if scatter else 1
    sizes = [lax.axis_size(axis) for axis in gathers]
    n_args = len(own_args) + (1 if scatter else 0)
    n_outs = len(own_outs) + len(gathers)

    def kernel(*refs):
        args, outs, scratch = refs[:n_args], refs[n_args : n_args + n_outs], refs[n_args + n_outs :]
        own_out_refs, gathered = outs[: len(own_outs)], outs[len(own_outs) :]
        core = lax.axis_index("section")
        sibling = 1 - core
        axes = ["section"] + sorted(set(gathers) | ({scatter} if scatter else set()))

        if scatter:
            terms = args[0]
            args = args[1:]
            to_sib, from_sib, to_peer, from_peer, total_ref = scratch[:5]
            sib_send, sib_recv, peer_send, peer_recv = scratch[5:9]
            scratch = scratch[9:]
            me = lax.axis_index(scatter)

            def packed(tree, place, at):
                low = rows * place // 16 * 16
                high = -(-rows * (place + 1) // 16) * 16
                skip = rows * place - low
                parts = [
                    terms[tree, low:high, pl.ds(side * half + at, CHUNK)].astype(F32)[
                        skip : skip + rows
                    ]
                    for side in range(2)
                ]
                return jnp.concatenate(parts, axis=0)

            def columns(step):
                return pl.multiple_of(step * CHUNK, CHUNK)

            for place in range(scatter_size):
                @pl.loop(0, half // CHUNK)
                def _(step):
                    at = columns(step)
                    to_sib[place, :, pl.ds(at, CHUNK)] = packed(sibling, place, at).astype(BF16)

            greet(axes)
            to_sibling = [
                remote(
                    to_sib.at[place], from_sib.at[place], sib_send.at[place], sib_recv.at[place],
                    {"section": sibling},
                )
                for place in range(scatter_size)
            ]
            for copy in to_sibling:
                copy.start()

            def peer_copy(place, slot):
                return remote(
                    to_peer.at[place], from_peer.at[slot], peer_send.at[place],
                    peer_recv.at[slot], {scatter: place},
                )

            for place in range(scatter_size):
                to_sibling[place].wait_recv()

                @pl.loop(0, half // CHUNK)
                def _(step):
                    at = columns(step)
                    both = packed(core, place, at) + from_sib[place, :, pl.ds(at, CHUNK)].astype(F32)
                    to_peer[place, :, pl.ds(at, CHUNK)] = both.astype(BF16)

                    @pl.when(place == me)
                    def _():
                        total_ref[:, pl.ds(at, CHUNK)] = both

                @pl.when(place != me)
                def _():
                    peer_copy(place, me).start()

            for place in range(scatter_size):
                @pl.when(place != me)
                def _():
                    peer_copy(place, place).wait_recv()
                    total_ref[...] += from_peer[place].astype(F32)

            total = total_ref[...]
            total = jnp.concatenate([total[:rows], total[rows:]], axis=1)
        else:
            greet(axes)
            total = None

        result = body(total, args, own_out_refs)
        piece = jnp.concatenate([result[:, :half], result[:, half:]], axis=0).astype(BF16)
        gather_state = []
        for index, axis in enumerate(gathers):
            board, send, recv, relay_send, relay_recv = scratch[5 * index : 5 * index + 5]
            me_there = lax.axis_index(axis)
            board[core, me_there] = piece

            def spread(place, slot, board=board, send=send, recv=recv, axis=axis):
                return remote(
                    board.at[core, slot], board.at[core, slot], send.at[place], recv.at[slot],
                    {axis: place},
                )

            def relay(tree, slot, board=board, send=relay_send, recv=relay_recv):
                return remote(
                    board.at[tree, slot], board.at[tree, slot], send.at[slot], recv.at[slot],
                    {"section": sibling},
                )

            for place in range(sizes[index]):
                @pl.when(place != me_there)
                def _():
                    spread(place, me_there).start()

            relay(core, me_there).start()
            gather_state.append((board, me_there, spread, relay))

        def unpack(out, board, tree, size):
            @pl.loop(0, half // CHUNK)
            def _(step):
                at = pl.multiple_of(step * CHUNK, CHUNK)
                blocks = [board[tree, place, :, pl.ds(at, CHUNK)].astype(F32) for place in range(size)]
                for side in range(2):
                    whole = jnp.concatenate(
                        [block[side * rows : (side + 1) * rows] for block in blocks], axis=0
                    )
                    out[tree, :, pl.ds(side * half + at, CHUNK)] = whole.astype(BF16)

        for (board, me_there, spread, relay), size in zip(gather_state, sizes):
            for place in range(size):
                @pl.when(place != me_there)
                def _():
                    spread(place, place).wait_recv()
                    relay(core, place).start()

        for (board, me_there, spread, relay), size, out in zip(gather_state, sizes, gathered):
            unpack(out, board, core, size)

        for (board, me_there, spread, relay), size, out in zip(gather_state, sizes, gathered):
            for place in range(size):
                relay(sibling, place).wait_recv()
            unpack(out, board, sibling, size)

        if scatter:
            for place in range(scatter_size):
                to_sibling[place].wait_send()

                @pl.when(place != me)
                def _():
                    peer_copy(place, me).wait_send()

        for (board, me_there, spread, relay), size in zip(gather_state, sizes):
            for place in range(size):
                relay(core, place).wait_send()

                @pl.when(place != me_there)
                def _():
                    spread(place, me_there).wait_send()

    sem = pltpu.SemaphoreType.DMA
    scratch = []
    if scatter:
        boxes = pltpu.VMEM((scatter_size, 2 * rows, half), BF16)
        scratch += [boxes] * 4 + [pltpu.VMEM((2 * rows, half), F32)] + [sem((scatter_size,))] * 4
    for size in sizes:
        scratch += [pltpu.VMEM((trees, size, 2 * rows, half), BF16)] + [sem((size,))] * 4
    out_shape = [jax.ShapeDtypeStruct(shape, F32) for shape in own_outs] + [
        jax.ShapeDtypeStruct((trees, size * rows, depth), BF16) for size in sizes
    ]
    ins = ([partial_sums] if scatter else []) + list(own_args)
    return kernel_call(kernel, out_shape, scratch, collective_id, cost_us, *ins)


def hub_plain(partial_sums, own_args, body, own_outs, scatter, gathers):
    total = None
    if scatter:
        mine = lax.psum_scatter(partial_sums, "section", scatter_dimension=0, tiled=True)
        mine = lax.psum_scatter(mine, scatter, scatter_dimension=1, tiled=True)[0]
        total = mine.astype(F32)

    class Cell:
        def __setitem__(self, _, value):
            self.value = value

    cells = [Cell() for _ in own_outs]
    result = body(total, own_args, cells).astype(BF16)
    gathered = [
        lax.all_gather(lax.all_gather(result, axis, axis=0, tiled=True), "section", axis=0)
        for axis in gathers
    ]
    return [cell.value for cell in cells] + gathered


class LineGather:
    def __init__(self, own, block, send, recv, chunks):
        self.own, self.block, self.send, self.recv, self.chunks = own, block, send, recv, chunks
        self.me = lax.axis_index("dp")
        self.size = lax.axis_size("dp")

    def direct(self, place):
        if self.size != 4:
            return place != self.me
        return (place != self.me) & (place + self.me != 3) | ((self.me == 3 - place) & (place % 3 != 0))

    def copy(self, place, slot, chunk):
        return remote(
            self.own(chunk), self.block(slot, chunk),
            self.send.at[place, chunk], self.recv.at[slot, chunk], {"dp": place},
        )

    def passed(self, place, slot, chunk):
        return remote(
            self.block(slot, chunk), self.block(slot, chunk),
            self.send.at[self.me, chunk], self.recv.at[slot, chunk], {"dp": place},
        )

    def start(self, chunk):
        for place in range(self.size):
            @pl.when(self.direct(place))
            def _():
                self.copy(place, self.me, chunk).start()

    def relays(self):
        return [(2, 0, 3), (1, 3, 0)] if self.size == 4 else []

    def arrive(self, place, chunk):
        @pl.when(place != self.me)
        def _():
            self.copy(place, place, chunk).wait_recv()

        for via, source, target in self.relays():
            if source == place:
                @pl.when(self.me == via)
                def _():
                    self.passed(target, source, chunk).start()

    def finish(self):
        for chunk in range(self.chunks):
            for place in range(self.size):
                @pl.when(self.direct(place))
                def _():
                    self.copy(place, self.me, chunk).wait_send()
            for via, source, target in self.relays():
                @pl.when(self.me == via)
                def _():
                    self.passed(target, source, chunk).wait_send()


def line_order(size):
    return [1, 2, 0, 3] if size == 4 else list(range(size))


def gather_kv(own):
    trees, rows, width = own.shape
    if rows % 16:
        return lax.all_gather(own, "dp", axis=1, tiled=True)
    size = lax.axis_size("dp")

    def kernel(own_ref, out_ref, send, recv):
        greet(["dp"])
        line = LineGather(
            lambda chunk: own_ref.at[chunk], lambda slot, chunk: out_ref.at[chunk, slot],
            send, recv, trees,
        )
        for chunk in range(trees):
            line.start(chunk)
        out_ref[:, line.me] = own_ref[...]
        for chunk in range(trees):
            for place in line_order(size):
                line.arrive(place, chunk)
        line.finish()

    shape = jax.ShapeDtypeStruct((trees, size, rows, width), BF16)
    sem = pltpu.SemaphoreType.DMA
    whole = kernel_call(kernel, shape, [sem((size, trees))] * 2, 1, 30, own)
    return whole.reshape(trees, size * rows, width)


def gather_shards(own):
    rows, width = own.shape
    chunks = 4
    size = lax.axis_size("dp")
    if rows % (16 * chunks):
        return lax.all_gather(own, "dp", axis=0, tiled=True)

    def kernel(own_ref, out_ref, keep, send, recv):
        greet(["dp"])
        line = LineGather(
            lambda chunk: own_ref.at[chunk], lambda slot, chunk: out_ref.at[slot, chunk],
            send, recv, chunks,
        )
        for chunk in range(chunks):
            line.start(chunk)
        local = pltpu.make_async_copy(own_ref, out_ref.at[line.me], keep)
        local.start()
        for chunk in range(chunks):
            for place in line_order(size):
                line.arrive(place, chunk)
        local.wait()
        line.finish()

    sem = pltpu.SemaphoreType.DMA
    hbm = pl.BlockSpec(memory_space=pl.ANY)
    whole = pl.pallas_call(
        kernel,
        out_shape=jax.ShapeDtypeStruct((size, chunks, rows // chunks, width), BF16),
        in_specs=[hbm],
        out_specs=hbm,
        scratch_shapes=[sem, sem((size, chunks)), sem((size, chunks))],
        cost_estimate=pl.CostEstimate(flops=0, bytes_accessed=200_000_000, transcendentals=0),
        compiler_params=pltpu.CompilerParams(collective_id=9, has_side_effects=True),
    )(own.reshape(chunks, rows // chunks, width))
    return whole.reshape(size * rows, width)


def exchange_shards(pieces):
    size, rows, width = pieces.shape
    if rows % 16 or width % 128:
        return exchange(pieces, "dp").transpose(1, 0, 2).reshape(rows, -1)

    def kernel(in_ref, out_ref, keep, send, recv):
        me = lax.axis_index("dp")
        greet(["dp"])

        def lands(slot):
            return out_ref.at[:, pl.ds(pl.multiple_of(slot * width, width), width)]

        def spread(place, slot):
            return remote(
                in_ref.at[place], lands(slot), send.at[place], recv.at[slot], {"dp": place}
            )

        for place in range(size):
            @pl.when(place != me)
            def _():
                spread(place, me).start()

        local = pltpu.make_async_copy(in_ref.at[me], lands(me), keep)
        local.start()
        for place in range(size):
            @pl.when(place != me)
            def _():
                spread(place, place).wait_recv()
                spread(place, me).wait_send()

        local.wait()

    sem = pltpu.SemaphoreType.DMA
    hbm = pl.BlockSpec(memory_space=pl.ANY)
    return pl.pallas_call(
        kernel,
        out_shape=jax.ShapeDtypeStruct((rows, size * width), BF16),
        in_specs=[hbm],
        out_specs=hbm,
        scratch_shapes=[sem, sem((size,)), sem((size,))],
        cost_estimate=pl.CostEstimate(flops=0, bytes_accessed=70_000_000, transcendentals=0),
        compiler_params=pltpu.CompilerParams(collective_id=10, has_side_effects=True),
    )(pieces)


def scatter_kv(whole):
    trees, all_rows, width = whole.shape
    size = lax.axis_size("dp")
    rows = all_rows // size
    if rows % 16:
        return lax.psum_scatter(whole, "dp", scatter_dimension=1, tiled=True)
    relays = [(0, 1, 3), (3, 2, 0)] if size == 4 else []

    def kernel(in_ref, out_ref, boxes, joint, send, recv, join_send, join_recv):
        me = lax.axis_index("dp")
        greet(["dp"])

        def spread(place, slot, chunk):
            return remote(
                in_ref.at[chunk, place], boxes.at[slot, chunk], send.at[place, chunk],
                recv.at[slot, chunk], {"dp": place},
            )

        def by_way(via, target, chunk):
            return remote(
                in_ref.at[chunk, target], joint.at[chunk], join_send.at[chunk],
                join_recv.at[chunk], {"dp": via},
            )

        def joined(via, target, chunk):
            return remote(
                joint.at[chunk], boxes.at[via, chunk], send.at[target, chunk],
                recv.at[via, chunk], {"dp": target},
            )

        def plain(place):
            ok = place != me
            for source, via, target in relays:
                if place == target:
                    ok = ok & (me != source) & (me != via)
            return ok

        def expected(place):
            ok = place != me
            for source, via, target in relays:
                if place == source:
                    ok = ok & (me != target)
            return ok

        for chunk in range(trees):
            for source, via, target in relays:
                @pl.when(me == source)
                def _():
                    by_way(via, target, chunk).start()

            for place in range(size):
                @pl.when(plain(place))
                def _():
                    spread(place, me, chunk).start()

        for chunk in range(trees):
            for source, via, target in relays:
                @pl.when(me == via)
                def _():
                    by_way(via, target, chunk).wait_recv()
                    both = joint[chunk].astype(F32) + in_ref[chunk, target].astype(F32)
                    joint[chunk] = both.astype(BF16)
                    joined(via, target, chunk).start()

        for chunk in range(trees):
            out_ref[chunk] = in_ref[chunk, me].astype(F32)
            for place in range(size):
                @pl.when(expected(place))
                def _():
                    spread(place, place, chunk).wait_recv()
                    out_ref[chunk] += boxes[place, chunk].astype(F32)

        for chunk in range(trees):
            for place in range(size):
                @pl.when(plain(place))
                def _():
                    spread(place, me, chunk).wait_send()

            for source, via, target in relays:
                @pl.when(me == source)
                def _():
                    by_way(via, target, chunk).wait_send()

                @pl.when(me == via)
                def _():
                    joined(via, target, chunk).wait_send()

    shape = jax.ShapeDtypeStruct((trees, rows, width), F32)
    sem = pltpu.SemaphoreType.DMA
    box = pltpu.VMEM((size, trees, rows, width), BF16)
    scratch = [box, pltpu.VMEM((trees, rows, width), BF16), sem((size, trees)), sem((size, trees))]
    scratch += [sem((trees,)), sem((trees,))]
    return kernel_call(
        kernel, shape, scratch, 2, 30, whole.reshape(trees, size, rows, width)
    )


def total_over_all(own):
    axes = ["section", "tensor", "dp"]
    sizes = [lax.axis_size(axis) for axis in axes]

    def kernel(own_ref, out_ref, *scratch):
        boxes, sends, recvs = scratch[:3], scratch[3:6], scratch[6:9]
        greet(axes)
        out_ref[...] = own_ref[...]
        for axis, size, box, send, recv in zip(axes, sizes, boxes, sends, recvs):
            me = lax.axis_index(axis)
            box[me] = out_ref[...]

            def spread(place, slot):
                return remote(box.at[me], box.at[slot], send.at[place], recv.at[slot], {axis: place})

            for place in range(size):
                @pl.when(place != me)
                def _():
                    spread(place, me).start()

            for place in range(size):
                @pl.when(place != me)
                def _():
                    spread(place, place).wait_recv()
                    spread(place, me).wait_send()

            total = box[0]
            for place in range(1, size):
                total += box[place]
            out_ref[...] = total

    sem = pltpu.SemaphoreType.DMA
    scratch = [pltpu.VMEM((size,) + own.shape, F32) for size in sizes]
    scratch += [sem((size,)) for size in sizes] * 2
    return kernel_call(kernel, jax.ShapeDtypeStruct(own.shape, F32), scratch, 11, 12, own)


def meet(partial_sums, own_args, body, own_outs, scatter, gathers, collective_id, cost_us):
    rows, depth = own_args[0].shape
    if rows % 8 or depth % (2 * CHUNK):
        return hub_plain(partial_sums, own_args, body, own_outs, scatter, gathers)
    return hub(partial_sums, own_args, body, own_outs, scatter, gathers, collective_id, cost_us)


def norm_body(total, args, outs):
    middle = args[0][...] + total
    outs[0][...] = middle
    mean_sq = jnp.mean(middle * middle, axis=1, keepdims=True)
    return middle * lax.rsqrt(mean_sq + EPSILON) * args[1][...]


def add_body(total, args, outs):
    result = args[0][...] + total
    outs[0][...] = result
    return result


def norm_back_body(total, args, outs):
    values, gain = args[0][...], args[1][...]
    scale = lax.rsqrt(jnp.mean(values * values, axis=1, keepdims=True) + EPSILON)
    unit = values * scale
    outs[1][...] = jnp.sum(total * unit, axis=0, keepdims=True)
    scaled = total * gain
    along = jnp.mean(scaled * unit, axis=1, keepdims=True)
    result = (scaled - unit * along) * scale + args[2][...]
    outs[0][...] = result
    return result


def pass_body(total, args, outs):
    return args[0][...]


def embed(q_pre, k_pre, q_scale, k_scale, cos_table, sine_table):
    queries = rms_scale(q_pre, q_scale)
    keys = rms_scale(k_pre, k_scale)
    return (
        rotate(queries, cos_table[:, :, None], sine_table[:, :, None]),
        rotate(keys, cos_table, sine_table),
    )


def layer_forward(hidden_in, own_in, weights, gains, slot):
    attn_scale, mlp_scale, q_scale, k_scale = gains
    w_qkv, w_outt, w_gate, w_up, w_down = weights
    allowed, cos_table, sine_table = slot
    trees, row_count, depth = hidden_in.shape
    q_width = w_outt.shape[1]
    normed = rms_scale(hidden_in.astype(F32), attn_scale).astype(BF16).reshape(-1, depth)
    qkv = dot(normed, w_qkv).reshape(trees, row_count, -1)
    q_pre = qkv[:, :, :q_width].reshape(trees, row_count, -1, HD)
    k_pre = qkv[:, :, q_width : q_width + HD]
    value_bf = qkv[:, :, q_width + HD :].astype(BF16)
    queries, keys_rot = embed(q_pre, k_pre, q_scale, k_scale, cos_table, sine_table)
    query_bf = queries.astype(BF16)
    kv_all = gather_kv(jnp.concatenate([keys_rot.astype(BF16), value_bf], axis=2))
    key_all = kv_all[:, :, :HD]
    value_all = kv_all[:, :, HD:]
    scores = masked_scores(query_bf, key_all, allowed)
    row_max = jnp.max(scores, axis=-1, keepdims=True)
    exp_scores = jnp.exp(scores - row_max)
    row_total = jnp.sum(exp_scores, axis=-1, keepdims=True)
    prob_bf = (exp_scores / row_total).astype(BF16)
    log_total = row_max + jnp.log(row_total)
    attended = jnp.einsum("bgrt,btd->brgd", prob_bf, value_all, preferred_element_type=F32)
    attended_bf = attended.reshape(trees * row_count, -1).astype(BF16)
    attn_partial = dot_inner(attended_bf, w_outt).astype(BF16).reshape(trees, row_count, depth)
    own_shape = own_in.shape
    middle, mlp_in = meet(
        attn_partial, [own_in, mlp_scale[None]], norm_body, [own_shape], "tensor", ["dp"], 3, 50
    )
    mlp_in = mlp_in.reshape(-1, depth)
    gate_pre = dot_inner(mlp_in, w_gate)
    upward = dot_inner(mlp_in, w_up)
    hidden_bf = swiglu(gate_pre, upward).astype(BF16)
    mlp_partial = dot(hidden_bf, w_down).astype(BF16).reshape(trees, -1, depth)
    output_own, output_bf = meet(
        mlp_partial, [middle], add_body, [own_shape], "dp", ["tensor"], 4, 50
    )
    stored = (
        own_in, normed, q_pre, k_pre, query_bf, key_all, value_all, log_total, attended_bf,
        middle, mlp_in, gate_pre, upward, hidden_bf,
    )
    return (output_bf, output_own.astype(BF16).astype(F32), stored)


def layer_backward(grad_own, grad_mlp, stored, weights, gains, slot, shared_kv, is_first):
    attn_scale, mlp_scale, q_scale, k_scale = gains
    w_qkv, w_outt, w_gate, w_up, w_down = weights
    allowed, cos_table, sine_table = slot
    (
        own_in, normed, q_pre, k_pre, query_bf, key_all, value_all, log_total, attended_bf,
        middle, mlp_in, gate_pre, upward, hidden_bf,
    ) = stored
    trees, row_count = query_bf.shape[:2]
    depth = normed.shape[1]
    grad_hidden = dot_inner(grad_mlp, w_down)
    _, swiglu_pull = jax.vjp(swiglu, gate_pre, upward)
    grad_gate, grad_upward = swiglu_pull(grad_hidden)
    gate_bf = grad_gate.astype(BF16)
    up_bf = grad_upward.astype(BF16)
    mlp_partial = (dot(gate_bf, w_gate) + dot(up_bf, w_up)).astype(BF16)
    own_outs = [own_in.shape, (1, depth)]
    grad_middle, grad_mlp_scale, grad_attn = meet(
        mlp_partial.reshape(trees, -1, depth),
        [middle, mlp_scale[None], grad_own],
        norm_back_body, own_outs, "dp", ["tensor"], 5, 50,
    )
    grad_attn = grad_attn.reshape(-1, depth)
    grad_heads = dot(grad_attn, w_outt).astype(BF16).reshape(query_bf.shape)
    scores = masked_scores(query_bf, key_all, allowed)
    prob_full = jnp.exp(scores - log_total)
    grad_prob = jnp.einsum("brgd,btd->bgrt", grad_heads, value_all, preferred_element_type=F32)
    row_dot = jnp.sum(prob_full * grad_prob, axis=-1, keepdims=True)
    grad_scores = (prob_full * (grad_prob - row_dot)).astype(BF16)
    scale_factor = HD ** (-0.5)
    grad_query = (
        jnp.einsum("bgrt,btd->brgd", grad_scores, key_all, preferred_element_type=F32)
        * scale_factor
    )
    grad_key_all = (
        jnp.einsum("bgrt,brgd->btd", grad_scores, query_bf, preferred_element_type=F32)
        * scale_factor
    )
    grad_value_all = jnp.einsum(
        "bgrt,brgd->btd", prob_full.astype(BF16), grad_heads, preferred_element_type=F32
    )
    grad_kv = scatter_kv(jnp.concatenate([grad_key_all, grad_value_all], axis=2).astype(BF16))
    grad_kv = grad_kv.astype(BF16)
    if shared_kv:
        total = lax.psum(grad_kv, "section")
        grad_kv = jnp.where(lax.axis_index("section") == 0, total, jnp.zeros_like(total))
    _, embedding_pull = jax.vjp(
        partial(embed, cos_table=cos_table, sine_table=sine_table), q_pre, k_pre, q_scale, k_scale
    )
    grad_q_pre, grad_k_pre, grad_q_scale, grad_k_scale = embedding_pull(
        (grad_query, grad_kv[:, :, :HD].astype(F32))
    )
    qkv_grad = jnp.concatenate(
        [
            grad_q_pre.astype(BF16).reshape(trees, row_count, -1),
            grad_k_pre.astype(BF16),
            grad_kv[:, :, HD:],
        ],
        axis=2,
    ).reshape(trees * row_count, -1)
    attn_partial = dot_inner(qkv_grad, w_qkv).astype(BF16).reshape(trees, row_count, depth)
    gathers = ["tensor"] if is_first else ["tensor", "dp"]
    incoming_own, grad_attn_scale, *gathered = meet(
        attn_partial, [own_in, attn_scale[None], grad_middle],
        norm_back_body, own_outs, "tensor", gathers, 6 if is_first else 7, 40,
    )
    products = (
        (normed, qkv_grad),
        (grad_attn, attended_bf),
        (gate_bf, mlp_in),
        (up_bf, mlp_in),
        (hidden_bf, grad_mlp),
    )
    gain_grads = jnp.concatenate(
        [grad_attn_scale[0], grad_mlp_scale[0], grad_q_scale, grad_k_scale]
    )
    return (gathered, incoming_own.astype(BF16).astype(F32), products, gain_grads)


def swap_cores(mine, other):
    core = lax.axis_index("section")
    arrived = lax.ppermute(other, "section", [(0, 1), (1, 0)])
    return (jnp.where(core == 0, mine, arrived), jnp.where(core == 0, arrived, mine))


def on_device(
    inputs, cotangent, seg_ids, parents, order, attn_gain, w_query, w_key, w_value, w_out,
    q_gain, k_gain, mlp_gain, w_gate, w_up, w_down,
):
    core = lax.axis_index("section")
    data_index = lax.axis_index("dp")
    tensor_index = lax.axis_index("tensor")
    dp_size = lax.axis_size("dp")
    tensor_size = lax.axis_size("tensor")
    trees, row_count, depth = inputs.shape
    own_rows = row_count // tensor_size
    row_start = data_index * row_count
    own_depth = w_query.shape[1]
    q_width = w_query.shape[2] // 2
    shared_kv = w_key.shape[2] == HD
    k_width = HD if shared_kv else w_key.shape[2] // 2
    own_units = w_gate.shape[2]
    share = own_units // (2 * dp_size)

    def pick(stacked, index):
        return lax.dynamic_index_in_dim(stacked, index, 0, keepdims=False)

    gains_own = jnp.concatenate([attn_gain[0], mlp_gain[0], q_gain[0], k_gain[0]])
    gains_all = lax.all_gather(gains_own, ("section", "dp")).astype(F32)
    gains_all = gains_all.reshape(2, dp_size, -1)
    gains = [
        (
            gains_all[layer, :, :own_depth].reshape(depth),
            gains_all[layer, :, own_depth : 2 * own_depth].reshape(depth),
            gains_all[layer, 0, 2 * own_depth : 2 * own_depth + HD],
            gains_all[layer, 0, 2 * own_depth + HD :],
        )
        for layer in range(2)
    ]

    def halves(width, array):
        return [array[:, :width], array[:, array.shape[1] - width :]]

    attn_halves = jnp.stack(
        [
            jnp.concatenate(parts, axis=1)
            for parts in zip(
                halves(q_width, w_query[0]),
                halves(k_width, w_key[0]),
                halves(k_width, w_value[0]),
                halves(q_width, w_out[0].T),
            )
        ]
    )
    attn_shards = swap_cores(pick(attn_halves, core), pick(attn_halves, 1 - core))
    unit_blocks = jnp.stack([w_gate[0].T, w_up[0].T, w_down[0]]).reshape(
        3, 2, dp_size, share, own_depth
    )
    unit_blocks = unit_blocks.transpose(1, 2, 0, 3, 4)
    unit_shards = swap_cores(pick(unit_blocks, core), pick(unit_blocks, 1 - core))

    qkv_width = q_width + 2 * k_width

    def after(first, *then):
        return lax.optimization_barrier((first, *then))[1:]

    def spread_units(rows):
        return gather_by_permutes(rows, "tensor").reshape(-1, depth)

    def exchanged(pieces):
        return exchange(pieces, "dp").transpose(1, 0, 2).reshape(share, depth)

    gate_rows = exchange_shards(unit_shards[0][:, 0])
    (attn_shard,) = after(gate_rows, attn_shards[0])
    attn_all = gather_shards(attn_shard)
    gate_all = spread_units(gate_rows)
    units, attn_shard = after(attn_all, unit_shards[0], attn_shards[1])
    up_all = spread_units(exchanged(units[:, 1]))
    down_all = spread_units(exchanged(units[:, 2]))
    weights = [(attn_all[:, :qkv_width], attn_all[:, qkv_width:], gate_all, up_all, down_all)]
    attn_all = gather_by_permutes(attn_shard, "dp").reshape(depth, -1)
    (units,) = after(attn_all, unit_shards[1])
    weights.append(
        (
            attn_all[:, :qkv_width], attn_all[:, qkv_width:],
            *(spread_units(exchanged(units[:, i])) for i in range(3)),
        )
    )

    def slot_setup(slot_index):
        tree_id = pick(order, slot_index)
        allowed, row_positions = path_mask(
            pick(seg_ids, tree_id), pick(parents, tree_id), row_start, row_count
        )
        cos_table, sine_table = rope_tables(row_positions, HD)
        return (pick(inputs, tree_id), allowed, cos_table[:, 0], sine_table[:, 0])

    setups = [slot_setup(i) for i in range(trees)]
    hidden, *slot = (jnp.stack(item) for item in zip(*setups))

    def own_part(whole):
        return lax.dynamic_slice_in_dim(
            pick(whole, core), tensor_index * own_rows, own_rows, 0
        )

    own_in = own_part(hidden).astype(F32)
    outputs, kept = [], []
    for layer in range(2):
        hidden, own_in, stored = layer_forward(hidden, own_in, weights[layer], gains[layer], slot)
        outputs.append(hidden)
        kept.append(stored)

    grad_own = own_part(cotangent).astype(F32)
    grad_mlp = gather_by_permutes(grad_own.astype(BF16), "dp").reshape(-1, depth)
    grad_mlp = gather_by_permutes(grad_mlp, "section")
    grads, weight_grads, gain_grads = [None, None], [None, None], [None, None]
    for layer in (1, 0):
        gathered, grad_own, products, gain_grads[layer] = layer_backward(
            grad_own, grad_mlp.reshape(-1, depth), kept[layer], weights[layer], gains[layer], slot,
            shared_kv, layer == 0,
        )
        grads[layer], grad_mlp = gathered[0], gathered[-1]
        whole = [dot_outer(left, right).astype(BF16) for left, right in products]
        attn_grad = scatter_by_permutes(
            jnp.concatenate(whole[:2], axis=1).reshape(dp_size, own_depth, -1), "dp"
        )
        unit_grad = [
            scatter_by_permutes(item.reshape(tensor_size, share, depth), "tensor")
            for item in whole[2:]
        ]
        pieces = jnp.stack(unit_grad).reshape(3, share, dp_size, own_depth).transpose(2, 0, 1, 3)
        weight_grads[layer] = (attn_grad, exchange(pieces, "dp"))

    def bring_home(first, second):
        mine, other = jnp.where(core == 0, first, second), jnp.where(core == 0, second, first)
        arrived = lax.ppermute(other, "section", [(0, 1), (1, 0)])
        return (jnp.where(core == 0, mine, arrived), jnp.where(core == 0, arrived, mine))

    attn_home = bring_home(weight_grads[0][0], weight_grads[1][0])
    unit_home = jnp.stack(bring_home(weight_grads[0][1], weight_grads[1][1]))
    unit_home = unit_home.transpose(2, 0, 1, 3, 4).reshape(3, own_units, own_depth)

    def joined(start, width):
        parts = [half[:, start : start + width] for half in attn_home]
        if shared_kv and start in (q_width, q_width + k_width):
            return parts[0].astype(F32)
        return jnp.concatenate(parts, axis=1).astype(F32)

    gain_total = jnp.stack(gain_grads)
    gain_total = total_over_all(gain_total.reshape(-1, 128)).reshape(gain_total.shape)
    gain_own = pick(gain_total, core)
    share_width = attn_gain.shape[1]
    attn_gain_grad = lax.dynamic_slice_in_dim(gain_own, data_index * share_width, share_width, 0)
    mlp_gain_grad = lax.dynamic_slice_in_dim(
        gain_own, depth + data_index * share_width, share_width, 0
    )
    return (
        jnp.where(core == 0, outputs[0], outputs[1])[None],
        jnp.where(core == 0, grads[0], grads[1])[None],
        attn_gain_grad[None],
        joined(0, q_width)[None],
        joined(q_width, k_width)[None],
        joined(q_width + k_width, k_width)[None],
        joined(qkv_width, q_width).T[None],
        gain_own[2 * depth : 2 * depth + HD][None],
        gain_own[2 * depth + HD :][None],
        mlp_gain_grad[None],
        unit_home[0].T.astype(F32)[None],
        unit_home[1].T.astype(F32)[None],
        unit_home[2].astype(F32)[None],
    )


def solution(mesh):
    rows = P(None, "dp", None)
    wide = P("section", "dp", "tensor")
    tall = P("section", "tensor", "dp")
    gain = P("section", "dp")
    head_gain = P("section", None)
    slots = P("section", None, "dp", None)
    in_specs = (
        rows, rows, P(), P(), P(), gain, wide, wide, wide, tall, head_gain, head_gain, gain,
        wide, wide, tall,
    )
    out_specs = (
        slots, slots, gain, wide, wide, wide, tall, head_gain, head_gain, gain, wide, wide, tall,
    )
    return jax.shard_map(
        on_device, mesh=mesh, in_specs=in_specs, out_specs=out_specs, check_vma=False
    )
```

```python
from functools import partial

import jax
import jax.numpy as jnp
from jax import lax
from jax.experimental import pallas as pl
from jax.experimental.pallas import tpu as pltpu
from jax.sharding import PartitionSpec as P

HD = 128
TRUNK = 512
BRANCH = 96
NB = 4
TREE = 1152
SEGS = 9


EPSILON = 1e-06
THETA = 1000000.0
MASKED = -1e30
F32 = jnp.float32
BF16 = jnp.bfloat16


def rms_scale(values, weight_gain):
    mean_sq = jnp.mean(values * values, axis=-1, keepdims=True)
    return values * lax.rsqrt(mean_sq + EPSILON) * weight_gain


def rotate(values, cos_table, sine_table):
    middle_at = values.shape[-1] // 2
    leading = values[..., :middle_at]
    trailing = values[..., middle_at:]
    return jnp.concatenate(
        [leading * cos_table - trailing * sine_table, trailing * cos_table + leading * sine_table],
        axis=-1,
    )


def rope_tables(positions, head_dim):
    half_steps = jnp.arange(head_dim // 2, dtype=F32)
    inverse = THETA ** (-2.0 * half_steps / head_dim)
    angles = positions.astype(F32)[:, None] * inverse[None, :]
    return (jnp.cos(angles)[:, None, :], jnp.sin(angles)[:, None, :])


def swiglu(gate_in, up_in):
    return jax.nn.silu(gate_in) * up_in


def embed_heads(q_pre, k_pre, q_scale, k_scale, cos_table, sine_table):
    row_count = q_pre.shape[0]
    queries = rms_scale(q_pre.reshape(row_count, -1, HD), q_scale)
    keys_part = rms_scale(k_pre.reshape(row_count, -1, HD), k_scale)
    return (rotate(queries, cos_table, sine_table), rotate(keys_part, cos_table, sine_table))


def tree_layout(seg_row, parent_row):
    labels = jnp.arange(SEGS, dtype=jnp.int32)
    places = jnp.arange(TREE, dtype=jnp.int32)
    member = seg_row[None, :] == labels[:, None]
    starts = jnp.min(jnp.where(member, places[None, :], TREE), axis=1)
    depth_base = jnp.where(labels == 0, 0, jnp.where(labels <= NB, TRUNK, TRUNK + BRANCH))
    shifts = depth_base - starts
    positions = places + jnp.sum(jnp.where(member, shifts[:, None], 0), axis=0)
    grandparent = jnp.sum(
        jnp.where(parent_row[:, None] == labels[None, :], parent_row[None, :], 0), axis=1
    )
    ancestor = (
        (labels[None, :] == labels[:, None])
        | (labels[None, :] == parent_row[:, None])
        | (labels[None, :] == grandparent[:, None])
    )
    return (positions, member.astype(F32), ancestor.astype(F32))


def path_mask(seg_row, parent_row, row_start, row_count):
    positions, member, ancestor = tree_layout(seg_row, parent_row)
    member_rows = lax.dynamic_slice_in_dim(member, row_start, row_count, 1)
    seg_rows = lax.dynamic_slice_in_dim(seg_row, row_start, row_count, 0)
    reach_table = jnp.dot(jnp.dot(member_rows.T, ancestor), member)
    places = jnp.arange(TREE, dtype=jnp.int32)
    row_places = row_start + jnp.arange(row_count, dtype=jnp.int32)
    same_seg = seg_rows[:, None] == seg_row[None, :]
    causal = places[None, :] <= row_places[:, None]
    allowed = (reach_table > 0.5) & (jnp.logical_not(same_seg) | causal)
    row_positions = lax.dynamic_slice_in_dim(positions, row_start, row_count, 0)
    return (allowed, row_positions)


OUTER = (((0,), (0,)), ((), ()))
INNER = (((1,), (1,)), ((), ()))


def dot(left, right):
    return jnp.dot(left, right, preferred_element_type=F32)


def dot_inner(left, right):
    return lax.dot_general(left, right, INNER, preferred_element_type=F32)


def dot_outer(left, right):
    return lax.dot_general(left, right, OUTER, preferred_element_type=F32)


def exchange(pieces, axis):
    size = lax.axis_size(axis)
    me = lax.axis_index(axis)
    got = jnp.zeros_like(pieces)
    own = lax.dynamic_index_in_dim(pieces, me, 0, keepdims=True)
    got = lax.dynamic_update_slice_in_dim(got, own, me, 0)
    for step in range(1, size):
        other = me ^ step
        piece = lax.dynamic_index_in_dim(pieces, other, 0, keepdims=True)
        arrived = lax.ppermute(piece, axis, [(i, i ^ step) for i in range(size)])
        got = lax.dynamic_update_slice_in_dim(got, arrived, other, 0)
    return got


def masked_scores(query_bf, key_all, allowed):
    raw_scores = jnp.einsum(
        "brgd,btd->bgrt", query_bf, key_all, preferred_element_type=F32
    ) * HD ** (-0.5)
    return jnp.where(allowed[:, None], raw_scores, MASKED)


MESH = pl.DeviceIdType.MESH
CHUNK = 256
SEM = pltpu.SemaphoreType.DMA
VMEM = pl.BlockSpec(memory_space=pltpu.VMEM)
HBM = pl.BlockSpec(memory_space=pl.ANY)


def remote(src, dst, send_sem, recv_sem, device_id):
    return pltpu.make_async_remote_copy(
        src_ref=src, dst_ref=dst, send_sem=send_sem, recv_sem=recv_sem,
        device_id=device_id, device_id_type=MESH,
    )


def greet(axes, across):
    barrier = pltpu.get_barrier_semaphore()
    count = 0
    for axis in axes:
        size = lax.axis_size(axis)
        me = lax.axis_index(axis)
        for step in range(1, size):
            pl.semaphore_signal(
                barrier, inc=1, device_id={axis: lax.rem(me + step, size)}, device_id_type=MESH
            )
        count += size - 1
    if across:
        size = lax.axis_size("dp")
        me = lax.axis_index("dp")
        sibling = 1 - lax.axis_index("section")
        for step in range(1, size):
            pl.semaphore_signal(
                barrier, inc=1, device_id={"section": sibling, "dp": lax.rem(me + step, size)},
                device_id_type=MESH,
            )
        count += size - 1
    pl.semaphore_wait(barrier, count)


class Part:
    ins, outs, scratch = (), (), ()

    def bind(self, ins, outs, scratch):
        self.in_refs, self.out_refs, self.refs = ins, outs, scratch

    def prepare(self):
        pass

    def start(self):
        pass

    def run(self):
        pass

    def finish(self):
        pass


def fused(parts, axes, across, collective_id, cost_us):
    counts = [(len(part.ins), len(part.outs), len(part.scratch)) for part in parts]

    def kernel(*refs):
        refs = list(refs)
        groups = []
        for kind in range(3):
            groups.append([])
            for count in counts:
                groups[kind].append(refs[: count[kind]])
                del refs[: count[kind]]
        for part, ins, outs, scratch in zip(parts, *groups):
            part.bind(ins, outs, scratch)
        for part in parts:
            part.prepare()
        greet(axes, across)
        for part in parts:
            part.start()
        for part in parts:
            part.run()
        for part in parts:
            part.finish()

    ins = [item for part in parts for item in part.ins]
    outs = [item for part in parts for item in part.outs]
    results = pl.pallas_call(
        kernel,
        out_shape=[item[0] for item in outs],
        in_specs=[item[1] for item in ins],
        out_specs=[item[1] for item in outs],
        scratch_shapes=[item for part in parts for item in part.scratch],
        cost_estimate=pl.CostEstimate(
            flops=0, bytes_accessed=cost_us * 3_000_000, transcendentals=0
        ),
        compiler_params=pltpu.CompilerParams(
            collective_id=collective_id, has_side_effects=True, vmem_limit_bytes=40 << 20
        ),
    )(*[item[0] for item in ins])
    results = list(results)
    split = []
    for count in counts:
        split.append(results[: count[1]])
        del results[: count[1]]
    return split


def columns_of(place, width):
    return pl.ds(pl.multiple_of(place * width, width), width)


class UnitsOut(Part):
    def __init__(self, pieces, layer):
        self.layer = layer
        cores, self.size, mats, share, self.width = pieces.shape
        self.ins = [(pieces, HBM)]
        shape = jax.ShapeDtypeStruct((mats, share, self.size * self.width), BF16)
        self.outs = [(shape, HBM)]
        self.scratch = [SEM, SEM((cores, self.size)), SEM((self.size,))]

    def bind(self, ins, outs, scratch):
        (self.src,), (self.dst,), (self.keep, self.send, self.recv) = ins, outs, scratch
        self.core, self.me = lax.axis_index("section"), lax.axis_index("dp")

    def lands(self, slot):
        return self.dst.at[:, :, columns_of(slot, self.width)]

    def copy(self, core, place, slot):
        return remote(
            self.src.at[core, place], self.lands(slot), self.send.at[core, place],
            self.recv.at[slot], {"section": core, "dp": place},
        )

    def local(self):
        return pltpu.make_async_copy(self.src.at[self.layer, self.me], self.lands(self.me), self.keep)

    def targets(self):
        for core in range(2):
            for place in range(self.size):
                yield core, place, (place != self.me) | (core != self.layer)

    def start(self):
        @pl.when(self.core == self.layer)
        def _():
            for core, place, is_other in self.targets():
                @pl.when(is_other)
                def _():
                    self.copy(core, place, self.me).start()

            self.local().start()

    def finish(self):
        for place in range(self.size):
            @pl.when((self.core != self.layer) | (place != self.me))
            def _():
                self.copy(0, 0, place).wait_recv()

        @pl.when(self.core == self.layer)
        def _():
            for core, place, is_other in self.targets():
                @pl.when(is_other)
                def _():
                    self.copy(core, place, self.me).wait_send()

            self.local().wait()


class UnitsHome(Part):
    def __init__(self, rows, layer):
        self.layer = layer
        self.size = lax.axis_size("dp")
        mats, share, depth = rows.shape
        self.width = depth // self.size
        self.ins = [(rows, HBM)]
        shape = jax.ShapeDtypeStruct((mats, 2, self.size, share, self.width), BF16)
        self.outs = [(shape, HBM)]
        self.scratch = [SEM, SEM((self.size,)), SEM((2, self.size))]

    def bind(self, ins, outs, scratch):
        (self.src,), (self.dst,), (self.keep, self.send, self.recv) = ins, outs, scratch
        self.core, self.me = lax.axis_index("section"), lax.axis_index("dp")

    def copy(self, place, core, slot):
        return remote(
            self.src.at[:, :, columns_of(place, self.width)], self.dst.at[:, core, slot],
            self.send.at[place], self.recv.at[core, slot], {"section": self.layer, "dp": place},
        )

    def local(self):
        return pltpu.make_async_copy(
            self.src.at[:, :, columns_of(self.me, self.width)],
            self.dst.at[:, self.layer, self.me], self.keep,
        )

    def start(self):
        for place in range(self.size):
            @pl.when((self.core != self.layer) | (place != self.me))
            def _():
                self.copy(place, self.core, self.me).start()

        @pl.when(self.core == self.layer)
        def _():
            self.local().start()

    def finish(self):
        @pl.when(self.core == self.layer)
        def _():
            for core in range(2):
                for place in range(self.size):
                    @pl.when((core != self.layer) | (place != self.me))
                    def _():
                        self.copy(0, core, place).wait_recv()

            self.local().wait()

        for place in range(self.size):
            @pl.when((self.core != self.layer) | (place != self.me))
            def _():
                self.copy(place, self.core, self.me).wait_send()


class SharedRows(Part):
    def __init__(self, own):
        self.size = lax.axis_size("dp")
        self.ins = [(own, VMEM)]
        self.outs = [(jax.ShapeDtypeStruct((2, self.size) + own.shape, F32), VMEM)]
        self.scratch = [SEM((2, self.size)), SEM((2, self.size))]

    def copy(self, core, place, from_core, from_place):
        return remote(
            self.in_refs[0], self.out_refs[0].at[from_core, from_place],
            self.refs[0].at[core, place], self.refs[1].at[from_core, from_place],
            {"section": core, "dp": place},
        )

    def others(self):
        core, me = lax.axis_index("section"), lax.axis_index("dp")
        for other in range(2):
            for place in range(self.size):
                yield other, place, (other != core) | (place != me)

    def start(self):
        core, me = lax.axis_index("section"), lax.axis_index("dp")
        for other, place, is_other in self.others():
            @pl.when(is_other)
            def _():
                self.copy(other, place, core, me).start()

        self.out_refs[0][core, me] = self.in_refs[0][...]

    def finish(self):
        core, me = lax.axis_index("section"), lax.axis_index("dp")
        for other, place, is_other in self.others():
            @pl.when(is_other)
            def _():
                self.copy(other, place, other, place).wait_recv()
                self.copy(other, place, core, me).wait_send()


def far_pair(place, me):
    return (place + me == 3) & ((place == 0) | (place == 3))


def line_relays(size):
    return [(2, 0, 3), (1, 3, 0)] if size == 4 else []


def line_order(size):
    return [1, 2, 0, 3] if size == 4 else list(range(size))


class AttnOut(Part):
    def __init__(self, halves, layer):
        self.layer = layer
        self.size = lax.axis_size("dp")
        self.chunks = halves.shape[1]
        self.ins = [(halves, HBM)]
        self.outs = [(jax.ShapeDtypeStruct((self.size,) + halves.shape[1:], BF16), HBM)]
        self.scratch = [
            SEM, SEM((2, self.size, self.chunks)), SEM((self.size, self.chunks)), SEM((self.chunks,)),
        ]

    def bind(self, ins, outs, scratch):
        (self.src,), (self.dst,) = ins, outs
        self.keep, self.send, self.recv, self.relay_send = scratch
        self.core, self.me = lax.axis_index("section"), lax.axis_index("dp")

    def copy(self, core, place, slot, chunk):
        return remote(
            self.src.at[core, chunk], self.dst.at[slot, chunk], self.send.at[core, place, chunk],
            self.recv.at[slot, chunk], {"section": core, "dp": place},
        )

    def relay(self, source, target, chunk):
        return remote(
            self.dst.at[source, chunk], self.dst.at[source, chunk], self.relay_send.at[chunk],
            self.recv.at[source, chunk], {"dp": target},
        )

    def local(self):
        return pltpu.make_async_copy(self.src.at[self.layer], self.dst.at[self.me], self.keep)

    def targets(self):
        for chunk in range(self.chunks):
            for core in range(2):
                for place in range(self.size):
                    sent = (place != self.me) | (core != self.layer)
                    if self.size == 4:
                        sent = sent & jnp.logical_not(far_pair(place, self.me))
                    yield core, place, chunk, sent

    def start(self):
        @pl.when(self.core == self.layer)
        def _():
            for core, place, chunk, sent in self.targets():
                @pl.when(sent)
                def _():
                    self.copy(core, place, self.me, chunk).start()

            self.local().start()

    def run(self):
        for chunk in range(self.chunks):
            for place in line_order(self.size):
                @pl.when((self.core != self.layer) | (place != self.me))
                def _():
                    self.copy(0, 0, place, chunk).wait_recv()

                for via, source, target in line_relays(self.size):
                    if source == place:
                        @pl.when(self.me == via)
                        def _():
                            self.relay(source, target, chunk).start()

    def finish(self):
        @pl.when(self.core == self.layer)
        def _():
            for core, place, chunk, sent in self.targets():
                @pl.when(sent)
                def _():
                    self.copy(core, place, self.me, chunk).wait_send()

            self.local().wait()

        for via, source, target in line_relays(self.size):
            @pl.when(self.me == via)
            def _():
                for chunk in range(self.chunks):
                    self.relay(source, target, chunk).wait_send()


class HalfOver(Part):
    def __init__(self, halves):
        self.ins = [(halves, HBM)]
        self.outs = [(jax.ShapeDtypeStruct(halves.shape[1:], BF16), HBM)]
        self.scratch = [SEM, SEM, SEM]

    def start(self):
        self.over = remote(
            self.in_refs[0].at[0], self.out_refs[0], self.refs[0], self.refs[1], {"section": 0}
        )
        self.keep = pltpu.make_async_copy(self.in_refs[0].at[1], self.out_refs[0], self.refs[2])

        @pl.when(lax.axis_index("section") == 1)
        def _():
            self.over.start()
            self.keep.start()

    def finish(self):
        @pl.when(lax.axis_index("section") == 1)
        def _():
            self.over.wait_send()
            self.keep.wait()

        @pl.when(lax.axis_index("section") == 0)
        def _():
            self.over.wait_recv()


class Swap(Part):
    def __init__(self, own):
        self.ins = [(own, HBM)]
        self.outs = [(jax.ShapeDtypeStruct(own.shape, own.dtype), HBM)]
        self.scratch = [SEM, SEM]

    def start(self):
        sibling = 1 - lax.axis_index("section")
        self.copy = remote(
            self.in_refs[0], self.out_refs[0], self.refs[0], self.refs[1], {"section": sibling}
        )
        self.copy.start()

    def finish(self):
        self.copy.wait()


class GatherKV(Part):
    def __init__(self, own):
        trees, rows, width = own.shape
        self.trees, self.size = trees, lax.axis_size("dp")
        self.ins = [(own, VMEM)]
        self.outs = [(jax.ShapeDtypeStruct((trees, self.size, rows, width), BF16), VMEM)]
        self.scratch = [SEM((self.size, trees)), SEM((self.size, trees)), SEM((trees,))]

    def bind(self, ins, outs, scratch):
        (self.own,), (self.out,) = ins, outs
        self.send, self.recv, self.relay_send = scratch
        self.me = lax.axis_index("dp")

    def copy(self, place, slot, tree):
        return remote(
            self.own.at[tree], self.out.at[tree, slot], self.send.at[place, tree],
            self.recv.at[slot, tree], {"dp": place},
        )

    def relay(self, source, target, tree):
        return remote(
            self.out.at[tree, source], self.out.at[tree, source], self.relay_send.at[tree],
            self.recv.at[source, tree], {"dp": target},
        )

    def targets(self):
        for tree in range(self.trees):
            for place in range(self.size):
                sent = place != self.me
                if self.size == 4:
                    sent = sent & jnp.logical_not(far_pair(place, self.me))
                yield place, tree, sent

    def start(self):
        for place, tree, sent in self.targets():
            @pl.when(sent)
            def _():
                self.copy(place, self.me, tree).start()

        self.out[:, self.me] = self.own[...]

    def run(self):
        for tree in range(self.trees):
            for place in line_order(self.size):
                @pl.when(place != self.me)
                def _():
                    self.copy(place, place, tree).wait_recv()

                for via, source, target in line_relays(self.size):
                    if source == place:
                        @pl.when(self.me == via)
                        def _():
                            self.relay(source, target, tree).start()

    def finish(self):
        for place, tree, sent in self.targets():
            @pl.when(sent)
            def _():
                self.copy(place, self.me, tree).wait_send()

        for via, source, target in line_relays(self.size):
            @pl.when(self.me == via)
            def _():
                for tree in range(self.trees):
                    self.relay(source, target, tree).wait_send()


class ScatterKV(Part):
    def __init__(self, whole):
        trees, size, rows, width = whole.shape
        self.trees, self.size = trees, size
        self.sides = [(0, 1, 3), (3, 2, 0)] if size == 4 else []
        self.ins = [(whole, VMEM)]
        self.outs = [(jax.ShapeDtypeStruct((trees, rows, width), F32), VMEM)]
        self.scratch = [
            pltpu.VMEM((size, trees, rows, width), BF16), pltpu.VMEM((trees, rows, width), BF16),
            SEM((size, trees)), SEM((size, trees)), SEM((trees,)), SEM((trees,)),
        ]

    def bind(self, ins, outs, scratch):
        (self.terms,), (self.out,) = ins, outs
        self.boxes, self.joint, self.send, self.recv, self.join_send, self.join_recv = scratch
        self.me = lax.axis_index("dp")

    def copy(self, place, slot, tree):
        return remote(
            self.terms.at[tree, place], self.boxes.at[slot, tree], self.send.at[place, tree],
            self.recv.at[slot, tree], {"dp": place},
        )

    def by_way(self, via, target, tree):
        return remote(
            self.terms.at[tree, target], self.joint.at[tree], self.join_send.at[tree],
            self.join_recv.at[tree], {"dp": via},
        )

    def joined(self, via, target, tree):
        return remote(
            self.joint.at[tree], self.boxes.at[via, tree], self.send.at[target, tree],
            self.recv.at[via, tree], {"dp": target},
        )

    def plain(self, place):
        ok = place != self.me
        for source, via, target in self.sides:
            if place == target:
                ok = ok & (self.me != source) & (self.me != via)
        return ok

    def expected(self, place):
        ok = place != self.me
        for source, via, target in self.sides:
            if place == source:
                ok = ok & (self.me != target)
        return ok

    def start(self):
        for tree in range(self.trees):
            for source, via, target in self.sides:
                @pl.when(self.me == source)
                def _():
                    self.by_way(via, target, tree).start()

            for place in range(self.size):
                @pl.when(self.plain(place))
                def _():
                    self.copy(place, self.me, tree).start()

    def run(self):
        for tree in range(self.trees):
            for source, via, target in self.sides:
                @pl.when(self.me == via)
                def _():
                    self.by_way(via, target, tree).wait_recv()
                    both = self.joint[tree].astype(F32) + self.terms[tree, target].astype(F32)
                    self.joint[tree] = both.astype(BF16)
                    self.joined(via, target, tree).start()

        for tree in range(self.trees):
            self.out[tree] = self.terms[tree, self.me].astype(F32)
            for place in line_order(self.size):
                @pl.when(self.expected(place))
                def _():
                    self.copy(place, place, tree).wait_recv()
                    self.out[tree] += self.boxes[place, tree].astype(F32)

    def finish(self):
        for tree in range(self.trees):
            for place in range(self.size):
                @pl.when(self.plain(place))
                def _():
                    self.copy(place, self.me, tree).wait_send()

            for source, via, target in self.sides:
                @pl.when(self.me == source)
                def _():
                    self.by_way(via, target, tree).wait_send()

                @pl.when(self.me == via)
                def _():
                    self.joined(via, target, tree).wait_send()


class TotalOverAll(Part):
    axes = ("section", "tensor", "dp")

    def __init__(self, own):
        sizes = [lax.axis_size(axis) for axis in self.axes]
        self.ins = [(own, VMEM)]
        self.outs = [(jax.ShapeDtypeStruct(own.shape, F32), VMEM)]
        self.scratch = [pltpu.VMEM((size,) + own.shape, F32) for size in sizes]
        self.scratch += [SEM((size,)) for size in sizes] * 2

    def run(self):
        out = self.out_refs[0]
        out[...] = self.in_refs[0][...]
        for axis, box, send, recv in zip(self.axes, self.refs[:3], self.refs[3:6], self.refs[6:9]):
            size, me = lax.axis_size(axis), lax.axis_index(axis)
            box[me] = out[...]

            def spread(place, slot):
                return remote(box.at[me], box.at[slot], send.at[place], recv.at[slot], {axis: place})

            for place in range(size):
                @pl.when(place != me)
                def _():
                    spread(place, me).start()

            for place in range(size):
                @pl.when(place != me)
                def _():
                    spread(place, place).wait_recv()
                    spread(place, me).wait_send()

            total = box[0]
            for place in range(1, size):
                total += box[place]
            out[...] = total


class Hub(Part):
    def __init__(self, terms, own_args, body, own_outs, scatter, gathers):
        self.body, self.scatter, self.gathers = body, scatter, gathers
        self.n_own = len(own_outs)
        self.rows, depth = own_args[0].shape
        rows, half = self.rows, depth // 2
        self.half = half
        self.sizes = [lax.axis_size(axis) for axis in gathers]
        self.ins = [(arg, VMEM) for arg in own_args]
        self.outs = [(jax.ShapeDtypeStruct(shape, F32), VMEM) for shape in own_outs]
        self.outs += [
            (jax.ShapeDtypeStruct((2, size * rows, depth), BF16), VMEM) for size in self.sizes
        ]
        self.scratch = []
        if scatter:
            self.ins = [(terms, VMEM)] + self.ins
            size = self.size = lax.axis_size(scatter)
            boxes = pltpu.VMEM((size, 2 * rows, half), BF16)
            self.scratch += [boxes] * 4 + [pltpu.VMEM((2 * rows, half), F32)] + [SEM((size,))] * 4
        for size in self.sizes:
            self.scratch += [pltpu.VMEM((2, size, 2 * rows, half), BF16)] + [SEM((size,))] * 4

    def bind(self, ins, outs, scratch):
        self.own_outs, self.gathered = outs[: self.n_own], outs[self.n_own :]
        self.core = lax.axis_index("section")
        self.sibling = 1 - self.core
        if self.scatter:
            self.terms, *self.args = ins
            self.to_sib, self.from_sib, self.to_peer, self.from_peer, self.total = scratch[:5]
            self.sib_send, self.sib_recv, self.peer_send, self.peer_recv = scratch[5:9]
            scratch = scratch[9:]
            self.me = lax.axis_index(self.scatter)
        else:
            self.args = ins
        self.boards = [scratch[5 * i : 5 * i + 5] for i in range(len(self.gathers))]

    def packed(self, tree, place, at):
        rows = self.rows
        low = rows * place // 16 * 16
        high = -(-rows * (place + 1) // 16) * 16
        skip = rows * place - low
        parts = [
            self.terms[tree, low:high, pl.ds(side * self.half + at, CHUNK)].astype(F32)[
                skip : skip + rows
            ]
            for side in range(2)
        ]
        return jnp.concatenate(parts, axis=0)

    def over_columns(self, step_body):
        @pl.loop(0, self.half // CHUNK)
        def _(step):
            step_body(pl.multiple_of(step * CHUNK, CHUNK))

    def prepare(self):
        if not self.scatter:
            return
        for place in range(self.size):
            def pack(at):
                self.to_sib[place, :, pl.ds(at, CHUNK)] = self.packed(
                    self.sibling, place, at
                ).astype(BF16)

            self.over_columns(pack)

    def sib_copy(self, place):
        return remote(
            self.to_sib.at[place], self.from_sib.at[place], self.sib_send.at[place],
            self.sib_recv.at[place], {"section": self.sibling},
        )

    def peer_copy(self, place, slot):
        return remote(
            self.to_peer.at[place], self.from_peer.at[slot], self.peer_send.at[place],
            self.peer_recv.at[slot], {self.scatter: place},
        )

    def spread(self, index, place, slot):
        board, send, recv, _, _ = self.boards[index]
        return remote(
            board.at[self.core, slot], board.at[self.core, slot], send.at[place], recv.at[slot],
            {self.gathers[index]: place},
        )

    def relay(self, index, tree, slot):
        board, _, _, send, recv = self.boards[index]
        return remote(
            board.at[tree, slot], board.at[tree, slot], send.at[slot], recv.at[slot],
            {"section": self.sibling},
        )

    def start(self):
        if self.scatter:
            for place in range(self.size):
                self.sib_copy(place).start()

    def summed(self):
        for place in range(self.size):
            self.sib_copy(place).wait_recv()

            def add(at):
                both = self.packed(self.core, place, at)
                both += self.from_sib[place, :, pl.ds(at, CHUNK)].astype(F32)
                self.to_peer[place, :, pl.ds(at, CHUNK)] = both.astype(BF16)

                @pl.when(place == self.me)
                def _():
                    self.total[:, pl.ds(at, CHUNK)] = both

            self.over_columns(add)

            @pl.when(place != self.me)
            def _():
                self.peer_copy(place, self.me).start()

        for place in range(self.size):
            @pl.when(place != self.me)
            def _():
                self.peer_copy(place, place).wait_recv()
                self.total[...] += self.from_peer[place].astype(F32)

        total = self.total[...]
        return jnp.concatenate([total[: self.rows], total[self.rows :]], axis=1)

    def unpack(self, index, tree):
        board, out, rows = self.boards[index][0], self.gathered[index], self.rows

        def step_body(at):
            blocks = [
                board[tree, place, :, pl.ds(at, CHUNK)].astype(F32)
                for place in range(self.sizes[index])
            ]
            for side in range(2):
                whole = [block[side * rows : (side + 1) * rows] for block in blocks]
                out[tree, :, pl.ds(side * self.half + at, CHUNK)] = jnp.concatenate(
                    whole, axis=0
                ).astype(BF16)

        self.over_columns(step_body)

    def run(self):
        total = self.summed() if self.scatter else None
        result = self.body(total, self.args, self.own_outs)
        half = self.half
        piece = jnp.concatenate([result[:, :half], result[:, half:]], axis=0).astype(BF16)
        places = [lax.axis_index(axis) for axis in self.gathers]
        for index, size in enumerate(self.sizes):
            self.boards[index][0][self.core, places[index]] = piece
            for place in range(size):
                @pl.when(place != places[index])
                def _():
                    self.spread(index, place, places[index]).start()

            self.relay(index, self.core, places[index]).start()

        for index, size in enumerate(self.sizes):
            for place in range(size):
                @pl.when(place != places[index])
                def _():
                    self.spread(index, place, place).wait_recv()
                    self.relay(index, self.core, place).start()

        for index in range(len(self.sizes)):
            self.unpack(index, self.core)
        for index, size in enumerate(self.sizes):
            for place in range(size):
                self.relay(index, self.sibling, place).wait_recv()
            self.unpack(index, self.sibling)

    def finish(self):
        if self.scatter:
            for place in range(self.size):
                self.sib_copy(place).wait_send()

                @pl.when(place != self.me)
                def _():
                    self.peer_copy(place, self.me).wait_send()

        for index, size in enumerate(self.sizes):
            me = lax.axis_index(self.gathers[index])
            for place in range(size):
                self.relay(index, self.core, place).wait_send()

                @pl.when(place != me)
                def _():
                    self.spread(index, place, me).wait_send()


def hub_plain(terms, own_args, body, own_outs, scatter, gathers):
    total = None
    if scatter:
        mine = lax.psum_scatter(terms, "section", scatter_dimension=0, tiled=True)
        mine = lax.psum_scatter(mine, scatter, scatter_dimension=1, tiled=True)[0]
        total = mine.astype(F32)

    class Cell:
        def __setitem__(self, _, value):
            self.value = value

    cells = [Cell() for _ in own_outs]
    result = body(total, own_args, cells).astype(BF16)
    gathered = [
        lax.all_gather(lax.all_gather(result, axis, axis=0, tiled=True), "section", axis=0)
        for axis in gathers
    ]
    return [cell.value for cell in cells] + gathered


def gather_kv(own, cargo, fast, collective_id):
    trees, rows, width = own.shape
    if not fast:
        return lax.all_gather(own, "dp", axis=1, tiled=True), []
    whole, *outs = fused(
        cargo + [GatherKV(own)], ["section", "dp"], bool(cargo), collective_id, 30
    )[::-1]
    return whole[0].reshape(trees, -1, width), outs[::-1]


def scatter_kv(whole, cargo, fast, collective_id):
    trees, all_rows, width = whole.shape
    size = lax.axis_size("dp")
    if not fast:
        return lax.psum_scatter(whole, "dp", scatter_dimension=1, tiled=True).astype(F32), []
    part = ScatterKV(whole.reshape(trees, size, all_rows // size, width))
    total, *outs = fused(cargo + [part], ["section", "dp"], bool(cargo), collective_id, 30)[::-1]
    return total[0], outs[::-1]


def meet(terms, own_args, body, own_outs, scatter, gathers, cargo, fast, collective_id):
    if not fast:
        return hub_plain(terms, own_args, body, own_outs, scatter, gathers), []
    axes = ["section"] + sorted(set(gathers) | {scatter} | ({"dp"} if cargo else set()))
    part = Hub(terms, own_args, body, own_outs, scatter, gathers)
    outs, *others = fused(cargo + [part], axes, bool(cargo), collective_id, 50)[::-1]
    return outs, others[::-1]


def norm_body(total, args, outs):
    middle = args[0][...] + total
    outs[0][...] = middle
    mean_sq = jnp.mean(middle * middle, axis=1, keepdims=True)
    return middle * lax.rsqrt(mean_sq + EPSILON) * args[1][...]


def add_body(total, args, outs):
    result = args[0][...] + total
    outs[0][...] = result
    return result


def norm_back_body(total, args, outs):
    values, gain = args[0][...], args[1][...]
    scale = lax.rsqrt(jnp.mean(values * values, axis=1, keepdims=True) + EPSILON)
    unit = values * scale
    outs[1][...] = jnp.sum(total * unit, axis=0, keepdims=True)
    scaled = total * gain
    along = jnp.mean(scaled * unit, axis=1, keepdims=True)
    result = (scaled - unit * along) * scale + args[2][...]
    outs[0][...] = result
    return result


def embed(q_pre, k_pre, q_scale, k_scale, cos_table, sine_table):
    queries = rms_scale(q_pre, q_scale)
    keys = rms_scale(k_pre, k_scale)
    return (
        rotate(queries, cos_table[:, :, None], sine_table[:, :, None]),
        rotate(keys, cos_table, sine_table),
    )


def layer_forward(hidden_in, own_in, weights, gains, slot, cargo, fast, ids):
    attn_scale, mlp_scale, q_scale, k_scale = gains
    w_qkv, w_outt, w_gate, w_up, w_down = weights
    carried = []
    allowed, cos_table, sine_table = slot
    trees, row_count, depth = hidden_in.shape
    q_width = w_outt.shape[1]
    normed = rms_scale(hidden_in.astype(F32), attn_scale).astype(BF16).reshape(-1, depth)
    qkv = dot(normed, w_qkv).reshape(trees, row_count, -1)
    q_pre = qkv[:, :, :q_width].reshape(trees, row_count, -1, HD)
    k_pre = qkv[:, :, q_width : q_width + HD]
    value_bf = qkv[:, :, q_width + HD :].astype(BF16)
    queries, keys_rot = embed(q_pre, k_pre, q_scale, k_scale, cos_table, sine_table)
    query_bf = queries.astype(BF16)
    kv_all, outs = gather_kv(
        jnp.concatenate([keys_rot.astype(BF16), value_bf], axis=2), cargo(0), fast, ids[0]
    )
    carried += outs
    key_all = kv_all[:, :, :HD]
    value_all = kv_all[:, :, HD:]
    scores = masked_scores(query_bf, key_all, allowed)
    row_max = jnp.max(scores, axis=-1, keepdims=True)
    exp_scores = jnp.exp(scores - row_max)
    row_total = jnp.sum(exp_scores, axis=-1, keepdims=True)
    prob_bf = (exp_scores / row_total).astype(BF16)
    log_total = row_max + jnp.log(row_total)
    attended = jnp.einsum("bgrt,btd->brgd", prob_bf, value_all, preferred_element_type=F32)
    attended_bf = attended.reshape(trees * row_count, -1).astype(BF16)
    attn_partial = dot_inner(attended_bf, w_outt).astype(BF16).reshape(trees, row_count, depth)
    own_shape = own_in.shape
    (middle, mlp_in), outs = meet(
        attn_partial, [own_in, mlp_scale[None]], norm_body, [own_shape], "tensor", ["dp"],
        cargo(1), fast, ids[1],
    )
    carried += outs
    mlp_in = mlp_in.reshape(-1, depth)
    gate_pre = dot_inner(mlp_in, w_gate)
    upward = dot_inner(mlp_in, w_up)
    hidden_bf = swiglu(gate_pre, upward).astype(BF16)
    mlp_partial = dot(hidden_bf, w_down).astype(BF16).reshape(trees, -1, depth)
    (output_own, output_bf), outs = meet(
        mlp_partial, [middle], add_body, [own_shape], "dp", ["tensor"], cargo(2), fast, ids[2]
    )
    carried += outs
    stored = (
        own_in, normed, q_pre, k_pre, query_bf, key_all, value_all, log_total, attended_bf,
        middle, mlp_in, gate_pre, upward, hidden_bf,
    )
    return (output_bf, output_own.astype(BF16).astype(F32), stored, carried)


def layer_backward(grad_own, grad_mlp, stored, weights, gains, slot, shared_kv, is_first, cargo, fast, ids):
    attn_scale, mlp_scale, q_scale, k_scale = gains
    w_qkv, w_outt, w_gate, w_up, w_down = weights
    allowed, cos_table, sine_table = slot
    (
        own_in, normed, q_pre, k_pre, query_bf, key_all, value_all, log_total, attended_bf,
        middle, mlp_in, gate_pre, upward, hidden_bf,
    ) = stored
    trees, row_count = query_bf.shape[:2]
    depth = normed.shape[1]
    grad_hidden = dot_inner(grad_mlp, w_down)
    _, swiglu_pull = jax.vjp(swiglu, gate_pre, upward)
    grad_gate, grad_upward = swiglu_pull(grad_hidden)
    gate_bf = grad_gate.astype(BF16)
    up_bf = grad_upward.astype(BF16)
    mlp_partial = (dot(gate_bf, w_gate) + dot(up_bf, w_up)).astype(BF16)
    own_outs = [own_in.shape, (1, depth)]
    (grad_middle, grad_mlp_scale, grad_attn), carried = meet(
        mlp_partial.reshape(trees, -1, depth),
        [middle, mlp_scale[None], grad_own],
        norm_back_body, own_outs, "dp", ["tensor"], cargo(0), fast, ids[0],
    )
    grad_attn = grad_attn.reshape(-1, depth)
    grad_heads = dot(grad_attn, w_outt).astype(BF16).reshape(query_bf.shape)
    scores = masked_scores(query_bf, key_all, allowed)
    prob_full = jnp.exp(scores - log_total)
    grad_prob = jnp.einsum("brgd,btd->bgrt", grad_heads, value_all, preferred_element_type=F32)
    row_dot = jnp.sum(prob_full * grad_prob, axis=-1, keepdims=True)
    grad_scores = (prob_full * (grad_prob - row_dot)).astype(BF16)
    scale_factor = HD ** (-0.5)
    grad_query = (
        jnp.einsum("bgrt,btd->brgd", grad_scores, key_all, preferred_element_type=F32)
        * scale_factor
    )
    grad_key_all = (
        jnp.einsum("bgrt,brgd->btd", grad_scores, query_bf, preferred_element_type=F32)
        * scale_factor
    )
    grad_value_all = jnp.einsum(
        "bgrt,brgd->btd", prob_full.astype(BF16), grad_heads, preferred_element_type=F32
    )
    grad_kv, outs = scatter_kv(
        jnp.concatenate([grad_key_all, grad_value_all], axis=2).astype(BF16),
        cargo(1), fast, ids[1],
    )
    carried += outs
    grad_kv = grad_kv.astype(BF16)
    if shared_kv:
        total = lax.psum(grad_kv, "section")
        grad_kv = jnp.where(lax.axis_index("section") == 0, total, jnp.zeros_like(total))
    _, embedding_pull = jax.vjp(
        partial(embed, cos_table=cos_table, sine_table=sine_table), q_pre, k_pre, q_scale, k_scale
    )
    grad_q_pre, grad_k_pre, grad_q_scale, grad_k_scale = embedding_pull(
        (grad_query, grad_kv[:, :, :HD].astype(F32))
    )
    qkv_grad = jnp.concatenate(
        [
            grad_q_pre.astype(BF16).reshape(trees, row_count, -1),
            grad_k_pre.astype(BF16),
            grad_kv[:, :, HD:],
        ],
        axis=2,
    ).reshape(trees * row_count, -1)
    attn_partial = dot_inner(qkv_grad, w_qkv).astype(BF16).reshape(trees, row_count, depth)
    gathers = ["tensor"] if is_first else ["tensor", "dp"]
    (incoming_own, grad_attn_scale, *gathered), outs = meet(
        attn_partial, [own_in, attn_scale[None], grad_middle],
        norm_back_body, own_outs, "tensor", gathers, cargo(2), fast, ids[2],
    )
    carried += outs
    products = (
        (normed, qkv_grad),
        (grad_attn, attended_bf),
        (gate_bf, mlp_in),
        (up_bf, mlp_in),
        (hidden_bf, grad_mlp),
    )
    gain_grads = jnp.concatenate(
        [grad_attn_scale[0], grad_mlp_scale[0], grad_q_scale, grad_k_scale]
    )
    return (gathered, incoming_own.astype(BF16).astype(F32), products, gain_grads, carried)


def swap_cores(mine, other):
    core = lax.axis_index("section")
    arrived = lax.ppermute(other, "section", [(0, 1), (1, 0)])
    return (jnp.where(core == 0, mine, arrived), jnp.where(core == 0, arrived, mine))


def on_device(
    inputs, cotangent, seg_ids, parents, order, attn_gain, w_query, w_key, w_value, w_out,
    q_gain, k_gain, mlp_gain, w_gate, w_up, w_down,
):
    core = lax.axis_index("section")
    data_index = lax.axis_index("dp")
    tensor_index = lax.axis_index("tensor")
    dp_size = lax.axis_size("dp")
    tensor_size = lax.axis_size("tensor")
    trees, row_count, depth = inputs.shape
    own_rows = row_count // tensor_size
    row_start = data_index * row_count
    own_depth = w_query.shape[1]
    q_width = w_query.shape[2] // 2
    shared_kv = w_key.shape[2] == HD
    k_width = HD if shared_kv else w_key.shape[2] // 2
    own_units = w_gate.shape[2]
    share = own_units // (2 * dp_size)

    def pick(stacked, index):
        return lax.dynamic_index_in_dim(stacked, index, 0, keepdims=False)

    fast = (
        own_rows % 8 == 0
        and depth % (2 * CHUNK) == 0
        and row_count % 16 == 0
        and share % 16 == 0
        and own_depth % 128 == 0
        and not shared_kv
    )

    def halves(width, array):
        return [array[:, :width], array[:, array.shape[1] - width :]]

    attn_halves = jnp.stack(
        [
            jnp.concatenate(parts, axis=1)
            for parts in zip(
                halves(q_width, w_query[0]),
                halves(k_width, w_key[0]),
                halves(k_width, w_value[0]),
                halves(q_width, w_out[0].T),
            )
        ]
    )
    unit_blocks = jnp.stack([w_gate[0].T, w_up[0].T, w_down[0]]).reshape(
        3, 2, dp_size, share, own_depth
    )
    unit_blocks = unit_blocks.transpose(1, 2, 0, 3, 4)
    qkv_width = q_width + 2 * k_width
    gains_own = jnp.concatenate([attn_gain[0], mlp_gain[0], q_gain[0], k_gain[0]]).astype(F32)

    def spread_units(rows):
        return lax.all_gather(rows, "tensor", axis=0, tiled=True)

    def attn_of(whole):
        whole = whole.reshape(depth, -1)
        return (whole[:, :qkv_width], whole[:, qkv_width:])

    def joint(gate_up, down):
        return (spread_units(gate_up[0]), spread_units(gate_up[1]), spread_units(down[0]))

    if fast:
        group = ["section", "dp"]
        (gate_up,), (gains_all,) = fused(
            [
                UnitsOut(unit_blocks[:, :, :2], 0),
                SharedRows(gains_own.reshape(-1, 128)),
            ],
            group, True, 1, 45,
        )
        attn_chunks = attn_halves.reshape(2, 4, own_depth // 4, -1)
        attn_chunks, gate_up = lax.optimization_barrier((attn_chunks, gate_up))
        (attn_all,), (down,), (attn_shard,) = fused(
            [
                AttnOut(attn_chunks, 0), UnitsOut(unit_blocks[:, :, 2:], 0), HalfOver(attn_chunks),
            ],
            group, True, 2, 80,
        )
        attn_next = lax.all_gather(attn_shard.reshape(own_depth, -1), "dp", axis=0, tiled=True)
        first_weights = attn_of(attn_all) + joint(gate_up, down)
    else:
        gains_all = lax.all_gather(gains_own, ("section", "dp"))
        attn_shards = swap_cores(pick(attn_halves, core), pick(attn_halves, 1 - core))
        unit_shards = swap_cores(pick(unit_blocks, core), pick(unit_blocks, 1 - core))
        both_weights = []
        for layer in range(2):
            attn_all = lax.all_gather(attn_shards[layer], "dp", axis=0, tiled=True)
            pieces = exchange(unit_shards[layer], "dp")
            pieces = pieces.transpose(1, 2, 0, 3).reshape(3, share, depth)
            both_weights.append(attn_of(attn_all) + joint(pieces[:2], pieces[2:]))
        first_weights = both_weights[0]

    gains_all = gains_all.reshape(2, dp_size, -1)
    gains = [
        (
            gains_all[layer, :, :own_depth].reshape(depth),
            gains_all[layer, :, own_depth : 2 * own_depth].reshape(depth),
            gains_all[layer, 0, 2 * own_depth : 2 * own_depth + HD],
            gains_all[layer, 0, 2 * own_depth + HD :],
        )
        for layer in range(2)
    ]

    def slot_setup(slot_index):
        tree_id = pick(order, slot_index)
        allowed, row_positions = path_mask(
            pick(seg_ids, tree_id), pick(parents, tree_id), row_start, row_count
        )
        cos_table, sine_table = rope_tables(row_positions, HD)
        return (pick(inputs, tree_id), allowed, cos_table[:, 0], sine_table[:, 0])

    setups = [slot_setup(i) for i in range(trees)]
    hidden, *slot = (jnp.stack(item) for item in zip(*setups))

    def own_part(whole):
        return lax.dynamic_slice_in_dim(
            pick(whole, core), tensor_index * own_rows, own_rows, 0
        )

    own_in = own_part(hidden).astype(F32)
    def no_cargo(_):
        return []

    def next_units(index):
        return [UnitsOut(unit_blocks[:, :, index : index + 1], 1)] if fast else []

    output, own_in, kept_first, carried = layer_forward(
        hidden, own_in, first_weights, gains[0], slot, next_units, fast, (3, 4, 5)
    )
    outputs, kept = [output], [kept_first]
    if fast:
        rows = [out[0][0] for out in carried]
        second_weights = attn_of(attn_next) + tuple(spread_units(item) for item in rows)
    else:
        second_weights = both_weights[1]
    output, _, kept_second, _ = layer_forward(
        output, own_in, second_weights, gains[1], slot, no_cargo, fast, (6, 7, 8)
    )
    outputs.append(output)
    kept.append(kept_second)
    weights = [first_weights, second_weights]

    grad_own = own_part(cotangent).astype(F32)
    grad_mlp = lax.all_gather(grad_own.astype(BF16), "dp", axis=0, tiled=True)
    grad_mlp = lax.all_gather(grad_mlp, "section", axis=0)
    grads, weight_grads, gain_grads = [None, None], [None, None], [None, None]
    unit_grad = None
    for layer in (1, 0):
        def home_units(index):
            if not fast or layer == 1 or index == 0:
                return []
            return [UnitsHome(unit_grad[:1] if index == 1 else unit_grad[1:], 1)]

        gathered, grad_own, products, gain_grads[layer], carried = layer_backward(
            grad_own, grad_mlp.reshape(-1, depth), kept[layer], weights[layer], gains[layer], slot,
            shared_kv, layer == 0, home_units, fast, (9, 10, 11) if layer else (12, 13, 14),
        )
        grads[layer], grad_mlp = gathered[0], gathered[-1]
        whole = [dot_outer(left, right).astype(BF16) for left, right in products]
        unit_grad = jnp.stack(
            [
                lax.psum_scatter(item, "tensor", scatter_dimension=0, tiled=True)
                for item in whole[2:]
            ]
        )
        attn_grad = lax.psum_scatter(
            jnp.concatenate(whole[:2], axis=1), "dp", scatter_dimension=0, tiled=True
        )
        weight_grads[layer] = (attn_grad, unit_grad)

    gain_total = jnp.stack(gain_grads)
    if fast:
        mine = jnp.where(core == 0, weight_grads[0][0], weight_grads[1][0])
        other = jnp.where(core == 0, weight_grads[1][0], weight_grads[0][0])
        (gain_total,), (arrived,), (first_home,) = fused(
            [TotalOverAll(gain_total.reshape(-1, 128)), Swap(other), UnitsHome(unit_grad, 0)],
            ["section", "dp", "tensor"], True, 15, 60,
        )
        attn_home = (jnp.where(core == 0, mine, arrived), jnp.where(core == 0, arrived, mine))
        second_home = jnp.concatenate([out[0] for out in carried], axis=0)
        unit_home = jnp.where(core == 0, first_home, second_home).reshape(3, own_units, own_depth)
        gain_total = gain_total.reshape(2, -1)
    else:
        def bring_home(first, second):
            mine, other = jnp.where(core == 0, first, second), jnp.where(core == 0, second, first)
            arrived = lax.ppermute(other, "section", [(0, 1), (1, 0)])
            return (jnp.where(core == 0, mine, arrived), jnp.where(core == 0, arrived, mine))

        def pieces_of(grad):
            return exchange(
                grad.reshape(3, share, dp_size, own_depth).transpose(2, 0, 1, 3), "dp"
            )

        attn_home = bring_home(weight_grads[0][0], weight_grads[1][0])
        unit_home = jnp.stack(bring_home(pieces_of(weight_grads[0][1]), pieces_of(weight_grads[1][1])))
        unit_home = unit_home.transpose(2, 0, 1, 3, 4).reshape(3, own_units, own_depth)
        gain_total = lax.psum(gain_total, ("section", "dp", "tensor"))

    def joined(start, width):
        parts = [half[:, start : start + width] for half in attn_home]
        if shared_kv and start in (q_width, q_width + k_width):
            return parts[0].astype(F32)
        return jnp.concatenate(parts, axis=1).astype(F32)

    gain_own = pick(gain_total, core)
    share_width = attn_gain.shape[1]
    attn_gain_grad = lax.dynamic_slice_in_dim(gain_own, data_index * share_width, share_width, 0)
    mlp_gain_grad = lax.dynamic_slice_in_dim(
        gain_own, depth + data_index * share_width, share_width, 0
    )
    return (
        jnp.where(core == 0, outputs[0], outputs[1])[None],
        jnp.where(core == 0, grads[0], grads[1])[None],
        attn_gain_grad[None],
        joined(0, q_width)[None],
        joined(q_width, k_width)[None],
        joined(q_width + k_width, k_width)[None],
        joined(qkv_width, q_width).T[None],
        gain_own[2 * depth : 2 * depth + HD][None],
        gain_own[2 * depth + HD :][None],
        mlp_gain_grad[None],
        unit_home[0].T.astype(F32)[None],
        unit_home[1].T.astype(F32)[None],
        unit_home[2].astype(F32)[None],
    )


def solution(mesh):
    rows = P(None, "dp", None)
    wide = P("section", "dp", "tensor")
    tall = P("section", "tensor", "dp")
    gain = P("section", "dp")
    head_gain = P("section", None)
    slots = P("section", None, "dp", None)
    in_specs = (
        rows, rows, P(), P(), P(), gain, wide, wide, wide, tall, head_gain, head_gain, gain,
        wide, wide, tall,
    )
    out_specs = (
        slots, slots, gain, wide, wide, wide, tall, head_gain, head_gain, gain, wide, wide, tall,
    )
    return jax.shard_map(
        on_device, mesh=mesh, in_specs=in_specs, out_specs=out_specs, check_vma=False
    )
```

```python
from functools import partial

import jax
import jax.numpy as jnp
from jax import lax
from jax.experimental import pallas as pl
from jax.experimental.pallas import tpu as pltpu
from jax.sharding import PartitionSpec as P

HD = 128
TRUNK = 512
BRANCH = 96
NB = 4
TREE = 1152
SEGS = 9


EPSILON = 1e-06
THETA = 1000000.0
MASKED = -1e30
F32 = jnp.float32
BF16 = jnp.bfloat16


def rms_scale(values, weight_gain):
    mean_sq = jnp.mean(values * values, axis=-1, keepdims=True)
    return values * lax.rsqrt(mean_sq + EPSILON) * weight_gain


def rotate(values, cos_table, sine_table):
    middle_at = values.shape[-1] // 2
    leading = values[..., :middle_at]
    trailing = values[..., middle_at:]
    return jnp.concatenate(
        [leading * cos_table - trailing * sine_table, trailing * cos_table + leading * sine_table],
        axis=-1,
    )


def rope_tables(positions, head_dim):
    half_steps = jnp.arange(head_dim // 2, dtype=F32)
    inverse = THETA ** (-2.0 * half_steps / head_dim)
    angles = positions.astype(F32)[:, None] * inverse[None, :]
    return (jnp.cos(angles)[:, None, :], jnp.sin(angles)[:, None, :])


def swiglu(gate_in, up_in):
    return jax.nn.silu(gate_in) * up_in


def embed_heads(q_pre, k_pre, q_scale, k_scale, cos_table, sine_table):
    row_count = q_pre.shape[0]
    queries = rms_scale(q_pre.reshape(row_count, -1, HD), q_scale)
    keys_part = rms_scale(k_pre.reshape(row_count, -1, HD), k_scale)
    return (rotate(queries, cos_table, sine_table), rotate(keys_part, cos_table, sine_table))


def tree_layout(seg_row, parent_row):
    labels = jnp.arange(SEGS, dtype=jnp.int32)
    places = jnp.arange(TREE, dtype=jnp.int32)
    member = seg_row[None, :] == labels[:, None]
    starts = jnp.min(jnp.where(member, places[None, :], TREE), axis=1)
    depth_base = jnp.where(labels == 0, 0, jnp.where(labels <= NB, TRUNK, TRUNK + BRANCH))
    shifts = depth_base - starts
    positions = places + jnp.sum(jnp.where(member, shifts[:, None], 0), axis=0)
    grandparent = jnp.sum(
        jnp.where(parent_row[:, None] == labels[None, :], parent_row[None, :], 0), axis=1
    )
    ancestor = (
        (labels[None, :] == labels[:, None])
        | (labels[None, :] == parent_row[:, None])
        | (labels[None, :] == grandparent[:, None])
    )
    return (positions, member.astype(F32), ancestor.astype(F32))


def path_mask(seg_row, parent_row, row_start, row_count):
    positions, member, ancestor = tree_layout(seg_row, parent_row)
    member_rows = lax.dynamic_slice_in_dim(member, row_start, row_count, 1)
    seg_rows = lax.dynamic_slice_in_dim(seg_row, row_start, row_count, 0)
    reach_table = jnp.dot(jnp.dot(member_rows.T, ancestor), member)
    places = jnp.arange(TREE, dtype=jnp.int32)
    row_places = row_start + jnp.arange(row_count, dtype=jnp.int32)
    same_seg = seg_rows[:, None] == seg_row[None, :]
    causal = places[None, :] <= row_places[:, None]
    allowed = (reach_table > 0.5) & (jnp.logical_not(same_seg) | causal)
    row_positions = lax.dynamic_slice_in_dim(positions, row_start, row_count, 0)
    return (allowed, row_positions)


OUTER = (((0,), (0,)), ((), ()))
INNER = (((1,), (1,)), ((), ()))


def dot(left, right):
    return jnp.dot(left, right, preferred_element_type=F32)


def dot_inner(left, right):
    return lax.dot_general(left, right, INNER, preferred_element_type=F32)


def dot_outer(left, right):
    return lax.dot_general(left, right, OUTER, preferred_element_type=F32)


def exchange(pieces, axis):
    size = lax.axis_size(axis)
    me = lax.axis_index(axis)
    got = jnp.zeros_like(pieces)
    own = lax.dynamic_index_in_dim(pieces, me, 0, keepdims=True)
    got = lax.dynamic_update_slice_in_dim(got, own, me, 0)
    for step in range(1, size):
        other = me ^ step
        piece = lax.dynamic_index_in_dim(pieces, other, 0, keepdims=True)
        arrived = lax.ppermute(piece, axis, [(i, i ^ step) for i in range(size)])
        got = lax.dynamic_update_slice_in_dim(got, arrived, other, 0)
    return got


def masked_scores(query_bf, key_all, allowed):
    raw_scores = jnp.einsum(
        "brgd,btd->bgrt", query_bf, key_all, preferred_element_type=F32
    ) * HD ** (-0.5)
    return jnp.where(allowed[:, None], raw_scores, MASKED)


MESH = pl.DeviceIdType.MESH
CHUNK = 256
SEM = pltpu.SemaphoreType.DMA
VMEM = pl.BlockSpec(memory_space=pltpu.VMEM)
HBM = pl.BlockSpec(memory_space=pl.ANY)


def remote(src, dst, send_sem, recv_sem, device_id):
    return pltpu.make_async_remote_copy(
        src_ref=src, dst_ref=dst, send_sem=send_sem, recv_sem=recv_sem,
        device_id=device_id, device_id_type=MESH,
    )


def greet(axes, across):
    barrier = pltpu.get_barrier_semaphore()
    count = 0
    for axis in axes:
        size = lax.axis_size(axis)
        me = lax.axis_index(axis)
        for step in range(1, size):
            pl.semaphore_signal(
                barrier, inc=1, device_id={axis: lax.rem(me + step, size)}, device_id_type=MESH
            )
        count += size - 1
    if across:
        size = lax.axis_size("dp")
        me = lax.axis_index("dp")
        sibling = 1 - lax.axis_index("section")
        for step in range(1, size):
            pl.semaphore_signal(
                barrier, inc=1, device_id={"section": sibling, "dp": lax.rem(me + step, size)},
                device_id_type=MESH,
            )
        count += size - 1
    pl.semaphore_wait(barrier, count)


class Part:
    ins, outs, scratch = (), (), ()

    def bind(self, ins, outs, scratch):
        self.in_refs, self.out_refs, self.refs = ins, outs, scratch

    def prepare(self):
        pass

    def start(self):
        pass

    def run(self):
        pass

    def finish(self):
        pass


def fused(parts, axes, across, collective_id, cost_us, vmem=40):
    counts = [(len(part.ins), len(part.outs), len(part.scratch)) for part in parts]

    def kernel(*refs):
        refs = list(refs)
        groups = []
        for kind in range(3):
            groups.append([])
            for count in counts:
                groups[kind].append(refs[: count[kind]])
                del refs[: count[kind]]
        for part, ins, outs, scratch in zip(parts, *groups):
            part.bind(ins, outs, scratch)
        for part in parts:
            part.prepare()
        greet(axes, across)
        for part in parts:
            part.start()
        for part in parts:
            part.run()
        for part in parts:
            part.finish()

    ins = [item for part in parts for item in part.ins]
    outs = [item for part in parts for item in part.outs]
    results = pl.pallas_call(
        kernel,
        out_shape=[item[0] for item in outs],
        in_specs=[item[1] for item in ins],
        out_specs=[item[1] for item in outs],
        scratch_shapes=[item for part in parts for item in part.scratch],
        cost_estimate=pl.CostEstimate(
            flops=0, bytes_accessed=cost_us * 3_000_000, transcendentals=0
        ),
        compiler_params=pltpu.CompilerParams(
            collective_id=collective_id, has_side_effects=True, vmem_limit_bytes=vmem << 20
        ),
    )(*[item[0] for item in ins])
    results = list(results)
    split = []
    for count in counts:
        split.append(results[: count[1]])
        del results[: count[1]]
    return split


def columns_of(place, width):
    return pl.ds(pl.multiple_of(place * width, width), width)


class UnitsOut(Part):
    def __init__(self, pieces, layer):
        self.layer = layer
        cores, self.size, mats, share, self.width = pieces.shape
        self.ins = [(pieces, HBM)]
        shape = jax.ShapeDtypeStruct((mats, share, self.size * self.width), BF16)
        self.outs = [(shape, HBM)]
        self.scratch = [SEM, SEM((cores, self.size)), SEM((self.size,))]

    def bind(self, ins, outs, scratch):
        (self.src,), (self.dst,), (self.keep, self.send, self.recv) = ins, outs, scratch
        self.core, self.me = lax.axis_index("section"), lax.axis_index("dp")

    def lands(self, slot):
        return self.dst.at[:, :, columns_of(slot, self.width)]

    def copy(self, core, place, slot):
        return remote(
            self.src.at[core, place], self.lands(slot), self.send.at[core, place],
            self.recv.at[slot], {"section": core, "dp": place},
        )

    def local(self):
        return pltpu.make_async_copy(self.src.at[self.layer, self.me], self.lands(self.me), self.keep)

    def targets(self):
        for core in range(2):
            for place in range(self.size):
                yield core, place, (place != self.me) | (core != self.layer)

    def start(self):
        @pl.when(self.core == self.layer)
        def _():
            for core, place, is_other in self.targets():
                @pl.when(is_other)
                def _():
                    self.copy(core, place, self.me).start()

            self.local().start()

    def finish(self):
        for place in range(self.size):
            @pl.when((self.core != self.layer) | (place != self.me))
            def _():
                self.copy(0, 0, place).wait_recv()

        @pl.when(self.core == self.layer)
        def _():
            for core, place, is_other in self.targets():
                @pl.when(is_other)
                def _():
                    self.copy(core, place, self.me).wait_send()

            self.local().wait()


class UnitsHome(Part):
    def __init__(self, rows, layer):
        self.layer = layer
        self.size = lax.axis_size("dp")
        mats, share, depth = rows.shape
        self.width = depth // self.size
        self.ins = [(rows, HBM)]
        shape = jax.ShapeDtypeStruct((mats, 2, self.size, share, self.width), BF16)
        self.outs = [(shape, HBM)]
        self.scratch = [SEM, SEM((self.size,)), SEM((2, self.size))]

    def bind(self, ins, outs, scratch):
        (self.src,), (self.dst,), (self.keep, self.send, self.recv) = ins, outs, scratch
        self.core, self.me = lax.axis_index("section"), lax.axis_index("dp")

    def copy(self, place, core, slot):
        return remote(
            self.src.at[:, :, columns_of(place, self.width)], self.dst.at[:, core, slot],
            self.send.at[place], self.recv.at[core, slot], {"section": self.layer, "dp": place},
        )

    def local(self):
        return pltpu.make_async_copy(
            self.src.at[:, :, columns_of(self.me, self.width)],
            self.dst.at[:, self.layer, self.me], self.keep,
        )

    def start(self):
        for place in range(self.size):
            @pl.when((self.core != self.layer) | (place != self.me))
            def _():
                self.copy(place, self.core, self.me).start()

        @pl.when(self.core == self.layer)
        def _():
            self.local().start()

    def finish(self):
        @pl.when(self.core == self.layer)
        def _():
            for core in range(2):
                for place in range(self.size):
                    @pl.when((core != self.layer) | (place != self.me))
                    def _():
                        self.copy(0, core, place).wait_recv()

            self.local().wait()

        for place in range(self.size):
            @pl.when((self.core != self.layer) | (place != self.me))
            def _():
                self.copy(place, self.core, self.me).wait_send()


class SharedRows(Part):
    def __init__(self, own):
        self.size = lax.axis_size("dp")
        self.ins = [(own, VMEM)]
        self.outs = [(jax.ShapeDtypeStruct((2, self.size) + own.shape, F32), VMEM)]
        self.scratch = [SEM((2, self.size)), SEM((2, self.size))]

    def copy(self, core, place, from_core, from_place):
        return remote(
            self.in_refs[0], self.out_refs[0].at[from_core, from_place],
            self.refs[0].at[core, place], self.refs[1].at[from_core, from_place],
            {"section": core, "dp": place},
        )

    def others(self):
        core, me = lax.axis_index("section"), lax.axis_index("dp")
        for other in range(2):
            for place in range(self.size):
                yield other, place, (other != core) | (place != me)

    def start(self):
        core, me = lax.axis_index("section"), lax.axis_index("dp")
        for other, place, is_other in self.others():
            @pl.when(is_other)
            def _():
                self.copy(other, place, core, me).start()

        self.out_refs[0][core, me] = self.in_refs[0][...]

    def finish(self):
        core, me = lax.axis_index("section"), lax.axis_index("dp")
        for other, place, is_other in self.others():
            @pl.when(is_other)
            def _():
                self.copy(other, place, other, place).wait_recv()
                self.copy(other, place, core, me).wait_send()


def far_pair(place, me):
    return (place + me == 3) & ((place == 0) | (place == 3))


def line_relays(size):
    return [(2, 0, 3), (1, 3, 0)] if size == 4 else []


def line_order(size):
    return [1, 2, 0, 3] if size == 4 else list(range(size))


class AttnOut(Part):
    def __init__(self, halves, layer):
        self.layer = layer
        self.size = lax.axis_size("dp")
        self.chunks = halves.shape[1]
        self.ins = [(halves, HBM)]
        self.outs = [(jax.ShapeDtypeStruct((self.size,) + halves.shape[1:], BF16), HBM)]
        self.scratch = [
            SEM, SEM((2, self.size, self.chunks)), SEM((self.size, self.chunks)), SEM((self.chunks,)),
        ]

    def bind(self, ins, outs, scratch):
        (self.src,), (self.dst,) = ins, outs
        self.keep, self.send, self.recv, self.relay_send = scratch
        self.core, self.me = lax.axis_index("section"), lax.axis_index("dp")

    def copy(self, core, place, slot, chunk):
        return remote(
            self.src.at[core, chunk], self.dst.at[slot, chunk], self.send.at[core, place, chunk],
            self.recv.at[slot, chunk], {"section": core, "dp": place},
        )

    def relay(self, source, target, chunk):
        return remote(
            self.dst.at[source, chunk], self.dst.at[source, chunk], self.relay_send.at[chunk],
            self.recv.at[source, chunk], {"dp": target},
        )

    def local(self):
        return pltpu.make_async_copy(self.src.at[self.layer], self.dst.at[self.me], self.keep)

    def targets(self):
        for chunk in range(self.chunks):
            for core in range(2):
                for place in range(self.size):
                    sent = (place != self.me) | (core != self.layer)
                    if self.size == 4:
                        sent = sent & jnp.logical_not(far_pair(place, self.me))
                    yield core, place, chunk, sent

    def start(self):
        @pl.when(self.core == self.layer)
        def _():
            for core, place, chunk, sent in self.targets():
                @pl.when(sent)
                def _():
                    self.copy(core, place, self.me, chunk).start()

            self.local().start()

    def run(self):
        for chunk in range(self.chunks):
            for place in line_order(self.size):
                @pl.when((self.core != self.layer) | (place != self.me))
                def _():
                    self.copy(0, 0, place, chunk).wait_recv()

                for via, source, target in line_relays(self.size):
                    if source == place:
                        @pl.when(self.me == via)
                        def _():
                            self.relay(source, target, chunk).start()

    def finish(self):
        @pl.when(self.core == self.layer)
        def _():
            for core, place, chunk, sent in self.targets():
                @pl.when(sent)
                def _():
                    self.copy(core, place, self.me, chunk).wait_send()

            self.local().wait()

        for via, source, target in line_relays(self.size):
            @pl.when(self.me == via)
            def _():
                for chunk in range(self.chunks):
                    self.relay(source, target, chunk).wait_send()


class HalfOver(Part):
    def __init__(self, halves):
        self.ins = [(halves, HBM)]
        self.outs = [(jax.ShapeDtypeStruct(halves.shape[1:], BF16), HBM)]
        self.scratch = [SEM, SEM, SEM]

    def start(self):
        self.over = remote(
            self.in_refs[0].at[0], self.out_refs[0], self.refs[0], self.refs[1], {"section": 0}
        )
        self.keep = pltpu.make_async_copy(self.in_refs[0].at[1], self.out_refs[0], self.refs[2])

        @pl.when(lax.axis_index("section") == 1)
        def _():
            self.over.start()
            self.keep.start()

    def finish(self):
        @pl.when(lax.axis_index("section") == 1)
        def _():
            self.over.wait_send()
            self.keep.wait()

        @pl.when(lax.axis_index("section") == 0)
        def _():
            self.over.wait_recv()


class Swap(Part):
    def __init__(self, own):
        self.ins = [(own, HBM)]
        self.outs = [(jax.ShapeDtypeStruct(own.shape, own.dtype), HBM)]
        self.scratch = [SEM, SEM]

    def start(self):
        sibling = 1 - lax.axis_index("section")
        self.copy = remote(
            self.in_refs[0], self.out_refs[0], self.refs[0], self.refs[1], {"section": sibling}
        )
        self.copy.start()

    def finish(self):
        self.copy.wait()


class GatherKV(Part):
    def __init__(self, own):
        trees, rows, width = own.shape
        self.trees, self.size = trees, lax.axis_size("dp")
        self.ins = [(own, VMEM)]
        self.outs = [(jax.ShapeDtypeStruct((trees, self.size, rows, width), BF16), VMEM)]
        self.scratch = [SEM((self.size, trees)), SEM((self.size, trees)), SEM((trees,))]

    def bind(self, ins, outs, scratch):
        (self.own,), (self.out,) = ins, outs
        self.send, self.recv, self.relay_send = scratch
        self.me = lax.axis_index("dp")

    def copy(self, place, slot, tree):
        return remote(
            self.own.at[tree], self.out.at[tree, slot], self.send.at[place, tree],
            self.recv.at[slot, tree], {"dp": place},
        )

    def relay(self, source, target, tree):
        return remote(
            self.out.at[tree, source], self.out.at[tree, source], self.relay_send.at[tree],
            self.recv.at[source, tree], {"dp": target},
        )

    def targets(self):
        for tree in range(self.trees):
            for place in range(self.size):
                sent = place != self.me
                if self.size == 4:
                    sent = sent & jnp.logical_not(far_pair(place, self.me))
                yield place, tree, sent

    def start(self):
        for place, tree, sent in self.targets():
            @pl.when(sent)
            def _():
                self.copy(place, self.me, tree).start()

        self.out[:, self.me] = self.own[...]

    def run(self):
        for tree in range(self.trees):
            for place in line_order(self.size):
                @pl.when(place != self.me)
                def _():
                    self.copy(place, place, tree).wait_recv()

                for via, source, target in line_relays(self.size):
                    if source == place:
                        @pl.when(self.me == via)
                        def _():
                            self.relay(source, target, tree).start()

    def finish(self):
        for place, tree, sent in self.targets():
            @pl.when(sent)
            def _():
                self.copy(place, self.me, tree).wait_send()

        for via, source, target in line_relays(self.size):
            @pl.when(self.me == via)
            def _():
                for tree in range(self.trees):
                    self.relay(source, target, tree).wait_send()


class ScatterKV(Part):
    def __init__(self, whole):
        trees, size, rows, width = whole.shape
        self.trees, self.size = trees, size
        self.sides = [(0, 1, 3), (3, 2, 0)] if size == 4 else []
        self.ins = [(whole, VMEM)]
        self.outs = [(jax.ShapeDtypeStruct((trees, rows, width), F32), VMEM)]
        self.scratch = [
            pltpu.VMEM((size, trees, rows, width), BF16), pltpu.VMEM((trees, rows, width), BF16),
            SEM((size, trees)), SEM((size, trees)), SEM((trees,)), SEM((trees,)),
        ]

    def bind(self, ins, outs, scratch):
        (self.terms,), (self.out,) = ins, outs
        self.boxes, self.joint, self.send, self.recv, self.join_send, self.join_recv = scratch
        self.me = lax.axis_index("dp")

    def copy(self, place, slot, tree):
        return remote(
            self.terms.at[tree, place], self.boxes.at[slot, tree], self.send.at[place, tree],
            self.recv.at[slot, tree], {"dp": place},
        )

    def by_way(self, via, target, tree):
        return remote(
            self.terms.at[tree, target], self.joint.at[tree], self.join_send.at[tree],
            self.join_recv.at[tree], {"dp": via},
        )

    def joined(self, via, target, tree):
        return remote(
            self.joint.at[tree], self.boxes.at[via, tree], self.send.at[target, tree],
            self.recv.at[via, tree], {"dp": target},
        )

    def plain(self, place):
        ok = place != self.me
        for source, via, target in self.sides:
            if place == target:
                ok = ok & (self.me != source) & (self.me != via)
        return ok

    def expected(self, place):
        ok = place != self.me
        for source, via, target in self.sides:
            if place == source:
                ok = ok & (self.me != target)
        return ok

    def start(self):
        for tree in range(self.trees):
            for source, via, target in self.sides:
                @pl.when(self.me == source)
                def _():
                    self.by_way(via, target, tree).start()

            for place in range(self.size):
                @pl.when(self.plain(place))
                def _():
                    self.copy(place, self.me, tree).start()

    def run(self):
        for tree in range(self.trees):
            for source, via, target in self.sides:
                @pl.when(self.me == via)
                def _():
                    self.by_way(via, target, tree).wait_recv()
                    both = self.joint[tree].astype(F32) + self.terms[tree, target].astype(F32)
                    self.joint[tree] = both.astype(BF16)
                    self.joined(via, target, tree).start()

        for tree in range(self.trees):
            self.out[tree] = self.terms[tree, self.me].astype(F32)
            for place in line_order(self.size):
                @pl.when(self.expected(place))
                def _():
                    self.copy(place, place, tree).wait_recv()
                    self.out[tree] += self.boxes[place, tree].astype(F32)

    def finish(self):
        for tree in range(self.trees):
            for place in range(self.size):
                @pl.when(self.plain(place))
                def _():
                    self.copy(place, self.me, tree).wait_send()

            for source, via, target in self.sides:
                @pl.when(self.me == source)
                def _():
                    self.by_way(via, target, tree).wait_send()

                @pl.when(self.me == via)
                def _():
                    self.joined(via, target, tree).wait_send()


class TotalOverAll(Part):
    axes = ("section", "tensor", "dp")

    def __init__(self, own):
        sizes = [lax.axis_size(axis) for axis in self.axes]
        self.ins = [(own, VMEM)]
        self.outs = [(jax.ShapeDtypeStruct(own.shape, F32), VMEM)]
        self.scratch = [pltpu.VMEM((size,) + own.shape, F32) for size in sizes]
        self.scratch += [SEM((size,)) for size in sizes] * 2

    def run(self):
        out = self.out_refs[0]
        out[...] = self.in_refs[0][...]
        for axis, box, send, recv in zip(self.axes, self.refs[:3], self.refs[3:6], self.refs[6:9]):
            size, me = lax.axis_size(axis), lax.axis_index(axis)
            box[me] = out[...]

            def spread(place, slot):
                return remote(box.at[me], box.at[slot], send.at[place], recv.at[slot], {axis: place})

            for place in range(size):
                @pl.when(place != me)
                def _():
                    spread(place, me).start()

            for place in range(size):
                @pl.when(place != me)
                def _():
                    spread(place, place).wait_recv()
                    spread(place, me).wait_send()

            total = box[0]
            for place in range(1, size):
                total += box[place]
            out[...] = total


class Gatherer:
    def __init__(self, axis, rows, half):
        self.axis, self.rows, self.half = axis, rows, half
        self.size = size = lax.axis_size(axis)
        self.scratch = [pltpu.VMEM((2, size, 2 * rows, half), BF16)]
        self.scratch += [SEM((size,))] * 4 + [SEM]

    def bind(self, refs):
        self.board, self.send, self.recv, self.sib_send, self.sib_recv, self.relay_send = refs
        self.core = lax.axis_index("section")
        self.sibling = 1 - self.core
        self.me = lax.axis_index(self.axis)
        self.relays = line_relays(self.size) if self.axis == "dp" else []

    def direct(self, place):
        sent = place != self.me
        if self.relays:
            sent = sent & jnp.logical_not(far_pair(place, self.me))
        return sent

    def spread(self, place, slot):
        return remote(
            self.board.at[self.core, slot], self.board.at[self.core, slot], self.send.at[place],
            self.recv.at[slot], {self.axis: place},
        )

    def passed(self, source, target):
        return remote(
            self.board.at[self.core, source], self.board.at[self.core, source], self.relay_send,
            self.recv.at[source], {self.axis: target},
        )

    def over(self, tree, slot):
        return remote(
            self.board.at[tree, slot], self.board.at[tree, slot], self.sib_send.at[slot],
            self.sib_recv.at[slot], {"section": self.sibling},
        )

    def begin(self, result):
        half = self.half
        piece = jnp.concatenate([result[:, :half], result[:, half:]], axis=0)
        self.board[self.core, self.me] = piece.astype(BF16)
        for place in range(self.size):
            @pl.when(self.direct(place))
            def _():
                self.spread(place, self.me).start()

        self.over(self.core, self.me).start()

    def arrive(self, place):
        @pl.when(place != self.me)
        def _():
            self.spread(place, place).wait_recv()

        for via, source, target in self.relays:
            @pl.when((self.me == via) & (place == source))
            def _():
                self.passed(source, target).start()

        @pl.when(place != self.me)
        def _():
            self.over(self.core, place).start()

    def arrive_over(self, place):
        self.over(self.sibling, place).wait_recv()

    def unpack(self, out, tree):
        rows = self.rows

        @pl.loop(0, self.half // CHUNK)
        def _(step):
            at = pl.multiple_of(step * CHUNK, CHUNK)
            blocks = [
                self.board[tree, place, :, pl.ds(at, CHUNK)].astype(F32)
                for place in range(self.size)
            ]
            for side in range(2):
                whole = [block[side * rows : (side + 1) * rows] for block in blocks]
                out[tree, :, pl.ds(side * self.half + at, CHUNK)] = jnp.concatenate(
                    whole, axis=0
                ).astype(BF16)

    def unpack_place(self, out, place):
        rows = self.rows

        @pl.loop(0, self.half // CHUNK)
        def _(step):
            at = pl.multiple_of(step * CHUNK, CHUNK)
            blocks = [self.board[tree, place, :, pl.ds(at, CHUNK)].astype(F32) for tree in range(2)]
            for side in range(2):
                whole = [block[side * rows : (side + 1) * rows] for block in blocks]
                out[place, :, pl.ds(side * self.half + at, CHUNK)] = jnp.concatenate(
                    whole, axis=0
                ).astype(BF16)

    def complete(self, out):
        for place in range(self.size):
            self.arrive(place)
        self.unpack(out, self.core)
        for place in range(self.size):
            self.arrive_over(place)
        self.unpack(out, self.sibling)

    def finish(self):
        for place in range(self.size):
            @pl.when(self.direct(place))
            def _():
                self.spread(place, self.me).wait_send()

            self.over(self.core, place).wait_send()

        for via, source, target in self.relays:
            @pl.when(self.me == via)
            def _():
                self.passed(source, target).wait_send()


class Scatterer:
    def __init__(self, axis, rows, half):
        self.axis, self.rows, self.half = axis, rows, half
        self.size = size = lax.axis_size(axis)
        self.scratch = [pltpu.VMEM((size, 2 * rows, half), BF16)] * 4
        self.scratch += [pltpu.VMEM((2 * rows, half), F32)] + [SEM((size,))] * 4

    def bind(self, refs):
        self.to_sib, self.from_sib, self.to_peer, self.from_peer, self.total = refs[:5]
        self.sib_send, self.sib_recv, self.peer_send, self.peer_recv = refs[5:]
        self.core = lax.axis_index("section")
        self.sibling = 1 - self.core
        self.me = lax.axis_index(self.axis)

    def over(self, place):
        return remote(
            self.to_sib.at[place], self.from_sib.at[place], self.sib_send.at[place],
            self.sib_recv.at[place], {"section": self.sibling},
        )

    def spread(self, place, slot):
        return remote(
            self.to_peer.at[place], self.from_peer.at[slot], self.peer_send.at[place],
            self.peer_recv.at[slot], {self.axis: place},
        )

    def over_columns(self, body):
        @pl.loop(0, self.half // CHUNK)
        def _(step):
            body(pl.multiple_of(step * CHUNK, CHUNK))

    def absorb(self, place, mine):
        self.over(place).wait_recv()

        def add(at):
            both = mine(at) + self.from_sib[place, :, pl.ds(at, CHUNK)].astype(F32)
            self.to_peer[place, :, pl.ds(at, CHUNK)] = both.astype(BF16)

            @pl.when(place == self.me)
            def _():
                self.total[:, pl.ds(at, CHUNK)] = both

        self.over_columns(add)

        @pl.when(place != self.me)
        def _():
            self.spread(place, self.me).start()

    def collect(self):
        for place in range(self.size):
            @pl.when(place != self.me)
            def _():
                self.spread(place, place).wait_recv()
                self.total[...] += self.from_peer[place].astype(F32)

        total = self.total[...]
        return jnp.concatenate([total[: self.rows], total[self.rows :]], axis=1)

    def finish(self):
        for place in range(self.size):
            self.over(place).wait_send()

            @pl.when(place != self.me)
            def _():
                self.spread(place, self.me).wait_send()


class RowScatterer(Scatterer):
    def packed(self, tree, place, at):
        rows = self.rows
        low = rows * place // 16 * 16
        high = -(-rows * (place + 1) // 16) * 16
        skip = rows * place - low
        parts = [
            self.terms[tree, low:high, pl.ds(side * self.half + at, CHUNK)].astype(F32)[
                skip : skip + rows
            ]
            for side in range(2)
        ]
        return jnp.concatenate(parts, axis=0)

    def prepare(self, terms):
        self.terms = terms
        for place in range(self.size):
            def pack(at):
                self.to_sib[place, :, pl.ds(at, CHUNK)] = self.packed(
                    self.sibling, place, at
                ).astype(BF16)

            self.over_columns(pack)

    def start(self):
        for place in range(self.size):
            self.over(place).start()

    def summed(self):
        for place in range(self.size):
            self.absorb(place, lambda at: self.packed(self.core, place, at))
        return self.collect()


class Staged(Part):
    def __init__(self, ins, outs, scratch, helpers):
        self.in_names, self.out_names, self.scratch_names = list(ins), list(outs), list(scratch)
        self.ins, self.outs = list(ins.values()), list(outs.values())
        self.helpers = helpers
        self.scratch = list(scratch.values())
        for helper in helpers:
            self.scratch += helper.scratch

    def bind(self, ins, outs, scratch):
        scratch = list(scratch)
        names = self.in_names + self.out_names + self.scratch_names
        count = len(self.scratch_names)
        for name, ref in zip(names, list(ins) + list(outs) + scratch[:count]):
            setattr(self, name, ref)
        del scratch[:count]
        for helper in self.helpers:
            helper.bind(scratch[: len(helper.scratch)])
            del scratch[: len(helper.scratch)]

    def finish(self):
        for helper in self.helpers:
            helper.finish()


def vmem_f32(*shape):
    return (jax.ShapeDtypeStruct(shape, F32), VMEM)


def vmem_bf16(*shape):
    return (jax.ShapeDtypeStruct(shape, BF16), VMEM)


class LastHub(Staged):
    def __init__(self, terms, values, gain, add):
        rows, depth = values.shape
        half = depth // 2
        self.rows_in = RowScatterer("tensor", rows, half)
        self.rows_out = Gatherer("tensor", rows, half)
        super().__init__(
            {"terms": (terms, VMEM), "values": (values, VMEM), "gain": (gain, VMEM), "add": (add, VMEM)},
            {
                "gain_grad": vmem_f32(1, depth),
                "gathered": vmem_bf16(2, self.rows_out.size * rows, depth),
            },
            {},
            [self.rows_in, self.rows_out],
        )

    def prepare(self):
        self.rows_in.prepare(self.terms)

    def start(self):
        self.rows_in.start()

    def run(self):
        total = self.rows_in.summed()
        result, self.gain_grad[...] = norm_back(total, self.values[...], self.gain[...])
        self.rows_out.begin(result + self.add[...])
        self.rows_out.complete(self.gathered)


class FeedForward(Staged):
    def __init__(self, terms, own, gain, weights, forward, backward, extra):
        rows, depth = own.shape
        half = depth // 2
        units = weights[0].shape[0]
        self.has_forward, self.has_backward, self.units = forward, backward, units
        self.depth = depth
        self.block = 2 * rows
        self.size = size = lax.axis_size("dp")
        self.rows_in = RowScatterer("tensor", rows, half)
        self.spread_in = Gatherer("dp", rows, half)
        helpers = [self.rows_in, self.spread_in]
        group_rows = 2 * rows
        tensor_rows = lax.axis_size("tensor") * rows
        matrix = pltpu.VMEM((units, depth), BF16)
        ins = {"terms": (terms, VMEM), "own": (own, VMEM), "gain": (gain, VMEM)}
        ins |= {name: (w, HBM) for name, w in zip(("gate_hbm", "up_hbm", "down_hbm"), weights)}
        ins |= {name: (value, VMEM) for name, value in extra.items()}
        outs = {}
        scratch = {"w_gate": matrix, "w_up": matrix, "w_down": matrix, "load": SEM((3,))}
        if forward:
            outs |= {
                "middle": vmem_f32(rows, depth),
                "mlp_in": vmem_bf16(size, group_rows, depth),
                "hidden": vmem_bf16(size, group_rows, units),
                "own_out": vmem_f32(rows, depth),
                "out": vmem_bf16(2, tensor_rows, depth),
            }
            self.back = Scatterer("dp", rows, half)
            self.out_rows = Gatherer("tensor", rows, half)
            helpers += [self.back, self.out_rows]
            scratch["kept"] = pltpu.VMEM((group_rows, half), F32)
        if forward and not backward:
            outs |= {"gate": vmem_f32(size, group_rows, units), "up": vmem_f32(size, group_rows, units)}
        if forward and backward:
            scratch |= {
                "gate": pltpu.VMEM((size, group_rows, units), F32),
                "up": pltpu.VMEM((size, group_rows, units), F32),
            }
        if backward:
            outs |= {
                "grad_gate": vmem_bf16(size, group_rows, units),
                "grad_up": vmem_bf16(size, group_rows, units),
                "grad_middle": vmem_f32(rows, depth),
                "mlp_gain_grad": vmem_f32(1, depth),
                "grad_attn": vmem_bf16(2, tensor_rows, depth),
            }
            self.grad_back = Scatterer("dp", rows, half)
            self.grad_rows = Gatherer("tensor", rows, half)
            helpers += [self.grad_back, self.grad_rows]
            scratch["grad_kept"] = pltpu.VMEM((group_rows, half), F32)
        if backward and not forward:
            outs |= {
                "gain_grad": vmem_f32(1, depth),
                "incoming": vmem_bf16(2, tensor_rows, depth),
                "grad_mlp": vmem_bf16(size, group_rows, depth),
            }
            scratch["grad_own"] = pltpu.VMEM((rows, depth), F32)
            self.incoming_rows = Gatherer("tensor", rows, half)
            helpers += [self.incoming_rows]
        super().__init__(ins, outs, scratch, helpers)

    def loads(self):
        pairs = [(self.gate_hbm, self.w_gate), (self.up_hbm, self.w_up), (self.down_hbm, self.w_down)]
        return [
            pltpu.make_async_copy(src, dst, self.load.at[i]) for i, (src, dst) in enumerate(pairs)
        ]

    def prepare(self):
        for copy in self.loads():
            copy.start()
        self.rows_in.prepare(self.terms)

    def start(self):
        self.rows_in.start()

    def run(self):
        total = self.rows_in.summed()
        if self.has_forward:
            middle = self.own[...] + total
            self.middle[...] = middle
            mean_sq = jnp.mean(middle * middle, axis=1, keepdims=True)
            self.spread_in.begin(middle * lax.rsqrt(mean_sq + EPSILON) * self.gain[...])
        else:
            result, self.gain_grad[...] = norm_back(total, self.own[...], self.gain[...])
            result = (result + self.add[...]).astype(BF16).astype(F32)
            self.grad_own[...] = result
            self.spread_in.begin(result)
            self.incoming_rows.begin(result)
        for copy in self.loads():
            copy.wait()

        me = lax.axis_index("dp")
        turn = 1 - 2 * (me // (self.size // 2))

        @pl.loop(0, self.size)
        def _(step):
            place = lax.rem(me + turn * step + self.size, self.size)
            self.spread_in.arrive(place)
            self.spread_in.arrive_over(place)
            if self.has_forward:
                self.spread_in.unpack_place(self.mlp_in, place)
                self.forward_place(place)
            else:
                self.spread_in.unpack_place(self.grad_mlp, place)
            if self.has_backward:
                self.backward_place(place)
            if self.has_forward:
                self.back.absorb(place, lambda at: self.kept[:, pl.ds(at, CHUNK)])
            if self.has_backward:
                self.grad_back.absorb(place, lambda at: self.grad_kept[:, pl.ds(at, CHUNK)])

        if self.has_forward:
            output = (self.middle[...] + self.back.collect()).astype(BF16).astype(F32)
            self.own_out[...] = output
            if not self.has_backward:
                self.out_rows.begin(output)
        if self.has_backward:
            values = self.middle if self.has_forward else self.middle_in
            gain = self.gain if self.has_forward else self.mlp_gain
            result, self.mlp_gain_grad[...] = norm_back(
                self.grad_back.collect(), values[...], gain[...]
            )
            result += self.grad_own[...]
            self.grad_middle[...] = result
            self.grad_rows.begin(result)
            if self.has_forward:
                self.out_rows.begin(self.own_out[...])
            self.grad_rows.complete(self.grad_attn)
        if self.has_forward:
            self.out_rows.complete(self.out)
        else:
            self.incoming_rows.complete(self.incoming)

    def unit_tiles(self, body):
        tile = 256

        @pl.loop(0, self.units // tile)
        def _(step):
            body(pl.ds(pl.multiple_of(step * tile, tile), tile))

    def forward_place(self, place):
        def tile(at):
            rows = self.mlp_in[place]
            gate = dot_inner(rows, self.w_gate[at, :])
            up = dot_inner(rows, self.w_up[at, :])
            self.gate[place, :, at] = gate
            self.up[place, :, at] = up
            self.hidden[place, :, at] = (gate * jax.nn.sigmoid(gate) * up).astype(BF16)

        self.unit_tiles(tile)
        self.terms_out(
            place, self.back, self.kept, lambda at: dot(self.hidden[place], self.w_down[:, at])
        )

    def backward_place(self, place):
        def tile(at):
            grad_hidden = dot_inner(self.grad_mlp[place], self.w_down[at, :])
            gate, up = self.gate[place, :, at], self.up[place, :, at]
            share = jax.nn.sigmoid(gate)
            act = gate * share
            self.grad_up[place, :, at] = (grad_hidden * act).astype(BF16)
            self.grad_gate[place, :, at] = (
                grad_hidden * up * (share + act * (1.0 - share))
            ).astype(BF16)

        self.unit_tiles(tile)
        self.terms_out(
            place, self.grad_back, self.grad_kept,
            lambda at: dot(self.grad_gate[place], self.w_gate[:, at])
            + dot(self.grad_up[place], self.w_up[:, at]),
        )

    def terms_out(self, place, scatterer, kept, product):
        rows, half = self.block // 2, self.depth // 2
        first = lax.axis_index("section") == 0

        @pl.loop(0, half // CHUNK)
        def _(step):
            low = pl.multiple_of(step * CHUNK, CHUNK)
            sides = [product(pl.ds(side * half + low, CHUNK)) for side in range(2)]
            trees = [
                jnp.concatenate([side[tree * rows : (tree + 1) * rows] for side in sides], axis=0)
                for tree in range(2)
            ]
            at = pl.ds(low, CHUNK)
            kept[:, at] = jnp.where(first, trees[0], trees[1])
            scatterer.to_sib[place, :, at] = jnp.where(first, trees[1], trees[0]).astype(BF16)

        scatterer.over(place).start()


def hub_plain(terms, own_args, body, own_outs, scatter, gathers):
    total = None
    if scatter:
        mine = lax.psum_scatter(terms, "section", scatter_dimension=0, tiled=True)
        mine = lax.psum_scatter(mine, scatter, scatter_dimension=1, tiled=True)[0]
        total = mine.astype(F32)

    class Cell:
        def __setitem__(self, _, value):
            self.value = value

    cells = [Cell() for _ in own_outs]
    result = body(total, own_args, cells).astype(BF16)
    gathered = [
        lax.all_gather(lax.all_gather(result, axis, axis=0, tiled=True), "section", axis=0)
        for axis in gathers
    ]
    return [cell.value for cell in cells] + gathered


def with_cargo(part, cargo, axes, collective_id, cost_us, vmem=40):
    outs = fused(cargo + [part], axes, bool(cargo), collective_id, cost_us, vmem)
    return outs[-1], outs[:-1]


def norm_back(total, values, gain):
    scale = lax.rsqrt(jnp.mean(values * values, axis=1, keepdims=True) + EPSILON)
    unit = values * scale
    gain_grad = jnp.sum(total * unit, axis=0, keepdims=True)
    scaled = total * gain
    along = jnp.mean(scaled * unit, axis=1, keepdims=True)
    return ((scaled - unit * along) * scale, gain_grad)


def norm_body(total, args, outs):
    middle = args[0] + total
    outs[0][...] = middle
    return rms_scale(middle, args[1])


def add_body(total, args, outs):
    result = args[0] + total
    outs[0][...] = result
    return result


def norm_back_body(total, args, outs):
    result, outs[1][...] = norm_back(total, args[0], args[1])
    result += args[2]
    outs[0][...] = result
    return result


def embed(q_pre, k_pre, q_scale, k_scale, cos_table, sine_table):
    queries = rms_scale(q_pre, q_scale)
    keys = rms_scale(k_pre, k_scale)
    return (
        rotate(queries, cos_table[:, :, None], sine_table[:, :, None]),
        rotate(keys, cos_table, sine_table),
    )


def attn_forward(hidden_in, weights, gains, slot, gather):
    attn_scale, _, q_scale, k_scale = gains
    w_qkv, w_outt = weights[:2]
    allowed, cos_table, sine_table = slot
    trees, row_count, depth = hidden_in.shape
    q_width = w_outt.shape[1]
    normed = rms_scale(hidden_in.astype(F32), attn_scale).astype(BF16).reshape(-1, depth)
    qkv = dot(normed, w_qkv).reshape(trees, row_count, -1)
    q_pre = qkv[:, :, :q_width].reshape(trees, row_count, -1, HD)
    k_pre = qkv[:, :, q_width : q_width + HD]
    value_bf = qkv[:, :, q_width + HD :].astype(BF16)
    queries, keys_rot = embed(q_pre, k_pre, q_scale, k_scale, cos_table, sine_table)
    query_bf = queries.astype(BF16)
    kv_all = gather(jnp.concatenate([keys_rot.astype(BF16), value_bf], axis=2))
    key_all = kv_all[:, :, :HD]
    value_all = kv_all[:, :, HD:]
    scores = masked_scores(query_bf, key_all, allowed)
    row_max = jnp.max(scores, axis=-1, keepdims=True)
    exp_scores = jnp.exp(scores - row_max)
    row_total = jnp.sum(exp_scores, axis=-1, keepdims=True)
    prob_bf = (exp_scores / row_total).astype(BF16)
    log_total = row_max + jnp.log(row_total)
    attended = jnp.einsum("bgrt,btd->brgd", prob_bf, value_all, preferred_element_type=F32)
    attended_bf = attended.reshape(trees * row_count, -1).astype(BF16)
    terms = dot_inner(attended_bf, w_outt).astype(BF16).reshape(trees, row_count, depth)
    saved = (normed, q_pre, k_pre, query_bf, key_all, value_all, log_total, attended_bf)
    return (terms, saved)


def attn_backward(grad_attn, saved, weights, gains, slot, scatter):
    _, _, q_scale, k_scale = gains
    w_qkv, w_outt = weights[:2]
    allowed, cos_table, sine_table = slot
    normed, q_pre, k_pre, query_bf, key_all, value_all, log_total, attended_bf = saved
    trees, row_count = query_bf.shape[:2]
    depth = normed.shape[1]
    grad_attn = grad_attn.reshape(-1, depth)
    grad_heads = dot(grad_attn, w_outt).astype(BF16).reshape(query_bf.shape)
    scores = masked_scores(query_bf, key_all, allowed)
    prob_full = jnp.exp(scores - log_total)
    grad_prob = jnp.einsum("brgd,btd->bgrt", grad_heads, value_all, preferred_element_type=F32)
    row_dot = jnp.sum(prob_full * grad_prob, axis=-1, keepdims=True)
    grad_scores = (prob_full * (grad_prob - row_dot)).astype(BF16)
    scale_factor = HD ** (-0.5)
    grad_query = (
        jnp.einsum("bgrt,btd->brgd", grad_scores, key_all, preferred_element_type=F32)
        * scale_factor
    )
    grad_key_all = (
        jnp.einsum("bgrt,brgd->btd", grad_scores, query_bf, preferred_element_type=F32)
        * scale_factor
    )
    grad_value_all = jnp.einsum(
        "bgrt,brgd->btd", prob_full.astype(BF16), grad_heads, preferred_element_type=F32
    )
    grad_kv = scatter(jnp.concatenate([grad_key_all, grad_value_all], axis=2).astype(BF16))
    _, embedding_pull = jax.vjp(
        partial(embed, cos_table=cos_table, sine_table=sine_table), q_pre, k_pre, q_scale, k_scale
    )
    grad_q_pre, grad_k_pre, grad_q_scale, grad_k_scale = embedding_pull(
        (grad_query, grad_kv[:, :, :HD].astype(F32))
    )
    qkv_grad = jnp.concatenate(
        [
            grad_q_pre.astype(BF16).reshape(trees, row_count, -1),
            grad_k_pre.astype(BF16),
            grad_kv[:, :, HD:].astype(BF16),
        ],
        axis=2,
    ).reshape(trees * row_count, -1)
    terms = dot_inner(qkv_grad, w_qkv).astype(BF16).reshape(trees, row_count, depth)
    return (terms, [(normed, qkv_grad), (grad_attn, attended_bf)], [grad_q_scale, grad_k_scale])


def plain_layers(hidden, own_in, grad_own, weights, gains, slot, shared_kv):
    depth = own_in.shape[1]
    own_shape = own_in.shape

    def gather(own):
        return lax.all_gather(own, "dp", axis=1, tiled=True)

    def scatter(whole):
        total = lax.psum_scatter(whole, "dp", scatter_dimension=1, tiled=True)
        if shared_kv:
            total = lax.psum(total, "section")
            total = jnp.where(lax.axis_index("section") == 0, total, jnp.zeros_like(total))
        return total

    outputs, kept = [], []
    for layer in range(2):
        _, _, w_gate, w_up, w_down = weights[layer]
        terms, saved = attn_forward(hidden, weights[layer], gains[layer], slot, gather)
        mlp_scale = gains[layer][1][None]
        middle, mlp_in = hub_plain(
            terms, [own_in, mlp_scale], norm_body, [own_shape], "tensor", ["dp"]
        )
        mlp_in = mlp_in.reshape(-1, depth)
        gate, up = dot_inner(mlp_in, w_gate), dot_inner(mlp_in, w_up)
        hidden_bf = swiglu(gate, up).astype(BF16)
        terms = dot(hidden_bf, w_down).astype(BF16).reshape(2, -1, depth)
        kept.append((own_in, saved, middle, mlp_in, gate, up, hidden_bf))
        own_in, hidden = hub_plain(terms, [middle], add_body, [own_shape], "dp", ["tensor"])
        own_in = own_in.astype(BF16).astype(F32)
        outputs.append(hidden)

    own_outs = [own_shape, (1, depth)]
    grads, products, gain_grads = [None, None], [None, None], [None, None]
    (grad_mlp,) = hub_plain(None, [grad_own], lambda total, args, outs: args[0], [], None, ["dp"])
    for layer in (1, 0):
        _, _, w_gate, w_up, w_down = weights[layer]
        own_in, saved, middle, mlp_in, gate, up, hidden_bf = kept[layer]
        grad_mlp = grad_mlp.reshape(-1, depth)
        _, pull = jax.vjp(swiglu, gate, up)
        grad_gate, grad_up = (item.astype(BF16) for item in pull(dot_inner(grad_mlp, w_down)))
        terms = (dot(grad_gate, w_gate) + dot(grad_up, w_up)).astype(BF16).reshape(2, -1, depth)
        grad_middle, mlp_gain_grad, grad_attn = hub_plain(
            terms, [middle, gains[layer][1][None], grad_own], norm_back_body, own_outs, "dp",
            ["tensor"],
        )
        terms, pairs, head_grads = attn_backward(
            grad_attn, saved, weights[layer], gains[layer], slot, scatter
        )
        grad_own, gain_grad, grads[layer], grad_next = hub_plain(
            terms, [own_in, gains[layer][0][None], grad_middle], norm_back_body, own_outs, "tensor",
            ["tensor", "dp"],
        )
        grad_own = grad_own.astype(BF16).astype(F32)
        pairs += [(grad_gate, mlp_in), (grad_up, mlp_in), (hidden_bf, grad_mlp)]
        products[layer] = pairs
        gain_grads[layer] = jnp.concatenate([gain_grad[0], mlp_gain_grad[0], *head_grads])
        grad_mlp = grad_next
    return (outputs, grads, products, gain_grads)


def swap_cores(mine, other):
    core = lax.axis_index("section")
    arrived = lax.ppermute(other, "section", [(0, 1), (1, 0)])
    return (jnp.where(core == 0, mine, arrived), jnp.where(core == 0, arrived, mine))


def on_device(
    inputs, cotangent, seg_ids, parents, order, attn_gain, w_query, w_key, w_value, w_out,
    q_gain, k_gain, mlp_gain, w_gate, w_up, w_down,
):
    core = lax.axis_index("section")
    data_index = lax.axis_index("dp")
    tensor_index = lax.axis_index("tensor")
    dp_size = lax.axis_size("dp")
    tensor_size = lax.axis_size("tensor")
    trees, row_count, depth = inputs.shape
    own_rows = row_count // tensor_size
    row_start = data_index * row_count
    own_depth = w_query.shape[1]
    q_width = w_query.shape[2] // 2
    shared_kv = w_key.shape[2] == HD
    k_width = HD if shared_kv else w_key.shape[2] // 2
    own_units = w_gate.shape[2]
    share = own_units // (2 * dp_size)

    def pick(stacked, index):
        return lax.dynamic_index_in_dim(stacked, index, 0, keepdims=False)

    fast = (
        own_rows % 8 == 0
        and depth % (2 * CHUNK) == 0
        and row_count % 16 == 0
        and share % 16 == 0
        and own_depth % 128 == 0
        and not shared_kv
    )

    def halves(width, array):
        return [array[:, :width], array[:, array.shape[1] - width :]]

    attn_halves = jnp.stack(
        [
            jnp.concatenate(parts, axis=1)
            for parts in zip(
                halves(q_width, w_query[0]),
                halves(k_width, w_key[0]),
                halves(k_width, w_value[0]),
                halves(q_width, w_out[0].T),
            )
        ]
    )
    unit_blocks = jnp.stack([w_gate[0].T, w_up[0].T, w_down[0]]).reshape(
        3, 2, dp_size, share, own_depth
    )
    unit_blocks = unit_blocks.transpose(1, 2, 0, 3, 4)
    qkv_width = q_width + 2 * k_width
    gains_own = jnp.concatenate([attn_gain[0], mlp_gain[0], q_gain[0], k_gain[0]]).astype(F32)

    def spread_units(rows):
        return lax.all_gather(rows, "tensor", axis=0, tiled=True)

    def attn_of(whole):
        whole = whole.reshape(depth, -1)
        return (whole[:, :qkv_width], whole[:, qkv_width:])

    def joint(gate_up, down):
        return (spread_units(gate_up[0]), spread_units(gate_up[1]), spread_units(down[0]))

    if fast:
        group = ["section", "dp"]
        (gate_up,), (gains_all,) = fused(
            [
                UnitsOut(unit_blocks[:, :, :2], 0),
                SharedRows(gains_own.reshape(-1, 128)),
            ],
            group, True, 1, 45,
        )
        attn_chunks = attn_halves.reshape(2, 4, own_depth // 4, -1)
        attn_chunks, gate_up = lax.optimization_barrier((attn_chunks, gate_up))
        (attn_all,), (down,), (attn_shard,) = fused(
            [
                AttnOut(attn_chunks, 0), UnitsOut(unit_blocks[:, :, 2:], 0), HalfOver(attn_chunks),
            ],
            group, True, 2, 80,
        )
        attn_next = lax.all_gather(attn_shard.reshape(own_depth, -1), "dp", axis=0, tiled=True)
        first_weights = attn_of(attn_all) + joint(gate_up, down)
    else:
        gains_all = lax.all_gather(gains_own, ("section", "dp"))
        attn_shards = swap_cores(pick(attn_halves, core), pick(attn_halves, 1 - core))
        unit_shards = swap_cores(pick(unit_blocks, core), pick(unit_blocks, 1 - core))
        both_weights = []
        for layer in range(2):
            attn_all = lax.all_gather(attn_shards[layer], "dp", axis=0, tiled=True)
            pieces = exchange(unit_shards[layer], "dp")
            pieces = pieces.transpose(1, 2, 0, 3).reshape(3, share, depth)
            both_weights.append(attn_of(attn_all) + joint(pieces[:2], pieces[2:]))

    gains_all = gains_all.reshape(2, dp_size, -1)
    gains = [
        (
            gains_all[layer, :, :own_depth].reshape(depth),
            gains_all[layer, :, own_depth : 2 * own_depth].reshape(depth),
            gains_all[layer, 0, 2 * own_depth : 2 * own_depth + HD],
            gains_all[layer, 0, 2 * own_depth + HD :],
        )
        for layer in range(2)
    ]

    def slot_setup(slot_index):
        tree_id = pick(order, slot_index)
        allowed, row_positions = path_mask(
            pick(seg_ids, tree_id), pick(parents, tree_id), row_start, row_count
        )
        cos_table, sine_table = rope_tables(row_positions, HD)
        return (pick(inputs, tree_id), allowed, cos_table[:, 0], sine_table[:, 0])

    setups = [slot_setup(i) for i in range(trees)]
    hidden, *slot = (jnp.stack(item) for item in zip(*setups))

    def own_part(whole):
        return lax.dynamic_slice_in_dim(
            pick(whole, core), tensor_index * own_rows, own_rows, 0
        )

    own_in = own_part(hidden).astype(F32)
    grad_own = own_part(cotangent).astype(F32)

    def weight_products(pairs):
        return [dot_outer(left, right).astype(BF16) for left, right in pairs]

    def scatter_units(products):
        return jnp.stack(
            [lax.psum_scatter(item, "tensor", scatter_dimension=0, tiled=True) for item in products]
        )

    def scatter_shards(products):
        return lax.psum_scatter(
            jnp.concatenate(products, axis=1), "dp", scatter_dimension=0, tiled=True
        )

    if fast:
        line = ["section", "dp"]
        everyone = ["section", "dp", "tensor"]

        def units_on(index):
            return [UnitsOut(unit_blocks[:, :, index : index + 1], 1)]

        def kv_gather(own, cargo, collective_id, carried):
            (whole,), outs = with_cargo(GatherKV(own), cargo, line, collective_id, 30)
            carried += outs
            return whole.reshape(trees, -1, 2 * HD)

        def kv_scatter(whole, cargo, collective_id, carried):
            part = ScatterKV(whole.reshape(trees, dp_size, row_count, 2 * HD))
            (total,), outs = with_cargo(part, cargo, line, collective_id, 30)
            carried += outs
            return total

        def flat(array):
            return array.reshape(-1, array.shape[-1])

        carried = []
        terms, saved_first = attn_forward(
            hidden, first_weights, gains[0], slot,
            lambda own: kv_gather(own, units_on(0), 3, carried),
        )
        part = FeedForward(
            terms, own_in, gains[0][1][None], first_weights[2:], True, False, {}
        )
        outs, others = with_cargo(part, units_on(1) + units_on(2), everyone, 4, 90, 56)
        carried += others
        middle_first, mlp_in_first, hidden_first, own_next, output_first, gate_first, up_first = outs
        terms, grad_late = lax.optimization_barrier((terms, grad_own.astype(BF16)))
        grad_mlp = lax.all_gather(grad_late, "dp", axis=0)
        grad_mlp = lax.all_gather(grad_mlp, "section", axis=0).transpose(1, 0, 2, 3)
        grad_mlp = grad_mlp.reshape(dp_size, -1, depth)
        second_weights = attn_of(attn_next) + tuple(spread_units(out[0][0]) for out in carried)
        terms, saved_second = attn_forward(
            output_first, second_weights, gains[1], slot, lambda own: kv_gather(own, [], 5, [])
        )
        part = FeedForward(
            terms, own_next, gains[1][1][None], second_weights[2:], True, True,
            {"grad_mlp": grad_mlp, "grad_own": grad_own},
        )
        outs, _ = with_cargo(part, [], everyone, 6, 100, 60)
        (
            middle, mlp_in, hidden_bf, _, output_second,
            grad_gate, grad_up, grad_middle, mlp_gain_second, grad_attn,
        ) = outs
        unit_grad = scatter_units(
            weight_products(
                [
                    (flat(grad_gate), flat(mlp_in)),
                    (flat(grad_up), flat(mlp_in)),
                    (flat(hidden_bf), flat(grad_mlp)),
                ]
            )
        )
        terms, pairs, head_second = attn_backward(
            grad_attn, saved_second, second_weights, gains[1], slot,
            lambda whole: kv_scatter(whole, [], 7, []),
        )
        attn_second = scatter_shards(weight_products(pairs))
        part = FeedForward(
            terms, own_next, gains[1][0][None], first_weights[2:], False, True,
            {
                "add": grad_middle, "gate": gate_first, "up": up_first,
                "middle_in": middle_first, "mlp_gain": gains[0][1][None],
            },
        )
        outs, _ = with_cargo(part, [], everyone, 8, 90, 60)
        (
            grad_gate, grad_up, grad_middle, mlp_gain_first, grad_attn,
            attn_gain_second, incoming_second, grad_mlp,
        ) = outs
        unit_home_second = unit_grad
        unit_grad = scatter_units(
            weight_products(
                [
                    (flat(grad_gate), flat(mlp_in_first)),
                    (flat(grad_up), flat(mlp_in_first)),
                    (flat(hidden_first), flat(grad_mlp)),
                ]
            )
        )
        carried = []
        terms, pairs, head_first = attn_backward(
            grad_attn, saved_first, first_weights, gains[0], slot,
            lambda whole: kv_scatter(whole, [UnitsHome(unit_home_second[:1], 1)], 9, carried),
        )
        attn_first = scatter_shards(weight_products(pairs))
        part = LastHub(terms, own_in, gains[0][0][None], grad_middle)
        (attn_gain_first, incoming_first), others = with_cargo(
            part, [UnitsHome(unit_home_second[1:], 1)], everyone, 10, 50
        )
        carried += others
        outputs = [output_first, output_second]
        grads = [incoming_first, incoming_second]
        weight_grads = [(attn_first, unit_grad), (attn_second, None)]
        gain_grads = [
            jnp.concatenate([attn_gain_first[0], mlp_gain_first[0], *head_first]),
            jnp.concatenate([attn_gain_second[0], mlp_gain_second[0], *head_second]),
        ]
    else:
        outputs, grads, products, gain_grads = plain_layers(
            hidden, own_in, grad_own, both_weights, gains, slot, shared_kv
        )
        weight_grads = []
        for pairs in products:
            whole = weight_products(pairs)
            weight_grads.append((scatter_shards(whole[:2]), scatter_units(whole[2:])))

    gain_total = jnp.stack(gain_grads)
    if fast:
        mine = jnp.where(core == 0, weight_grads[0][0], weight_grads[1][0])
        other = jnp.where(core == 0, weight_grads[1][0], weight_grads[0][0])
        (gain_total,), (arrived,), (first_home,) = fused(
            [TotalOverAll(gain_total.reshape(-1, 128)), Swap(other), UnitsHome(unit_grad, 0)],
            everyone, True, 11, 60,
        )
        attn_home = (jnp.where(core == 0, mine, arrived), jnp.where(core == 0, arrived, mine))
        second_home = jnp.concatenate([out[0] for out in carried], axis=0)
        unit_home = jnp.where(core == 0, first_home, second_home).reshape(3, own_units, own_depth)
        gain_total = gain_total.reshape(2, -1)
    else:
        def bring_home(first, second):
            mine, other = jnp.where(core == 0, first, second), jnp.where(core == 0, second, first)
            arrived = lax.ppermute(other, "section", [(0, 1), (1, 0)])
            return (jnp.where(core == 0, mine, arrived), jnp.where(core == 0, arrived, mine))

        def pieces_of(grad):
            return exchange(
                grad.reshape(3, share, dp_size, own_depth).transpose(2, 0, 1, 3), "dp"
            )

        attn_home = bring_home(weight_grads[0][0], weight_grads[1][0])
        unit_home = jnp.stack(bring_home(pieces_of(weight_grads[0][1]), pieces_of(weight_grads[1][1])))
        unit_home = unit_home.transpose(2, 0, 1, 3, 4).reshape(3, own_units, own_depth)
        gain_total = lax.psum(gain_total, ("section", "dp", "tensor"))

    def joined(start, width):
        parts = [half[:, start : start + width] for half in attn_home]
        if shared_kv and start in (q_width, q_width + k_width):
            return parts[0].astype(F32)
        return jnp.concatenate(parts, axis=1).astype(F32)

    gain_own = pick(gain_total, core)
    share_width = attn_gain.shape[1]
    attn_gain_grad = lax.dynamic_slice_in_dim(gain_own, data_index * share_width, share_width, 0)
    mlp_gain_grad = lax.dynamic_slice_in_dim(
        gain_own, depth + data_index * share_width, share_width, 0
    )
    return (
        jnp.where(core == 0, outputs[0], outputs[1])[None],
        jnp.where(core == 0, grads[0], grads[1])[None],
        attn_gain_grad[None],
        joined(0, q_width)[None],
        joined(q_width, k_width)[None],
        joined(q_width + k_width, k_width)[None],
        joined(qkv_width, q_width).T[None],
        gain_own[2 * depth : 2 * depth + HD][None],
        gain_own[2 * depth + HD :][None],
        mlp_gain_grad[None],
        unit_home[0].T.astype(F32)[None],
        unit_home[1].T.astype(F32)[None],
        unit_home[2].astype(F32)[None],
    )


def solution(mesh):
    rows = P(None, "dp", None)
    wide = P("section", "dp", "tensor")
    tall = P("section", "tensor", "dp")
    gain = P("section", "dp")
    head_gain = P("section", None)
    slots = P("section", None, "dp", None)
    in_specs = (
        rows, rows, P(), P(), P(), gain, wide, wide, wide, tall, head_gain, head_gain, gain,
        wide, wide, tall,
    )
    out_specs = (
        slots, slots, gain, wide, wide, wide, tall, head_gain, head_gain, gain, wide, wide, tall,
    )
    return jax.shard_map(
        on_device, mesh=mesh, in_specs=in_specs, out_specs=out_specs, check_vma=False
    )
```

```python
from functools import partial

import jax
import jax.numpy as jnp
from jax import lax
from jax.experimental import pallas as pl
from jax.experimental.pallas import tpu as pltpu
from jax.sharding import PartitionSpec as P

HD = 128
TRUNK = 512
BRANCH = 96
NB = 4
TREE = 1152
SEGS = 9


EPSILON = 1e-06
THETA = 1000000.0
MASKED = -1e30
F32 = jnp.float32
BF16 = jnp.bfloat16


def rms_scale(values, weight_gain):
    mean_sq = jnp.mean(values * values, axis=-1, keepdims=True)
    return values * lax.rsqrt(mean_sq + EPSILON) * weight_gain


def rotate(values, cos_table, sine_table):
    middle_at = values.shape[-1] // 2
    leading = values[..., :middle_at]
    trailing = values[..., middle_at:]
    return jnp.concatenate(
        [leading * cos_table - trailing * sine_table, trailing * cos_table + leading * sine_table],
        axis=-1,
    )


def rope_tables(positions, head_dim):
    half_steps = jnp.arange(head_dim // 2, dtype=F32)
    inverse = THETA ** (-2.0 * half_steps / head_dim)
    angles = positions.astype(F32)[:, None] * inverse[None, :]
    return (jnp.cos(angles)[:, None, :], jnp.sin(angles)[:, None, :])


def swiglu(gate_in, up_in):
    return jax.nn.silu(gate_in) * up_in


def embed_heads(q_pre, k_pre, q_scale, k_scale, cos_table, sine_table):
    row_count = q_pre.shape[0]
    queries = rms_scale(q_pre.reshape(row_count, -1, HD), q_scale)
    keys_part = rms_scale(k_pre.reshape(row_count, -1, HD), k_scale)
    return (rotate(queries, cos_table, sine_table), rotate(keys_part, cos_table, sine_table))


def tree_layout(seg_row, parent_row):
    labels = jnp.arange(SEGS, dtype=jnp.int32)
    places = jnp.arange(TREE, dtype=jnp.int32)
    member = seg_row[None, :] == labels[:, None]
    starts = jnp.min(jnp.where(member, places[None, :], TREE), axis=1)
    depth_base = jnp.where(labels == 0, 0, jnp.where(labels <= NB, TRUNK, TRUNK + BRANCH))
    shifts = depth_base - starts
    positions = places + jnp.sum(jnp.where(member, shifts[:, None], 0), axis=0)
    grandparent = jnp.sum(
        jnp.where(parent_row[:, None] == labels[None, :], parent_row[None, :], 0), axis=1
    )
    ancestor = (
        (labels[None, :] == labels[:, None])
        | (labels[None, :] == parent_row[:, None])
        | (labels[None, :] == grandparent[:, None])
    )
    return (positions, member.astype(F32), ancestor.astype(F32))


def path_mask(seg_row, parent_row, row_start, row_count):
    positions, member, ancestor = tree_layout(seg_row, parent_row)
    member_rows = lax.dynamic_slice_in_dim(member, row_start, row_count, 1)
    seg_rows = lax.dynamic_slice_in_dim(seg_row, row_start, row_count, 0)
    reach_table = jnp.dot(jnp.dot(member_rows.T, ancestor), member)
    places = jnp.arange(TREE, dtype=jnp.int32)
    row_places = row_start + jnp.arange(row_count, dtype=jnp.int32)
    same_seg = seg_rows[:, None] == seg_row[None, :]
    causal = places[None, :] <= row_places[:, None]
    allowed = (reach_table > 0.5) & (jnp.logical_not(same_seg) | causal)
    row_positions = lax.dynamic_slice_in_dim(positions, row_start, row_count, 0)
    return (allowed, row_positions)


OUTER = (((0,), (0,)), ((), ()))
INNER = (((1,), (1,)), ((), ()))


def dot(left, right):
    return jnp.dot(left, right, preferred_element_type=F32)


def dot_inner(left, right):
    return lax.dot_general(left, right, INNER, preferred_element_type=F32)


def dot_outer(left, right):
    return lax.dot_general(left, right, OUTER, preferred_element_type=F32)


def exchange(pieces, axis):
    size = lax.axis_size(axis)
    me = lax.axis_index(axis)
    got = jnp.zeros_like(pieces)
    own = lax.dynamic_index_in_dim(pieces, me, 0, keepdims=True)
    got = lax.dynamic_update_slice_in_dim(got, own, me, 0)
    for step in range(1, size):
        other = me ^ step
        piece = lax.dynamic_index_in_dim(pieces, other, 0, keepdims=True)
        arrived = lax.ppermute(piece, axis, [(i, i ^ step) for i in range(size)])
        got = lax.dynamic_update_slice_in_dim(got, arrived, other, 0)
    return got


def masked_scores(query_bf, key_all, allowed):
    raw_scores = jnp.einsum(
        "brgd,btd->bgrt", query_bf, key_all, preferred_element_type=F32
    ) * HD ** (-0.5)
    return jnp.where(allowed[:, None], raw_scores, MASKED)


MESH = pl.DeviceIdType.MESH
CHUNK = 256
SEM = pltpu.SemaphoreType.DMA
VMEM = pl.BlockSpec(memory_space=pltpu.VMEM)
HBM = pl.BlockSpec(memory_space=pl.ANY)


def remote(src, dst, send_sem, recv_sem, device_id):
    return pltpu.make_async_remote_copy(
        src_ref=src, dst_ref=dst, send_sem=send_sem, recv_sem=recv_sem,
        device_id=device_id, device_id_type=MESH,
    )


def greet(axes, across):
    barrier = pltpu.get_barrier_semaphore()
    count = 0
    for axis in axes:
        size = lax.axis_size(axis)
        me = lax.axis_index(axis)
        for step in range(1, size):
            pl.semaphore_signal(
                barrier, inc=1, device_id={axis: lax.rem(me + step, size)}, device_id_type=MESH
            )
        count += size - 1
    if across:
        size = lax.axis_size("dp")
        me = lax.axis_index("dp")
        sibling = 1 - lax.axis_index("section")
        for step in range(1, size):
            pl.semaphore_signal(
                barrier, inc=1, device_id={"section": sibling, "dp": lax.rem(me + step, size)},
                device_id_type=MESH,
            )
        count += size - 1
    pl.semaphore_wait(barrier, count)


class Part:
    ins, outs, scratch = (), (), ()

    def bind(self, ins, outs, scratch):
        self.in_refs, self.out_refs, self.refs = ins, outs, scratch

    def prepare(self):
        pass

    def start(self):
        pass

    def run(self):
        pass

    def finish(self):
        pass


def fused(parts, axes, across, collective_id, cost_us, vmem=40):
    counts = [(len(part.ins), len(part.outs), len(part.scratch)) for part in parts]

    def kernel(*refs):
        refs = list(refs)
        groups = []
        for kind in range(3):
            groups.append([])
            for count in counts:
                groups[kind].append(refs[: count[kind]])
                del refs[: count[kind]]
        for part, ins, outs, scratch in zip(parts, *groups):
            part.bind(ins, outs, scratch)
        for part in parts:
            part.prepare()
        greet(axes, across)
        for part in parts:
            part.start()
        for part in parts:
            part.run()
        for part in parts:
            part.finish()

    ins = [item for part in parts for item in part.ins]
    outs = [item for part in parts for item in part.outs]
    results = pl.pallas_call(
        kernel,
        out_shape=[item[0] for item in outs],
        in_specs=[item[1] for item in ins],
        out_specs=[item[1] for item in outs],
        scratch_shapes=[item for part in parts for item in part.scratch],
        cost_estimate=pl.CostEstimate(
            flops=0, bytes_accessed=cost_us * 3_000_000, transcendentals=0
        ),
        compiler_params=pltpu.CompilerParams(
            collective_id=collective_id, has_side_effects=True, vmem_limit_bytes=vmem << 20
        ),
    )(*[item[0] for item in ins])
    results = list(results)
    split = []
    for count in counts:
        split.append(results[: count[1]])
        del results[: count[1]]
    return split


def columns_of(place, width):
    return pl.ds(pl.multiple_of(place * width, width), width)


class UnitsOut(Part):
    def __init__(self, mats, layer):
        self.layer, self.count = layer, len(mats)
        self.size = lax.axis_size("dp")
        rows, self.width = mats[0].shape
        self.share = rows // (2 * self.size)
        self.ins = [(mat, HBM) for mat in mats]
        shape = jax.ShapeDtypeStruct((self.share, self.size * self.width), BF16)
        self.outs = [(shape, HBM)] * self.count
        self.scratch = [SEM((self.count,)), SEM((self.count, 2, self.size)), SEM((self.count, self.size))]

    def bind(self, ins, outs, scratch):
        self.src, self.dst = ins, outs
        self.keep, self.send, self.recv = scratch
        self.core, self.me = lax.axis_index("section"), lax.axis_index("dp")

    def piece(self, index, core, place):
        start = pl.multiple_of((core * self.size + place) * self.share, self.share)
        return self.src[index].at[pl.ds(start, self.share)]

    def lands(self, index, slot):
        return self.dst[index].at[:, columns_of(slot, self.width)]

    def copy(self, index, core, place, slot):
        return remote(
            self.piece(index, core, place), self.lands(index, slot),
            self.send.at[index, core, place], self.recv.at[index, slot],
            {"section": core, "dp": place},
        )

    def local(self, index):
        return pltpu.make_async_copy(
            self.piece(index, self.layer, self.me), self.lands(index, self.me), self.keep.at[index]
        )

    def targets(self):
        for index in range(self.count):
            for core in range(2):
                for place in range(self.size):
                    yield index, core, place, (place != self.me) | (core != self.layer)

    def start(self):
        @pl.when(self.core == self.layer)
        def _():
            for index, core, place, is_other in self.targets():
                @pl.when(is_other)
                def _():
                    self.copy(index, core, place, self.me).start()

            for index in range(self.count):
                self.local(index).start()

    def finish(self):
        for index in range(self.count):
            for place in range(self.size):
                @pl.when((self.core != self.layer) | (place != self.me))
                def _():
                    self.copy(index, 0, 0, place).wait_recv()

        @pl.when(self.core == self.layer)
        def _():
            for index, core, place, is_other in self.targets():
                @pl.when(is_other)
                def _():
                    self.copy(index, core, place, self.me).wait_send()

            for index in range(self.count):
                self.local(index).wait()


class UnitsHome(Part):
    def __init__(self, mats, layer):
        self.layer, self.count = layer, len(mats)
        self.size = lax.axis_size("dp")
        self.share, depth = mats[0].shape
        self.width = depth // self.size
        self.ins = [(mat, HBM) for mat in mats]
        shape = jax.ShapeDtypeStruct((2 * self.size * self.share, self.width), BF16)
        self.outs = [(shape, HBM)] * self.count
        self.scratch = [SEM((self.count,)), SEM((self.count, self.size)), SEM((self.count, 2, self.size))]

    def bind(self, ins, outs, scratch):
        self.src, self.dst = ins, outs
        self.keep, self.send, self.recv = scratch
        self.core, self.me = lax.axis_index("section"), lax.axis_index("dp")

    def lands(self, index, core, slot):
        start = pl.multiple_of((core * self.size + slot) * self.share, self.share)
        return self.dst[index].at[pl.ds(start, self.share)]

    def copy(self, index, place, core, slot):
        return remote(
            self.src[index].at[:, columns_of(place, self.width)], self.lands(index, core, slot),
            self.send.at[index, place], self.recv.at[index, core, slot],
            {"section": self.layer, "dp": place},
        )

    def local(self, index):
        return pltpu.make_async_copy(
            self.src[index].at[:, columns_of(self.me, self.width)],
            self.lands(index, self.layer, self.me), self.keep.at[index],
        )

    def start(self):
        for index in range(self.count):
            for place in range(self.size):
                @pl.when((self.core != self.layer) | (place != self.me))
                def _():
                    self.copy(index, place, self.core, self.me).start()

            @pl.when(self.core == self.layer)
            def _():
                self.local(index).start()

    def finish(self):
        for index in range(self.count):
            @pl.when(self.core == self.layer)
            def _():
                for core in range(2):
                    for place in range(self.size):
                        @pl.when((core != self.layer) | (place != self.me))
                        def _():
                            self.copy(index, 0, core, place).wait_recv()

                self.local(index).wait()

            for place in range(self.size):
                @pl.when((self.core != self.layer) | (place != self.me))
                def _():
                    self.copy(index, place, self.core, self.me).wait_send()


class UnitsSpread(Part):
    def __init__(self, rows):
        self.size = lax.axis_size("tensor")
        self.share, depth = rows.shape
        self.ins = [(rows, HBM)]
        self.outs = [(jax.ShapeDtypeStruct((self.size * self.share, depth), BF16), HBM)]
        self.scratch = [SEM, SEM((self.size,)), SEM((self.size,))]

    def bind(self, ins, outs, scratch):
        (self.src,), (self.dst,), (self.keep, self.send, self.recv) = ins, outs, scratch
        self.me = lax.axis_index("tensor")

    def lands(self, slot):
        return self.dst.at[pl.ds(pl.multiple_of(slot * self.share, self.share), self.share)]

    def copy(self, place, slot):
        return remote(
            self.src, self.lands(slot), self.send.at[place], self.recv.at[slot], {"tensor": place}
        )

    def start(self):
        for place in range(self.size):
            @pl.when(place != self.me)
            def _():
                self.copy(place, self.me).start()

        pltpu.make_async_copy(self.src, self.lands(self.me), self.keep).start()

    def finish(self):
        for place in range(self.size):
            @pl.when(place != self.me)
            def _():
                self.copy(place, place).wait_recv()
                self.copy(place, self.me).wait_send()

        pltpu.make_async_copy(self.src, self.lands(self.me), self.keep).wait()


class SharedRows(Part):
    def __init__(self, own):
        self.size = lax.axis_size("dp")
        self.ins = [(own, VMEM)]
        self.outs = [(jax.ShapeDtypeStruct((2, self.size) + own.shape, F32), VMEM)]
        self.scratch = [SEM((2, self.size)), SEM((2, self.size))]

    def copy(self, core, place, from_core, from_place):
        return remote(
            self.in_refs[0], self.out_refs[0].at[from_core, from_place],
            self.refs[0].at[core, place], self.refs[1].at[from_core, from_place],
            {"section": core, "dp": place},
        )

    def others(self):
        core, me = lax.axis_index("section"), lax.axis_index("dp")
        for other in range(2):
            for place in range(self.size):
                yield other, place, (other != core) | (place != me)

    def start(self):
        core, me = lax.axis_index("section"), lax.axis_index("dp")
        for other, place, is_other in self.others():
            @pl.when(is_other)
            def _():
                self.copy(other, place, core, me).start()

        self.out_refs[0][core, me] = self.in_refs[0][...]

    def finish(self):
        core, me = lax.axis_index("section"), lax.axis_index("dp")
        for other, place, is_other in self.others():
            @pl.when(is_other)
            def _():
                self.copy(other, place, other, place).wait_recv()
                self.copy(other, place, core, me).wait_send()


def far_pair(place, me):
    return (place + me == 3) & ((place == 0) | (place == 3))


def line_relays(size):
    return [(2, 0, 3), (1, 3, 0)] if size == 4 else []


def line_order(size):
    return [1, 2, 0, 3] if size == 4 else list(range(size))


class AttnShards:
    def __init__(self, w_query, w_key, w_value, w_out):
        self.arrays = [w_query, w_key, w_value, w_out]
        self.depth = w_query.shape[0]
        self.q_width, self.k_width = w_query.shape[1] // 2, w_key.shape[1] // 2
        self.width = self.q_width + 2 * self.k_width
        half = self.depth // 2
        parts = self.q_width // 2
        self.items = [
            (0, lambda ref, core: ref.at[pl.ds(0, half), columns_of(core, self.q_width)]),
            (0, lambda ref, core: ref.at[pl.ds(half, half), columns_of(core, self.q_width)]),
            (1, lambda ref, core: ref.at[:, columns_of(core, self.k_width)]),
            (2, lambda ref, core: ref.at[:, columns_of(core, self.k_width)]),
            (3, lambda ref, core: ref.at[pl.ds(core * self.q_width, parts)]),
            (3, lambda ref, core: ref.at[pl.ds(core * self.q_width + parts, parts)]),
        ]
        q_width, k_width, depth = self.q_width, self.k_width, self.depth
        self.qkv_rows = [(0, half), (half, half), (0, depth), (0, depth)]
        self.qkv_columns = [
            (0, q_width), (0, q_width), (q_width, k_width), (q_width + k_width, k_width)
        ]
        self.out_rows = [(0, parts), (parts, parts)]

    def source(self, refs, index, core):
        array, cut = self.items[index]
        return cut(refs[array], core)

    def lands(self, qkv, out, index, slot):
        if index < 4:
            (start, rows), (left, columns) = self.qkv_rows[index], self.qkv_columns[index]
            at = pl.multiple_of(slot * self.depth + start, rows)
            return qkv.at[pl.ds(at, rows), pl.ds(left, columns)]
        start, rows = self.out_rows[index - 4]
        return out.at[pl.ds(start, rows), columns_of(slot, self.depth)]


class AttnOut(Part):
    def __init__(self, shards, layer):
        self.layer, self.shards = layer, shards
        self.size = lax.axis_size("dp")
        self.count = len(shards.items)
        depth = self.size * shards.depth
        self.ins = [(array, HBM) for array in shards.arrays]
        self.outs = [
            (jax.ShapeDtypeStruct((depth, shards.width), BF16), HBM),
            (jax.ShapeDtypeStruct((shards.q_width, depth), BF16), HBM),
        ]
        self.scratch = [
            SEM((self.count,)), SEM((2, self.size, self.count)), SEM((self.size, self.count)),
            SEM((self.count,)),
        ]

    def bind(self, ins, outs, scratch):
        self.src = ins
        self.qkv, self.out = outs
        self.keep, self.send, self.recv, self.relay_send = scratch
        self.core, self.me = lax.axis_index("section"), lax.axis_index("dp")

    def lands(self, index, slot):
        return self.shards.lands(self.qkv, self.out, index, slot)

    def copy(self, core, place, slot, index):
        return remote(
            self.shards.source(self.src, index, core), self.lands(index, slot),
            self.send.at[core, place, index], self.recv.at[slot, index],
            {"section": core, "dp": place},
        )

    def relay(self, source, target, index):
        block = self.lands(index, source)
        return remote(
            block, block, self.relay_send.at[index], self.recv.at[source, index], {"dp": target}
        )

    def local(self, index):
        return pltpu.make_async_copy(
            self.shards.source(self.src, index, self.layer), self.lands(index, self.me),
            self.keep.at[index],
        )

    def targets(self):
        for index in range(self.count):
            for core in range(2):
                for place in range(self.size):
                    sent = (place != self.me) | (core != self.layer)
                    if self.size == 4:
                        sent = sent & jnp.logical_not(far_pair(place, self.me))
                    yield core, place, index, sent

    def start(self):
        @pl.when(self.core == self.layer)
        def _():
            for core, place, index, sent in self.targets():
                @pl.when(sent)
                def _():
                    self.copy(core, place, self.me, index).start()

            for index in range(self.count):
                self.local(index).start()

    def run(self):
        for index in range(self.count):
            for place in line_order(self.size):
                @pl.when((self.core != self.layer) | (place != self.me))
                def _():
                    self.copy(0, 0, place, index).wait_recv()

                for via, source, target in line_relays(self.size):
                    if source == place:
                        @pl.when(self.me == via)
                        def _():
                            self.relay(source, target, index).start()

    def finish(self):
        @pl.when(self.core == self.layer)
        def _():
            for core, place, index, sent in self.targets():
                @pl.when(sent)
                def _():
                    self.copy(core, place, self.me, index).wait_send()

            for index in range(self.count):
                self.local(index).wait()

        for via, source, target in line_relays(self.size):
            @pl.when(self.me == via)
            def _():
                for index in range(self.count):
                    self.relay(source, target, index).wait_send()


class HalfOver(Part):
    def __init__(self, shards):
        self.shards = shards
        self.count = len(shards.items)
        rows = shards.depth + shards.q_width
        self.ins = [(array, HBM) for array in shards.arrays]
        self.outs = [(jax.ShapeDtypeStruct((rows, shards.depth), BF16), HBM)]
        self.scratch = [SEM((self.count,)), SEM((self.count,)), SEM((self.count,))]

    def lands(self, index):
        depth, q_width = self.shards.depth, self.shards.q_width
        packed = self.out_refs[0]
        return self.shards.lands(
            packed.at[pl.ds(0, depth)], packed.at[pl.ds(depth, q_width)], index, 0
        )

    def over(self, index):
        return remote(
            self.shards.source(self.in_refs, index, 0), self.lands(index), self.refs[0].at[index],
            self.refs[1].at[index], {"section": 0},
        )

    def keep(self, index):
        return pltpu.make_async_copy(
            self.shards.source(self.in_refs, index, 1), self.lands(index), self.refs[2].at[index]
        )

    def start(self):
        @pl.when(lax.axis_index("section") == 1)
        def _():
            for index in range(self.count):
                self.over(index).start()
                self.keep(index).start()

    def finish(self):
        @pl.when(lax.axis_index("section") == 1)
        def _():
            for index in range(self.count):
                self.over(index).wait_send()
                self.keep(index).wait()

        @pl.when(lax.axis_index("section") == 0)
        def _():
            for index in range(self.count):
                self.over(index).wait_recv()


class Swap(Part):
    def __init__(self, own):
        self.ins = [(own, HBM)]
        self.outs = [(jax.ShapeDtypeStruct(own.shape, own.dtype), HBM)]
        self.scratch = [SEM, SEM]

    def start(self):
        sibling = 1 - lax.axis_index("section")
        self.copy = remote(
            self.in_refs[0], self.out_refs[0], self.refs[0], self.refs[1], {"section": sibling}
        )
        self.copy.start()

    def finish(self):
        self.copy.wait()


class GatherKV(Part):
    def __init__(self, own):
        trees, rows, width = own.shape
        self.trees, self.size = trees, lax.axis_size("dp")
        self.ins = [(own, VMEM)]
        self.outs = [(jax.ShapeDtypeStruct((trees, self.size, rows, width), BF16), VMEM)]
        self.scratch = [SEM((self.size, trees)), SEM((self.size, trees)), SEM((trees,))]

    def bind(self, ins, outs, scratch):
        (self.own,), (self.out,) = ins, outs
        self.send, self.recv, self.relay_send = scratch
        self.me = lax.axis_index("dp")

    def copy(self, place, slot, tree):
        return remote(
            self.own.at[tree], self.out.at[tree, slot], self.send.at[place, tree],
            self.recv.at[slot, tree], {"dp": place},
        )

    def relay(self, source, target, tree):
        return remote(
            self.out.at[tree, source], self.out.at[tree, source], self.relay_send.at[tree],
            self.recv.at[source, tree], {"dp": target},
        )

    def targets(self):
        for tree in range(self.trees):
            for place in range(self.size):
                sent = place != self.me
                if self.size == 4:
                    sent = sent & jnp.logical_not(far_pair(place, self.me))
                yield place, tree, sent

    def start(self):
        for place, tree, sent in self.targets():
            @pl.when(sent)
            def _():
                self.copy(place, self.me, tree).start()

        self.out[:, self.me] = self.own[...]

    def run(self):
        for tree in range(self.trees):
            for place in line_order(self.size):
                @pl.when(place != self.me)
                def _():
                    self.copy(place, place, tree).wait_recv()

                for via, source, target in line_relays(self.size):
                    if source == place:
                        @pl.when(self.me == via)
                        def _():
                            self.relay(source, target, tree).start()

    def finish(self):
        for place, tree, sent in self.targets():
            @pl.when(sent)
            def _():
                self.copy(place, self.me, tree).wait_send()

        for via, source, target in line_relays(self.size):
            @pl.when(self.me == via)
            def _():
                for tree in range(self.trees):
                    self.relay(source, target, tree).wait_send()


class ScatterKV(Part):
    def __init__(self, whole):
        trees, size, rows, width = whole.shape
        self.trees, self.size = trees, size
        self.sides = [(0, 1, 3), (3, 2, 0)] if size == 4 else []
        self.ins = [(whole, VMEM)]
        self.outs = [(jax.ShapeDtypeStruct((trees, rows, width), F32), VMEM)]
        self.scratch = [
            pltpu.VMEM((size, trees, rows, width), BF16), pltpu.VMEM((trees, rows, width), BF16),
            SEM((size, trees)), SEM((size, trees)), SEM((trees,)), SEM((trees,)),
        ]

    def bind(self, ins, outs, scratch):
        (self.terms,), (self.out,) = ins, outs
        self.boxes, self.joint, self.send, self.recv, self.join_send, self.join_recv = scratch
        self.me = lax.axis_index("dp")

    def copy(self, place, slot, tree):
        return remote(
            self.terms.at[tree, place], self.boxes.at[slot, tree], self.send.at[place, tree],
            self.recv.at[slot, tree], {"dp": place},
        )

    def by_way(self, via, target, tree):
        return remote(
            self.terms.at[tree, target], self.joint.at[tree], self.join_send.at[tree],
            self.join_recv.at[tree], {"dp": via},
        )

    def joined(self, via, target, tree):
        return remote(
            self.joint.at[tree], self.boxes.at[via, tree], self.send.at[target, tree],
            self.recv.at[via, tree], {"dp": target},
        )

    def plain(self, place):
        ok = place != self.me
        for source, via, target in self.sides:
            if place == target:
                ok = ok & (self.me != source) & (self.me != via)
        return ok

    def expected(self, place):
        ok = place != self.me
        for source, via, target in self.sides:
            if place == source:
                ok = ok & (self.me != target)
        return ok

    def start(self):
        for tree in range(self.trees):
            for source, via, target in self.sides:
                @pl.when(self.me == source)
                def _():
                    self.by_way(via, target, tree).start()

            for place in range(self.size):
                @pl.when(self.plain(place))
                def _():
                    self.copy(place, self.me, tree).start()

    def run(self):
        for tree in range(self.trees):
            for source, via, target in self.sides:
                @pl.when(self.me == via)
                def _():
                    self.by_way(via, target, tree).wait_recv()
                    both = self.joint[tree].astype(F32) + self.terms[tree, target].astype(F32)
                    self.joint[tree] = both.astype(BF16)
                    self.joined(via, target, tree).start()

        for tree in range(self.trees):
            self.out[tree] = self.terms[tree, self.me].astype(F32)
            for place in line_order(self.size):
                @pl.when(self.expected(place))
                def _():
                    self.copy(place, place, tree).wait_recv()
                    self.out[tree] += self.boxes[place, tree].astype(F32)

    def finish(self):
        for tree in range(self.trees):
            for place in range(self.size):
                @pl.when(self.plain(place))
                def _():
                    self.copy(place, self.me, tree).wait_send()

            for source, via, target in self.sides:
                @pl.when(self.me == source)
                def _():
                    self.by_way(via, target, tree).wait_send()

                @pl.when(self.me == via)
                def _():
                    self.joined(via, target, tree).wait_send()


class TotalOverAll(Part):
    axes = ("section", "tensor", "dp")

    def __init__(self, own):
        sizes = [lax.axis_size(axis) for axis in self.axes]
        self.ins = [(own, VMEM)]
        self.outs = [(jax.ShapeDtypeStruct(own.shape, F32), VMEM)]
        self.scratch = [pltpu.VMEM((size,) + own.shape, F32) for size in sizes]
        self.scratch += [SEM((size,)) for size in sizes] * 2

    def run(self):
        out = self.out_refs[0]
        out[...] = self.in_refs[0][...]
        for axis, box, send, recv in zip(self.axes, self.refs[:3], self.refs[3:6], self.refs[6:9]):
            size, me = lax.axis_size(axis), lax.axis_index(axis)
            box[me] = out[...]

            def spread(place, slot):
                return remote(box.at[me], box.at[slot], send.at[place], recv.at[slot], {axis: place})

            for place in range(size):
                @pl.when(place != me)
                def _():
                    spread(place, me).start()

            for place in range(size):
                @pl.when(place != me)
                def _():
                    spread(place, place).wait_recv()
                    spread(place, me).wait_send()

            total = box[0]
            for place in range(1, size):
                total += box[place]
            out[...] = total


class Gatherer:
    def __init__(self, axis, rows, half):
        self.axis, self.rows, self.half = axis, rows, half
        self.size = size = lax.axis_size(axis)
        self.scratch = [pltpu.VMEM((2, size, 2 * rows, half), BF16)]
        self.scratch += [SEM((size,))] * 4 + [SEM]

    def bind(self, refs):
        self.board, self.send, self.recv, self.sib_send, self.sib_recv, self.relay_send = refs
        self.core = lax.axis_index("section")
        self.sibling = 1 - self.core
        self.me = lax.axis_index(self.axis)
        self.relays = line_relays(self.size) if self.axis == "dp" else []

    def direct(self, place):
        sent = place != self.me
        if self.relays:
            sent = sent & jnp.logical_not(far_pair(place, self.me))
        return sent

    def spread(self, place, slot):
        return remote(
            self.board.at[self.core, slot], self.board.at[self.core, slot], self.send.at[place],
            self.recv.at[slot], {self.axis: place},
        )

    def passed(self, source, target):
        return remote(
            self.board.at[self.core, source], self.board.at[self.core, source], self.relay_send,
            self.recv.at[source], {self.axis: target},
        )

    def over(self, tree, slot):
        return remote(
            self.board.at[tree, slot], self.board.at[tree, slot], self.sib_send.at[slot],
            self.sib_recv.at[slot], {"section": self.sibling},
        )

    def begin(self, result):
        half = self.half
        piece = jnp.concatenate([result[:, :half], result[:, half:]], axis=0)
        self.board[self.core, self.me] = piece.astype(BF16)
        for place in range(self.size):
            @pl.when(self.direct(place))
            def _():
                self.spread(place, self.me).start()

        self.over(self.core, self.me).start()

    def arrive(self, place):
        @pl.when(place != self.me)
        def _():
            self.spread(place, place).wait_recv()

        for via, source, target in self.relays:
            @pl.when((self.me == via) & (place == source))
            def _():
                self.passed(source, target).start()

        @pl.when(place != self.me)
        def _():
            self.over(self.core, place).start()

    def arrive_over(self, place):
        self.over(self.sibling, place).wait_recv()

    def unpack(self, out, tree):
        rows = self.rows

        @pl.loop(0, self.half // CHUNK)
        def _(step):
            at = pl.multiple_of(step * CHUNK, CHUNK)
            blocks = [
                self.board[tree, place, :, pl.ds(at, CHUNK)].astype(F32)
                for place in range(self.size)
            ]
            for side in range(2):
                whole = [block[side * rows : (side + 1) * rows] for block in blocks]
                out[tree, :, pl.ds(side * self.half + at, CHUNK)] = jnp.concatenate(
                    whole, axis=0
                ).astype(BF16)

    def unpack_place(self, out, place):
        rows = self.rows

        @pl.loop(0, self.half // CHUNK)
        def _(step):
            at = pl.multiple_of(step * CHUNK, CHUNK)
            blocks = [self.board[tree, place, :, pl.ds(at, CHUNK)].astype(F32) for tree in range(2)]
            for side in range(2):
                whole = [block[side * rows : (side + 1) * rows] for block in blocks]
                out[place, :, pl.ds(side * self.half + at, CHUNK)] = jnp.concatenate(
                    whole, axis=0
                ).astype(BF16)

    def complete(self, out):
        for place in range(self.size):
            self.arrive(place)
        self.unpack(out, self.core)
        for place in range(self.size):
            self.arrive_over(place)
        self.unpack(out, self.sibling)

    def finish(self):
        for place in range(self.size):
            @pl.when(self.direct(place))
            def _():
                self.spread(place, self.me).wait_send()

            self.over(self.core, place).wait_send()

        for via, source, target in self.relays:
            @pl.when(self.me == via)
            def _():
                self.passed(source, target).wait_send()


class Scatterer:
    def __init__(self, axis, rows, half):
        self.axis, self.rows, self.half = axis, rows, half
        self.size = size = lax.axis_size(axis)
        self.scratch = [pltpu.VMEM((size, 2 * rows, half), BF16)] * 4
        self.scratch += [pltpu.VMEM((2 * rows, half), F32)] + [SEM((size,))] * 4

    def bind(self, refs):
        self.to_sib, self.from_sib, self.to_peer, self.from_peer, self.total = refs[:5]
        self.sib_send, self.sib_recv, self.peer_send, self.peer_recv = refs[5:]
        self.core = lax.axis_index("section")
        self.sibling = 1 - self.core
        self.me = lax.axis_index(self.axis)

    def over(self, place):
        return remote(
            self.to_sib.at[place], self.from_sib.at[place], self.sib_send.at[place],
            self.sib_recv.at[place], {"section": self.sibling},
        )

    def spread(self, place, slot):
        return remote(
            self.to_peer.at[place], self.from_peer.at[slot], self.peer_send.at[place],
            self.peer_recv.at[slot], {self.axis: place},
        )

    def over_columns(self, body):
        @pl.loop(0, self.half // CHUNK)
        def _(step):
            body(pl.multiple_of(step * CHUNK, CHUNK))

    def absorb(self, place, mine):
        self.over(place).wait_recv()

        def add(at):
            both = mine(at) + self.from_sib[place, :, pl.ds(at, CHUNK)].astype(F32)
            self.to_peer[place, :, pl.ds(at, CHUNK)] = both.astype(BF16)

            @pl.when(place == self.me)
            def _():
                self.total[:, pl.ds(at, CHUNK)] = both

        self.over_columns(add)

        @pl.when(place != self.me)
        def _():
            self.spread(place, self.me).start()

    def collect(self):
        for place in range(self.size):
            @pl.when(place != self.me)
            def _():
                self.spread(place, place).wait_recv()
                self.total[...] += self.from_peer[place].astype(F32)

        total = self.total[...]
        return jnp.concatenate([total[: self.rows], total[self.rows :]], axis=1)

    def finish(self):
        for place in range(self.size):
            self.over(place).wait_send()

            @pl.when(place != self.me)
            def _():
                self.spread(place, self.me).wait_send()


class RowScatterer(Scatterer):
    def packed(self, tree, place, at):
        rows = self.rows
        low = rows * place // 16 * 16
        high = -(-rows * (place + 1) // 16) * 16
        skip = rows * place - low
        parts = [
            self.terms[tree, low:high, pl.ds(side * self.half + at, CHUNK)].astype(F32)[
                skip : skip + rows
            ]
            for side in range(2)
        ]
        return jnp.concatenate(parts, axis=0)

    def prepare(self, terms):
        self.terms = terms
        for place in range(self.size):
            def pack(at):
                self.to_sib[place, :, pl.ds(at, CHUNK)] = self.packed(
                    self.sibling, place, at
                ).astype(BF16)

            self.over_columns(pack)

    def start(self):
        for place in range(self.size):
            self.over(place).start()

    def summed(self):
        for place in range(self.size):
            self.absorb(place, lambda at: self.packed(self.core, place, at))
        return self.collect()


class Staged(Part):
    def __init__(self, ins, outs, scratch, helpers):
        self.in_names, self.out_names, self.scratch_names = list(ins), list(outs), list(scratch)
        self.ins, self.outs = list(ins.values()), list(outs.values())
        self.helpers = helpers
        self.scratch = list(scratch.values())
        for helper in helpers:
            self.scratch += helper.scratch

    def bind(self, ins, outs, scratch):
        scratch = list(scratch)
        names = self.in_names + self.out_names + self.scratch_names
        count = len(self.scratch_names)
        for name, ref in zip(names, list(ins) + list(outs) + scratch[:count]):
            setattr(self, name, ref)
        del scratch[:count]
        for helper in self.helpers:
            helper.bind(scratch[: len(helper.scratch)])
            del scratch[: len(helper.scratch)]

    def finish(self):
        for helper in self.helpers:
            helper.finish()


def vmem_f32(*shape):
    return (jax.ShapeDtypeStruct(shape, F32), VMEM)


def vmem_bf16(*shape):
    return (jax.ShapeDtypeStruct(shape, BF16), VMEM)


class LastHub(Staged):
    def __init__(self, terms, values, gain, add):
        rows, depth = values.shape
        half = depth // 2
        self.rows_in = RowScatterer("tensor", rows, half)
        self.rows_out = Gatherer("tensor", rows, half)
        super().__init__(
            {"terms": (terms, VMEM), "values": (values, VMEM), "gain": (gain, VMEM), "add": (add, VMEM)},
            {
                "gain_grad": vmem_f32(1, depth),
                "gathered": vmem_bf16(2, self.rows_out.size * rows, depth),
            },
            {},
            [self.rows_in, self.rows_out],
        )

    def prepare(self):
        self.rows_in.prepare(self.terms)

    def start(self):
        self.rows_in.start()

    def run(self):
        total = self.rows_in.summed()
        result, self.gain_grad[...] = norm_back(total, self.values[...], self.gain[...])
        self.rows_out.begin(result + self.add[...])
        self.rows_out.complete(self.gathered)


class FeedForward(Staged):
    def __init__(self, terms, own, gain, weights, forward, backward, extra):
        rows, depth = own.shape
        half = depth // 2
        units = weights[0].shape[0]
        self.has_forward, self.has_backward, self.units = forward, backward, units
        self.depth = depth
        self.block = 2 * rows
        self.size = size = lax.axis_size("dp")
        self.rows_in = RowScatterer("tensor", rows, half)
        self.spread_in = Gatherer("dp", rows, half)
        helpers = [self.rows_in, self.spread_in]
        group_rows = 2 * rows
        tensor_rows = lax.axis_size("tensor") * rows
        matrix = pltpu.VMEM((units, depth), BF16)
        ins = {"terms": (terms, VMEM), "own": (own, VMEM), "gain": (gain, VMEM)}
        ins |= {name: (w, HBM) for name, w in zip(("gate_hbm", "up_hbm", "down_hbm"), weights)}
        ins |= {name: (value, VMEM) for name, value in extra.items()}
        outs = {}
        scratch = {"w_gate": matrix, "w_up": matrix, "w_down": matrix, "load": SEM((3,))}
        if forward:
            outs |= {
                "middle": vmem_f32(rows, depth),
                "mlp_in": vmem_bf16(size, group_rows, depth),
                "hidden": vmem_bf16(size, group_rows, units),
                "own_out": vmem_f32(rows, depth),
                "out": vmem_bf16(2, tensor_rows, depth),
            }
            self.back = Scatterer("dp", rows, half)
            self.out_rows = Gatherer("tensor", rows, half)
            helpers += [self.back, self.out_rows]
            scratch["kept"] = pltpu.VMEM((group_rows, half), F32)
        if forward and not backward:
            outs |= {"gate": vmem_f32(size, group_rows, units), "up": vmem_f32(size, group_rows, units)}
        if forward and backward:
            outs["grad_mlp"] = vmem_bf16(size, group_rows, depth)
            self.grad_in = Gatherer("dp", rows, half)
            helpers += [self.grad_in]
            scratch |= {
                "gate": pltpu.VMEM((size, group_rows, units), F32),
                "up": pltpu.VMEM((size, group_rows, units), F32),
            }
        if backward:
            outs |= {
                "grad_gate": vmem_bf16(size, group_rows, units),
                "grad_up": vmem_bf16(size, group_rows, units),
                "grad_middle": vmem_f32(rows, depth),
                "mlp_gain_grad": vmem_f32(1, depth),
                "grad_attn": vmem_bf16(2, tensor_rows, depth),
            }
            self.grad_back = Scatterer("dp", rows, half)
            self.grad_rows = Gatherer("tensor", rows, half)
            helpers += [self.grad_back, self.grad_rows]
            scratch["grad_kept"] = pltpu.VMEM((group_rows, half), F32)
        if backward and not forward:
            outs |= {
                "gain_grad": vmem_f32(1, depth),
                "incoming": vmem_bf16(2, tensor_rows, depth),
                "grad_mlp": vmem_bf16(size, group_rows, depth),
            }
            scratch["grad_own"] = pltpu.VMEM((rows, depth), F32)
            self.incoming_rows = Gatherer("tensor", rows, half)
            helpers += [self.incoming_rows]
        super().__init__(ins, outs, scratch, helpers)

    def loads(self):
        pairs = [(self.gate_hbm, self.w_gate), (self.up_hbm, self.w_up), (self.down_hbm, self.w_down)]
        return [
            pltpu.make_async_copy(src, dst, self.load.at[i]) for i, (src, dst) in enumerate(pairs)
        ]

    def prepare(self):
        for copy in self.loads():
            copy.start()
        self.rows_in.prepare(self.terms)

    def start(self):
        self.rows_in.start()
        if self.has_forward and self.has_backward:
            self.grad_in.begin(self.grad_own[...])

    def run(self):
        total = self.rows_in.summed()
        if self.has_forward:
            middle = self.own[...] + total
            self.middle[...] = middle
            mean_sq = jnp.mean(middle * middle, axis=1, keepdims=True)
            self.spread_in.begin(middle * lax.rsqrt(mean_sq + EPSILON) * self.gain[...])
        else:
            result, self.gain_grad[...] = norm_back(total, self.own[...], self.gain[...])
            result = (result + self.add[...]).astype(BF16).astype(F32)
            self.grad_own[...] = result
            self.spread_in.begin(result)
            self.incoming_rows.begin(result)
        for copy in self.loads():
            copy.wait()

        me = lax.axis_index("dp")
        turn = 1 - 2 * (me // (self.size // 2))

        def turned(step):
            return lax.rem(me + turn * step + self.size, self.size)

        if self.has_forward and self.has_backward:
            for place in line_order(self.size):
                self.grad_in.arrive(place)
        self.spread_in.arrive(me)

        @pl.loop(0, self.size)
        def _(step):
            place = turned(step)
            self.spread_in.arrive_over(place)
            if self.has_forward and self.has_backward:
                self.grad_in.arrive_over(place)
                self.grad_in.unpack_place(self.grad_mlp, place)
            if self.has_forward:
                self.spread_in.unpack_place(self.mlp_in, place)
                self.forward_place(place)
            else:
                self.spread_in.unpack_place(self.grad_mlp, place)
            if self.has_backward:
                self.backward_place(place)

            @pl.when(step + 1 < self.size)
            def _():
                self.spread_in.arrive(turned(step + 1))

            if self.has_forward:
                self.back.absorb(place, lambda at: self.kept[:, pl.ds(at, CHUNK)])
            if self.has_backward:
                self.grad_back.absorb(place, lambda at: self.grad_kept[:, pl.ds(at, CHUNK)])

        if self.has_forward:
            output = (self.middle[...] + self.back.collect()).astype(BF16).astype(F32)
            self.own_out[...] = output
            if not self.has_backward:
                self.out_rows.begin(output)
        if self.has_backward:
            values = self.middle if self.has_forward else self.middle_in
            gain = self.gain if self.has_forward else self.mlp_gain
            result, self.mlp_gain_grad[...] = norm_back(
                self.grad_back.collect(), values[...], gain[...]
            )
            result += self.grad_own[...]
            self.grad_middle[...] = result
            self.grad_rows.begin(result)
            if self.has_forward:
                self.out_rows.begin(self.own_out[...])
            self.grad_rows.complete(self.grad_attn)
        if self.has_forward:
            self.out_rows.complete(self.out)
        else:
            self.incoming_rows.complete(self.incoming)

    def unit_tiles(self, body):
        tile = 256

        @pl.loop(0, self.units // tile)
        def _(step):
            body(pl.ds(pl.multiple_of(step * tile, tile), tile))

    def forward_place(self, place):
        def tile(at):
            rows = self.mlp_in[place]
            gate = dot_inner(rows, self.w_gate[at, :])
            up = dot_inner(rows, self.w_up[at, :])
            self.gate[place, :, at] = gate
            self.up[place, :, at] = up
            self.hidden[place, :, at] = (gate * jax.nn.sigmoid(gate) * up).astype(BF16)

        self.unit_tiles(tile)
        self.terms_out(
            place, self.back, self.kept, lambda at: dot(self.hidden[place], self.w_down[:, at])
        )

    def backward_place(self, place):
        def tile(at):
            grad_hidden = dot_inner(self.grad_mlp[place], self.w_down[at, :])
            gate, up = self.gate[place, :, at], self.up[place, :, at]
            share = jax.nn.sigmoid(gate)
            act = gate * share
            self.grad_up[place, :, at] = (grad_hidden * act).astype(BF16)
            self.grad_gate[place, :, at] = (
                grad_hidden * up * (share + act * (1.0 - share))
            ).astype(BF16)

        self.unit_tiles(tile)
        self.terms_out(
            place, self.grad_back, self.grad_kept,
            lambda at: dot(self.grad_gate[place], self.w_gate[:, at])
            + dot(self.grad_up[place], self.w_up[:, at]),
        )

    def terms_out(self, place, scatterer, kept, product):
        rows, half = self.block // 2, self.depth // 2
        first = lax.axis_index("section") == 0

        @pl.loop(0, half // CHUNK)
        def _(step):
            low = pl.multiple_of(step * CHUNK, CHUNK)
            sides = [product(pl.ds(side * half + low, CHUNK)) for side in range(2)]
            trees = [
                jnp.concatenate([side[tree * rows : (tree + 1) * rows] for side in sides], axis=0)
                for tree in range(2)
            ]
            at = pl.ds(low, CHUNK)
            kept[:, at] = jnp.where(first, trees[0], trees[1])
            scatterer.to_sib[place, :, at] = jnp.where(first, trees[1], trees[0]).astype(BF16)

        scatterer.over(place).start()


def hub_plain(terms, own_args, body, own_outs, scatter, gathers):
    total = None
    if scatter:
        mine = lax.psum_scatter(terms, "section", scatter_dimension=0, tiled=True)
        mine = lax.psum_scatter(mine, scatter, scatter_dimension=1, tiled=True)[0]
        total = mine.astype(F32)

    class Cell:
        def __setitem__(self, _, value):
            self.value = value

    cells = [Cell() for _ in own_outs]
    result = body(total, own_args, cells).astype(BF16)
    gathered = [
        lax.all_gather(lax.all_gather(result, axis, axis=0, tiled=True), "section", axis=0)
        for axis in gathers
    ]
    return [cell.value for cell in cells] + gathered


def with_cargo(part, cargo, axes, collective_id, cost_us, vmem=40):
    outs = fused(cargo + [part], axes, bool(cargo), collective_id, cost_us, vmem)
    return outs[-1], outs[:-1]


def norm_back(total, values, gain):
    scale = lax.rsqrt(jnp.mean(values * values, axis=1, keepdims=True) + EPSILON)
    unit = values * scale
    gain_grad = jnp.sum(total * unit, axis=0, keepdims=True)
    scaled = total * gain
    along = jnp.mean(scaled * unit, axis=1, keepdims=True)
    return ((scaled - unit * along) * scale, gain_grad)


def norm_body(total, args, outs):
    middle = args[0] + total
    outs[0][...] = middle
    return rms_scale(middle, args[1])


def add_body(total, args, outs):
    result = args[0] + total
    outs[0][...] = result
    return result


def norm_back_body(total, args, outs):
    result, outs[1][...] = norm_back(total, args[0], args[1])
    result += args[2]
    outs[0][...] = result
    return result


def embed(q_pre, k_pre, q_scale, k_scale, cos_table, sine_table):
    queries = rms_scale(q_pre, q_scale)
    keys = rms_scale(k_pre, k_scale)
    return (
        rotate(queries, cos_table[:, :, None], sine_table[:, :, None]),
        rotate(keys, cos_table, sine_table),
    )


def attn_forward(hidden_in, weights, gains, slot, gather):
    attn_scale, _, q_scale, k_scale = gains
    w_qkv, w_out = weights[:2]
    allowed, cos_table, sine_table = slot
    trees, row_count, depth = hidden_in.shape
    q_width = w_out.shape[0]
    normed = rms_scale(hidden_in.astype(F32), attn_scale).astype(BF16).reshape(-1, depth)
    qkv = dot(normed, w_qkv).reshape(trees, row_count, -1)
    q_pre = qkv[:, :, :q_width].reshape(trees, row_count, -1, HD)
    k_pre = qkv[:, :, q_width : q_width + HD]
    value_bf = qkv[:, :, q_width + HD :].astype(BF16)
    queries, keys_rot = embed(q_pre, k_pre, q_scale, k_scale, cos_table, sine_table)
    query_bf = queries.astype(BF16)
    kv_all = gather(jnp.concatenate([keys_rot.astype(BF16), value_bf], axis=2))
    key_all = kv_all[:, :, :HD]
    value_all = kv_all[:, :, HD:]
    scores = masked_scores(query_bf, key_all, allowed)
    row_max = jnp.max(scores, axis=-1, keepdims=True)
    exp_scores = jnp.exp(scores - row_max)
    row_total = jnp.sum(exp_scores, axis=-1, keepdims=True)
    prob_bf = (exp_scores / row_total).astype(BF16)
    log_total = row_max + jnp.log(row_total)
    attended = jnp.einsum("bgrt,btd->brgd", prob_bf, value_all, preferred_element_type=F32)
    attended_bf = attended.reshape(trees * row_count, -1).astype(BF16)
    terms = dot(attended_bf, w_out).astype(BF16).reshape(trees, row_count, depth)
    saved = (normed, q_pre, k_pre, query_bf, key_all, value_all, log_total, attended_bf)
    return (terms, saved)


def attn_backward(grad_attn, saved, weights, gains, slot, scatter):
    _, _, q_scale, k_scale = gains
    w_qkv, w_out = weights[:2]
    allowed, cos_table, sine_table = slot
    normed, q_pre, k_pre, query_bf, key_all, value_all, log_total, attended_bf = saved
    trees, row_count = query_bf.shape[:2]
    depth = normed.shape[1]
    grad_attn = grad_attn.reshape(-1, depth)
    grad_heads = dot_inner(grad_attn, w_out).astype(BF16).reshape(query_bf.shape)
    scores = masked_scores(query_bf, key_all, allowed)
    prob_full = jnp.exp(scores - log_total)
    grad_prob = jnp.einsum("brgd,btd->bgrt", grad_heads, value_all, preferred_element_type=F32)
    row_dot = jnp.sum(prob_full * grad_prob, axis=-1, keepdims=True)
    grad_scores = (prob_full * (grad_prob - row_dot)).astype(BF16)
    scale_factor = HD ** (-0.5)
    grad_query = (
        jnp.einsum("bgrt,btd->brgd", grad_scores, key_all, preferred_element_type=F32)
        * scale_factor
    )
    grad_key_all = (
        jnp.einsum("bgrt,brgd->btd", grad_scores, query_bf, preferred_element_type=F32)
        * scale_factor
    )
    grad_value_all = jnp.einsum(
        "bgrt,brgd->btd", prob_full.astype(BF16), grad_heads, preferred_element_type=F32
    )
    grad_kv = scatter(jnp.concatenate([grad_key_all, grad_value_all], axis=2).astype(BF16))
    _, embedding_pull = jax.vjp(
        partial(embed, cos_table=cos_table, sine_table=sine_table), q_pre, k_pre, q_scale, k_scale
    )
    grad_q_pre, grad_k_pre, grad_q_scale, grad_k_scale = embedding_pull(
        (grad_query, grad_kv[:, :, :HD].astype(F32))
    )
    qkv_grad = jnp.concatenate(
        [
            grad_q_pre.astype(BF16).reshape(trees, row_count, -1),
            grad_k_pre.astype(BF16),
            grad_kv[:, :, HD:].astype(BF16),
        ],
        axis=2,
    ).reshape(trees * row_count, -1)
    terms = dot_inner(qkv_grad, w_qkv).astype(BF16).reshape(trees, row_count, depth)
    return (terms, [(normed, qkv_grad), (grad_attn, attended_bf)], [grad_q_scale, grad_k_scale])


def plain_layers(hidden, own_in, grad_own, weights, gains, slot, shared_kv):
    depth = own_in.shape[1]
    own_shape = own_in.shape

    def gather(own):
        return lax.all_gather(own, "dp", axis=1, tiled=True)

    def scatter(whole):
        total = lax.psum_scatter(whole, "dp", scatter_dimension=1, tiled=True)
        if shared_kv:
            total = lax.psum(total, "section")
            total = jnp.where(lax.axis_index("section") == 0, total, jnp.zeros_like(total))
        return total

    outputs, kept = [], []
    for layer in range(2):
        _, _, w_gate, w_up, w_down = weights[layer]
        terms, saved = attn_forward(hidden, weights[layer], gains[layer], slot, gather)
        mlp_scale = gains[layer][1][None]
        middle, mlp_in = hub_plain(
            terms, [own_in, mlp_scale], norm_body, [own_shape], "tensor", ["dp"]
        )
        mlp_in = mlp_in.reshape(-1, depth)
        gate, up = dot_inner(mlp_in, w_gate), dot_inner(mlp_in, w_up)
        hidden_bf = swiglu(gate, up).astype(BF16)
        terms = dot(hidden_bf, w_down).astype(BF16).reshape(2, -1, depth)
        kept.append((own_in, saved, middle, mlp_in, gate, up, hidden_bf))
        own_in, hidden = hub_plain(terms, [middle], add_body, [own_shape], "dp", ["tensor"])
        own_in = own_in.astype(BF16).astype(F32)
        outputs.append(hidden)

    own_outs = [own_shape, (1, depth)]
    grads, products, gain_grads = [None, None], [None, None], [None, None]
    (grad_mlp,) = hub_plain(None, [grad_own], lambda total, args, outs: args[0], [], None, ["dp"])
    for layer in (1, 0):
        _, _, w_gate, w_up, w_down = weights[layer]
        own_in, saved, middle, mlp_in, gate, up, hidden_bf = kept[layer]
        grad_mlp = grad_mlp.reshape(-1, depth)
        _, pull = jax.vjp(swiglu, gate, up)
        grad_gate, grad_up = (item.astype(BF16) for item in pull(dot_inner(grad_mlp, w_down)))
        terms = (dot(grad_gate, w_gate) + dot(grad_up, w_up)).astype(BF16).reshape(2, -1, depth)
        grad_middle, mlp_gain_grad, grad_attn = hub_plain(
            terms, [middle, gains[layer][1][None], grad_own], norm_back_body, own_outs, "dp",
            ["tensor"],
        )
        terms, pairs, head_grads = attn_backward(
            grad_attn, saved, weights[layer], gains[layer], slot, scatter
        )
        grad_own, gain_grad, grads[layer], grad_next = hub_plain(
            terms, [own_in, gains[layer][0][None], grad_middle], norm_back_body, own_outs, "tensor",
            ["tensor", "dp"],
        )
        grad_own = grad_own.astype(BF16).astype(F32)
        pairs += [(grad_gate, mlp_in), (grad_up, mlp_in), (hidden_bf, grad_mlp)]
        products[layer] = pairs
        gain_grads[layer] = jnp.concatenate([gain_grad[0], mlp_gain_grad[0], *head_grads])
        grad_mlp = grad_next
    return (outputs, grads, products, gain_grads)


def swap_cores(mine, other):
    core = lax.axis_index("section")
    arrived = lax.ppermute(other, "section", [(0, 1), (1, 0)])
    return (jnp.where(core == 0, mine, arrived), jnp.where(core == 0, arrived, mine))


def on_device(
    inputs, cotangent, seg_ids, parents, order, attn_gain, w_query, w_key, w_value, w_out,
    q_gain, k_gain, mlp_gain, w_gate, w_up, w_down,
):
    core = lax.axis_index("section")
    data_index = lax.axis_index("dp")
    tensor_index = lax.axis_index("tensor")
    dp_size = lax.axis_size("dp")
    tensor_size = lax.axis_size("tensor")
    trees, row_count, depth = inputs.shape
    own_rows = row_count // tensor_size
    row_start = data_index * row_count
    own_depth = w_query.shape[1]
    q_width = w_query.shape[2] // 2
    shared_kv = w_key.shape[2] == HD
    k_width = HD if shared_kv else w_key.shape[2] // 2
    own_units = w_gate.shape[2]
    share = own_units // (2 * dp_size)

    def pick(stacked, index):
        return lax.dynamic_index_in_dim(stacked, index, 0, keepdims=False)

    fast = (
        own_rows % 8 == 0
        and depth % (2 * CHUNK) == 0
        and row_count % 16 == 0
        and share % 16 == 0
        and own_depth % 128 == 0
        and not shared_kv
    )

    def halves(width, array):
        return [array[:, :width], array[:, array.shape[1] - width :]]

    unit_mats = [w_gate[0].T, w_up[0].T, w_down[0]]
    qkv_width = q_width + 2 * k_width
    gains_own = jnp.concatenate([attn_gain[0], mlp_gain[0], q_gain[0], k_gain[0]]).astype(F32)

    def spread_units(rows):
        return lax.all_gather(rows, "tensor", axis=0, tiled=True)

    def tied(value, *before):
        return lax.optimization_barrier((value, *before))[0]

    if fast:
        line = ["section", "dp"]
        everyone = ["section", "dp", "tensor"]
        (gate_rows, up_rows), (gains_all,) = fused(
            [UnitsOut(unit_mats[:2], 0), SharedRows(gains_own.reshape(-1, 128))], line, True, 1, 45
        )
        shards = AttnShards(w_query[0], w_key[0], w_value[0], w_out[0])
        shards.arrays[0] = tied(shards.arrays[0], gate_rows)
        (w_qkv, w_heads), (down_rows,), (attn_shard,) = fused(
            [AttnOut(shards, 0), UnitsOut(unit_mats[2:], 0), HalfOver(shards)], line, True, 2, 80
        )
        first_weights = [w_qkv, w_heads, spread_units(gate_rows), spread_units(up_rows)]
        attn_next = lax.all_gather(attn_shard, "dp", axis=0)
    else:
        gains_all = lax.all_gather(gains_own, ("section", "dp"))
        attn_halves = jnp.stack(
            [
                jnp.concatenate(parts, axis=1)
                for parts in zip(
                    halves(q_width, w_query[0]),
                    halves(k_width, w_key[0]),
                    halves(k_width, w_value[0]),
                    halves(q_width, w_out[0].T),
                )
            ]
        )
        attn_shards = swap_cores(pick(attn_halves, core), pick(attn_halves, 1 - core))
        unit_blocks = jnp.stack(unit_mats).reshape(3, 2, dp_size, share, own_depth)
        unit_blocks = unit_blocks.transpose(1, 2, 0, 3, 4)
        unit_shards = swap_cores(pick(unit_blocks, core), pick(unit_blocks, 1 - core))
        both_weights = []
        for layer in range(2):
            attn_all = lax.all_gather(attn_shards[layer], "dp", axis=0, tiled=True)
            pieces = exchange(unit_shards[layer], "dp")
            pieces = pieces.transpose(1, 2, 0, 3).reshape(3, share, depth)
            both_weights.append(
                (
                    attn_all[:, :qkv_width], attn_all[:, qkv_width:].T,
                    *(spread_units(pieces[i]) for i in range(3)),
                )
            )

    gains_all = gains_all.reshape(2, dp_size, -1)
    gains = [
        (
            gains_all[layer, :, :own_depth].reshape(depth),
            gains_all[layer, :, own_depth : 2 * own_depth].reshape(depth),
            gains_all[layer, 0, 2 * own_depth : 2 * own_depth + HD],
            gains_all[layer, 0, 2 * own_depth + HD :],
        )
        for layer in range(2)
    ]

    def slot_setup(slot_index):
        tree_id = pick(order, slot_index)
        allowed, row_positions = path_mask(
            pick(seg_ids, tree_id), pick(parents, tree_id), row_start, row_count
        )
        cos_table, sine_table = rope_tables(row_positions, HD)
        return (pick(inputs, tree_id), allowed, cos_table[:, 0], sine_table[:, 0])

    setups = [slot_setup(i) for i in range(trees)]
    hidden, *slot = (jnp.stack(item) for item in zip(*setups))

    def own_part(whole):
        return lax.dynamic_slice_in_dim(
            pick(whole, core), tensor_index * own_rows, own_rows, 0
        )

    own_in = own_part(hidden).astype(F32)
    grad_own = own_part(cotangent).astype(F32)

    def weight_products(pairs):
        return [dot_outer(left, right).astype(BF16) for left, right in pairs]

    def scatter_units(products):
        return [
            lax.psum_scatter(item, "tensor", scatter_dimension=0, tiled=True) for item in products
        ]

    def scatter_shards(products):
        return lax.psum_scatter(
            jnp.concatenate(products, axis=1), "dp", scatter_dimension=0, tiled=True
        )

    if fast:
        def units_on(*which):
            return [UnitsOut([unit_mats[i] for i in which], 1)]

        def kv_gather(own, cargo, collective_id, carried):
            (whole,), outs = with_cargo(GatherKV(own), cargo, everyone, collective_id, 40)
            carried += outs
            return whole.reshape(trees, -1, 2 * HD)

        def kv_scatter(whole, cargo, collective_id, carried):
            part = ScatterKV(whole.reshape(trees, dp_size, row_count, 2 * HD))
            (total,), outs = with_cargo(part, cargo, line, collective_id, 30)
            carried += outs
            return total

        def flat(array):
            return array.reshape(-1, array.shape[-1])

        carried = []
        terms, saved_first = attn_forward(
            hidden, first_weights, gains[0], slot,
            lambda own: kv_gather(
                tied(own, *first_weights[2:]), [UnitsSpread(down_rows)] + units_on(0), 3, carried
            ),
        )
        (down_all,), (gate_rows,) = carried
        first_weights.append(down_all)
        part = FeedForward(
            terms, own_in, gains[0][1][None], first_weights[2:], True, False, {}
        )
        outs, ((up_rows, down_rows),) = with_cargo(part, units_on(1, 2), everyone, 4, 90, 56)
        middle_first, mlp_in_first, hidden_first, own_next, output_first, gate_first, up_first = outs
        second_weights = [
            attn_next[:, :own_depth].reshape(depth, -1),
            attn_next[:, own_depth:].transpose(1, 0, 2).reshape(q_width, depth),
            spread_units(gate_rows), spread_units(up_rows),
        ]
        carried = []
        terms, saved_second = attn_forward(
            output_first, second_weights, gains[1], slot,
            lambda own: kv_gather(
                tied(own, second_weights[2]), [UnitsSpread(down_rows)], 5, carried
            ),
        )
        ((down_all,),) = carried
        second_weights.append(down_all)
        part = FeedForward(
            terms, own_next, gains[1][1][None], second_weights[2:], True, True,
            {"grad_own": grad_own},
        )
        outs, _ = with_cargo(part, [], everyone, 6, 100, 60)
        (
            middle, mlp_in, hidden_bf, _, output_second, grad_mlp,
            grad_gate, grad_up, grad_middle, mlp_gain_second, grad_attn,
        ) = outs
        unit_second = scatter_units(
            weight_products(
                [
                    (flat(grad_gate), flat(mlp_in)),
                    (flat(grad_up), flat(mlp_in)),
                    (flat(hidden_bf), flat(grad_mlp)),
                ]
            )
        )
        terms, pairs, head_second = attn_backward(
            grad_attn, saved_second, second_weights, gains[1], slot,
            lambda whole: kv_scatter(whole, [], 7, []),
        )
        attn_second = scatter_shards(weight_products(pairs))
        part = FeedForward(
            terms, own_next, gains[1][0][None], first_weights[2:], False, True,
            {
                "add": grad_middle, "gate": gate_first, "up": up_first,
                "middle_in": middle_first, "mlp_gain": gains[0][1][None],
            },
        )
        outs, _ = with_cargo(part, [], everyone, 8, 90, 60)
        (
            grad_gate, grad_up, grad_middle, mlp_gain_first, grad_attn,
            attn_gain_second, incoming_second, grad_mlp,
        ) = outs
        unit_first = scatter_units(
            weight_products(
                [
                    (flat(grad_gate), flat(mlp_in_first)),
                    (flat(grad_up), flat(mlp_in_first)),
                    (flat(hidden_first), flat(grad_mlp)),
                ]
            )
        )
        carried = []
        terms, pairs, head_first = attn_backward(
            grad_attn, saved_first, first_weights, gains[0], slot,
            lambda whole: kv_scatter(whole, [UnitsHome(unit_second, 1)], 9, carried),
        )
        (home_second,) = carried
        whole = jnp.concatenate(weight_products(pairs), axis=1).reshape(dp_size, 4, -1, q_width + qkv_width)
        part = LastHub(terms, own_in, gains[0][0][None], grad_middle)
        (attn_gain_first, incoming_first), ((attn_first,),) = with_cargo(
            part, [ScatterKV(whole.transpose(1, 0, 2, 3))], everyone, 10, 60, 56
        )
        attn_first = attn_first.reshape(own_depth, -1).astype(BF16)
        outputs = [output_first, output_second]
        grads = [incoming_first, incoming_second]
        weight_grads = [(attn_first, None), (attn_second, None)]
        gain_grads = [
            jnp.concatenate([attn_gain_first[0], mlp_gain_first[0], *head_first]),
            jnp.concatenate([attn_gain_second[0], mlp_gain_second[0], *head_second]),
        ]
    else:
        outputs, grads, products, gain_grads = plain_layers(
            hidden, own_in, grad_own, both_weights, gains, slot, shared_kv
        )
        weight_grads = []
        for pairs in products:
            whole = weight_products(pairs)
            weight_grads.append((scatter_shards(whole[:2]), scatter_units(whole[2:])))

    gain_total = jnp.stack(gain_grads)
    if fast:
        mine = jnp.where(core == 0, weight_grads[0][0], weight_grads[1][0])
        other = jnp.where(core == 0, weight_grads[1][0], weight_grads[0][0])
        (gain_total,), (arrived,), home_first = fused(
            [TotalOverAll(gain_total.reshape(-1, 128)), Swap(other), UnitsHome(unit_first, 0)],
            everyone, True, 11, 60,
        )
        attn_home = (jnp.where(core == 0, mine, arrived), jnp.where(core == 0, arrived, mine))
        unit_home = [
            jnp.where(core == 0, first, second) for first, second in zip(home_first, home_second)
        ]
        gain_total = gain_total.reshape(2, -1)
    else:
        def bring_home(first, second):
            mine, other = jnp.where(core == 0, first, second), jnp.where(core == 0, second, first)
            arrived = lax.ppermute(other, "section", [(0, 1), (1, 0)])
            return (jnp.where(core == 0, mine, arrived), jnp.where(core == 0, arrived, mine))

        def pieces_of(grad):
            return exchange(
                jnp.stack(grad).reshape(3, share, dp_size, own_depth).transpose(2, 0, 1, 3), "dp"
            )

        attn_home = bring_home(weight_grads[0][0], weight_grads[1][0])
        unit_home = jnp.stack(bring_home(pieces_of(weight_grads[0][1]), pieces_of(weight_grads[1][1])))
        unit_home = unit_home.transpose(2, 0, 1, 3, 4).reshape(3, own_units, own_depth)
        gain_total = lax.psum(gain_total, ("section", "dp", "tensor"))

    def joined(start, width):
        parts = [half[:, start : start + width] for half in attn_home]
        if shared_kv and start in (q_width, q_width + k_width):
            return parts[0].astype(F32)
        return jnp.concatenate(parts, axis=1).astype(F32)

    gain_own = pick(gain_total, core)
    share_width = attn_gain.shape[1]
    attn_gain_grad = lax.dynamic_slice_in_dim(gain_own, data_index * share_width, share_width, 0)
    mlp_gain_grad = lax.dynamic_slice_in_dim(
        gain_own, depth + data_index * share_width, share_width, 0
    )
    return (
        jnp.where(core == 0, outputs[0], outputs[1])[None],
        jnp.where(core == 0, grads[0], grads[1])[None],
        attn_gain_grad[None],
        joined(0, q_width)[None],
        joined(q_width, k_width)[None],
        joined(q_width + k_width, k_width)[None],
        joined(qkv_width, q_width).T[None],
        gain_own[2 * depth : 2 * depth + HD][None],
        gain_own[2 * depth + HD :][None],
        mlp_gain_grad[None],
        unit_home[0].T.astype(F32)[None],
        unit_home[1].T.astype(F32)[None],
        unit_home[2].astype(F32)[None],
    )


def solution(mesh):
    rows = P(None, "dp", None)
    wide = P("section", "dp", "tensor")
    tall = P("section", "tensor", "dp")
    gain = P("section", "dp")
    head_gain = P("section", None)
    slots = P("section", None, "dp", None)
    in_specs = (
        rows, rows, P(), P(), P(), gain, wide, wide, wide, tall, head_gain, head_gain, gain,
        wide, wide, tall,
    )
    out_specs = (
        slots, slots, gain, wide, wide, wide, tall, head_gain, head_gain, gain, wide, wide, tall,
    )
    return jax.shard_map(
        on_device, mesh=mesh, in_specs=in_specs, out_specs=out_specs, check_vma=False
    )
```

```python
from functools import partial

import jax
import jax.numpy as jnp
from jax import lax
from jax.experimental import pallas as pl
from jax.experimental.pallas import tpu as pltpu
from jax.sharding import PartitionSpec as P

HD = 128
TRUNK = 512
BRANCH = 96
NB = 4
TREE = 1152
SEGS = 9


EPSILON = 1e-06
THETA = 1000000.0
MASKED = -1e30
F32 = jnp.float32
BF16 = jnp.bfloat16


def rms_scale(values, weight_gain):
    mean_sq = jnp.mean(values * values, axis=-1, keepdims=True)
    return values * lax.rsqrt(mean_sq + EPSILON) * weight_gain


def rotate(values, cos_table, sine_table):
    middle_at = values.shape[-1] // 2
    leading = values[..., :middle_at]
    trailing = values[..., middle_at:]
    return jnp.concatenate(
        [leading * cos_table - trailing * sine_table, trailing * cos_table + leading * sine_table],
        axis=-1,
    )


def rope_tables(positions, head_dim):
    half_steps = jnp.arange(head_dim // 2, dtype=F32)
    inverse = THETA ** (-2.0 * half_steps / head_dim)
    angles = positions.astype(F32)[:, None] * inverse[None, :]
    return (jnp.cos(angles)[:, None, :], jnp.sin(angles)[:, None, :])


def swiglu(gate_in, up_in):
    return jax.nn.silu(gate_in) * up_in


def embed_heads(q_pre, k_pre, q_scale, k_scale, cos_table, sine_table):
    row_count = q_pre.shape[0]
    queries = rms_scale(q_pre.reshape(row_count, -1, HD), q_scale)
    keys_part = rms_scale(k_pre.reshape(row_count, -1, HD), k_scale)
    return (rotate(queries, cos_table, sine_table), rotate(keys_part, cos_table, sine_table))


def tree_layout(seg_row, parent_row):
    labels = jnp.arange(SEGS, dtype=jnp.int32)
    places = jnp.arange(TREE, dtype=jnp.int32)
    member = seg_row[None, :] == labels[:, None]
    starts = jnp.min(jnp.where(member, places[None, :], TREE), axis=1)
    depth_base = jnp.where(labels == 0, 0, jnp.where(labels <= NB, TRUNK, TRUNK + BRANCH))
    shifts = depth_base - starts
    positions = places + jnp.sum(jnp.where(member, shifts[:, None], 0), axis=0)
    grandparent = jnp.sum(
        jnp.where(parent_row[:, None] == labels[None, :], parent_row[None, :], 0), axis=1
    )
    ancestor = (
        (labels[None, :] == labels[:, None])
        | (labels[None, :] == parent_row[:, None])
        | (labels[None, :] == grandparent[:, None])
    )
    return (positions, member.astype(F32), ancestor.astype(F32))


def path_mask(seg_row, parent_row, row_start, row_count):
    positions, member, ancestor = tree_layout(seg_row, parent_row)
    member_rows = lax.dynamic_slice_in_dim(member, row_start, row_count, 1)
    seg_rows = lax.dynamic_slice_in_dim(seg_row, row_start, row_count, 0)
    reach_table = jnp.dot(jnp.dot(member_rows.T, ancestor), member)
    places = jnp.arange(TREE, dtype=jnp.int32)
    row_places = row_start + jnp.arange(row_count, dtype=jnp.int32)
    same_seg = seg_rows[:, None] == seg_row[None, :]
    causal = places[None, :] <= row_places[:, None]
    allowed = (reach_table > 0.5) & (jnp.logical_not(same_seg) | causal)
    row_positions = lax.dynamic_slice_in_dim(positions, row_start, row_count, 0)
    return (allowed, row_positions)


OUTER = (((0,), (0,)), ((), ()))
INNER = (((1,), (1,)), ((), ()))


def dot(left, right):
    return jnp.dot(left, right, preferred_element_type=F32)


def dot_inner(left, right):
    return lax.dot_general(left, right, INNER, preferred_element_type=F32)


def dot_outer(left, right):
    return lax.dot_general(left, right, OUTER, preferred_element_type=F32)


def exchange(pieces, axis):
    size = lax.axis_size(axis)
    me = lax.axis_index(axis)
    got = jnp.zeros_like(pieces)
    own = lax.dynamic_index_in_dim(pieces, me, 0, keepdims=True)
    got = lax.dynamic_update_slice_in_dim(got, own, me, 0)
    for step in range(1, size):
        other = me ^ step
        piece = lax.dynamic_index_in_dim(pieces, other, 0, keepdims=True)
        arrived = lax.ppermute(piece, axis, [(i, i ^ step) for i in range(size)])
        got = lax.dynamic_update_slice_in_dim(got, arrived, other, 0)
    return got


def masked_scores(query_bf, key_all, allowed):
    raw_scores = jnp.einsum(
        "brgd,btd->bgrt", query_bf, key_all, preferred_element_type=F32
    ) * HD ** (-0.5)
    return jnp.where(allowed[:, None], raw_scores, MASKED)


MESH = pl.DeviceIdType.MESH
CHUNK = 256
SEM = pltpu.SemaphoreType.DMA
VMEM = pl.BlockSpec(memory_space=pltpu.VMEM)
HBM = pl.BlockSpec(memory_space=pl.ANY)


def remote(src, dst, send_sem, recv_sem, device_id):
    return pltpu.make_async_remote_copy(
        src_ref=src, dst_ref=dst, send_sem=send_sem, recv_sem=recv_sem,
        device_id=device_id, device_id_type=MESH,
    )


def greet(axes, across):
    barrier = pltpu.get_barrier_semaphore()
    count = 0
    for axis in axes:
        size = lax.axis_size(axis)
        me = lax.axis_index(axis)
        for step in range(1, size):
            pl.semaphore_signal(
                barrier, inc=1, device_id={axis: lax.rem(me + step, size)}, device_id_type=MESH
            )
        count += size - 1
    if across:
        size = lax.axis_size("dp")
        me = lax.axis_index("dp")
        sibling = 1 - lax.axis_index("section")
        for step in range(1, size):
            pl.semaphore_signal(
                barrier, inc=1, device_id={"section": sibling, "dp": lax.rem(me + step, size)},
                device_id_type=MESH,
            )
        count += size - 1
    pl.semaphore_wait(barrier, count)


class Part:
    ins, outs, scratch = (), (), ()

    def bind(self, ins, outs, scratch):
        self.in_refs, self.out_refs, self.refs = ins, outs, scratch

    def prepare(self):
        pass

    def start(self):
        pass

    def run(self):
        pass

    def finish(self):
        pass


def fused(parts, axes, across, collective_id, cost_us, vmem=40):
    counts = [(len(part.ins), len(part.outs), len(part.scratch)) for part in parts]

    def kernel(*refs):
        refs = list(refs)
        groups = []
        for kind in range(3):
            groups.append([])
            for count in counts:
                groups[kind].append(refs[: count[kind]])
                del refs[: count[kind]]
        for part, ins, outs, scratch in zip(parts, *groups):
            part.bind(ins, outs, scratch)
        for part in parts:
            part.prepare()
        greet(axes, across)
        for part in parts:
            part.start()
        for part in reversed(parts):
            part.run()
        for part in parts:
            part.finish()

    ins = [item for part in parts for item in part.ins]
    outs = [item for part in parts for item in part.outs]
    results = pl.pallas_call(
        kernel,
        out_shape=[item[0] for item in outs],
        in_specs=[item[1] for item in ins],
        out_specs=[item[1] for item in outs],
        scratch_shapes=[item for part in parts for item in part.scratch],
        cost_estimate=pl.CostEstimate(
            flops=0, bytes_accessed=cost_us * 3_000_000, transcendentals=0
        ),
        compiler_params=pltpu.CompilerParams(
            collective_id=collective_id, has_side_effects=True, vmem_limit_bytes=vmem << 20
        ),
    )(*[item[0] for item in ins])
    results = list(results)
    split = []
    for count in counts:
        split.append(results[: count[1]])
        del results[: count[1]]
    return split


def columns_of(place, width):
    return pl.ds(pl.multiple_of(place * width, width), width)


class UnitsOut(Part):
    def __init__(self, mats, layer):
        self.layer, self.count = layer, len(mats)
        self.size = lax.axis_size("dp")
        rows, self.width = mats[0].shape
        self.share = rows // (2 * self.size)
        self.ins = [(mat, HBM) for mat in mats]
        shape = jax.ShapeDtypeStruct((self.share, self.size * self.width), BF16)
        self.outs = [(shape, HBM)] * self.count
        self.scratch = [SEM((self.count,)), SEM((self.count, 2, self.size)), SEM((self.count, self.size))]

    def bind(self, ins, outs, scratch):
        self.src, self.dst = ins, outs
        self.keep, self.send, self.recv = scratch
        self.core, self.me = lax.axis_index("section"), lax.axis_index("dp")

    def piece(self, index, core, place):
        start = pl.multiple_of((core * self.size + place) * self.share, self.share)
        return self.src[index].at[pl.ds(start, self.share)]

    def lands(self, index, slot):
        return self.dst[index].at[:, columns_of(slot, self.width)]

    def copy(self, index, core, place, slot):
        return remote(
            self.piece(index, core, place), self.lands(index, slot),
            self.send.at[index, core, place], self.recv.at[index, slot],
            {"section": core, "dp": place},
        )

    def local(self, index):
        return pltpu.make_async_copy(
            self.piece(index, self.layer, self.me), self.lands(index, self.me), self.keep.at[index]
        )

    def targets(self):
        for index in range(self.count):
            for core in range(2):
                for place in range(self.size):
                    yield index, core, place, (place != self.me) | (core != self.layer)

    def start(self):
        @pl.when(self.core == self.layer)
        def _():
            for index, core, place, is_other in self.targets():
                @pl.when(is_other)
                def _():
                    self.copy(index, core, place, self.me).start()

            for index in range(self.count):
                self.local(index).start()

    def finish(self):
        for index in range(self.count):
            for place in range(self.size):
                @pl.when((self.core != self.layer) | (place != self.me))
                def _():
                    self.copy(index, 0, 0, place).wait_recv()

        @pl.when(self.core == self.layer)
        def _():
            for index, core, place, is_other in self.targets():
                @pl.when(is_other)
                def _():
                    self.copy(index, core, place, self.me).wait_send()

            for index in range(self.count):
                self.local(index).wait()


class UnitsHome(Part):
    def __init__(self, mats, layer):
        self.layer, self.count = layer, len(mats)
        self.size = lax.axis_size("dp")
        self.share, depth = mats[0].shape
        self.width = depth // self.size
        self.ins = [(mat, HBM) for mat in mats]
        shape = jax.ShapeDtypeStruct((2 * self.size * self.share, self.width), BF16)
        self.outs = [(shape, HBM)] * self.count
        self.scratch = [SEM((self.count,)), SEM((self.count, self.size)), SEM((self.count, 2, self.size))]

    def bind(self, ins, outs, scratch):
        self.src, self.dst = ins, outs
        self.keep, self.send, self.recv = scratch
        self.core, self.me = lax.axis_index("section"), lax.axis_index("dp")

    def lands(self, index, core, slot):
        start = pl.multiple_of((core * self.size + slot) * self.share, self.share)
        return self.dst[index].at[pl.ds(start, self.share)]

    def copy(self, index, place, core, slot):
        return remote(
            self.src[index].at[:, columns_of(place, self.width)], self.lands(index, core, slot),
            self.send.at[index, place], self.recv.at[index, core, slot],
            {"section": self.layer, "dp": place},
        )

    def local(self, index):
        return pltpu.make_async_copy(
            self.src[index].at[:, columns_of(self.me, self.width)],
            self.lands(index, self.layer, self.me), self.keep.at[index],
        )

    def start(self):
        for index in range(self.count):
            for place in range(self.size):
                @pl.when((self.core != self.layer) | (place != self.me))
                def _():
                    self.copy(index, place, self.core, self.me).start()

            @pl.when(self.core == self.layer)
            def _():
                self.local(index).start()

    def finish(self):
        for index in range(self.count):
            @pl.when(self.core == self.layer)
            def _():
                for core in range(2):
                    for place in range(self.size):
                        @pl.when((core != self.layer) | (place != self.me))
                        def _():
                            self.copy(index, 0, core, place).wait_recv()

                self.local(index).wait()

            for place in range(self.size):
                @pl.when((self.core != self.layer) | (place != self.me))
                def _():
                    self.copy(index, place, self.core, self.me).wait_send()


class UnitsSpread(Part):
    def __init__(self, rows):
        self.size = lax.axis_size("tensor")
        self.share, depth = rows.shape
        self.ins = [(rows, HBM)]
        self.outs = [(jax.ShapeDtypeStruct((self.size * self.share, depth), BF16), HBM)]
        self.scratch = [SEM, SEM((self.size,)), SEM((self.size,))]

    def bind(self, ins, outs, scratch):
        (self.src,), (self.dst,), (self.keep, self.send, self.recv) = ins, outs, scratch
        self.me = lax.axis_index("tensor")

    def lands(self, slot):
        return self.dst.at[pl.ds(pl.multiple_of(slot * self.share, self.share), self.share)]

    def copy(self, place, slot):
        return remote(
            self.src, self.lands(slot), self.send.at[place], self.recv.at[slot], {"tensor": place}
        )

    def start(self):
        for place in range(self.size):
            @pl.when(place != self.me)
            def _():
                self.copy(place, self.me).start()

        pltpu.make_async_copy(self.src, self.lands(self.me), self.keep).start()

    def finish(self):
        for place in range(self.size):
            @pl.when(place != self.me)
            def _():
                self.copy(place, place).wait_recv()
                self.copy(place, self.me).wait_send()

        pltpu.make_async_copy(self.src, self.lands(self.me), self.keep).wait()


class SharedRows(Part):
    def __init__(self, own):
        self.size = lax.axis_size("dp")
        self.ins = [(own, VMEM)]
        self.outs = [(jax.ShapeDtypeStruct((2, self.size) + own.shape, F32), VMEM)]
        self.scratch = [SEM((2, self.size)), SEM((2, self.size))]

    def copy(self, core, place, from_core, from_place):
        return remote(
            self.in_refs[0], self.out_refs[0].at[from_core, from_place],
            self.refs[0].at[core, place], self.refs[1].at[from_core, from_place],
            {"section": core, "dp": place},
        )

    def others(self):
        core, me = lax.axis_index("section"), lax.axis_index("dp")
        for other in range(2):
            for place in range(self.size):
                yield other, place, (other != core) | (place != me)

    def start(self):
        core, me = lax.axis_index("section"), lax.axis_index("dp")
        for other, place, is_other in self.others():
            @pl.when(is_other)
            def _():
                self.copy(other, place, core, me).start()

        self.out_refs[0][core, me] = self.in_refs[0][...]

    def finish(self):
        core, me = lax.axis_index("section"), lax.axis_index("dp")
        for other, place, is_other in self.others():
            @pl.when(is_other)
            def _():
                self.copy(other, place, other, place).wait_recv()
                self.copy(other, place, core, me).wait_send()


def far_pair(place, me):
    return (place + me == 3) & ((place == 0) | (place == 3))


def line_relays(size):
    return [(2, 0, 3), (1, 3, 0)] if size == 4 else []


def line_order(size):
    return [1, 2, 0, 3] if size == 4 else list(range(size))


class AttnShards:
    def __init__(self, w_query, w_key, w_value, w_out):
        self.arrays = [w_query, w_key, w_value, w_out]
        self.depth = w_query.shape[0]
        self.q_width, self.k_width = w_query.shape[1] // 2, w_key.shape[1] // 2
        self.width = self.q_width + 2 * self.k_width
        half = self.depth // 2
        parts = self.q_width // 2
        self.items = [
            (0, lambda ref, core: ref.at[pl.ds(0, half), columns_of(core, self.q_width)]),
            (0, lambda ref, core: ref.at[pl.ds(half, half), columns_of(core, self.q_width)]),
            (1, lambda ref, core: ref.at[:, columns_of(core, self.k_width)]),
            (2, lambda ref, core: ref.at[:, columns_of(core, self.k_width)]),
            (3, lambda ref, core: ref.at[pl.ds(core * self.q_width, parts)]),
            (3, lambda ref, core: ref.at[pl.ds(core * self.q_width + parts, parts)]),
        ]
        q_width, k_width, depth = self.q_width, self.k_width, self.depth
        self.qkv_rows = [(0, half), (half, half), (0, depth), (0, depth)]
        self.qkv_columns = [
            (0, q_width), (0, q_width), (q_width, k_width), (q_width + k_width, k_width)
        ]
        self.out_rows = [(0, parts), (parts, parts)]

    def source(self, refs, index, core):
        array, cut = self.items[index]
        return cut(refs[array], core)

    def lands(self, qkv, out, index, slot):
        if index < 4:
            (start, rows), (left, columns) = self.qkv_rows[index], self.qkv_columns[index]
            at = pl.multiple_of(slot * self.depth + start, rows)
            return qkv.at[pl.ds(at, rows), pl.ds(left, columns)]
        start, rows = self.out_rows[index - 4]
        return out.at[pl.ds(start, rows), columns_of(slot, self.depth)]


class AttnOut(Part):
    def __init__(self, shards, layer):
        self.layer, self.shards = layer, shards
        self.size = lax.axis_size("dp")
        self.count = len(shards.items)
        depth = self.size * shards.depth
        self.ins = [(array, HBM) for array in shards.arrays]
        self.outs = [
            (jax.ShapeDtypeStruct((depth, shards.width), BF16), HBM),
            (jax.ShapeDtypeStruct((shards.q_width, depth), BF16), HBM),
        ]
        self.scratch = [
            SEM((self.count,)), SEM((2, self.size, self.count)), SEM((self.size, self.count)),
            SEM((self.count,)),
        ]

    def bind(self, ins, outs, scratch):
        self.src = ins
        self.qkv, self.out = outs
        self.keep, self.send, self.recv, self.relay_send = scratch
        self.core, self.me = lax.axis_index("section"), lax.axis_index("dp")

    def lands(self, index, slot):
        return self.shards.lands(self.qkv, self.out, index, slot)

    def copy(self, core, place, slot, index):
        return remote(
            self.shards.source(self.src, index, core), self.lands(index, slot),
            self.send.at[core, place, index], self.recv.at[slot, index],
            {"section": core, "dp": place},
        )

    def relay(self, source, target, index):
        block = self.lands(index, source)
        return remote(
            block, block, self.relay_send.at[index], self.recv.at[source, index], {"dp": target}
        )

    def local(self, index):
        return pltpu.make_async_copy(
            self.shards.source(self.src, index, self.layer), self.lands(index, self.me),
            self.keep.at[index],
        )

    def targets(self):
        for index in range(self.count):
            for core in range(2):
                for place in range(self.size):
                    sent = (place != self.me) | (core != self.layer)
                    if self.size == 4:
                        sent = sent & jnp.logical_not(far_pair(place, self.me))
                    yield core, place, index, sent

    def start(self):
        @pl.when(self.core == self.layer)
        def _():
            for core, place, index, sent in self.targets():
                @pl.when(sent)
                def _():
                    self.copy(core, place, self.me, index).start()

            for index in range(self.count):
                self.local(index).start()

    def run(self):
        for index in range(self.count):
            for place in line_order(self.size):
                @pl.when((self.core != self.layer) | (place != self.me))
                def _():
                    self.copy(0, 0, place, index).wait_recv()

                for via, source, target in line_relays(self.size):
                    if source == place:
                        @pl.when(self.me == via)
                        def _():
                            self.relay(source, target, index).start()

    def finish(self):
        @pl.when(self.core == self.layer)
        def _():
            for core, place, index, sent in self.targets():
                @pl.when(sent)
                def _():
                    self.copy(core, place, self.me, index).wait_send()

            for index in range(self.count):
                self.local(index).wait()

        for via, source, target in line_relays(self.size):
            @pl.when(self.me == via)
            def _():
                for index in range(self.count):
                    self.relay(source, target, index).wait_send()


class HalfOver(Part):
    def __init__(self, shards):
        self.shards = shards
        self.count = len(shards.items)
        rows = shards.depth + shards.q_width
        self.ins = [(array, HBM) for array in shards.arrays]
        self.outs = [(jax.ShapeDtypeStruct((rows, shards.depth), BF16), HBM)]
        self.scratch = [SEM((self.count,)), SEM((self.count,)), SEM((self.count,))]

    def lands(self, index):
        depth, q_width = self.shards.depth, self.shards.q_width
        packed = self.out_refs[0]
        return self.shards.lands(
            packed.at[pl.ds(0, depth)], packed.at[pl.ds(depth, q_width)], index, 0
        )

    def over(self, index):
        return remote(
            self.shards.source(self.in_refs, index, 0), self.lands(index), self.refs[0].at[index],
            self.refs[1].at[index], {"section": 0},
        )

    def keep(self, index):
        return pltpu.make_async_copy(
            self.shards.source(self.in_refs, index, 1), self.lands(index), self.refs[2].at[index]
        )

    def start(self):
        @pl.when(lax.axis_index("section") == 1)
        def _():
            for index in range(self.count):
                self.over(index).start()
                self.keep(index).start()

    def finish(self):
        @pl.when(lax.axis_index("section") == 1)
        def _():
            for index in range(self.count):
                self.over(index).wait_send()
                self.keep(index).wait()

        @pl.when(lax.axis_index("section") == 0)
        def _():
            for index in range(self.count):
                self.over(index).wait_recv()


class Swap(Part):
    def __init__(self, own):
        self.ins = [(own, HBM)]
        self.outs = [(jax.ShapeDtypeStruct(own.shape, own.dtype), HBM)]
        self.scratch = [SEM, SEM]

    def start(self):
        sibling = 1 - lax.axis_index("section")
        self.copy = remote(
            self.in_refs[0], self.out_refs[0], self.refs[0], self.refs[1], {"section": sibling}
        )
        self.copy.start()

    def finish(self):
        self.copy.wait()


class GatherKV(Part):
    def __init__(self, own):
        trees, rows, width = own.shape
        self.trees, self.size = trees, lax.axis_size("dp")
        self.ins = [(own, VMEM)]
        self.outs = [(jax.ShapeDtypeStruct((trees, self.size, rows, width), BF16), VMEM)]
        self.scratch = [SEM((self.size, trees)), SEM((self.size, trees)), SEM((trees,))]

    def bind(self, ins, outs, scratch):
        (self.own,), (self.out,) = ins, outs
        self.send, self.recv, self.relay_send = scratch
        self.me = lax.axis_index("dp")

    def copy(self, place, slot, tree):
        return remote(
            self.own.at[tree], self.out.at[tree, slot], self.send.at[place, tree],
            self.recv.at[slot, tree], {"dp": place},
        )

    def relay(self, source, target, tree):
        return remote(
            self.out.at[tree, source], self.out.at[tree, source], self.relay_send.at[tree],
            self.recv.at[source, tree], {"dp": target},
        )

    def targets(self):
        for tree in range(self.trees):
            for place in range(self.size):
                sent = place != self.me
                if self.size == 4:
                    sent = sent & jnp.logical_not(far_pair(place, self.me))
                yield place, tree, sent

    def start(self):
        for place, tree, sent in self.targets():
            @pl.when(sent)
            def _():
                self.copy(place, self.me, tree).start()

        self.out[:, self.me] = self.own[...]

    def run(self):
        for tree in range(self.trees):
            for place in line_order(self.size):
                @pl.when(place != self.me)
                def _():
                    self.copy(place, place, tree).wait_recv()

                for via, source, target in line_relays(self.size):
                    if source == place:
                        @pl.when(self.me == via)
                        def _():
                            self.relay(source, target, tree).start()

    def finish(self):
        for place, tree, sent in self.targets():
            @pl.when(sent)
            def _():
                self.copy(place, self.me, tree).wait_send()

        for via, source, target in line_relays(self.size):
            @pl.when(self.me == via)
            def _():
                for tree in range(self.trees):
                    self.relay(source, target, tree).wait_send()


class ScatterKV(Part):
    def __init__(self, whole):
        trees, size, rows, width = whole.shape
        self.trees, self.size = trees, size
        self.sides = [(0, 1, 3), (3, 2, 0)] if size == 4 else []
        self.ins = [(whole, VMEM)]
        self.outs = [(jax.ShapeDtypeStruct((trees, rows, width), F32), VMEM)]
        self.scratch = [
            pltpu.VMEM((size, trees, rows, width), BF16), pltpu.VMEM((trees, rows, width), BF16),
            SEM((size, trees)), SEM((size, trees)), SEM((trees,)), SEM((trees,)),
        ]

    def bind(self, ins, outs, scratch):
        (self.terms,), (self.out,) = ins, outs
        self.boxes, self.joint, self.send, self.recv, self.join_send, self.join_recv = scratch
        self.me = lax.axis_index("dp")

    def copy(self, place, slot, tree):
        return remote(
            self.terms.at[tree, place], self.boxes.at[slot, tree], self.send.at[place, tree],
            self.recv.at[slot, tree], {"dp": place},
        )

    def by_way(self, via, target, tree):
        return remote(
            self.terms.at[tree, target], self.joint.at[tree], self.join_send.at[tree],
            self.join_recv.at[tree], {"dp": via},
        )

    def joined(self, via, target, tree):
        return remote(
            self.joint.at[tree], self.boxes.at[via, tree], self.send.at[target, tree],
            self.recv.at[via, tree], {"dp": target},
        )

    def plain(self, place):
        ok = place != self.me
        for source, via, target in self.sides:
            if place == target:
                ok = ok & (self.me != source) & (self.me != via)
        return ok

    def expected(self, place):
        ok = place != self.me
        for source, via, target in self.sides:
            if place == source:
                ok = ok & (self.me != target)
        return ok

    def start(self):
        for tree in range(self.trees):
            for source, via, target in self.sides:
                @pl.when(self.me == source)
                def _():
                    self.by_way(via, target, tree).start()

            for place in range(self.size):
                @pl.when(self.plain(place))
                def _():
                    self.copy(place, self.me, tree).start()

    def run(self):
        for tree in range(self.trees):
            for source, via, target in self.sides:
                @pl.when(self.me == via)
                def _():
                    self.by_way(via, target, tree).wait_recv()
                    both = self.joint[tree].astype(F32) + self.terms[tree, target].astype(F32)
                    self.joint[tree] = both.astype(BF16)
                    self.joined(via, target, tree).start()

        for tree in range(self.trees):
            self.out[tree] = self.terms[tree, self.me].astype(F32)
            for place in line_order(self.size):
                @pl.when(self.expected(place))
                def _():
                    self.copy(place, place, tree).wait_recv()
                    self.out[tree] += self.boxes[place, tree].astype(F32)

    def finish(self):
        for tree in range(self.trees):
            for place in range(self.size):
                @pl.when(self.plain(place))
                def _():
                    self.copy(place, self.me, tree).wait_send()

            for source, via, target in self.sides:
                @pl.when(self.me == source)
                def _():
                    self.by_way(via, target, tree).wait_send()

                @pl.when(self.me == via)
                def _():
                    self.joined(via, target, tree).wait_send()


class TotalOverAll(Part):
    axes = ("section", "tensor", "dp")

    def __init__(self, own):
        sizes = [lax.axis_size(axis) for axis in self.axes]
        self.ins = [(own, VMEM)]
        self.outs = [(jax.ShapeDtypeStruct(own.shape, F32), VMEM)]
        self.scratch = [pltpu.VMEM((size,) + own.shape, F32) for size in sizes]
        self.scratch += [SEM((size,)) for size in sizes] * 2

    def run(self):
        out = self.out_refs[0]
        out[...] = self.in_refs[0][...]
        for axis, box, send, recv in zip(self.axes, self.refs[:3], self.refs[3:6], self.refs[6:9]):
            size, me = lax.axis_size(axis), lax.axis_index(axis)
            box[me] = out[...]

            def spread(place, slot):
                return remote(box.at[me], box.at[slot], send.at[place], recv.at[slot], {axis: place})

            for place in range(size):
                @pl.when(place != me)
                def _():
                    spread(place, me).start()

            for place in range(size):
                @pl.when(place != me)
                def _():
                    spread(place, place).wait_recv()
                    spread(place, me).wait_send()

            total = box[0]
            for place in range(1, size):
                total += box[place]
            out[...] = total


def chunk_count(rows):
    return 3 if rows % 24 == 0 else 1


class Gatherer:
    def __init__(self, axis, rows, half):
        self.axis, self.half = axis, half
        self.size = size = lax.axis_size(axis)
        self.chunks = chunks = chunk_count(rows)
        self.rows = rows // chunks
        self.scratch = [pltpu.VMEM((2, chunks, size, 2 * self.rows, half), BF16)]
        self.scratch += [SEM((chunks, size))] * 4 + [SEM((chunks,))]

    def bind(self, refs):
        self.board, self.send, self.recv, self.sib_send, self.sib_recv, self.relay_send = refs
        self.core = lax.axis_index("section")
        self.sibling = 1 - self.core
        self.me = lax.axis_index(self.axis)
        self.relays = line_relays(self.size) if self.axis == "dp" else []
        self.order = line_order(self.size) if self.axis == "dp" else range(self.size)

    def direct(self, place):
        sent = place != self.me
        if self.relays:
            sent = sent & jnp.logical_not(far_pair(place, self.me))
        return sent

    def spread(self, chunk, place, slot):
        block = self.board.at[self.core, chunk, slot]
        return remote(
            block, block, self.send.at[chunk, place], self.recv.at[chunk, slot], {self.axis: place}
        )

    def passed(self, chunk, source, target):
        block = self.board.at[self.core, chunk, source]
        return remote(
            block, block, self.relay_send.at[chunk], self.recv.at[chunk, source],
            {self.axis: target},
        )

    def over(self, tree, chunk, slot):
        block = self.board.at[tree, chunk, slot]
        return remote(
            block, block, self.sib_send.at[chunk, slot], self.sib_recv.at[chunk, slot],
            {"section": self.sibling},
        )

    def begin(self, chunk, result):
        half = self.half
        piece = jnp.concatenate([result[:, :half], result[:, half:]], axis=0)
        self.board[self.core, chunk, self.me] = piece.astype(BF16)
        for place in range(self.size):
            @pl.when(self.direct(place))
            def _():
                self.spread(chunk, place, self.me).start()

        self.over(self.core, chunk, self.me).start()

    def arrive(self, chunk):
        for place in self.order:
            @pl.when(place != self.me)
            def _():
                self.spread(chunk, place, place).wait_recv()

            for via, source, target in self.relays:
                if source == place:
                    @pl.when(self.me == via)
                    def _():
                        self.passed(chunk, source, target).start()

            @pl.when(place != self.me)
            def _():
                self.over(self.core, chunk, place).start()

    def arrive_over(self, chunk):
        for place in range(self.size):
            self.over(self.sibling, chunk, place).wait_recv()

    def side_rows(self, block, side):
        return block[side * self.rows : (side + 1) * self.rows]

    def unpack(self, out, tree):
        @pl.loop(0, self.half // CHUNK)
        def _(step):
            at = pl.multiple_of(step * CHUNK, CHUNK)
            blocks = [
                self.board[tree, chunk, place, :, pl.ds(at, CHUNK)].astype(F32)
                for place in range(self.size)
                for chunk in range(self.chunks)
            ]
            for side in range(2):
                whole = [self.side_rows(block, side) for block in blocks]
                out[tree, :, pl.ds(side * self.half + at, CHUNK)] = jnp.concatenate(
                    whole, axis=0
                ).astype(BF16)

    def unpack_chunk(self, out, chunk):
        @pl.loop(0, self.half // CHUNK)
        def _(step):
            at = pl.multiple_of(step * CHUNK, CHUNK)
            blocks = [
                self.board[tree, chunk, place, :, pl.ds(at, CHUNK)].astype(F32)
                for place in range(self.size)
                for tree in range(2)
            ]
            for side in range(2):
                whole = [self.side_rows(block, side) for block in blocks]
                out[chunk, :, pl.ds(side * self.half + at, CHUNK)] = jnp.concatenate(
                    whole, axis=0
                ).astype(BF16)

    def complete(self, out):
        for chunk in range(self.chunks):
            self.arrive(chunk)
        self.unpack(out, self.core)
        for chunk in range(self.chunks):
            self.arrive_over(chunk)
        self.unpack(out, self.sibling)

    def finish(self):
        for chunk in range(self.chunks):
            for place in range(self.size):
                @pl.when(self.direct(place))
                def _():
                    self.spread(chunk, place, self.me).wait_send()

                self.over(self.core, chunk, place).wait_send()

            for via, source, target in self.relays:
                @pl.when(self.me == via)
                def _():
                    self.passed(chunk, source, target).wait_send()


class Scatterer:
    def __init__(self, axis, rows, half):
        self.axis, self.half = axis, half
        self.size = size = lax.axis_size(axis)
        self.chunks = chunks = chunk_count(rows)
        self.rows = rows // chunks
        block = (2 * self.rows, half)
        self.scratch = [pltpu.VMEM((chunks, size) + block, BF16)] * 4
        self.scratch += [pltpu.VMEM((chunks,) + block, F32), pltpu.VMEM((chunks,) + block, BF16)]
        self.scratch += [SEM((chunks, size))] * 4 + [SEM((chunks,))] * 2

    def bind(self, refs):
        self.to_sib, self.from_sib, self.to_peer, self.from_peer, self.total, self.joint = refs[:6]
        self.sib_send, self.sib_recv, self.peer_send, self.peer_recv = refs[6:10]
        self.join_send, self.join_recv = refs[10:]
        self.core = lax.axis_index("section")
        self.sibling = 1 - self.core
        self.me = lax.axis_index(self.axis)
        self.sides = [(0, 1, 3), (3, 2, 0)] if self.axis == "dp" and self.size == 4 else []
        self.order = [0, 3, 1, 2] if self.sides else range(self.size)

    def over(self, chunk, place):
        return remote(
            self.to_sib.at[chunk, place], self.from_sib.at[chunk, place],
            self.sib_send.at[chunk, place], self.sib_recv.at[chunk, place],
            {"section": self.sibling},
        )

    def spread(self, chunk, place, slot):
        return remote(
            self.to_peer.at[chunk, place], self.from_peer.at[chunk, slot],
            self.peer_send.at[chunk, place], self.peer_recv.at[chunk, slot], {self.axis: place},
        )

    def by_way(self, chunk, via, target):
        return remote(
            self.to_peer.at[chunk, target], self.joint.at[chunk], self.join_send.at[chunk],
            self.join_recv.at[chunk], {self.axis: via},
        )

    def plain(self, place):
        ok = place != self.me
        for source, via, target in self.sides:
            if place == target:
                ok = ok & (self.me != source) & (self.me != via)
        return ok

    def expected(self, place):
        ok = place != self.me
        for source, via, target in self.sides:
            if place == source:
                ok = ok & (self.me != target)
        return ok

    def over_columns(self, body):
        @pl.loop(0, self.half // CHUNK)
        def _(step):
            body(pl.multiple_of(step * CHUNK, CHUNK))

    def absorb(self, chunk, mine):
        for place in self.order:
            self.over(chunk, place).wait_recv()

            def add(at):
                both = mine(place, at)
                both += self.from_sib[chunk, place, :, pl.ds(at, CHUNK)].astype(F32)
                self.to_peer[chunk, place, :, pl.ds(at, CHUNK)] = both.astype(BF16)

                @pl.when(place == self.me)
                def _():
                    self.total[chunk, :, pl.ds(at, CHUNK)] = both

            self.over_columns(add)

            for source, via, target in self.sides:
                if place == target:
                    @pl.when(self.me == source)
                    def _():
                        self.by_way(chunk, via, target).start()

            @pl.when(self.plain(place))
            def _():
                self.spread(chunk, place, self.me).start()

        for source, via, target in self.sides:
            @pl.when(self.me == via)
            def _():
                self.by_way(chunk, via, target).wait_recv()

                def add(at):
                    at = pl.ds(at, CHUNK)
                    both = self.to_peer[chunk, target, :, at].astype(F32)
                    both += self.joint[chunk, :, at].astype(F32)
                    self.to_peer[chunk, target, :, at] = both.astype(BF16)

                self.over_columns(add)
                self.spread(chunk, target, self.me).start()

    def collect(self, chunk):
        for place in self.order:
            @pl.when(self.expected(place))
            def _():
                self.spread(chunk, place, place).wait_recv()
                self.total[chunk] += self.from_peer[chunk, place].astype(F32)

        total = self.total[chunk]
        return jnp.concatenate([total[: self.rows], total[self.rows :]], axis=1)

    def finish(self):
        for chunk in range(self.chunks):
            for place in range(self.size):
                self.over(chunk, place).wait_send()

                @pl.when(self.plain(place))
                def _():
                    self.spread(chunk, place, self.me).wait_send()

            for source, via, target in self.sides:
                @pl.when(self.me == source)
                def _():
                    self.by_way(chunk, via, target).wait_send()

                @pl.when(self.me == via)
                def _():
                    self.spread(chunk, target, self.me).wait_send()


class RowScatterer(Scatterer):
    def packed(self, tree, chunk, place, at):
        rows = self.rows
        first = rows * (place * self.chunks + chunk)
        low = first // 16 * 16
        high = -(-(first + rows) // 16) * 16
        parts = [
            self.terms[tree, low:high, pl.ds(side * self.half + at, CHUNK)].astype(F32)[
                first - low : first - low + rows
            ]
            for side in range(2)
        ]
        return jnp.concatenate(parts, axis=0)

    def prepare(self, terms):
        self.terms = terms
        for chunk in range(self.chunks):
            for place in range(self.size):
                def pack(at):
                    self.to_sib[chunk, place, :, pl.ds(at, CHUNK)] = self.packed(
                        self.sibling, chunk, place, at
                    ).astype(BF16)

                self.over_columns(pack)

    def start(self):
        for chunk in range(self.chunks):
            for place in range(self.size):
                self.over(chunk, place).start()

    def send_on(self):
        for chunk in range(self.chunks):
            self.absorb(chunk, lambda place, at: self.packed(self.core, chunk, place, at))


class Staged(Part):
    def __init__(self, ins, outs, scratch, helpers):
        self.in_names, self.out_names, self.scratch_names = list(ins), list(outs), list(scratch)
        self.ins, self.outs = list(ins.values()), list(outs.values())
        self.helpers = helpers
        self.scratch = list(scratch.values())
        for helper in helpers:
            self.scratch += helper.scratch

    def bind(self, ins, outs, scratch):
        scratch = list(scratch)
        names = self.in_names + self.out_names + self.scratch_names
        count = len(self.scratch_names)
        for name, ref in zip(names, list(ins) + list(outs) + scratch[:count]):
            setattr(self, name, ref)
        del scratch[:count]
        for helper in self.helpers:
            helper.bind(scratch[: len(helper.scratch)])
            del scratch[: len(helper.scratch)]

    def finish(self):
        for helper in self.helpers:
            helper.finish()


def vmem_f32(*shape):
    return (jax.ShapeDtypeStruct(shape, F32), VMEM)


def vmem_bf16(*shape):
    return (jax.ShapeDtypeStruct(shape, BF16), VMEM)


def rows_at(chunk, rows):
    return pl.ds(pl.multiple_of(chunk * rows, 8), rows)


class LastHub(Staged):
    def __init__(self, terms, values, gain, add):
        rows, depth = values.shape
        half = depth // 2
        self.rows_in = RowScatterer("tensor", rows, half)
        self.rows_out = Gatherer("tensor", rows, half)
        super().__init__(
            {"terms": (terms, VMEM), "values": (values, VMEM), "gain": (gain, VMEM), "add": (add, VMEM)},
            {
                "gain_grad": vmem_f32(1, depth),
                "gathered": vmem_bf16(2, self.rows_out.size * rows, depth),
            },
            {},
            [self.rows_in, self.rows_out],
        )

    def prepare(self):
        self.rows_in.prepare(self.terms)

    def start(self):
        self.rows_in.start()

    def run(self):
        self.rows_in.send_on()
        self.gain_grad[...] = jnp.zeros_like(self.gain_grad)
        for chunk in range(self.rows_in.chunks):
            at = rows_at(chunk, self.rows_in.rows)
            result, gain_grad = norm_back(
                self.rows_in.collect(chunk), self.values[at], self.gain[...]
            )
            self.gain_grad[...] += gain_grad
            self.rows_out.begin(chunk, result + self.add[at])
        self.rows_out.complete(self.gathered)


class FeedForward(Staged):
    def __init__(self, terms, own, gain, weights, forward, backward, extra):
        rows, depth = own.shape
        half = depth // 2
        units = weights[0].shape[0]
        self.has_forward, self.has_backward, self.units = forward, backward, units
        self.depth = depth
        self.size = size = lax.axis_size("dp")
        self.rows_in = RowScatterer("tensor", rows, half)
        self.spread_in = Gatherer("dp", rows, half)
        self.chunks, self.rows = self.rows_in.chunks, self.rows_in.rows
        chunks, chunk_rows = self.chunks, 2 * size * self.rows
        helpers = [self.rows_in, self.spread_in]
        tensor_rows = lax.axis_size("tensor") * rows
        matrix = pltpu.VMEM((units, depth), BF16)
        ins = {"terms": (terms, VMEM), "own": (own, VMEM), "gain": (gain, VMEM)}
        ins |= {name: (w, HBM) for name, w in zip(("gate_hbm", "up_hbm", "down_hbm"), weights)}
        ins |= {name: (value, VMEM) for name, value in extra.items()}
        outs = {}
        scratch = {"w_gate": matrix, "w_up": matrix, "w_down": matrix, "load": SEM((3,))}
        kept = pltpu.VMEM((size, 2 * self.rows, half), F32)
        if forward:
            outs |= {
                "middle": vmem_f32(rows, depth),
                "mlp_in": vmem_bf16(chunks, chunk_rows, depth),
                "hidden": vmem_bf16(chunks, chunk_rows, units),
                "own_out": vmem_f32(rows, depth),
                "out": vmem_bf16(2, tensor_rows, depth),
            }
            self.back = Scatterer("dp", rows, half)
            self.out_rows = Gatherer("tensor", rows, half)
            helpers += [self.back, self.out_rows]
            scratch["kept"] = kept
        if forward and not backward:
            outs |= {"gate": vmem_f32(chunks, chunk_rows, units), "up": vmem_f32(chunks, chunk_rows, units)}
        if forward and backward:
            outs["grad_mlp"] = vmem_bf16(chunks, chunk_rows, depth)
            self.grad_in = Gatherer("dp", rows, half)
            helpers += [self.grad_in]
            scratch |= {
                "gate": pltpu.VMEM((chunks, chunk_rows, units), F32),
                "up": pltpu.VMEM((chunks, chunk_rows, units), F32),
            }
        if backward:
            outs |= {
                "grad_gate": vmem_bf16(chunks, chunk_rows, units),
                "grad_up": vmem_bf16(chunks, chunk_rows, units),
                "grad_middle": vmem_f32(rows, depth),
                "mlp_gain_grad": vmem_f32(1, depth),
                "grad_attn": vmem_bf16(2, tensor_rows, depth),
            }
            self.grad_back = Scatterer("dp", rows, half)
            self.grad_rows = Gatherer("tensor", rows, half)
            helpers += [self.grad_back, self.grad_rows]
            scratch["grad_kept"] = kept
        if backward and not forward:
            outs |= {
                "gain_grad": vmem_f32(1, depth),
                "incoming": vmem_bf16(2, tensor_rows, depth),
                "grad_mlp": vmem_bf16(chunks, chunk_rows, depth),
            }
            scratch["grad_own"] = pltpu.VMEM((rows, depth), F32)
            self.incoming_rows = Gatherer("tensor", rows, half)
            helpers += [self.incoming_rows]
        super().__init__(ins, outs, scratch, helpers)

    def loads(self):
        pairs = [(self.gate_hbm, self.w_gate), (self.up_hbm, self.w_up), (self.down_hbm, self.w_down)]
        return [
            pltpu.make_async_copy(src, dst, self.load.at[i]) for i, (src, dst) in enumerate(pairs)
        ]

    def prepare(self):
        for copy in self.loads():
            copy.start()
        self.rows_in.prepare(self.terms)

    def start(self):
        self.rows_in.start()
        if self.has_forward and self.has_backward:
            for chunk in range(self.chunks):
                self.grad_in.begin(chunk, self.grad_own[rows_at(chunk, self.rows)])

    def run(self):
        self.rows_in.send_on()
        if self.has_backward:
            self.mlp_gain_grad[...] = jnp.zeros_like(self.mlp_gain_grad)
        if not self.has_forward:
            self.gain_grad[...] = jnp.zeros_like(self.gain_grad)
        for chunk in range(self.chunks):
            at = rows_at(chunk, self.rows)
            total = self.rows_in.collect(chunk)
            if self.has_forward:
                middle = self.own[at] + total
                self.middle[at] = middle
                mean_sq = jnp.mean(middle * middle, axis=1, keepdims=True)
                normed = middle * lax.rsqrt(mean_sq + EPSILON) * self.gain[...]
                self.spread_in.begin(chunk, normed)
            else:
                result, gain_grad = norm_back(total, self.own[at], self.gain[...])
                self.gain_grad[...] += gain_grad
                result = (result + self.add[at]).astype(BF16).astype(F32)
                self.grad_own[at] = result
                self.spread_in.begin(chunk, result)
                self.incoming_rows.begin(chunk, result)
        for copy in self.loads():
            copy.wait()

        self.spread_in.arrive(0)
        if self.has_forward and self.has_backward:
            self.grad_in.arrive(0)

        @pl.loop(0, self.chunks)
        def _(chunk):
            self.spread_in.arrive_over(chunk)
            if self.has_forward:
                self.spread_in.unpack_chunk(self.mlp_in, chunk)
                self.forward_chunk(chunk)
            else:
                self.spread_in.unpack_chunk(self.grad_mlp, chunk)
            if self.has_forward and self.has_backward:
                self.grad_in.arrive_over(chunk)
                self.grad_in.unpack_chunk(self.grad_mlp, chunk)
            if self.has_backward:
                self.backward_chunk(chunk)

            @pl.when(chunk + 1 < self.chunks)
            def _():
                self.spread_in.arrive(chunk + 1)
                if self.has_forward and self.has_backward:
                    self.grad_in.arrive(chunk + 1)

            if self.has_forward:
                self.back.absorb(chunk, lambda place, at: self.kept[place, :, pl.ds(at, CHUNK)])
            if self.has_backward:
                self.grad_back.absorb(
                    chunk, lambda place, at: self.grad_kept[place, :, pl.ds(at, CHUNK)]
                )

            @pl.when(chunk > 0)
            def _():
                self.hand_back(chunk - 1)

        self.hand_back(self.chunks - 1)
        if self.has_backward:
            self.grad_rows.complete(self.grad_attn)
        if self.has_forward:
            self.out_rows.complete(self.out)
        else:
            self.incoming_rows.complete(self.incoming)

    def hand_back(self, chunk):
        at = rows_at(chunk, self.rows)
        if self.has_backward:
            values = self.middle if self.has_forward else self.middle_in
            gain = self.gain if self.has_forward else self.mlp_gain
            result, gain_grad = norm_back(self.grad_back.collect(chunk), values[at], gain[...])
            self.mlp_gain_grad[...] += gain_grad
            result += self.grad_own[at]
            self.grad_middle[at] = result
            self.grad_rows.begin(chunk, result)
        if self.has_forward:
            output = (self.middle[at] + self.back.collect(chunk)).astype(BF16).astype(F32)
            self.own_out[at] = output
            self.out_rows.begin(chunk, output)

    def unit_tiles(self, body):
        tile = 256

        @pl.loop(0, self.units // tile)
        def _(step):
            body(pl.ds(pl.multiple_of(step * tile, tile), tile))

    def forward_chunk(self, chunk):
        def tile(at):
            rows = self.mlp_in[chunk]
            gate = dot_inner(rows, self.w_gate[at, :])
            up = dot_inner(rows, self.w_up[at, :])
            self.gate[chunk, :, at] = gate
            self.up[chunk, :, at] = up
            self.hidden[chunk, :, at] = (gate * jax.nn.sigmoid(gate) * up).astype(BF16)

        self.unit_tiles(tile)
        self.terms_out(
            chunk, self.back, self.kept, lambda at: dot(self.hidden[chunk], self.w_down[:, at])
        )

    def backward_chunk(self, chunk):
        def tile(at):
            grad_hidden = dot_inner(self.grad_mlp[chunk], self.w_down[at, :])
            gate, up = self.gate[chunk, :, at], self.up[chunk, :, at]
            share = jax.nn.sigmoid(gate)
            act = gate * share
            self.grad_up[chunk, :, at] = (grad_hidden * act).astype(BF16)
            self.grad_gate[chunk, :, at] = (
                grad_hidden * up * (share + act * (1.0 - share))
            ).astype(BF16)

        self.unit_tiles(tile)
        self.terms_out(
            chunk, self.grad_back, self.grad_kept,
            lambda at: dot(self.grad_gate[chunk], self.w_gate[:, at])
            + dot(self.grad_up[chunk], self.w_up[:, at]),
        )

    def terms_out(self, chunk, scatterer, kept, product):
        rows, half = self.rows, self.depth // 2
        first = lax.axis_index("section") == 0

        @pl.loop(0, half // CHUNK)
        def _(step):
            low = pl.multiple_of(step * CHUNK, CHUNK)
            at = pl.ds(low, CHUNK)
            sides = [product(pl.ds(side * half + low, CHUNK)) for side in range(2)]
            for place in range(self.size):
                trees = []
                for tree in range(2):
                    start = (2 * place + tree) * rows
                    trees.append(
                        jnp.concatenate([side[start : start + rows] for side in sides], axis=0)
                    )
                kept[place, :, at] = jnp.where(first, trees[0], trees[1])
                scatterer.to_sib[chunk, place, :, at] = jnp.where(
                    first, trees[1], trees[0]
                ).astype(BF16)

        for place in range(self.size):
            scatterer.over(chunk, place).start()


def hub_plain(terms, own_args, body, own_outs, scatter, gathers):
    total = None
    if scatter:
        mine = lax.psum_scatter(terms, "section", scatter_dimension=0, tiled=True)
        mine = lax.psum_scatter(mine, scatter, scatter_dimension=1, tiled=True)[0]
        total = mine.astype(F32)

    class Cell:
        def __setitem__(self, _, value):
            self.value = value

    cells = [Cell() for _ in own_outs]
    result = body(total, own_args, cells).astype(BF16)
    gathered = [
        lax.all_gather(lax.all_gather(result, axis, axis=0, tiled=True), "section", axis=0)
        for axis in gathers
    ]
    return [cell.value for cell in cells] + gathered


def with_cargo(part, cargo, axes, collective_id, cost_us, vmem=40):
    outs = fused(cargo + [part], axes, bool(cargo), collective_id, cost_us, vmem)
    return outs[-1], outs[:-1]


def norm_back(total, values, gain):
    scale = lax.rsqrt(jnp.mean(values * values, axis=1, keepdims=True) + EPSILON)
    unit = values * scale
    gain_grad = jnp.sum(total * unit, axis=0, keepdims=True)
    scaled = total * gain
    along = jnp.mean(scaled * unit, axis=1, keepdims=True)
    return ((scaled - unit * along) * scale, gain_grad)


def norm_body(total, args, outs):
    middle = args[0] + total
    outs[0][...] = middle
    return rms_scale(middle, args[1])


def add_body(total, args, outs):
    result = args[0] + total
    outs[0][...] = result
    return result


def norm_back_body(total, args, outs):
    result, outs[1][...] = norm_back(total, args[0], args[1])
    result += args[2]
    outs[0][...] = result
    return result


def embed(q_pre, k_pre, q_scale, k_scale, cos_table, sine_table):
    queries = rms_scale(q_pre, q_scale)
    keys = rms_scale(k_pre, k_scale)
    return (
        rotate(queries, cos_table[:, :, None], sine_table[:, :, None]),
        rotate(keys, cos_table, sine_table),
    )


def attn_forward(hidden_in, weights, gains, slot, gather):
    attn_scale, _, q_scale, k_scale = gains
    w_qkv, w_out = weights[:2]
    allowed, cos_table, sine_table = slot
    trees, row_count, depth = hidden_in.shape
    q_width = w_out.shape[0]
    normed = rms_scale(hidden_in.astype(F32), attn_scale).astype(BF16).reshape(-1, depth)
    qkv = dot(normed, w_qkv).reshape(trees, row_count, -1)
    q_pre = qkv[:, :, :q_width].reshape(trees, row_count, -1, HD)
    k_pre = qkv[:, :, q_width : q_width + HD]
    value_bf = qkv[:, :, q_width + HD :].astype(BF16)
    queries, keys_rot = embed(q_pre, k_pre, q_scale, k_scale, cos_table, sine_table)
    query_bf = queries.astype(BF16)
    kv_all = gather(jnp.concatenate([keys_rot.astype(BF16), value_bf], axis=2))
    key_all = kv_all[:, :, :HD]
    value_all = kv_all[:, :, HD:]
    scores = masked_scores(query_bf, key_all, allowed)
    row_max = jnp.max(scores, axis=-1, keepdims=True)
    exp_scores = jnp.exp(scores - row_max)
    row_total = jnp.sum(exp_scores, axis=-1, keepdims=True)
    prob_bf = (exp_scores / row_total).astype(BF16)
    log_total = row_max + jnp.log(row_total)
    attended = jnp.einsum("bgrt,btd->brgd", prob_bf, value_all, preferred_element_type=F32)
    attended_bf = attended.reshape(trees * row_count, -1).astype(BF16)
    terms = dot(attended_bf, w_out).astype(BF16).reshape(trees, row_count, depth)
    saved = (normed, q_pre, k_pre, query_bf, key_all, value_all, log_total, attended_bf)
    return (terms, saved)


def attn_backward(grad_attn, saved, weights, gains, slot, scatter):
    _, _, q_scale, k_scale = gains
    w_qkv, w_out = weights[:2]
    allowed, cos_table, sine_table = slot
    normed, q_pre, k_pre, query_bf, key_all, value_all, log_total, attended_bf = saved
    trees, row_count = query_bf.shape[:2]
    depth = normed.shape[1]
    grad_attn = grad_attn.reshape(-1, depth)
    grad_heads = dot_inner(grad_attn, w_out).astype(BF16).reshape(query_bf.shape)
    scores = masked_scores(query_bf, key_all, allowed)
    prob_full = jnp.exp(scores - log_total)
    grad_prob = jnp.einsum("brgd,btd->bgrt", grad_heads, value_all, preferred_element_type=F32)
    row_dot = jnp.sum(prob_full * grad_prob, axis=-1, keepdims=True)
    grad_scores = (prob_full * (grad_prob - row_dot)).astype(BF16)
    scale_factor = HD ** (-0.5)
    grad_query = (
        jnp.einsum("bgrt,btd->brgd", grad_scores, key_all, preferred_element_type=F32)
        * scale_factor
    )
    grad_key_all = (
        jnp.einsum("bgrt,brgd->btd", grad_scores, query_bf, preferred_element_type=F32)
        * scale_factor
    )
    grad_value_all = jnp.einsum(
        "bgrt,brgd->btd", prob_full.astype(BF16), grad_heads, preferred_element_type=F32
    )
    grad_kv = scatter(jnp.concatenate([grad_key_all, grad_value_all], axis=2).astype(BF16))
    _, embedding_pull = jax.vjp(
        partial(embed, cos_table=cos_table, sine_table=sine_table), q_pre, k_pre, q_scale, k_scale
    )
    grad_q_pre, grad_k_pre, grad_q_scale, grad_k_scale = embedding_pull(
        (grad_query, grad_kv[:, :, :HD].astype(F32))
    )
    qkv_grad = jnp.concatenate(
        [
            grad_q_pre.astype(BF16).reshape(trees, row_count, -1),
            grad_k_pre.astype(BF16),
            grad_kv[:, :, HD:].astype(BF16),
        ],
        axis=2,
    ).reshape(trees * row_count, -1)
    terms = dot_inner(qkv_grad, w_qkv).astype(BF16).reshape(trees, row_count, depth)
    return (terms, [(normed, qkv_grad), (grad_attn, attended_bf)], [grad_q_scale, grad_k_scale])


def plain_layers(hidden, own_in, grad_own, weights, gains, slot, shared_kv):
    depth = own_in.shape[1]
    own_shape = own_in.shape

    def gather(own):
        return lax.all_gather(own, "dp", axis=1, tiled=True)

    def scatter(whole):
        total = lax.psum_scatter(whole, "dp", scatter_dimension=1, tiled=True)
        if shared_kv:
            total = lax.psum(total, "section")
            total = jnp.where(lax.axis_index("section") == 0, total, jnp.zeros_like(total))
        return total

    outputs, kept = [], []
    for layer in range(2):
        _, _, w_gate, w_up, w_down = weights[layer]
        terms, saved = attn_forward(hidden, weights[layer], gains[layer], slot, gather)
        mlp_scale = gains[layer][1][None]
        middle, mlp_in = hub_plain(
            terms, [own_in, mlp_scale], norm_body, [own_shape], "tensor", ["dp"]
        )
        mlp_in = mlp_in.reshape(-1, depth)
        gate, up = dot_inner(mlp_in, w_gate), dot_inner(mlp_in, w_up)
        hidden_bf = swiglu(gate, up).astype(BF16)
        terms = dot(hidden_bf, w_down).astype(BF16).reshape(2, -1, depth)
        kept.append((own_in, saved, middle, mlp_in, gate, up, hidden_bf))
        own_in, hidden = hub_plain(terms, [middle], add_body, [own_shape], "dp", ["tensor"])
        own_in = own_in.astype(BF16).astype(F32)
        outputs.append(hidden)

    own_outs = [own_shape, (1, depth)]
    grads, products, gain_grads = [None, None], [None, None], [None, None]
    (grad_mlp,) = hub_plain(None, [grad_own], lambda total, args, outs: args[0], [], None, ["dp"])
    for layer in (1, 0):
        _, _, w_gate, w_up, w_down = weights[layer]
        own_in, saved, middle, mlp_in, gate, up, hidden_bf = kept[layer]
        grad_mlp = grad_mlp.reshape(-1, depth)
        _, pull = jax.vjp(swiglu, gate, up)
        grad_gate, grad_up = (item.astype(BF16) for item in pull(dot_inner(grad_mlp, w_down)))
        terms = (dot(grad_gate, w_gate) + dot(grad_up, w_up)).astype(BF16).reshape(2, -1, depth)
        grad_middle, mlp_gain_grad, grad_attn = hub_plain(
            terms, [middle, gains[layer][1][None], grad_own], norm_back_body, own_outs, "dp",
            ["tensor"],
        )
        terms, pairs, head_grads = attn_backward(
            grad_attn, saved, weights[layer], gains[layer], slot, scatter
        )
        grad_own, gain_grad, grads[layer], grad_next = hub_plain(
            terms, [own_in, gains[layer][0][None], grad_middle], norm_back_body, own_outs, "tensor",
            ["tensor", "dp"],
        )
        grad_own = grad_own.astype(BF16).astype(F32)
        pairs += [(grad_gate, mlp_in), (grad_up, mlp_in), (hidden_bf, grad_mlp)]
        products[layer] = pairs
        gain_grads[layer] = jnp.concatenate([gain_grad[0], mlp_gain_grad[0], *head_grads])
        grad_mlp = grad_next
    return (outputs, grads, products, gain_grads)


def swap_cores(mine, other):
    core = lax.axis_index("section")
    arrived = lax.ppermute(other, "section", [(0, 1), (1, 0)])
    return (jnp.where(core == 0, mine, arrived), jnp.where(core == 0, arrived, mine))


def on_device(
    inputs, cotangent, seg_ids, parents, order, attn_gain, w_query, w_key, w_value, w_out,
    q_gain, k_gain, mlp_gain, w_gate, w_up, w_down,
):
    core = lax.axis_index("section")
    data_index = lax.axis_index("dp")
    tensor_index = lax.axis_index("tensor")
    dp_size = lax.axis_size("dp")
    tensor_size = lax.axis_size("tensor")
    trees, row_count, depth = inputs.shape
    own_rows = row_count // tensor_size
    row_start = data_index * row_count
    own_depth = w_query.shape[1]
    q_width = w_query.shape[2] // 2
    shared_kv = w_key.shape[2] == HD
    k_width = HD if shared_kv else w_key.shape[2] // 2
    own_units = w_gate.shape[2]
    share = own_units // (2 * dp_size)

    def pick(stacked, index):
        return lax.dynamic_index_in_dim(stacked, index, 0, keepdims=False)

    fast = (
        own_rows % 8 == 0
        and depth % (2 * CHUNK) == 0
        and row_count % 16 == 0
        and share % 16 == 0
        and own_depth % 128 == 0
        and not shared_kv
    )

    def halves(width, array):
        return [array[:, :width], array[:, array.shape[1] - width :]]

    unit_mats = [w_gate[0].T, w_up[0].T, w_down[0]]
    qkv_width = q_width + 2 * k_width
    gains_own = jnp.concatenate([attn_gain[0], mlp_gain[0], q_gain[0], k_gain[0]]).astype(F32)

    def spread_units(rows):
        return lax.all_gather(rows, "tensor", axis=0, tiled=True)

    def tied(value, *before):
        return lax.optimization_barrier((value, *before))[0]

    if fast:
        line = ["section", "dp"]
        everyone = ["section", "dp", "tensor"]
        (gate_rows, up_rows), (gains_all,) = fused(
            [UnitsOut(unit_mats[:2], 0), SharedRows(gains_own.reshape(-1, 128))], line, True, 1, 45
        )
        shards = AttnShards(w_query[0], w_key[0], w_value[0], w_out[0])
        shards.arrays[0] = tied(shards.arrays[0], gate_rows)
        (w_qkv, w_heads), (down_rows,), (attn_shard,) = fused(
            [AttnOut(shards, 0), UnitsOut(unit_mats[2:], 0), HalfOver(shards)], line, True, 2, 80
        )
        first_weights = [w_qkv, w_heads, spread_units(gate_rows), spread_units(up_rows)]
        attn_next = lax.all_gather(attn_shard, "dp", axis=0)
    else:
        gains_all = lax.all_gather(gains_own, ("section", "dp"))
        attn_halves = jnp.stack(
            [
                jnp.concatenate(parts, axis=1)
                for parts in zip(
                    halves(q_width, w_query[0]),
                    halves(k_width, w_key[0]),
                    halves(k_width, w_value[0]),
                    halves(q_width, w_out[0].T),
                )
            ]
        )
        attn_shards = swap_cores(pick(attn_halves, core), pick(attn_halves, 1 - core))
        unit_blocks = jnp.stack(unit_mats).reshape(3, 2, dp_size, share, own_depth)
        unit_blocks = unit_blocks.transpose(1, 2, 0, 3, 4)
        unit_shards = swap_cores(pick(unit_blocks, core), pick(unit_blocks, 1 - core))
        both_weights = []
        for layer in range(2):
            attn_all = lax.all_gather(attn_shards[layer], "dp", axis=0, tiled=True)
            pieces = exchange(unit_shards[layer], "dp")
            pieces = pieces.transpose(1, 2, 0, 3).reshape(3, share, depth)
            both_weights.append(
                (
                    attn_all[:, :qkv_width], attn_all[:, qkv_width:].T,
                    *(spread_units(pieces[i]) for i in range(3)),
                )
            )

    gains_all = gains_all.reshape(2, dp_size, -1)
    gains = [
        (
            gains_all[layer, :, :own_depth].reshape(depth),
            gains_all[layer, :, own_depth : 2 * own_depth].reshape(depth),
            gains_all[layer, 0, 2 * own_depth : 2 * own_depth + HD],
            gains_all[layer, 0, 2 * own_depth + HD :],
        )
        for layer in range(2)
    ]

    def slot_setup(slot_index):
        tree_id = pick(order, slot_index)
        allowed, row_positions = path_mask(
            pick(seg_ids, tree_id), pick(parents, tree_id), row_start, row_count
        )
        cos_table, sine_table = rope_tables(row_positions, HD)
        return (pick(inputs, tree_id), allowed, cos_table[:, 0], sine_table[:, 0])

    setups = [slot_setup(i) for i in range(trees)]
    hidden, *slot = (jnp.stack(item) for item in zip(*setups))

    def own_part(whole):
        return lax.dynamic_slice_in_dim(
            pick(whole, core), tensor_index * own_rows, own_rows, 0
        )

    own_in = own_part(hidden).astype(F32)
    grad_own = own_part(cotangent).astype(F32)

    def weight_products(pairs):
        return [dot_outer(left, right).astype(BF16) for left, right in pairs]

    def scatter_units(products):
        return [
            lax.psum_scatter(item, "tensor", scatter_dimension=0, tiled=True) for item in products
        ]

    def scatter_shards(products):
        return lax.psum_scatter(
            jnp.concatenate(products, axis=1), "dp", scatter_dimension=0, tiled=True
        )

    if fast:
        def units_on(*which):
            return [UnitsOut([unit_mats[i] for i in which], 1)]

        def kv_gather(own, cargo, collective_id, carried):
            (whole,), outs = with_cargo(GatherKV(own), cargo, everyone, collective_id, 40)
            carried += outs
            return whole.reshape(trees, -1, 2 * HD)

        def kv_scatter(whole, cargo, collective_id, carried):
            part = ScatterKV(whole.reshape(trees, dp_size, row_count, 2 * HD))
            (total,), outs = with_cargo(part, cargo, line, collective_id, 30)
            carried += outs
            return total

        def flat(array):
            return array.reshape(-1, array.shape[-1])

        carried = []
        terms, saved_first = attn_forward(
            hidden, first_weights, gains[0], slot,
            lambda own: kv_gather(
                tied(own, *first_weights[2:]), [UnitsSpread(down_rows)] + units_on(0), 3, carried
            ),
        )
        (down_all,), (gate_rows,) = carried
        first_weights.append(down_all)
        part = FeedForward(
            terms, own_in, gains[0][1][None], first_weights[2:], True, False, {}
        )
        outs, ((up_rows, down_rows),) = with_cargo(part, units_on(1, 2), everyone, 4, 90, 56)
        middle_first, mlp_in_first, hidden_first, own_next, output_first, gate_first, up_first = outs
        second_weights = [
            attn_next[:, :own_depth].reshape(depth, -1),
            attn_next[:, own_depth:].transpose(1, 0, 2).reshape(q_width, depth),
            spread_units(gate_rows), spread_units(up_rows),
        ]
        carried = []
        terms, saved_second = attn_forward(
            output_first, second_weights, gains[1], slot,
            lambda own: kv_gather(
                tied(own, second_weights[2]), [UnitsSpread(down_rows)], 5, carried
            ),
        )
        ((down_all,),) = carried
        second_weights.append(down_all)
        part = FeedForward(
            terms, own_next, gains[1][1][None], second_weights[2:], True, True,
            {"grad_own": grad_own},
        )
        outs, _ = with_cargo(part, [], everyone, 6, 100, 60)
        (
            middle, mlp_in, hidden_bf, _, output_second, grad_mlp,
            grad_gate, grad_up, grad_middle, mlp_gain_second, grad_attn,
        ) = outs
        unit_second = scatter_units(
            weight_products(
                [
                    (flat(grad_gate), flat(mlp_in)),
                    (flat(grad_up), flat(mlp_in)),
                    (flat(hidden_bf), flat(grad_mlp)),
                ]
            )
        )
        terms, pairs, head_second = attn_backward(
            grad_attn, saved_second, second_weights, gains[1], slot,
            lambda whole: kv_scatter(whole, [], 7, []),
        )
        attn_second = scatter_shards(weight_products(pairs))
        part = FeedForward(
            terms, own_next, gains[1][0][None], first_weights[2:], False, True,
            {
                "add": grad_middle, "gate": gate_first, "up": up_first,
                "middle_in": middle_first, "mlp_gain": gains[0][1][None],
            },
        )
        outs, _ = with_cargo(part, [], everyone, 8, 90, 60)
        (
            grad_gate, grad_up, grad_middle, mlp_gain_first, grad_attn,
            attn_gain_second, incoming_second, grad_mlp,
        ) = outs
        products = weight_products(
            [
                (flat(grad_gate), flat(mlp_in_first)),
                (flat(grad_up), flat(mlp_in_first)),
                (flat(hidden_first), flat(grad_mlp)),
            ]
        )
        unit_first = scatter_units(products[:2])
        unit_first += scatter_units([tied(products[2], *unit_first)])
        carried = []
        terms, pairs, head_first = attn_backward(
            grad_attn, saved_first, first_weights, gains[0], slot,
            lambda whole: kv_scatter(whole, [UnitsHome(unit_second, 1)], 9, carried),
        )
        (home_second,) = carried
        whole = jnp.concatenate(weight_products(pairs), axis=1).reshape(dp_size, 4, -1, q_width + qkv_width)
        part = LastHub(terms, own_in, gains[0][0][None], grad_middle)
        (attn_gain_first, incoming_first), ((attn_first,), home_first) = with_cargo(
            part, [ScatterKV(whole.transpose(1, 0, 2, 3)), UnitsHome(unit_first[:2], 0)], everyone,
            10, 60, 56,
        )
        attn_first = attn_first.reshape(own_depth, -1).astype(BF16)
        outputs = [output_first, output_second]
        grads = [incoming_first, incoming_second]
        weight_grads = [(attn_first, None), (attn_second, None)]
        gain_grads = [
            jnp.concatenate([attn_gain_first[0], mlp_gain_first[0], *head_first]),
            jnp.concatenate([attn_gain_second[0], mlp_gain_second[0], *head_second]),
        ]
    else:
        outputs, grads, products, gain_grads = plain_layers(
            hidden, own_in, grad_own, both_weights, gains, slot, shared_kv
        )
        weight_grads = []
        for pairs in products:
            whole = weight_products(pairs)
            weight_grads.append((scatter_shards(whole[:2]), scatter_units(whole[2:])))

    gain_total = jnp.stack(gain_grads)
    if fast:
        mine = jnp.where(core == 0, weight_grads[0][0], weight_grads[1][0])
        other = jnp.where(core == 0, weight_grads[1][0], weight_grads[0][0])
        (gain_total,), (arrived,), down_home = fused(
            [TotalOverAll(gain_total.reshape(-1, 128)), Swap(other), UnitsHome(unit_first[2:], 0)],
            everyone, True, 11, 60,
        )
        attn_home = (jnp.where(core == 0, mine, arrived), jnp.where(core == 0, arrived, mine))
        unit_home = [
            jnp.where(core == 0, first, second) for first, second in zip(home_first + down_home, home_second)
        ]
        gain_total = gain_total.reshape(2, -1)
    else:
        def bring_home(first, second):
            mine, other = jnp.where(core == 0, first, second), jnp.where(core == 0, second, first)
            arrived = lax.ppermute(other, "section", [(0, 1), (1, 0)])
            return (jnp.where(core == 0, mine, arrived), jnp.where(core == 0, arrived, mine))

        def pieces_of(grad):
            return exchange(
                jnp.stack(grad).reshape(3, share, dp_size, own_depth).transpose(2, 0, 1, 3), "dp"
            )

        attn_home = bring_home(weight_grads[0][0], weight_grads[1][0])
        unit_home = jnp.stack(bring_home(pieces_of(weight_grads[0][1]), pieces_of(weight_grads[1][1])))
        unit_home = unit_home.transpose(2, 0, 1, 3, 4).reshape(3, own_units, own_depth)
        gain_total = lax.psum(gain_total, ("section", "dp", "tensor"))

    def joined(start, width):
        parts = [half[:, start : start + width] for half in attn_home]
        if shared_kv and start in (q_width, q_width + k_width):
            return parts[0].astype(F32)
        return jnp.concatenate(parts, axis=1).astype(F32)

    gain_own = pick(gain_total, core)
    share_width = attn_gain.shape[1]
    attn_gain_grad = lax.dynamic_slice_in_dim(gain_own, data_index * share_width, share_width, 0)
    mlp_gain_grad = lax.dynamic_slice_in_dim(
        gain_own, depth + data_index * share_width, share_width, 0
    )
    return (
        jnp.where(core == 0, outputs[0], outputs[1])[None],
        jnp.where(core == 0, grads[0], grads[1])[None],
        attn_gain_grad[None],
        joined(0, q_width)[None],
        joined(q_width, k_width)[None],
        joined(q_width + k_width, k_width)[None],
        joined(qkv_width, q_width).T[None],
        gain_own[2 * depth : 2 * depth + HD][None],
        gain_own[2 * depth + HD :][None],
        mlp_gain_grad[None],
        unit_home[0].T.astype(F32)[None],
        unit_home[1].T.astype(F32)[None],
        unit_home[2].astype(F32)[None],
    )


def solution(mesh):
    rows = P(None, "dp", None)
    wide = P("section", "dp", "tensor")
    tall = P("section", "tensor", "dp")
    gain = P("section", "dp")
    head_gain = P("section", None)
    slots = P("section", None, "dp", None)
    in_specs = (
        rows, rows, P(), P(), P(), gain, wide, wide, wide, tall, head_gain, head_gain, gain,
        wide, wide, tall,
    )
    out_specs = (
        slots, slots, gain, wide, wide, wide, tall, head_gain, head_gain, gain, wide, wide, tall,
    )
    return jax.shard_map(
        on_device, mesh=mesh, in_specs=in_specs, out_specs=out_specs, check_vma=False
    )
```

```python
from functools import partial

import jax
import jax.numpy as jnp
from jax import lax
from jax.experimental import pallas as pl
from jax.experimental.pallas import tpu as pltpu
from jax.sharding import PartitionSpec as P

HD = 128
TRUNK = 512
BRANCH = 96
NB = 4
TREE = 1152
SEGS = 9


EPSILON = 1e-06
THETA = 1000000.0
MASKED = -1e30
F32 = jnp.float32
BF16 = jnp.bfloat16


def rms_scale(values, weight_gain):
    mean_sq = jnp.mean(values * values, axis=-1, keepdims=True)
    return values * lax.rsqrt(mean_sq + EPSILON) * weight_gain


def rotate(values, cos_table, sine_table):
    middle_at = values.shape[-1] // 2
    leading = values[..., :middle_at]
    trailing = values[..., middle_at:]
    return jnp.concatenate(
        [leading * cos_table - trailing * sine_table, trailing * cos_table + leading * sine_table],
        axis=-1,
    )


def rope_tables(positions, head_dim):
    half_steps = jnp.arange(head_dim // 2, dtype=F32)
    inverse = THETA ** (-2.0 * half_steps / head_dim)
    angles = positions.astype(F32)[:, None] * inverse[None, :]
    return (jnp.cos(angles)[:, None, :], jnp.sin(angles)[:, None, :])


def swiglu(gate_in, up_in):
    return jax.nn.silu(gate_in) * up_in


def embed_heads(q_pre, k_pre, q_scale, k_scale, cos_table, sine_table):
    row_count = q_pre.shape[0]
    queries = rms_scale(q_pre.reshape(row_count, -1, HD), q_scale)
    keys_part = rms_scale(k_pre.reshape(row_count, -1, HD), k_scale)
    return (rotate(queries, cos_table, sine_table), rotate(keys_part, cos_table, sine_table))


def tree_layout(seg_row, parent_row):
    labels = jnp.arange(SEGS, dtype=jnp.int32)
    places = jnp.arange(TREE, dtype=jnp.int32)
    member = seg_row[None, :] == labels[:, None]
    starts = jnp.min(jnp.where(member, places[None, :], TREE), axis=1)
    depth_base = jnp.where(labels == 0, 0, jnp.where(labels <= NB, TRUNK, TRUNK + BRANCH))
    shifts = depth_base - starts
    positions = places + jnp.sum(jnp.where(member, shifts[:, None], 0), axis=0)
    grandparent = jnp.sum(
        jnp.where(parent_row[:, None] == labels[None, :], parent_row[None, :], 0), axis=1
    )
    ancestor = (
        (labels[None, :] == labels[:, None])
        | (labels[None, :] == parent_row[:, None])
        | (labels[None, :] == grandparent[:, None])
    )
    return (positions, member.astype(F32), ancestor.astype(F32))


def path_mask(seg_row, parent_row, row_start, row_count):
    positions, member, ancestor = tree_layout(seg_row, parent_row)
    member_rows = lax.dynamic_slice_in_dim(member, row_start, row_count, 1)
    seg_rows = lax.dynamic_slice_in_dim(seg_row, row_start, row_count, 0)
    reach_table = jnp.dot(jnp.dot(member_rows.T, ancestor), member)
    places = jnp.arange(TREE, dtype=jnp.int32)
    row_places = row_start + jnp.arange(row_count, dtype=jnp.int32)
    same_seg = seg_rows[:, None] == seg_row[None, :]
    causal = places[None, :] <= row_places[:, None]
    allowed = (reach_table > 0.5) & (jnp.logical_not(same_seg) | causal)
    row_positions = lax.dynamic_slice_in_dim(positions, row_start, row_count, 0)
    return (allowed, row_positions)


OUTER = (((0,), (0,)), ((), ()))
INNER = (((1,), (1,)), ((), ()))


def dot(left, right):
    return jnp.dot(left, right, preferred_element_type=F32)


def dot_inner(left, right):
    return lax.dot_general(left, right, INNER, preferred_element_type=F32)


def dot_outer(left, right):
    return lax.dot_general(left, right, OUTER, preferred_element_type=F32)


def exchange(pieces, axis):
    size = lax.axis_size(axis)
    me = lax.axis_index(axis)
    got = jnp.zeros_like(pieces)
    own = lax.dynamic_index_in_dim(pieces, me, 0, keepdims=True)
    got = lax.dynamic_update_slice_in_dim(got, own, me, 0)
    for step in range(1, size):
        other = me ^ step
        piece = lax.dynamic_index_in_dim(pieces, other, 0, keepdims=True)
        arrived = lax.ppermute(piece, axis, [(i, i ^ step) for i in range(size)])
        got = lax.dynamic_update_slice_in_dim(got, arrived, other, 0)
    return got


def masked_scores(query_bf, key_all, allowed):
    raw_scores = jnp.einsum(
        "brgd,btd->bgrt", query_bf, key_all, preferred_element_type=F32
    ) * HD ** (-0.5)
    return jnp.where(allowed[:, None], raw_scores, MASKED)


MESH = pl.DeviceIdType.MESH
CHUNK = 256
SEM = pltpu.SemaphoreType.DMA
VMEM = pl.BlockSpec(memory_space=pltpu.VMEM)
HBM = pl.BlockSpec(memory_space=pl.ANY)


def remote(src, dst, send_sem, recv_sem, device_id):
    return pltpu.make_async_remote_copy(
        src_ref=src, dst_ref=dst, send_sem=send_sem, recv_sem=recv_sem,
        device_id=device_id, device_id_type=MESH,
    )


def greet(axes, across):
    barrier = pltpu.get_barrier_semaphore()
    count = 0
    for axis in axes:
        size = lax.axis_size(axis)
        me = lax.axis_index(axis)
        for step in range(1, size):
            pl.semaphore_signal(
                barrier, inc=1, device_id={axis: lax.rem(me + step, size)}, device_id_type=MESH
            )
        count += size - 1
    if across:
        size = lax.axis_size("dp")
        me = lax.axis_index("dp")
        sibling = 1 - lax.axis_index("section")
        for step in range(1, size):
            pl.semaphore_signal(
                barrier, inc=1, device_id={"section": sibling, "dp": lax.rem(me + step, size)},
                device_id_type=MESH,
            )
        count += size - 1
    pl.semaphore_wait(barrier, count)


class Part:
    ins, outs, scratch = (), (), ()

    def bind(self, ins, outs, scratch):
        self.in_refs, self.out_refs, self.refs = ins, outs, scratch

    def prepare(self):
        pass

    def start(self):
        pass

    def run(self):
        pass

    def finish(self):
        pass


def fused(parts, axes, across, collective_id, cost_us, vmem=40):
    counts = [(len(part.ins), len(part.outs), len(part.scratch)) for part in parts]

    def kernel(*refs):
        refs = list(refs)
        groups = []
        for kind in range(3):
            groups.append([])
            for count in counts:
                groups[kind].append(refs[: count[kind]])
                del refs[: count[kind]]
        for part, ins, outs, scratch in zip(parts, *groups):
            part.bind(ins, outs, scratch)
        for part in parts:
            part.prepare()
        greet(axes, across)
        for part in parts:
            part.start()
        for part in reversed(parts):
            part.run()
        for part in parts:
            part.finish()

    ins = [item for part in parts for item in part.ins]
    outs = [item for part in parts for item in part.outs]
    results = pl.pallas_call(
        kernel,
        out_shape=[item[0] for item in outs],
        in_specs=[item[1] for item in ins],
        out_specs=[item[1] for item in outs],
        scratch_shapes=[item for part in parts for item in part.scratch],
        cost_estimate=pl.CostEstimate(
            flops=0, bytes_accessed=cost_us * 3_000_000, transcendentals=0
        ),
        compiler_params=pltpu.CompilerParams(
            collective_id=collective_id, has_side_effects=True, vmem_limit_bytes=vmem << 20
        ),
    )(*[item[0] for item in ins])
    results = list(results)
    split = []
    for count in counts:
        split.append(results[: count[1]])
        del results[: count[1]]
    return split


def columns_of(place, width):
    return pl.ds(pl.multiple_of(place * width, width), width)


class UnitsOut(Part):
    def __init__(self, mats, layer):
        self.layer, self.count = layer, len(mats)
        self.size = lax.axis_size("dp")
        rows, self.width = mats[0].shape
        self.share = rows // (2 * self.size)
        self.ins = [(mat, HBM) for mat in mats]
        shape = jax.ShapeDtypeStruct((self.share, self.size * self.width), BF16)
        self.outs = [(shape, HBM)] * self.count
        self.scratch = [SEM((self.count,)), SEM((self.count, 2, self.size)), SEM((self.count, self.size))]

    def bind(self, ins, outs, scratch):
        self.src, self.dst = ins, outs
        self.keep, self.send, self.recv = scratch
        self.core, self.me = lax.axis_index("section"), lax.axis_index("dp")

    def piece(self, index, core, place):
        start = pl.multiple_of((core * self.size + place) * self.share, self.share)
        return self.src[index].at[pl.ds(start, self.share)]

    def lands(self, index, slot):
        return self.dst[index].at[:, columns_of(slot, self.width)]

    def copy(self, index, core, place, slot):
        return remote(
            self.piece(index, core, place), self.lands(index, slot),
            self.send.at[index, core, place], self.recv.at[index, slot],
            {"section": core, "dp": place},
        )

    def local(self, index):
        return pltpu.make_async_copy(
            self.piece(index, self.layer, self.me), self.lands(index, self.me), self.keep.at[index]
        )

    def targets(self):
        for index in range(self.count):
            for core in range(2):
                for place in range(self.size):
                    yield index, core, place, (place != self.me) | (core != self.layer)

    def start(self):
        @pl.when(self.core == self.layer)
        def _():
            for index, core, place, is_other in self.targets():
                @pl.when(is_other)
                def _():
                    self.copy(index, core, place, self.me).start()

            for index in range(self.count):
                self.local(index).start()

    def finish(self):
        for index in range(self.count):
            for place in range(self.size):
                @pl.when((self.core != self.layer) | (place != self.me))
                def _():
                    self.copy(index, 0, 0, place).wait_recv()

        @pl.when(self.core == self.layer)
        def _():
            for index, core, place, is_other in self.targets():
                @pl.when(is_other)
                def _():
                    self.copy(index, core, place, self.me).wait_send()

            for index in range(self.count):
                self.local(index).wait()


class UnitsHome(Part):
    def __init__(self, mats, layer):
        self.layer, self.count = layer, len(mats)
        self.size = lax.axis_size("dp")
        self.share, depth = mats[0].shape
        self.width = depth // self.size
        self.ins = [(mat, HBM) for mat in mats]
        shape = jax.ShapeDtypeStruct((2 * self.size * self.share, self.width), BF16)
        self.outs = [(shape, HBM)] * self.count
        self.scratch = [SEM((self.count,)), SEM((self.count, self.size)), SEM((self.count, 2, self.size))]

    def bind(self, ins, outs, scratch):
        self.src, self.dst = ins, outs
        self.keep, self.send, self.recv = scratch
        self.core, self.me = lax.axis_index("section"), lax.axis_index("dp")

    def lands(self, index, core, slot):
        start = pl.multiple_of((core * self.size + slot) * self.share, self.share)
        return self.dst[index].at[pl.ds(start, self.share)]

    def copy(self, index, place, core, slot):
        return remote(
            self.src[index].at[:, columns_of(place, self.width)], self.lands(index, core, slot),
            self.send.at[index, place], self.recv.at[index, core, slot],
            {"section": self.layer, "dp": place},
        )

    def local(self, index):
        return pltpu.make_async_copy(
            self.src[index].at[:, columns_of(self.me, self.width)],
            self.lands(index, self.layer, self.me), self.keep.at[index],
        )

    def start(self):
        for index in range(self.count):
            for place in range(self.size):
                @pl.when((self.core != self.layer) | (place != self.me))
                def _():
                    self.copy(index, place, self.core, self.me).start()

            @pl.when(self.core == self.layer)
            def _():
                self.local(index).start()

    def finish(self):
        for index in range(self.count):
            @pl.when(self.core == self.layer)
            def _():
                for core in range(2):
                    for place in range(self.size):
                        @pl.when((core != self.layer) | (place != self.me))
                        def _():
                            self.copy(index, 0, core, place).wait_recv()

                self.local(index).wait()

            for place in range(self.size):
                @pl.when((self.core != self.layer) | (place != self.me))
                def _():
                    self.copy(index, place, self.core, self.me).wait_send()


class UnitsSpread(Part):
    def __init__(self, rows):
        self.size = lax.axis_size("tensor")
        self.share, depth = rows.shape
        self.ins = [(rows, HBM)]
        self.outs = [(jax.ShapeDtypeStruct((self.size * self.share, depth), BF16), HBM)]
        self.scratch = [SEM, SEM((self.size,)), SEM((self.size,))]

    def bind(self, ins, outs, scratch):
        (self.src,), (self.dst,), (self.keep, self.send, self.recv) = ins, outs, scratch
        self.me = lax.axis_index("tensor")

    def lands(self, slot):
        return self.dst.at[pl.ds(pl.multiple_of(slot * self.share, self.share), self.share)]

    def copy(self, place, slot):
        return remote(
            self.src, self.lands(slot), self.send.at[place], self.recv.at[slot], {"tensor": place}
        )

    def start(self):
        for place in range(self.size):
            @pl.when(place != self.me)
            def _():
                self.copy(place, self.me).start()

        pltpu.make_async_copy(self.src, self.lands(self.me), self.keep).start()

    def finish(self):
        for place in range(self.size):
            @pl.when(place != self.me)
            def _():
                self.copy(place, place).wait_recv()
                self.copy(place, self.me).wait_send()

        pltpu.make_async_copy(self.src, self.lands(self.me), self.keep).wait()


class SharedRows(Part):
    def __init__(self, own):
        self.size = lax.axis_size("dp")
        self.ins = [(own, VMEM)]
        self.outs = [(jax.ShapeDtypeStruct((2, self.size) + own.shape, F32), VMEM)]
        self.scratch = [SEM((2, self.size)), SEM((2, self.size))]

    def copy(self, core, place, from_core, from_place):
        return remote(
            self.in_refs[0], self.out_refs[0].at[from_core, from_place],
            self.refs[0].at[core, place], self.refs[1].at[from_core, from_place],
            {"section": core, "dp": place},
        )

    def others(self):
        core, me = lax.axis_index("section"), lax.axis_index("dp")
        for other in range(2):
            for place in range(self.size):
                yield other, place, (other != core) | (place != me)

    def start(self):
        core, me = lax.axis_index("section"), lax.axis_index("dp")
        for other, place, is_other in self.others():
            @pl.when(is_other)
            def _():
                self.copy(other, place, core, me).start()

        self.out_refs[0][core, me] = self.in_refs[0][...]

    def finish(self):
        core, me = lax.axis_index("section"), lax.axis_index("dp")
        for other, place, is_other in self.others():
            @pl.when(is_other)
            def _():
                self.copy(other, place, other, place).wait_recv()
                self.copy(other, place, core, me).wait_send()


def far_pair(place, me):
    return (place + me == 3) & ((place == 0) | (place == 3))


def line_relays(size):
    return [(2, 0, 3), (1, 3, 0)] if size == 4 else []


def line_order(size):
    return [1, 2, 0, 3] if size == 4 else list(range(size))


class AttnShards:
    def __init__(self, w_query, w_key, w_value, w_out):
        self.arrays = [w_query, w_key, w_value, w_out]
        self.depth = w_query.shape[0]
        self.q_width, self.k_width = w_query.shape[1] // 2, w_key.shape[1] // 2
        self.width = self.q_width + 2 * self.k_width
        half = self.depth // 2
        parts = self.q_width // 2
        self.items = [
            (0, lambda ref, core: ref.at[pl.ds(0, half), columns_of(core, self.q_width)]),
            (0, lambda ref, core: ref.at[pl.ds(half, half), columns_of(core, self.q_width)]),
            (1, lambda ref, core: ref.at[:, columns_of(core, self.k_width)]),
            (2, lambda ref, core: ref.at[:, columns_of(core, self.k_width)]),
            (3, lambda ref, core: ref.at[pl.ds(core * self.q_width, parts)]),
            (3, lambda ref, core: ref.at[pl.ds(core * self.q_width + parts, parts)]),
        ]
        q_width, k_width, depth = self.q_width, self.k_width, self.depth
        self.qkv_rows = [(0, half), (half, half), (0, depth), (0, depth)]
        self.qkv_columns = [
            (0, q_width), (0, q_width), (q_width, k_width), (q_width + k_width, k_width)
        ]
        self.out_rows = [(0, parts), (parts, parts)]

    def source(self, refs, index, core):
        array, cut = self.items[index]
        return cut(refs[array], core)

    def lands(self, qkv, out, index, slot):
        if index < 4:
            (start, rows), (left, columns) = self.qkv_rows[index], self.qkv_columns[index]
            at = pl.multiple_of(slot * self.depth + start, rows)
            return qkv.at[pl.ds(at, rows), pl.ds(left, columns)]
        start, rows = self.out_rows[index - 4]
        return out.at[pl.ds(start, rows), columns_of(slot, self.depth)]


class AttnOut(Part):
    def __init__(self, shards, layer):
        self.layer, self.shards = layer, shards
        self.size = lax.axis_size("dp")
        self.count = len(shards.items)
        depth = self.size * shards.depth
        self.ins = [(array, HBM) for array in shards.arrays]
        self.outs = [
            (jax.ShapeDtypeStruct((depth, shards.width), BF16), HBM),
            (jax.ShapeDtypeStruct((shards.q_width, depth), BF16), HBM),
        ]
        self.scratch = [
            SEM((self.count,)), SEM((2, self.size, self.count)), SEM((self.size, self.count)),
            SEM((self.count,)),
        ]

    def bind(self, ins, outs, scratch):
        self.src = ins
        self.qkv, self.out = outs
        self.keep, self.send, self.recv, self.relay_send = scratch
        self.core, self.me = lax.axis_index("section"), lax.axis_index("dp")

    def lands(self, index, slot):
        return self.shards.lands(self.qkv, self.out, index, slot)

    def copy(self, core, place, slot, index):
        return remote(
            self.shards.source(self.src, index, core), self.lands(index, slot),
            self.send.at[core, place, index], self.recv.at[slot, index],
            {"section": core, "dp": place},
        )

    def relay(self, source, target, index):
        block = self.lands(index, source)
        return remote(
            block, block, self.relay_send.at[index], self.recv.at[source, index], {"dp": target}
        )

    def local(self, index):
        return pltpu.make_async_copy(
            self.shards.source(self.src, index, self.layer), self.lands(index, self.me),
            self.keep.at[index],
        )

    def targets(self):
        for index in range(self.count):
            for core in range(2):
                for place in range(self.size):
                    sent = (place != self.me) | (core != self.layer)
                    if self.size == 4:
                        sent = sent & jnp.logical_not(far_pair(place, self.me))
                    yield core, place, index, sent

    def start(self):
        @pl.when(self.core == self.layer)
        def _():
            for core, place, index, sent in self.targets():
                @pl.when(sent)
                def _():
                    self.copy(core, place, self.me, index).start()

            for index in range(self.count):
                self.local(index).start()

    def run(self):
        for index in range(self.count):
            for place in line_order(self.size):
                @pl.when((self.core != self.layer) | (place != self.me))
                def _():
                    self.copy(0, 0, place, index).wait_recv()

                for via, source, target in line_relays(self.size):
                    if source == place:
                        @pl.when(self.me == via)
                        def _():
                            self.relay(source, target, index).start()

    def finish(self):
        @pl.when(self.core == self.layer)
        def _():
            for core, place, index, sent in self.targets():
                @pl.when(sent)
                def _():
                    self.copy(core, place, self.me, index).wait_send()

            for index in range(self.count):
                self.local(index).wait()

        for via, source, target in line_relays(self.size):
            @pl.when(self.me == via)
            def _():
                for index in range(self.count):
                    self.relay(source, target, index).wait_send()


class HalfOver(Part):
    def __init__(self, shards):
        self.shards = shards
        self.count = len(shards.items)
        rows = shards.depth + shards.q_width
        self.ins = [(array, HBM) for array in shards.arrays]
        self.outs = [(jax.ShapeDtypeStruct((rows, shards.depth), BF16), HBM)]
        self.scratch = [SEM((self.count,)), SEM((self.count,)), SEM((self.count,))]

    def lands(self, index):
        depth, q_width = self.shards.depth, self.shards.q_width
        packed = self.out_refs[0]
        return self.shards.lands(
            packed.at[pl.ds(0, depth)], packed.at[pl.ds(depth, q_width)], index, 0
        )

    def over(self, index):
        return remote(
            self.shards.source(self.in_refs, index, 0), self.lands(index), self.refs[0].at[index],
            self.refs[1].at[index], {"section": 0},
        )

    def keep(self, index):
        return pltpu.make_async_copy(
            self.shards.source(self.in_refs, index, 1), self.lands(index), self.refs[2].at[index]
        )

    def start(self):
        @pl.when(lax.axis_index("section") == 1)
        def _():
            for index in range(self.count):
                self.over(index).start()
                self.keep(index).start()

    def finish(self):
        @pl.when(lax.axis_index("section") == 1)
        def _():
            for index in range(self.count):
                self.over(index).wait_send()
                self.keep(index).wait()

        @pl.when(lax.axis_index("section") == 0)
        def _():
            for index in range(self.count):
                self.over(index).wait_recv()


class Swap(Part):
    def __init__(self, own):
        self.ins = [(own, HBM)]
        self.outs = [(jax.ShapeDtypeStruct(own.shape, own.dtype), HBM)]
        self.scratch = [SEM, SEM]

    def start(self):
        sibling = 1 - lax.axis_index("section")
        self.copy = remote(
            self.in_refs[0], self.out_refs[0], self.refs[0], self.refs[1], {"section": sibling}
        )
        self.copy.start()

    def finish(self):
        self.copy.wait()


class GatherKV(Part):
    def __init__(self, own):
        trees, rows, width = own.shape
        self.trees, self.size = trees, lax.axis_size("dp")
        self.ins = [(own, VMEM)]
        self.outs = [(jax.ShapeDtypeStruct((trees, self.size, rows, width), BF16), VMEM)]
        self.scratch = [SEM((self.size, trees)), SEM((self.size, trees)), SEM((trees,))]

    def bind(self, ins, outs, scratch):
        (self.own,), (self.out,) = ins, outs
        self.send, self.recv, self.relay_send = scratch
        self.me = lax.axis_index("dp")

    def copy(self, place, slot, tree):
        return remote(
            self.own.at[tree], self.out.at[tree, slot], self.send.at[place, tree],
            self.recv.at[slot, tree], {"dp": place},
        )

    def relay(self, source, target, tree):
        return remote(
            self.out.at[tree, source], self.out.at[tree, source], self.relay_send.at[tree],
            self.recv.at[source, tree], {"dp": target},
        )

    def targets(self):
        for tree in range(self.trees):
            for place in range(self.size):
                sent = place != self.me
                if self.size == 4:
                    sent = sent & jnp.logical_not(far_pair(place, self.me))
                yield place, tree, sent

    def start(self):
        for place, tree, sent in self.targets():
            @pl.when(sent)
            def _():
                self.copy(place, self.me, tree).start()

        self.out[:, self.me] = self.own[...]

    def run(self):
        for tree in range(self.trees):
            for place in line_order(self.size):
                @pl.when(place != self.me)
                def _():
                    self.copy(place, place, tree).wait_recv()

                for via, source, target in line_relays(self.size):
                    if source == place:
                        @pl.when(self.me == via)
                        def _():
                            self.relay(source, target, tree).start()

    def finish(self):
        for place, tree, sent in self.targets():
            @pl.when(sent)
            def _():
                self.copy(place, self.me, tree).wait_send()

        for via, source, target in line_relays(self.size):
            @pl.when(self.me == via)
            def _():
                for tree in range(self.trees):
                    self.relay(source, target, tree).wait_send()


class ScatterKV(Part):
    def __init__(self, whole):
        trees, size, rows, width = whole.shape
        self.trees, self.size = trees, size
        self.sides = [(0, 1, 3), (3, 2, 0)] if size == 4 else []
        self.ins = [(whole, VMEM)]
        self.outs = [(jax.ShapeDtypeStruct((trees, rows, width), F32), VMEM)]
        self.scratch = [
            pltpu.VMEM((size, trees, rows, width), BF16), pltpu.VMEM((trees, rows, width), BF16),
            SEM((size, trees)), SEM((size, trees)), SEM((trees,)), SEM((trees,)),
        ]

    def bind(self, ins, outs, scratch):
        (self.terms,), (self.out,) = ins, outs
        self.boxes, self.joint, self.send, self.recv, self.join_send, self.join_recv = scratch
        self.me = lax.axis_index("dp")

    def copy(self, place, slot, tree):
        return remote(
            self.terms.at[tree, place], self.boxes.at[slot, tree], self.send.at[place, tree],
            self.recv.at[slot, tree], {"dp": place},
        )

    def by_way(self, via, target, tree):
        return remote(
            self.terms.at[tree, target], self.joint.at[tree], self.join_send.at[tree],
            self.join_recv.at[tree], {"dp": via},
        )

    def joined(self, via, target, tree):
        return remote(
            self.joint.at[tree], self.boxes.at[via, tree], self.send.at[target, tree],
            self.recv.at[via, tree], {"dp": target},
        )

    def plain(self, place):
        ok = place != self.me
        for source, via, target in self.sides:
            if place == target:
                ok = ok & (self.me != source) & (self.me != via)
        return ok

    def expected(self, place):
        ok = place != self.me
        for source, via, target in self.sides:
            if place == source:
                ok = ok & (self.me != target)
        return ok

    def start(self):
        for tree in range(self.trees):
            for source, via, target in self.sides:
                @pl.when(self.me == source)
                def _():
                    self.by_way(via, target, tree).start()

            for place in range(self.size):
                @pl.when(self.plain(place))
                def _():
                    self.copy(place, self.me, tree).start()

    def run(self):
        for tree in range(self.trees):
            for source, via, target in self.sides:
                @pl.when(self.me == via)
                def _():
                    self.by_way(via, target, tree).wait_recv()
                    both = self.joint[tree].astype(F32) + self.terms[tree, target].astype(F32)
                    self.joint[tree] = both.astype(BF16)
                    self.joined(via, target, tree).start()

        for tree in range(self.trees):
            self.out[tree] = self.terms[tree, self.me].astype(F32)
            for place in line_order(self.size):
                @pl.when(self.expected(place))
                def _():
                    self.copy(place, place, tree).wait_recv()
                    self.out[tree] += self.boxes[place, tree].astype(F32)

    def finish(self):
        for tree in range(self.trees):
            for place in range(self.size):
                @pl.when(self.plain(place))
                def _():
                    self.copy(place, self.me, tree).wait_send()

            for source, via, target in self.sides:
                @pl.when(self.me == source)
                def _():
                    self.by_way(via, target, tree).wait_send()

                @pl.when(self.me == via)
                def _():
                    self.joined(via, target, tree).wait_send()


class TotalOverAll(Part):
    axes = ("section", "tensor", "dp")

    def __init__(self, own):
        sizes = [lax.axis_size(axis) for axis in self.axes]
        self.ins = [(own, VMEM)]
        self.outs = [(jax.ShapeDtypeStruct(own.shape, F32), VMEM)]
        self.scratch = [pltpu.VMEM((size,) + own.shape, F32) for size in sizes]
        self.scratch += [SEM((size,)) for size in sizes] * 2

    def run(self):
        out = self.out_refs[0]
        out[...] = self.in_refs[0][...]
        for axis, box, send, recv in zip(self.axes, self.refs[:3], self.refs[3:6], self.refs[6:9]):
            size, me = lax.axis_size(axis), lax.axis_index(axis)
            box[me] = out[...]

            def spread(place, slot):
                return remote(box.at[me], box.at[slot], send.at[place], recv.at[slot], {axis: place})

            for place in range(size):
                @pl.when(place != me)
                def _():
                    spread(place, me).start()

            for place in range(size):
                @pl.when(place != me)
                def _():
                    spread(place, place).wait_recv()
                    spread(place, me).wait_send()

            total = box[0]
            for place in range(1, size):
                total += box[place]
            out[...] = total


def chunk_count(rows):
    return 3 if rows % 24 == 0 else 1


class Gatherer:
    def __init__(self, axis, rows, half):
        self.axis, self.half = axis, half
        self.size = size = lax.axis_size(axis)
        self.chunks = chunks = chunk_count(rows)
        self.rows = rows // chunks
        self.scratch = [pltpu.VMEM((2, chunks, size, 2 * self.rows, half), BF16)]
        self.scratch += [SEM((chunks, size))] * 4 + [SEM((chunks,))]

    def bind(self, refs):
        self.board, self.send, self.recv, self.sib_send, self.sib_recv, self.relay_send = refs
        self.core = lax.axis_index("section")
        self.sibling = 1 - self.core
        self.me = lax.axis_index(self.axis)
        self.relays = line_relays(self.size) if self.axis == "dp" else []
        self.order = line_order(self.size) if self.axis == "dp" else range(self.size)

    def direct(self, place):
        sent = place != self.me
        if self.relays:
            sent = sent & jnp.logical_not(far_pair(place, self.me))
        return sent

    def spread(self, chunk, place, slot):
        block = self.board.at[self.core, chunk, slot]
        return remote(
            block, block, self.send.at[chunk, place], self.recv.at[chunk, slot], {self.axis: place}
        )

    def passed(self, chunk, source, target):
        block = self.board.at[self.core, chunk, source]
        return remote(
            block, block, self.relay_send.at[chunk], self.recv.at[chunk, source],
            {self.axis: target},
        )

    def over(self, tree, chunk, slot):
        block = self.board.at[tree, chunk, slot]
        return remote(
            block, block, self.sib_send.at[chunk, slot], self.sib_recv.at[chunk, slot],
            {"section": self.sibling},
        )

    def begin(self, chunk, result):
        half = self.half
        piece = jnp.concatenate([result[:, :half], result[:, half:]], axis=0)
        self.board[self.core, chunk, self.me] = piece.astype(BF16)
        for place in range(self.size):
            @pl.when(self.direct(place))
            def _():
                self.spread(chunk, place, self.me).start()

        self.over(self.core, chunk, self.me).start()

    def arrive(self, chunk):
        for place in self.order:
            @pl.when(place != self.me)
            def _():
                self.spread(chunk, place, place).wait_recv()

            for via, source, target in self.relays:
                if source == place:
                    @pl.when(self.me == via)
                    def _():
                        self.passed(chunk, source, target).start()

            @pl.when(place != self.me)
            def _():
                self.over(self.core, chunk, place).start()

    def arrive_over(self, chunk):
        for place in range(self.size):
            self.over(self.sibling, chunk, place).wait_recv()

    def side_rows(self, block, side):
        return block[side * self.rows : (side + 1) * self.rows]

    def unpack(self, out, tree):
        @pl.loop(0, self.half // CHUNK)
        def _(step):
            at = pl.multiple_of(step * CHUNK, CHUNK)
            blocks = [
                self.board[tree, chunk, place, :, pl.ds(at, CHUNK)].astype(F32)
                for place in range(self.size)
                for chunk in range(self.chunks)
            ]
            for side in range(2):
                whole = [self.side_rows(block, side) for block in blocks]
                out[tree, :, pl.ds(side * self.half + at, CHUNK)] = jnp.concatenate(
                    whole, axis=0
                ).astype(BF16)

    def unpack_chunk(self, out, chunk):
        @pl.loop(0, self.half // CHUNK)
        def _(step):
            at = pl.multiple_of(step * CHUNK, CHUNK)
            blocks = [
                self.board[tree, chunk, place, :, pl.ds(at, CHUNK)].astype(F32)
                for place in range(self.size)
                for tree in range(2)
            ]
            for side in range(2):
                whole = [self.side_rows(block, side) for block in blocks]
                out[chunk, :, pl.ds(side * self.half + at, CHUNK)] = jnp.concatenate(
                    whole, axis=0
                ).astype(BF16)

    def complete(self, out):
        for chunk in range(self.chunks):
            self.arrive(chunk)
        self.unpack(out, self.core)
        for chunk in range(self.chunks):
            self.arrive_over(chunk)
        self.unpack(out, self.sibling)

    def finish(self):
        for chunk in range(self.chunks):
            for place in range(self.size):
                @pl.when(self.direct(place))
                def _():
                    self.spread(chunk, place, self.me).wait_send()

                self.over(self.core, chunk, place).wait_send()

            for via, source, target in self.relays:
                @pl.when(self.me == via)
                def _():
                    self.passed(chunk, source, target).wait_send()


class Scatterer:
    def __init__(self, axis, rows, half):
        self.axis, self.half = axis, half
        self.size = size = lax.axis_size(axis)
        self.chunks = chunks = chunk_count(rows)
        self.rows = rows // chunks
        block = (2 * self.rows, half)
        self.scratch = [pltpu.VMEM((chunks, size) + block, BF16)] * 4
        self.scratch += [pltpu.VMEM((chunks,) + block, F32), pltpu.VMEM((chunks,) + block, BF16)]
        self.scratch += [SEM((chunks, size))] * 4 + [SEM((chunks,))] * 2

    def bind(self, refs):
        self.to_sib, self.from_sib, self.to_peer, self.from_peer, self.total, self.joint = refs[:6]
        self.sib_send, self.sib_recv, self.peer_send, self.peer_recv = refs[6:10]
        self.join_send, self.join_recv = refs[10:]
        self.core = lax.axis_index("section")
        self.sibling = 1 - self.core
        self.me = lax.axis_index(self.axis)
        self.sides = [(0, 1, 3), (3, 2, 0)] if self.axis == "dp" and self.size == 4 else []
        self.order = [0, 3, 1, 2] if self.sides else range(self.size)

    def over(self, chunk, place):
        return remote(
            self.to_sib.at[chunk, place], self.from_sib.at[chunk, place],
            self.sib_send.at[chunk, place], self.sib_recv.at[chunk, place],
            {"section": self.sibling},
        )

    def spread(self, chunk, place, slot):
        return remote(
            self.to_peer.at[chunk, place], self.from_peer.at[chunk, slot],
            self.peer_send.at[chunk, place], self.peer_recv.at[chunk, slot], {self.axis: place},
        )

    def by_way(self, chunk, via, target):
        return remote(
            self.to_peer.at[chunk, target], self.joint.at[chunk], self.join_send.at[chunk],
            self.join_recv.at[chunk], {self.axis: via},
        )

    def plain(self, place):
        ok = place != self.me
        for source, via, target in self.sides:
            if place == target:
                ok = ok & (self.me != source) & (self.me != via)
        return ok

    def expected(self, place):
        ok = place != self.me
        for source, via, target in self.sides:
            if place == source:
                ok = ok & (self.me != target)
        return ok

    def over_columns(self, body):
        @pl.loop(0, self.half // CHUNK)
        def _(step):
            body(pl.multiple_of(step * CHUNK, CHUNK))

    def absorb(self, chunk, mine):
        for place in self.order:
            self.over(chunk, place).wait_recv()

            def add(at):
                both = mine(place, at)
                both += self.from_sib[chunk, place, :, pl.ds(at, CHUNK)].astype(F32)
                self.to_peer[chunk, place, :, pl.ds(at, CHUNK)] = both.astype(BF16)

                @pl.when(place == self.me)
                def _():
                    self.total[chunk, :, pl.ds(at, CHUNK)] = both

            self.over_columns(add)

            for source, via, target in self.sides:
                if place == target:
                    @pl.when(self.me == source)
                    def _():
                        self.by_way(chunk, via, target).start()

            @pl.when(self.plain(place))
            def _():
                self.spread(chunk, place, self.me).start()

        for source, via, target in self.sides:
            @pl.when(self.me == via)
            def _():
                self.by_way(chunk, via, target).wait_recv()

                def add(at):
                    at = pl.ds(at, CHUNK)
                    both = self.to_peer[chunk, target, :, at].astype(F32)
                    both += self.joint[chunk, :, at].astype(F32)
                    self.to_peer[chunk, target, :, at] = both.astype(BF16)

                self.over_columns(add)
                self.spread(chunk, target, self.me).start()

    def collect(self, chunk):
        for place in self.order:
            @pl.when(self.expected(place))
            def _():
                self.spread(chunk, place, place).wait_recv()
                self.total[chunk] += self.from_peer[chunk, place].astype(F32)

        total = self.total[chunk]
        return jnp.concatenate([total[: self.rows], total[self.rows :]], axis=1)

    def finish(self):
        for chunk in range(self.chunks):
            for place in range(self.size):
                self.over(chunk, place).wait_send()

                @pl.when(self.plain(place))
                def _():
                    self.spread(chunk, place, self.me).wait_send()

            for source, via, target in self.sides:
                @pl.when(self.me == source)
                def _():
                    self.by_way(chunk, via, target).wait_send()

                @pl.when(self.me == via)
                def _():
                    self.spread(chunk, target, self.me).wait_send()


class RowScatterer(Scatterer):
    def packed(self, tree, chunk, place, at):
        rows = self.rows
        first = rows * (place * self.chunks + chunk)
        low = first // 16 * 16
        high = -(-(first + rows) // 16) * 16
        parts = [
            self.terms[tree, low:high, pl.ds(side * self.half + at, CHUNK)].astype(F32)[
                first - low : first - low + rows
            ]
            for side in range(2)
        ]
        return jnp.concatenate(parts, axis=0)

    def prepare(self, terms):
        self.terms = terms
        for chunk in range(self.chunks):
            for place in range(self.size):
                def pack(at):
                    self.to_sib[chunk, place, :, pl.ds(at, CHUNK)] = self.packed(
                        self.sibling, chunk, place, at
                    ).astype(BF16)

                self.over_columns(pack)

    def start(self):
        for chunk in range(self.chunks):
            for place in range(self.size):
                self.over(chunk, place).start()

    def send_on(self):
        for chunk in range(self.chunks):
            self.absorb(chunk, lambda place, at: self.packed(self.core, chunk, place, at))


class Staged(Part):
    def __init__(self, ins, outs, scratch, helpers):
        self.in_names, self.out_names, self.scratch_names = list(ins), list(outs), list(scratch)
        self.ins, self.outs = list(ins.values()), list(outs.values())
        self.helpers = helpers
        self.scratch = list(scratch.values())
        for helper in helpers:
            self.scratch += helper.scratch

    def bind(self, ins, outs, scratch):
        scratch = list(scratch)
        names = self.in_names + self.out_names + self.scratch_names
        count = len(self.scratch_names)
        for name, ref in zip(names, list(ins) + list(outs) + scratch[:count]):
            setattr(self, name, ref)
        del scratch[:count]
        for helper in self.helpers:
            helper.bind(scratch[: len(helper.scratch)])
            del scratch[: len(helper.scratch)]

    def finish(self):
        for helper in self.helpers:
            helper.finish()


def vmem_f32(*shape):
    return (jax.ShapeDtypeStruct(shape, F32), VMEM)


def vmem_bf16(*shape):
    return (jax.ShapeDtypeStruct(shape, BF16), VMEM)


def rows_at(chunk, rows):
    return pl.ds(pl.multiple_of(chunk * rows, 8), rows)


class LastHub(Staged):
    def __init__(self, terms, values, gain, add):
        rows, depth = values.shape
        half = depth // 2
        self.rows_in = RowScatterer("tensor", rows, half)
        self.rows_out = Gatherer("tensor", rows, half)
        super().__init__(
            {"terms": (terms, VMEM), "values": (values, VMEM), "gain": (gain, VMEM), "add": (add, VMEM)},
            {
                "gain_grad": vmem_f32(1, depth),
                "gathered": vmem_bf16(2, self.rows_out.size * rows, depth),
            },
            {},
            [self.rows_in, self.rows_out],
        )

    def prepare(self):
        self.rows_in.prepare(self.terms)

    def start(self):
        self.rows_in.start()

    def run(self):
        self.rows_in.send_on()
        self.gain_grad[...] = jnp.zeros_like(self.gain_grad)
        for chunk in range(self.rows_in.chunks):
            at = rows_at(chunk, self.rows_in.rows)
            result, gain_grad = norm_back(
                self.rows_in.collect(chunk), self.values[at], self.gain[...]
            )
            self.gain_grad[...] += gain_grad
            self.rows_out.begin(chunk, result + self.add[at])
        self.rows_out.complete(self.gathered)


class FeedForward(Staged):
    def __init__(self, terms, own, gain, weights, forward, backward, extra):
        rows, depth = own.shape
        half = depth // 2
        units = weights[0].shape[0]
        self.has_forward, self.has_backward, self.units = forward, backward, units
        self.depth = depth
        self.size = size = lax.axis_size("dp")
        self.rows_in = RowScatterer("tensor", rows, half)
        self.spread_in = Gatherer("dp", rows, half)
        self.chunks, self.rows = self.rows_in.chunks, self.rows_in.rows
        chunks, chunk_rows = self.chunks, 2 * size * self.rows
        helpers = [self.rows_in, self.spread_in]
        tensor_rows = lax.axis_size("tensor") * rows
        matrix = pltpu.VMEM((units, depth), BF16)
        ins = {"terms": (terms, VMEM), "own": (own, VMEM), "gain": (gain, VMEM)}
        ins |= {name: (w, HBM) for name, w in zip(("gate_hbm", "up_hbm", "down_hbm"), weights)}
        ins |= {name: (value, VMEM) for name, value in extra.items()}
        outs = {}
        scratch = {"w_gate": matrix, "w_up": matrix, "w_down": matrix, "load": SEM((3,))}
        kept = pltpu.VMEM((size, 2 * self.rows, half), F32)
        if forward:
            outs |= {
                "middle": vmem_f32(rows, depth),
                "mlp_in": vmem_bf16(chunks, chunk_rows, depth),
                "hidden": vmem_bf16(chunks, chunk_rows, units),
                "own_out": vmem_f32(rows, depth),
                "out": vmem_bf16(2, tensor_rows, depth),
            }
            self.back = Scatterer("dp", rows, half)
            self.out_rows = Gatherer("tensor", rows, half)
            helpers += [self.back, self.out_rows]
            scratch["kept"] = kept
        if forward and not backward:
            outs |= {"gate": vmem_f32(chunks, chunk_rows, units), "up": vmem_f32(chunks, chunk_rows, units)}
        if forward and backward:
            outs["grad_mlp"] = vmem_bf16(chunks, chunk_rows, depth)
            self.grad_in = Gatherer("dp", rows, half)
            helpers += [self.grad_in]
            scratch |= {
                "gate": pltpu.VMEM((chunks, chunk_rows, units), F32),
                "up": pltpu.VMEM((chunks, chunk_rows, units), F32),
            }
        if backward:
            outs |= {
                "grad_gate": vmem_bf16(chunks, chunk_rows, units),
                "grad_up": vmem_bf16(chunks, chunk_rows, units),
                "grad_middle": vmem_f32(rows, depth),
                "mlp_gain_grad": vmem_f32(1, depth),
                "grad_attn": vmem_bf16(2, tensor_rows, depth),
            }
            self.grad_back = Scatterer("dp", rows, half)
            self.grad_rows = Gatherer("tensor", rows, half)
            helpers += [self.grad_back, self.grad_rows]
            scratch["grad_kept"] = kept
        if backward and not forward:
            outs |= {
                "gain_grad": vmem_f32(1, depth),
                "incoming": vmem_bf16(2, tensor_rows, depth),
                "grad_mlp": vmem_bf16(chunks, chunk_rows, depth),
            }
            scratch["grad_own"] = pltpu.VMEM((rows, depth), F32)
            self.incoming_rows = Gatherer("tensor", rows, half)
            helpers += [self.incoming_rows]
        super().__init__(ins, outs, scratch, helpers)

    def loads(self):
        pairs = [(self.gate_hbm, self.w_gate), (self.up_hbm, self.w_up), (self.down_hbm, self.w_down)]
        return [
            pltpu.make_async_copy(src, dst, self.load.at[i]) for i, (src, dst) in enumerate(pairs)
        ]

    def prepare(self):
        for copy in self.loads():
            copy.start()
        self.rows_in.prepare(self.terms)

    def start(self):
        self.rows_in.start()
        if self.has_forward and self.has_backward:
            for chunk in range(self.chunks):
                self.grad_in.begin(chunk, self.grad_own[rows_at(chunk, self.rows)])

    def run(self):
        self.rows_in.send_on()
        if self.has_backward:
            self.mlp_gain_grad[...] = jnp.zeros_like(self.mlp_gain_grad)
        if not self.has_forward:
            self.gain_grad[...] = jnp.zeros_like(self.gain_grad)
        for chunk in range(self.chunks):
            at = rows_at(chunk, self.rows)
            total = self.rows_in.collect(chunk)
            if self.has_forward:
                middle = self.own[at] + total
                self.middle[at] = middle
                mean_sq = jnp.mean(middle * middle, axis=1, keepdims=True)
                normed = middle * lax.rsqrt(mean_sq + EPSILON) * self.gain[...]
                self.spread_in.begin(chunk, normed)
            else:
                result, gain_grad = norm_back(total, self.own[at], self.gain[...])
                self.gain_grad[...] += gain_grad
                result = (result + self.add[at]).astype(BF16).astype(F32)
                self.grad_own[at] = result
                self.spread_in.begin(chunk, result)
                self.incoming_rows.begin(chunk, result)
        for copy in self.loads():
            copy.wait()

        self.spread_in.arrive(0)
        if self.has_forward and self.has_backward:
            self.grad_in.arrive(0)

        @pl.loop(0, self.chunks)
        def _(chunk):
            self.spread_in.arrive_over(chunk)
            if self.has_forward:
                self.spread_in.unpack_chunk(self.mlp_in, chunk)
                self.forward_chunk(chunk)
            else:
                self.spread_in.unpack_chunk(self.grad_mlp, chunk)
            if self.has_forward and self.has_backward:
                self.grad_in.arrive_over(chunk)
                self.grad_in.unpack_chunk(self.grad_mlp, chunk)
            if self.has_backward:
                self.backward_chunk(chunk)

            @pl.when(chunk + 1 < self.chunks)
            def _():
                self.spread_in.arrive(chunk + 1)
                if self.has_forward and self.has_backward:
                    self.grad_in.arrive(chunk + 1)

            if self.has_forward:
                self.back.absorb(chunk, lambda place, at: self.kept[place, :, pl.ds(at, CHUNK)])
            if self.has_backward:
                self.grad_back.absorb(
                    chunk, lambda place, at: self.grad_kept[place, :, pl.ds(at, CHUNK)]
                )

            @pl.when(chunk > 0)
            def _():
                self.hand_back(chunk - 1)

        self.hand_back(self.chunks - 1)
        if self.has_backward:
            self.grad_rows.complete(self.grad_attn)
        if self.has_forward:
            self.out_rows.complete(self.out)
        else:
            self.incoming_rows.complete(self.incoming)

    def hand_back(self, chunk):
        at = rows_at(chunk, self.rows)
        if self.has_backward:
            values = self.middle if self.has_forward else self.middle_in
            gain = self.gain if self.has_forward else self.mlp_gain
            result, gain_grad = norm_back(self.grad_back.collect(chunk), values[at], gain[...])
            self.mlp_gain_grad[...] += gain_grad
            result += self.grad_own[at]
            self.grad_middle[at] = result
            self.grad_rows.begin(chunk, result)
        if self.has_forward:
            output = (self.middle[at] + self.back.collect(chunk)).astype(BF16).astype(F32)
            self.own_out[at] = output
            self.out_rows.begin(chunk, output)

    def unit_tiles(self, body):
        tile = 256

        @pl.loop(0, self.units // tile)
        def _(step):
            body(pl.ds(pl.multiple_of(step * tile, tile), tile))

    def forward_chunk(self, chunk):
        def tile(at):
            rows = self.mlp_in[chunk]
            gate = dot_inner(rows, self.w_gate[at, :])
            up = dot_inner(rows, self.w_up[at, :])
            self.gate[chunk, :, at] = gate
            self.up[chunk, :, at] = up
            self.hidden[chunk, :, at] = (gate * jax.nn.sigmoid(gate) * up).astype(BF16)

        self.unit_tiles(tile)
        self.terms_out(
            chunk, self.back, self.kept, lambda at: dot(self.hidden[chunk], self.w_down[:, at])
        )

    def backward_chunk(self, chunk):
        def tile(at):
            grad_hidden = dot_inner(self.grad_mlp[chunk], self.w_down[at, :])
            gate, up = self.gate[chunk, :, at], self.up[chunk, :, at]
            share = jax.nn.sigmoid(gate)
            act = gate * share
            self.grad_up[chunk, :, at] = (grad_hidden * act).astype(BF16)
            self.grad_gate[chunk, :, at] = (
                grad_hidden * up * (share + act * (1.0 - share))
            ).astype(BF16)

        self.unit_tiles(tile)
        self.terms_out(
            chunk, self.grad_back, self.grad_kept,
            lambda at: dot(self.grad_gate[chunk], self.w_gate[:, at])
            + dot(self.grad_up[chunk], self.w_up[:, at]),
        )

    def terms_out(self, chunk, scatterer, kept, product):
        rows, half = self.rows, self.depth // 2
        first = lax.axis_index("section") == 0

        @pl.loop(0, half // CHUNK)
        def _(step):
            low = pl.multiple_of(step * CHUNK, CHUNK)
            at = pl.ds(low, CHUNK)
            sides = [product(pl.ds(side * half + low, CHUNK)) for side in range(2)]
            for place in range(self.size):
                trees = []
                for tree in range(2):
                    start = (2 * place + tree) * rows
                    trees.append(
                        jnp.concatenate([side[start : start + rows] for side in sides], axis=0)
                    )
                kept[place, :, at] = jnp.where(first, trees[0], trees[1])
                scatterer.to_sib[chunk, place, :, at] = jnp.where(
                    first, trees[1], trees[0]
                ).astype(BF16)

        for place in range(self.size):
            scatterer.over(chunk, place).start()


def hub_plain(terms, own_args, body, own_outs, scatter, gathers):
    total = None
    if scatter:
        mine = lax.psum_scatter(terms, "section", scatter_dimension=0, tiled=True)
        mine = lax.psum_scatter(mine, scatter, scatter_dimension=1, tiled=True)[0]
        total = mine.astype(F32)

    class Cell:
        def __setitem__(self, _, value):
            self.value = value

    cells = [Cell() for _ in own_outs]
    result = body(total, own_args, cells).astype(BF16)
    gathered = [
        lax.all_gather(lax.all_gather(result, axis, axis=0, tiled=True), "section", axis=0)
        for axis in gathers
    ]
    return [cell.value for cell in cells] + gathered


def with_cargo(part, cargo, axes, collective_id, cost_us, vmem=40):
    outs = fused(cargo + [part], axes, bool(cargo), collective_id, cost_us, vmem)
    return outs[-1], outs[:-1]


def norm_back(total, values, gain):
    scale = lax.rsqrt(jnp.mean(values * values, axis=1, keepdims=True) + EPSILON)
    unit = values * scale
    gain_grad = jnp.sum(total * unit, axis=0, keepdims=True)
    scaled = total * gain
    along = jnp.mean(scaled * unit, axis=1, keepdims=True)
    return ((scaled - unit * along) * scale, gain_grad)


def norm_body(total, args, outs):
    middle = args[0] + total
    outs[0][...] = middle
    return rms_scale(middle, args[1])


def add_body(total, args, outs):
    result = args[0] + total
    outs[0][...] = result
    return result


def norm_back_body(total, args, outs):
    result, outs[1][...] = norm_back(total, args[0], args[1])
    result += args[2]
    outs[0][...] = result
    return result


def embed(q_pre, k_pre, q_scale, k_scale, cos_table, sine_table):
    queries = rms_scale(q_pre, q_scale)
    keys = rms_scale(k_pre, k_scale)
    return (
        rotate(queries, cos_table[:, :, None], sine_table[:, :, None]),
        rotate(keys, cos_table, sine_table),
    )


def attn_forward(hidden_in, weights, gains, slot, gather):
    attn_scale, _, q_scale, k_scale = gains
    w_qkv, w_out = weights[:2]
    allowed, cos_table, sine_table = slot
    trees, row_count, depth = hidden_in.shape
    q_width = w_out.shape[0]
    normed = rms_scale(hidden_in.astype(F32), attn_scale).astype(BF16).reshape(-1, depth)
    qkv = dot(normed, w_qkv).reshape(trees, row_count, -1)
    q_pre = qkv[:, :, :q_width].reshape(trees, row_count, -1, HD)
    k_pre = qkv[:, :, q_width : q_width + HD]
    value_bf = qkv[:, :, q_width + HD :].astype(BF16)
    queries, keys_rot = embed(q_pre, k_pre, q_scale, k_scale, cos_table, sine_table)
    query_bf = queries.astype(BF16)
    kv_all = gather(jnp.concatenate([keys_rot.astype(BF16), value_bf], axis=2))
    key_all = kv_all[:, :, :HD]
    value_all = kv_all[:, :, HD:]
    scores = masked_scores(query_bf, key_all, allowed)
    row_max = jnp.max(scores, axis=-1, keepdims=True)
    exp_scores = jnp.exp(scores - row_max)
    row_total = jnp.sum(exp_scores, axis=-1, keepdims=True)
    prob_bf = (exp_scores / row_total).astype(BF16)
    log_total = row_max + jnp.log(row_total)
    attended = jnp.einsum("bgrt,btd->brgd", prob_bf, value_all, preferred_element_type=F32)
    attended_bf = attended.reshape(trees * row_count, -1).astype(BF16)
    terms = dot(attended_bf, w_out).astype(BF16).reshape(trees, row_count, depth)
    saved = (normed, q_pre, k_pre, query_bf, key_all, value_all, log_total, attended_bf)
    return (terms, saved)


def attn_backward(grad_attn, saved, weights, gains, slot, scatter):
    _, _, q_scale, k_scale = gains
    w_qkv, w_out = weights[:2]
    allowed, cos_table, sine_table = slot
    normed, q_pre, k_pre, query_bf, key_all, value_all, log_total, attended_bf = saved
    trees, row_count = query_bf.shape[:2]
    depth = normed.shape[1]
    grad_attn = grad_attn.reshape(-1, depth)
    grad_heads = dot_inner(grad_attn, w_out).astype(BF16).reshape(query_bf.shape)
    scores = masked_scores(query_bf, key_all, allowed)
    prob_full = jnp.exp(scores - log_total)
    grad_prob = jnp.einsum("brgd,btd->bgrt", grad_heads, value_all, preferred_element_type=F32)
    row_dot = jnp.sum(prob_full * grad_prob, axis=-1, keepdims=True)
    grad_scores = (prob_full * (grad_prob - row_dot)).astype(BF16)
    scale_factor = HD ** (-0.5)
    grad_query = (
        jnp.einsum("bgrt,btd->brgd", grad_scores, key_all, preferred_element_type=F32)
        * scale_factor
    )
    grad_key_all = (
        jnp.einsum("bgrt,brgd->btd", grad_scores, query_bf, preferred_element_type=F32)
        * scale_factor
    )
    grad_value_all = jnp.einsum(
        "bgrt,brgd->btd", prob_full.astype(BF16), grad_heads, preferred_element_type=F32
    )
    grad_kv = scatter(jnp.concatenate([grad_key_all, grad_value_all], axis=2).astype(BF16))
    _, embedding_pull = jax.vjp(
        partial(embed, cos_table=cos_table, sine_table=sine_table), q_pre, k_pre, q_scale, k_scale
    )
    grad_q_pre, grad_k_pre, grad_q_scale, grad_k_scale = embedding_pull(
        (grad_query, grad_kv[:, :, :HD].astype(F32))
    )
    qkv_grad = jnp.concatenate(
        [
            grad_q_pre.astype(BF16).reshape(trees, row_count, -1),
            grad_k_pre.astype(BF16),
            grad_kv[:, :, HD:].astype(BF16),
        ],
        axis=2,
    ).reshape(trees * row_count, -1)
    terms = dot_inner(qkv_grad, w_qkv).astype(BF16).reshape(trees, row_count, depth)
    return (terms, [(normed, qkv_grad), (grad_attn, attended_bf)], [grad_q_scale, grad_k_scale])


def plain_layers(hidden, own_in, grad_own, weights, gains, slot, shared_kv):
    depth = own_in.shape[1]
    own_shape = own_in.shape

    def gather(own):
        return lax.all_gather(own, "dp", axis=1, tiled=True)

    def scatter(whole):
        total = lax.psum_scatter(whole, "dp", scatter_dimension=1, tiled=True)
        if shared_kv:
            total = lax.psum(total, "section")
            total = jnp.where(lax.axis_index("section") == 0, total, jnp.zeros_like(total))
        return total

    outputs, kept = [], []
    for layer in range(2):
        _, _, w_gate, w_up, w_down = weights[layer]
        terms, saved = attn_forward(hidden, weights[layer], gains[layer], slot, gather)
        mlp_scale = gains[layer][1][None]
        middle, mlp_in = hub_plain(
            terms, [own_in, mlp_scale], norm_body, [own_shape], "tensor", ["dp"]
        )
        mlp_in = mlp_in.reshape(-1, depth)
        gate, up = dot_inner(mlp_in, w_gate), dot_inner(mlp_in, w_up)
        hidden_bf = swiglu(gate, up).astype(BF16)
        terms = dot(hidden_bf, w_down).astype(BF16).reshape(2, -1, depth)
        kept.append((own_in, saved, middle, mlp_in, gate, up, hidden_bf))
        own_in, hidden = hub_plain(terms, [middle], add_body, [own_shape], "dp", ["tensor"])
        own_in = own_in.astype(BF16).astype(F32)
        outputs.append(hidden)

    own_outs = [own_shape, (1, depth)]
    grads, products, gain_grads = [None, None], [None, None], [None, None]
    (grad_mlp,) = hub_plain(None, [grad_own], lambda total, args, outs: args[0], [], None, ["dp"])
    for layer in (1, 0):
        _, _, w_gate, w_up, w_down = weights[layer]
        own_in, saved, middle, mlp_in, gate, up, hidden_bf = kept[layer]
        grad_mlp = grad_mlp.reshape(-1, depth)
        _, pull = jax.vjp(swiglu, gate, up)
        grad_gate, grad_up = (item.astype(BF16) for item in pull(dot_inner(grad_mlp, w_down)))
        terms = (dot(grad_gate, w_gate) + dot(grad_up, w_up)).astype(BF16).reshape(2, -1, depth)
        grad_middle, mlp_gain_grad, grad_attn = hub_plain(
            terms, [middle, gains[layer][1][None], grad_own], norm_back_body, own_outs, "dp",
            ["tensor"],
        )
        terms, pairs, head_grads = attn_backward(
            grad_attn, saved, weights[layer], gains[layer], slot, scatter
        )
        grad_own, gain_grad, grads[layer], grad_next = hub_plain(
            terms, [own_in, gains[layer][0][None], grad_middle], norm_back_body, own_outs, "tensor",
            ["tensor", "dp"],
        )
        grad_own = grad_own.astype(BF16).astype(F32)
        pairs += [(grad_gate, mlp_in), (grad_up, mlp_in), (hidden_bf, grad_mlp)]
        products[layer] = pairs
        gain_grads[layer] = jnp.concatenate([gain_grad[0], mlp_gain_grad[0], *head_grads])
        grad_mlp = grad_next
    return (outputs, grads, products, gain_grads)


def swap_cores(mine, other):
    core = lax.axis_index("section")
    arrived = lax.ppermute(other, "section", [(0, 1), (1, 0)])
    return (jnp.where(core == 0, mine, arrived), jnp.where(core == 0, arrived, mine))


def on_device(
    inputs, cotangent, seg_ids, parents, order, attn_gain, w_query, w_key, w_value, w_out,
    q_gain, k_gain, mlp_gain, w_gate, w_up, w_down,
):
    core = lax.axis_index("section")
    data_index = lax.axis_index("dp")
    tensor_index = lax.axis_index("tensor")
    dp_size = lax.axis_size("dp")
    tensor_size = lax.axis_size("tensor")
    trees, row_count, depth = inputs.shape
    own_rows = row_count // tensor_size
    row_start = data_index * row_count
    own_depth = w_query.shape[1]
    q_width = w_query.shape[2] // 2
    shared_kv = w_key.shape[2] == HD
    k_width = HD if shared_kv else w_key.shape[2] // 2
    own_units = w_gate.shape[2]
    share = own_units // (2 * dp_size)

    def pick(stacked, index):
        return lax.dynamic_index_in_dim(stacked, index, 0, keepdims=False)

    fast = (
        own_rows % 8 == 0
        and depth % (2 * CHUNK) == 0
        and row_count % 16 == 0
        and share % 16 == 0
        and own_depth % 128 == 0
        and not shared_kv
    )

    def halves(width, array):
        return [array[:, :width], array[:, array.shape[1] - width :]]

    unit_mats = [w_gate[0].T, w_up[0].T, w_down[0]]
    qkv_width = q_width + 2 * k_width
    gains_own = jnp.concatenate([attn_gain[0], mlp_gain[0], q_gain[0], k_gain[0]]).astype(F32)

    def spread_units(rows):
        return lax.all_gather(rows, "tensor", axis=0, tiled=True)

    def tied(value, *before):
        return lax.optimization_barrier((value, *before))[0]

    if fast:
        line = ["section", "dp"]
        everyone = ["section", "dp", "tensor"]
        (gate_rows, up_rows), (gains_all,) = fused(
            [UnitsOut(unit_mats[:2], 0), SharedRows(gains_own.reshape(-1, 128))], line, True, 1, 45
        )
        shards = AttnShards(w_query[0], w_key[0], w_value[0], w_out[0])
        shards.arrays[0] = tied(shards.arrays[0], gate_rows)
        (w_qkv, w_heads), (down_rows,), (attn_shard,) = fused(
            [AttnOut(shards, 0), UnitsOut(unit_mats[2:], 0), HalfOver(shards)], line, True, 2, 80
        )
        first_weights = [w_qkv, w_heads, spread_units(gate_rows), spread_units(up_rows)]
        attn_next = lax.all_gather(attn_shard, "dp", axis=0)
    else:
        gains_all = lax.all_gather(gains_own, ("section", "dp"))
        attn_halves = jnp.stack(
            [
                jnp.concatenate(parts, axis=1)
                for parts in zip(
                    halves(q_width, w_query[0]),
                    halves(k_width, w_key[0]),
                    halves(k_width, w_value[0]),
                    halves(q_width, w_out[0].T),
                )
            ]
        )
        attn_shards = swap_cores(pick(attn_halves, core), pick(attn_halves, 1 - core))
        unit_blocks = jnp.stack(unit_mats).reshape(3, 2, dp_size, share, own_depth)
        unit_blocks = unit_blocks.transpose(1, 2, 0, 3, 4)
        unit_shards = swap_cores(pick(unit_blocks, core), pick(unit_blocks, 1 - core))
        both_weights = []
        for layer in range(2):
            attn_all = lax.all_gather(attn_shards[layer], "dp", axis=0, tiled=True)
            pieces = exchange(unit_shards[layer], "dp")
            pieces = pieces.transpose(1, 2, 0, 3).reshape(3, share, depth)
            both_weights.append(
                (
                    attn_all[:, :qkv_width], attn_all[:, qkv_width:].T,
                    *(spread_units(pieces[i]) for i in range(3)),
                )
            )

    gains_all = gains_all.reshape(2, dp_size, -1)
    gains = [
        (
            gains_all[layer, :, :own_depth].reshape(depth),
            gains_all[layer, :, own_depth : 2 * own_depth].reshape(depth),
            gains_all[layer, 0, 2 * own_depth : 2 * own_depth + HD],
            gains_all[layer, 0, 2 * own_depth + HD :],
        )
        for layer in range(2)
    ]

    def slot_setup(slot_index):
        tree_id = pick(order, slot_index)
        allowed, row_positions = path_mask(
            pick(seg_ids, tree_id), pick(parents, tree_id), row_start, row_count
        )
        cos_table, sine_table = rope_tables(row_positions, HD)
        return (pick(inputs, tree_id), allowed, cos_table[:, 0], sine_table[:, 0])

    setups = [slot_setup(i) for i in range(trees)]
    hidden, *slot = (jnp.stack(item) for item in zip(*setups))

    def own_part(whole):
        return lax.dynamic_slice_in_dim(
            pick(whole, core), tensor_index * own_rows, own_rows, 0
        )

    own_in = own_part(hidden).astype(F32)
    grad_own = own_part(cotangent).astype(F32)

    def weight_products(pairs):
        return [dot_outer(left, right).astype(BF16) for left, right in pairs]

    def scatter_units(products):
        return [
            lax.psum_scatter(item, "tensor", scatter_dimension=0, tiled=True) for item in products
        ]

    def scatter_shards(products):
        return lax.psum_scatter(
            jnp.concatenate(products, axis=1), "dp", scatter_dimension=0, tiled=True
        )

    if fast:
        def units_on(*which):
            return [UnitsOut([unit_mats[i] for i in which], 1)]

        def kv_gather(own, cargo, collective_id, carried):
            (whole,), outs = with_cargo(GatherKV(own), cargo, everyone, collective_id, 40)
            carried += outs
            return whole.reshape(trees, -1, 2 * HD)

        def kv_scatter(whole, cargo, collective_id, carried):
            part = ScatterKV(whole.reshape(trees, dp_size, row_count, 2 * HD))
            (total,), outs = with_cargo(part, cargo, line, collective_id, 30)
            carried += outs
            return total

        def flat(array):
            return array.reshape(-1, array.shape[-1])

        carried = []
        terms, saved_first = attn_forward(
            hidden, first_weights, gains[0], slot,
            lambda own: kv_gather(
                tied(own, *first_weights[2:]), [UnitsSpread(down_rows)] + units_on(0), 3, carried
            ),
        )
        (down_all,), (gate_rows,) = carried
        first_weights.append(down_all)
        part = FeedForward(
            terms, own_in, gains[0][1][None], first_weights[2:], True, False, {}
        )
        outs, ((up_rows, down_rows),) = with_cargo(part, units_on(1, 2), everyone, 4, 90, 56)
        middle_first, mlp_in_first, hidden_first, own_next, output_first, gate_first, up_first = outs
        second_weights = [
            attn_next[:, :own_depth].reshape(depth, -1),
            attn_next[:, own_depth:].transpose(1, 0, 2).reshape(q_width, depth),
            spread_units(gate_rows), spread_units(up_rows),
        ]
        carried = []
        terms, saved_second = attn_forward(
            output_first, second_weights, gains[1], slot,
            lambda own: kv_gather(
                tied(own, second_weights[2]), [UnitsSpread(down_rows)], 5, carried
            ),
        )
        ((down_all,),) = carried
        second_weights.append(down_all)
        part = FeedForward(
            terms, own_next, gains[1][1][None], second_weights[2:], True, True,
            {"grad_own": grad_own},
        )
        outs, _ = with_cargo(part, [], everyone, 6, 100, 60)
        (
            middle, mlp_in, hidden_bf, _, output_second, grad_mlp,
            grad_gate, grad_up, grad_middle, mlp_gain_second, grad_attn,
        ) = outs
        products_second = weight_products(
            [
                (flat(grad_gate), flat(mlp_in)),
                (flat(grad_up), flat(mlp_in)),
                (flat(hidden_bf), flat(grad_mlp)),
            ]
        )
        unit_second = scatter_units(products_second)
        terms, pairs, head_second = attn_backward(
            grad_attn, saved_second, second_weights, gains[1], slot,
            lambda whole: kv_scatter(tied(whole, *products_second), [], 7, []),
        )
        attn_second = scatter_shards(weight_products(pairs))
        terms = tied(terms, unit_second[0])
        part = FeedForward(
            terms, own_next, gains[1][0][None], first_weights[2:], False, True,
            {
                "add": grad_middle, "gate": gate_first, "up": up_first,
                "middle_in": middle_first, "mlp_gain": gains[0][1][None],
            },
        )
        outs, _ = with_cargo(part, [], everyone, 8, 90, 60)
        (
            grad_gate, grad_up, grad_middle, mlp_gain_first, grad_attn,
            attn_gain_second, incoming_second, grad_mlp,
        ) = outs
        products = weight_products(
            [
                (flat(grad_gate), flat(mlp_in_first)),
                (flat(grad_up), flat(mlp_in_first)),
                (flat(hidden_first), flat(grad_mlp)),
            ]
        )
        grad_attn = tied(grad_attn, unit_second[1], *products)
        unit_first = scatter_units(products[:2])
        unit_first += scatter_units([tied(products[2], *unit_first)])
        carried = []
        terms, pairs, head_first = attn_backward(
            grad_attn, saved_first, first_weights, gains[0], slot,
            lambda whole: kv_scatter(
                tied(whole, attn_second), [UnitsHome(unit_second, 1)], 9, carried
            ),
        )
        (home_second,) = carried
        whole = jnp.concatenate(weight_products(pairs), axis=1).reshape(dp_size, 4, -1, q_width + qkv_width)
        part = LastHub(terms, own_in, gains[0][0][None], grad_middle)
        (attn_gain_first, incoming_first), ((attn_first,), home_first) = with_cargo(
            part, [ScatterKV(whole.transpose(1, 0, 2, 3)), UnitsHome(unit_first[:2], 0)], everyone,
            10, 60, 56,
        )
        attn_first = attn_first.reshape(own_depth, -1).astype(BF16)
        outputs = [output_first, output_second]
        grads = [incoming_first, incoming_second]
        weight_grads = [(attn_first, None), (attn_second, None)]
        gain_grads = [
            jnp.concatenate([attn_gain_first[0], mlp_gain_first[0], *head_first]),
            jnp.concatenate([attn_gain_second[0], mlp_gain_second[0], *head_second]),
        ]
    else:
        outputs, grads, products, gain_grads = plain_layers(
            hidden, own_in, grad_own, both_weights, gains, slot, shared_kv
        )
        weight_grads = []
        for pairs in products:
            whole = weight_products(pairs)
            weight_grads.append((scatter_shards(whole[:2]), scatter_units(whole[2:])))

    gain_total = jnp.stack(gain_grads)
    if fast:
        mine = jnp.where(core == 0, weight_grads[0][0], weight_grads[1][0])
        other = jnp.where(core == 0, weight_grads[1][0], weight_grads[0][0])
        (gain_total,), (arrived,), down_home = fused(
            [TotalOverAll(gain_total.reshape(-1, 128)), Swap(other), UnitsHome(unit_first[2:], 0)],
            everyone, True, 11, 60,
        )
        attn_home = (jnp.where(core == 0, mine, arrived), jnp.where(core == 0, arrived, mine))
        unit_home = [
            jnp.where(core == 0, first, second) for first, second in zip(home_first + down_home, home_second)
        ]
        gain_total = gain_total.reshape(2, -1)
    else:
        def bring_home(first, second):
            mine, other = jnp.where(core == 0, first, second), jnp.where(core == 0, second, first)
            arrived = lax.ppermute(other, "section", [(0, 1), (1, 0)])
            return (jnp.where(core == 0, mine, arrived), jnp.where(core == 0, arrived, mine))

        def pieces_of(grad):
            return exchange(
                jnp.stack(grad).reshape(3, share, dp_size, own_depth).transpose(2, 0, 1, 3), "dp"
            )

        attn_home = bring_home(weight_grads[0][0], weight_grads[1][0])
        unit_home = jnp.stack(bring_home(pieces_of(weight_grads[0][1]), pieces_of(weight_grads[1][1])))
        unit_home = unit_home.transpose(2, 0, 1, 3, 4).reshape(3, own_units, own_depth)
        gain_total = lax.psum(gain_total, ("section", "dp", "tensor"))

    def joined(start, width):
        parts = [half[:, start : start + width] for half in attn_home]
        if shared_kv and start in (q_width, q_width + k_width):
            return parts[0].astype(F32)
        return jnp.concatenate(parts, axis=1).astype(F32)

    gain_own = pick(gain_total, core)
    share_width = attn_gain.shape[1]
    attn_gain_grad = lax.dynamic_slice_in_dim(gain_own, data_index * share_width, share_width, 0)
    mlp_gain_grad = lax.dynamic_slice_in_dim(
        gain_own, depth + data_index * share_width, share_width, 0
    )
    return (
        jnp.where(core == 0, outputs[0], outputs[1])[None],
        jnp.where(core == 0, grads[0], grads[1])[None],
        attn_gain_grad[None],
        joined(0, q_width)[None],
        joined(q_width, k_width)[None],
        joined(q_width + k_width, k_width)[None],
        joined(qkv_width, q_width).T[None],
        gain_own[2 * depth : 2 * depth + HD][None],
        gain_own[2 * depth + HD :][None],
        mlp_gain_grad[None],
        unit_home[0].T.astype(F32)[None],
        unit_home[1].T.astype(F32)[None],
        unit_home[2].astype(F32)[None],
    )


def solution(mesh):
    rows = P(None, "dp", None)
    wide = P("section", "dp", "tensor")
    tall = P("section", "tensor", "dp")
    gain = P("section", "dp")
    head_gain = P("section", None)
    slots = P("section", None, "dp", None)
    in_specs = (
        rows, rows, P(), P(), P(), gain, wide, wide, wide, tall, head_gain, head_gain, gain,
        wide, wide, tall,
    )
    out_specs = (
        slots, slots, gain, wide, wide, wide, tall, head_gain, head_gain, gain, wide, wide, tall,
    )
    return jax.shard_map(
        on_device, mesh=mesh, in_specs=in_specs, out_specs=out_specs, check_vma=False
    )
```

```python
from functools import partial

import jax
import jax.numpy as jnp
from jax import lax
from jax.experimental import pallas as pl
from jax.experimental.pallas import tpu as pltpu
from jax.sharding import PartitionSpec as P

HD = 128
TRUNK = 512
BRANCH = 96
NB = 4
TREE = 1152
SEGS = 9


EPSILON = 1e-06
THETA = 1000000.0
MASKED = -1e30
F32 = jnp.float32
BF16 = jnp.bfloat16


def rms_scale(values, weight_gain):
    mean_sq = jnp.mean(values * values, axis=-1, keepdims=True)
    return values * lax.rsqrt(mean_sq + EPSILON) * weight_gain


def rotate(values, cos_table, sine_table):
    middle_at = values.shape[-1] // 2
    leading = values[..., :middle_at]
    trailing = values[..., middle_at:]
    return jnp.concatenate(
        [leading * cos_table - trailing * sine_table, trailing * cos_table + leading * sine_table],
        axis=-1,
    )


def rope_tables(positions, head_dim):
    half_steps = jnp.arange(head_dim // 2, dtype=F32)
    inverse = THETA ** (-2.0 * half_steps / head_dim)
    angles = positions.astype(F32)[:, None] * inverse[None, :]
    return (jnp.cos(angles)[:, None, :], jnp.sin(angles)[:, None, :])


def swiglu(gate_in, up_in):
    return jax.nn.silu(gate_in) * up_in


def embed_heads(q_pre, k_pre, q_scale, k_scale, cos_table, sine_table):
    row_count = q_pre.shape[0]
    queries = rms_scale(q_pre.reshape(row_count, -1, HD), q_scale)
    keys_part = rms_scale(k_pre.reshape(row_count, -1, HD), k_scale)
    return (rotate(queries, cos_table, sine_table), rotate(keys_part, cos_table, sine_table))


def tree_layout(seg_row, parent_row):
    labels = jnp.arange(SEGS, dtype=jnp.int32)
    places = jnp.arange(TREE, dtype=jnp.int32)
    member = seg_row[None, :] == labels[:, None]
    starts = jnp.min(jnp.where(member, places[None, :], TREE), axis=1)
    depth_base = jnp.where(labels == 0, 0, jnp.where(labels <= NB, TRUNK, TRUNK + BRANCH))
    shifts = depth_base - starts
    positions = places + jnp.sum(jnp.where(member, shifts[:, None], 0), axis=0)
    grandparent = jnp.sum(
        jnp.where(parent_row[:, None] == labels[None, :], parent_row[None, :], 0), axis=1
    )
    ancestor = (
        (labels[None, :] == labels[:, None])
        | (labels[None, :] == parent_row[:, None])
        | (labels[None, :] == grandparent[:, None])
    )
    return (positions, member.astype(F32), ancestor.astype(F32))


def path_mask(seg_row, parent_row, row_start, row_count):
    positions, member, ancestor = tree_layout(seg_row, parent_row)
    member_rows = lax.dynamic_slice_in_dim(member, row_start, row_count, 1)
    seg_rows = lax.dynamic_slice_in_dim(seg_row, row_start, row_count, 0)
    reach_table = jnp.dot(jnp.dot(member_rows.T, ancestor), member)
    places = jnp.arange(TREE, dtype=jnp.int32)
    row_places = row_start + jnp.arange(row_count, dtype=jnp.int32)
    same_seg = seg_rows[:, None] == seg_row[None, :]
    causal = places[None, :] <= row_places[:, None]
    allowed = (reach_table > 0.5) & (jnp.logical_not(same_seg) | causal)
    row_positions = lax.dynamic_slice_in_dim(positions, row_start, row_count, 0)
    return (allowed, row_positions)


OUTER = (((0,), (0,)), ((), ()))
INNER = (((1,), (1,)), ((), ()))


def dot(left, right):
    return jnp.dot(left, right, preferred_element_type=F32)


def dot_inner(left, right):
    return lax.dot_general(left, right, INNER, preferred_element_type=F32)


def dot_outer(left, right):
    return lax.dot_general(left, right, OUTER, preferred_element_type=F32)


def exchange(pieces, axis):
    size = lax.axis_size(axis)
    me = lax.axis_index(axis)
    got = jnp.zeros_like(pieces)
    own = lax.dynamic_index_in_dim(pieces, me, 0, keepdims=True)
    got = lax.dynamic_update_slice_in_dim(got, own, me, 0)
    for step in range(1, size):
        other = me ^ step
        piece = lax.dynamic_index_in_dim(pieces, other, 0, keepdims=True)
        arrived = lax.ppermute(piece, axis, [(i, i ^ step) for i in range(size)])
        got = lax.dynamic_update_slice_in_dim(got, arrived, other, 0)
    return got


def masked_scores(query_bf, key_all, allowed):
    raw_scores = jnp.einsum(
        "brgd,btd->bgrt", query_bf, key_all, preferred_element_type=F32
    ) * HD ** (-0.5)
    return jnp.where(allowed[:, None], raw_scores, MASKED)


MESH = pl.DeviceIdType.MESH
CHUNK = 256
SEM = pltpu.SemaphoreType.DMA
VMEM = pl.BlockSpec(memory_space=pltpu.VMEM)
HBM = pl.BlockSpec(memory_space=pl.ANY)


def remote(src, dst, send_sem, recv_sem, device_id):
    return pltpu.make_async_remote_copy(
        src_ref=src, dst_ref=dst, send_sem=send_sem, recv_sem=recv_sem,
        device_id=device_id, device_id_type=MESH,
    )


def greet(axes, across):
    barrier = pltpu.get_barrier_semaphore()
    count = 0
    for axis in axes:
        size = lax.axis_size(axis)
        me = lax.axis_index(axis)
        for step in range(1, size):
            pl.semaphore_signal(
                barrier, inc=1, device_id={axis: lax.rem(me + step, size)}, device_id_type=MESH
            )
        count += size - 1
    if across:
        size = lax.axis_size("dp")
        me = lax.axis_index("dp")
        sibling = 1 - lax.axis_index("section")
        for step in range(1, size):
            pl.semaphore_signal(
                barrier, inc=1, device_id={"section": sibling, "dp": lax.rem(me + step, size)},
                device_id_type=MESH,
            )
        count += size - 1
    pl.semaphore_wait(barrier, count)


class Part:
    ins, outs, scratch = (), (), ()

    def bind(self, ins, outs, scratch):
        self.in_refs, self.out_refs, self.refs = ins, outs, scratch

    def prepare(self):
        pass

    def start(self):
        pass

    def run(self):
        pass

    def finish(self):
        pass


def fused(parts, axes, across, collective_id, cost_us, vmem=40):
    counts = [(len(part.ins), len(part.outs), len(part.scratch)) for part in parts]

    def kernel(*refs):
        refs = list(refs)
        groups = []
        for kind in range(3):
            groups.append([])
            for count in counts:
                groups[kind].append(refs[: count[kind]])
                del refs[: count[kind]]
        for part, ins, outs, scratch in zip(parts, *groups):
            part.bind(ins, outs, scratch)
        for part in parts:
            part.prepare()
        greet(axes, across)
        for part in parts:
            part.start()
        for part in reversed(parts):
            part.run()
        for part in parts:
            part.finish()

    ins = [item for part in parts for item in part.ins]
    outs = [item for part in parts for item in part.outs]
    results = pl.pallas_call(
        kernel,
        out_shape=[item[0] for item in outs],
        in_specs=[item[1] for item in ins],
        out_specs=[item[1] for item in outs],
        scratch_shapes=[item for part in parts for item in part.scratch],
        cost_estimate=pl.CostEstimate(
            flops=0, bytes_accessed=cost_us * 3_000_000, transcendentals=0
        ),
        compiler_params=pltpu.CompilerParams(
            collective_id=collective_id, has_side_effects=True, vmem_limit_bytes=vmem << 20
        ),
    )(*[item[0] for item in ins])
    results = list(results)
    split = []
    for count in counts:
        split.append(results[: count[1]])
        del results[: count[1]]
    return split


def columns_of(place, width):
    return pl.ds(pl.multiple_of(place * width, width), width)


class UnitsOut(Part):
    def __init__(self, mats, layer):
        self.layer, self.count = layer, len(mats)
        self.size = lax.axis_size("dp")
        rows, self.width = mats[0].shape
        self.share = rows // (2 * self.size)
        self.ins = [(mat, HBM) for mat in mats]
        shape = jax.ShapeDtypeStruct((self.share, self.size * self.width), BF16)
        self.outs = [(shape, HBM)] * self.count
        self.scratch = [SEM((self.count,)), SEM((self.count, 2, self.size)), SEM((self.count, self.size))]

    def bind(self, ins, outs, scratch):
        self.src, self.dst = ins, outs
        self.keep, self.send, self.recv = scratch
        self.core, self.me = lax.axis_index("section"), lax.axis_index("dp")

    def piece(self, index, core, place):
        start = pl.multiple_of((core * self.size + place) * self.share, self.share)
        return self.src[index].at[pl.ds(start, self.share)]

    def lands(self, index, slot):
        return self.dst[index].at[:, columns_of(slot, self.width)]

    def copy(self, index, core, place, slot):
        return remote(
            self.piece(index, core, place), self.lands(index, slot),
            self.send.at[index, core, place], self.recv.at[index, slot],
            {"section": core, "dp": place},
        )

    def local(self, index):
        return pltpu.make_async_copy(
            self.piece(index, self.layer, self.me), self.lands(index, self.me), self.keep.at[index]
        )

    def targets(self):
        for index in range(self.count):
            for core in range(2):
                for place in range(self.size):
                    yield index, core, place, (place != self.me) | (core != self.layer)

    def start(self):
        @pl.when(self.core == self.layer)
        def _():
            for index, core, place, is_other in self.targets():
                @pl.when(is_other)
                def _():
                    self.copy(index, core, place, self.me).start()

            for index in range(self.count):
                self.local(index).start()

    def finish(self):
        for index in range(self.count):
            for place in range(self.size):
                @pl.when((self.core != self.layer) | (place != self.me))
                def _():
                    self.copy(index, 0, 0, place).wait_recv()

        @pl.when(self.core == self.layer)
        def _():
            for index, core, place, is_other in self.targets():
                @pl.when(is_other)
                def _():
                    self.copy(index, core, place, self.me).wait_send()

            for index in range(self.count):
                self.local(index).wait()


class UnitsHome(Part):
    def __init__(self, mats, layer):
        self.layer, self.count = layer, len(mats)
        self.size = lax.axis_size("dp")
        self.share, depth = mats[0].shape
        self.width = depth // self.size
        self.ins = [(mat, HBM) for mat in mats]
        shape = jax.ShapeDtypeStruct((2 * self.size * self.share, self.width), BF16)
        self.outs = [(shape, HBM)] * self.count
        self.scratch = [SEM((self.count,)), SEM((self.count, self.size)), SEM((self.count, 2, self.size))]

    def bind(self, ins, outs, scratch):
        self.src, self.dst = ins, outs
        self.keep, self.send, self.recv = scratch
        self.core, self.me = lax.axis_index("section"), lax.axis_index("dp")

    def lands(self, index, core, slot):
        start = pl.multiple_of((core * self.size + slot) * self.share, self.share)
        return self.dst[index].at[pl.ds(start, self.share)]

    def copy(self, index, place, core, slot):
        return remote(
            self.src[index].at[:, columns_of(place, self.width)], self.lands(index, core, slot),
            self.send.at[index, place], self.recv.at[index, core, slot],
            {"section": self.layer, "dp": place},
        )

    def local(self, index):
        return pltpu.make_async_copy(
            self.src[index].at[:, columns_of(self.me, self.width)],
            self.lands(index, self.layer, self.me), self.keep.at[index],
        )

    def start(self):
        for index in range(self.count):
            for place in range(self.size):
                @pl.when((self.core != self.layer) | (place != self.me))
                def _():
                    self.copy(index, place, self.core, self.me).start()

            @pl.when(self.core == self.layer)
            def _():
                self.local(index).start()

    def finish(self):
        for index in range(self.count):
            @pl.when(self.core == self.layer)
            def _():
                for core in range(2):
                    for place in range(self.size):
                        @pl.when((core != self.layer) | (place != self.me))
                        def _():
                            self.copy(index, 0, core, place).wait_recv()

                self.local(index).wait()

            for place in range(self.size):
                @pl.when((self.core != self.layer) | (place != self.me))
                def _():
                    self.copy(index, place, self.core, self.me).wait_send()


class UnitsSpread(Part):
    def __init__(self, rows):
        self.size = lax.axis_size("tensor")
        self.share, depth = rows.shape
        self.ins = [(rows, HBM)]
        self.outs = [(jax.ShapeDtypeStruct((self.size * self.share, depth), BF16), HBM)]
        self.scratch = [SEM, SEM((self.size,)), SEM((self.size,))]

    def bind(self, ins, outs, scratch):
        (self.src,), (self.dst,), (self.keep, self.send, self.recv) = ins, outs, scratch
        self.me = lax.axis_index("tensor")

    def lands(self, slot):
        return self.dst.at[pl.ds(pl.multiple_of(slot * self.share, self.share), self.share)]

    def copy(self, place, slot):
        return remote(
            self.src, self.lands(slot), self.send.at[place], self.recv.at[slot], {"tensor": place}
        )

    def start(self):
        for place in range(self.size):
            @pl.when(place != self.me)
            def _():
                self.copy(place, self.me).start()

        pltpu.make_async_copy(self.src, self.lands(self.me), self.keep).start()

    def finish(self):
        for place in range(self.size):
            @pl.when(place != self.me)
            def _():
                self.copy(place, place).wait_recv()
                self.copy(place, self.me).wait_send()

        pltpu.make_async_copy(self.src, self.lands(self.me), self.keep).wait()


class SharedRows(Part):
    def __init__(self, own):
        self.size = lax.axis_size("dp")
        self.ins = [(own, VMEM)]
        self.outs = [(jax.ShapeDtypeStruct((2, self.size) + own.shape, F32), VMEM)]
        self.scratch = [SEM((2, self.size)), SEM((2, self.size))]

    def copy(self, core, place, from_core, from_place):
        return remote(
            self.in_refs[0], self.out_refs[0].at[from_core, from_place],
            self.refs[0].at[core, place], self.refs[1].at[from_core, from_place],
            {"section": core, "dp": place},
        )

    def others(self):
        core, me = lax.axis_index("section"), lax.axis_index("dp")
        for other in range(2):
            for place in range(self.size):
                yield other, place, (other != core) | (place != me)

    def start(self):
        core, me = lax.axis_index("section"), lax.axis_index("dp")
        for other, place, is_other in self.others():
            @pl.when(is_other)
            def _():
                self.copy(other, place, core, me).start()

        self.out_refs[0][core, me] = self.in_refs[0][...]

    def finish(self):
        core, me = lax.axis_index("section"), lax.axis_index("dp")
        for other, place, is_other in self.others():
            @pl.when(is_other)
            def _():
                self.copy(other, place, other, place).wait_recv()
                self.copy(other, place, core, me).wait_send()


def far_pair(place, me):
    return (place + me == 3) & ((place == 0) | (place == 3))


def line_relays(size):
    return [(2, 0, 3), (1, 3, 0)] if size == 4 else []


def line_order(size):
    return [1, 2, 0, 3] if size == 4 else list(range(size))


class AttnShards:
    def __init__(self, w_query, w_key, w_value, w_out):
        self.arrays = [w_query, w_key, w_value, w_out]
        self.depth = w_query.shape[0]
        self.q_width, self.k_width = w_query.shape[1] // 2, w_key.shape[1] // 2
        self.width = self.q_width + 2 * self.k_width
        half = self.depth // 2
        parts = self.q_width // 2
        self.items = [
            (0, lambda ref, core: ref.at[pl.ds(0, half), columns_of(core, self.q_width)]),
            (0, lambda ref, core: ref.at[pl.ds(half, half), columns_of(core, self.q_width)]),
            (1, lambda ref, core: ref.at[:, columns_of(core, self.k_width)]),
            (2, lambda ref, core: ref.at[:, columns_of(core, self.k_width)]),
            (3, lambda ref, core: ref.at[pl.ds(core * self.q_width, parts)]),
            (3, lambda ref, core: ref.at[pl.ds(core * self.q_width + parts, parts)]),
        ]
        q_width, k_width, depth = self.q_width, self.k_width, self.depth
        self.qkv_rows = [(0, half), (half, half), (0, depth), (0, depth)]
        self.qkv_columns = [
            (0, q_width), (0, q_width), (q_width, k_width), (q_width + k_width, k_width)
        ]
        self.out_rows = [(0, parts), (parts, parts)]

    def source(self, refs, index, core):
        array, cut = self.items[index]
        return cut(refs[array], core)

    def lands(self, qkv, out, index, slot):
        if index < 4:
            (start, rows), (left, columns) = self.qkv_rows[index], self.qkv_columns[index]
            at = pl.multiple_of(slot * self.depth + start, rows)
            return qkv.at[pl.ds(at, rows), pl.ds(left, columns)]
        start, rows = self.out_rows[index - 4]
        return out.at[pl.ds(start, rows), columns_of(slot, self.depth)]


class AttnOut(Part):
    def __init__(self, shards, layer):
        self.layer, self.shards = layer, shards
        self.size = lax.axis_size("dp")
        self.count = len(shards.items)
        depth = self.size * shards.depth
        self.ins = [(array, HBM) for array in shards.arrays]
        self.outs = [
            (jax.ShapeDtypeStruct((depth, shards.width), BF16), HBM),
            (jax.ShapeDtypeStruct((shards.q_width, depth), BF16), HBM),
        ]
        self.scratch = [
            SEM((self.count,)), SEM((2, self.size, self.count)), SEM((self.size, self.count)),
            SEM((self.count,)),
        ]

    def bind(self, ins, outs, scratch):
        self.src = ins
        self.qkv, self.out = outs
        self.keep, self.send, self.recv, self.relay_send = scratch
        self.core, self.me = lax.axis_index("section"), lax.axis_index("dp")

    def lands(self, index, slot):
        return self.shards.lands(self.qkv, self.out, index, slot)

    def copy(self, core, place, slot, index):
        return remote(
            self.shards.source(self.src, index, core), self.lands(index, slot),
            self.send.at[core, place, index], self.recv.at[slot, index],
            {"section": core, "dp": place},
        )

    def relay(self, source, target, index):
        block = self.lands(index, source)
        return remote(
            block, block, self.relay_send.at[index], self.recv.at[source, index], {"dp": target}
        )

    def local(self, index):
        return pltpu.make_async_copy(
            self.shards.source(self.src, index, self.layer), self.lands(index, self.me),
            self.keep.at[index],
        )

    def targets(self):
        for index in range(self.count):
            for core in range(2):
                for place in range(self.size):
                    sent = (place != self.me) | (core != self.layer)
                    if self.size == 4:
                        sent = sent & jnp.logical_not(far_pair(place, self.me))
                    yield core, place, index, sent

    def start(self):
        @pl.when(self.core == self.layer)
        def _():
            for core, place, index, sent in self.targets():
                @pl.when(sent)
                def _():
                    self.copy(core, place, self.me, index).start()

            for index in range(self.count):
                self.local(index).start()

    def run(self):
        for index in range(self.count):
            for place in line_order(self.size):
                @pl.when((self.core != self.layer) | (place != self.me))
                def _():
                    self.copy(0, 0, place, index).wait_recv()

                for via, source, target in line_relays(self.size):
                    if source == place:
                        @pl.when(self.me == via)
                        def _():
                            self.relay(source, target, index).start()

    def finish(self):
        @pl.when(self.core == self.layer)
        def _():
            for core, place, index, sent in self.targets():
                @pl.when(sent)
                def _():
                    self.copy(core, place, self.me, index).wait_send()

            for index in range(self.count):
                self.local(index).wait()

        for via, source, target in line_relays(self.size):
            @pl.when(self.me == via)
            def _():
                for index in range(self.count):
                    self.relay(source, target, index).wait_send()


class HalfOver(Part):
    def __init__(self, shards):
        self.shards = shards
        self.count = len(shards.items)
        rows = shards.depth + shards.q_width
        self.ins = [(array, HBM) for array in shards.arrays]
        self.outs = [(jax.ShapeDtypeStruct((rows, shards.depth), BF16), HBM)]
        self.scratch = [SEM((self.count,)), SEM((self.count,)), SEM((self.count,))]

    def lands(self, index):
        depth, q_width = self.shards.depth, self.shards.q_width
        packed = self.out_refs[0]
        return self.shards.lands(
            packed.at[pl.ds(0, depth)], packed.at[pl.ds(depth, q_width)], index, 0
        )

    def over(self, index):
        return remote(
            self.shards.source(self.in_refs, index, 0), self.lands(index), self.refs[0].at[index],
            self.refs[1].at[index], {"section": 0},
        )

    def keep(self, index):
        return pltpu.make_async_copy(
            self.shards.source(self.in_refs, index, 1), self.lands(index), self.refs[2].at[index]
        )

    def start(self):
        @pl.when(lax.axis_index("section") == 1)
        def _():
            for index in range(self.count):
                self.over(index).start()
                self.keep(index).start()

    def finish(self):
        @pl.when(lax.axis_index("section") == 1)
        def _():
            for index in range(self.count):
                self.over(index).wait_send()
                self.keep(index).wait()

        @pl.when(lax.axis_index("section") == 0)
        def _():
            for index in range(self.count):
                self.over(index).wait_recv()


class Swap(Part):
    def __init__(self, own):
        self.ins = [(own, HBM)]
        self.outs = [(jax.ShapeDtypeStruct(own.shape, own.dtype), HBM)]
        self.scratch = [SEM, SEM]

    def start(self):
        sibling = 1 - lax.axis_index("section")
        self.copy = remote(
            self.in_refs[0], self.out_refs[0], self.refs[0], self.refs[1], {"section": sibling}
        )
        self.copy.start()

    def finish(self):
        self.copy.wait()


class GatherKV(Part):
    def __init__(self, own):
        trees, rows, width = own.shape
        self.trees, self.size = trees, lax.axis_size("dp")
        self.ins = [(own, VMEM)]
        self.outs = [(jax.ShapeDtypeStruct((trees, self.size, rows, width), BF16), VMEM)]
        self.scratch = [SEM((self.size, trees)), SEM((self.size, trees)), SEM((trees,))]

    def bind(self, ins, outs, scratch):
        (self.own,), (self.out,) = ins, outs
        self.send, self.recv, self.relay_send = scratch
        self.me = lax.axis_index("dp")

    def copy(self, place, slot, tree):
        return remote(
            self.own.at[tree], self.out.at[tree, slot], self.send.at[place, tree],
            self.recv.at[slot, tree], {"dp": place},
        )

    def relay(self, source, target, tree):
        return remote(
            self.out.at[tree, source], self.out.at[tree, source], self.relay_send.at[tree],
            self.recv.at[source, tree], {"dp": target},
        )

    def targets(self):
        for tree in range(self.trees):
            for place in range(self.size):
                sent = place != self.me
                if self.size == 4:
                    sent = sent & jnp.logical_not(far_pair(place, self.me))
                yield place, tree, sent

    def start(self):
        for place, tree, sent in self.targets():
            @pl.when(sent)
            def _():
                self.copy(place, self.me, tree).start()

        self.out[:, self.me] = self.own[...]

    def run(self):
        for tree in range(self.trees):
            for place in line_order(self.size):
                @pl.when(place != self.me)
                def _():
                    self.copy(place, place, tree).wait_recv()

                for via, source, target in line_relays(self.size):
                    if source == place:
                        @pl.when(self.me == via)
                        def _():
                            self.relay(source, target, tree).start()

    def finish(self):
        for place, tree, sent in self.targets():
            @pl.when(sent)
            def _():
                self.copy(place, self.me, tree).wait_send()

        for via, source, target in line_relays(self.size):
            @pl.when(self.me == via)
            def _():
                for tree in range(self.trees):
                    self.relay(source, target, tree).wait_send()


class ScatterKV(Part):
    def __init__(self, whole):
        trees, size, rows, width = whole.shape
        self.trees, self.size = trees, size
        self.sides = [(0, 1, 3), (3, 2, 0)] if size == 4 else []
        self.ins = [(whole, VMEM)]
        self.outs = [(jax.ShapeDtypeStruct((trees, rows, width), F32), VMEM)]
        self.scratch = [
            pltpu.VMEM((size, trees, rows, width), BF16), pltpu.VMEM((trees, rows, width), BF16),
            SEM((size, trees)), SEM((size, trees)), SEM((trees,)), SEM((trees,)),
        ]

    def bind(self, ins, outs, scratch):
        (self.terms,), (self.out,) = ins, outs
        self.boxes, self.joint, self.send, self.recv, self.join_send, self.join_recv = scratch
        self.me = lax.axis_index("dp")

    def copy(self, place, slot, tree):
        return remote(
            self.terms.at[tree, place], self.boxes.at[slot, tree], self.send.at[place, tree],
            self.recv.at[slot, tree], {"dp": place},
        )

    def by_way(self, via, target, tree):
        return remote(
            self.terms.at[tree, target], self.joint.at[tree], self.join_send.at[tree],
            self.join_recv.at[tree], {"dp": via},
        )

    def joined(self, via, target, tree):
        return remote(
            self.joint.at[tree], self.boxes.at[via, tree], self.send.at[target, tree],
            self.recv.at[via, tree], {"dp": target},
        )

    def plain(self, place):
        ok = place != self.me
        for source, via, target in self.sides:
            if place == target:
                ok = ok & (self.me != source) & (self.me != via)
        return ok

    def expected(self, place):
        ok = place != self.me
        for source, via, target in self.sides:
            if place == source:
                ok = ok & (self.me != target)
        return ok

    def start(self):
        for tree in range(self.trees):
            for source, via, target in self.sides:
                @pl.when(self.me == source)
                def _():
                    self.by_way(via, target, tree).start()

            for place in range(self.size):
                @pl.when(self.plain(place))
                def _():
                    self.copy(place, self.me, tree).start()

    def run(self):
        for tree in range(self.trees):
            for source, via, target in self.sides:
                @pl.when(self.me == via)
                def _():
                    self.by_way(via, target, tree).wait_recv()
                    both = self.joint[tree].astype(F32) + self.terms[tree, target].astype(F32)
                    self.joint[tree] = both.astype(BF16)
                    self.joined(via, target, tree).start()

        for tree in range(self.trees):
            self.out[tree] = self.terms[tree, self.me].astype(F32)
            for place in line_order(self.size):
                @pl.when(self.expected(place))
                def _():
                    self.copy(place, place, tree).wait_recv()
                    self.out[tree] += self.boxes[place, tree].astype(F32)

    def finish(self):
        for tree in range(self.trees):
            for place in range(self.size):
                @pl.when(self.plain(place))
                def _():
                    self.copy(place, self.me, tree).wait_send()

            for source, via, target in self.sides:
                @pl.when(self.me == source)
                def _():
                    self.by_way(via, target, tree).wait_send()

                @pl.when(self.me == via)
                def _():
                    self.joined(via, target, tree).wait_send()


class TotalOverAll(Part):
    axes = ("section", "tensor", "dp")

    def __init__(self, own):
        sizes = [lax.axis_size(axis) for axis in self.axes]
        self.ins = [(own, VMEM)]
        self.outs = [(jax.ShapeDtypeStruct(own.shape, F32), VMEM)]
        self.scratch = [pltpu.VMEM((size,) + own.shape, F32) for size in sizes]
        self.scratch += [SEM((size,)) for size in sizes] * 2

    def run(self):
        out = self.out_refs[0]
        out[...] = self.in_refs[0][...]
        for axis, box, send, recv in zip(self.axes, self.refs[:3], self.refs[3:6], self.refs[6:9]):
            size, me = lax.axis_size(axis), lax.axis_index(axis)
            box[me] = out[...]

            def spread(place, slot):
                return remote(box.at[me], box.at[slot], send.at[place], recv.at[slot], {axis: place})

            for place in range(size):
                @pl.when(place != me)
                def _():
                    spread(place, me).start()

            for place in range(size):
                @pl.when(place != me)
                def _():
                    spread(place, place).wait_recv()
                    spread(place, me).wait_send()

            total = box[0]
            for place in range(1, size):
                total += box[place]
            out[...] = total


def chunk_count(rows):
    return 3 if rows % 24 == 0 else 1


class Gatherer:
    def __init__(self, axis, rows, half):
        self.axis, self.half = axis, half
        self.size = size = lax.axis_size(axis)
        self.chunks = chunks = chunk_count(rows)
        self.rows = rows // chunks
        self.scratch = [pltpu.VMEM((2, chunks, size, 2 * self.rows, half), BF16)]
        self.scratch += [SEM((chunks, size))] * 4 + [SEM((chunks,))]

    def bind(self, refs):
        self.board, self.send, self.recv, self.sib_send, self.sib_recv, self.relay_send = refs
        self.core = lax.axis_index("section")
        self.sibling = 1 - self.core
        self.me = lax.axis_index(self.axis)
        self.relays = line_relays(self.size) if self.axis == "dp" else []
        self.order = line_order(self.size) if self.axis == "dp" else range(self.size)

    def direct(self, place):
        sent = place != self.me
        if self.relays:
            sent = sent & jnp.logical_not(far_pair(place, self.me))
        return sent

    def spread(self, chunk, place, slot):
        block = self.board.at[self.core, chunk, slot]
        return remote(
            block, block, self.send.at[chunk, place], self.recv.at[chunk, slot], {self.axis: place}
        )

    def passed(self, chunk, source, target):
        block = self.board.at[self.core, chunk, source]
        return remote(
            block, block, self.relay_send.at[chunk], self.recv.at[chunk, source],
            {self.axis: target},
        )

    def over(self, tree, chunk, slot):
        block = self.board.at[tree, chunk, slot]
        return remote(
            block, block, self.sib_send.at[chunk, slot], self.sib_recv.at[chunk, slot],
            {"section": self.sibling},
        )

    def begin(self, chunk, result):
        half = self.half
        piece = jnp.concatenate([result[:, :half], result[:, half:]], axis=0)
        self.board[self.core, chunk, self.me] = piece.astype(BF16)
        for place in range(self.size):
            @pl.when(self.direct(place))
            def _():
                self.spread(chunk, place, self.me).start()

        self.over(self.core, chunk, self.me).start()

    def arrive(self, chunk):
        for place in self.order:
            @pl.when(place != self.me)
            def _():
                self.spread(chunk, place, place).wait_recv()

            for via, source, target in self.relays:
                if source == place:
                    @pl.when(self.me == via)
                    def _():
                        self.passed(chunk, source, target).start()

            @pl.when(place != self.me)
            def _():
                self.over(self.core, chunk, place).start()

    def arrive_over(self, chunk):
        for place in range(self.size):
            self.over(self.sibling, chunk, place).wait_recv()

    def side_rows(self, block, side):
        return block[side * self.rows : (side + 1) * self.rows]

    def unpack(self, out, tree):
        @pl.loop(0, self.half // CHUNK)
        def _(step):
            at = pl.multiple_of(step * CHUNK, CHUNK)
            blocks = [
                self.board[tree, chunk, place, :, pl.ds(at, CHUNK)].astype(F32)
                for place in range(self.size)
                for chunk in range(self.chunks)
            ]
            for side in range(2):
                whole = [self.side_rows(block, side) for block in blocks]
                out[tree, :, pl.ds(side * self.half + at, CHUNK)] = jnp.concatenate(
                    whole, axis=0
                ).astype(BF16)

    def unpack_chunk(self, out, chunk):
        @pl.loop(0, self.half // CHUNK)
        def _(step):
            at = pl.multiple_of(step * CHUNK, CHUNK)
            blocks = [
                self.board[tree, chunk, place, :, pl.ds(at, CHUNK)].astype(F32)
                for place in range(self.size)
                for tree in range(2)
            ]
            for side in range(2):
                whole = [self.side_rows(block, side) for block in blocks]
                out[chunk, :, pl.ds(side * self.half + at, CHUNK)] = jnp.concatenate(
                    whole, axis=0
                ).astype(BF16)

    def complete(self, out):
        for chunk in range(self.chunks):
            self.arrive(chunk)
        self.unpack(out, self.core)
        for chunk in range(self.chunks):
            self.arrive_over(chunk)
        self.unpack(out, self.sibling)

    def finish(self):
        for chunk in range(self.chunks):
            for place in range(self.size):
                @pl.when(self.direct(place))
                def _():
                    self.spread(chunk, place, self.me).wait_send()

                self.over(self.core, chunk, place).wait_send()

            for via, source, target in self.relays:
                @pl.when(self.me == via)
                def _():
                    self.passed(chunk, source, target).wait_send()


class Scatterer:
    def __init__(self, axis, rows, half):
        self.axis, self.half = axis, half
        self.size = size = lax.axis_size(axis)
        self.chunks = chunks = chunk_count(rows)
        self.rows = rows // chunks
        block = (2 * self.rows, half)
        self.scratch = [pltpu.VMEM((chunks, size) + block, BF16)] * 4
        self.scratch += [pltpu.VMEM((chunks,) + block, F32), pltpu.VMEM((chunks,) + block, BF16)]
        self.scratch += [SEM((chunks, size))] * 4 + [SEM((chunks,))] * 2

    def bind(self, refs):
        self.to_sib, self.from_sib, self.to_peer, self.from_peer, self.total, self.joint = refs[:6]
        self.sib_send, self.sib_recv, self.peer_send, self.peer_recv = refs[6:10]
        self.join_send, self.join_recv = refs[10:]
        self.core = lax.axis_index("section")
        self.sibling = 1 - self.core
        self.me = lax.axis_index(self.axis)
        self.sides = [(0, 1, 3), (3, 2, 0)] if self.axis == "dp" and self.size == 4 else []
        self.order = [0, 3, 1, 2] if self.sides else range(self.size)

    def over(self, chunk, place):
        return remote(
            self.to_sib.at[chunk, place], self.from_sib.at[chunk, place],
            self.sib_send.at[chunk, place], self.sib_recv.at[chunk, place],
            {"section": self.sibling},
        )

    def spread(self, chunk, place, slot):
        return remote(
            self.to_peer.at[chunk, place], self.from_peer.at[chunk, slot],
            self.peer_send.at[chunk, place], self.peer_recv.at[chunk, slot], {self.axis: place},
        )

    def by_way(self, chunk, via, target):
        return remote(
            self.to_peer.at[chunk, target], self.joint.at[chunk], self.join_send.at[chunk],
            self.join_recv.at[chunk], {self.axis: via},
        )

    def plain(self, place):
        ok = place != self.me
        for source, via, target in self.sides:
            if place == target:
                ok = ok & (self.me != source) & (self.me != via)
        return ok

    def expected(self, place):
        ok = place != self.me
        for source, via, target in self.sides:
            if place == source:
                ok = ok & (self.me != target)
        return ok

    def over_columns(self, body):
        @pl.loop(0, self.half // CHUNK)
        def _(step):
            body(pl.multiple_of(step * CHUNK, CHUNK))

    def absorb(self, chunk, mine):
        for place in self.order:
            self.over(chunk, place).wait_recv()

            def add(at):
                both = mine(place, at)
                both += self.from_sib[chunk, place, :, pl.ds(at, CHUNK)].astype(F32)
                self.to_peer[chunk, place, :, pl.ds(at, CHUNK)] = both.astype(BF16)

                @pl.when(place == self.me)
                def _():
                    self.total[chunk, :, pl.ds(at, CHUNK)] = both

            self.over_columns(add)

            for source, via, target in self.sides:
                if place == target:
                    @pl.when(self.me == source)
                    def _():
                        self.by_way(chunk, via, target).start()

            @pl.when(self.plain(place))
            def _():
                self.spread(chunk, place, self.me).start()

        for source, via, target in self.sides:
            @pl.when(self.me == via)
            def _():
                self.by_way(chunk, via, target).wait_recv()

                def add(at):
                    at = pl.ds(at, CHUNK)
                    both = self.to_peer[chunk, target, :, at].astype(F32)
                    both += self.joint[chunk, :, at].astype(F32)
                    self.to_peer[chunk, target, :, at] = both.astype(BF16)

                self.over_columns(add)
                self.spread(chunk, target, self.me).start()

    def collect(self, chunk):
        for place in self.order:
            @pl.when(self.expected(place))
            def _():
                self.spread(chunk, place, place).wait_recv()
                self.total[chunk] += self.from_peer[chunk, place].astype(F32)

        total = self.total[chunk]
        return jnp.concatenate([total[: self.rows], total[self.rows :]], axis=1)

    def finish(self):
        for chunk in range(self.chunks):
            for place in range(self.size):
                self.over(chunk, place).wait_send()

                @pl.when(self.plain(place))
                def _():
                    self.spread(chunk, place, self.me).wait_send()

            for source, via, target in self.sides:
                @pl.when(self.me == source)
                def _():
                    self.by_way(chunk, via, target).wait_send()

                @pl.when(self.me == via)
                def _():
                    self.spread(chunk, target, self.me).wait_send()


class RowScatterer(Scatterer):
    def packed(self, tree, chunk, place, at):
        rows = self.rows
        first = rows * (place * self.chunks + chunk)
        low = first // 16 * 16
        high = -(-(first + rows) // 16) * 16
        parts = [
            self.terms[tree, low:high, pl.ds(side * self.half + at, CHUNK)].astype(F32)[
                first - low : first - low + rows
            ]
            for side in range(2)
        ]
        return jnp.concatenate(parts, axis=0)

    def prepare(self, terms):
        self.terms = terms
        for chunk in range(self.chunks):
            for place in range(self.size):
                def pack(at):
                    self.to_sib[chunk, place, :, pl.ds(at, CHUNK)] = self.packed(
                        self.sibling, chunk, place, at
                    ).astype(BF16)

                self.over_columns(pack)

    def start(self):
        for chunk in range(self.chunks):
            for place in range(self.size):
                self.over(chunk, place).start()

    def send_on(self):
        for chunk in range(self.chunks):
            self.absorb(chunk, lambda place, at: self.packed(self.core, chunk, place, at))


class Staged(Part):
    def __init__(self, ins, outs, scratch, helpers):
        self.in_names, self.out_names, self.scratch_names = list(ins), list(outs), list(scratch)
        self.ins, self.outs = list(ins.values()), list(outs.values())
        self.helpers = helpers
        self.scratch = list(scratch.values())
        for helper in helpers:
            self.scratch += helper.scratch

    def bind(self, ins, outs, scratch):
        scratch = list(scratch)
        names = self.in_names + self.out_names + self.scratch_names
        count = len(self.scratch_names)
        for name, ref in zip(names, list(ins) + list(outs) + scratch[:count]):
            setattr(self, name, ref)
        del scratch[:count]
        for helper in self.helpers:
            helper.bind(scratch[: len(helper.scratch)])
            del scratch[: len(helper.scratch)]

    def finish(self):
        for helper in self.helpers:
            helper.finish()


def vmem_f32(*shape):
    return (jax.ShapeDtypeStruct(shape, F32), VMEM)


def vmem_bf16(*shape):
    return (jax.ShapeDtypeStruct(shape, BF16), VMEM)


def rows_at(chunk, rows):
    return pl.ds(pl.multiple_of(chunk * rows, 8), rows)


class LastHub(Staged):
    def __init__(self, terms, values, gain, add):
        rows, depth = values.shape
        half = depth // 2
        self.rows_in = RowScatterer("tensor", rows, half)
        self.rows_out = Gatherer("tensor", rows, half)
        super().__init__(
            {"terms": (terms, VMEM), "values": (values, VMEM), "gain": (gain, VMEM), "add": (add, VMEM)},
            {
                "gain_grad": vmem_f32(1, depth),
                "gathered": vmem_bf16(2, self.rows_out.size * rows, depth),
            },
            {},
            [self.rows_in, self.rows_out],
        )

    def prepare(self):
        self.rows_in.prepare(self.terms)

    def start(self):
        self.rows_in.start()

    def run(self):
        self.rows_in.send_on()
        self.gain_grad[...] = jnp.zeros_like(self.gain_grad)
        for chunk in range(self.rows_in.chunks):
            at = rows_at(chunk, self.rows_in.rows)
            result, gain_grad = norm_back(
                self.rows_in.collect(chunk), self.values[at], self.gain[...]
            )
            self.gain_grad[...] += gain_grad
            self.rows_out.begin(chunk, result + self.add[at])
        self.rows_out.complete(self.gathered)


class FeedForward(Staged):
    def __init__(self, terms, own, gain, weights, forward, backward, extra):
        rows, depth = own.shape
        half = depth // 2
        units = weights[0].shape[0]
        self.has_forward, self.has_backward, self.units = forward, backward, units
        self.depth = depth
        self.size = size = lax.axis_size("dp")
        self.rows_in = RowScatterer("tensor", rows, half)
        self.spread_in = Gatherer("dp", rows, half)
        self.chunks, self.rows = self.rows_in.chunks, self.rows_in.rows
        chunks, chunk_rows = self.chunks, 2 * size * self.rows
        helpers = [self.rows_in, self.spread_in]
        tensor_rows = lax.axis_size("tensor") * rows
        matrix = pltpu.VMEM((units, depth), BF16)
        ins = {"terms": (terms, VMEM), "own": (own, VMEM), "gain": (gain, VMEM)}
        ins |= {name: (w, HBM) for name, w in zip(("gate_hbm", "up_hbm", "down_hbm"), weights)}
        ins |= {name: (value, VMEM) for name, value in extra.items()}
        outs = {}
        scratch = {"w_gate": matrix, "w_up": matrix, "w_down": matrix, "load": SEM((3,))}
        kept = pltpu.VMEM((size, 2 * self.rows, half), F32)
        if forward:
            outs |= {
                "middle": vmem_f32(rows, depth),
                "mlp_in": vmem_bf16(chunks, chunk_rows, depth),
                "hidden": vmem_bf16(chunks, chunk_rows, units),
                "own_out": vmem_f32(rows, depth),
                "out": vmem_bf16(2, tensor_rows, depth),
            }
            self.back = Scatterer("dp", rows, half)
            self.out_rows = Gatherer("tensor", rows, half)
            helpers += [self.back, self.out_rows]
            scratch["kept"] = kept
        if forward and not backward:
            outs |= {"gate": vmem_f32(chunks, chunk_rows, units), "up": vmem_f32(chunks, chunk_rows, units)}
        if forward and backward:
            outs["grad_mlp"] = vmem_bf16(chunks, chunk_rows, depth)
            self.grad_in = Gatherer("dp", rows, half)
            helpers += [self.grad_in]
            scratch |= {
                "gate": pltpu.VMEM((chunks, chunk_rows, units), F32),
                "up": pltpu.VMEM((chunks, chunk_rows, units), F32),
            }
        if backward:
            outs |= {
                "grad_gate": vmem_bf16(chunks, chunk_rows, units),
                "grad_up": vmem_bf16(chunks, chunk_rows, units),
                "grad_middle": vmem_f32(rows, depth),
                "mlp_gain_grad": vmem_f32(1, depth),
                "grad_attn": vmem_bf16(2, tensor_rows, depth),
            }
            self.grad_back = Scatterer("dp", rows, half)
            self.grad_rows = Gatherer("tensor", rows, half)
            helpers += [self.grad_back, self.grad_rows]
            scratch["grad_kept"] = kept
        if backward and not forward:
            outs |= {
                "gain_grad": vmem_f32(1, depth),
                "incoming": vmem_bf16(2, tensor_rows, depth),
                "grad_mlp": vmem_bf16(chunks, chunk_rows, depth),
            }
            scratch["grad_own"] = pltpu.VMEM((rows, depth), F32)
            self.incoming_rows = Gatherer("tensor", rows, half)
            helpers += [self.incoming_rows]
        super().__init__(ins, outs, scratch, helpers)

    def loads(self):
        pairs = [(self.gate_hbm, self.w_gate), (self.up_hbm, self.w_up), (self.down_hbm, self.w_down)]
        return [
            pltpu.make_async_copy(src, dst, self.load.at[i]) for i, (src, dst) in enumerate(pairs)
        ]

    def prepare(self):
        for copy in self.loads():
            copy.start()
        self.rows_in.prepare(self.terms)

    def start(self):
        self.rows_in.start()
        if self.has_forward and self.has_backward:
            for chunk in range(self.chunks):
                self.grad_in.begin(chunk, self.grad_own[rows_at(chunk, self.rows)])

    def run(self):
        self.rows_in.send_on()
        if self.has_backward:
            self.mlp_gain_grad[...] = jnp.zeros_like(self.mlp_gain_grad)
        if not self.has_forward:
            self.gain_grad[...] = jnp.zeros_like(self.gain_grad)
        for chunk in range(self.chunks):
            at = rows_at(chunk, self.rows)
            total = self.rows_in.collect(chunk)
            if self.has_forward:
                middle = self.own[at] + total
                self.middle[at] = middle
                mean_sq = jnp.mean(middle * middle, axis=1, keepdims=True)
                normed = middle * lax.rsqrt(mean_sq + EPSILON) * self.gain[...]
                self.spread_in.begin(chunk, normed)
            else:
                result, gain_grad = norm_back(total, self.own[at], self.gain[...])
                self.gain_grad[...] += gain_grad
                result = (result + self.add[at]).astype(BF16).astype(F32)
                self.grad_own[at] = result
                self.spread_in.begin(chunk, result)
                self.incoming_rows.begin(chunk, result)
        for copy in self.loads():
            copy.wait()

        self.spread_in.arrive(0)
        if self.has_forward and self.has_backward:
            self.grad_in.arrive(0)

        @pl.loop(0, self.chunks)
        def _(chunk):
            self.spread_in.arrive_over(chunk)
            if self.has_forward:
                self.spread_in.unpack_chunk(self.mlp_in, chunk)
                self.forward_chunk(chunk)
            else:
                self.spread_in.unpack_chunk(self.grad_mlp, chunk)
            if self.has_forward and self.has_backward:
                self.grad_in.arrive_over(chunk)
                self.grad_in.unpack_chunk(self.grad_mlp, chunk)
            if self.has_backward:
                self.backward_chunk(chunk)

            @pl.when(chunk + 1 < self.chunks)
            def _():
                self.spread_in.arrive(chunk + 1)
                if self.has_forward and self.has_backward:
                    self.grad_in.arrive(chunk + 1)

            if self.has_forward:
                self.back.absorb(chunk, lambda place, at: self.kept[place, :, pl.ds(at, CHUNK)])
            if self.has_backward:
                self.grad_back.absorb(
                    chunk, lambda place, at: self.grad_kept[place, :, pl.ds(at, CHUNK)]
                )

            @pl.when(chunk > 0)
            def _():
                self.hand_back(chunk - 1)

        self.hand_back(self.chunks - 1)
        if self.has_backward:
            self.grad_rows.complete(self.grad_attn)
        if self.has_forward:
            self.out_rows.complete(self.out)
        else:
            self.incoming_rows.complete(self.incoming)

    def hand_back(self, chunk):
        at = rows_at(chunk, self.rows)
        if self.has_backward:
            values = self.middle if self.has_forward else self.middle_in
            gain = self.gain if self.has_forward else self.mlp_gain
            result, gain_grad = norm_back(self.grad_back.collect(chunk), values[at], gain[...])
            self.mlp_gain_grad[...] += gain_grad
            result += self.grad_own[at]
            self.grad_middle[at] = result
            self.grad_rows.begin(chunk, result)
        if self.has_forward:
            output = (self.middle[at] + self.back.collect(chunk)).astype(BF16).astype(F32)
            self.own_out[at] = output
            self.out_rows.begin(chunk, output)

    def unit_tiles(self, body):
        tile = 256

        @pl.loop(0, self.units // tile)
        def _(step):
            body(pl.ds(pl.multiple_of(step * tile, tile), tile))

    def forward_chunk(self, chunk):
        def tile(at):
            rows = self.mlp_in[chunk]
            gate = dot_inner(rows, self.w_gate[at, :])
            up = dot_inner(rows, self.w_up[at, :])
            self.gate[chunk, :, at] = gate
            self.up[chunk, :, at] = up
            self.hidden[chunk, :, at] = (gate * jax.nn.sigmoid(gate) * up).astype(BF16)

        self.unit_tiles(tile)
        self.terms_out(
            chunk, self.back, self.kept, lambda at: dot(self.hidden[chunk], self.w_down[:, at])
        )

    def backward_chunk(self, chunk):
        def tile(at):
            grad_hidden = dot_inner(self.grad_mlp[chunk], self.w_down[at, :])
            gate, up = self.gate[chunk, :, at], self.up[chunk, :, at]
            share = jax.nn.sigmoid(gate)
            act = gate * share
            self.grad_up[chunk, :, at] = (grad_hidden * act).astype(BF16)
            self.grad_gate[chunk, :, at] = (
                grad_hidden * up * (share + act * (1.0 - share))
            ).astype(BF16)

        self.unit_tiles(tile)
        self.terms_out(
            chunk, self.grad_back, self.grad_kept,
            lambda at: dot(self.grad_gate[chunk], self.w_gate[:, at])
            + dot(self.grad_up[chunk], self.w_up[:, at]),
        )

    def terms_out(self, chunk, scatterer, kept, product):
        rows, half = self.rows, self.depth // 2
        first = lax.axis_index("section") == 0

        @pl.loop(0, half // CHUNK)
        def _(step):
            low = pl.multiple_of(step * CHUNK, CHUNK)
            at = pl.ds(low, CHUNK)
            sides = [product(pl.ds(side * half + low, CHUNK)) for side in range(2)]
            for place in range(self.size):
                trees = []
                for tree in range(2):
                    start = (2 * place + tree) * rows
                    trees.append(
                        jnp.concatenate([side[start : start + rows] for side in sides], axis=0)
                    )
                kept[place, :, at] = jnp.where(first, trees[0], trees[1])
                scatterer.to_sib[chunk, place, :, at] = jnp.where(
                    first, trees[1], trees[0]
                ).astype(BF16)

        for place in range(self.size):
            scatterer.over(chunk, place).start()


def hub_plain(terms, own_args, body, own_outs, scatter, gathers):
    total = None
    if scatter:
        mine = lax.psum_scatter(terms, "section", scatter_dimension=0, tiled=True)
        mine = lax.psum_scatter(mine, scatter, scatter_dimension=1, tiled=True)[0]
        total = mine.astype(F32)

    class Cell:
        def __setitem__(self, _, value):
            self.value = value

    cells = [Cell() for _ in own_outs]
    result = body(total, own_args, cells).astype(BF16)
    gathered = [
        lax.all_gather(lax.all_gather(result, axis, axis=0, tiled=True), "section", axis=0)
        for axis in gathers
    ]
    return [cell.value for cell in cells] + gathered


def with_cargo(part, cargo, axes, collective_id, cost_us, vmem=40):
    outs = fused(cargo + [part], axes, bool(cargo), collective_id, cost_us, vmem)
    return outs[-1], outs[:-1]


def norm_back(total, values, gain):
    scale = lax.rsqrt(jnp.mean(values * values, axis=1, keepdims=True) + EPSILON)
    unit = values * scale
    gain_grad = jnp.sum(total * unit, axis=0, keepdims=True)
    scaled = total * gain
    along = jnp.mean(scaled * unit, axis=1, keepdims=True)
    return ((scaled - unit * along) * scale, gain_grad)


def norm_body(total, args, outs):
    middle = args[0] + total
    outs[0][...] = middle
    return rms_scale(middle, args[1])


def add_body(total, args, outs):
    result = args[0] + total
    outs[0][...] = result
    return result


def norm_back_body(total, args, outs):
    result, outs[1][...] = norm_back(total, args[0], args[1])
    result += args[2]
    outs[0][...] = result
    return result


def embed(q_pre, k_pre, q_scale, k_scale, cos_table, sine_table):
    queries = rms_scale(q_pre, q_scale)
    keys = rms_scale(k_pre, k_scale)
    return (
        rotate(queries, cos_table[:, :, None], sine_table[:, :, None]),
        rotate(keys, cos_table, sine_table),
    )


def attn_forward(hidden_in, weights, gains, slot, gather):
    attn_scale, _, q_scale, k_scale = gains
    w_qkv, w_out = weights[:2]
    allowed, cos_table, sine_table = slot
    trees, row_count, depth = hidden_in.shape
    q_width = w_out.shape[0]
    normed = rms_scale(hidden_in.astype(F32), attn_scale).astype(BF16).reshape(-1, depth)
    qkv = dot(normed, w_qkv).reshape(trees, row_count, -1)
    q_pre = qkv[:, :, :q_width].reshape(trees, row_count, -1, HD)
    k_pre = qkv[:, :, q_width : q_width + HD]
    value_bf = qkv[:, :, q_width + HD :].astype(BF16)
    queries, keys_rot = embed(q_pre, k_pre, q_scale, k_scale, cos_table, sine_table)
    query_bf = queries.astype(BF16)
    kv_all = gather(jnp.concatenate([keys_rot.astype(BF16), value_bf], axis=2))
    key_all = kv_all[:, :, :HD]
    value_all = kv_all[:, :, HD:]
    scores = masked_scores(query_bf, key_all, allowed)
    row_max = jnp.max(scores, axis=-1, keepdims=True)
    exp_scores = jnp.exp(scores - row_max)
    row_total = jnp.sum(exp_scores, axis=-1, keepdims=True)
    prob_bf = (exp_scores / row_total).astype(BF16)
    log_total = row_max + jnp.log(row_total)
    attended = jnp.einsum("bgrt,btd->brgd", prob_bf, value_all, preferred_element_type=F32)
    attended_bf = attended.reshape(trees * row_count, -1).astype(BF16)
    terms = dot(attended_bf, w_out).astype(BF16).reshape(trees, row_count, depth)
    saved = (normed, q_pre, k_pre, query_bf, key_all, value_all, log_total, attended_bf)
    return (terms, saved)


def attn_backward(grad_attn, saved, weights, gains, slot, scatter):
    _, _, q_scale, k_scale = gains
    w_qkv, w_out = weights[:2]
    allowed, cos_table, sine_table = slot
    normed, q_pre, k_pre, query_bf, key_all, value_all, log_total, attended_bf = saved
    trees, row_count = query_bf.shape[:2]
    depth = normed.shape[1]
    grad_attn = grad_attn.reshape(-1, depth)
    grad_heads = dot_inner(grad_attn, w_out).astype(BF16).reshape(query_bf.shape)
    scores = masked_scores(query_bf, key_all, allowed)
    prob_full = jnp.exp(scores - log_total)
    grad_prob = jnp.einsum("brgd,btd->bgrt", grad_heads, value_all, preferred_element_type=F32)
    row_dot = jnp.sum(prob_full * grad_prob, axis=-1, keepdims=True)
    grad_scores = (prob_full * (grad_prob - row_dot)).astype(BF16)
    scale_factor = HD ** (-0.5)
    grad_query = (
        jnp.einsum("bgrt,btd->brgd", grad_scores, key_all, preferred_element_type=F32)
        * scale_factor
    )
    grad_key_all = (
        jnp.einsum("bgrt,brgd->btd", grad_scores, query_bf, preferred_element_type=F32)
        * scale_factor
    )
    grad_value_all = jnp.einsum(
        "bgrt,brgd->btd", prob_full.astype(BF16), grad_heads, preferred_element_type=F32
    )
    grad_kv = scatter(jnp.concatenate([grad_key_all, grad_value_all], axis=2).astype(BF16))
    _, embedding_pull = jax.vjp(
        partial(embed, cos_table=cos_table, sine_table=sine_table), q_pre, k_pre, q_scale, k_scale
    )
    grad_q_pre, grad_k_pre, grad_q_scale, grad_k_scale = embedding_pull(
        (grad_query, grad_kv[:, :, :HD].astype(F32))
    )
    qkv_grad = jnp.concatenate(
        [
            grad_q_pre.astype(BF16).reshape(trees, row_count, -1),
            grad_k_pre.astype(BF16),
            grad_kv[:, :, HD:].astype(BF16),
        ],
        axis=2,
    ).reshape(trees * row_count, -1)
    terms = dot_inner(qkv_grad, w_qkv).astype(BF16).reshape(trees, row_count, depth)
    return (terms, [(normed, qkv_grad), (grad_attn, attended_bf)], [grad_q_scale, grad_k_scale])


def plain_layers(hidden, own_in, grad_own, weights, gains, slot, shared_kv):
    depth = own_in.shape[1]
    own_shape = own_in.shape

    def gather(own):
        return lax.all_gather(own, "dp", axis=1, tiled=True)

    def scatter(whole):
        total = lax.psum_scatter(whole, "dp", scatter_dimension=1, tiled=True)
        if shared_kv:
            total = lax.psum(total, "section")
            total = jnp.where(lax.axis_index("section") == 0, total, jnp.zeros_like(total))
        return total

    outputs, kept = [], []
    for layer in range(2):
        _, _, w_gate, w_up, w_down = weights[layer]
        terms, saved = attn_forward(hidden, weights[layer], gains[layer], slot, gather)
        mlp_scale = gains[layer][1][None]
        middle, mlp_in = hub_plain(
            terms, [own_in, mlp_scale], norm_body, [own_shape], "tensor", ["dp"]
        )
        mlp_in = mlp_in.reshape(-1, depth)
        gate, up = dot_inner(mlp_in, w_gate), dot_inner(mlp_in, w_up)
        hidden_bf = swiglu(gate, up).astype(BF16)
        terms = dot(hidden_bf, w_down).astype(BF16).reshape(2, -1, depth)
        kept.append((own_in, saved, middle, mlp_in, gate, up, hidden_bf))
        own_in, hidden = hub_plain(terms, [middle], add_body, [own_shape], "dp", ["tensor"])
        own_in = own_in.astype(BF16).astype(F32)
        outputs.append(hidden)

    own_outs = [own_shape, (1, depth)]
    grads, products, gain_grads = [None, None], [None, None], [None, None]
    (grad_mlp,) = hub_plain(None, [grad_own], lambda total, args, outs: args[0], [], None, ["dp"])
    for layer in (1, 0):
        _, _, w_gate, w_up, w_down = weights[layer]
        own_in, saved, middle, mlp_in, gate, up, hidden_bf = kept[layer]
        grad_mlp = grad_mlp.reshape(-1, depth)
        _, pull = jax.vjp(swiglu, gate, up)
        grad_gate, grad_up = (item.astype(BF16) for item in pull(dot_inner(grad_mlp, w_down)))
        terms = (dot(grad_gate, w_gate) + dot(grad_up, w_up)).astype(BF16).reshape(2, -1, depth)
        grad_middle, mlp_gain_grad, grad_attn = hub_plain(
            terms, [middle, gains[layer][1][None], grad_own], norm_back_body, own_outs, "dp",
            ["tensor"],
        )
        terms, pairs, head_grads = attn_backward(
            grad_attn, saved, weights[layer], gains[layer], slot, scatter
        )
        grad_own, gain_grad, grads[layer], grad_next = hub_plain(
            terms, [own_in, gains[layer][0][None], grad_middle], norm_back_body, own_outs, "tensor",
            ["tensor", "dp"],
        )
        grad_own = grad_own.astype(BF16).astype(F32)
        pairs += [(grad_gate, mlp_in), (grad_up, mlp_in), (hidden_bf, grad_mlp)]
        products[layer] = pairs
        gain_grads[layer] = jnp.concatenate([gain_grad[0], mlp_gain_grad[0], *head_grads])
        grad_mlp = grad_next
    return (outputs, grads, products, gain_grads)


def swap_cores(mine, other):
    core = lax.axis_index("section")
    arrived = lax.ppermute(other, "section", [(0, 1), (1, 0)])
    return (jnp.where(core == 0, mine, arrived), jnp.where(core == 0, arrived, mine))


def on_device(
    inputs, cotangent, seg_ids, parents, order, attn_gain, w_query, w_key, w_value, w_out,
    q_gain, k_gain, mlp_gain, w_gate, w_up, w_down,
):
    core = lax.axis_index("section")
    data_index = lax.axis_index("dp")
    tensor_index = lax.axis_index("tensor")
    dp_size = lax.axis_size("dp")
    tensor_size = lax.axis_size("tensor")
    trees, row_count, depth = inputs.shape
    own_rows = row_count // tensor_size
    row_start = data_index * row_count
    own_depth = w_query.shape[1]
    q_width = w_query.shape[2] // 2
    shared_kv = w_key.shape[2] == HD
    k_width = HD if shared_kv else w_key.shape[2] // 2
    own_units = w_gate.shape[2]
    share = own_units // (2 * dp_size)

    def pick(stacked, index):
        return lax.dynamic_index_in_dim(stacked, index, 0, keepdims=False)

    fast = (
        own_rows % 8 == 0
        and depth % (2 * CHUNK) == 0
        and row_count % 16 == 0
        and share % 16 == 0
        and own_depth % 128 == 0
        and not shared_kv
    )

    def halves(width, array):
        return [array[:, :width], array[:, array.shape[1] - width :]]

    unit_mats = [w_gate[0].T, w_up[0].T, w_down[0]]
    qkv_width = q_width + 2 * k_width
    gains_own = jnp.concatenate([attn_gain[0], mlp_gain[0], q_gain[0], k_gain[0]]).astype(F32)

    def spread_units(rows):
        return lax.all_gather(rows, "tensor", axis=0, tiled=True)

    def tied(value, *before):
        return lax.optimization_barrier((value, *before))[0]

    if fast:
        line = ["section", "dp"]
        everyone = ["section", "dp", "tensor"]
        (gate_rows, up_rows), (gains_all,) = fused(
            [UnitsOut(unit_mats[:2], 0), SharedRows(gains_own.reshape(-1, 128))], line, True, 1, 45
        )
        shards = AttnShards(w_query[0], w_key[0], w_value[0], w_out[0])
        shards.arrays[0] = tied(shards.arrays[0], gate_rows)
        (w_qkv, w_heads), (down_rows,), (attn_shard,) = fused(
            [AttnOut(shards, 0), UnitsOut(unit_mats[2:], 0), HalfOver(shards)], line, True, 2, 80
        )
        first_weights = [w_qkv, w_heads, spread_units(gate_rows), spread_units(up_rows)]
        attn_next = lax.all_gather(attn_shard, "dp", axis=0)
    else:
        gains_all = lax.all_gather(gains_own, ("section", "dp"))
        attn_halves = jnp.stack(
            [
                jnp.concatenate(parts, axis=1)
                for parts in zip(
                    halves(q_width, w_query[0]),
                    halves(k_width, w_key[0]),
                    halves(k_width, w_value[0]),
                    halves(q_width, w_out[0].T),
                )
            ]
        )
        attn_shards = swap_cores(pick(attn_halves, core), pick(attn_halves, 1 - core))
        unit_blocks = jnp.stack(unit_mats).reshape(3, 2, dp_size, share, own_depth)
        unit_blocks = unit_blocks.transpose(1, 2, 0, 3, 4)
        unit_shards = swap_cores(pick(unit_blocks, core), pick(unit_blocks, 1 - core))
        both_weights = []
        for layer in range(2):
            attn_all = lax.all_gather(attn_shards[layer], "dp", axis=0, tiled=True)
            pieces = exchange(unit_shards[layer], "dp")
            pieces = pieces.transpose(1, 2, 0, 3).reshape(3, share, depth)
            both_weights.append(
                (
                    attn_all[:, :qkv_width], attn_all[:, qkv_width:].T,
                    *(spread_units(pieces[i]) for i in range(3)),
                )
            )

    gains_all = gains_all.reshape(2, dp_size, -1)
    gains = [
        (
            gains_all[layer, :, :own_depth].reshape(depth),
            gains_all[layer, :, own_depth : 2 * own_depth].reshape(depth),
            gains_all[layer, 0, 2 * own_depth : 2 * own_depth + HD],
            gains_all[layer, 0, 2 * own_depth + HD :],
        )
        for layer in range(2)
    ]

    def slot_setup(slot_index):
        tree_id = pick(order, slot_index)
        allowed, row_positions = path_mask(
            pick(seg_ids, tree_id), pick(parents, tree_id), row_start, row_count
        )
        cos_table, sine_table = rope_tables(row_positions, HD)
        return (pick(inputs, tree_id), allowed, cos_table[:, 0], sine_table[:, 0])

    setups = [slot_setup(i) for i in range(trees)]
    hidden, *slot = (jnp.stack(item) for item in zip(*setups))

    def own_part(whole):
        return lax.dynamic_slice_in_dim(
            pick(whole, core), tensor_index * own_rows, own_rows, 0
        )

    own_in = own_part(hidden).astype(F32)
    grad_own = own_part(cotangent).astype(F32)

    def weight_products(pairs):
        return [dot_outer(left, right).astype(BF16) for left, right in pairs]

    def scatter_units(products):
        return [
            lax.psum_scatter(item, "tensor", scatter_dimension=0, tiled=True) for item in products
        ]

    def scatter_shards(products):
        return lax.psum_scatter(
            jnp.concatenate(products, axis=1), "dp", scatter_dimension=0, tiled=True
        )

    if fast:
        def units_on(*which):
            return [UnitsOut([unit_mats[i] for i in which], 1)]

        def kv_gather(own, cargo, collective_id, carried):
            (whole,), outs = with_cargo(GatherKV(own), cargo, everyone, collective_id, 40)
            carried += outs
            return whole.reshape(trees, -1, 2 * HD)

        def kv_scatter(whole, cargo, collective_id, carried):
            part = ScatterKV(whole.reshape(trees, dp_size, row_count, 2 * HD))
            (total,), outs = with_cargo(part, cargo, line, collective_id, 30)
            carried += outs
            return total

        def flat(array):
            return array.reshape(-1, array.shape[-1])

        carried = []
        terms, saved_first = attn_forward(
            hidden, first_weights, gains[0], slot,
            lambda own: kv_gather(
                tied(own, *first_weights[2:]), [UnitsSpread(down_rows)] + units_on(0, 1), 3, carried
            ),
        )
        (down_all,), (gate_rows, up_rows) = carried
        first_weights.append(down_all)
        part = FeedForward(
            terms, own_in, gains[0][1][None], first_weights[2:], True, False, {}
        )
        outs, ((down_rows,),) = with_cargo(part, units_on(2), everyone, 4, 90, 56)
        middle_first, mlp_in_first, hidden_first, own_next, output_first, gate_first, up_first = outs
        second_weights = [
            attn_next[:, :own_depth].reshape(depth, -1),
            attn_next[:, own_depth:].transpose(1, 0, 2).reshape(q_width, depth),
            spread_units(gate_rows), spread_units(up_rows),
        ]
        carried = []
        terms, saved_second = attn_forward(
            output_first, second_weights, gains[1], slot,
            lambda own: kv_gather(
                tied(own, second_weights[2]), [UnitsSpread(down_rows)], 5, carried
            ),
        )
        ((down_all,),) = carried
        second_weights.append(down_all)
        part = FeedForward(
            terms, own_next, gains[1][1][None], second_weights[2:], True, True,
            {"grad_own": grad_own},
        )
        outs, _ = with_cargo(part, [], everyone, 6, 100, 60)
        (
            middle, mlp_in, hidden_bf, _, output_second, grad_mlp,
            grad_gate, grad_up, grad_middle, mlp_gain_second, grad_attn,
        ) = outs
        products_second = weight_products(
            [
                (flat(grad_gate), flat(mlp_in)),
                (flat(grad_up), flat(mlp_in)),
                (flat(hidden_bf), flat(grad_mlp)),
            ]
        )
        unit_second = scatter_units(products_second)
        terms, pairs, head_second = attn_backward(
            grad_attn, saved_second, second_weights, gains[1], slot,
            lambda whole: kv_scatter(tied(whole, *products_second), [], 7, []),
        )
        pairs = weight_products(pairs)
        attn_second = scatter_shards([tied(pairs[0], unit_second[2]), pairs[1]])
        terms = tied(terms, unit_second[0])
        part = FeedForward(
            terms, own_next, gains[1][0][None], first_weights[2:], False, True,
            {
                "add": grad_middle, "gate": gate_first, "up": up_first,
                "middle_in": middle_first, "mlp_gain": gains[0][1][None],
            },
        )
        outs, (home_second,) = with_cargo(
            part, [UnitsHome(unit_second[:1], 1)], everyone, 8, 90, 60
        )
        (
            grad_gate, grad_up, grad_middle, mlp_gain_first, grad_attn,
            attn_gain_second, incoming_second, grad_mlp,
        ) = outs
        products = weight_products(
            [
                (flat(grad_gate), flat(mlp_in_first)),
                (flat(grad_up), flat(mlp_in_first)),
                (flat(hidden_first), flat(grad_mlp)),
            ]
        )
        grad_attn = tied(grad_attn, *unit_second[1:], *products)
        unit_first = scatter_units([tied(item, attn_second) for item in products[:2]])
        unit_first += scatter_units([tied(products[2], *unit_first)])
        carried = []
        terms, pairs, head_first = attn_backward(
            grad_attn, saved_first, first_weights, gains[0], slot,
            lambda whole: kv_scatter(whole, [UnitsHome(unit_second[1:], 1)], 9, carried),
        )
        home_second += carried[0]
        whole = jnp.concatenate(weight_products(pairs), axis=1).reshape(dp_size, 4, -1, q_width + qkv_width)
        part = LastHub(terms, own_in, gains[0][0][None], grad_middle)
        (attn_gain_first, incoming_first), ((attn_first,), home_first) = with_cargo(
            part, [ScatterKV(whole.transpose(1, 0, 2, 3)), UnitsHome(unit_first[:2], 0)], everyone,
            10, 60, 56,
        )
        attn_first = attn_first.reshape(own_depth, -1).astype(BF16)
        outputs = [output_first, output_second]
        grads = [incoming_first, incoming_second]
        weight_grads = [(attn_first, None), (attn_second, None)]
        gain_grads = [
            jnp.concatenate([attn_gain_first[0], mlp_gain_first[0], *head_first]),
            jnp.concatenate([attn_gain_second[0], mlp_gain_second[0], *head_second]),
        ]
    else:
        outputs, grads, products, gain_grads = plain_layers(
            hidden, own_in, grad_own, both_weights, gains, slot, shared_kv
        )
        weight_grads = []
        for pairs in products:
            whole = weight_products(pairs)
            weight_grads.append((scatter_shards(whole[:2]), scatter_units(whole[2:])))

    gain_total = jnp.stack(gain_grads)
    if fast:
        mine = jnp.where(core == 0, weight_grads[0][0], weight_grads[1][0])
        other = jnp.where(core == 0, weight_grads[1][0], weight_grads[0][0])
        (gain_total,), (arrived,), down_home = fused(
            [TotalOverAll(gain_total.reshape(-1, 128)), Swap(other), UnitsHome(unit_first[2:], 0)],
            everyone, True, 11, 60,
        )
        attn_home = (jnp.where(core == 0, mine, arrived), jnp.where(core == 0, arrived, mine))
        unit_home = [
            jnp.where(core == 0, first, second) for first, second in zip(home_first + down_home, home_second)
        ]
        gain_total = gain_total.reshape(2, -1)
    else:
        def bring_home(first, second):
            mine, other = jnp.where(core == 0, first, second), jnp.where(core == 0, second, first)
            arrived = lax.ppermute(other, "section", [(0, 1), (1, 0)])
            return (jnp.where(core == 0, mine, arrived), jnp.where(core == 0, arrived, mine))

        def pieces_of(grad):
            return exchange(
                jnp.stack(grad).reshape(3, share, dp_size, own_depth).transpose(2, 0, 1, 3), "dp"
            )

        attn_home = bring_home(weight_grads[0][0], weight_grads[1][0])
        unit_home = jnp.stack(bring_home(pieces_of(weight_grads[0][1]), pieces_of(weight_grads[1][1])))
        unit_home = unit_home.transpose(2, 0, 1, 3, 4).reshape(3, own_units, own_depth)
        gain_total = lax.psum(gain_total, ("section", "dp", "tensor"))

    def joined(start, width):
        parts = [half[:, start : start + width] for half in attn_home]
        if shared_kv and start in (q_width, q_width + k_width):
            return parts[0].astype(F32)
        return jnp.concatenate(parts, axis=1).astype(F32)

    gain_own = pick(gain_total, core)
    share_width = attn_gain.shape[1]
    attn_gain_grad = lax.dynamic_slice_in_dim(gain_own, data_index * share_width, share_width, 0)
    mlp_gain_grad = lax.dynamic_slice_in_dim(
        gain_own, depth + data_index * share_width, share_width, 0
    )
    return (
        jnp.where(core == 0, outputs[0], outputs[1])[None],
        jnp.where(core == 0, grads[0], grads[1])[None],
        attn_gain_grad[None],
        joined(0, q_width)[None],
        joined(q_width, k_width)[None],
        joined(q_width + k_width, k_width)[None],
        joined(qkv_width, q_width).T[None],
        gain_own[2 * depth : 2 * depth + HD][None],
        gain_own[2 * depth + HD :][None],
        mlp_gain_grad[None],
        unit_home[0].T.astype(F32)[None],
        unit_home[1].T.astype(F32)[None],
        unit_home[2].astype(F32)[None],
    )


def solution(mesh):
    rows = P(None, "dp", None)
    wide = P("section", "dp", "tensor")
    tall = P("section", "tensor", "dp")
    gain = P("section", "dp")
    head_gain = P("section", None)
    slots = P("section", None, "dp", None)
    in_specs = (
        rows, rows, P(), P(), P(), gain, wide, wide, wide, tall, head_gain, head_gain, gain,
        wide, wide, tall,
    )
    out_specs = (
        slots, slots, gain, wide, wide, wide, tall, head_gain, head_gain, gain, wide, wide, tall,
    )
    return jax.shard_map(
        on_device, mesh=mesh, in_specs=in_specs, out_specs=out_specs, check_vma=False
    )
```

```python
from functools import partial

import jax
import jax.numpy as jnp
from jax import lax
from jax.experimental import pallas as pl
from jax.experimental.pallas import tpu as pltpu
from jax.sharding import PartitionSpec as P

HD = 128
TRUNK = 512
BRANCH = 96
NB = 4
TREE = 1152
SEGS = 9


EPSILON = 1e-06
THETA = 1000000.0
MASKED = -1e30
F32 = jnp.float32
BF16 = jnp.bfloat16


def rms_scale(values, weight_gain):
    mean_sq = jnp.mean(values * values, axis=-1, keepdims=True)
    return values * lax.rsqrt(mean_sq + EPSILON) * weight_gain


def rotate(values, cos_table, sine_table):
    middle_at = values.shape[-1] // 2
    leading = values[..., :middle_at]
    trailing = values[..., middle_at:]
    return jnp.concatenate(
        [leading * cos_table - trailing * sine_table, trailing * cos_table + leading * sine_table],
        axis=-1,
    )


def rope_tables(positions, head_dim):
    half_steps = jnp.arange(head_dim // 2, dtype=F32)
    inverse = THETA ** (-2.0 * half_steps / head_dim)
    angles = positions.astype(F32)[:, None] * inverse[None, :]
    return (jnp.cos(angles)[:, None, :], jnp.sin(angles)[:, None, :])


def swiglu(gate_in, up_in):
    return jax.nn.silu(gate_in) * up_in


def embed_heads(q_pre, k_pre, q_scale, k_scale, cos_table, sine_table):
    row_count = q_pre.shape[0]
    queries = rms_scale(q_pre.reshape(row_count, -1, HD), q_scale)
    keys_part = rms_scale(k_pre.reshape(row_count, -1, HD), k_scale)
    return (rotate(queries, cos_table, sine_table), rotate(keys_part, cos_table, sine_table))


def tree_layout(seg_row, parent_row):
    labels = jnp.arange(SEGS, dtype=jnp.int32)
    places = jnp.arange(TREE, dtype=jnp.int32)
    member = seg_row[None, :] == labels[:, None]
    starts = jnp.min(jnp.where(member, places[None, :], TREE), axis=1)
    depth_base = jnp.where(labels == 0, 0, jnp.where(labels <= NB, TRUNK, TRUNK + BRANCH))
    shifts = depth_base - starts
    positions = places + jnp.sum(jnp.where(member, shifts[:, None], 0), axis=0)
    grandparent = jnp.sum(
        jnp.where(parent_row[:, None] == labels[None, :], parent_row[None, :], 0), axis=1
    )
    ancestor = (
        (labels[None, :] == labels[:, None])
        | (labels[None, :] == parent_row[:, None])
        | (labels[None, :] == grandparent[:, None])
    )
    return (positions, member.astype(F32), ancestor.astype(F32))


def path_mask(seg_row, parent_row, row_start, row_count):
    positions, member, ancestor = tree_layout(seg_row, parent_row)
    member_rows = lax.dynamic_slice_in_dim(member, row_start, row_count, 1)
    seg_rows = lax.dynamic_slice_in_dim(seg_row, row_start, row_count, 0)
    reach_table = jnp.dot(jnp.dot(member_rows.T, ancestor), member)
    places = jnp.arange(TREE, dtype=jnp.int32)
    row_places = row_start + jnp.arange(row_count, dtype=jnp.int32)
    same_seg = seg_rows[:, None] == seg_row[None, :]
    causal = places[None, :] <= row_places[:, None]
    allowed = (reach_table > 0.5) & (jnp.logical_not(same_seg) | causal)
    row_positions = lax.dynamic_slice_in_dim(positions, row_start, row_count, 0)
    return (allowed, row_positions)


OUTER = (((0,), (0,)), ((), ()))
INNER = (((1,), (1,)), ((), ()))


def dot(left, right):
    return jnp.dot(left, right, preferred_element_type=F32)


def dot_inner(left, right):
    return lax.dot_general(left, right, INNER, preferred_element_type=F32)


def dot_outer(left, right):
    return lax.dot_general(left, right, OUTER, preferred_element_type=F32)


def exchange(pieces, axis):
    size = lax.axis_size(axis)
    me = lax.axis_index(axis)
    got = jnp.zeros_like(pieces)
    own = lax.dynamic_index_in_dim(pieces, me, 0, keepdims=True)
    got = lax.dynamic_update_slice_in_dim(got, own, me, 0)
    for step in range(1, size):
        other = me ^ step
        piece = lax.dynamic_index_in_dim(pieces, other, 0, keepdims=True)
        arrived = lax.ppermute(piece, axis, [(i, i ^ step) for i in range(size)])
        got = lax.dynamic_update_slice_in_dim(got, arrived, other, 0)
    return got


def masked_scores(query_bf, key_all, allowed):
    raw_scores = jnp.einsum(
        "brgd,btd->bgrt", query_bf, key_all, preferred_element_type=F32
    ) * HD ** (-0.5)
    return jnp.where(allowed[:, None], raw_scores, MASKED)


MESH = pl.DeviceIdType.MESH
CHUNK = 256
SEM = pltpu.SemaphoreType.DMA
VMEM = pl.BlockSpec(memory_space=pltpu.VMEM)
HBM = pl.BlockSpec(memory_space=pl.ANY)


def remote(src, dst, send_sem, recv_sem, device_id):
    return pltpu.make_async_remote_copy(
        src_ref=src, dst_ref=dst, send_sem=send_sem, recv_sem=recv_sem,
        device_id=device_id, device_id_type=MESH,
    )


def greet(axes, across):
    barrier = pltpu.get_barrier_semaphore()
    count = 0
    for axis in axes:
        size = lax.axis_size(axis)
        me = lax.axis_index(axis)
        for step in range(1, size):
            pl.semaphore_signal(
                barrier, inc=1, device_id={axis: lax.rem(me + step, size)}, device_id_type=MESH
            )
        count += size - 1
    if across:
        size = lax.axis_size("dp")
        me = lax.axis_index("dp")
        sibling = 1 - lax.axis_index("section")
        for step in range(1, size):
            pl.semaphore_signal(
                barrier, inc=1, device_id={"section": sibling, "dp": lax.rem(me + step, size)},
                device_id_type=MESH,
            )
        count += size - 1
    pl.semaphore_wait(barrier, count)


class Part:
    ins, outs, scratch = (), (), ()

    def bind(self, ins, outs, scratch):
        self.in_refs, self.out_refs, self.refs = ins, outs, scratch

    def prepare(self):
        pass

    def start(self):
        pass

    def run(self):
        pass

    def finish(self):
        pass


def fused(parts, axes, across, collective_id, cost_us, vmem=40):
    counts = [(len(part.ins), len(part.outs), len(part.scratch)) for part in parts]

    def kernel(*refs):
        refs = list(refs)
        groups = []
        for kind in range(3):
            groups.append([])
            for count in counts:
                groups[kind].append(refs[: count[kind]])
                del refs[: count[kind]]
        for part, ins, outs, scratch in zip(parts, *groups):
            part.bind(ins, outs, scratch)
        for part in parts:
            part.prepare()
        greet(axes, across)
        for part in parts:
            part.start()
        for part in reversed(parts):
            part.run()
        for part in parts:
            part.finish()

    ins = [item for part in parts for item in part.ins]
    outs = [item for part in parts for item in part.outs]
    results = pl.pallas_call(
        kernel,
        out_shape=[item[0] for item in outs],
        in_specs=[item[1] for item in ins],
        out_specs=[item[1] for item in outs],
        scratch_shapes=[item for part in parts for item in part.scratch],
        cost_estimate=pl.CostEstimate(
            flops=0, bytes_accessed=cost_us * 3_000_000, transcendentals=0
        ),
        compiler_params=pltpu.CompilerParams(
            collective_id=collective_id, has_side_effects=True, vmem_limit_bytes=vmem << 20
        ),
    )(*[item[0] for item in ins])
    results = list(results)
    split = []
    for count in counts:
        split.append(results[: count[1]])
        del results[: count[1]]
    return split


def columns_of(place, width):
    return pl.ds(pl.multiple_of(place * width, width), width)


class UnitsOut(Part):
    def __init__(self, mats, layer):
        self.layer, self.count = layer, len(mats)
        self.size = lax.axis_size("dp")
        rows, self.width = mats[0].shape
        self.share = rows // (2 * self.size)
        self.ins = [(mat, HBM) for mat in mats]
        shape = jax.ShapeDtypeStruct((self.share, self.size * self.width), BF16)
        self.outs = [(shape, HBM)] * self.count
        self.scratch = [SEM((self.count,)), SEM((self.count, 2, self.size)), SEM((self.count, self.size))]

    def bind(self, ins, outs, scratch):
        self.src, self.dst = ins, outs
        self.keep, self.send, self.recv = scratch
        self.core, self.me = lax.axis_index("section"), lax.axis_index("dp")

    def piece(self, index, core, place):
        start = pl.multiple_of((core * self.size + place) * self.share, self.share)
        return self.src[index].at[pl.ds(start, self.share)]

    def lands(self, index, slot):
        return self.dst[index].at[:, columns_of(slot, self.width)]

    def copy(self, index, core, place, slot):
        return remote(
            self.piece(index, core, place), self.lands(index, slot),
            self.send.at[index, core, place], self.recv.at[index, slot],
            {"section": core, "dp": place},
        )

    def local(self, index):
        return pltpu.make_async_copy(
            self.piece(index, self.layer, self.me), self.lands(index, self.me), self.keep.at[index]
        )

    def targets(self):
        for index in range(self.count):
            for core in range(2):
                for place in range(self.size):
                    yield index, core, place, (place != self.me) | (core != self.layer)

    def start(self):
        @pl.when(self.core == self.layer)
        def _():
            for index, core, place, is_other in self.targets():
                @pl.when(is_other)
                def _():
                    self.copy(index, core, place, self.me).start()

            for index in range(self.count):
                self.local(index).start()

    def finish(self):
        for index in range(self.count):
            for place in range(self.size):
                @pl.when((self.core != self.layer) | (place != self.me))
                def _():
                    self.copy(index, 0, 0, place).wait_recv()

        @pl.when(self.core == self.layer)
        def _():
            for index, core, place, is_other in self.targets():
                @pl.when(is_other)
                def _():
                    self.copy(index, core, place, self.me).wait_send()

            for index in range(self.count):
                self.local(index).wait()


class UnitsHome(Part):
    def __init__(self, mats, layer):
        self.layer, self.count = layer, len(mats)
        self.size = lax.axis_size("dp")
        self.share, depth = mats[0].shape
        self.width = depth // self.size
        self.ins = [(mat, HBM) for mat in mats]
        shape = jax.ShapeDtypeStruct((2 * self.size * self.share, self.width), BF16)
        self.outs = [(shape, HBM)] * self.count
        self.scratch = [SEM((self.count,)), SEM((self.count, self.size)), SEM((self.count, 2, self.size))]

    def bind(self, ins, outs, scratch):
        self.src, self.dst = ins, outs
        self.keep, self.send, self.recv = scratch
        self.core, self.me = lax.axis_index("section"), lax.axis_index("dp")

    def lands(self, index, core, slot):
        start = pl.multiple_of((core * self.size + slot) * self.share, self.share)
        return self.dst[index].at[pl.ds(start, self.share)]

    def copy(self, index, place, core, slot):
        return remote(
            self.src[index].at[:, columns_of(place, self.width)], self.lands(index, core, slot),
            self.send.at[index, place], self.recv.at[index, core, slot],
            {"section": self.layer, "dp": place},
        )

    def local(self, index):
        return pltpu.make_async_copy(
            self.src[index].at[:, columns_of(self.me, self.width)],
            self.lands(index, self.layer, self.me), self.keep.at[index],
        )

    def start(self):
        for index in range(self.count):
            for place in range(self.size):
                @pl.when((self.core != self.layer) | (place != self.me))
                def _():
                    self.copy(index, place, self.core, self.me).start()

            @pl.when(self.core == self.layer)
            def _():
                self.local(index).start()

    def finish(self):
        for index in range(self.count):
            @pl.when(self.core == self.layer)
            def _():
                for core in range(2):
                    for place in range(self.size):
                        @pl.when((core != self.layer) | (place != self.me))
                        def _():
                            self.copy(index, 0, core, place).wait_recv()

                self.local(index).wait()

            for place in range(self.size):
                @pl.when((self.core != self.layer) | (place != self.me))
                def _():
                    self.copy(index, place, self.core, self.me).wait_send()


class UnitsSpread(Part):
    def __init__(self, rows):
        self.size = lax.axis_size("tensor")
        self.share, depth = rows.shape
        self.ins = [(rows, HBM)]
        self.outs = [(jax.ShapeDtypeStruct((self.size * self.share, depth), BF16), HBM)]
        self.scratch = [SEM, SEM((self.size,)), SEM((self.size,))]

    def bind(self, ins, outs, scratch):
        (self.src,), (self.dst,), (self.keep, self.send, self.recv) = ins, outs, scratch
        self.me = lax.axis_index("tensor")

    def lands(self, slot):
        return self.dst.at[pl.ds(pl.multiple_of(slot * self.share, self.share), self.share)]

    def copy(self, place, slot):
        return remote(
            self.src, self.lands(slot), self.send.at[place], self.recv.at[slot], {"tensor": place}
        )

    def start(self):
        for place in range(self.size):
            @pl.when(place != self.me)
            def _():
                self.copy(place, self.me).start()

        pltpu.make_async_copy(self.src, self.lands(self.me), self.keep).start()

    def finish(self):
        for place in range(self.size):
            @pl.when(place != self.me)
            def _():
                self.copy(place, place).wait_recv()
                self.copy(place, self.me).wait_send()

        pltpu.make_async_copy(self.src, self.lands(self.me), self.keep).wait()


class SharedRows(Part):
    def __init__(self, own):
        self.size = lax.axis_size("dp")
        self.ins = [(own, VMEM)]
        self.outs = [(jax.ShapeDtypeStruct((2, self.size) + own.shape, F32), VMEM)]
        self.scratch = [SEM((2, self.size)), SEM((2, self.size))]

    def copy(self, core, place, from_core, from_place):
        return remote(
            self.in_refs[0], self.out_refs[0].at[from_core, from_place],
            self.refs[0].at[core, place], self.refs[1].at[from_core, from_place],
            {"section": core, "dp": place},
        )

    def others(self):
        core, me = lax.axis_index("section"), lax.axis_index("dp")
        for other in range(2):
            for place in range(self.size):
                yield other, place, (other != core) | (place != me)

    def start(self):
        core, me = lax.axis_index("section"), lax.axis_index("dp")
        for other, place, is_other in self.others():
            @pl.when(is_other)
            def _():
                self.copy(other, place, core, me).start()

        self.out_refs[0][core, me] = self.in_refs[0][...]

    def finish(self):
        core, me = lax.axis_index("section"), lax.axis_index("dp")
        for other, place, is_other in self.others():
            @pl.when(is_other)
            def _():
                self.copy(other, place, other, place).wait_recv()
                self.copy(other, place, core, me).wait_send()


def far_pair(place, me):
    return (place + me == 3) & ((place == 0) | (place == 3))


def line_relays(size):
    return [(2, 0, 3), (1, 3, 0)] if size == 4 else []


def line_order(size):
    return [1, 2, 0, 3] if size == 4 else list(range(size))


class AttnShards:
    def __init__(self, w_query, w_key, w_value, w_out):
        self.arrays = [w_query, w_key, w_value, w_out]
        self.depth = w_query.shape[0]
        self.q_width, self.k_width = w_query.shape[1] // 2, w_key.shape[1] // 2
        self.width = self.q_width + 2 * self.k_width
        half = self.depth // 2
        parts = self.q_width // 2
        self.items = [
            (0, lambda ref, core: ref.at[pl.ds(0, half), columns_of(core, self.q_width)]),
            (0, lambda ref, core: ref.at[pl.ds(half, half), columns_of(core, self.q_width)]),
            (1, lambda ref, core: ref.at[:, columns_of(core, self.k_width)]),
            (2, lambda ref, core: ref.at[:, columns_of(core, self.k_width)]),
            (3, lambda ref, core: ref.at[pl.ds(core * self.q_width, parts)]),
            (3, lambda ref, core: ref.at[pl.ds(core * self.q_width + parts, parts)]),
        ]
        q_width, k_width, depth = self.q_width, self.k_width, self.depth
        self.qkv_rows = [(0, half), (half, half), (0, depth), (0, depth)]
        self.qkv_columns = [
            (0, q_width), (0, q_width), (q_width, k_width), (q_width + k_width, k_width)
        ]
        self.out_rows = [(0, parts), (parts, parts)]

    def source(self, refs, index, core):
        array, cut = self.items[index]
        return cut(refs[array], core)

    def lands(self, qkv, out, index, slot):
        if index < 4:
            (start, rows), (left, columns) = self.qkv_rows[index], self.qkv_columns[index]
            at = pl.multiple_of(slot * self.depth + start, rows)
            return qkv.at[pl.ds(at, rows), pl.ds(left, columns)]
        start, rows = self.out_rows[index - 4]
        return out.at[pl.ds(start, rows), columns_of(slot, self.depth)]


class AttnOut(Part):
    def __init__(self, shards, layer):
        self.layer, self.shards = layer, shards
        self.size = lax.axis_size("dp")
        self.count = len(shards.items)
        depth = self.size * shards.depth
        self.ins = [(array, HBM) for array in shards.arrays]
        self.outs = [
            (jax.ShapeDtypeStruct((depth, shards.width), BF16), HBM),
            (jax.ShapeDtypeStruct((shards.q_width, depth), BF16), HBM),
        ]
        self.scratch = [
            SEM((self.count,)), SEM((2, self.size, self.count)), SEM((self.size, self.count)),
            SEM((self.count,)),
        ]

    def bind(self, ins, outs, scratch):
        self.src = ins
        self.qkv, self.out = outs
        self.keep, self.send, self.recv, self.relay_send = scratch
        self.core, self.me = lax.axis_index("section"), lax.axis_index("dp")

    def lands(self, index, slot):
        return self.shards.lands(self.qkv, self.out, index, slot)

    def copy(self, core, place, slot, index):
        return remote(
            self.shards.source(self.src, index, core), self.lands(index, slot),
            self.send.at[core, place, index], self.recv.at[slot, index],
            {"section": core, "dp": place},
        )

    def relay(self, source, target, index):
        block = self.lands(index, source)
        return remote(
            block, block, self.relay_send.at[index], self.recv.at[source, index], {"dp": target}
        )

    def local(self, index):
        return pltpu.make_async_copy(
            self.shards.source(self.src, index, self.layer), self.lands(index, self.me),
            self.keep.at[index],
        )

    def targets(self):
        for index in range(self.count):
            for core in range(2):
                for place in range(self.size):
                    sent = (place != self.me) | (core != self.layer)
                    if self.size == 4:
                        sent = sent & jnp.logical_not(far_pair(place, self.me))
                    yield core, place, index, sent

    def start(self):
        @pl.when(self.core == self.layer)
        def _():
            for core, place, index, sent in self.targets():
                @pl.when(sent)
                def _():
                    self.copy(core, place, self.me, index).start()

            for index in range(self.count):
                self.local(index).start()

    def run(self):
        for index in range(self.count):
            for place in line_order(self.size):
                @pl.when((self.core != self.layer) | (place != self.me))
                def _():
                    self.copy(0, 0, place, index).wait_recv()

                for via, source, target in line_relays(self.size):
                    if source == place:
                        @pl.when(self.me == via)
                        def _():
                            self.relay(source, target, index).start()

    def finish(self):
        @pl.when(self.core == self.layer)
        def _():
            for core, place, index, sent in self.targets():
                @pl.when(sent)
                def _():
                    self.copy(core, place, self.me, index).wait_send()

            for index in range(self.count):
                self.local(index).wait()

        for via, source, target in line_relays(self.size):
            @pl.when(self.me == via)
            def _():
                for index in range(self.count):
                    self.relay(source, target, index).wait_send()


class HalfOver(Part):
    def __init__(self, shards):
        self.shards = shards
        self.count = len(shards.items)
        rows = shards.depth + shards.q_width
        self.ins = [(array, HBM) for array in shards.arrays]
        self.outs = [(jax.ShapeDtypeStruct((rows, shards.depth), BF16), HBM)]
        self.scratch = [SEM((self.count,)), SEM((self.count,)), SEM((self.count,))]

    def lands(self, index):
        depth, q_width = self.shards.depth, self.shards.q_width
        packed = self.out_refs[0]
        return self.shards.lands(
            packed.at[pl.ds(0, depth)], packed.at[pl.ds(depth, q_width)], index, 0
        )

    def over(self, index):
        return remote(
            self.shards.source(self.in_refs, index, 0), self.lands(index), self.refs[0].at[index],
            self.refs[1].at[index], {"section": 0},
        )

    def keep(self, index):
        return pltpu.make_async_copy(
            self.shards.source(self.in_refs, index, 1), self.lands(index), self.refs[2].at[index]
        )

    def start(self):
        @pl.when(lax.axis_index("section") == 1)
        def _():
            for index in range(self.count):
                self.over(index).start()
                self.keep(index).start()

    def finish(self):
        @pl.when(lax.axis_index("section") == 1)
        def _():
            for index in range(self.count):
                self.over(index).wait_send()
                self.keep(index).wait()

        @pl.when(lax.axis_index("section") == 0)
        def _():
            for index in range(self.count):
                self.over(index).wait_recv()


class Swap(Part):
    def __init__(self, own):
        self.ins = [(own, HBM)]
        self.outs = [(jax.ShapeDtypeStruct(own.shape, own.dtype), HBM)]
        self.scratch = [SEM, SEM]

    def start(self):
        sibling = 1 - lax.axis_index("section")
        self.copy = remote(
            self.in_refs[0], self.out_refs[0], self.refs[0], self.refs[1], {"section": sibling}
        )
        self.copy.start()

    def finish(self):
        self.copy.wait()


class GatherKV(Part):
    def __init__(self, own):
        trees, rows, width = own.shape
        self.trees, self.size = trees, lax.axis_size("dp")
        self.ins = [(own, VMEM)]
        self.outs = [(jax.ShapeDtypeStruct((trees, self.size, rows, width), BF16), VMEM)]
        self.scratch = [SEM((self.size, trees)), SEM((self.size, trees)), SEM((trees,))]

    def bind(self, ins, outs, scratch):
        (self.own,), (self.out,) = ins, outs
        self.send, self.recv, self.relay_send = scratch
        self.me = lax.axis_index("dp")

    def copy(self, place, slot, tree):
        return remote(
            self.own.at[tree], self.out.at[tree, slot], self.send.at[place, tree],
            self.recv.at[slot, tree], {"dp": place},
        )

    def relay(self, source, target, tree):
        return remote(
            self.out.at[tree, source], self.out.at[tree, source], self.relay_send.at[tree],
            self.recv.at[source, tree], {"dp": target},
        )

    def targets(self):
        for tree in range(self.trees):
            for place in range(self.size):
                sent = place != self.me
                if self.size == 4:
                    sent = sent & jnp.logical_not(far_pair(place, self.me))
                yield place, tree, sent

    def start(self):
        for place, tree, sent in self.targets():
            @pl.when(sent)
            def _():
                self.copy(place, self.me, tree).start()

        self.out[:, self.me] = self.own[...]

    def run(self):
        for tree in range(self.trees):
            for place in line_order(self.size):
                @pl.when(place != self.me)
                def _():
                    self.copy(place, place, tree).wait_recv()

                for via, source, target in line_relays(self.size):
                    if source == place:
                        @pl.when(self.me == via)
                        def _():
                            self.relay(source, target, tree).start()

    def finish(self):
        for place, tree, sent in self.targets():
            @pl.when(sent)
            def _():
                self.copy(place, self.me, tree).wait_send()

        for via, source, target in line_relays(self.size):
            @pl.when(self.me == via)
            def _():
                for tree in range(self.trees):
                    self.relay(source, target, tree).wait_send()


class ScatterKV(Part):
    def __init__(self, whole):
        trees, size, rows, width = whole.shape
        self.trees, self.size = trees, size
        self.sides = [(0, 1, 3), (3, 2, 0)] if size == 4 else []
        self.ins = [(whole, VMEM)]
        self.outs = [(jax.ShapeDtypeStruct((trees, rows, width), F32), VMEM)]
        self.scratch = [
            pltpu.VMEM((size, trees, rows, width), BF16), pltpu.VMEM((trees, rows, width), BF16),
            SEM((size, trees)), SEM((size, trees)), SEM((trees,)), SEM((trees,)),
        ]

    def bind(self, ins, outs, scratch):
        (self.terms,), (self.out,) = ins, outs
        self.boxes, self.joint, self.send, self.recv, self.join_send, self.join_recv = scratch
        self.me = lax.axis_index("dp")

    def copy(self, place, slot, tree):
        return remote(
            self.terms.at[tree, place], self.boxes.at[slot, tree], self.send.at[place, tree],
            self.recv.at[slot, tree], {"dp": place},
        )

    def by_way(self, via, target, tree):
        return remote(
            self.terms.at[tree, target], self.joint.at[tree], self.join_send.at[tree],
            self.join_recv.at[tree], {"dp": via},
        )

    def joined(self, via, target, tree):
        return remote(
            self.joint.at[tree], self.boxes.at[via, tree], self.send.at[target, tree],
            self.recv.at[via, tree], {"dp": target},
        )

    def plain(self, place):
        ok = place != self.me
        for source, via, target in self.sides:
            if place == target:
                ok = ok & (self.me != source) & (self.me != via)
        return ok

    def expected(self, place):
        ok = place != self.me
        for source, via, target in self.sides:
            if place == source:
                ok = ok & (self.me != target)
        return ok

    def start(self):
        for tree in range(self.trees):
            for source, via, target in self.sides:
                @pl.when(self.me == source)
                def _():
                    self.by_way(via, target, tree).start()

            for place in range(self.size):
                @pl.when(self.plain(place))
                def _():
                    self.copy(place, self.me, tree).start()

    def run(self):
        for tree in range(self.trees):
            for source, via, target in self.sides:
                @pl.when(self.me == via)
                def _():
                    self.by_way(via, target, tree).wait_recv()
                    both = self.joint[tree].astype(F32) + self.terms[tree, target].astype(F32)
                    self.joint[tree] = both.astype(BF16)
                    self.joined(via, target, tree).start()

        for tree in range(self.trees):
            self.out[tree] = self.terms[tree, self.me].astype(F32)
            for place in line_order(self.size):
                @pl.when(self.expected(place))
                def _():
                    self.copy(place, place, tree).wait_recv()
                    self.out[tree] += self.boxes[place, tree].astype(F32)

    def finish(self):
        for tree in range(self.trees):
            for place in range(self.size):
                @pl.when(self.plain(place))
                def _():
                    self.copy(place, self.me, tree).wait_send()

            for source, via, target in self.sides:
                @pl.when(self.me == source)
                def _():
                    self.by_way(via, target, tree).wait_send()

                @pl.when(self.me == via)
                def _():
                    self.joined(via, target, tree).wait_send()


class TotalOverAll(Part):
    axes = ("section", "tensor", "dp")

    def __init__(self, own):
        sizes = [lax.axis_size(axis) for axis in self.axes]
        self.ins = [(own, VMEM)]
        self.outs = [(jax.ShapeDtypeStruct(own.shape, F32), VMEM)]
        self.scratch = [pltpu.VMEM((size,) + own.shape, F32) for size in sizes]
        self.scratch += [SEM((size,)) for size in sizes] * 2

    def run(self):
        out = self.out_refs[0]
        out[...] = self.in_refs[0][...]
        for axis, box, send, recv in zip(self.axes, self.refs[:3], self.refs[3:6], self.refs[6:9]):
            size, me = lax.axis_size(axis), lax.axis_index(axis)
            box[me] = out[...]

            def spread(place, slot):
                return remote(box.at[me], box.at[slot], send.at[place], recv.at[slot], {axis: place})

            for place in range(size):
                @pl.when(place != me)
                def _():
                    spread(place, me).start()

            for place in range(size):
                @pl.when(place != me)
                def _():
                    spread(place, place).wait_recv()
                    spread(place, me).wait_send()

            total = box[0]
            for place in range(1, size):
                total += box[place]
            out[...] = total


def chunk_count(rows):
    return 3 if rows % 24 == 0 else 1


class Gatherer:
    def __init__(self, axis, rows, half):
        self.axis, self.half = axis, half
        self.size = size = lax.axis_size(axis)
        self.chunks = chunks = chunk_count(rows)
        self.rows = rows // chunks
        self.scratch = [pltpu.VMEM((2, chunks, size, 2 * self.rows, half), BF16)]
        self.scratch += [SEM((chunks, size))] * 4 + [SEM((chunks,))]

    def bind(self, refs):
        self.board, self.send, self.recv, self.sib_send, self.sib_recv, self.relay_send = refs
        self.core = lax.axis_index("section")
        self.sibling = 1 - self.core
        self.me = lax.axis_index(self.axis)
        self.relays = line_relays(self.size) if self.axis == "dp" else []
        self.order = line_order(self.size) if self.axis == "dp" else range(self.size)

    def direct(self, place):
        sent = place != self.me
        if self.relays:
            sent = sent & jnp.logical_not(far_pair(place, self.me))
        return sent

    def spread(self, chunk, place, slot):
        block = self.board.at[self.core, chunk, slot]
        return remote(
            block, block, self.send.at[chunk, place], self.recv.at[chunk, slot], {self.axis: place}
        )

    def passed(self, chunk, source, target):
        block = self.board.at[self.core, chunk, source]
        return remote(
            block, block, self.relay_send.at[chunk], self.recv.at[chunk, source],
            {self.axis: target},
        )

    def over(self, tree, chunk, slot):
        block = self.board.at[tree, chunk, slot]
        return remote(
            block, block, self.sib_send.at[chunk, slot], self.sib_recv.at[chunk, slot],
            {"section": self.sibling},
        )

    def begin(self, chunk, result):
        half = self.half
        piece = jnp.concatenate([result[:, :half], result[:, half:]], axis=0)
        self.board[self.core, chunk, self.me] = piece.astype(BF16)
        for place in range(self.size):
            @pl.when(self.direct(place))
            def _():
                self.spread(chunk, place, self.me).start()

        self.over(self.core, chunk, self.me).start()

    def arrive(self, chunk):
        for place in self.order:
            @pl.when(place != self.me)
            def _():
                self.spread(chunk, place, place).wait_recv()

            for via, source, target in self.relays:
                if source == place:
                    @pl.when(self.me == via)
                    def _():
                        self.passed(chunk, source, target).start()

            @pl.when(place != self.me)
            def _():
                self.over(self.core, chunk, place).start()

    def arrive_over(self, chunk):
        for place in range(self.size):
            self.over(self.sibling, chunk, place).wait_recv()

    def side_rows(self, block, side):
        return block[side * self.rows : (side + 1) * self.rows]

    def unpack(self, out, tree):
        @pl.loop(0, self.half // CHUNK)
        def _(step):
            at = pl.multiple_of(step * CHUNK, CHUNK)
            blocks = [
                self.board[tree, chunk, place, :, pl.ds(at, CHUNK)].astype(F32)
                for place in range(self.size)
                for chunk in range(self.chunks)
            ]
            for side in range(2):
                whole = [self.side_rows(block, side) for block in blocks]
                out[tree, :, pl.ds(side * self.half + at, CHUNK)] = jnp.concatenate(
                    whole, axis=0
                ).astype(BF16)

    def unpack_chunk(self, out, chunk):
        @pl.loop(0, self.half // CHUNK)
        def _(step):
            at = pl.multiple_of(step * CHUNK, CHUNK)
            blocks = [
                self.board[tree, chunk, place, :, pl.ds(at, CHUNK)].astype(F32)
                for place in range(self.size)
                for tree in range(2)
            ]
            for side in range(2):
                whole = [self.side_rows(block, side) for block in blocks]
                out[chunk, :, pl.ds(side * self.half + at, CHUNK)] = jnp.concatenate(
                    whole, axis=0
                ).astype(BF16)

    def complete(self, out):
        for chunk in range(self.chunks):
            self.arrive(chunk)
        self.unpack(out, self.core)
        for chunk in range(self.chunks):
            self.arrive_over(chunk)
        self.unpack(out, self.sibling)

    def finish(self):
        for chunk in range(self.chunks):
            for place in range(self.size):
                @pl.when(self.direct(place))
                def _():
                    self.spread(chunk, place, self.me).wait_send()

                self.over(self.core, chunk, place).wait_send()

            for via, source, target in self.relays:
                @pl.when(self.me == via)
                def _():
                    self.passed(chunk, source, target).wait_send()


class Scatterer:
    def __init__(self, axis, rows, half):
        self.axis, self.half = axis, half
        self.size = size = lax.axis_size(axis)
        self.chunks = chunks = chunk_count(rows)
        self.rows = rows // chunks
        block = (2 * self.rows, half)
        self.scratch = [pltpu.VMEM((chunks, size) + block, BF16)] * 4
        self.scratch += [pltpu.VMEM((chunks,) + block, F32), pltpu.VMEM((chunks,) + block, BF16)]
        self.scratch += [SEM((chunks, size))] * 4 + [SEM((chunks,))] * 2

    def bind(self, refs):
        self.to_sib, self.from_sib, self.to_peer, self.from_peer, self.total, self.joint = refs[:6]
        self.sib_send, self.sib_recv, self.peer_send, self.peer_recv = refs[6:10]
        self.join_send, self.join_recv = refs[10:]
        self.core = lax.axis_index("section")
        self.sibling = 1 - self.core
        self.me = lax.axis_index(self.axis)
        self.sides = [(0, 1, 3), (3, 2, 0)] if self.axis == "dp" and self.size == 4 else []
        self.order = [0, 3, 1, 2] if self.sides else range(self.size)

    def over(self, chunk, place):
        return remote(
            self.to_sib.at[chunk, place], self.from_sib.at[chunk, place],
            self.sib_send.at[chunk, place], self.sib_recv.at[chunk, place],
            {"section": self.sibling},
        )

    def spread(self, chunk, place, slot):
        return remote(
            self.to_peer.at[chunk, place], self.from_peer.at[chunk, slot],
            self.peer_send.at[chunk, place], self.peer_recv.at[chunk, slot], {self.axis: place},
        )

    def by_way(self, chunk, via, target):
        return remote(
            self.to_peer.at[chunk, target], self.joint.at[chunk], self.join_send.at[chunk],
            self.join_recv.at[chunk], {self.axis: via},
        )

    def plain(self, place):
        ok = place != self.me
        for source, via, target in self.sides:
            if place == target:
                ok = ok & (self.me != source) & (self.me != via)
        return ok

    def expected(self, place):
        ok = place != self.me
        for source, via, target in self.sides:
            if place == source:
                ok = ok & (self.me != target)
        return ok

    def over_columns(self, body):
        @pl.loop(0, self.half // CHUNK)
        def _(step):
            body(pl.multiple_of(step * CHUNK, CHUNK))

    def absorb(self, chunk, mine):
        for place in self.order:
            self.over(chunk, place).wait_recv()

            def add(at):
                both = mine(place, at)
                both += self.from_sib[chunk, place, :, pl.ds(at, CHUNK)].astype(F32)
                self.to_peer[chunk, place, :, pl.ds(at, CHUNK)] = both.astype(BF16)

                @pl.when(place == self.me)
                def _():
                    self.total[chunk, :, pl.ds(at, CHUNK)] = both

            self.over_columns(add)

            for source, via, target in self.sides:
                if place == target:
                    @pl.when(self.me == source)
                    def _():
                        self.by_way(chunk, via, target).start()

            @pl.when(self.plain(place))
            def _():
                self.spread(chunk, place, self.me).start()

        for source, via, target in self.sides:
            @pl.when(self.me == via)
            def _():
                self.by_way(chunk, via, target).wait_recv()

                def add(at):
                    at = pl.ds(at, CHUNK)
                    both = self.to_peer[chunk, target, :, at].astype(F32)
                    both += self.joint[chunk, :, at].astype(F32)
                    self.to_peer[chunk, target, :, at] = both.astype(BF16)

                self.over_columns(add)
                self.spread(chunk, target, self.me).start()

    def collect(self, chunk):
        for place in self.order:
            @pl.when(self.expected(place))
            def _():
                self.spread(chunk, place, place).wait_recv()
                self.total[chunk] += self.from_peer[chunk, place].astype(F32)

        total = self.total[chunk]
        return jnp.concatenate([total[: self.rows], total[self.rows :]], axis=1)

    def finish(self):
        for chunk in range(self.chunks):
            for place in range(self.size):
                self.over(chunk, place).wait_send()

                @pl.when(self.plain(place))
                def _():
                    self.spread(chunk, place, self.me).wait_send()

            for source, via, target in self.sides:
                @pl.when(self.me == source)
                def _():
                    self.by_way(chunk, via, target).wait_send()

                @pl.when(self.me == via)
                def _():
                    self.spread(chunk, target, self.me).wait_send()


class RowScatterer(Scatterer):
    def packed(self, tree, chunk, place, at):
        rows = self.rows
        first = rows * (place * self.chunks + chunk)
        low = first // 16 * 16
        high = -(-(first + rows) // 16) * 16
        parts = [
            self.terms[tree, low:high, pl.ds(side * self.half + at, CHUNK)].astype(F32)[
                first - low : first - low + rows
            ]
            for side in range(2)
        ]
        return jnp.concatenate(parts, axis=0)

    def prepare(self, terms):
        self.terms = terms
        for chunk in range(self.chunks):
            for place in range(self.size):
                def pack(at):
                    self.to_sib[chunk, place, :, pl.ds(at, CHUNK)] = self.packed(
                        self.sibling, chunk, place, at
                    ).astype(BF16)

                self.over_columns(pack)

    def start(self):
        for chunk in range(self.chunks):
            for place in range(self.size):
                self.over(chunk, place).start()

    def send_on(self):
        for chunk in range(self.chunks):
            self.absorb(chunk, lambda place, at: self.packed(self.core, chunk, place, at))


class Staged(Part):
    def __init__(self, ins, outs, scratch, helpers):
        self.in_names, self.out_names, self.scratch_names = list(ins), list(outs), list(scratch)
        self.ins, self.outs = list(ins.values()), list(outs.values())
        self.helpers = helpers
        self.scratch = list(scratch.values())
        for helper in helpers:
            self.scratch += helper.scratch

    def bind(self, ins, outs, scratch):
        scratch = list(scratch)
        names = self.in_names + self.out_names + self.scratch_names
        count = len(self.scratch_names)
        for name, ref in zip(names, list(ins) + list(outs) + scratch[:count]):
            setattr(self, name, ref)
        del scratch[:count]
        for helper in self.helpers:
            helper.bind(scratch[: len(helper.scratch)])
            del scratch[: len(helper.scratch)]

    def finish(self):
        for helper in self.helpers:
            helper.finish()


def vmem_f32(*shape):
    return (jax.ShapeDtypeStruct(shape, F32), VMEM)


def vmem_bf16(*shape):
    return (jax.ShapeDtypeStruct(shape, BF16), VMEM)


def rows_at(chunk, rows):
    return pl.ds(pl.multiple_of(chunk * rows, 8), rows)


class LastHub(Staged):
    def __init__(self, terms, values, gain, add):
        rows, depth = values.shape
        half = depth // 2
        self.rows_in = RowScatterer("tensor", rows, half)
        self.rows_out = Gatherer("tensor", rows, half)
        super().__init__(
            {"terms": (terms, VMEM), "values": (values, VMEM), "gain": (gain, VMEM), "add": (add, VMEM)},
            {
                "gain_grad": vmem_f32(1, depth),
                "gathered": vmem_bf16(2, self.rows_out.size * rows, depth),
            },
            {},
            [self.rows_in, self.rows_out],
        )

    def prepare(self):
        self.rows_in.prepare(self.terms)

    def start(self):
        self.rows_in.start()

    def run(self):
        self.rows_in.send_on()
        self.gain_grad[...] = jnp.zeros_like(self.gain_grad)
        for chunk in range(self.rows_in.chunks):
            at = rows_at(chunk, self.rows_in.rows)
            result, gain_grad = norm_back(
                self.rows_in.collect(chunk), self.values[at], self.gain[...]
            )
            self.gain_grad[...] += gain_grad
            self.rows_out.begin(chunk, result + self.add[at])
        self.rows_out.complete(self.gathered)


class RowsOut(Staged):
    def __init__(self, own):
        rows, depth = own.shape
        self.rows_out = Gatherer("tensor", rows, depth // 2)
        super().__init__(
            {"own": (own, VMEM)},
            {"gathered": vmem_bf16(2, self.rows_out.size * rows, depth)},
            {},
            [self.rows_out],
        )

    def start(self):
        for chunk in range(self.rows_out.chunks):
            self.rows_out.begin(chunk, self.own[rows_at(chunk, self.rows_out.rows)])

    def run(self):
        self.rows_out.complete(self.gathered)


class FeedForward(Staged):
    def __init__(self, terms, own, gain, weights, forward, backward, extra):
        rows, depth = own.shape
        half = depth // 2
        units = weights[0].shape[0]
        self.has_forward, self.has_backward, self.units = forward, backward, units
        self.depth = depth
        self.size = size = lax.axis_size("dp")
        self.rows_in = RowScatterer("tensor", rows, half)
        self.spread_in = Gatherer("dp", rows, half)
        self.chunks, self.rows = self.rows_in.chunks, self.rows_in.rows
        chunks, chunk_rows = self.chunks, 2 * size * self.rows
        helpers = [self.rows_in, self.spread_in]
        tensor_rows = lax.axis_size("tensor") * rows
        matrix = pltpu.VMEM((units, depth), BF16)
        ins = {"terms": (terms, VMEM), "own": (own, VMEM), "gain": (gain, VMEM)}
        ins |= {name: (w, HBM) for name, w in zip(("gate_hbm", "up_hbm", "down_hbm"), weights)}
        ins |= {name: (value, VMEM) for name, value in extra.items()}
        outs = {}
        scratch = {"w_gate": matrix, "w_up": matrix, "w_down": matrix, "load": SEM((3,))}
        kept = pltpu.VMEM((size, 2 * self.rows, half), F32)
        if forward:
            outs |= {
                "middle": vmem_f32(rows, depth),
                "mlp_in": vmem_bf16(chunks, chunk_rows, depth),
                "hidden": vmem_bf16(chunks, chunk_rows, units),
                "own_out": vmem_f32(rows, depth),
            }
            self.back = Scatterer("dp", rows, half)
            helpers += [self.back]
            scratch["kept"] = kept
        if forward and not backward:
            outs |= {
                "out": vmem_bf16(2, tensor_rows, depth),
                "gate": vmem_f32(chunks, chunk_rows, units),
                "up": vmem_f32(chunks, chunk_rows, units),
            }
            self.out_rows = Gatherer("tensor", rows, half)
            helpers += [self.out_rows]
        if forward and backward:
            outs["grad_mlp"] = vmem_bf16(chunks, chunk_rows, depth)
            self.grad_in = Gatherer("dp", rows, half)
            helpers += [self.grad_in]
            scratch |= {
                "gate": pltpu.VMEM((chunks, chunk_rows, units), F32),
                "up": pltpu.VMEM((chunks, chunk_rows, units), F32),
            }
        if backward:
            outs |= {
                "grad_gate": vmem_bf16(chunks, chunk_rows, units),
                "grad_up": vmem_bf16(chunks, chunk_rows, units),
                "grad_middle": vmem_f32(rows, depth),
                "mlp_gain_grad": vmem_f32(1, depth),
                "grad_attn": vmem_bf16(2, tensor_rows, depth),
            }
            self.grad_back = Scatterer("dp", rows, half)
            self.grad_rows = Gatherer("tensor", rows, half)
            helpers += [self.grad_back, self.grad_rows]
            scratch["grad_kept"] = kept
        if backward and not forward:
            outs |= {
                "gain_grad": vmem_f32(1, depth),
                "grad_own": vmem_f32(rows, depth),
                "grad_mlp": vmem_bf16(chunks, chunk_rows, depth),
            }
        super().__init__(ins, outs, scratch, helpers)

    def loads(self):
        pairs = [(self.gate_hbm, self.w_gate), (self.up_hbm, self.w_up), (self.down_hbm, self.w_down)]
        return [
            pltpu.make_async_copy(src, dst, self.load.at[i]) for i, (src, dst) in enumerate(pairs)
        ]

    def prepare(self):
        for copy in self.loads():
            copy.start()
        self.rows_in.prepare(self.terms)

    def start(self):
        self.rows_in.start()
        if self.has_forward and self.has_backward:
            for chunk in range(self.chunks):
                self.grad_in.begin(chunk, self.grad_own[rows_at(chunk, self.rows)])

    def run(self):
        self.rows_in.send_on()
        if self.has_backward:
            self.mlp_gain_grad[...] = jnp.zeros_like(self.mlp_gain_grad)
        if not self.has_forward:
            self.gain_grad[...] = jnp.zeros_like(self.gain_grad)
        for chunk in range(self.chunks):
            at = rows_at(chunk, self.rows)
            total = self.rows_in.collect(chunk)
            if self.has_forward:
                middle = self.own[at] + total
                self.middle[at] = middle
                mean_sq = jnp.mean(middle * middle, axis=1, keepdims=True)
                normed = middle * lax.rsqrt(mean_sq + EPSILON) * self.gain[...]
                self.spread_in.begin(chunk, normed)
            else:
                result, gain_grad = norm_back(total, self.own[at], self.gain[...])
                self.gain_grad[...] += gain_grad
                result = (result + self.add[at]).astype(BF16).astype(F32)
                self.grad_own[at] = result
                self.spread_in.begin(chunk, result)
        for copy in self.loads():
            copy.wait()

        self.spread_in.arrive(0)
        if self.has_forward and self.has_backward:
            self.grad_in.arrive(0)

        @pl.loop(0, self.chunks)
        def _(chunk):
            self.spread_in.arrive_over(chunk)
            if self.has_forward:
                self.spread_in.unpack_chunk(self.mlp_in, chunk)
                self.forward_chunk(chunk)
            else:
                self.spread_in.unpack_chunk(self.grad_mlp, chunk)
            if self.has_forward and self.has_backward:
                self.grad_in.arrive_over(chunk)
                self.grad_in.unpack_chunk(self.grad_mlp, chunk)
            if self.has_backward:
                self.backward_chunk(chunk)

            @pl.when(chunk + 1 < self.chunks)
            def _():
                self.spread_in.arrive(chunk + 1)
                if self.has_forward and self.has_backward:
                    self.grad_in.arrive(chunk + 1)

            if self.has_forward:
                self.back.absorb(chunk, lambda place, at: self.kept[place, :, pl.ds(at, CHUNK)])
            if self.has_backward:
                self.grad_back.absorb(
                    chunk, lambda place, at: self.grad_kept[place, :, pl.ds(at, CHUNK)]
                )

            @pl.when(chunk > 0)
            def _():
                self.hand_back(chunk - 1)

        self.hand_back(self.chunks - 1)
        if self.has_backward:
            self.grad_rows.complete(self.grad_attn)
        else:
            self.out_rows.complete(self.out)

    def hand_back(self, chunk):
        at = rows_at(chunk, self.rows)
        if self.has_backward:
            values = self.middle if self.has_forward else self.middle_in
            gain = self.gain if self.has_forward else self.mlp_gain
            result, gain_grad = norm_back(self.grad_back.collect(chunk), values[at], gain[...])
            self.mlp_gain_grad[...] += gain_grad
            result += self.grad_own[at]
            self.grad_middle[at] = result
            self.grad_rows.begin(chunk, result)
        if self.has_forward:
            output = (self.middle[at] + self.back.collect(chunk)).astype(BF16).astype(F32)
            self.own_out[at] = output
            if not self.has_backward:
                self.out_rows.begin(chunk, output)

    def unit_tiles(self, body):
        tile = 256

        @pl.loop(0, self.units // tile)
        def _(step):
            body(pl.ds(pl.multiple_of(step * tile, tile), tile))

    def forward_chunk(self, chunk):
        def tile(at):
            rows = self.mlp_in[chunk]
            gate = dot_inner(rows, self.w_gate[at, :])
            up = dot_inner(rows, self.w_up[at, :])
            self.gate[chunk, :, at] = gate
            self.up[chunk, :, at] = up
            self.hidden[chunk, :, at] = (gate * jax.nn.sigmoid(gate) * up).astype(BF16)

        self.unit_tiles(tile)
        self.terms_out(
            chunk, self.back, self.kept, lambda at: dot(self.hidden[chunk], self.w_down[:, at])
        )

    def backward_chunk(self, chunk):
        def tile(at):
            grad_hidden = dot_inner(self.grad_mlp[chunk], self.w_down[at, :])
            gate, up = self.gate[chunk, :, at], self.up[chunk, :, at]
            share = jax.nn.sigmoid(gate)
            act = gate * share
            self.grad_up[chunk, :, at] = (grad_hidden * act).astype(BF16)
            self.grad_gate[chunk, :, at] = (
                grad_hidden * up * (share + act * (1.0 - share))
            ).astype(BF16)

        self.unit_tiles(tile)
        self.terms_out(
            chunk, self.grad_back, self.grad_kept,
            lambda at: dot(self.grad_gate[chunk], self.w_gate[:, at])
            + dot(self.grad_up[chunk], self.w_up[:, at]),
        )

    def terms_out(self, chunk, scatterer, kept, product):
        rows, half = self.rows, self.depth // 2
        first = lax.axis_index("section") == 0

        @pl.loop(0, half // CHUNK)
        def _(step):
            low = pl.multiple_of(step * CHUNK, CHUNK)
            at = pl.ds(low, CHUNK)
            sides = [product(pl.ds(side * half + low, CHUNK)) for side in range(2)]
            for place in range(self.size):
                trees = []
                for tree in range(2):
                    start = (2 * place + tree) * rows
                    trees.append(
                        jnp.concatenate([side[start : start + rows] for side in sides], axis=0)
                    )
                kept[place, :, at] = jnp.where(first, trees[0], trees[1])
                scatterer.to_sib[chunk, place, :, at] = jnp.where(
                    first, trees[1], trees[0]
                ).astype(BF16)

        for place in range(self.size):
            scatterer.over(chunk, place).start()


def finish_units(first, second, core, tile=256):
    units, own_depth = first[0].shape

    def kernel(core_ref, *refs):
        ins, (gate, up, down) = refs[:6], refs[6:]
        rows = lax.broadcasted_iota(jnp.int32, (own_depth, own_depth), 0)
        identity = (rows == lax.broadcasted_iota(jnp.int32, rows.shape, 1)).astype(BF16)
        picked = [
            jnp.where(core_ref[0] == 0, ins[i][...], ins[3 + i][...]) for i in range(3)
        ]
        gate[...] = dot_inner(identity, picked[0])
        up[...] = dot_inner(identity, picked[1])
        down[...] = picked[2].astype(F32)

    tall = pl.BlockSpec((tile, own_depth), lambda step: (step, 0))
    wide = pl.BlockSpec((own_depth, tile), lambda step: (0, step))
    return pl.pallas_call(
        kernel,
        grid=(units // tile,),
        out_shape=[jax.ShapeDtypeStruct((own_depth, units), F32)] * 2
        + [jax.ShapeDtypeStruct((units, own_depth), F32)],
        in_specs=[pl.BlockSpec(memory_space=pltpu.SMEM)] + [tall] * 6,
        out_specs=[wide, wide, tall],
        cost_estimate=pl.CostEstimate(flops=0, bytes_accessed=25_000_000, transcendentals=0),
    )(core.reshape(1), *first, *second)


def hub_plain(terms, own_args, body, own_outs, scatter, gathers):
    total = None
    if scatter:
        mine = lax.psum_scatter(terms, "section", scatter_dimension=0, tiled=True)
        mine = lax.psum_scatter(mine, scatter, scatter_dimension=1, tiled=True)[0]
        total = mine.astype(F32)

    class Cell:
        def __setitem__(self, _, value):
            self.value = value

    cells = [Cell() for _ in own_outs]
    result = body(total, own_args, cells).astype(BF16)
    gathered = [
        lax.all_gather(lax.all_gather(result, axis, axis=0, tiled=True), "section", axis=0)
        for axis in gathers
    ]
    return [cell.value for cell in cells] + gathered


def with_cargo(part, cargo, axes, collective_id, cost_us, vmem=40):
    outs = fused(cargo + [part], axes, bool(cargo), collective_id, cost_us, vmem)
    return outs[-1], outs[:-1]


def norm_back(total, values, gain):
    scale = lax.rsqrt(jnp.mean(values * values, axis=1, keepdims=True) + EPSILON)
    unit = values * scale
    gain_grad = jnp.sum(total * unit, axis=0, keepdims=True)
    scaled = total * gain
    along = jnp.mean(scaled * unit, axis=1, keepdims=True)
    return ((scaled - unit * along) * scale, gain_grad)


def norm_body(total, args, outs):
    middle = args[0] + total
    outs[0][...] = middle
    return rms_scale(middle, args[1])


def add_body(total, args, outs):
    result = args[0] + total
    outs[0][...] = result
    return result


def norm_back_body(total, args, outs):
    result, outs[1][...] = norm_back(total, args[0], args[1])
    result += args[2]
    outs[0][...] = result
    return result


def embed(q_pre, k_pre, q_scale, k_scale, cos_table, sine_table):
    queries = rms_scale(q_pre, q_scale)
    keys = rms_scale(k_pre, k_scale)
    return (
        rotate(queries, cos_table[:, :, None], sine_table[:, :, None]),
        rotate(keys, cos_table, sine_table),
    )


def attn_forward(hidden_in, weights, gains, slot, gather):
    attn_scale, _, q_scale, k_scale = gains
    w_qkv, w_out = weights[:2]
    allowed, cos_table, sine_table = slot
    trees, row_count, depth = hidden_in.shape
    q_width = w_out.shape[0]
    normed = rms_scale(hidden_in.astype(F32), attn_scale).astype(BF16).reshape(-1, depth)
    qkv = dot(normed, w_qkv).reshape(trees, row_count, -1)
    q_pre = qkv[:, :, :q_width].reshape(trees, row_count, -1, HD)
    k_pre = qkv[:, :, q_width : q_width + HD]
    value_bf = qkv[:, :, q_width + HD :].astype(BF16)
    queries, keys_rot = embed(q_pre, k_pre, q_scale, k_scale, cos_table, sine_table)
    query_bf = queries.astype(BF16)
    kv_all = gather(jnp.concatenate([keys_rot.astype(BF16), value_bf], axis=2))
    key_all = kv_all[:, :, :HD]
    value_all = kv_all[:, :, HD:]
    scores = masked_scores(query_bf, key_all, allowed)
    row_max = jnp.max(scores, axis=-1, keepdims=True)
    exp_scores = jnp.exp(scores - row_max)
    row_total = jnp.sum(exp_scores, axis=-1, keepdims=True)
    prob_bf = (exp_scores / row_total).astype(BF16)
    log_total = row_max + jnp.log(row_total)
    attended = jnp.einsum("bgrt,btd->brgd", prob_bf, value_all, preferred_element_type=F32)
    attended_bf = attended.reshape(trees * row_count, -1).astype(BF16)
    terms = dot(attended_bf, w_out).astype(BF16).reshape(trees, row_count, depth)
    saved = (normed, q_pre, k_pre, query_bf, key_all, value_all, log_total, attended_bf)
    return (terms, saved)


def attn_backward(grad_attn, saved, weights, gains, slot, scatter):
    _, _, q_scale, k_scale = gains
    w_qkv, w_out = weights[:2]
    allowed, cos_table, sine_table = slot
    normed, q_pre, k_pre, query_bf, key_all, value_all, log_total, attended_bf = saved
    trees, row_count = query_bf.shape[:2]
    depth = normed.shape[1]
    grad_attn = grad_attn.reshape(-1, depth)
    grad_heads = dot_inner(grad_attn, w_out).astype(BF16).reshape(query_bf.shape)
    scores = masked_scores(query_bf, key_all, allowed)
    prob_full = jnp.exp(scores - log_total)
    grad_prob = jnp.einsum("brgd,btd->bgrt", grad_heads, value_all, preferred_element_type=F32)
    row_dot = jnp.sum(prob_full * grad_prob, axis=-1, keepdims=True)
    grad_scores = (prob_full * (grad_prob - row_dot)).astype(BF16)
    scale_factor = HD ** (-0.5)
    grad_query = (
        jnp.einsum("bgrt,btd->brgd", grad_scores, key_all, preferred_element_type=F32)
        * scale_factor
    )
    grad_key_all = (
        jnp.einsum("bgrt,brgd->btd", grad_scores, query_bf, preferred_element_type=F32)
        * scale_factor
    )
    grad_value_all = jnp.einsum(
        "bgrt,brgd->btd", prob_full.astype(BF16), grad_heads, preferred_element_type=F32
    )
    grad_kv = scatter(jnp.concatenate([grad_key_all, grad_value_all], axis=2).astype(BF16))
    _, embedding_pull = jax.vjp(
        partial(embed, cos_table=cos_table, sine_table=sine_table), q_pre, k_pre, q_scale, k_scale
    )
    grad_q_pre, grad_k_pre, grad_q_scale, grad_k_scale = embedding_pull(
        (grad_query, grad_kv[:, :, :HD].astype(F32))
    )
    qkv_grad = jnp.concatenate(
        [
            grad_q_pre.astype(BF16).reshape(trees, row_count, -1),
            grad_k_pre.astype(BF16),
            grad_kv[:, :, HD:].astype(BF16),
        ],
        axis=2,
    ).reshape(trees * row_count, -1)
    terms = dot_inner(qkv_grad, w_qkv).astype(BF16).reshape(trees, row_count, depth)
    return (terms, [(normed, qkv_grad), (grad_attn, attended_bf)], [grad_q_scale, grad_k_scale])


def plain_layers(hidden, own_in, grad_own, weights, gains, slot, shared_kv):
    depth = own_in.shape[1]
    own_shape = own_in.shape

    def gather(own):
        return lax.all_gather(own, "dp", axis=1, tiled=True)

    def scatter(whole):
        total = lax.psum_scatter(whole, "dp", scatter_dimension=1, tiled=True)
        if shared_kv:
            total = lax.psum(total, "section")
            total = jnp.where(lax.axis_index("section") == 0, total, jnp.zeros_like(total))
        return total

    outputs, kept = [], []
    for layer in range(2):
        _, _, w_gate, w_up, w_down = weights[layer]
        terms, saved = attn_forward(hidden, weights[layer], gains[layer], slot, gather)
        mlp_scale = gains[layer][1][None]
        middle, mlp_in = hub_plain(
            terms, [own_in, mlp_scale], norm_body, [own_shape], "tensor", ["dp"]
        )
        mlp_in = mlp_in.reshape(-1, depth)
        gate, up = dot_inner(mlp_in, w_gate), dot_inner(mlp_in, w_up)
        hidden_bf = swiglu(gate, up).astype(BF16)
        terms = dot(hidden_bf, w_down).astype(BF16).reshape(2, -1, depth)
        kept.append((own_in, saved, middle, mlp_in, gate, up, hidden_bf))
        own_in, hidden = hub_plain(terms, [middle], add_body, [own_shape], "dp", ["tensor"])
        own_in = own_in.astype(BF16).astype(F32)
        outputs.append(hidden)

    own_outs = [own_shape, (1, depth)]
    grads, products, gain_grads = [None, None], [None, None], [None, None]
    (grad_mlp,) = hub_plain(None, [grad_own], lambda total, args, outs: args[0], [], None, ["dp"])
    for layer in (1, 0):
        _, _, w_gate, w_up, w_down = weights[layer]
        own_in, saved, middle, mlp_in, gate, up, hidden_bf = kept[layer]
        grad_mlp = grad_mlp.reshape(-1, depth)
        _, pull = jax.vjp(swiglu, gate, up)
        grad_gate, grad_up = (item.astype(BF16) for item in pull(dot_inner(grad_mlp, w_down)))
        terms = (dot(grad_gate, w_gate) + dot(grad_up, w_up)).astype(BF16).reshape(2, -1, depth)
        grad_middle, mlp_gain_grad, grad_attn = hub_plain(
            terms, [middle, gains[layer][1][None], grad_own], norm_back_body, own_outs, "dp",
            ["tensor"],
        )
        terms, pairs, head_grads = attn_backward(
            grad_attn, saved, weights[layer], gains[layer], slot, scatter
        )
        grad_own, gain_grad, grads[layer], grad_next = hub_plain(
            terms, [own_in, gains[layer][0][None], grad_middle], norm_back_body, own_outs, "tensor",
            ["tensor", "dp"],
        )
        grad_own = grad_own.astype(BF16).astype(F32)
        pairs += [(grad_gate, mlp_in), (grad_up, mlp_in), (hidden_bf, grad_mlp)]
        products[layer] = pairs
        gain_grads[layer] = jnp.concatenate([gain_grad[0], mlp_gain_grad[0], *head_grads])
        grad_mlp = grad_next
    return (outputs, grads, products, gain_grads)


def swap_cores(mine, other):
    core = lax.axis_index("section")
    arrived = lax.ppermute(other, "section", [(0, 1), (1, 0)])
    return (jnp.where(core == 0, mine, arrived), jnp.where(core == 0, arrived, mine))


def on_device(
    inputs, cotangent, seg_ids, parents, order, attn_gain, w_query, w_key, w_value, w_out,
    q_gain, k_gain, mlp_gain, w_gate, w_up, w_down,
):
    core = lax.axis_index("section")
    data_index = lax.axis_index("dp")
    tensor_index = lax.axis_index("tensor")
    dp_size = lax.axis_size("dp")
    tensor_size = lax.axis_size("tensor")
    trees, row_count, depth = inputs.shape
    own_rows = row_count // tensor_size
    row_start = data_index * row_count
    own_depth = w_query.shape[1]
    q_width = w_query.shape[2] // 2
    shared_kv = w_key.shape[2] == HD
    k_width = HD if shared_kv else w_key.shape[2] // 2
    own_units = w_gate.shape[2]
    share = own_units // (2 * dp_size)

    def pick(stacked, index):
        return lax.dynamic_index_in_dim(stacked, index, 0, keepdims=False)

    fast = (
        own_rows % 8 == 0
        and depth % (2 * CHUNK) == 0
        and row_count % 16 == 0
        and share % 16 == 0
        and own_depth % 128 == 0
        and not shared_kv
    )

    def halves(width, array):
        return [array[:, :width], array[:, array.shape[1] - width :]]

    unit_mats = [w_gate[0].T, w_up[0].T, w_down[0]]
    qkv_width = q_width + 2 * k_width
    gains_own = jnp.concatenate([attn_gain[0], mlp_gain[0], q_gain[0], k_gain[0]]).astype(F32)

    def spread_units(rows):
        return lax.all_gather(rows, "tensor", axis=0, tiled=True)

    def tied(value, *before):
        return lax.optimization_barrier((value, *before))[0]

    if fast:
        line = ["section", "dp"]
        everyone = ["section", "dp", "tensor"]
        (gate_rows, up_rows), (gains_all,) = fused(
            [UnitsOut(unit_mats[:2], 0), SharedRows(gains_own.reshape(-1, 128))], line, True, 1, 45
        )
        shards = AttnShards(w_query[0], w_key[0], w_value[0], w_out[0])
        shards.arrays[0] = tied(shards.arrays[0], gate_rows)
        (w_qkv, w_heads), (down_rows,), (attn_shard,) = fused(
            [AttnOut(shards, 0), UnitsOut(unit_mats[2:], 0), HalfOver(shards)], line, True, 2, 80
        )
        first_weights = [w_qkv, w_heads, spread_units(gate_rows), spread_units(up_rows)]
        attn_next = lax.all_gather(attn_shard, "dp", axis=0)
    else:
        gains_all = lax.all_gather(gains_own, ("section", "dp"))
        attn_halves = jnp.stack(
            [
                jnp.concatenate(parts, axis=1)
                for parts in zip(
                    halves(q_width, w_query[0]),
                    halves(k_width, w_key[0]),
                    halves(k_width, w_value[0]),
                    halves(q_width, w_out[0].T),
                )
            ]
        )
        attn_shards = swap_cores(pick(attn_halves, core), pick(attn_halves, 1 - core))
        unit_blocks = jnp.stack(unit_mats).reshape(3, 2, dp_size, share, own_depth)
        unit_blocks = unit_blocks.transpose(1, 2, 0, 3, 4)
        unit_shards = swap_cores(pick(unit_blocks, core), pick(unit_blocks, 1 - core))
        both_weights = []
        for layer in range(2):
            attn_all = lax.all_gather(attn_shards[layer], "dp", axis=0, tiled=True)
            pieces = exchange(unit_shards[layer], "dp")
            pieces = pieces.transpose(1, 2, 0, 3).reshape(3, share, depth)
            both_weights.append(
                (
                    attn_all[:, :qkv_width], attn_all[:, qkv_width:].T,
                    *(spread_units(pieces[i]) for i in range(3)),
                )
            )

    gains_all = gains_all.reshape(2, dp_size, -1)
    gains = [
        (
            gains_all[layer, :, :own_depth].reshape(depth),
            gains_all[layer, :, own_depth : 2 * own_depth].reshape(depth),
            gains_all[layer, 0, 2 * own_depth : 2 * own_depth + HD],
            gains_all[layer, 0, 2 * own_depth + HD :],
        )
        for layer in range(2)
    ]

    def slot_setup(slot_index):
        tree_id = pick(order, slot_index)
        allowed, row_positions = path_mask(
            pick(seg_ids, tree_id), pick(parents, tree_id), row_start, row_count
        )
        cos_table, sine_table = rope_tables(row_positions, HD)
        return (pick(inputs, tree_id), allowed, cos_table[:, 0], sine_table[:, 0])

    setups = [slot_setup(i) for i in range(trees)]
    hidden, *slot = (jnp.stack(item) for item in zip(*setups))

    def own_part(whole):
        return lax.dynamic_slice_in_dim(
            pick(whole, core), tensor_index * own_rows, own_rows, 0
        )

    own_in = own_part(hidden).astype(F32)
    grad_own = own_part(cotangent).astype(F32)

    def weight_products(pairs):
        return [dot_outer(left, right).astype(BF16) for left, right in pairs]

    def scatter_units(products):
        return [
            lax.psum_scatter(item, "tensor", scatter_dimension=0, tiled=True) for item in products
        ]

    def scatter_shards(products):
        return lax.psum_scatter(
            jnp.concatenate(products, axis=1), "dp", scatter_dimension=0, tiled=True
        )

    if fast:
        def units_on(*which):
            return [UnitsOut([unit_mats[i] for i in which], 1)]

        def kv_gather(own, cargo, collective_id, carried):
            (whole,), outs = with_cargo(GatherKV(own), cargo, everyone, collective_id, 40)
            carried += outs
            return whole.reshape(trees, -1, 2 * HD)

        def kv_scatter(whole, cargo, collective_id, carried):
            part = ScatterKV(whole.reshape(trees, dp_size, row_count, 2 * HD))
            (total,), outs = with_cargo(part, cargo, everyone, collective_id, 30)
            carried += outs
            return total

        def in_order(pairs):
            done = []
            for left, right in pairs:
                done += weight_products([(tied(left, *done[-1:]), right)])
            return done

        def flat(array):
            return array.reshape(-1, array.shape[-1])

        carried = []
        terms, saved_first = attn_forward(
            hidden, first_weights, gains[0], slot,
            lambda own: kv_gather(
                tied(own, *first_weights[2:]), [UnitsSpread(down_rows)] + units_on(0, 1), 3, carried
            ),
        )
        (down_all,), (gate_rows, up_rows) = carried
        first_weights.append(down_all)
        part = FeedForward(
            terms, own_in, gains[0][1][None], first_weights[2:], True, False, {}
        )
        outs, ((down_rows,),) = with_cargo(part, units_on(2), everyone, 4, 90, 56)
        middle_first, mlp_in_first, hidden_first, own_next, output_first, gate_first, up_first = outs
        second_weights = [
            attn_next[:, :own_depth].reshape(depth, -1),
            attn_next[:, own_depth:].transpose(1, 0, 2).reshape(q_width, depth),
            spread_units(gate_rows), spread_units(up_rows),
        ]
        carried = []
        terms, saved_second = attn_forward(
            output_first, second_weights, gains[1], slot,
            lambda own: kv_gather(
                tied(own, second_weights[2]), [UnitsSpread(down_rows)], 5, carried
            ),
        )
        ((down_all,),) = carried
        second_weights.append(down_all)
        part = FeedForward(
            terms, own_next, gains[1][1][None], second_weights[2:], True, True,
            {"grad_own": grad_own},
        )
        outs, _ = with_cargo(part, [], everyone, 6, 100, 60)
        (
            middle, mlp_in, hidden_bf, own_second, grad_mlp,
            grad_gate, grad_up, grad_middle, mlp_gain_second, grad_attn,
        ) = outs
        products = in_order([(flat(grad_gate), flat(mlp_in)), (flat(grad_up), flat(mlp_in))])
        unit_second = scatter_units(products)
        carried = []
        terms, pairs, head_second = attn_backward(
            grad_attn, saved_second, second_weights, gains[1], slot,
            lambda whole: kv_scatter(
                tied(whole, *products), [RowsOut(own_second)], 7, carried
            ),
        )
        ((output_second,),) = carried
        unit_second += scatter_units(
            weight_products([(tied(flat(hidden_bf), output_second), flat(grad_mlp))])
        )
        pairs = weight_products(pairs)
        attn_second = scatter_shards([tied(pairs[0], unit_second[2]), pairs[1]])
        terms = tied(terms, unit_second[0])
        part = FeedForward(
            terms, own_next, gains[1][0][None], first_weights[2:], False, True,
            {
                "add": grad_middle, "gate": gate_first, "up": up_first,
                "middle_in": middle_first, "mlp_gain": gains[0][1][None],
            },
        )
        outs, _ = with_cargo(part, [], everyone, 8, 90, 60)
        (
            grad_gate, grad_up, grad_middle, mlp_gain_first, grad_attn,
            attn_gain_second, own_incoming, grad_mlp,
        ) = outs
        products = in_order(
            [(flat(grad_gate), flat(mlp_in_first)), (flat(grad_up), flat(mlp_in_first))]
        )
        grad_attn = tied(grad_attn, *unit_second[1:], *products)
        unit_first = scatter_units(products)
        carried = []
        terms, pairs, head_first = attn_backward(
            grad_attn, saved_first, first_weights, gains[0], slot,
            lambda whole: kv_scatter(
                whole, [UnitsHome(unit_second, 1), RowsOut(own_incoming)], 9, carried
            ),
        )
        home_second, (incoming_second,) = carried
        unit_first += scatter_units(
            weight_products([(tied(flat(hidden_first), incoming_second), flat(grad_mlp))])
        )
        whole = jnp.concatenate(weight_products(pairs), axis=1).reshape(dp_size, 4, -1, q_width + qkv_width)
        part = LastHub(terms, own_in, gains[0][0][None], grad_middle)
        (attn_gain_first, incoming_first), ((attn_first,), home_first) = with_cargo(
            part, [ScatterKV(whole.transpose(1, 0, 2, 3)), UnitsHome(unit_first[:2], 0)], everyone,
            10, 60, 56,
        )
        attn_first = attn_first.reshape(own_depth, -1).astype(BF16)
        outputs = [output_first, output_second]
        grads = [incoming_first, incoming_second]
        weight_grads = [(attn_first, None), (attn_second, None)]
        gain_grads = [
            jnp.concatenate([attn_gain_first[0], mlp_gain_first[0], *head_first]),
            jnp.concatenate([attn_gain_second[0], mlp_gain_second[0], *head_second]),
        ]
    else:
        outputs, grads, products, gain_grads = plain_layers(
            hidden, own_in, grad_own, both_weights, gains, slot, shared_kv
        )
        weight_grads = []
        for pairs in products:
            whole = weight_products(pairs)
            weight_grads.append((scatter_shards(whole[:2]), scatter_units(whole[2:])))

    gain_total = jnp.stack(gain_grads)
    if fast:
        mine = jnp.where(core == 0, weight_grads[0][0], weight_grads[1][0])
        other = jnp.where(core == 0, weight_grads[1][0], weight_grads[0][0])
        (gain_total,), (arrived,), down_home = fused(
            [TotalOverAll(gain_total.reshape(-1, 128)), Swap(other), UnitsHome(unit_first[2:], 0)],
            everyone, True, 11, 60,
        )
        attn_home = (jnp.where(core == 0, mine, arrived), jnp.where(core == 0, arrived, mine))
        grad_gate, grad_up, grad_down = finish_units(home_first + down_home, home_second, core)
        gain_total = gain_total.reshape(2, -1)
    else:
        def bring_home(first, second):
            mine, other = jnp.where(core == 0, first, second), jnp.where(core == 0, second, first)
            arrived = lax.ppermute(other, "section", [(0, 1), (1, 0)])
            return (jnp.where(core == 0, mine, arrived), jnp.where(core == 0, arrived, mine))

        def pieces_of(grad):
            return exchange(
                jnp.stack(grad).reshape(3, share, dp_size, own_depth).transpose(2, 0, 1, 3), "dp"
            )

        attn_home = bring_home(weight_grads[0][0], weight_grads[1][0])
        unit_home = jnp.stack(bring_home(pieces_of(weight_grads[0][1]), pieces_of(weight_grads[1][1])))
        unit_home = unit_home.transpose(2, 0, 1, 3, 4).reshape(3, own_units, own_depth).astype(F32)
        grad_gate, grad_up, grad_down = unit_home[0].T, unit_home[1].T, unit_home[2]
        gain_total = lax.psum(gain_total, ("section", "dp", "tensor"))

    def joined(start, width):
        parts = [half[:, start : start + width] for half in attn_home]
        if shared_kv and start in (q_width, q_width + k_width):
            return parts[0].astype(F32)
        return jnp.concatenate(parts, axis=1).astype(F32)

    gain_own = pick(gain_total, core)
    share_width = attn_gain.shape[1]
    attn_gain_grad = lax.dynamic_slice_in_dim(gain_own, data_index * share_width, share_width, 0)
    mlp_gain_grad = lax.dynamic_slice_in_dim(
        gain_own, depth + data_index * share_width, share_width, 0
    )
    return (
        jnp.where(core == 0, outputs[0], outputs[1])[None],
        jnp.where(core == 0, grads[0], grads[1])[None],
        attn_gain_grad[None],
        joined(0, q_width)[None],
        joined(q_width, k_width)[None],
        joined(q_width + k_width, k_width)[None],
        joined(qkv_width, q_width).T[None],
        gain_own[2 * depth : 2 * depth + HD][None],
        gain_own[2 * depth + HD :][None],
        mlp_gain_grad[None],
        grad_gate[None],
        grad_up[None],
        grad_down[None],
    )


def solution(mesh):
    rows = P(None, "dp", None)
    wide = P("section", "dp", "tensor")
    tall = P("section", "tensor", "dp")
    gain = P("section", "dp")
    head_gain = P("section", None)
    slots = P("section", None, "dp", None)
    in_specs = (
        rows, rows, P(), P(), P(), gain, wide, wide, wide, tall, head_gain, head_gain, gain,
        wide, wide, tall,
    )
    out_specs = (
        slots, slots, gain, wide, wide, wide, tall, head_gain, head_gain, gain, wide, wide, tall,
    )
    return jax.shard_map(
        on_device, mesh=mesh, in_specs=in_specs, out_specs=out_specs, check_vma=False
    )
```

```python
from functools import partial

import jax
import jax.numpy as jnp
from jax import lax
from jax.experimental import pallas as pl
from jax.experimental.pallas import tpu as pltpu
from jax.sharding import PartitionSpec as P

HD = 128
TRUNK = 512
BRANCH = 96
NB = 4
TREE = 1152
SEGS = 9


EPSILON = 1e-06
THETA = 1000000.0
MASKED = -1e30
F32 = jnp.float32
BF16 = jnp.bfloat16


def rms_scale(values, weight_gain):
    mean_sq = jnp.mean(values * values, axis=-1, keepdims=True)
    return values * lax.rsqrt(mean_sq + EPSILON) * weight_gain


def rotate(values, cos_table, sine_table):
    middle_at = values.shape[-1] // 2
    leading = values[..., :middle_at]
    trailing = values[..., middle_at:]
    return jnp.concatenate(
        [leading * cos_table - trailing * sine_table, trailing * cos_table + leading * sine_table],
        axis=-1,
    )


def rope_tables(positions, head_dim):
    half_steps = jnp.arange(head_dim // 2, dtype=F32)
    inverse = THETA ** (-2.0 * half_steps / head_dim)
    angles = positions.astype(F32)[:, None] * inverse[None, :]
    return (jnp.cos(angles)[:, None, :], jnp.sin(angles)[:, None, :])


def swiglu(gate_in, up_in):
    return jax.nn.silu(gate_in) * up_in


def embed_heads(q_pre, k_pre, q_scale, k_scale, cos_table, sine_table):
    row_count = q_pre.shape[0]
    queries = rms_scale(q_pre.reshape(row_count, -1, HD), q_scale)
    keys_part = rms_scale(k_pre.reshape(row_count, -1, HD), k_scale)
    return (rotate(queries, cos_table, sine_table), rotate(keys_part, cos_table, sine_table))


def tree_layout(seg_row, parent_row):
    labels = jnp.arange(SEGS, dtype=jnp.int32)
    places = jnp.arange(TREE, dtype=jnp.int32)
    member = seg_row[None, :] == labels[:, None]
    starts = jnp.min(jnp.where(member, places[None, :], TREE), axis=1)
    depth_base = jnp.where(labels == 0, 0, jnp.where(labels <= NB, TRUNK, TRUNK + BRANCH))
    shifts = depth_base - starts
    positions = places + jnp.sum(jnp.where(member, shifts[:, None], 0), axis=0)
    grandparent = jnp.sum(
        jnp.where(parent_row[:, None] == labels[None, :], parent_row[None, :], 0), axis=1
    )
    ancestor = (
        (labels[None, :] == labels[:, None])
        | (labels[None, :] == parent_row[:, None])
        | (labels[None, :] == grandparent[:, None])
    )
    return (positions, member.astype(F32), ancestor.astype(F32))


def path_mask(seg_row, parent_row, row_start, row_count):
    positions, member, ancestor = tree_layout(seg_row, parent_row)
    member_rows = lax.dynamic_slice_in_dim(member, row_start, row_count, 1)
    seg_rows = lax.dynamic_slice_in_dim(seg_row, row_start, row_count, 0)
    reach_table = jnp.dot(jnp.dot(member_rows.T, ancestor), member)
    places = jnp.arange(TREE, dtype=jnp.int32)
    row_places = row_start + jnp.arange(row_count, dtype=jnp.int32)
    same_seg = seg_rows[:, None] == seg_row[None, :]
    causal = places[None, :] <= row_places[:, None]
    allowed = (reach_table > 0.5) & (jnp.logical_not(same_seg) | causal)
    row_positions = lax.dynamic_slice_in_dim(positions, row_start, row_count, 0)
    return (allowed, row_positions)


OUTER = (((0,), (0,)), ((), ()))
INNER = (((1,), (1,)), ((), ()))


def dot(left, right):
    return jnp.dot(left, right, preferred_element_type=F32)


def dot_inner(left, right):
    return lax.dot_general(left, right, INNER, preferred_element_type=F32)


def dot_outer(left, right):
    return lax.dot_general(left, right, OUTER, preferred_element_type=F32)


def exchange(pieces, axis):
    size = lax.axis_size(axis)
    me = lax.axis_index(axis)
    got = jnp.zeros_like(pieces)
    own = lax.dynamic_index_in_dim(pieces, me, 0, keepdims=True)
    got = lax.dynamic_update_slice_in_dim(got, own, me, 0)
    for step in range(1, size):
        other = me ^ step
        piece = lax.dynamic_index_in_dim(pieces, other, 0, keepdims=True)
        arrived = lax.ppermute(piece, axis, [(i, i ^ step) for i in range(size)])
        got = lax.dynamic_update_slice_in_dim(got, arrived, other, 0)
    return got


def masked_scores(query_bf, key_all, allowed):
    raw_scores = jnp.einsum(
        "brgd,btd->bgrt", query_bf, key_all, preferred_element_type=F32
    ) * HD ** (-0.5)
    return jnp.where(allowed[:, None], raw_scores, MASKED)


MESH = pl.DeviceIdType.MESH
CHUNK = 256
SEM = pltpu.SemaphoreType.DMA
VMEM = pl.BlockSpec(memory_space=pltpu.VMEM)
HBM = pl.BlockSpec(memory_space=pl.ANY)


def remote(src, dst, send_sem, recv_sem, device_id):
    return pltpu.make_async_remote_copy(
        src_ref=src, dst_ref=dst, send_sem=send_sem, recv_sem=recv_sem,
        device_id=device_id, device_id_type=MESH,
    )


def greet(axes, across):
    barrier = pltpu.get_barrier_semaphore()
    count = 0
    for axis in axes:
        size = lax.axis_size(axis)
        me = lax.axis_index(axis)
        for step in range(1, size):
            pl.semaphore_signal(
                barrier, inc=1, device_id={axis: lax.rem(me + step, size)}, device_id_type=MESH
            )
        count += size - 1
    if across:
        size = lax.axis_size("dp")
        me = lax.axis_index("dp")
        sibling = 1 - lax.axis_index("section")
        for step in range(1, size):
            pl.semaphore_signal(
                barrier, inc=1, device_id={"section": sibling, "dp": lax.rem(me + step, size)},
                device_id_type=MESH,
            )
        count += size - 1
    pl.semaphore_wait(barrier, count)


class Part:
    ins, outs, scratch = (), (), ()

    def bind(self, ins, outs, scratch):
        self.in_refs, self.out_refs, self.refs = ins, outs, scratch

    def prepare(self):
        pass

    def start(self):
        pass

    def run(self):
        pass

    def finish(self):
        pass


def fused(parts, axes, across, collective_id, cost_us, vmem):
    counts = [(len(part.ins), len(part.outs), len(part.scratch)) for part in parts]

    def kernel(*refs):
        refs = list(refs)
        groups = []
        for kind in range(3):
            groups.append([])
            for count in counts:
                groups[kind].append(refs[: count[kind]])
                del refs[: count[kind]]
        for part, ins, outs, scratch in zip(parts, *groups):
            part.bind(ins, outs, scratch)
        for part in parts:
            part.prepare()
        greet(axes, across)
        for part in parts:
            part.start()
        for part in reversed(parts):
            part.run()
        for part in parts:
            part.finish()

    ins = [item for part in parts for item in part.ins]
    outs = [item for part in parts for item in part.outs]
    results = pl.pallas_call(
        kernel,
        out_shape=[item[0] for item in outs],
        in_specs=[item[1] for item in ins],
        out_specs=[item[1] for item in outs],
        scratch_shapes=[item for part in parts for item in part.scratch],
        cost_estimate=pl.CostEstimate(
            flops=0, bytes_accessed=cost_us * 3_000_000, transcendentals=0
        ),
        compiler_params=pltpu.CompilerParams(
            collective_id=collective_id, has_side_effects=True, vmem_limit_bytes=vmem << 20
        ),
    )(*[item[0] for item in ins])
    results = list(results)
    split = []
    for count in counts:
        split.append(results[: count[1]])
        del results[: count[1]]
    return split


def columns_of(place, width):
    return pl.ds(pl.multiple_of(place * width, width), width)


class UnitsOut(Part):
    def __init__(self, mats, layer):
        self.layer, self.count = layer, len(mats)
        self.size = lax.axis_size("dp")
        rows, self.width = mats[0].shape
        self.share = rows // (2 * self.size)
        self.ins = [(mat, HBM) for mat in mats]
        shape = jax.ShapeDtypeStruct((self.share, self.size * self.width), BF16)
        self.outs = [(shape, HBM)] * self.count
        self.scratch = [SEM((self.count,)), SEM((self.count, 2, self.size)), SEM((self.count, self.size))]

    def bind(self, ins, outs, scratch):
        self.src, self.dst = ins, outs
        self.keep, self.send, self.recv = scratch
        self.core, self.me = lax.axis_index("section"), lax.axis_index("dp")

    def piece(self, index, core, place):
        start = pl.multiple_of((core * self.size + place) * self.share, self.share)
        return self.src[index].at[pl.ds(start, self.share)]

    def lands(self, index, slot):
        return self.dst[index].at[:, columns_of(slot, self.width)]

    def copy(self, index, core, place, slot):
        return remote(
            self.piece(index, core, place), self.lands(index, slot),
            self.send.at[index, core, place], self.recv.at[index, slot],
            {"section": core, "dp": place},
        )

    def local(self, index):
        return pltpu.make_async_copy(
            self.piece(index, self.layer, self.me), self.lands(index, self.me), self.keep.at[index]
        )

    def targets(self):
        for index in range(self.count):
            for core in range(2):
                for place in range(self.size):
                    yield index, core, place, (place != self.me) | (core != self.layer)

    def start(self):
        @pl.when(self.core == self.layer)
        def _():
            for index, core, place, is_other in self.targets():
                @pl.when(is_other)
                def _():
                    self.copy(index, core, place, self.me).start()

            for index in range(self.count):
                self.local(index).start()

    def finish(self):
        for index in range(self.count):
            for place in range(self.size):
                @pl.when((self.core != self.layer) | (place != self.me))
                def _():
                    self.copy(index, 0, 0, place).wait_recv()

        @pl.when(self.core == self.layer)
        def _():
            for index, core, place, is_other in self.targets():
                @pl.when(is_other)
                def _():
                    self.copy(index, core, place, self.me).wait_send()

            for index in range(self.count):
                self.local(index).wait()


class UnitsHome(Part):
    def __init__(self, mats, layer):
        self.layer, self.count = layer, len(mats)
        self.size = lax.axis_size("dp")
        self.share, depth = mats[0].shape
        self.width = depth // self.size
        self.ins = [(mat, HBM) for mat in mats]
        shape = jax.ShapeDtypeStruct((2 * self.size * self.share, self.width), BF16)
        self.outs = [(shape, HBM)] * self.count
        self.scratch = [SEM((self.count,)), SEM((self.count, self.size)), SEM((self.count, 2, self.size))]

    def bind(self, ins, outs, scratch):
        self.src, self.dst = ins, outs
        self.keep, self.send, self.recv = scratch
        self.core, self.me = lax.axis_index("section"), lax.axis_index("dp")

    def lands(self, index, core, slot):
        start = pl.multiple_of((core * self.size + slot) * self.share, self.share)
        return self.dst[index].at[pl.ds(start, self.share)]

    def copy(self, index, place, core, slot):
        return remote(
            self.src[index].at[:, columns_of(place, self.width)], self.lands(index, core, slot),
            self.send.at[index, place], self.recv.at[index, core, slot],
            {"section": self.layer, "dp": place},
        )

    def local(self, index):
        return pltpu.make_async_copy(
            self.src[index].at[:, columns_of(self.me, self.width)],
            self.lands(index, self.layer, self.me), self.keep.at[index],
        )

    def start(self):
        for index in range(self.count):
            for place in range(self.size):
                @pl.when((self.core != self.layer) | (place != self.me))
                def _():
                    self.copy(index, place, self.core, self.me).start()

            @pl.when(self.core == self.layer)
            def _():
                self.local(index).start()

    def finish(self):
        for index in range(self.count):
            @pl.when(self.core == self.layer)
            def _():
                for core in range(2):
                    for place in range(self.size):
                        @pl.when((core != self.layer) | (place != self.me))
                        def _():
                            self.copy(index, 0, core, place).wait_recv()

                self.local(index).wait()

            for place in range(self.size):
                @pl.when((self.core != self.layer) | (place != self.me))
                def _():
                    self.copy(index, place, self.core, self.me).wait_send()


class UnitsSpread(Part):
    def __init__(self, rows):
        self.size = lax.axis_size("tensor")
        self.share, depth = rows.shape
        self.ins = [(rows, HBM)]
        self.outs = [(jax.ShapeDtypeStruct((self.size * self.share, depth), BF16), HBM)]
        self.scratch = [SEM, SEM((self.size,)), SEM((self.size,))]

    def bind(self, ins, outs, scratch):
        (self.src,), (self.dst,), (self.keep, self.send, self.recv) = ins, outs, scratch
        self.me = lax.axis_index("tensor")

    def lands(self, slot):
        return self.dst.at[pl.ds(pl.multiple_of(slot * self.share, self.share), self.share)]

    def copy(self, place, slot):
        return remote(
            self.src, self.lands(slot), self.send.at[place], self.recv.at[slot], {"tensor": place}
        )

    def start(self):
        for place in range(self.size):
            @pl.when(place != self.me)
            def _():
                self.copy(place, self.me).start()

        pltpu.make_async_copy(self.src, self.lands(self.me), self.keep).start()

    def finish(self):
        for place in range(self.size):
            @pl.when(place != self.me)
            def _():
                self.copy(place, place).wait_recv()
                self.copy(place, self.me).wait_send()

        pltpu.make_async_copy(self.src, self.lands(self.me), self.keep).wait()


class SharedRows(Part):
    def __init__(self, own):
        self.size = lax.axis_size("dp")
        self.ins = [(own, VMEM)]
        self.outs = [(jax.ShapeDtypeStruct((2, self.size) + own.shape, F32), VMEM)]
        self.scratch = [SEM((2, self.size)), SEM((2, self.size))]

    def copy(self, core, place, from_core, from_place):
        return remote(
            self.in_refs[0], self.out_refs[0].at[from_core, from_place],
            self.refs[0].at[core, place], self.refs[1].at[from_core, from_place],
            {"section": core, "dp": place},
        )

    def others(self):
        core, me = lax.axis_index("section"), lax.axis_index("dp")
        for other in range(2):
            for place in range(self.size):
                yield other, place, (other != core) | (place != me)

    def start(self):
        core, me = lax.axis_index("section"), lax.axis_index("dp")
        for other, place, is_other in self.others():
            @pl.when(is_other)
            def _():
                self.copy(other, place, core, me).start()

        self.out_refs[0][core, me] = self.in_refs[0][...]

    def finish(self):
        core, me = lax.axis_index("section"), lax.axis_index("dp")
        for other, place, is_other in self.others():
            @pl.when(is_other)
            def _():
                self.copy(other, place, other, place).wait_recv()
                self.copy(other, place, core, me).wait_send()


def far_pair(place, me):
    return (place + me == 3) & ((place == 0) | (place == 3))


def line_relays(size):
    return [(2, 0, 3), (1, 3, 0)] if size == 4 else []


def line_order(size):
    return [1, 2, 0, 3] if size == 4 else list(range(size))


class AttnShards:
    def __init__(self, w_query, w_key, w_value, w_out):
        self.arrays = [w_query, w_key, w_value, w_out]
        self.depth = w_query.shape[0]
        self.q_width, self.k_width = w_query.shape[1] // 2, w_key.shape[1] // 2
        self.width = self.q_width + 2 * self.k_width
        half = self.depth // 2
        parts = self.q_width // 2
        self.items = [
            (0, lambda ref, core: ref.at[pl.ds(0, half), columns_of(core, self.q_width)]),
            (0, lambda ref, core: ref.at[pl.ds(half, half), columns_of(core, self.q_width)]),
            (1, lambda ref, core: ref.at[:, columns_of(core, self.k_width)]),
            (2, lambda ref, core: ref.at[:, columns_of(core, self.k_width)]),
            (3, lambda ref, core: ref.at[pl.ds(core * self.q_width, parts)]),
            (3, lambda ref, core: ref.at[pl.ds(core * self.q_width + parts, parts)]),
        ]
        q_width, k_width, depth = self.q_width, self.k_width, self.depth
        self.qkv_rows = [(0, half), (half, half), (0, depth), (0, depth)]
        self.qkv_columns = [
            (0, q_width), (0, q_width), (q_width, k_width), (q_width + k_width, k_width)
        ]
        self.out_rows = [(0, parts), (parts, parts)]

    def source(self, refs, index, core):
        array, cut = self.items[index]
        return cut(refs[array], core)

    def lands(self, qkv, out, index, slot):
        if index < 4:
            (start, rows), (left, columns) = self.qkv_rows[index], self.qkv_columns[index]
            at = pl.multiple_of(slot * self.depth + start, rows)
            return qkv.at[pl.ds(at, rows), pl.ds(left, columns)]
        start, rows = self.out_rows[index - 4]
        return out.at[pl.ds(start, rows), columns_of(slot, self.depth)]


class AttnOut(Part):
    def __init__(self, shards, layer):
        self.layer, self.shards = layer, shards
        self.size = lax.axis_size("dp")
        self.count = len(shards.items)
        depth = self.size * shards.depth
        self.ins = [(array, HBM) for array in shards.arrays]
        self.outs = [
            (jax.ShapeDtypeStruct((depth, shards.width), BF16), HBM),
            (jax.ShapeDtypeStruct((shards.q_width, depth), BF16), HBM),
        ]
        self.scratch = [
            SEM((self.count,)), SEM((2, self.size, self.count)), SEM((self.size, self.count)),
            SEM((self.count,)),
        ]

    def bind(self, ins, outs, scratch):
        self.src = ins
        self.qkv, self.out = outs
        self.keep, self.send, self.recv, self.relay_send = scratch
        self.core, self.me = lax.axis_index("section"), lax.axis_index("dp")

    def lands(self, index, slot):
        return self.shards.lands(self.qkv, self.out, index, slot)

    def copy(self, core, place, slot, index):
        return remote(
            self.shards.source(self.src, index, core), self.lands(index, slot),
            self.send.at[core, place, index], self.recv.at[slot, index],
            {"section": core, "dp": place},
        )

    def relay(self, source, target, index):
        block = self.lands(index, source)
        return remote(
            block, block, self.relay_send.at[index], self.recv.at[source, index], {"dp": target}
        )

    def local(self, index):
        return pltpu.make_async_copy(
            self.shards.source(self.src, index, self.layer), self.lands(index, self.me),
            self.keep.at[index],
        )

    def targets(self):
        for index in range(self.count):
            for core in range(2):
                for place in range(self.size):
                    sent = (place != self.me) | (core != self.layer)
                    if self.size == 4:
                        sent = sent & jnp.logical_not(far_pair(place, self.me))
                    yield core, place, index, sent

    def start(self):
        @pl.when(self.core == self.layer)
        def _():
            for core, place, index, sent in self.targets():
                @pl.when(sent)
                def _():
                    self.copy(core, place, self.me, index).start()

            for index in range(self.count):
                self.local(index).start()

    def run(self):
        for index in range(self.count):
            for place in line_order(self.size):
                @pl.when((self.core != self.layer) | (place != self.me))
                def _():
                    self.copy(0, 0, place, index).wait_recv()

                for via, source, target in line_relays(self.size):
                    if source == place:
                        @pl.when(self.me == via)
                        def _():
                            self.relay(source, target, index).start()

    def finish(self):
        @pl.when(self.core == self.layer)
        def _():
            for core, place, index, sent in self.targets():
                @pl.when(sent)
                def _():
                    self.copy(core, place, self.me, index).wait_send()

            for index in range(self.count):
                self.local(index).wait()

        for via, source, target in line_relays(self.size):
            @pl.when(self.me == via)
            def _():
                for index in range(self.count):
                    self.relay(source, target, index).wait_send()


class HalfOver(Part):
    def __init__(self, shards):
        self.shards = shards
        self.count = len(shards.items)
        rows = shards.depth + shards.q_width
        self.ins = [(array, HBM) for array in shards.arrays]
        self.outs = [(jax.ShapeDtypeStruct((rows, shards.depth), BF16), HBM)]
        self.scratch = [SEM((self.count,)), SEM((self.count,)), SEM((self.count,))]

    def lands(self, index):
        depth, q_width = self.shards.depth, self.shards.q_width
        packed = self.out_refs[0]
        return self.shards.lands(
            packed.at[pl.ds(0, depth)], packed.at[pl.ds(depth, q_width)], index, 0
        )

    def over(self, index):
        return remote(
            self.shards.source(self.in_refs, index, 0), self.lands(index), self.refs[0].at[index],
            self.refs[1].at[index], {"section": 0},
        )

    def keep(self, index):
        return pltpu.make_async_copy(
            self.shards.source(self.in_refs, index, 1), self.lands(index), self.refs[2].at[index]
        )

    def start(self):
        @pl.when(lax.axis_index("section") == 1)
        def _():
            for index in range(self.count):
                self.over(index).start()
                self.keep(index).start()

    def finish(self):
        @pl.when(lax.axis_index("section") == 1)
        def _():
            for index in range(self.count):
                self.over(index).wait_send()
                self.keep(index).wait()

        @pl.when(lax.axis_index("section") == 0)
        def _():
            for index in range(self.count):
                self.over(index).wait_recv()


class Swap(Part):
    def __init__(self, own):
        self.ins = [(own, HBM)]
        self.outs = [(jax.ShapeDtypeStruct(own.shape, own.dtype), HBM)]
        self.scratch = [SEM, SEM]

    def start(self):
        sibling = 1 - lax.axis_index("section")
        self.copy = remote(
            self.in_refs[0], self.out_refs[0], self.refs[0], self.refs[1], {"section": sibling}
        )
        self.copy.start()

    def finish(self):
        self.copy.wait()


class GatherKV(Part):
    def __init__(self, own):
        trees, rows, width = own.shape
        self.trees, self.size = trees, lax.axis_size("dp")
        self.ins = [(own, VMEM)]
        self.outs = [(jax.ShapeDtypeStruct((trees, self.size, rows, width), BF16), VMEM)]
        self.scratch = [SEM((self.size, trees)), SEM((self.size, trees)), SEM((trees,))]

    def bind(self, ins, outs, scratch):
        (self.own,), (self.out,) = ins, outs
        self.send, self.recv, self.relay_send = scratch
        self.me = lax.axis_index("dp")

    def copy(self, place, slot, tree):
        return remote(
            self.own.at[tree], self.out.at[tree, slot], self.send.at[place, tree],
            self.recv.at[slot, tree], {"dp": place},
        )

    def relay(self, source, target, tree):
        return remote(
            self.out.at[tree, source], self.out.at[tree, source], self.relay_send.at[tree],
            self.recv.at[source, tree], {"dp": target},
        )

    def targets(self):
        for tree in range(self.trees):
            for place in range(self.size):
                sent = place != self.me
                if self.size == 4:
                    sent = sent & jnp.logical_not(far_pair(place, self.me))
                yield place, tree, sent

    def start(self):
        for place, tree, sent in self.targets():
            @pl.when(sent)
            def _():
                self.copy(place, self.me, tree).start()

        self.out[:, self.me] = self.own[...]

    def run(self):
        for tree in range(self.trees):
            for place in line_order(self.size):
                @pl.when(place != self.me)
                def _():
                    self.copy(place, place, tree).wait_recv()

                for via, source, target in line_relays(self.size):
                    if source == place:
                        @pl.when(self.me == via)
                        def _():
                            self.relay(source, target, tree).start()

    def finish(self):
        for place, tree, sent in self.targets():
            @pl.when(sent)
            def _():
                self.copy(place, self.me, tree).wait_send()

        for via, source, target in line_relays(self.size):
            @pl.when(self.me == via)
            def _():
                for tree in range(self.trees):
                    self.relay(source, target, tree).wait_send()


class ScatterKV(Part):
    def __init__(self, whole, place_first=False, kept_as=F32):
        self.place_first = place_first
        trees, size, rows, width = whole.shape
        if place_first:
            trees, size = size, trees
        self.trees, self.size = trees, size
        self.sides = [(0, 1, 3), (3, 2, 0)] if size == 4 else []
        self.ins = [(whole, VMEM)]
        self.outs = [(jax.ShapeDtypeStruct((trees, rows, width), kept_as), VMEM)]
        self.scratch = [
            pltpu.VMEM((rows, width), F32),
            pltpu.VMEM((size, trees, rows, width), BF16), pltpu.VMEM((trees, rows, width), BF16),
            SEM((size, trees)), SEM((size, trees)), SEM((trees,)), SEM((trees,)),
        ]

    def bind(self, ins, outs, scratch):
        (self.terms,), (self.out,) = ins, outs
        self.total, self.boxes, self.joint, self.send, self.recv, self.join_send, self.join_recv = scratch
        self.me = lax.axis_index("dp")

    def term(self, tree, place):
        return self.terms.at[place, tree] if self.place_first else self.terms.at[tree, place]

    def copy(self, place, slot, tree):
        return remote(
            self.term(tree, place), self.boxes.at[slot, tree], self.send.at[place, tree],
            self.recv.at[slot, tree], {"dp": place},
        )

    def by_way(self, via, target, tree):
        return remote(
            self.term(tree, target), self.joint.at[tree], self.join_send.at[tree],
            self.join_recv.at[tree], {"dp": via},
        )

    def joined(self, via, target, tree):
        return remote(
            self.joint.at[tree], self.boxes.at[via, tree], self.send.at[target, tree],
            self.recv.at[via, tree], {"dp": target},
        )

    def plain(self, place):
        ok = place != self.me
        for source, via, target in self.sides:
            if place == target:
                ok = ok & (self.me != source) & (self.me != via)
        return ok

    def expected(self, place):
        ok = place != self.me
        for source, via, target in self.sides:
            if place == source:
                ok = ok & (self.me != target)
        return ok

    def start(self):
        for tree in range(self.trees):
            for source, via, target in self.sides:
                @pl.when(self.me == source)
                def _():
                    self.by_way(via, target, tree).start()

            for place in range(self.size):
                @pl.when(self.plain(place))
                def _():
                    self.copy(place, self.me, tree).start()

    def run(self):
        for tree in range(self.trees):
            for source, via, target in self.sides:
                @pl.when(self.me == via)
                def _():
                    self.by_way(via, target, tree).wait_recv()
                    both = self.joint[tree].astype(F32) + self.term(tree, target)[...].astype(F32)
                    self.joint[tree] = both.astype(BF16)
                    self.joined(via, target, tree).start()

        for tree in range(self.trees):
            self.total[...] = self.term(tree, self.me)[...].astype(F32)
            for place in line_order(self.size):
                @pl.when(self.expected(place))
                def _():
                    self.copy(place, place, tree).wait_recv()
                    self.total[...] += self.boxes[place, tree].astype(F32)

            self.out[tree] = self.total[...].astype(self.out.dtype)

    def finish(self):
        for tree in range(self.trees):
            for place in range(self.size):
                @pl.when(self.plain(place))
                def _():
                    self.copy(place, self.me, tree).wait_send()

            for source, via, target in self.sides:
                @pl.when(self.me == source)
                def _():
                    self.by_way(via, target, tree).wait_send()

                @pl.when(self.me == via)
                def _():
                    self.joined(via, target, tree).wait_send()


class TotalOverAll(Part):
    axes = ("section", "tensor", "dp")

    def __init__(self, own):
        sizes = [lax.axis_size(axis) for axis in self.axes]
        self.ins = [(own, VMEM)]
        self.outs = [(jax.ShapeDtypeStruct(own.shape, F32), VMEM)]
        self.scratch = [pltpu.VMEM((size,) + own.shape, F32) for size in sizes]
        self.scratch += [SEM((size,)) for size in sizes] * 2

    def run(self):
        out = self.out_refs[0]
        out[...] = self.in_refs[0][...]
        for axis, box, send, recv in zip(self.axes, self.refs[:3], self.refs[3:6], self.refs[6:9]):
            size, me = lax.axis_size(axis), lax.axis_index(axis)
            box[me] = out[...]

            def spread(place, slot):
                return remote(box.at[me], box.at[slot], send.at[place], recv.at[slot], {axis: place})

            for place in range(size):
                @pl.when(place != me)
                def _():
                    spread(place, me).start()

            for place in range(size):
                @pl.when(place != me)
                def _():
                    spread(place, place).wait_recv()
                    spread(place, me).wait_send()

            total = box[0]
            for place in range(1, size):
                total += box[place]
            out[...] = total


def chunk_count(rows):
    return 3 if rows % 24 == 0 else 1


class Gatherer:
    def __init__(self, axis, rows, half):
        self.axis, self.half = axis, half
        self.size = size = lax.axis_size(axis)
        self.chunks = chunks = chunk_count(rows)
        self.rows = rows // chunks
        self.scratch = [pltpu.VMEM((2, chunks, size, 2 * self.rows, half), BF16)]
        self.scratch += [SEM((chunks, size))] * 4 + [SEM((chunks,))]

    def bind(self, refs):
        self.board, self.send, self.recv, self.sib_send, self.sib_recv, self.relay_send = refs
        self.core = lax.axis_index("section")
        self.sibling = 1 - self.core
        self.me = lax.axis_index(self.axis)
        self.relays = line_relays(self.size) if self.axis == "dp" else []
        self.order = line_order(self.size) if self.axis == "dp" else range(self.size)

    def direct(self, place):
        sent = place != self.me
        if self.relays:
            sent = sent & jnp.logical_not(far_pair(place, self.me))
        return sent

    def spread(self, chunk, place, slot):
        block = self.board.at[self.core, chunk, slot]
        return remote(
            block, block, self.send.at[chunk, place], self.recv.at[chunk, slot], {self.axis: place}
        )

    def passed(self, chunk, source, target):
        block = self.board.at[self.core, chunk, source]
        return remote(
            block, block, self.relay_send.at[chunk], self.recv.at[chunk, source],
            {self.axis: target},
        )

    def over(self, tree, chunk, slot):
        block = self.board.at[tree, chunk, slot]
        return remote(
            block, block, self.sib_send.at[chunk, slot], self.sib_recv.at[chunk, slot],
            {"section": self.sibling},
        )

    def begin(self, chunk, result):
        half = self.half
        piece = jnp.concatenate([result[:, :half], result[:, half:]], axis=0)
        self.board[self.core, chunk, self.me] = piece.astype(BF16)
        for place in range(self.size):
            @pl.when(self.direct(place))
            def _():
                self.spread(chunk, place, self.me).start()

        self.over(self.core, chunk, self.me).start()

    def arrive(self, chunk):
        for place in self.order:
            @pl.when(place != self.me)
            def _():
                self.spread(chunk, place, place).wait_recv()

            for via, source, target in self.relays:
                if source == place:
                    @pl.when(self.me == via)
                    def _():
                        self.passed(chunk, source, target).start()

            @pl.when(place != self.me)
            def _():
                self.over(self.core, chunk, place).start()

    def arrive_over(self, chunk):
        for place in range(self.size):
            self.over(self.sibling, chunk, place).wait_recv()

    def side_rows(self, block, side):
        return block[side * self.rows : (side + 1) * self.rows]

    def unpack(self, out, tree):
        @pl.loop(0, self.half // CHUNK)
        def _(step):
            at = pl.multiple_of(step * CHUNK, CHUNK)
            blocks = [
                self.board[tree, chunk, place, :, pl.ds(at, CHUNK)].astype(F32)
                for place in range(self.size)
                for chunk in range(self.chunks)
            ]
            for side in range(2):
                whole = [self.side_rows(block, side) for block in blocks]
                out[tree, :, pl.ds(side * self.half + at, CHUNK)] = jnp.concatenate(
                    whole, axis=0
                ).astype(BF16)

    def unpack_chunk(self, out, chunk):
        @pl.loop(0, self.half // CHUNK)
        def _(step):
            at = pl.multiple_of(step * CHUNK, CHUNK)
            blocks = [
                self.board[tree, chunk, place, :, pl.ds(at, CHUNK)].astype(F32)
                for place in range(self.size)
                for tree in range(2)
            ]
            for side in range(2):
                whole = [self.side_rows(block, side) for block in blocks]
                out[chunk, :, pl.ds(side * self.half + at, CHUNK)] = jnp.concatenate(
                    whole, axis=0
                ).astype(BF16)

    def complete(self, out):
        for chunk in range(self.chunks):
            self.arrive(chunk)
        self.unpack(out, self.core)
        for chunk in range(self.chunks):
            self.arrive_over(chunk)
        self.unpack(out, self.sibling)

    def finish(self):
        for chunk in range(self.chunks):
            for place in range(self.size):
                @pl.when(self.direct(place))
                def _():
                    self.spread(chunk, place, self.me).wait_send()

                self.over(self.core, chunk, place).wait_send()

            for via, source, target in self.relays:
                @pl.when(self.me == via)
                def _():
                    self.passed(chunk, source, target).wait_send()


class Scatterer:
    def __init__(self, axis, rows, half):
        self.axis, self.half = axis, half
        self.size = size = lax.axis_size(axis)
        self.chunks = chunks = chunk_count(rows)
        self.rows = rows // chunks
        block = (2 * self.rows, half)
        self.scratch = [pltpu.VMEM((chunks, size) + block, BF16)] * 4
        self.scratch += [pltpu.VMEM((chunks,) + block, F32), pltpu.VMEM((chunks,) + block, BF16)]
        self.scratch += [SEM((chunks, size))] * 4 + [SEM((chunks,))] * 2

    def bind(self, refs):
        self.to_sib, self.from_sib, self.to_peer, self.from_peer, self.total, self.joint = refs[:6]
        self.sib_send, self.sib_recv, self.peer_send, self.peer_recv = refs[6:10]
        self.join_send, self.join_recv = refs[10:]
        self.core = lax.axis_index("section")
        self.sibling = 1 - self.core
        self.me = lax.axis_index(self.axis)
        self.sides = [(0, 1, 3), (3, 2, 0)] if self.axis == "dp" and self.size == 4 else []
        self.order = [0, 3, 1, 2] if self.sides else range(self.size)

    def over(self, chunk, place):
        return remote(
            self.to_sib.at[chunk, place], self.from_sib.at[chunk, place],
            self.sib_send.at[chunk, place], self.sib_recv.at[chunk, place],
            {"section": self.sibling},
        )

    def spread(self, chunk, place, slot):
        return remote(
            self.to_peer.at[chunk, place], self.from_peer.at[chunk, slot],
            self.peer_send.at[chunk, place], self.peer_recv.at[chunk, slot], {self.axis: place},
        )

    def by_way(self, chunk, via, target):
        return remote(
            self.to_peer.at[chunk, target], self.joint.at[chunk], self.join_send.at[chunk],
            self.join_recv.at[chunk], {self.axis: via},
        )

    def plain(self, place):
        ok = place != self.me
        for source, via, target in self.sides:
            if place == target:
                ok = ok & (self.me != source) & (self.me != via)
        return ok

    def expected(self, place):
        ok = place != self.me
        for source, via, target in self.sides:
            if place == source:
                ok = ok & (self.me != target)
        return ok

    def over_columns(self, body):
        @pl.loop(0, self.half // CHUNK)
        def _(step):
            body(pl.multiple_of(step * CHUNK, CHUNK))

    def absorb(self, chunk, mine):
        for place in self.order:
            self.over(chunk, place).wait_recv()

            def add(at):
                both = mine(place, at)
                both += self.from_sib[chunk, place, :, pl.ds(at, CHUNK)].astype(F32)
                self.to_peer[chunk, place, :, pl.ds(at, CHUNK)] = both.astype(BF16)

                @pl.when(place == self.me)
                def _():
                    self.total[chunk, :, pl.ds(at, CHUNK)] = both

            self.over_columns(add)

            for source, via, target in self.sides:
                if place == target:
                    @pl.when(self.me == source)
                    def _():
                        self.by_way(chunk, via, target).start()

            @pl.when(self.plain(place))
            def _():
                self.spread(chunk, place, self.me).start()

        for source, via, target in self.sides:
            @pl.when(self.me == via)
            def _():
                self.by_way(chunk, via, target).wait_recv()

                def add(at):
                    at = pl.ds(at, CHUNK)
                    both = self.to_peer[chunk, target, :, at].astype(F32)
                    both += self.joint[chunk, :, at].astype(F32)
                    self.to_peer[chunk, target, :, at] = both.astype(BF16)

                self.over_columns(add)
                self.spread(chunk, target, self.me).start()

    def collect(self, chunk):
        for place in self.order:
            @pl.when(self.expected(place))
            def _():
                self.spread(chunk, place, place).wait_recv()
                self.total[chunk] += self.from_peer[chunk, place].astype(F32)

        total = self.total[chunk]
        return jnp.concatenate([total[: self.rows], total[self.rows :]], axis=1)

    def finish(self):
        for chunk in range(self.chunks):
            for place in range(self.size):
                self.over(chunk, place).wait_send()

                @pl.when(self.plain(place))
                def _():
                    self.spread(chunk, place, self.me).wait_send()

            for source, via, target in self.sides:
                @pl.when(self.me == source)
                def _():
                    self.by_way(chunk, via, target).wait_send()

                @pl.when(self.me == via)
                def _():
                    self.spread(chunk, target, self.me).wait_send()


class RowScatterer(Scatterer):
    def packed(self, tree, chunk, place, at):
        rows = self.rows
        first = rows * (place * self.chunks + chunk)
        low = first // 16 * 16
        high = -(-(first + rows) // 16) * 16
        parts = [
            self.terms[tree, low:high, pl.ds(side * self.half + at, CHUNK)].astype(F32)[
                first - low : first - low + rows
            ]
            for side in range(2)
        ]
        return jnp.concatenate(parts, axis=0)

    def prepare(self, terms):
        self.terms = terms
        for chunk in range(self.chunks):
            for place in range(self.size):
                def pack(at):
                    self.to_sib[chunk, place, :, pl.ds(at, CHUNK)] = self.packed(
                        self.sibling, chunk, place, at
                    ).astype(BF16)

                self.over_columns(pack)

    def start(self):
        for chunk in range(self.chunks):
            for place in range(self.size):
                self.over(chunk, place).start()

    def send_on(self):
        for chunk in range(self.chunks):
            self.absorb(chunk, lambda place, at: self.packed(self.core, chunk, place, at))


class Staged(Part):
    def __init__(self, ins, outs, scratch, helpers):
        self.in_names, self.out_names, self.scratch_names = list(ins), list(outs), list(scratch)
        self.ins, self.outs = list(ins.values()), list(outs.values())
        self.helpers = helpers
        self.scratch = list(scratch.values())
        for helper in helpers:
            self.scratch += helper.scratch

    def bind(self, ins, outs, scratch):
        scratch = list(scratch)
        names = self.in_names + self.out_names + self.scratch_names
        count = len(self.scratch_names)
        for name, ref in zip(names, list(ins) + list(outs) + scratch[:count]):
            setattr(self, name, ref)
        del scratch[:count]
        for helper in self.helpers:
            helper.bind(scratch[: len(helper.scratch)])
            del scratch[: len(helper.scratch)]

    def finish(self):
        for helper in self.helpers:
            helper.finish()


def vmem_f32(*shape):
    return (jax.ShapeDtypeStruct(shape, F32), VMEM)


def vmem_bf16(*shape):
    return (jax.ShapeDtypeStruct(shape, BF16), VMEM)


def rows_at(chunk, rows):
    return pl.ds(pl.multiple_of(chunk * rows, 8), rows)


class LastHub(Staged):
    def __init__(self, terms, values, gain, add, other):
        rows, depth = values.shape
        half = depth // 2
        self.rows_in = RowScatterer("tensor", rows, half)
        self.rows_out = Gatherer("tensor", rows, half)
        super().__init__(
            {
                "terms": (terms, VMEM), "values": (values, VMEM), "gain": (gain, VMEM),
                "add": (add, VMEM), "other": (other, VMEM),
            },
            {
                "gain_grad": vmem_f32(1, depth),
                "gathered": vmem_bf16(2, self.rows_out.size * rows, depth),
            },
            {},
            [self.rows_in, self.rows_out],
        )

    def prepare(self):
        self.rows_in.prepare(self.terms)

    def start(self):
        self.rows_in.start()

    def run(self):
        self.rows_in.send_on()
        self.gain_grad[...] = jnp.zeros_like(self.gain_grad)
        for chunk in range(self.rows_in.chunks):
            at = rows_at(chunk, self.rows_in.rows)
            result, gain_grad = norm_back(
                self.rows_in.collect(chunk), self.values[at], self.gain[...]
            )
            self.gain_grad[...] += gain_grad
            self.rows_out.begin(chunk, result + self.add[at])
        self.rows_out.complete(self.gathered)

        @pl.when(lax.axis_index("section") == 1)
        def _():
            self.gathered[...] = self.other[...]


class RowsOut(Staged):
    def __init__(self, own, other=None):
        rows, depth = own.shape
        self.rows_out = Gatherer("tensor", rows, depth // 2)
        self.has_other = other is not None
        super().__init__(
            {"own": (own, VMEM)} | ({"other": (other, VMEM)} if self.has_other else {}),
            {"gathered": vmem_bf16(2, self.rows_out.size * rows, depth)},
            {},
            [self.rows_out],
        )

    def start(self):
        for chunk in range(self.rows_out.chunks):
            self.rows_out.begin(chunk, self.own[rows_at(chunk, self.rows_out.rows)])

    def run(self):
        self.rows_out.complete(self.gathered)
        if self.has_other:
            @pl.when(lax.axis_index("section") == 0)
            def _():
                self.gathered[...] = self.other[...]


class FeedForward(Staged):
    def __init__(self, terms, own, gain, weights, forward, backward, extra):
        rows, depth = own.shape
        half = depth // 2
        units = weights[0].shape[0]
        self.has_forward, self.has_backward, self.units = forward, backward, units
        self.depth = depth
        self.size = size = lax.axis_size("dp")
        self.rows_in = RowScatterer("tensor", rows, half)
        self.spread_in = Gatherer("dp", rows, half)
        self.chunks, self.rows = self.rows_in.chunks, self.rows_in.rows
        chunks, chunk_rows = self.chunks, 2 * size * self.rows
        helpers = [self.rows_in, self.spread_in]
        tensor_rows = lax.axis_size("tensor") * rows
        matrix = pltpu.VMEM((units, depth), BF16)
        ins = {"terms": (terms, VMEM), "own": (own, VMEM), "gain": (gain, VMEM)}
        ins |= {name: (w, HBM) for name, w in zip(("gate_hbm", "up_hbm", "down_hbm"), weights)}
        ins |= {name: (value, VMEM) for name, value in extra.items()}
        outs = {}
        scratch = {"w_gate": matrix, "w_up": matrix, "w_down": matrix, "load": SEM((3,))}
        kept = pltpu.VMEM((size, 2 * self.rows, half), F32)
        if forward:
            outs |= {
                "middle": vmem_f32(rows, depth),
                "mlp_in": vmem_bf16(chunks, chunk_rows, depth),
                "hidden": vmem_bf16(chunks, chunk_rows, units),
                "own_out": vmem_f32(rows, depth),
            }
            self.back = Scatterer("dp", rows, half)
            helpers += [self.back]
            scratch["kept"] = kept
        if forward and not backward:
            outs |= {
                "out": vmem_bf16(2, tensor_rows, depth),
                "gate": vmem_bf16(chunks, chunk_rows, units),
                "up": vmem_bf16(chunks, chunk_rows, units),
            }
            self.out_rows = Gatherer("tensor", rows, half)
            helpers += [self.out_rows]
        if forward and backward:
            outs["grad_mlp"] = vmem_bf16(chunks, chunk_rows, depth)
            self.grad_in = Gatherer("dp", rows, half)
            helpers += [self.grad_in]
            scratch |= {
                "gate": pltpu.VMEM((chunks, chunk_rows, units), F32),
                "up": pltpu.VMEM((chunks, chunk_rows, units), F32),
            }
        if backward:
            outs |= {
                "grad_gate": vmem_bf16(chunks, chunk_rows, units),
                "grad_up": vmem_bf16(chunks, chunk_rows, units),
                "grad_middle": vmem_f32(rows, depth),
                "mlp_gain_grad": vmem_f32(1, depth),
                "grad_attn": vmem_bf16(2, tensor_rows, depth),
            }
            self.grad_back = Scatterer("dp", rows, half)
            self.grad_rows = Gatherer("tensor", rows, half)
            helpers += [self.grad_back, self.grad_rows]
            scratch["grad_kept"] = kept
        if backward and not forward:
            outs |= {
                "gain_grad": vmem_f32(1, depth),
                "grad_own": vmem_f32(rows, depth),
                "grad_mlp": vmem_bf16(chunks, chunk_rows, depth),
            }
        super().__init__(ins, outs, scratch, helpers)

    def loads(self):
        pairs = [(self.gate_hbm, self.w_gate), (self.up_hbm, self.w_up), (self.down_hbm, self.w_down)]
        return [
            pltpu.make_async_copy(src, dst, self.load.at[i]) for i, (src, dst) in enumerate(pairs)
        ]

    def prepare(self):
        for copy in self.loads():
            copy.start()
        self.rows_in.prepare(self.terms)

    def start(self):
        self.rows_in.start()
        if self.has_forward and self.has_backward:
            for chunk in range(self.chunks):
                self.grad_in.begin(chunk, self.grad_own[rows_at(chunk, self.rows)])

    def run(self):
        self.rows_in.send_on()
        if self.has_backward:
            self.mlp_gain_grad[...] = jnp.zeros_like(self.mlp_gain_grad)
        if not self.has_forward:
            self.gain_grad[...] = jnp.zeros_like(self.gain_grad)
        for chunk in range(self.chunks):
            at = rows_at(chunk, self.rows)
            total = self.rows_in.collect(chunk)
            if self.has_forward:
                middle = self.own[at] + total
                self.middle[at] = middle
                mean_sq = jnp.mean(middle * middle, axis=1, keepdims=True)
                normed = middle * lax.rsqrt(mean_sq + EPSILON) * self.gain[...]
                self.spread_in.begin(chunk, normed)
            else:
                result, gain_grad = norm_back(total, self.own[at], self.gain[...])
                self.gain_grad[...] += gain_grad
                result = (result + self.add[at]).astype(BF16).astype(F32)
                self.grad_own[at] = result
                self.spread_in.begin(chunk, result)
        for copy in self.loads():
            copy.wait()

        self.spread_in.arrive(0)
        if self.has_forward and self.has_backward:
            self.grad_in.arrive(0)

        @pl.loop(0, self.chunks)
        def _(chunk):
            self.spread_in.arrive_over(chunk)
            if self.has_forward:
                self.spread_in.unpack_chunk(self.mlp_in, chunk)
                self.forward_chunk(chunk)
            else:
                self.spread_in.unpack_chunk(self.grad_mlp, chunk)
            if self.has_forward and self.has_backward:
                self.grad_in.arrive_over(chunk)
                self.grad_in.unpack_chunk(self.grad_mlp, chunk)
            if self.has_backward:
                self.backward_chunk(chunk)

            @pl.when(chunk + 1 < self.chunks)
            def _():
                self.spread_in.arrive(chunk + 1)
                if self.has_forward and self.has_backward:
                    self.grad_in.arrive(chunk + 1)

            if self.has_forward:
                self.back.absorb(chunk, lambda place, at: self.kept[place, :, pl.ds(at, CHUNK)])
            if self.has_backward:
                self.grad_back.absorb(
                    chunk, lambda place, at: self.grad_kept[place, :, pl.ds(at, CHUNK)]
                )

            @pl.when(chunk > 0)
            def _():
                self.hand_back(chunk - 1)

        self.hand_back(self.chunks - 1)
        if self.has_backward:
            self.grad_rows.complete(self.grad_attn)
        else:
            self.out_rows.complete(self.out)

    def hand_back(self, chunk):
        at = rows_at(chunk, self.rows)
        if self.has_backward:
            values = self.middle if self.has_forward else self.middle_in
            gain = self.gain if self.has_forward else self.mlp_gain
            result, gain_grad = norm_back(self.grad_back.collect(chunk), values[at], gain[...])
            self.mlp_gain_grad[...] += gain_grad
            result += self.grad_own[at]
            self.grad_middle[at] = result
            self.grad_rows.begin(chunk, result)
        if self.has_forward:
            output = (self.middle[at] + self.back.collect(chunk)).astype(BF16).astype(F32)
            self.own_out[at] = output
            if not self.has_backward:
                self.out_rows.begin(chunk, output)

    def unit_tiles(self, body):
        tile = 256

        @pl.loop(0, self.units // tile)
        def _(step):
            body(pl.ds(pl.multiple_of(step * tile, tile), tile))

    def forward_chunk(self, chunk):
        def tile(at):
            rows = self.mlp_in[chunk]
            gate = dot_inner(rows, self.w_gate[at, :])
            up = dot_inner(rows, self.w_up[at, :])
            self.gate[chunk, :, at] = gate.astype(self.gate.dtype)
            self.up[chunk, :, at] = up.astype(self.up.dtype)
            self.hidden[chunk, :, at] = (gate * jax.nn.sigmoid(gate) * up).astype(BF16)

        self.unit_tiles(tile)
        self.terms_out(
            chunk, self.back, self.kept, lambda at: dot(self.hidden[chunk], self.w_down[:, at])
        )

    def backward_chunk(self, chunk):
        def tile(at):
            grad_hidden = dot_inner(self.grad_mlp[chunk], self.w_down[at, :])
            gate, up = self.gate[chunk, :, at].astype(F32), self.up[chunk, :, at].astype(F32)
            share = jax.nn.sigmoid(gate)
            act = gate * share
            self.grad_up[chunk, :, at] = (grad_hidden * act).astype(BF16)
            self.grad_gate[chunk, :, at] = (
                grad_hidden * up * (share + act * (1.0 - share))
            ).astype(BF16)

        self.unit_tiles(tile)
        self.terms_out(
            chunk, self.grad_back, self.grad_kept,
            lambda at: dot(self.grad_gate[chunk], self.w_gate[:, at])
            + dot(self.grad_up[chunk], self.w_up[:, at]),
        )

    def terms_out(self, chunk, scatterer, kept, product):
        rows, half = self.rows, self.depth // 2
        first = lax.axis_index("section") == 0

        @pl.loop(0, half // CHUNK)
        def _(step):
            low = pl.multiple_of(step * CHUNK, CHUNK)
            at = pl.ds(low, CHUNK)
            sides = [product(pl.ds(side * half + low, CHUNK)) for side in range(2)]
            for place in range(self.size):
                trees = []
                for tree in range(2):
                    start = (2 * place + tree) * rows
                    trees.append(
                        jnp.concatenate([side[start : start + rows] for side in sides], axis=0)
                    )
                kept[place, :, at] = jnp.where(first, trees[0], trees[1])
                scatterer.to_sib[chunk, place, :, at] = jnp.where(
                    first, trees[1], trees[0]
                ).astype(BF16)

        for place in range(self.size):
            scatterer.over(chunk, place).start()


def finish_weights(first, second, attn_first, attn_second, arrived, widths, core, rows_out, tile=256):
    units, own_depth = first[0].shape
    q_width, k_width, _, _ = widths
    starts = [0, q_width, q_width + k_width, 0]
    steps = units // tile
    count = len(rows_out)

    def transposed(block):
        size = block.shape[1]
        rows = lax.broadcasted_iota(jnp.int32, (size, size), 0)
        identity = (rows == lax.broadcasted_iota(jnp.int32, rows.shape, 1)).astype(BF16)
        return dot_inner(identity, block)

    def kernel(core_ref, *refs):
        ins, passed_in = refs[:12], refs[12 : 12 + count]
        (gate, up, down), attn_outs = refs[12 + count : 15 + count], refs[15 + count : 19 + count]
        for src, dst in zip(passed_in, refs[19 + count :]):
            dst[...] = src[...]

        on_first = core_ref[0] == 0
        picked = [jnp.where(on_first, ins[i][...], ins[3 + i][...]) for i in range(3)]
        gate[...] = transposed(picked[0])
        up[...] = transposed(picked[1])
        down[...] = picked[2].astype(F32)

        @pl.when(pl.program_id(0) == 0)
        def _():
            for index, (out, start, width) in enumerate(zip(attn_outs, starts, widths)):
                at = pl.ds(start, width)
                mine, other, came = (ins[6 + 2 * i + index // 3][:, at] for i in range(3))
                halves = [jnp.where(on_first, mine, came), jnp.where(on_first, came, other)]
                for half, values in enumerate(halves):
                    if index == 3:
                        out[pl.ds(half * width, width)] = transposed(values)
                    else:
                        out[:, pl.ds(half * width, width)] = values.astype(F32)

    def whole(shape):
        return pl.BlockSpec(shape, lambda step: (0, 0))

    tall = pl.BlockSpec((tile, own_depth), lambda step: (step, 0))
    wide = pl.BlockSpec((own_depth, tile), lambda step: (0, step))
    attn_ins = [*attn_first, *attn_second, *arrived]
    flat_rows = [item.reshape(-1, item.shape[-1]) for item in rows_out]
    passed = [
        pl.BlockSpec((item.shape[0] // steps, item.shape[1]), lambda step: (step, 0))
        for item in flat_rows
    ]
    attn_shapes = [(own_depth, 2 * width) for width in widths[:3]] + [(2 * q_width, own_depth)]
    shapes = [(own_depth, units)] * 2 + [(units, own_depth)] + attn_shapes
    return pl.pallas_call(
        kernel,
        grid=(steps,),
        out_shape=[jax.ShapeDtypeStruct(shape, F32) for shape in shapes]
        + [jax.ShapeDtypeStruct(item.shape, item.dtype) for item in flat_rows],
        in_specs=[pl.BlockSpec(memory_space=pltpu.SMEM)]
        + [tall] * 6
        + [whole(item.shape) for item in attn_ins]
        + passed,
        out_specs=[wide, wide, tall] + [whole(shape) for shape in attn_shapes] + passed,
        cost_estimate=pl.CostEstimate(flops=0, bytes_accessed=25_000_000, transcendentals=0),
        compiler_params=pltpu.CompilerParams(vmem_limit_bytes=60 << 20),
    )(core.reshape(1), *first, *second, *attn_ins, *flat_rows)


def hub_plain(terms, own_args, body, own_outs, scatter, gathers):
    total = None
    if scatter:
        mine = lax.psum_scatter(terms, "section", scatter_dimension=0, tiled=True)
        mine = lax.psum_scatter(mine, scatter, scatter_dimension=1, tiled=True)[0]
        total = mine.astype(F32)

    class Cell:
        def __setitem__(self, _, value):
            self.value = value

    cells = [Cell() for _ in own_outs]
    result = body(total, own_args, cells).astype(BF16)
    gathered = [
        lax.all_gather(lax.all_gather(result, axis, axis=0, tiled=True), "section", axis=0)
        for axis in gathers
    ]
    return [cell.value for cell in cells] + gathered


def with_cargo(part, cargo, axes, collective_id, cost_us, vmem):
    outs = fused(cargo + [part], axes, bool(cargo), collective_id, cost_us, vmem)
    return outs[-1], outs[:-1]


def norm_back(total, values, gain):
    scale = lax.rsqrt(jnp.mean(values * values, axis=1, keepdims=True) + EPSILON)
    unit = values * scale
    gain_grad = jnp.sum(total * unit, axis=0, keepdims=True)
    scaled = total * gain
    along = jnp.mean(scaled * unit, axis=1, keepdims=True)
    return ((scaled - unit * along) * scale, gain_grad)


def norm_body(total, args, outs):
    middle = args[0] + total
    outs[0][...] = middle
    return rms_scale(middle, args[1])


def add_body(total, args, outs):
    result = args[0] + total
    outs[0][...] = result
    return result


def norm_back_body(total, args, outs):
    result, outs[1][...] = norm_back(total, args[0], args[1])
    result += args[2]
    outs[0][...] = result
    return result


def embed(q_pre, k_pre, q_scale, k_scale, cos_table, sine_table):
    queries = rms_scale(q_pre, q_scale)
    keys = rms_scale(k_pre, k_scale)
    return (
        rotate(queries, cos_table[:, :, None], sine_table[:, :, None]),
        rotate(keys, cos_table, sine_table),
    )


def attn_forward(hidden_in, weights, gains, slot, gather):
    attn_scale, _, q_scale, k_scale = gains
    w_qkv, w_out = weights[:2]
    allowed, cos_table, sine_table = slot
    trees, row_count, depth = hidden_in.shape
    q_width = w_out.shape[0]
    normed = rms_scale(hidden_in.astype(F32), attn_scale).astype(BF16).reshape(-1, depth)
    qkv = dot(normed, w_qkv).reshape(trees, row_count, -1)
    q_pre = qkv[:, :, :q_width].reshape(trees, row_count, -1, HD)
    k_pre = qkv[:, :, q_width : q_width + HD]
    value_bf = qkv[:, :, q_width + HD :].astype(BF16)
    queries, keys_rot = embed(q_pre, k_pre, q_scale, k_scale, cos_table, sine_table)
    query_bf = queries.astype(BF16)
    kv_all = gather(jnp.concatenate([keys_rot.astype(BF16), value_bf], axis=2))
    key_all = kv_all[:, :, :HD]
    value_all = kv_all[:, :, HD:]
    scores = masked_scores(query_bf, key_all, allowed)
    row_max = jnp.max(scores, axis=-1, keepdims=True)
    exp_scores = jnp.exp(scores - row_max)
    row_total = jnp.sum(exp_scores, axis=-1, keepdims=True)
    prob_bf = (exp_scores / row_total).astype(BF16)
    log_total = row_max + jnp.log(row_total)
    attended = jnp.einsum("bgrt,btd->brgd", prob_bf, value_all, preferred_element_type=F32)
    attended_bf = attended.reshape(trees * row_count, -1).astype(BF16)
    terms = dot(attended_bf, w_out).astype(BF16).reshape(trees, row_count, depth)
    saved = (normed, q_pre, k_pre, query_bf, key_all, value_all, log_total, attended_bf)
    return (terms, saved)


def attn_backward(grad_attn, saved, weights, gains, slot, scatter):
    _, _, q_scale, k_scale = gains
    w_qkv, w_out = weights[:2]
    allowed, cos_table, sine_table = slot
    normed, q_pre, k_pre, query_bf, key_all, value_all, log_total, attended_bf = saved
    trees, row_count = query_bf.shape[:2]
    depth = normed.shape[1]
    grad_attn = grad_attn.reshape(-1, depth)
    grad_heads = dot_inner(grad_attn, w_out).astype(BF16).reshape(query_bf.shape)
    scores = masked_scores(query_bf, key_all, allowed)
    prob_full = jnp.exp(scores - log_total)
    grad_prob = jnp.einsum("brgd,btd->bgrt", grad_heads, value_all, preferred_element_type=F32)
    row_dot = jnp.sum(prob_full * grad_prob, axis=-1, keepdims=True)
    grad_scores = (prob_full * (grad_prob - row_dot)).astype(BF16)
    scale_factor = HD ** (-0.5)
    grad_query = (
        jnp.einsum("bgrt,btd->brgd", grad_scores, key_all, preferred_element_type=F32)
        * scale_factor
    )
    grad_key_all = (
        jnp.einsum("bgrt,brgd->btd", grad_scores, query_bf, preferred_element_type=F32)
        * scale_factor
    )
    grad_value_all = jnp.einsum(
        "bgrt,brgd->btd", prob_full.astype(BF16), grad_heads, preferred_element_type=F32
    )
    grad_kv = scatter(jnp.concatenate([grad_key_all, grad_value_all], axis=2).astype(BF16))
    _, embedding_pull = jax.vjp(
        partial(embed, cos_table=cos_table, sine_table=sine_table), q_pre, k_pre, q_scale, k_scale
    )
    grad_q_pre, grad_k_pre, grad_q_scale, grad_k_scale = embedding_pull(
        (grad_query, grad_kv[:, :, :HD].astype(F32))
    )
    qkv_grad = jnp.concatenate(
        [
            grad_q_pre.astype(BF16).reshape(trees, row_count, -1),
            grad_k_pre.astype(BF16),
            grad_kv[:, :, HD:].astype(BF16),
        ],
        axis=2,
    ).reshape(trees * row_count, -1)
    terms = dot_inner(qkv_grad, w_qkv).astype(BF16).reshape(trees, row_count, depth)
    return (terms, [(normed, qkv_grad), (grad_attn, attended_bf)], [grad_q_scale, grad_k_scale])


def plain_layers(hidden, own_in, grad_own, weights, gains, slot, shared_kv):
    depth = own_in.shape[1]
    own_shape = own_in.shape

    def gather(own):
        return lax.all_gather(own, "dp", axis=1, tiled=True)

    def scatter(whole):
        total = lax.psum_scatter(whole, "dp", scatter_dimension=1, tiled=True)
        if shared_kv:
            total = lax.psum(total, "section")
            total = jnp.where(lax.axis_index("section") == 0, total, jnp.zeros_like(total))
        return total

    outputs, kept = [], []
    for layer in range(2):
        _, _, w_gate, w_up, w_down = weights[layer]
        terms, saved = attn_forward(hidden, weights[layer], gains[layer], slot, gather)
        mlp_scale = gains[layer][1][None]
        middle, mlp_in = hub_plain(
            terms, [own_in, mlp_scale], norm_body, [own_shape], "tensor", ["dp"]
        )
        mlp_in = mlp_in.reshape(-1, depth)
        gate, up = dot_inner(mlp_in, w_gate), dot_inner(mlp_in, w_up)
        hidden_bf = swiglu(gate, up).astype(BF16)
        terms = dot(hidden_bf, w_down).astype(BF16).reshape(2, -1, depth)
        kept.append((own_in, saved, middle, mlp_in, gate, up, hidden_bf))
        own_in, hidden = hub_plain(terms, [middle], add_body, [own_shape], "dp", ["tensor"])
        own_in = own_in.astype(BF16).astype(F32)
        outputs.append(hidden)

    own_outs = [own_shape, (1, depth)]
    grads, products, gain_grads = [None, None], [None, None], [None, None]
    (grad_mlp,) = hub_plain(None, [grad_own], lambda total, args, outs: args[0], [], None, ["dp"])
    for layer in (1, 0):
        _, _, w_gate, w_up, w_down = weights[layer]
        own_in, saved, middle, mlp_in, gate, up, hidden_bf = kept[layer]
        grad_mlp = grad_mlp.reshape(-1, depth)
        _, pull = jax.vjp(swiglu, gate, up)
        grad_gate, grad_up = (item.astype(BF16) for item in pull(dot_inner(grad_mlp, w_down)))
        terms = (dot(grad_gate, w_gate) + dot(grad_up, w_up)).astype(BF16).reshape(2, -1, depth)
        grad_middle, mlp_gain_grad, grad_attn = hub_plain(
            terms, [middle, gains[layer][1][None], grad_own], norm_back_body, own_outs, "dp",
            ["tensor"],
        )
        terms, pairs, head_grads = attn_backward(
            grad_attn, saved, weights[layer], gains[layer], slot, scatter
        )
        grad_own, gain_grad, grads[layer], grad_next = hub_plain(
            terms, [own_in, gains[layer][0][None], grad_middle], norm_back_body, own_outs, "tensor",
            ["tensor", "dp"],
        )
        grad_own = grad_own.astype(BF16).astype(F32)
        pairs += [(grad_gate, mlp_in), (grad_up, mlp_in), (hidden_bf, grad_mlp)]
        products[layer] = pairs
        gain_grads[layer] = jnp.concatenate([gain_grad[0], mlp_gain_grad[0], *head_grads])
        grad_mlp = grad_next
    return (outputs, grads, products, gain_grads)


def swap_cores(mine, other):
    core = lax.axis_index("section")
    arrived = lax.ppermute(other, "section", [(0, 1), (1, 0)])
    return (jnp.where(core == 0, mine, arrived), jnp.where(core == 0, arrived, mine))


def on_device(
    inputs, cotangent, seg_ids, parents, order, attn_gain, w_query, w_key, w_value, w_out,
    q_gain, k_gain, mlp_gain, w_gate, w_up, w_down,
):
    core = lax.axis_index("section")
    data_index = lax.axis_index("dp")
    tensor_index = lax.axis_index("tensor")
    dp_size = lax.axis_size("dp")
    tensor_size = lax.axis_size("tensor")
    trees, row_count, depth = inputs.shape
    own_rows = row_count // tensor_size
    row_start = data_index * row_count
    own_depth = w_query.shape[1]
    q_width = w_query.shape[2] // 2
    shared_kv = w_key.shape[2] == HD
    k_width = HD if shared_kv else w_key.shape[2] // 2
    own_units = w_gate.shape[2]
    share = own_units // (2 * dp_size)

    def pick(stacked, index):
        return lax.dynamic_index_in_dim(stacked, index, 0, keepdims=False)

    fast = (
        own_rows % 8 == 0
        and depth % (2 * CHUNK) == 0
        and row_count % 16 == 0
        and share % 16 == 0
        and own_depth % 128 == 0
        and not shared_kv
    )

    def halves(width, array):
        return [array[:, :width], array[:, array.shape[1] - width :]]

    unit_mats = [w_gate[0].T, w_up[0].T, w_down[0]]
    qkv_width = q_width + 2 * k_width
    gains_own = jnp.concatenate([attn_gain[0], mlp_gain[0], q_gain[0], k_gain[0]]).astype(F32)

    def spread_units(rows):
        return lax.all_gather(rows, "tensor", axis=0, tiled=True)

    def tied(value, *before):
        return lax.optimization_barrier((value, *before))[0]

    if fast:
        line = ["section", "dp"]
        everyone = ["section", "dp", "tensor"]
        (gate_rows, up_rows), (gains_all,) = fused(
            [UnitsOut(unit_mats[:2], 0), SharedRows(gains_own.reshape(-1, 128))], line, True, 1, 45, 40
        )
        shards = AttnShards(w_query[0], w_key[0], w_value[0], w_out[0])
        shards.arrays[0] = tied(shards.arrays[0], gate_rows)
        (w_qkv, w_heads), (down_rows,), (attn_shard,) = fused(
            [AttnOut(shards, 0), UnitsOut(unit_mats[2:], 0), HalfOver(shards)], line, True, 2, 80, 40
        )
        first_weights = [w_qkv, w_heads, spread_units(gate_rows), spread_units(up_rows)]
    else:
        gains_all = lax.all_gather(gains_own, ("section", "dp"))
        attn_halves = jnp.stack(
            [
                jnp.concatenate(parts, axis=1)
                for parts in zip(
                    halves(q_width, w_query[0]),
                    halves(k_width, w_key[0]),
                    halves(k_width, w_value[0]),
                    halves(q_width, w_out[0].T),
                )
            ]
        )
        attn_shards = swap_cores(pick(attn_halves, core), pick(attn_halves, 1 - core))
        unit_blocks = jnp.stack(unit_mats).reshape(3, 2, dp_size, share, own_depth)
        unit_blocks = unit_blocks.transpose(1, 2, 0, 3, 4)
        unit_shards = swap_cores(pick(unit_blocks, core), pick(unit_blocks, 1 - core))
        both_weights = []
        for layer in range(2):
            attn_all = lax.all_gather(attn_shards[layer], "dp", axis=0, tiled=True)
            pieces = exchange(unit_shards[layer], "dp")
            pieces = pieces.transpose(1, 2, 0, 3).reshape(3, share, depth)
            both_weights.append(
                (
                    attn_all[:, :qkv_width], attn_all[:, qkv_width:].T,
                    *(spread_units(pieces[i]) for i in range(3)),
                )
            )

    gains_all = gains_all.reshape(2, dp_size, -1)
    gains = [
        (
            gains_all[layer, :, :own_depth].reshape(depth),
            gains_all[layer, :, own_depth : 2 * own_depth].reshape(depth),
            gains_all[layer, 0, 2 * own_depth : 2 * own_depth + HD],
            gains_all[layer, 0, 2 * own_depth + HD :],
        )
        for layer in range(2)
    ]

    def slot_setup(slot_index):
        tree_id = pick(order, slot_index)
        allowed, row_positions = path_mask(
            pick(seg_ids, tree_id), pick(parents, tree_id), row_start, row_count
        )
        cos_table, sine_table = rope_tables(row_positions, HD)
        return (pick(inputs, tree_id), allowed, cos_table[:, 0], sine_table[:, 0])

    setups = [slot_setup(i) for i in range(trees)]
    hidden, *slot = (jnp.stack(item) for item in zip(*setups))

    def own_part(whole):
        return lax.dynamic_slice_in_dim(
            pick(whole, core), tensor_index * own_rows, own_rows, 0
        )

    own_in = own_part(hidden).astype(F32)
    grad_own = own_part(cotangent).astype(F32)

    def weight_products(pairs):
        return [dot_outer(left, right).astype(BF16) for left, right in pairs]

    def scatter_units(products):
        return [
            lax.psum_scatter(item, "tensor", scatter_dimension=0, tiled=True) for item in products
        ]

    def scatter_shards(products):
        return lax.psum_scatter(
            jnp.concatenate(products, axis=1), "dp", scatter_dimension=0, tiled=True
        )

    if fast:
        def units_on(*which):
            return [UnitsOut([unit_mats[i] for i in which], 1)]

        def kv_gather(own, cargo, collective_id, carried):
            (whole,), outs = with_cargo(GatherKV(own), cargo, everyone, collective_id, 40, 40)
            carried += outs
            return whole.reshape(trees, -1, 2 * HD)

        def kv_scatter(whole, cargo, collective_id, carried):
            part = ScatterKV(whole.reshape(trees, dp_size, row_count, 2 * HD))
            (total,), outs = with_cargo(part, cargo, everyone, collective_id, 30, 40)
            carried += outs
            return total

        def in_order(pairs):
            done = []
            for left, right in pairs:
                done += weight_products([(tied(left, *done[-1:]), right)])
            return done

        def flat(array):
            return array.reshape(-1, array.shape[-1])

        carried = []
        terms, saved_first = attn_forward(
            hidden, first_weights, gains[0], slot,
            lambda own: kv_gather(
                tied(own, *first_weights[2:]), [UnitsSpread(down_rows)] + units_on(0, 1, 2), 3, carried
            ),
        )
        (down_all,), (gate_rows, up_rows, down_rows) = carried
        first_weights.append(down_all)
        part = FeedForward(
            terms, own_in, gains[0][1][None], first_weights[2:], True, False, {}
        )
        outs, ((down_next,),) = with_cargo(part, [UnitsSpread(down_rows)], everyone, 4, 90, 56)
        middle_first, mlp_in_first, hidden_first, own_next, output_first, gate_first, up_first = outs
        attn_next = lax.all_gather(tied(attn_shard, gate_rows), "dp", axis=0)
        second_weights = [
            attn_next[:, :own_depth].reshape(depth, -1),
            attn_next[:, own_depth:].transpose(1, 0, 2).reshape(q_width, depth),
            spread_units(gate_rows), spread_units(up_rows),
        ]
        carried = []
        terms, saved_second = attn_forward(
            output_first, second_weights, gains[1], slot,
            lambda own: kv_gather(tied(own, second_weights[2]), [], 5, carried),
        )
        second_weights.append(down_next)
        part = FeedForward(
            terms, own_next, gains[1][1][None], second_weights[2:], True, True,
            {"grad_own": grad_own},
        )
        outs, _ = with_cargo(part, [], everyone, 6, 100, 60)
        (
            middle, mlp_in, hidden_bf, own_second, grad_mlp,
            grad_gate, grad_up, grad_middle, mlp_gain_second, grad_attn,
        ) = outs
        products = in_order([(flat(grad_gate), flat(mlp_in)), (flat(grad_up), flat(mlp_in))])
        unit_second = scatter_units(products)
        carried = []
        terms, pairs, head_second = attn_backward(
            grad_attn, saved_second, second_weights, gains[1], slot,
            lambda whole: kv_scatter(
                tied(whole, *products), [RowsOut(own_second, output_first)], 7, carried
            ),
        )
        ((layer_out,),) = carried
        unit_second += scatter_units(
            weight_products([(tied(flat(hidden_bf), layer_out), flat(grad_mlp))])
        )
        pairs = weight_products(pairs)
        attn_second = scatter_shards([tied(pairs[0], unit_second[1]), pairs[1]])
        terms = tied(terms, unit_second[0])
        part = FeedForward(
            terms, own_next, gains[1][0][None], first_weights[2:], False, True,
            {
                "add": grad_middle, "gate": gate_first, "up": up_first,
                "middle_in": middle_first, "mlp_gain": gains[0][1][None],
            },
        )
        outs, _ = with_cargo(part, [], everyone, 8, 90, 60)
        (
            grad_gate, grad_up, grad_middle, mlp_gain_first, grad_attn,
            attn_gain_second, own_incoming, grad_mlp,
        ) = outs
        products = in_order(
            [(flat(grad_gate), flat(mlp_in_first)), (flat(grad_up), flat(mlp_in_first))]
        )
        grad_attn = tied(grad_attn, *unit_second[1:], *products)
        unit_first = scatter_units(products)
        carried = []
        terms, pairs, head_first = attn_backward(
            grad_attn, saved_first, first_weights, gains[0], slot,
            lambda whole: kv_scatter(
                whole, [UnitsHome(unit_second, 1), RowsOut(own_incoming)], 9, carried
            ),
        )
        home_second, (incoming_second,) = carried
        unit_first += scatter_units(
            weight_products([(tied(flat(hidden_first), incoming_second), flat(grad_mlp))])
        )
        parts = [
            ScatterKV(item.reshape(dp_size, 4, own_depth // 4, -1), True, BF16)
            for item in weight_products(pairs)
        ]
        part = LastHub(terms, own_in, gains[0][0][None], grad_middle, incoming_second)
        (attn_gain_first, input_grad), (*attn_first, home_first) = with_cargo(
            part, parts + [UnitsHome(unit_first[:2], 0)], everyone, 10, 60, 56
        )
        attn_first = [item.reshape(own_depth, -1) for (item,) in attn_first]
        attn_second = [attn_second[:, :qkv_width], attn_second[:, qkv_width:]]
        gain_grads = [
            jnp.concatenate([attn_gain_first[0], mlp_gain_first[0], *head_first]),
            jnp.concatenate([attn_gain_second[0], mlp_gain_second[0], *head_second]),
        ]
    else:
        outputs, grads, products, gain_grads = plain_layers(
            hidden, own_in, grad_own, both_weights, gains, slot, shared_kv
        )
        layer_out = jnp.where(core == 0, *outputs)
        input_grad = jnp.where(core == 0, *grads)
        weight_grads = []
        for pairs in products:
            whole = weight_products(pairs)
            weight_grads.append((scatter_shards(whole[:2]), scatter_units(whole[2:])))

    gain_total = jnp.stack(gain_grads)
    if fast:
        others = [
            Swap(jnp.where(core == 0, second, first))
            for first, second in zip(attn_first, attn_second)
        ]
        (gain_total,), *arrived, down_home = fused(
            [TotalOverAll(gain_total.reshape(-1, 128)), *others, UnitsHome(unit_first[2:], 0)],
            everyone, True, 11, 60, 40,
        )
        grad_gate, grad_up, grad_down, *attn_grads, layer_out, input_grad = finish_weights(
            home_first + down_home, home_second, attn_first, attn_second,
            [item for (item,) in arrived], (q_width, k_width, k_width, q_width), core,
            (layer_out, input_grad),
        )
        layer_out = layer_out.reshape(trees, row_count, depth)
        input_grad = input_grad.reshape(trees, row_count, depth)
        gain_total = gain_total.reshape(2, -1)
    else:
        def bring_home(first, second):
            mine, other = jnp.where(core == 0, first, second), jnp.where(core == 0, second, first)
            arrived = lax.ppermute(other, "section", [(0, 1), (1, 0)])
            return (jnp.where(core == 0, mine, arrived), jnp.where(core == 0, arrived, mine))

        def pieces_of(grad):
            return exchange(
                jnp.stack(grad).reshape(3, share, dp_size, own_depth).transpose(2, 0, 1, 3), "dp"
            )

        attn_home = bring_home(weight_grads[0][0], weight_grads[1][0])
        unit_home = jnp.stack(bring_home(pieces_of(weight_grads[0][1]), pieces_of(weight_grads[1][1])))
        unit_home = unit_home.transpose(2, 0, 1, 3, 4).reshape(3, own_units, own_depth).astype(F32)
        grad_gate, grad_up, grad_down = unit_home[0].T, unit_home[1].T, unit_home[2]
        gain_total = lax.psum(gain_total, ("section", "dp", "tensor"))

        def joined(start, width):
            parts = [half[:, start : start + width] for half in attn_home]
            if shared_kv and start in (q_width, q_width + k_width):
                return parts[0].astype(F32)
            return jnp.concatenate(parts, axis=1).astype(F32)

        attn_grads = [
            joined(0, q_width), joined(q_width, k_width), joined(q_width + k_width, k_width),
            joined(qkv_width, q_width).T,
        ]

    gain_own = pick(gain_total, core)
    share_width = attn_gain.shape[1]
    attn_gain_grad = lax.dynamic_slice_in_dim(gain_own, data_index * share_width, share_width, 0)
    mlp_gain_grad = lax.dynamic_slice_in_dim(
        gain_own, depth + data_index * share_width, share_width, 0
    )
    return (
        layer_out[None],
        input_grad[None],
        attn_gain_grad[None],
        *(item[None] for item in attn_grads),
        gain_own[2 * depth : 2 * depth + HD][None],
        gain_own[2 * depth + HD :][None],
        mlp_gain_grad[None],
        grad_gate[None],
        grad_up[None],
        grad_down[None],
    )


def solution(mesh):
    rows = P(None, "dp", None)
    wide = P("section", "dp", "tensor")
    tall = P("section", "tensor", "dp")
    gain = P("section", "dp")
    head_gain = P("section", None)
    slots = P("section", None, "dp", None)
    in_specs = (
        rows, rows, P(), P(), P(), gain, wide, wide, wide, tall, head_gain, head_gain, gain,
        wide, wide, tall,
    )
    out_specs = (
        slots, slots, gain, wide, wide, wide, tall, head_gain, head_gain, gain, wide, wide, tall,
    )
    return jax.shard_map(
        on_device, mesh=mesh, in_specs=in_specs, out_specs=out_specs, check_vma=False
    )
```

```python
from functools import partial

import jax
import jax.numpy as jnp
from jax import lax
from jax.experimental import pallas as pl
from jax.experimental.pallas import tpu as pltpu
from jax.sharding import PartitionSpec as P

HD = 128
TRUNK = 512
BRANCH = 96
NB = 4
TREE = 1152
SEGS = 9


EPSILON = 1e-06
THETA = 1000000.0
MASKED = -1e30
F32 = jnp.float32
BF16 = jnp.bfloat16


def rms_scale(values, weight_gain):
    mean_sq = jnp.mean(values * values, axis=-1, keepdims=True)
    return values * lax.rsqrt(mean_sq + EPSILON) * weight_gain


def rotate(values, cos_table, sine_table):
    middle_at = values.shape[-1] // 2
    leading = values[..., :middle_at]
    trailing = values[..., middle_at:]
    return jnp.concatenate(
        [leading * cos_table - trailing * sine_table, trailing * cos_table + leading * sine_table],
        axis=-1,
    )


def rope_tables(positions, head_dim):
    half_steps = jnp.arange(head_dim // 2, dtype=F32)
    inverse = THETA ** (-2.0 * half_steps / head_dim)
    angles = positions.astype(F32)[:, None] * inverse[None, :]
    return (jnp.cos(angles)[:, None, :], jnp.sin(angles)[:, None, :])


def swiglu(gate_in, up_in):
    return jax.nn.silu(gate_in) * up_in


def embed_heads(q_pre, k_pre, q_scale, k_scale, cos_table, sine_table):
    row_count = q_pre.shape[0]
    queries = rms_scale(q_pre.reshape(row_count, -1, HD), q_scale)
    keys_part = rms_scale(k_pre.reshape(row_count, -1, HD), k_scale)
    return (rotate(queries, cos_table, sine_table), rotate(keys_part, cos_table, sine_table))


def tree_layout(seg_row, parent_row):
    labels = jnp.arange(SEGS, dtype=jnp.int32)
    places = jnp.arange(TREE, dtype=jnp.int32)
    member = seg_row[None, :] == labels[:, None]
    starts = jnp.min(jnp.where(member, places[None, :], TREE), axis=1)
    depth_base = jnp.where(labels == 0, 0, jnp.where(labels <= NB, TRUNK, TRUNK + BRANCH))
    shifts = depth_base - starts
    positions = places + jnp.sum(jnp.where(member, shifts[:, None], 0), axis=0)
    grandparent = jnp.sum(
        jnp.where(parent_row[:, None] == labels[None, :], parent_row[None, :], 0), axis=1
    )
    ancestor = (
        (labels[None, :] == labels[:, None])
        | (labels[None, :] == parent_row[:, None])
        | (labels[None, :] == grandparent[:, None])
    )
    return (positions, member.astype(F32), ancestor.astype(F32))


def path_mask(seg_row, parent_row, row_start, row_count):
    positions, member, ancestor = tree_layout(seg_row, parent_row)
    member_rows = lax.dynamic_slice_in_dim(member, row_start, row_count, 1)
    seg_rows = lax.dynamic_slice_in_dim(seg_row, row_start, row_count, 0)
    reach_table = jnp.dot(jnp.dot(member_rows.T, ancestor), member)
    places = jnp.arange(TREE, dtype=jnp.int32)
    row_places = row_start + jnp.arange(row_count, dtype=jnp.int32)
    same_seg = seg_rows[:, None] == seg_row[None, :]
    causal = places[None, :] <= row_places[:, None]
    allowed = (reach_table > 0.5) & (jnp.logical_not(same_seg) | causal)
    row_positions = lax.dynamic_slice_in_dim(positions, row_start, row_count, 0)
    return (allowed, row_positions)


OUTER = (((0,), (0,)), ((), ()))
INNER = (((1,), (1,)), ((), ()))


def dot(left, right):
    return jnp.dot(left, right, preferred_element_type=F32)


def dot_inner(left, right):
    return lax.dot_general(left, right, INNER, preferred_element_type=F32)


def dot_outer(left, right):
    return lax.dot_general(left, right, OUTER, preferred_element_type=F32)


def exchange(pieces, axis):
    size = lax.axis_size(axis)
    me = lax.axis_index(axis)
    got = jnp.zeros_like(pieces)
    own = lax.dynamic_index_in_dim(pieces, me, 0, keepdims=True)
    got = lax.dynamic_update_slice_in_dim(got, own, me, 0)
    for step in range(1, size):
        other = me ^ step
        piece = lax.dynamic_index_in_dim(pieces, other, 0, keepdims=True)
        arrived = lax.ppermute(piece, axis, [(i, i ^ step) for i in range(size)])
        got = lax.dynamic_update_slice_in_dim(got, arrived, other, 0)
    return got


def masked_scores(query_bf, key_all, allowed):
    raw_scores = jnp.einsum(
        "brgd,btd->bgrt", query_bf, key_all, preferred_element_type=F32
    ) * HD ** (-0.5)
    return jnp.where(allowed[:, None], raw_scores, MASKED)


MESH = pl.DeviceIdType.MESH
CHUNK = 256
SEM = pltpu.SemaphoreType.DMA
VMEM = pl.BlockSpec(memory_space=pltpu.VMEM)
HBM = pl.BlockSpec(memory_space=pl.ANY)


def remote(src, dst, send_sem, recv_sem, device_id):
    return pltpu.make_async_remote_copy(
        src_ref=src, dst_ref=dst, send_sem=send_sem, recv_sem=recv_sem,
        device_id=device_id, device_id_type=MESH,
    )


def greet(axes, across):
    barrier = pltpu.get_barrier_semaphore()
    count = 0
    for axis in axes:
        size = lax.axis_size(axis)
        me = lax.axis_index(axis)
        for step in range(1, size):
            pl.semaphore_signal(
                barrier, inc=1, device_id={axis: lax.rem(me + step, size)}, device_id_type=MESH
            )
        count += size - 1
    if across:
        size = lax.axis_size("dp")
        me = lax.axis_index("dp")
        sibling = 1 - lax.axis_index("section")
        for step in range(1, size):
            pl.semaphore_signal(
                barrier, inc=1, device_id={"section": sibling, "dp": lax.rem(me + step, size)},
                device_id_type=MESH,
            )
        count += size - 1
    pl.semaphore_wait(barrier, count)


class Part:
    ins, outs, scratch = (), (), ()

    def bind(self, ins, outs, scratch):
        self.in_refs, self.out_refs, self.refs = ins, outs, scratch

    def prepare(self):
        pass

    def start(self):
        pass

    def run(self):
        pass

    def pass_on(self):
        pass

    def late(self):
        pass

    def finish(self):
        pass


def fused(parts, axes, across, collective_id, cost_us, vmem):
    counts = [(len(part.ins), len(part.outs), len(part.scratch)) for part in parts]

    def kernel(*refs):
        refs = list(refs)
        groups = []
        for kind in range(3):
            groups.append([])
            for count in counts:
                groups[kind].append(refs[: count[kind]])
                del refs[: count[kind]]
        for part, ins, outs, scratch in zip(parts, *groups):
            part.bind(ins, outs, scratch)
        for part in parts:
            part.prepare()
        greet(axes, across)
        for part in parts:
            part.start()
        for part in reversed(parts):
            part.run()
        for part in reversed(parts):
            part.pass_on()
        for part in reversed(parts):
            part.late()
        for part in parts:
            part.finish()

    ins = [item for part in parts for item in part.ins]
    outs = [item for part in parts for item in part.outs]
    results = pl.pallas_call(
        kernel,
        out_shape=[item[0] for item in outs],
        in_specs=[item[1] for item in ins],
        out_specs=[item[1] for item in outs],
        scratch_shapes=[item for part in parts for item in part.scratch],
        cost_estimate=pl.CostEstimate(
            flops=0, bytes_accessed=cost_us * 3_000_000, transcendentals=0
        ),
        compiler_params=pltpu.CompilerParams(
            collective_id=collective_id, has_side_effects=True, vmem_limit_bytes=vmem << 20
        ),
    )(*[item[0] for item in ins])
    results = list(results)
    split = []
    for count in counts:
        split.append(results[: count[1]])
        del results[: count[1]]
    return split


def columns_of(place, width):
    return pl.ds(pl.multiple_of(place * width, width), width)


class UnitsOut(Part):
    def __init__(self, mats, layer):
        self.layer, self.count = layer, len(mats)
        self.size = lax.axis_size("dp")
        rows, self.width = mats[0].shape
        self.share = rows // (2 * self.size)
        self.ins = [(mat, HBM) for mat in mats]
        shape = jax.ShapeDtypeStruct((self.share, self.size * self.width), BF16)
        self.outs = [(shape, HBM)] * self.count
        self.scratch = [SEM((self.count,)), SEM((self.count, 2, self.size)), SEM((self.count, self.size))]

    def bind(self, ins, outs, scratch):
        self.src, self.dst = ins, outs
        self.keep, self.send, self.recv = scratch
        self.core, self.me = lax.axis_index("section"), lax.axis_index("dp")

    def piece(self, index, core, place):
        start = pl.multiple_of((core * self.size + place) * self.share, self.share)
        return self.src[index].at[pl.ds(start, self.share)]

    def lands(self, index, slot):
        return self.dst[index].at[:, columns_of(slot, self.width)]

    def copy(self, index, core, place, slot):
        return remote(
            self.piece(index, core, place), self.lands(index, slot),
            self.send.at[index, core, place], self.recv.at[index, slot],
            {"section": core, "dp": place},
        )

    def local(self, index):
        return pltpu.make_async_copy(
            self.piece(index, self.layer, self.me), self.lands(index, self.me), self.keep.at[index]
        )

    def targets(self):
        for index in range(self.count):
            for core in range(2):
                for place in range(self.size):
                    yield index, core, place, (place != self.me) | (core != self.layer)

    def start(self):
        @pl.when(self.core == self.layer)
        def _():
            for index, core, place, is_other in self.targets():
                @pl.when(is_other)
                def _():
                    self.copy(index, core, place, self.me).start()

            for index in range(self.count):
                self.local(index).start()

    def finish(self):
        for index in range(self.count):
            for place in range(self.size):
                @pl.when((self.core != self.layer) | (place != self.me))
                def _():
                    self.copy(index, 0, 0, place).wait_recv()

        @pl.when(self.core == self.layer)
        def _():
            for index, core, place, is_other in self.targets():
                @pl.when(is_other)
                def _():
                    self.copy(index, core, place, self.me).wait_send()

            for index in range(self.count):
                self.local(index).wait()


class UnitsHome(Part):
    def __init__(self, mats, layer):
        self.layer, self.count = layer, len(mats)
        self.size = lax.axis_size("dp")
        self.share, depth = mats[0].shape
        self.width = depth // self.size
        self.ins = [(mat, HBM) for mat in mats]
        shape = jax.ShapeDtypeStruct((2 * self.size * self.share, self.width), BF16)
        self.outs = [(shape, HBM)] * self.count
        self.scratch = [SEM((self.count,)), SEM((self.count, self.size)), SEM((self.count, 2, self.size))]

    def bind(self, ins, outs, scratch):
        self.src, self.dst = ins, outs
        self.keep, self.send, self.recv = scratch
        self.core, self.me = lax.axis_index("section"), lax.axis_index("dp")

    def lands(self, index, core, slot):
        start = pl.multiple_of((core * self.size + slot) * self.share, self.share)
        return self.dst[index].at[pl.ds(start, self.share)]

    def copy(self, index, place, core, slot):
        return remote(
            self.src[index].at[:, columns_of(place, self.width)], self.lands(index, core, slot),
            self.send.at[index, place], self.recv.at[index, core, slot],
            {"section": self.layer, "dp": place},
        )

    def local(self, index):
        return pltpu.make_async_copy(
            self.src[index].at[:, columns_of(self.me, self.width)],
            self.lands(index, self.layer, self.me), self.keep.at[index],
        )

    def start(self):
        for index in range(self.count):
            for place in range(self.size):
                @pl.when((self.core != self.layer) | (place != self.me))
                def _():
                    self.copy(index, place, self.core, self.me).start()

            @pl.when(self.core == self.layer)
            def _():
                self.local(index).start()

    def finish(self):
        for index in range(self.count):
            @pl.when(self.core == self.layer)
            def _():
                for core in range(2):
                    for place in range(self.size):
                        @pl.when((core != self.layer) | (place != self.me))
                        def _():
                            self.copy(index, 0, core, place).wait_recv()

                self.local(index).wait()

            for place in range(self.size):
                @pl.when((self.core != self.layer) | (place != self.me))
                def _():
                    self.copy(index, place, self.core, self.me).wait_send()


class UnitsSpread(Part):
    def __init__(self, rows):
        self.size = lax.axis_size("tensor")
        self.share, depth = rows.shape
        self.ins = [(rows, HBM)]
        self.outs = [(jax.ShapeDtypeStruct((self.size * self.share, depth), BF16), HBM)]
        self.scratch = [SEM, SEM((self.size,)), SEM((self.size,))]

    def bind(self, ins, outs, scratch):
        (self.src,), (self.dst,), (self.keep, self.send, self.recv) = ins, outs, scratch
        self.me = lax.axis_index("tensor")

    def lands(self, slot):
        return self.dst.at[pl.ds(pl.multiple_of(slot * self.share, self.share), self.share)]

    def copy(self, place, slot):
        return remote(
            self.src, self.lands(slot), self.send.at[place], self.recv.at[slot], {"tensor": place}
        )

    def start(self):
        for place in range(self.size):
            @pl.when(place != self.me)
            def _():
                self.copy(place, self.me).start()

        pltpu.make_async_copy(self.src, self.lands(self.me), self.keep).start()

    def finish(self):
        for place in range(self.size):
            @pl.when(place != self.me)
            def _():
                self.copy(place, place).wait_recv()
                self.copy(place, self.me).wait_send()

        pltpu.make_async_copy(self.src, self.lands(self.me), self.keep).wait()


class SharedRows(Part):
    def __init__(self, own):
        self.size = lax.axis_size("dp")
        self.ins = [(own, VMEM)]
        self.outs = [(jax.ShapeDtypeStruct((2, self.size) + own.shape, F32), VMEM)]
        self.scratch = [SEM((2, self.size)), SEM((2, self.size))]

    def copy(self, core, place, from_core, from_place):
        return remote(
            self.in_refs[0], self.out_refs[0].at[from_core, from_place],
            self.refs[0].at[core, place], self.refs[1].at[from_core, from_place],
            {"section": core, "dp": place},
        )

    def others(self):
        core, me = lax.axis_index("section"), lax.axis_index("dp")
        for other in range(2):
            for place in range(self.size):
                yield other, place, (other != core) | (place != me)

    def start(self):
        core, me = lax.axis_index("section"), lax.axis_index("dp")
        for other, place, is_other in self.others():
            @pl.when(is_other)
            def _():
                self.copy(other, place, core, me).start()

        self.out_refs[0][core, me] = self.in_refs[0][...]

    def finish(self):
        core, me = lax.axis_index("section"), lax.axis_index("dp")
        for other, place, is_other in self.others():
            @pl.when(is_other)
            def _():
                self.copy(other, place, other, place).wait_recv()
                self.copy(other, place, core, me).wait_send()


def passed_on(place, me):
    return ((place == 3) & (me <= 1)) | ((place == 0) & (me >= 2))


def line_relays(size):
    return [(2, 1, 3, 0), (2, 0, 3, 1), (1, 2, 0, 0), (1, 3, 0, 1)] if size == 4 else []


def line_order(size):
    return [1, 2, 0, 3] if size == 4 else list(range(size))


class AttnShards:
    def __init__(self, w_query, w_key, w_value, w_out):
        self.arrays = [w_query, w_key, w_value, w_out]
        self.depth = w_query.shape[0]
        self.q_width, self.k_width = w_query.shape[1] // 2, w_key.shape[1] // 2
        self.width = self.q_width + 2 * self.k_width
        half = self.depth // 2
        parts = self.q_width // 2
        self.items = [
            (0, lambda ref, core: ref.at[pl.ds(0, half), columns_of(core, self.q_width)]),
            (0, lambda ref, core: ref.at[pl.ds(half, half), columns_of(core, self.q_width)]),
            (1, lambda ref, core: ref.at[:, columns_of(core, self.k_width)]),
            (2, lambda ref, core: ref.at[:, columns_of(core, self.k_width)]),
            (3, lambda ref, core: ref.at[pl.ds(core * self.q_width, parts)]),
            (3, lambda ref, core: ref.at[pl.ds(core * self.q_width + parts, parts)]),
        ]
        q_width, k_width, depth = self.q_width, self.k_width, self.depth
        self.qkv_rows = [(0, half), (half, half), (0, depth), (0, depth)]
        self.qkv_columns = [
            (0, q_width), (0, q_width), (q_width, k_width), (q_width + k_width, k_width)
        ]
        self.out_rows = [(0, parts), (parts, parts)]

    def source(self, refs, index, core):
        array, cut = self.items[index]
        return cut(refs[array], core)

    def lands(self, qkv, out, index, slot):
        if index < 4:
            (start, rows), (left, columns) = self.qkv_rows[index], self.qkv_columns[index]
            at = pl.multiple_of(slot * self.depth + start, rows)
            return qkv.at[pl.ds(at, rows), pl.ds(left, columns)]
        start, rows = self.out_rows[index - 4]
        return out.at[pl.ds(start, rows), columns_of(slot, self.depth)]


class AttnOut(Part):
    def __init__(self, shards, layer):
        self.layer, self.shards = layer, shards
        self.size = lax.axis_size("dp")
        self.count = len(shards.items)
        depth = self.size * shards.depth
        self.ins = [(array, HBM) for array in shards.arrays]
        self.outs = [
            (jax.ShapeDtypeStruct((depth, shards.width), BF16), HBM),
            (jax.ShapeDtypeStruct((shards.q_width, depth), BF16), HBM),
        ]
        self.scratch = [
            SEM((self.count,)), SEM((2, self.size, self.count)), SEM((self.size, self.count)),
            SEM((self.count, 2)),
        ]

    def bind(self, ins, outs, scratch):
        self.src = ins
        self.qkv, self.out = outs
        self.keep, self.send, self.recv, self.relay_send = scratch
        self.core, self.me = lax.axis_index("section"), lax.axis_index("dp")

    def lands(self, index, slot):
        return self.shards.lands(self.qkv, self.out, index, slot)

    def copy(self, core, place, slot, index):
        return remote(
            self.shards.source(self.src, index, core), self.lands(index, slot),
            self.send.at[core, place, index], self.recv.at[slot, index],
            {"section": core, "dp": place},
        )

    def relay(self, source, target, turn, index):
        block = self.lands(index, source)
        return remote(
            block, block, self.relay_send.at[index, turn], self.recv.at[source, index],
            {"dp": target},
        )

    def local(self, index):
        return pltpu.make_async_copy(
            self.shards.source(self.src, index, self.layer), self.lands(index, self.me),
            self.keep.at[index],
        )

    def targets(self):
        for index in range(self.count):
            for core in range(2):
                for place in range(self.size):
                    sent = (place != self.me) | (core != self.layer)
                    if self.size == 4:
                        sent = sent & jnp.logical_not(passed_on(place, self.me))
                    yield core, place, index, sent

    def start(self):
        @pl.when(self.core == self.layer)
        def _():
            for core, place, index, sent in self.targets():
                @pl.when(sent)
                def _():
                    self.copy(core, place, self.me, index).start()

            for index in range(self.count):
                self.local(index).start()

    def run(self):
        for index in range(self.count):
            for place in line_order(self.size):
                @pl.when((self.core != self.layer) | (place != self.me))
                def _():
                    self.copy(0, 0, place, index).wait_recv()

                for via, source, target, turn in line_relays(self.size):
                    if source == place:
                        @pl.when(self.me == via)
                        def _():
                            self.relay(source, target, turn, index).start()

    def finish(self):
        @pl.when(self.core == self.layer)
        def _():
            for core, place, index, sent in self.targets():
                @pl.when(sent)
                def _():
                    self.copy(core, place, self.me, index).wait_send()

            for index in range(self.count):
                self.local(index).wait()

        for via, source, target, turn in line_relays(self.size):
            @pl.when(self.me == via)
            def _():
                for index in range(self.count):
                    self.relay(source, target, turn, index).wait_send()


class HalfOver(Part):
    def __init__(self, shards):
        self.shards = shards
        self.count = len(shards.items)
        rows = shards.depth + shards.q_width
        self.ins = [(array, HBM) for array in shards.arrays]
        self.outs = [(jax.ShapeDtypeStruct((rows, shards.depth), BF16), HBM)]
        self.scratch = [SEM((self.count,)), SEM((self.count,)), SEM((self.count,))]

    def lands(self, index):
        depth, q_width = self.shards.depth, self.shards.q_width
        packed = self.out_refs[0]
        return self.shards.lands(
            packed.at[pl.ds(0, depth)], packed.at[pl.ds(depth, q_width)], index, 0
        )

    def over(self, index):
        return remote(
            self.shards.source(self.in_refs, index, 0), self.lands(index), self.refs[0].at[index],
            self.refs[1].at[index], {"section": 0},
        )

    def keep(self, index):
        return pltpu.make_async_copy(
            self.shards.source(self.in_refs, index, 1), self.lands(index), self.refs[2].at[index]
        )

    def start(self):
        @pl.when(lax.axis_index("section") == 1)
        def _():
            for index in range(self.count):
                self.over(index).start()
                self.keep(index).start()

    def finish(self):
        @pl.when(lax.axis_index("section") == 1)
        def _():
            for index in range(self.count):
                self.over(index).wait_send()
                self.keep(index).wait()

        @pl.when(lax.axis_index("section") == 0)
        def _():
            for index in range(self.count):
                self.over(index).wait_recv()


class Swap(Part):
    def __init__(self, own):
        self.ins = [(own, HBM)]
        self.outs = [(jax.ShapeDtypeStruct(own.shape, own.dtype), HBM)]
        self.scratch = [SEM, SEM]

    def start(self):
        sibling = 1 - lax.axis_index("section")
        self.copy = remote(
            self.in_refs[0], self.out_refs[0], self.refs[0], self.refs[1], {"section": sibling}
        )
        self.copy.start()

    def finish(self):
        self.copy.wait()


class GatherKV(Part):
    def __init__(self, own):
        trees, rows, width = own.shape
        self.trees, self.size = trees, lax.axis_size("dp")
        self.ins = [(own, VMEM)]
        self.outs = [(jax.ShapeDtypeStruct((trees, self.size, rows, width), BF16), VMEM)]
        self.scratch = [SEM((self.size, trees)), SEM((self.size, trees)), SEM((trees, 2))]

    def bind(self, ins, outs, scratch):
        (self.own,), (self.out,) = ins, outs
        self.send, self.recv, self.relay_send = scratch
        self.me = lax.axis_index("dp")

    def copy(self, place, slot, tree):
        return remote(
            self.own.at[tree], self.out.at[tree, slot], self.send.at[place, tree],
            self.recv.at[slot, tree], {"dp": place},
        )

    def relay(self, source, target, turn, tree):
        return remote(
            self.out.at[tree, source], self.out.at[tree, source], self.relay_send.at[tree, turn],
            self.recv.at[source, tree], {"dp": target},
        )

    def targets(self):
        for tree in range(self.trees):
            for place in range(self.size):
                sent = place != self.me
                if self.size == 4:
                    sent = sent & jnp.logical_not(passed_on(place, self.me))
                yield place, tree, sent

    def start(self):
        for place, tree, sent in self.targets():
            @pl.when(sent)
            def _():
                self.copy(place, self.me, tree).start()

        self.out[:, self.me] = self.own[...]

    def run(self):
        for tree in range(self.trees):
            for place in line_order(self.size):
                @pl.when(place != self.me)
                def _():
                    self.copy(place, place, tree).wait_recv()

                for via, source, target, turn in line_relays(self.size):
                    if source == place:
                        @pl.when(self.me == via)
                        def _():
                            self.relay(source, target, turn, tree).start()

    def finish(self):
        for place, tree, sent in self.targets():
            @pl.when(sent)
            def _():
                self.copy(place, self.me, tree).wait_send()

        for via, source, target, turn in line_relays(self.size):
            @pl.when(self.me == via)
            def _():
                for tree in range(self.trees):
                    self.relay(source, target, turn, tree).wait_send()


class ScatterKV(Part):
    def __init__(self, whole, place_first=False, kept_as=F32, far_only=False):
        self.place_first = place_first
        trees, size, rows, width = whole.shape
        if place_first:
            trees, size = size, trees
        self.trees, self.size = trees, size
        self.sides = [(0, 1, 2, 0), (0, 1, 3, 1), (3, 2, 1, 0), (3, 2, 0, 1)] if size == 4 else []
        if far_only:
            self.sides = self.sides[1::2]
        self.ins = [(whole, VMEM)]
        self.outs = [(jax.ShapeDtypeStruct((trees, rows, width), kept_as), VMEM)]
        self.scratch = [
            pltpu.VMEM((rows, width), F32),
            pltpu.VMEM((size, trees, rows, width), BF16),
            pltpu.VMEM((2, trees, rows, width), BF16),
            SEM((size, trees)), SEM((size, trees)), SEM((2, trees)), SEM((2, trees)),
        ]

    def bind(self, ins, outs, scratch):
        (self.terms,), (self.out,) = ins, outs
        self.total, self.boxes, self.joint, self.send, self.recv, self.join_send, self.join_recv = scratch
        self.me = lax.axis_index("dp")

    def term(self, tree, place):
        return self.terms.at[place, tree] if self.place_first else self.terms.at[tree, place]

    def copy(self, place, slot, tree):
        return remote(
            self.term(tree, place), self.boxes.at[slot, tree], self.send.at[place, tree],
            self.recv.at[slot, tree], {"dp": place},
        )

    def by_way(self, via, target, turn, tree):
        return remote(
            self.term(tree, target), self.joint.at[turn, tree], self.join_send.at[turn, tree],
            self.join_recv.at[turn, tree], {"dp": via},
        )

    def joined(self, via, target, turn, tree):
        return remote(
            self.joint.at[turn, tree], self.boxes.at[via, tree], self.send.at[target, tree],
            self.recv.at[via, tree], {"dp": target},
        )

    def plain(self, place):
        ok = place != self.me
        for source, via, target, turn in self.sides:
            if place == target:
                ok = ok & (self.me != source) & (self.me != via)
        return ok

    def expected(self, place):
        ok = place != self.me
        for source, via, target, turn in self.sides:
            if place == source:
                ok = ok & (self.me != target)
        return ok

    def start(self):
        for tree in range(self.trees):
            for source, via, target, turn in self.sides:
                @pl.when(self.me == source)
                def _():
                    self.by_way(via, target, turn, tree).start()

            for place in range(self.size):
                @pl.when(self.plain(place))
                def _():
                    self.copy(place, self.me, tree).start()

    def pass_on(self):
        for tree in range(self.trees):
            for source, via, target, turn in self.sides:
                @pl.when(self.me == via)
                def _():
                    self.by_way(via, target, turn, tree).wait_recv()
                    both = self.joint[turn, tree].astype(F32)
                    both += self.term(tree, target)[...].astype(F32)
                    self.joint[turn, tree] = both.astype(BF16)
                    self.joined(via, target, turn, tree).start()

    def late(self):
        for tree in range(self.trees):
            self.total[...] = self.term(tree, self.me)[...].astype(F32)
            for place in line_order(self.size):
                @pl.when(self.expected(place))
                def _():
                    self.copy(place, place, tree).wait_recv()
                    self.total[...] += self.boxes[place, tree].astype(F32)

            self.out[tree] = self.total[...].astype(self.out.dtype)

    def finish(self):
        for tree in range(self.trees):
            for place in range(self.size):
                @pl.when(self.plain(place))
                def _():
                    self.copy(place, self.me, tree).wait_send()

            for source, via, target, turn in self.sides:
                @pl.when(self.me == source)
                def _():
                    self.by_way(via, target, turn, tree).wait_send()

                @pl.when(self.me == via)
                def _():
                    self.joined(via, target, turn, tree).wait_send()


class TotalOverAll(Part):
    axes = ("section", "tensor", "dp")

    def __init__(self, own):
        sizes = [lax.axis_size(axis) for axis in self.axes]
        self.ins = [(own, VMEM)]
        self.outs = [(jax.ShapeDtypeStruct(own.shape, F32), VMEM)]
        self.scratch = [pltpu.VMEM((size,) + own.shape, F32) for size in sizes]
        self.scratch += [SEM((size,)) for size in sizes] * 2

    def run(self):
        out = self.out_refs[0]
        out[...] = self.in_refs[0][...]
        for axis, box, send, recv in zip(self.axes, self.refs[:3], self.refs[3:6], self.refs[6:9]):
            size, me = lax.axis_size(axis), lax.axis_index(axis)
            box[me] = out[...]

            def spread(place, slot):
                return remote(box.at[me], box.at[slot], send.at[place], recv.at[slot], {axis: place})

            for place in range(size):
                @pl.when(place != me)
                def _():
                    spread(place, me).start()

            for place in range(size):
                @pl.when(place != me)
                def _():
                    spread(place, place).wait_recv()
                    spread(place, me).wait_send()

            total = box[0]
            for place in range(1, size):
                total += box[place]
            out[...] = total


def chunk_count(rows):
    return 3 if rows % 24 == 0 else 1


class Gatherer:
    def __init__(self, axis, rows, half):
        self.axis, self.half = axis, half
        self.size = size = lax.axis_size(axis)
        self.chunks = chunks = chunk_count(rows)
        self.rows = rows // chunks
        self.scratch = [pltpu.VMEM((2, chunks, size, 2 * self.rows, half), BF16)]
        self.scratch += [SEM((chunks, size))] * 4 + [SEM((chunks, 2))]

    def bind(self, refs):
        self.board, self.send, self.recv, self.sib_send, self.sib_recv, self.relay_send = refs
        self.core = lax.axis_index("section")
        self.sibling = 1 - self.core
        self.me = lax.axis_index(self.axis)
        self.relays = line_relays(self.size) if self.axis == "dp" else []
        self.order = line_order(self.size) if self.axis == "dp" else range(self.size)

    def direct(self, place):
        sent = place != self.me
        if self.relays:
            sent = sent & jnp.logical_not(passed_on(place, self.me))
        return sent

    def spread(self, chunk, place, slot):
        block = self.board.at[self.core, chunk, slot]
        return remote(
            block, block, self.send.at[chunk, place], self.recv.at[chunk, slot], {self.axis: place}
        )

    def passed(self, chunk, source, target, turn):
        block = self.board.at[self.core, chunk, source]
        return remote(
            block, block, self.relay_send.at[chunk, turn], self.recv.at[chunk, source],
            {self.axis: target},
        )

    def over(self, tree, chunk, slot):
        block = self.board.at[tree, chunk, slot]
        return remote(
            block, block, self.sib_send.at[chunk, slot], self.sib_recv.at[chunk, slot],
            {"section": self.sibling},
        )

    def begin(self, chunk, result):
        half = self.half
        piece = jnp.concatenate([result[:, :half], result[:, half:]], axis=0)
        self.board[self.core, chunk, self.me] = piece.astype(BF16)
        for place in range(self.size):
            @pl.when(self.direct(place))
            def _():
                self.spread(chunk, place, self.me).start()

        self.over(self.core, chunk, self.me).start()

    def arrive(self, chunk):
        for place in self.order:
            @pl.when(place != self.me)
            def _():
                self.spread(chunk, place, place).wait_recv()

            for via, source, target, turn in self.relays:
                if source == place:
                    @pl.when(self.me == via)
                    def _():
                        self.passed(chunk, source, target, turn).start()

            @pl.when(place != self.me)
            def _():
                self.over(self.core, chunk, place).start()

    def arrive_over(self, chunk):
        for place in range(self.size):
            self.over(self.sibling, chunk, place).wait_recv()

    def side_rows(self, block, side):
        return block[side * self.rows : (side + 1) * self.rows]

    def unpack(self, out, tree):
        @pl.loop(0, self.half // CHUNK)
        def _(step):
            at = pl.multiple_of(step * CHUNK, CHUNK)
            blocks = [
                self.board[tree, chunk, place, :, pl.ds(at, CHUNK)].astype(F32)
                for place in range(self.size)
                for chunk in range(self.chunks)
            ]
            for side in range(2):
                whole = [self.side_rows(block, side) for block in blocks]
                out[tree, :, pl.ds(side * self.half + at, CHUNK)] = jnp.concatenate(
                    whole, axis=0
                ).astype(BF16)

    def unpack_chunk(self, out, chunk):
        @pl.loop(0, self.half // CHUNK)
        def _(step):
            at = pl.multiple_of(step * CHUNK, CHUNK)
            blocks = [
                self.board[tree, chunk, place, :, pl.ds(at, CHUNK)].astype(F32)
                for place in range(self.size)
                for tree in range(2)
            ]
            for side in range(2):
                whole = [self.side_rows(block, side) for block in blocks]
                out[chunk, :, pl.ds(side * self.half + at, CHUNK)] = jnp.concatenate(
                    whole, axis=0
                ).astype(BF16)

    def complete(self, out):
        for chunk in range(self.chunks):
            self.arrive(chunk)
        self.unpack(out, self.core)
        for chunk in range(self.chunks):
            self.arrive_over(chunk)
        self.unpack(out, self.sibling)

    def finish(self):
        for chunk in range(self.chunks):
            for place in range(self.size):
                @pl.when(self.direct(place))
                def _():
                    self.spread(chunk, place, self.me).wait_send()

                self.over(self.core, chunk, place).wait_send()

            for via, source, target, turn in self.relays:
                @pl.when(self.me == via)
                def _():
                    self.passed(chunk, source, target, turn).wait_send()


class Scatterer:
    def __init__(self, axis, rows, half):
        self.axis, self.half = axis, half
        self.size = size = lax.axis_size(axis)
        self.chunks = chunks = chunk_count(rows)
        self.rows = rows // chunks
        block = (2 * self.rows, half)
        self.scratch = [pltpu.VMEM((chunks, size) + block, BF16)] * 4
        self.scratch += [pltpu.VMEM((chunks,) + block, F32), pltpu.VMEM((chunks,) + block, BF16)]
        self.scratch += [SEM((chunks, size))] * 4 + [SEM((chunks,))] * 2

    def bind(self, refs):
        self.to_sib, self.from_sib, self.to_peer, self.from_peer, self.total, self.joint = refs[:6]
        self.sib_send, self.sib_recv, self.peer_send, self.peer_recv = refs[6:10]
        self.join_send, self.join_recv = refs[10:]
        self.core = lax.axis_index("section")
        self.sibling = 1 - self.core
        self.me = lax.axis_index(self.axis)
        self.sides = [(0, 1, 3), (3, 2, 0)] if self.axis == "dp" and self.size == 4 else []
        self.order = [0, 3, 1, 2] if self.sides else range(self.size)

    def over(self, chunk, place):
        return remote(
            self.to_sib.at[chunk, place], self.from_sib.at[chunk, place],
            self.sib_send.at[chunk, place], self.sib_recv.at[chunk, place],
            {"section": self.sibling},
        )

    def spread(self, chunk, place, slot):
        return remote(
            self.to_peer.at[chunk, place], self.from_peer.at[chunk, slot],
            self.peer_send.at[chunk, place], self.peer_recv.at[chunk, slot], {self.axis: place},
        )

    def by_way(self, chunk, via, target):
        return remote(
            self.to_peer.at[chunk, target], self.joint.at[chunk], self.join_send.at[chunk],
            self.join_recv.at[chunk], {self.axis: via},
        )

    def plain(self, place):
        ok = place != self.me
        for source, via, target in self.sides:
            if place == target:
                ok = ok & (self.me != source) & (self.me != via)
        return ok

    def expected(self, place):
        ok = place != self.me
        for source, via, target in self.sides:
            if place == source:
                ok = ok & (self.me != target)
        return ok

    def over_columns(self, body):
        @pl.loop(0, self.half // CHUNK)
        def _(step):
            body(pl.multiple_of(step * CHUNK, CHUNK))

    def absorb(self, chunk, mine):
        for place in self.order:
            self.over(chunk, place).wait_recv()

            def add(at):
                both = mine(place, at)
                both += self.from_sib[chunk, place, :, pl.ds(at, CHUNK)].astype(F32)
                self.to_peer[chunk, place, :, pl.ds(at, CHUNK)] = both.astype(BF16)

                @pl.when(place == self.me)
                def _():
                    self.total[chunk, :, pl.ds(at, CHUNK)] = both

            self.over_columns(add)

            for source, via, target in self.sides:
                if place == target:
                    @pl.when(self.me == source)
                    def _():
                        self.by_way(chunk, via, target).start()

            @pl.when(self.plain(place))
            def _():
                self.spread(chunk, place, self.me).start()

        for source, via, target in self.sides:
            @pl.when(self.me == via)
            def _():
                self.by_way(chunk, via, target).wait_recv()

                def add(at):
                    at = pl.ds(at, CHUNK)
                    both = self.to_peer[chunk, target, :, at].astype(F32)
                    both += self.joint[chunk, :, at].astype(F32)
                    self.to_peer[chunk, target, :, at] = both.astype(BF16)

                self.over_columns(add)
                self.spread(chunk, target, self.me).start()

    def collect(self, chunk):
        for place in self.order:
            @pl.when(self.expected(place))
            def _():
                self.spread(chunk, place, place).wait_recv()
                self.total[chunk] += self.from_peer[chunk, place].astype(F32)

        total = self.total[chunk]
        return jnp.concatenate([total[: self.rows], total[self.rows :]], axis=1)

    def finish(self):
        for chunk in range(self.chunks):
            for place in range(self.size):
                self.over(chunk, place).wait_send()

                @pl.when(self.plain(place))
                def _():
                    self.spread(chunk, place, self.me).wait_send()

            for source, via, target in self.sides:
                @pl.when(self.me == source)
                def _():
                    self.by_way(chunk, via, target).wait_send()

                @pl.when(self.me == via)
                def _():
                    self.spread(chunk, target, self.me).wait_send()


class RowScatterer(Scatterer):
    def packed(self, tree, chunk, place, at):
        rows = self.rows
        first = rows * (place * self.chunks + chunk)
        low = first // 16 * 16
        high = -(-(first + rows) // 16) * 16
        parts = [
            self.terms[tree, low:high, pl.ds(side * self.half + at, CHUNK)].astype(F32)[
                first - low : first - low + rows
            ]
            for side in range(2)
        ]
        return jnp.concatenate(parts, axis=0)

    def prepare(self, terms):
        self.terms = terms
        for chunk in range(self.chunks):
            for place in range(self.size):
                def pack(at):
                    self.to_sib[chunk, place, :, pl.ds(at, CHUNK)] = self.packed(
                        self.sibling, chunk, place, at
                    ).astype(BF16)

                self.over_columns(pack)

    def start(self):
        for chunk in range(self.chunks):
            for place in range(self.size):
                self.over(chunk, place).start()

    def send_on(self):
        for chunk in range(self.chunks):
            self.absorb(chunk, lambda place, at: self.packed(self.core, chunk, place, at))


class Staged(Part):
    def __init__(self, ins, outs, scratch, helpers):
        self.in_names, self.out_names, self.scratch_names = list(ins), list(outs), list(scratch)
        self.ins, self.outs = list(ins.values()), list(outs.values())
        self.helpers = helpers
        self.scratch = list(scratch.values())
        for helper in helpers:
            self.scratch += helper.scratch

    def bind(self, ins, outs, scratch):
        scratch = list(scratch)
        names = self.in_names + self.out_names + self.scratch_names
        count = len(self.scratch_names)
        for name, ref in zip(names, list(ins) + list(outs) + scratch[:count]):
            setattr(self, name, ref)
        del scratch[:count]
        for helper in self.helpers:
            helper.bind(scratch[: len(helper.scratch)])
            del scratch[: len(helper.scratch)]

    def finish(self):
        for helper in self.helpers:
            helper.finish()


def vmem_f32(*shape):
    return (jax.ShapeDtypeStruct(shape, F32), VMEM)


def vmem_bf16(*shape):
    return (jax.ShapeDtypeStruct(shape, BF16), VMEM)


def rows_at(chunk, rows):
    return pl.ds(pl.multiple_of(chunk * rows, 8), rows)


class LastHub(Staged):
    def __init__(self, terms, values, gain, add, other):
        rows, depth = values.shape
        half = depth // 2
        self.rows_in = RowScatterer("tensor", rows, half)
        self.rows_out = Gatherer("tensor", rows, half)
        super().__init__(
            {
                "terms": (terms, VMEM), "values": (values, VMEM), "gain": (gain, VMEM),
                "add": (add, VMEM), "other": (other, VMEM),
            },
            {
                "gain_grad": vmem_f32(1, depth),
                "gathered": vmem_bf16(2, self.rows_out.size * rows, depth),
            },
            {},
            [self.rows_in, self.rows_out],
        )

    def prepare(self):
        self.rows_in.prepare(self.terms)

    def start(self):
        self.rows_in.start()

    def run(self):
        self.rows_in.send_on()
        self.gain_grad[...] = jnp.zeros_like(self.gain_grad)
        for chunk in range(self.rows_in.chunks):
            at = rows_at(chunk, self.rows_in.rows)
            result, gain_grad = norm_back(
                self.rows_in.collect(chunk), self.values[at], self.gain[...]
            )
            self.gain_grad[...] += gain_grad
            self.rows_out.begin(chunk, result + self.add[at])

    def late(self):
        self.rows_out.complete(self.gathered)

        @pl.when(lax.axis_index("section") == 1)
        def _():
            self.gathered[...] = self.other[...]


class RowsOut(Staged):
    def __init__(self, own, other=None):
        rows, depth = own.shape
        self.rows_out = Gatherer("tensor", rows, depth // 2)
        self.has_other = other is not None
        super().__init__(
            {"own": (own, VMEM)} | ({"other": (other, VMEM)} if self.has_other else {}),
            {"gathered": vmem_bf16(2, self.rows_out.size * rows, depth)},
            {},
            [self.rows_out],
        )

    def start(self):
        for chunk in range(self.rows_out.chunks):
            self.rows_out.begin(chunk, self.own[rows_at(chunk, self.rows_out.rows)])

    def late(self):
        self.rows_out.complete(self.gathered)
        if self.has_other:
            @pl.when(lax.axis_index("section") == 0)
            def _():
                self.gathered[...] = self.other[...]


class FeedForward(Staged):
    def __init__(self, terms, own, gain, weights, forward, backward, extra):
        rows, depth = own.shape
        half = depth // 2
        units = weights[0].shape[0]
        self.has_forward, self.has_backward, self.units = forward, backward, units
        self.depth = depth
        self.size = size = lax.axis_size("dp")
        self.rows_in = RowScatterer("tensor", rows, half)
        self.spread_in = Gatherer("dp", rows, half)
        self.chunks, self.rows = self.rows_in.chunks, self.rows_in.rows
        chunks, chunk_rows = self.chunks, 2 * size * self.rows
        helpers = [self.rows_in, self.spread_in]
        tensor_rows = lax.axis_size("tensor") * rows
        matrix = pltpu.VMEM((units, depth), BF16)
        ins = {"terms": (terms, VMEM), "own": (own, VMEM), "gain": (gain, VMEM)}
        ins |= {name: (w, HBM) for name, w in zip(("gate_hbm", "up_hbm", "down_hbm"), weights)}
        ins |= {name: (value, VMEM) for name, value in extra.items()}
        outs = {}
        scratch = {"w_gate": matrix, "w_up": matrix, "w_down": matrix, "load": SEM((3,))}
        kept = pltpu.VMEM((size, 2 * self.rows, half), F32)
        if forward:
            outs |= {
                "middle": vmem_f32(rows, depth),
                "mlp_in": vmem_bf16(chunks, chunk_rows, depth),
                "hidden": vmem_bf16(chunks, chunk_rows, units),
                "own_out": vmem_f32(rows, depth),
            }
            self.back = Scatterer("dp", rows, half)
            helpers += [self.back]
            scratch["kept"] = kept
        if forward and not backward:
            outs |= {
                "out": vmem_bf16(2, tensor_rows, depth),
                "gate": vmem_bf16(chunks, chunk_rows, units),
                "up": vmem_bf16(chunks, chunk_rows, units),
            }
            self.out_rows = Gatherer("tensor", rows, half)
            helpers += [self.out_rows]
        if forward and backward:
            outs["grad_mlp"] = vmem_bf16(chunks, chunk_rows, depth)
            self.grad_in = Gatherer("dp", rows, half)
            helpers += [self.grad_in]
            scratch |= {
                "gate": pltpu.VMEM((chunks, chunk_rows, units), F32),
                "up": pltpu.VMEM((chunks, chunk_rows, units), F32),
            }
        if backward:
            outs |= {
                "grad_gate": vmem_bf16(chunks, chunk_rows, units),
                "grad_up": vmem_bf16(chunks, chunk_rows, units),
                "grad_middle": vmem_f32(rows, depth),
                "mlp_gain_grad": vmem_f32(1, depth),
                "grad_attn": vmem_bf16(2, tensor_rows, depth),
            }
            self.grad_back = Scatterer("dp", rows, half)
            self.grad_rows = Gatherer("tensor", rows, half)
            helpers += [self.grad_back, self.grad_rows]
            scratch["grad_kept"] = kept
        if backward and not forward:
            outs |= {
                "gain_grad": vmem_f32(1, depth),
                "grad_own": vmem_f32(rows, depth),
                "grad_mlp": vmem_bf16(chunks, chunk_rows, depth),
            }
        super().__init__(ins, outs, scratch, helpers)

    def loads(self):
        pairs = [(self.gate_hbm, self.w_gate), (self.up_hbm, self.w_up), (self.down_hbm, self.w_down)]
        return [
            pltpu.make_async_copy(src, dst, self.load.at[i]) for i, (src, dst) in enumerate(pairs)
        ]

    def prepare(self):
        for copy in self.loads():
            copy.start()
        self.rows_in.prepare(self.terms)

    def start(self):
        self.rows_in.start()
        if self.has_forward and self.has_backward:
            for chunk in range(self.chunks):
                self.grad_in.begin(chunk, self.grad_own[rows_at(chunk, self.rows)])

    def run(self):
        self.rows_in.send_on()
        if self.has_backward:
            self.mlp_gain_grad[...] = jnp.zeros_like(self.mlp_gain_grad)
        if not self.has_forward:
            self.gain_grad[...] = jnp.zeros_like(self.gain_grad)
        for chunk in range(self.chunks):
            at = rows_at(chunk, self.rows)
            total = self.rows_in.collect(chunk)
            if self.has_forward:
                middle = self.own[at] + total
                self.middle[at] = middle
                mean_sq = jnp.mean(middle * middle, axis=1, keepdims=True)
                normed = middle * lax.rsqrt(mean_sq + EPSILON) * self.gain[...]
                self.spread_in.begin(chunk, normed)
            else:
                result, gain_grad = norm_back(total, self.own[at], self.gain[...])
                self.gain_grad[...] += gain_grad
                result = (result + self.add[at]).astype(BF16).astype(F32)
                self.grad_own[at] = result
                self.spread_in.begin(chunk, result)
        for copy in self.loads():
            copy.wait()

        self.spread_in.arrive(0)
        if self.has_forward and self.has_backward:
            self.grad_in.arrive(0)

        @pl.loop(0, self.chunks)
        def _(chunk):
            self.spread_in.arrive_over(chunk)
            if self.has_forward:
                self.spread_in.unpack_chunk(self.mlp_in, chunk)
                self.forward_chunk(chunk)
            else:
                self.spread_in.unpack_chunk(self.grad_mlp, chunk)
            if self.has_forward and self.has_backward:
                self.grad_in.arrive_over(chunk)
                self.grad_in.unpack_chunk(self.grad_mlp, chunk)
            if self.has_backward:
                self.backward_chunk(chunk)

            @pl.when(chunk + 1 < self.chunks)
            def _():
                self.spread_in.arrive(chunk + 1)
                if self.has_forward and self.has_backward:
                    self.grad_in.arrive(chunk + 1)

            if self.has_forward:
                self.back.absorb(chunk, lambda place, at: self.kept[place, :, pl.ds(at, CHUNK)])
            if self.has_backward:
                self.grad_back.absorb(
                    chunk, lambda place, at: self.grad_kept[place, :, pl.ds(at, CHUNK)]
                )

            @pl.when(chunk > 0)
            def _():
                self.hand_back(chunk - 1)

        self.hand_back(self.chunks - 1)
        if self.has_backward:
            self.grad_rows.complete(self.grad_attn)
        else:
            self.out_rows.complete(self.out)

    def hand_back(self, chunk):
        at = rows_at(chunk, self.rows)
        if self.has_backward:
            values = self.middle if self.has_forward else self.middle_in
            gain = self.gain if self.has_forward else self.mlp_gain
            result, gain_grad = norm_back(self.grad_back.collect(chunk), values[at], gain[...])
            self.mlp_gain_grad[...] += gain_grad
            result += self.grad_own[at]
            self.grad_middle[at] = result
            self.grad_rows.begin(chunk, result)
        if self.has_forward:
            output = (self.middle[at] + self.back.collect(chunk)).astype(BF16).astype(F32)
            self.own_out[at] = output
            if not self.has_backward:
                self.out_rows.begin(chunk, output)

    def unit_tiles(self, body):
        tile = 256

        @pl.loop(0, self.units // tile)
        def _(step):
            body(pl.ds(pl.multiple_of(step * tile, tile), tile))

    def forward_chunk(self, chunk):
        def tile(at):
            rows = self.mlp_in[chunk]
            gate = dot_inner(rows, self.w_gate[at, :])
            up = dot_inner(rows, self.w_up[at, :])
            self.gate[chunk, :, at] = gate.astype(self.gate.dtype)
            self.up[chunk, :, at] = up.astype(self.up.dtype)
            self.hidden[chunk, :, at] = (gate * jax.nn.sigmoid(gate) * up).astype(BF16)

        self.unit_tiles(tile)
        self.terms_out(
            chunk, self.back, self.kept, lambda at: dot(self.hidden[chunk], self.w_down[:, at])
        )

    def backward_chunk(self, chunk):
        def tile(at):
            grad_hidden = dot_inner(self.grad_mlp[chunk], self.w_down[at, :])
            gate, up = self.gate[chunk, :, at].astype(F32), self.up[chunk, :, at].astype(F32)
            share = jax.nn.sigmoid(gate)
            act = gate * share
            self.grad_up[chunk, :, at] = (grad_hidden * act).astype(BF16)
            self.grad_gate[chunk, :, at] = (
                grad_hidden * up * (share + act * (1.0 - share))
            ).astype(BF16)

        self.unit_tiles(tile)
        self.terms_out(
            chunk, self.grad_back, self.grad_kept,
            lambda at: dot(self.grad_gate[chunk], self.w_gate[:, at])
            + dot(self.grad_up[chunk], self.w_up[:, at]),
        )

    def terms_out(self, chunk, scatterer, kept, product):
        rows, half = self.rows, self.depth // 2
        first = lax.axis_index("section") == 0

        @pl.loop(0, half // CHUNK)
        def _(step):
            low = pl.multiple_of(step * CHUNK, CHUNK)
            at = pl.ds(low, CHUNK)
            sides = [product(pl.ds(side * half + low, CHUNK)) for side in range(2)]
            for place in range(self.size):
                trees = []
                for tree in range(2):
                    start = (2 * place + tree) * rows
                    trees.append(
                        jnp.concatenate([side[start : start + rows] for side in sides], axis=0)
                    )
                kept[place, :, at] = jnp.where(first, trees[0], trees[1])
                scatterer.to_sib[chunk, place, :, at] = jnp.where(
                    first, trees[1], trees[0]
                ).astype(BF16)

        for place in range(self.size):
            scatterer.over(chunk, place).start()


def finish_weights(first, second, attn_first, attn_second, arrived, widths, core, rows_out, tile=256):
    units, own_depth = first[0].shape
    q_width, k_width, _, _ = widths
    starts = [0, q_width, q_width + k_width, 0]
    steps = units // tile
    count = len(rows_out)

    def transposed(block):
        size = block.shape[1]
        rows = lax.broadcasted_iota(jnp.int32, (size, size), 0)
        identity = (rows == lax.broadcasted_iota(jnp.int32, rows.shape, 1)).astype(BF16)
        return dot_inner(identity, block)

    def kernel(core_ref, *refs):
        ins, passed_in = refs[:12], refs[12 : 12 + count]
        (gate, up, down), attn_outs = refs[12 + count : 15 + count], refs[15 + count : 19 + count]
        for src, dst in zip(passed_in, refs[19 + count :]):
            dst[...] = src[...]

        on_first = core_ref[0] == 0
        picked = [jnp.where(on_first, ins[i][...], ins[3 + i][...]) for i in range(3)]
        gate[...] = transposed(picked[0])
        up[...] = transposed(picked[1])
        down[...] = picked[2].astype(F32)

        @pl.when(pl.program_id(0) == 0)
        def _():
            for index, (out, start, width) in enumerate(zip(attn_outs, starts, widths)):
                at = pl.ds(start, width)
                mine, other, came = (ins[6 + 2 * i + index // 3][:, at] for i in range(3))
                halves = [jnp.where(on_first, mine, came), jnp.where(on_first, came, other)]
                for half, values in enumerate(halves):
                    if index == 3:
                        out[pl.ds(half * width, width)] = transposed(values)
                    else:
                        out[:, pl.ds(half * width, width)] = values.astype(F32)

    def whole(shape):
        return pl.BlockSpec(shape, lambda step: (0, 0))

    tall = pl.BlockSpec((tile, own_depth), lambda step: (step, 0))
    wide = pl.BlockSpec((own_depth, tile), lambda step: (0, step))
    attn_ins = [*attn_first, *attn_second, *arrived]
    flat_rows = [item.reshape(-1, item.shape[-1]) for item in rows_out]
    passed = [
        pl.BlockSpec((item.shape[0] // steps, item.shape[1]), lambda step: (step, 0))
        for item in flat_rows
    ]
    attn_shapes = [(own_depth, 2 * width) for width in widths[:3]] + [(2 * q_width, own_depth)]
    shapes = [(own_depth, units)] * 2 + [(units, own_depth)] + attn_shapes
    return pl.pallas_call(
        kernel,
        grid=(steps,),
        out_shape=[jax.ShapeDtypeStruct(shape, F32) for shape in shapes]
        + [jax.ShapeDtypeStruct(item.shape, item.dtype) for item in flat_rows],
        in_specs=[pl.BlockSpec(memory_space=pltpu.SMEM)]
        + [tall] * 6
        + [whole(item.shape) for item in attn_ins]
        + passed,
        out_specs=[wide, wide, tall] + [whole(shape) for shape in attn_shapes] + passed,
        cost_estimate=pl.CostEstimate(flops=0, bytes_accessed=25_000_000, transcendentals=0),
        compiler_params=pltpu.CompilerParams(vmem_limit_bytes=60 << 20),
    )(core.reshape(1), *first, *second, *attn_ins, *flat_rows)


def hub_plain(terms, own_args, body, own_outs, scatter, gathers):
    total = None
    if scatter:
        mine = lax.psum_scatter(terms, "section", scatter_dimension=0, tiled=True)
        mine = lax.psum_scatter(mine, scatter, scatter_dimension=1, tiled=True)[0]
        total = mine.astype(F32)

    class Cell:
        def __setitem__(self, _, value):
            self.value = value

    cells = [Cell() for _ in own_outs]
    result = body(total, own_args, cells).astype(BF16)
    gathered = [
        lax.all_gather(lax.all_gather(result, axis, axis=0, tiled=True), "section", axis=0)
        for axis in gathers
    ]
    return [cell.value for cell in cells] + gathered


def with_cargo(part, cargo, axes, collective_id, cost_us, vmem):
    outs = fused(cargo + [part], axes, bool(cargo), collective_id, cost_us, vmem)
    return outs[-1], outs[:-1]


def norm_back(total, values, gain):
    scale = lax.rsqrt(jnp.mean(values * values, axis=1, keepdims=True) + EPSILON)
    unit = values * scale
    gain_grad = jnp.sum(total * unit, axis=0, keepdims=True)
    scaled = total * gain
    along = jnp.mean(scaled * unit, axis=1, keepdims=True)
    return ((scaled - unit * along) * scale, gain_grad)


def norm_body(total, args, outs):
    middle = args[0] + total
    outs[0][...] = middle
    return rms_scale(middle, args[1])


def add_body(total, args, outs):
    result = args[0] + total
    outs[0][...] = result
    return result


def norm_back_body(total, args, outs):
    result, outs[1][...] = norm_back(total, args[0], args[1])
    result += args[2]
    outs[0][...] = result
    return result


def embed(q_pre, k_pre, q_scale, k_scale, cos_table, sine_table):
    queries = rms_scale(q_pre, q_scale)
    keys = rms_scale(k_pre, k_scale)
    return (
        rotate(queries, cos_table[:, :, None], sine_table[:, :, None]),
        rotate(keys, cos_table, sine_table),
    )


def attn_forward(hidden_in, weights, gains, slot, gather):
    attn_scale, _, q_scale, k_scale = gains
    w_qkv, w_out = weights[:2]
    allowed, cos_table, sine_table = slot
    trees, row_count, depth = hidden_in.shape
    q_width = w_out.shape[0]
    normed = rms_scale(hidden_in.astype(F32), attn_scale).astype(BF16).reshape(-1, depth)
    qkv = dot(normed, w_qkv).reshape(trees, row_count, -1)
    q_pre = qkv[:, :, :q_width].reshape(trees, row_count, -1, HD)
    k_pre = qkv[:, :, q_width : q_width + HD]
    value_bf = qkv[:, :, q_width + HD :].astype(BF16)
    queries, keys_rot = embed(q_pre, k_pre, q_scale, k_scale, cos_table, sine_table)
    query_bf = queries.astype(BF16)
    kv_all = gather(jnp.concatenate([keys_rot.astype(BF16), value_bf], axis=2))
    key_all = kv_all[:, :, :HD]
    value_all = kv_all[:, :, HD:]
    scores = masked_scores(query_bf, key_all, allowed)
    row_max = jnp.max(scores, axis=-1, keepdims=True)
    exp_scores = jnp.exp(scores - row_max)
    row_total = jnp.sum(exp_scores, axis=-1, keepdims=True)
    prob_bf = (exp_scores / row_total).astype(BF16)
    log_total = row_max + jnp.log(row_total)
    attended = jnp.einsum("bgrt,btd->brgd", prob_bf, value_all, preferred_element_type=F32)
    attended_bf = attended.reshape(trees * row_count, -1).astype(BF16)
    terms = dot(attended_bf, w_out).astype(BF16).reshape(trees, row_count, depth)
    saved = (normed, q_pre, k_pre, query_bf, key_all, value_all, log_total, attended_bf)
    return (terms, saved)


def attn_backward(grad_attn, saved, weights, gains, slot, scatter):
    _, _, q_scale, k_scale = gains
    w_qkv, w_out = weights[:2]
    allowed, cos_table, sine_table = slot
    normed, q_pre, k_pre, query_bf, key_all, value_all, log_total, attended_bf = saved
    trees, row_count = query_bf.shape[:2]
    depth = normed.shape[1]
    grad_attn = grad_attn.reshape(-1, depth)
    grad_heads = dot_inner(grad_attn, w_out).astype(BF16).reshape(query_bf.shape)
    scores = masked_scores(query_bf, key_all, allowed)
    prob_full = jnp.exp(scores - log_total)
    grad_prob = jnp.einsum("brgd,btd->bgrt", grad_heads, value_all, preferred_element_type=F32)
    row_dot = jnp.sum(prob_full * grad_prob, axis=-1, keepdims=True)
    grad_scores = (prob_full * (grad_prob - row_dot)).astype(BF16)
    scale_factor = HD ** (-0.5)
    grad_query = (
        jnp.einsum("bgrt,btd->brgd", grad_scores, key_all, preferred_element_type=F32)
        * scale_factor
    )
    grad_key_all = (
        jnp.einsum("bgrt,brgd->btd", grad_scores, query_bf, preferred_element_type=F32)
        * scale_factor
    )
    grad_value_all = jnp.einsum(
        "bgrt,brgd->btd", prob_full.astype(BF16), grad_heads, preferred_element_type=F32
    )
    grad_kv = scatter(jnp.concatenate([grad_key_all, grad_value_all], axis=2).astype(BF16))
    _, embedding_pull = jax.vjp(
        partial(embed, cos_table=cos_table, sine_table=sine_table), q_pre, k_pre, q_scale, k_scale
    )
    grad_q_pre, grad_k_pre, grad_q_scale, grad_k_scale = embedding_pull(
        (grad_query, grad_kv[:, :, :HD].astype(F32))
    )
    qkv_grad = jnp.concatenate(
        [
            grad_q_pre.astype(BF16).reshape(trees, row_count, -1),
            grad_k_pre.astype(BF16),
            grad_kv[:, :, HD:].astype(BF16),
        ],
        axis=2,
    ).reshape(trees * row_count, -1)
    terms = dot_inner(qkv_grad, w_qkv).astype(BF16).reshape(trees, row_count, depth)
    return (terms, [(normed, qkv_grad), (grad_attn, attended_bf)], [grad_q_scale, grad_k_scale])


def plain_layers(hidden, own_in, grad_own, weights, gains, slot, shared_kv):
    depth = own_in.shape[1]
    own_shape = own_in.shape

    def gather(own):
        return lax.all_gather(own, "dp", axis=1, tiled=True)

    def scatter(whole):
        total = lax.psum_scatter(whole, "dp", scatter_dimension=1, tiled=True)
        if shared_kv:
            total = lax.psum(total, "section")
            total = jnp.where(lax.axis_index("section") == 0, total, jnp.zeros_like(total))
        return total

    outputs, kept = [], []
    for layer in range(2):
        _, _, w_gate, w_up, w_down = weights[layer]
        terms, saved = attn_forward(hidden, weights[layer], gains[layer], slot, gather)
        mlp_scale = gains[layer][1][None]
        middle, mlp_in = hub_plain(
            terms, [own_in, mlp_scale], norm_body, [own_shape], "tensor", ["dp"]
        )
        mlp_in = mlp_in.reshape(-1, depth)
        gate, up = dot_inner(mlp_in, w_gate), dot_inner(mlp_in, w_up)
        hidden_bf = swiglu(gate, up).astype(BF16)
        terms = dot(hidden_bf, w_down).astype(BF16).reshape(2, -1, depth)
        kept.append((own_in, saved, middle, mlp_in, gate, up, hidden_bf))
        own_in, hidden = hub_plain(terms, [middle], add_body, [own_shape], "dp", ["tensor"])
        own_in = own_in.astype(BF16).astype(F32)
        outputs.append(hidden)

    own_outs = [own_shape, (1, depth)]
    grads, products, gain_grads = [None, None], [None, None], [None, None]
    (grad_mlp,) = hub_plain(None, [grad_own], lambda total, args, outs: args[0], [], None, ["dp"])
    for layer in (1, 0):
        _, _, w_gate, w_up, w_down = weights[layer]
        own_in, saved, middle, mlp_in, gate, up, hidden_bf = kept[layer]
        grad_mlp = grad_mlp.reshape(-1, depth)
        _, pull = jax.vjp(swiglu, gate, up)
        grad_gate, grad_up = (item.astype(BF16) for item in pull(dot_inner(grad_mlp, w_down)))
        terms = (dot(grad_gate, w_gate) + dot(grad_up, w_up)).astype(BF16).reshape(2, -1, depth)
        grad_middle, mlp_gain_grad, grad_attn = hub_plain(
            terms, [middle, gains[layer][1][None], grad_own], norm_back_body, own_outs, "dp",
            ["tensor"],
        )
        terms, pairs, head_grads = attn_backward(
            grad_attn, saved, weights[layer], gains[layer], slot, scatter
        )
        grad_own, gain_grad, grads[layer], grad_next = hub_plain(
            terms, [own_in, gains[layer][0][None], grad_middle], norm_back_body, own_outs, "tensor",
            ["tensor", "dp"],
        )
        grad_own = grad_own.astype(BF16).astype(F32)
        pairs += [(grad_gate, mlp_in), (grad_up, mlp_in), (hidden_bf, grad_mlp)]
        products[layer] = pairs
        gain_grads[layer] = jnp.concatenate([gain_grad[0], mlp_gain_grad[0], *head_grads])
        grad_mlp = grad_next
    return (outputs, grads, products, gain_grads)


def swap_cores(mine, other):
    core = lax.axis_index("section")
    arrived = lax.ppermute(other, "section", [(0, 1), (1, 0)])
    return (jnp.where(core == 0, mine, arrived), jnp.where(core == 0, arrived, mine))


def on_device(
    inputs, cotangent, seg_ids, parents, order, attn_gain, w_query, w_key, w_value, w_out,
    q_gain, k_gain, mlp_gain, w_gate, w_up, w_down,
):
    core = lax.axis_index("section")
    data_index = lax.axis_index("dp")
    tensor_index = lax.axis_index("tensor")
    dp_size = lax.axis_size("dp")
    tensor_size = lax.axis_size("tensor")
    trees, row_count, depth = inputs.shape
    own_rows = row_count // tensor_size
    row_start = data_index * row_count
    own_depth = w_query.shape[1]
    q_width = w_query.shape[2] // 2
    shared_kv = w_key.shape[2] == HD
    k_width = HD if shared_kv else w_key.shape[2] // 2
    own_units = w_gate.shape[2]
    share = own_units // (2 * dp_size)

    def pick(stacked, index):
        return lax.dynamic_index_in_dim(stacked, index, 0, keepdims=False)

    fast = (
        own_rows % 8 == 0
        and depth % (2 * CHUNK) == 0
        and row_count % 16 == 0
        and share % 16 == 0
        and own_depth % 128 == 0
        and not shared_kv
    )

    def halves(width, array):
        return [array[:, :width], array[:, array.shape[1] - width :]]

    unit_mats = [w_gate[0].T, w_up[0].T, w_down[0]]
    qkv_width = q_width + 2 * k_width
    gains_own = jnp.concatenate([attn_gain[0], mlp_gain[0], q_gain[0], k_gain[0]]).astype(F32)

    def spread_units(rows):
        return lax.all_gather(rows, "tensor", axis=0, tiled=True)

    def tied(value, *before):
        return lax.optimization_barrier((value, *before))[0]

    if fast:
        line = ["section", "dp"]
        everyone = ["section", "dp", "tensor"]
        (gate_rows, up_rows), (gains_all,) = fused(
            [UnitsOut(unit_mats[:2], 0), SharedRows(gains_own.reshape(-1, 128))], line, True, 1, 45, 40
        )
        shards = AttnShards(w_query[0], w_key[0], w_value[0], w_out[0])
        shards.arrays[0] = tied(shards.arrays[0], gate_rows)
        (w_qkv, w_heads), (down_rows,), (attn_shard,) = fused(
            [AttnOut(shards, 0), UnitsOut(unit_mats[2:], 0), HalfOver(shards)], line, True, 2, 80, 40
        )
        first_weights = [w_qkv, w_heads, spread_units(gate_rows), spread_units(up_rows)]
    else:
        gains_all = lax.all_gather(gains_own, ("section", "dp"))
        attn_halves = jnp.stack(
            [
                jnp.concatenate(parts, axis=1)
                for parts in zip(
                    halves(q_width, w_query[0]),
                    halves(k_width, w_key[0]),
                    halves(k_width, w_value[0]),
                    halves(q_width, w_out[0].T),
                )
            ]
        )
        attn_shards = swap_cores(pick(attn_halves, core), pick(attn_halves, 1 - core))
        unit_blocks = jnp.stack(unit_mats).reshape(3, 2, dp_size, share, own_depth)
        unit_blocks = unit_blocks.transpose(1, 2, 0, 3, 4)
        unit_shards = swap_cores(pick(unit_blocks, core), pick(unit_blocks, 1 - core))
        both_weights = []
        for layer in range(2):
            attn_all = lax.all_gather(attn_shards[layer], "dp", axis=0, tiled=True)
            pieces = exchange(unit_shards[layer], "dp")
            pieces = pieces.transpose(1, 2, 0, 3).reshape(3, share, depth)
            both_weights.append(
                (
                    attn_all[:, :qkv_width], attn_all[:, qkv_width:].T,
                    *(spread_units(pieces[i]) for i in range(3)),
                )
            )

    gains_all = gains_all.reshape(2, dp_size, -1)
    gains = [
        (
            gains_all[layer, :, :own_depth].reshape(depth),
            gains_all[layer, :, own_depth : 2 * own_depth].reshape(depth),
            gains_all[layer, 0, 2 * own_depth : 2 * own_depth + HD],
            gains_all[layer, 0, 2 * own_depth + HD :],
        )
        for layer in range(2)
    ]

    def slot_setup(slot_index):
        tree_id = pick(order, slot_index)
        allowed, row_positions = path_mask(
            pick(seg_ids, tree_id), pick(parents, tree_id), row_start, row_count
        )
        cos_table, sine_table = rope_tables(row_positions, HD)
        return (pick(inputs, tree_id), allowed, cos_table[:, 0], sine_table[:, 0])

    setups = [slot_setup(i) for i in range(trees)]
    hidden, *slot = (jnp.stack(item) for item in zip(*setups))

    def own_part(whole):
        return lax.dynamic_slice_in_dim(
            pick(whole, core), tensor_index * own_rows, own_rows, 0
        )

    own_in = own_part(hidden).astype(F32)
    grad_own = own_part(cotangent).astype(F32)

    def weight_products(pairs):
        return [dot_outer(left, right).astype(BF16) for left, right in pairs]

    def scatter_units(products):
        return [
            lax.psum_scatter(item, "tensor", scatter_dimension=0, tiled=True) for item in products
        ]

    def scatter_shards(products):
        return lax.psum_scatter(
            jnp.concatenate(products, axis=1), "dp", scatter_dimension=0, tiled=True
        )

    if fast:
        def units_on(*which):
            return [UnitsOut([unit_mats[i] for i in which], 1)]

        def kv_gather(own, cargo, collective_id, carried):
            (whole,), outs = with_cargo(GatherKV(own), cargo, everyone, collective_id, 40, 40)
            carried += outs
            return whole.reshape(trees, -1, 2 * HD)

        def kv_scatter(whole, cargo, collective_id, carried):
            part = ScatterKV(whole.reshape(trees, dp_size, row_count, 2 * HD))
            (total,), outs = with_cargo(part, cargo, everyone, collective_id, 30, 40)
            carried += outs
            return total

        def in_order(pairs):
            done = []
            for left, right in pairs:
                done += weight_products([(tied(left, *done[-1:]), right)])
            return done

        def flat(array):
            return array.reshape(-1, array.shape[-1])

        carried = []
        terms, saved_first = attn_forward(
            hidden, first_weights, gains[0], slot,
            lambda own: kv_gather(
                tied(own, *first_weights[2:]), [UnitsSpread(down_rows)] + units_on(0, 1, 2), 3, carried
            ),
        )
        (down_all,), (gate_rows, up_rows, down_rows) = carried
        first_weights.append(down_all)
        part = FeedForward(
            terms, own_in, gains[0][1][None], first_weights[2:], True, False, {}
        )
        outs, ((down_next,),) = with_cargo(part, [UnitsSpread(down_rows)], everyone, 4, 90, 56)
        middle_first, mlp_in_first, hidden_first, own_next, output_first, gate_first, up_first = outs
        attn_next = lax.all_gather(tied(attn_shard, gate_rows), "dp", axis=0)
        second_weights = [
            attn_next[:, :own_depth].reshape(depth, -1),
            attn_next[:, own_depth:].transpose(1, 0, 2).reshape(q_width, depth),
            spread_units(gate_rows), spread_units(up_rows),
        ]
        carried = []
        terms, saved_second = attn_forward(
            output_first, second_weights, gains[1], slot,
            lambda own: kv_gather(tied(own, second_weights[2]), [], 5, carried),
        )
        second_weights.append(down_next)
        part = FeedForward(
            terms, own_next, gains[1][1][None], second_weights[2:], True, True,
            {"grad_own": grad_own},
        )
        outs, _ = with_cargo(part, [], everyone, 6, 100, 60)
        (
            middle, mlp_in, hidden_bf, own_second, grad_mlp,
            grad_gate, grad_up, grad_middle, mlp_gain_second, grad_attn,
        ) = outs
        products = in_order([(flat(grad_gate), flat(mlp_in)), (flat(grad_up), flat(mlp_in))])
        unit_second = scatter_units(products)
        carried = []
        terms, pairs, head_second = attn_backward(
            grad_attn, saved_second, second_weights, gains[1], slot,
            lambda whole: kv_scatter(
                tied(whole, *products), [RowsOut(own_second, output_first)], 7, carried
            ),
        )
        ((layer_out,),) = carried
        unit_second += scatter_units(
            weight_products([(tied(flat(hidden_bf), layer_out), flat(grad_mlp))])
        )
        pairs = weight_products(pairs)
        attn_second = scatter_shards([tied(pairs[0], unit_second[1]), pairs[1]])
        terms = tied(terms, unit_second[0])
        part = FeedForward(
            terms, own_next, gains[1][0][None], first_weights[2:], False, True,
            {
                "add": grad_middle, "gate": gate_first, "up": up_first,
                "middle_in": middle_first, "mlp_gain": gains[0][1][None],
            },
        )
        outs, (home_second,) = with_cargo(
            part, [UnitsHome(unit_second[:1], 1)], everyone, 8, 90, 60
        )
        (
            grad_gate, grad_up, grad_middle, mlp_gain_first, grad_attn,
            attn_gain_second, own_incoming, grad_mlp,
        ) = outs
        products = in_order(
            [(flat(grad_gate), flat(mlp_in_first)), (flat(grad_up), flat(mlp_in_first))]
        )
        grad_attn = tied(grad_attn, *unit_second[1:], *products)
        unit_first = scatter_units([products[0], tied(products[1], attn_second)])
        carried = []
        terms, pairs, head_first = attn_backward(
            grad_attn, saved_first, first_weights, gains[0], slot,
            lambda whole: kv_scatter(
                whole, [UnitsHome(unit_second[1:], 1), RowsOut(own_incoming)], 9, carried
            ),
        )
        home_second += carried[0]
        (incoming_second,) = carried[1]
        unit_first += scatter_units(
            weight_products([(tied(flat(hidden_first), incoming_second), flat(grad_mlp))])
        )
        parts = [
            ScatterKV(item.reshape(dp_size, 4, own_depth // 4, -1), True, BF16, True)
            for item in weight_products(pairs)
        ]
        part = LastHub(terms, own_in, gains[0][0][None], grad_middle, incoming_second)
        (attn_gain_first, input_grad), (*attn_first, home_first) = with_cargo(
            part, parts + [UnitsHome(unit_first[:1], 0)], everyone, 10, 60, 56
        )
        attn_first = [item.reshape(own_depth, -1) for (item,) in attn_first]
        attn_second = [attn_second[:, :qkv_width], attn_second[:, qkv_width:]]
        gain_grads = [
            jnp.concatenate([attn_gain_first[0], mlp_gain_first[0], *head_first]),
            jnp.concatenate([attn_gain_second[0], mlp_gain_second[0], *head_second]),
        ]
    else:
        outputs, grads, products, gain_grads = plain_layers(
            hidden, own_in, grad_own, both_weights, gains, slot, shared_kv
        )
        layer_out = jnp.where(core == 0, *outputs)
        input_grad = jnp.where(core == 0, *grads)
        weight_grads = []
        for pairs in products:
            whole = weight_products(pairs)
            weight_grads.append((scatter_shards(whole[:2]), scatter_units(whole[2:])))

    gain_total = jnp.stack(gain_grads)
    if fast:
        others = [
            Swap(jnp.where(core == 0, second, first))
            for first, second in zip(attn_first, attn_second)
        ]
        (gain_total,), *arrived, down_home = fused(
            [TotalOverAll(gain_total.reshape(-1, 128)), *others, UnitsHome(unit_first[1:], 0)],
            everyone, True, 11, 60, 40,
        )
        grad_gate, grad_up, grad_down, *attn_grads, layer_out, input_grad = finish_weights(
            home_first + down_home, home_second, attn_first, attn_second,
            [item for (item,) in arrived], (q_width, k_width, k_width, q_width), core,
            (layer_out, input_grad),
        )
        layer_out = layer_out.reshape(trees, row_count, depth)
        input_grad = input_grad.reshape(trees, row_count, depth)
        gain_total = gain_total.reshape(2, -1)
    else:
        def bring_home(first, second):
            mine, other = jnp.where(core == 0, first, second), jnp.where(core == 0, second, first)
            arrived = lax.ppermute(other, "section", [(0, 1), (1, 0)])
            return (jnp.where(core == 0, mine, arrived), jnp.where(core == 0, arrived, mine))

        def pieces_of(grad):
            return exchange(
                jnp.stack(grad).reshape(3, share, dp_size, own_depth).transpose(2, 0, 1, 3), "dp"
            )

        attn_home = bring_home(weight_grads[0][0], weight_grads[1][0])
        unit_home = jnp.stack(bring_home(pieces_of(weight_grads[0][1]), pieces_of(weight_grads[1][1])))
        unit_home = unit_home.transpose(2, 0, 1, 3, 4).reshape(3, own_units, own_depth).astype(F32)
        grad_gate, grad_up, grad_down = unit_home[0].T, unit_home[1].T, unit_home[2]
        gain_total = lax.psum(gain_total, ("section", "dp", "tensor"))

        def joined(start, width):
            parts = [half[:, start : start + width] for half in attn_home]
            if shared_kv and start in (q_width, q_width + k_width):
                return parts[0].astype(F32)
            return jnp.concatenate(parts, axis=1).astype(F32)

        attn_grads = [
            joined(0, q_width), joined(q_width, k_width), joined(q_width + k_width, k_width),
            joined(qkv_width, q_width).T,
        ]

    gain_own = pick(gain_total, core)
    share_width = attn_gain.shape[1]
    attn_gain_grad = lax.dynamic_slice_in_dim(gain_own, data_index * share_width, share_width, 0)
    mlp_gain_grad = lax.dynamic_slice_in_dim(
        gain_own, depth + data_index * share_width, share_width, 0
    )
    return (
        layer_out[None],
        input_grad[None],
        attn_gain_grad[None],
        *(item[None] for item in attn_grads),
        gain_own[2 * depth : 2 * depth + HD][None],
        gain_own[2 * depth + HD :][None],
        mlp_gain_grad[None],
        grad_gate[None],
        grad_up[None],
        grad_down[None],
    )


def solution(mesh):
    rows = P(None, "dp", None)
    wide = P("section", "dp", "tensor")
    tall = P("section", "tensor", "dp")
    gain = P("section", "dp")
    head_gain = P("section", None)
    slots = P("section", None, "dp", None)
    in_specs = (
        rows, rows, P(), P(), P(), gain, wide, wide, wide, tall, head_gain, head_gain, gain,
        wide, wide, tall,
    )
    out_specs = (
        slots, slots, gain, wide, wide, wide, tall, head_gain, head_gain, gain, wide, wide, tall,
    )
    return jax.shard_map(
        on_device, mesh=mesh, in_specs=in_specs, out_specs=out_specs, check_vma=False
    )
```

```python
from functools import partial

import jax
import jax.numpy as jnp
from jax import lax
from jax.experimental import pallas as pl
from jax.experimental.pallas import tpu as pltpu
from jax.sharding import PartitionSpec as P

HD = 128
TRUNK = 512
BRANCH = 96
NB = 4
TREE = 1152
SEGS = 9


EPSILON = 1e-06
THETA = 1000000.0
MASKED = -1e30
F32 = jnp.float32
BF16 = jnp.bfloat16


def rms_scale(values, weight_gain):
    mean_sq = jnp.mean(values * values, axis=-1, keepdims=True)
    return values * lax.rsqrt(mean_sq + EPSILON) * weight_gain


def rotate(values, cos_table, sine_table):
    middle_at = values.shape[-1] // 2
    leading = values[..., :middle_at]
    trailing = values[..., middle_at:]
    return jnp.concatenate(
        [leading * cos_table - trailing * sine_table, trailing * cos_table + leading * sine_table],
        axis=-1,
    )


def rope_tables(positions, head_dim):
    half_steps = jnp.arange(head_dim // 2, dtype=F32)
    inverse = THETA ** (-2.0 * half_steps / head_dim)
    angles = positions.astype(F32)[:, None] * inverse[None, :]
    return (jnp.cos(angles)[:, None, :], jnp.sin(angles)[:, None, :])


def swiglu(gate_in, up_in):
    return jax.nn.silu(gate_in) * up_in


def embed_heads(q_pre, k_pre, q_scale, k_scale, cos_table, sine_table):
    row_count = q_pre.shape[0]
    queries = rms_scale(q_pre.reshape(row_count, -1, HD), q_scale)
    keys_part = rms_scale(k_pre.reshape(row_count, -1, HD), k_scale)
    return (rotate(queries, cos_table, sine_table), rotate(keys_part, cos_table, sine_table))


def tree_layout(seg_row, parent_row):
    labels = jnp.arange(SEGS, dtype=jnp.int32)
    places = jnp.arange(TREE, dtype=jnp.int32)
    member = seg_row[None, :] == labels[:, None]
    starts = jnp.min(jnp.where(member, places[None, :], TREE), axis=1)
    depth_base = jnp.where(labels == 0, 0, jnp.where(labels <= NB, TRUNK, TRUNK + BRANCH))
    shifts = depth_base - starts
    positions = places + jnp.sum(jnp.where(member, shifts[:, None], 0), axis=0)
    grandparent = jnp.sum(
        jnp.where(parent_row[:, None] == labels[None, :], parent_row[None, :], 0), axis=1
    )
    ancestor = (
        (labels[None, :] == labels[:, None])
        | (labels[None, :] == parent_row[:, None])
        | (labels[None, :] == grandparent[:, None])
    )
    return (positions, member.astype(F32), ancestor.astype(F32))


def path_mask(seg_row, parent_row, row_start, row_count):
    positions, member, ancestor = tree_layout(seg_row, parent_row)
    member_rows = lax.dynamic_slice_in_dim(member, row_start, row_count, 1)
    seg_rows = lax.dynamic_slice_in_dim(seg_row, row_start, row_count, 0)
    reach_table = jnp.dot(jnp.dot(member_rows.T, ancestor), member)
    places = jnp.arange(TREE, dtype=jnp.int32)
    row_places = row_start + jnp.arange(row_count, dtype=jnp.int32)
    same_seg = seg_rows[:, None] == seg_row[None, :]
    causal = places[None, :] <= row_places[:, None]
    allowed = (reach_table > 0.5) & (jnp.logical_not(same_seg) | causal)
    row_positions = lax.dynamic_slice_in_dim(positions, row_start, row_count, 0)
    return (allowed, row_positions)


OUTER = (((0,), (0,)), ((), ()))
INNER = (((1,), (1,)), ((), ()))


def dot(left, right):
    return jnp.dot(left, right, preferred_element_type=F32)


def dot_inner(left, right):
    return lax.dot_general(left, right, INNER, preferred_element_type=F32)


def dot_outer(left, right):
    return lax.dot_general(left, right, OUTER, preferred_element_type=F32)


def exchange(pieces, axis):
    size = lax.axis_size(axis)
    me = lax.axis_index(axis)
    got = jnp.zeros_like(pieces)
    own = lax.dynamic_index_in_dim(pieces, me, 0, keepdims=True)
    got = lax.dynamic_update_slice_in_dim(got, own, me, 0)
    for step in range(1, size):
        other = me ^ step
        piece = lax.dynamic_index_in_dim(pieces, other, 0, keepdims=True)
        arrived = lax.ppermute(piece, axis, [(i, i ^ step) for i in range(size)])
        got = lax.dynamic_update_slice_in_dim(got, arrived, other, 0)
    return got


def masked_scores(query_bf, key_all, allowed):
    raw_scores = jnp.einsum(
        "brgd,btd->bgrt", query_bf, key_all, preferred_element_type=F32
    ) * HD ** (-0.5)
    return jnp.where(allowed[:, None], raw_scores, MASKED)


MESH = pl.DeviceIdType.MESH
CHUNK = 256
SEM = pltpu.SemaphoreType.DMA
VMEM = pl.BlockSpec(memory_space=pltpu.VMEM)
HBM = pl.BlockSpec(memory_space=pl.ANY)


def remote(src, dst, send_sem, recv_sem, device_id):
    return pltpu.make_async_remote_copy(
        src_ref=src, dst_ref=dst, send_sem=send_sem, recv_sem=recv_sem,
        device_id=device_id, device_id_type=MESH,
    )


def greet(axes, across):
    barrier = pltpu.get_barrier_semaphore()
    count = 0
    for axis in axes:
        size = lax.axis_size(axis)
        me = lax.axis_index(axis)
        for step in range(1, size):
            pl.semaphore_signal(
                barrier, inc=1, device_id={axis: lax.rem(me + step, size)}, device_id_type=MESH
            )
        count += size - 1
    if across:
        size = lax.axis_size("dp")
        me = lax.axis_index("dp")
        sibling = 1 - lax.axis_index("section")
        for step in range(1, size):
            pl.semaphore_signal(
                barrier, inc=1, device_id={"section": sibling, "dp": lax.rem(me + step, size)},
                device_id_type=MESH,
            )
        count += size - 1
    pl.semaphore_wait(barrier, count)


class Part:
    ins, outs, scratch = (), (), ()

    def bind(self, ins, outs, scratch):
        self.in_refs, self.out_refs, self.refs = ins, outs, scratch

    def prepare(self):
        pass

    def start(self):
        pass

    def run(self):
        pass

    def pass_on(self):
        pass

    def late(self):
        pass

    def finish(self):
        pass


def fused(parts, axes, across, collective_id, cost_us, vmem):
    counts = [(len(part.ins), len(part.outs), len(part.scratch)) for part in parts]

    def kernel(*refs):
        refs = list(refs)
        groups = []
        for kind in range(3):
            groups.append([])
            for count in counts:
                groups[kind].append(refs[: count[kind]])
                del refs[: count[kind]]
        for part, ins, outs, scratch in zip(parts, *groups):
            part.bind(ins, outs, scratch)
        for part in parts:
            part.prepare()
        greet(axes, across)
        for part in parts:
            part.start()
        for part in reversed(parts):
            part.run()
        for part in reversed(parts):
            part.pass_on()
        for part in reversed(parts):
            part.late()
        for part in parts:
            part.finish()

    ins = [item for part in parts for item in part.ins]
    outs = [item for part in parts for item in part.outs]
    results = pl.pallas_call(
        kernel,
        out_shape=[item[0] for item in outs],
        in_specs=[item[1] for item in ins],
        out_specs=[item[1] for item in outs],
        scratch_shapes=[item for part in parts for item in part.scratch],
        cost_estimate=pl.CostEstimate(
            flops=0, bytes_accessed=cost_us * 3_000_000, transcendentals=0
        ),
        compiler_params=pltpu.CompilerParams(
            collective_id=collective_id, has_side_effects=True, vmem_limit_bytes=vmem << 20
        ),
    )(*[item[0] for item in ins])
    results = list(results)
    split = []
    for count in counts:
        split.append(results[: count[1]])
        del results[: count[1]]
    return split


def columns_of(place, width):
    return pl.ds(pl.multiple_of(place * width, width), width)


class UnitsOut(Part):
    def __init__(self, mats, layer):
        self.layer, self.count = layer, len(mats)
        self.size = lax.axis_size("dp")
        rows, self.width = mats[0].shape
        self.share = rows // (2 * self.size)
        self.ins = [(mat, HBM) for mat in mats]
        shape = jax.ShapeDtypeStruct((self.share, self.size * self.width), BF16)
        self.outs = [(shape, HBM)] * self.count
        self.scratch = [SEM((self.count,)), SEM((self.count, 2, self.size)), SEM((self.count, self.size))]

    def bind(self, ins, outs, scratch):
        self.src, self.dst = ins, outs
        self.keep, self.send, self.recv = scratch
        self.core, self.me = lax.axis_index("section"), lax.axis_index("dp")

    def piece(self, index, core, place):
        start = pl.multiple_of((core * self.size + place) * self.share, self.share)
        return self.src[index].at[pl.ds(start, self.share)]

    def lands(self, index, slot):
        return self.dst[index].at[:, columns_of(slot, self.width)]

    def copy(self, index, core, place, slot):
        return remote(
            self.piece(index, core, place), self.lands(index, slot),
            self.send.at[index, core, place], self.recv.at[index, slot],
            {"section": core, "dp": place},
        )

    def local(self, index):
        return pltpu.make_async_copy(
            self.piece(index, self.layer, self.me), self.lands(index, self.me), self.keep.at[index]
        )

    def targets(self):
        for index in range(self.count):
            for core in range(2):
                for place in range(self.size):
                    yield index, core, place, (place != self.me) | (core != self.layer)

    def start(self):
        @pl.when(self.core == self.layer)
        def _():
            for index, core, place, is_other in self.targets():
                @pl.when(is_other)
                def _():
                    self.copy(index, core, place, self.me).start()

            for index in range(self.count):
                self.local(index).start()

    def finish(self):
        for index in range(self.count):
            for place in range(self.size):
                @pl.when((self.core != self.layer) | (place != self.me))
                def _():
                    self.copy(index, 0, 0, place).wait_recv()

        @pl.when(self.core == self.layer)
        def _():
            for index, core, place, is_other in self.targets():
                @pl.when(is_other)
                def _():
                    self.copy(index, core, place, self.me).wait_send()

            for index in range(self.count):
                self.local(index).wait()


class UnitsHome(Part):
    def __init__(self, mats, layer):
        self.layer, self.count = layer, len(mats)
        self.size = lax.axis_size("dp")
        self.share, depth = mats[0].shape
        self.width = depth // self.size
        self.ins = [(mat, HBM) for mat in mats]
        shape = jax.ShapeDtypeStruct((2 * self.size * self.share, self.width), BF16)
        self.outs = [(shape, HBM)] * self.count
        self.scratch = [SEM((self.count,)), SEM((self.count, self.size)), SEM((self.count, 2, self.size))]

    def bind(self, ins, outs, scratch):
        self.src, self.dst = ins, outs
        self.keep, self.send, self.recv = scratch
        self.core, self.me = lax.axis_index("section"), lax.axis_index("dp")

    def lands(self, index, core, slot):
        start = pl.multiple_of((core * self.size + slot) * self.share, self.share)
        return self.dst[index].at[pl.ds(start, self.share)]

    def copy(self, index, place, core, slot):
        return remote(
            self.src[index].at[:, columns_of(place, self.width)], self.lands(index, core, slot),
            self.send.at[index, place], self.recv.at[index, core, slot],
            {"section": self.layer, "dp": place},
        )

    def local(self, index):
        return pltpu.make_async_copy(
            self.src[index].at[:, columns_of(self.me, self.width)],
            self.lands(index, self.layer, self.me), self.keep.at[index],
        )

    def start(self):
        for index in range(self.count):
            for place in range(self.size):
                @pl.when((self.core != self.layer) | (place != self.me))
                def _():
                    self.copy(index, place, self.core, self.me).start()

            @pl.when(self.core == self.layer)
            def _():
                self.local(index).start()

    def finish(self):
        for index in range(self.count):
            @pl.when(self.core == self.layer)
            def _():
                for core in range(2):
                    for place in range(self.size):
                        @pl.when((core != self.layer) | (place != self.me))
                        def _():
                            self.copy(index, 0, core, place).wait_recv()

                self.local(index).wait()

            for place in range(self.size):
                @pl.when((self.core != self.layer) | (place != self.me))
                def _():
                    self.copy(index, place, self.core, self.me).wait_send()


class UnitsSpread(Part):
    def __init__(self, rows):
        self.size = lax.axis_size("tensor")
        self.share, depth = rows.shape
        self.ins = [(rows, HBM)]
        self.outs = [(jax.ShapeDtypeStruct((self.size * self.share, depth), BF16), HBM)]
        self.scratch = [SEM, SEM((self.size,)), SEM((self.size,))]

    def bind(self, ins, outs, scratch):
        (self.src,), (self.dst,), (self.keep, self.send, self.recv) = ins, outs, scratch
        self.me = lax.axis_index("tensor")

    def lands(self, slot):
        return self.dst.at[pl.ds(pl.multiple_of(slot * self.share, self.share), self.share)]

    def copy(self, place, slot):
        return remote(
            self.src, self.lands(slot), self.send.at[place], self.recv.at[slot], {"tensor": place}
        )

    def start(self):
        for place in range(self.size):
            @pl.when(place != self.me)
            def _():
                self.copy(place, self.me).start()

        pltpu.make_async_copy(self.src, self.lands(self.me), self.keep).start()

    def finish(self):
        for place in range(self.size):
            @pl.when(place != self.me)
            def _():
                self.copy(place, place).wait_recv()
                self.copy(place, self.me).wait_send()

        pltpu.make_async_copy(self.src, self.lands(self.me), self.keep).wait()


class SharedRows(Part):
    def __init__(self, own):
        self.size = lax.axis_size("dp")
        self.ins = [(own, VMEM)]
        self.outs = [(jax.ShapeDtypeStruct((2, self.size) + own.shape, F32), VMEM)]
        self.scratch = [SEM((2, self.size)), SEM((2, self.size))]

    def copy(self, core, place, from_core, from_place):
        return remote(
            self.in_refs[0], self.out_refs[0].at[from_core, from_place],
            self.refs[0].at[core, place], self.refs[1].at[from_core, from_place],
            {"section": core, "dp": place},
        )

    def others(self):
        core, me = lax.axis_index("section"), lax.axis_index("dp")
        for other in range(2):
            for place in range(self.size):
                yield other, place, (other != core) | (place != me)

    def start(self):
        core, me = lax.axis_index("section"), lax.axis_index("dp")
        for other, place, is_other in self.others():
            @pl.when(is_other)
            def _():
                self.copy(other, place, core, me).start()

        self.out_refs[0][core, me] = self.in_refs[0][...]

    def finish(self):
        core, me = lax.axis_index("section"), lax.axis_index("dp")
        for other, place, is_other in self.others():
            @pl.when(is_other)
            def _():
                self.copy(other, place, other, place).wait_recv()
                self.copy(other, place, core, me).wait_send()


def passed_on(place, me):
    return ((place == 3) & (me <= 1)) | ((place == 0) & (me >= 2))


def line_relays(size):
    return [(2, 1, 3, 0), (2, 0, 3, 1), (1, 2, 0, 0), (1, 3, 0, 1)] if size == 4 else []


def line_order(size):
    return [1, 2, 0, 3] if size == 4 else list(range(size))


class AttnShards:
    def __init__(self, w_query, w_key, w_value, w_out):
        self.arrays = [w_query, w_key, w_value, w_out]
        self.depth = w_query.shape[0]
        self.q_width, self.k_width = w_query.shape[1] // 2, w_key.shape[1] // 2
        self.width = self.q_width + 2 * self.k_width
        half = self.depth // 2
        parts = self.q_width // 2
        self.items = [
            (0, lambda ref, core: ref.at[pl.ds(0, half), columns_of(core, self.q_width)]),
            (0, lambda ref, core: ref.at[pl.ds(half, half), columns_of(core, self.q_width)]),
            (1, lambda ref, core: ref.at[:, columns_of(core, self.k_width)]),
            (2, lambda ref, core: ref.at[:, columns_of(core, self.k_width)]),
            (3, lambda ref, core: ref.at[pl.ds(core * self.q_width, parts)]),
            (3, lambda ref, core: ref.at[pl.ds(core * self.q_width + parts, parts)]),
        ]
        q_width, k_width, depth = self.q_width, self.k_width, self.depth
        self.qkv_rows = [(0, half), (half, half), (0, depth), (0, depth)]
        self.qkv_columns = [
            (0, q_width), (0, q_width), (q_width, k_width), (q_width + k_width, k_width)
        ]
        self.out_rows = [(0, parts), (parts, parts)]

    def source(self, refs, index, core):
        array, cut = self.items[index]
        return cut(refs[array], core)

    def lands(self, qkv, out, index, slot):
        if index < 4:
            (start, rows), (left, columns) = self.qkv_rows[index], self.qkv_columns[index]
            at = pl.multiple_of(slot * self.depth + start, rows)
            return qkv.at[pl.ds(at, rows), pl.ds(left, columns)]
        start, rows = self.out_rows[index - 4]
        return out.at[pl.ds(start, rows), columns_of(slot, self.depth)]


class AttnOut(Part):
    def __init__(self, shards, layer):
        self.layer, self.shards = layer, shards
        self.size = lax.axis_size("dp")
        self.count = len(shards.items)
        depth = self.size * shards.depth
        self.ins = [(array, HBM) for array in shards.arrays]
        self.outs = [
            (jax.ShapeDtypeStruct((depth, shards.width), BF16), HBM),
            (jax.ShapeDtypeStruct((shards.q_width, depth), BF16), HBM),
        ]
        self.scratch = [
            SEM((self.count,)), SEM((2, self.size, self.count)), SEM((self.size, self.count)),
            SEM((self.count, 2)),
        ]

    def bind(self, ins, outs, scratch):
        self.src = ins
        self.qkv, self.out = outs
        self.keep, self.send, self.recv, self.relay_send = scratch
        self.core, self.me = lax.axis_index("section"), lax.axis_index("dp")

    def lands(self, index, slot):
        return self.shards.lands(self.qkv, self.out, index, slot)

    def copy(self, core, place, slot, index):
        return remote(
            self.shards.source(self.src, index, core), self.lands(index, slot),
            self.send.at[core, place, index], self.recv.at[slot, index],
            {"section": core, "dp": place},
        )

    def relay(self, source, target, turn, index):
        block = self.lands(index, source)
        return remote(
            block, block, self.relay_send.at[index, turn], self.recv.at[source, index],
            {"dp": target},
        )

    def local(self, index):
        return pltpu.make_async_copy(
            self.shards.source(self.src, index, self.layer), self.lands(index, self.me),
            self.keep.at[index],
        )

    def targets(self):
        for index in range(self.count):
            for core in range(2):
                for place in range(self.size):
                    sent = (place != self.me) | (core != self.layer)
                    if self.size == 4:
                        sent = sent & jnp.logical_not(passed_on(place, self.me))
                    yield core, place, index, sent

    def start(self):
        @pl.when(self.core == self.layer)
        def _():
            for core, place, index, sent in self.targets():
                @pl.when(sent)
                def _():
                    self.copy(core, place, self.me, index).start()

            for index in range(self.count):
                self.local(index).start()

    def run(self):
        for index in range(self.count):
            for place in line_order(self.size):
                @pl.when((self.core != self.layer) | (place != self.me))
                def _():
                    self.copy(0, 0, place, index).wait_recv()

                for via, source, target, turn in line_relays(self.size):
                    if source == place:
                        @pl.when(self.me == via)
                        def _():
                            self.relay(source, target, turn, index).start()

    def finish(self):
        @pl.when(self.core == self.layer)
        def _():
            for core, place, index, sent in self.targets():
                @pl.when(sent)
                def _():
                    self.copy(core, place, self.me, index).wait_send()

            for index in range(self.count):
                self.local(index).wait()

        for via, source, target, turn in line_relays(self.size):
            @pl.when(self.me == via)
            def _():
                for index in range(self.count):
                    self.relay(source, target, turn, index).wait_send()


class HalfOver(Part):
    def __init__(self, shards):
        self.shards = shards
        self.count = len(shards.items)
        rows = shards.depth + shards.q_width
        self.ins = [(array, HBM) for array in shards.arrays]
        self.outs = [(jax.ShapeDtypeStruct((rows, shards.depth), BF16), HBM)]
        self.scratch = [SEM((self.count,)), SEM((self.count,)), SEM((self.count,))]

    def lands(self, index):
        depth, q_width = self.shards.depth, self.shards.q_width
        packed = self.out_refs[0]
        return self.shards.lands(
            packed.at[pl.ds(0, depth)], packed.at[pl.ds(depth, q_width)], index, 0
        )

    def over(self, index):
        return remote(
            self.shards.source(self.in_refs, index, 0), self.lands(index), self.refs[0].at[index],
            self.refs[1].at[index], {"section": 0},
        )

    def keep(self, index):
        return pltpu.make_async_copy(
            self.shards.source(self.in_refs, index, 1), self.lands(index), self.refs[2].at[index]
        )

    def start(self):
        @pl.when(lax.axis_index("section") == 1)
        def _():
            for index in range(self.count):
                self.over(index).start()
                self.keep(index).start()

    def finish(self):
        @pl.when(lax.axis_index("section") == 1)
        def _():
            for index in range(self.count):
                self.over(index).wait_send()
                self.keep(index).wait()

        @pl.when(lax.axis_index("section") == 0)
        def _():
            for index in range(self.count):
                self.over(index).wait_recv()


class Swap(Part):
    def __init__(self, own):
        self.ins = [(own, HBM)]
        self.outs = [(jax.ShapeDtypeStruct(own.shape, own.dtype), HBM)]
        self.scratch = [SEM, SEM]

    def start(self):
        sibling = 1 - lax.axis_index("section")
        self.copy = remote(
            self.in_refs[0], self.out_refs[0], self.refs[0], self.refs[1], {"section": sibling}
        )
        self.copy.start()

    def finish(self):
        self.copy.wait()


class GatherKV(Part):
    def __init__(self, own):
        trees, rows, width = own.shape
        self.trees, self.size = trees, lax.axis_size("dp")
        self.ins = [(own, VMEM)]
        self.outs = [(jax.ShapeDtypeStruct((trees, self.size, rows, width), BF16), VMEM)]
        self.scratch = [SEM((self.size, trees)), SEM((self.size, trees)), SEM((trees, 2))]

    def bind(self, ins, outs, scratch):
        (self.own,), (self.out,) = ins, outs
        self.send, self.recv, self.relay_send = scratch
        self.me = lax.axis_index("dp")

    def copy(self, place, slot, tree):
        return remote(
            self.own.at[tree], self.out.at[tree, slot], self.send.at[place, tree],
            self.recv.at[slot, tree], {"dp": place},
        )

    def relay(self, source, target, turn, tree):
        return remote(
            self.out.at[tree, source], self.out.at[tree, source], self.relay_send.at[tree, turn],
            self.recv.at[source, tree], {"dp": target},
        )

    def targets(self):
        for tree in range(self.trees):
            for place in range(self.size):
                sent = place != self.me
                if self.size == 4:
                    sent = sent & jnp.logical_not(passed_on(place, self.me))
                yield place, tree, sent

    def start(self):
        for place, tree, sent in self.targets():
            @pl.when(sent)
            def _():
                self.copy(place, self.me, tree).start()

        self.out[:, self.me] = self.own[...]

    def run(self):
        for tree in range(self.trees):
            for place in line_order(self.size):
                @pl.when(place != self.me)
                def _():
                    self.copy(place, place, tree).wait_recv()

                for via, source, target, turn in line_relays(self.size):
                    if source == place:
                        @pl.when(self.me == via)
                        def _():
                            self.relay(source, target, turn, tree).start()

    def finish(self):
        for place, tree, sent in self.targets():
            @pl.when(sent)
            def _():
                self.copy(place, self.me, tree).wait_send()

        for via, source, target, turn in line_relays(self.size):
            @pl.when(self.me == via)
            def _():
                for tree in range(self.trees):
                    self.relay(source, target, turn, tree).wait_send()


class ScatterKV(Part):
    def __init__(self, whole, place_first=False, kept_as=F32, far_only=False):
        self.place_first = place_first
        trees, size, rows, width = whole.shape
        if place_first:
            trees, size = size, trees
        self.trees, self.size = trees, size
        self.sides = [(0, 1, 2, 0), (0, 1, 3, 1), (3, 2, 1, 0), (3, 2, 0, 1)] if size == 4 else []
        if far_only:
            self.sides = self.sides[1::2]
        self.ins = [(whole, VMEM)]
        self.outs = [(jax.ShapeDtypeStruct((trees, rows, width), kept_as), VMEM)]
        self.scratch = [
            pltpu.VMEM((rows, width), F32),
            pltpu.VMEM((size, trees, rows, width), BF16),
            pltpu.VMEM((2, trees, rows, width), BF16),
            SEM((size, trees)), SEM((size, trees)), SEM((2, trees)), SEM((2, trees)),
        ]

    def bind(self, ins, outs, scratch):
        (self.terms,), (self.out,) = ins, outs
        self.total, self.boxes, self.joint, self.send, self.recv, self.join_send, self.join_recv = scratch
        self.me = lax.axis_index("dp")

    def term(self, tree, place):
        return self.terms.at[place, tree] if self.place_first else self.terms.at[tree, place]

    def copy(self, place, slot, tree):
        return remote(
            self.term(tree, place), self.boxes.at[slot, tree], self.send.at[place, tree],
            self.recv.at[slot, tree], {"dp": place},
        )

    def by_way(self, via, target, turn, tree):
        return remote(
            self.term(tree, target), self.joint.at[turn, tree], self.join_send.at[turn, tree],
            self.join_recv.at[turn, tree], {"dp": via},
        )

    def joined(self, via, target, turn, tree):
        return remote(
            self.joint.at[turn, tree], self.boxes.at[via, tree], self.send.at[target, tree],
            self.recv.at[via, tree], {"dp": target},
        )

    def plain(self, place):
        ok = place != self.me
        for source, via, target, turn in self.sides:
            if place == target:
                ok = ok & (self.me != source) & (self.me != via)
        return ok

    def expected(self, place):
        ok = place != self.me
        for source, via, target, turn in self.sides:
            if place == source:
                ok = ok & (self.me != target)
        return ok

    def start(self):
        for tree in range(self.trees):
            for source, via, target, turn in self.sides:
                @pl.when(self.me == source)
                def _():
                    self.by_way(via, target, turn, tree).start()

            for place in range(self.size):
                @pl.when(self.plain(place))
                def _():
                    self.copy(place, self.me, tree).start()

    def pass_on(self):
        for tree in range(self.trees):
            for source, via, target, turn in self.sides:
                @pl.when(self.me == via)
                def _():
                    self.by_way(via, target, turn, tree).wait_recv()
                    both = self.joint[turn, tree].astype(F32)
                    both += self.term(tree, target)[...].astype(F32)
                    self.joint[turn, tree] = both.astype(BF16)
                    self.joined(via, target, turn, tree).start()

    def late(self):
        for tree in range(self.trees):
            self.total[...] = self.term(tree, self.me)[...].astype(F32)
            for place in line_order(self.size):
                @pl.when(self.expected(place))
                def _():
                    self.copy(place, place, tree).wait_recv()
                    self.total[...] += self.boxes[place, tree].astype(F32)

            self.out[tree] = self.total[...].astype(self.out.dtype)

    def finish(self):
        for tree in range(self.trees):
            for place in range(self.size):
                @pl.when(self.plain(place))
                def _():
                    self.copy(place, self.me, tree).wait_send()

            for source, via, target, turn in self.sides:
                @pl.when(self.me == source)
                def _():
                    self.by_way(via, target, turn, tree).wait_send()

                @pl.when(self.me == via)
                def _():
                    self.joined(via, target, turn, tree).wait_send()


class TotalOverAll(Part):
    axes = ("section", "tensor", "dp")

    def __init__(self, own):
        sizes = [lax.axis_size(axis) for axis in self.axes]
        self.ins = [(own, VMEM)]
        self.outs = [(jax.ShapeDtypeStruct(own.shape, F32), VMEM)]
        self.scratch = [pltpu.VMEM((size,) + own.shape, F32) for size in sizes]
        self.scratch += [SEM((size,)) for size in sizes] * 2

    def run(self):
        out = self.out_refs[0]
        out[...] = self.in_refs[0][...]
        for axis, box, send, recv in zip(self.axes, self.refs[:3], self.refs[3:6], self.refs[6:9]):
            size, me = lax.axis_size(axis), lax.axis_index(axis)
            box[me] = out[...]

            def spread(place, slot):
                return remote(box.at[me], box.at[slot], send.at[place], recv.at[slot], {axis: place})

            for place in range(size):
                @pl.when(place != me)
                def _():
                    spread(place, me).start()

            for place in range(size):
                @pl.when(place != me)
                def _():
                    spread(place, place).wait_recv()
                    spread(place, me).wait_send()

            total = box[0]
            for place in range(1, size):
                total += box[place]
            out[...] = total


def chunk_count(rows):
    return 3 if rows % 24 == 0 else 1


class Gatherer:
    def __init__(self, axis, rows, half):
        self.axis, self.half = axis, half
        self.size = size = lax.axis_size(axis)
        self.chunks = chunks = chunk_count(rows)
        self.rows = rows // chunks
        self.scratch = [pltpu.VMEM((2, chunks, size, 2 * self.rows, half), BF16)]
        self.scratch += [SEM((chunks, size))] * 4 + [SEM((chunks, 2))]

    def bind(self, refs):
        self.board, self.send, self.recv, self.sib_send, self.sib_recv, self.relay_send = refs
        self.core = lax.axis_index("section")
        self.sibling = 1 - self.core
        self.me = lax.axis_index(self.axis)
        self.relays = line_relays(self.size) if self.axis == "dp" else []
        self.order = line_order(self.size) if self.axis == "dp" else range(self.size)

    def direct(self, place):
        sent = place != self.me
        if self.relays:
            sent = sent & jnp.logical_not(passed_on(place, self.me))
        return sent

    def spread(self, chunk, place, slot):
        block = self.board.at[self.core, chunk, slot]
        return remote(
            block, block, self.send.at[chunk, place], self.recv.at[chunk, slot], {self.axis: place}
        )

    def passed(self, chunk, source, target, turn):
        block = self.board.at[self.core, chunk, source]
        return remote(
            block, block, self.relay_send.at[chunk, turn], self.recv.at[chunk, source],
            {self.axis: target},
        )

    def over(self, tree, chunk, slot):
        block = self.board.at[tree, chunk, slot]
        return remote(
            block, block, self.sib_send.at[chunk, slot], self.sib_recv.at[chunk, slot],
            {"section": self.sibling},
        )

    def begin(self, chunk, result):
        half = self.half
        piece = jnp.concatenate([result[:, :half], result[:, half:]], axis=0)
        self.board[self.core, chunk, self.me] = piece.astype(BF16)
        for place in range(self.size):
            @pl.when(self.direct(place))
            def _():
                self.spread(chunk, place, self.me).start()

        self.over(self.core, chunk, self.me).start()

    def arrive(self, chunk):
        for place in self.order:
            @pl.when(place != self.me)
            def _():
                self.spread(chunk, place, place).wait_recv()

            for via, source, target, turn in self.relays:
                if source == place:
                    @pl.when(self.me == via)
                    def _():
                        self.passed(chunk, source, target, turn).start()

            @pl.when(place != self.me)
            def _():
                self.over(self.core, chunk, place).start()

    def arrive_over(self, chunk):
        for place in range(self.size):
            self.over(self.sibling, chunk, place).wait_recv()

    def side_rows(self, block, side):
        return block[side * self.rows : (side + 1) * self.rows]

    def unpack(self, out, tree):
        @pl.loop(0, self.half // CHUNK)
        def _(step):
            at = pl.multiple_of(step * CHUNK, CHUNK)
            blocks = [
                self.board[tree, chunk, place, :, pl.ds(at, CHUNK)].astype(F32)
                for place in range(self.size)
                for chunk in range(self.chunks)
            ]
            for side in range(2):
                whole = [self.side_rows(block, side) for block in blocks]
                out[tree, :, pl.ds(side * self.half + at, CHUNK)] = jnp.concatenate(
                    whole, axis=0
                ).astype(BF16)

    def unpack_chunk(self, out, chunk):
        @pl.loop(0, self.half // CHUNK)
        def _(step):
            at = pl.multiple_of(step * CHUNK, CHUNK)
            blocks = [
                self.board[tree, chunk, place, :, pl.ds(at, CHUNK)].astype(F32)
                for place in range(self.size)
                for tree in range(2)
            ]
            for side in range(2):
                whole = [self.side_rows(block, side) for block in blocks]
                out[chunk, :, pl.ds(side * self.half + at, CHUNK)] = jnp.concatenate(
                    whole, axis=0
                ).astype(BF16)

    def complete(self, out):
        for chunk in range(self.chunks):
            self.arrive(chunk)
        self.unpack(out, self.core)
        for chunk in range(self.chunks):
            self.arrive_over(chunk)
        self.unpack(out, self.sibling)

    def finish(self):
        for chunk in range(self.chunks):
            for place in range(self.size):
                @pl.when(self.direct(place))
                def _():
                    self.spread(chunk, place, self.me).wait_send()

                self.over(self.core, chunk, place).wait_send()

            for via, source, target, turn in self.relays:
                @pl.when(self.me == via)
                def _():
                    self.passed(chunk, source, target, turn).wait_send()


class Scatterer:
    def __init__(self, axis, rows, half):
        self.axis, self.half = axis, half
        self.size = size = lax.axis_size(axis)
        self.chunks = chunks = chunk_count(rows)
        self.rows = rows // chunks
        block = (2 * self.rows, half)
        self.scratch = [pltpu.VMEM((chunks, size) + block, BF16)] * 4
        self.scratch += [pltpu.VMEM((chunks,) + block, F32), pltpu.VMEM((chunks,) + block, BF16)]
        self.scratch += [SEM((chunks, size))] * 4 + [SEM((chunks,))] * 2

    def bind(self, refs):
        self.to_sib, self.from_sib, self.to_peer, self.from_peer, self.total, self.joint = refs[:6]
        self.sib_send, self.sib_recv, self.peer_send, self.peer_recv = refs[6:10]
        self.join_send, self.join_recv = refs[10:]
        self.core = lax.axis_index("section")
        self.sibling = 1 - self.core
        self.me = lax.axis_index(self.axis)
        self.sides = [(0, 1, 3), (3, 2, 0)] if self.axis == "dp" and self.size == 4 else []
        self.order = [0, 3, 1, 2] if self.sides else range(self.size)

    def over(self, chunk, place):
        return remote(
            self.to_sib.at[chunk, place], self.from_sib.at[chunk, place],
            self.sib_send.at[chunk, place], self.sib_recv.at[chunk, place],
            {"section": self.sibling},
        )

    def spread(self, chunk, place, slot):
        return remote(
            self.to_peer.at[chunk, place], self.from_peer.at[chunk, slot],
            self.peer_send.at[chunk, place], self.peer_recv.at[chunk, slot], {self.axis: place},
        )

    def by_way(self, chunk, via, target):
        return remote(
            self.to_peer.at[chunk, target], self.joint.at[chunk], self.join_send.at[chunk],
            self.join_recv.at[chunk], {self.axis: via},
        )

    def plain(self, place):
        ok = place != self.me
        for source, via, target in self.sides:
            if place == target:
                ok = ok & (self.me != source) & (self.me != via)
        return ok

    def expected(self, place):
        ok = place != self.me
        for source, via, target in self.sides:
            if place == source:
                ok = ok & (self.me != target)
        return ok

    def over_columns(self, body):
        @pl.loop(0, self.half // CHUNK)
        def _(step):
            body(pl.multiple_of(step * CHUNK, CHUNK))

    def absorb(self, chunk, mine):
        for place in self.order:
            self.over(chunk, place).wait_recv()

            def add(at):
                both = mine(place, at)
                both += self.from_sib[chunk, place, :, pl.ds(at, CHUNK)].astype(F32)
                self.to_peer[chunk, place, :, pl.ds(at, CHUNK)] = both.astype(BF16)

                @pl.when(place == self.me)
                def _():
                    self.total[chunk, :, pl.ds(at, CHUNK)] = both

            self.over_columns(add)

            for source, via, target in self.sides:
                if place == target:
                    @pl.when(self.me == source)
                    def _():
                        self.by_way(chunk, via, target).start()

            @pl.when(self.plain(place))
            def _():
                self.spread(chunk, place, self.me).start()

        for source, via, target in self.sides:
            @pl.when(self.me == via)
            def _():
                self.by_way(chunk, via, target).wait_recv()

                def add(at):
                    at = pl.ds(at, CHUNK)
                    both = self.to_peer[chunk, target, :, at].astype(F32)
                    both += self.joint[chunk, :, at].astype(F32)
                    self.to_peer[chunk, target, :, at] = both.astype(BF16)

                self.over_columns(add)
                self.spread(chunk, target, self.me).start()

    def collect(self, chunk):
        for place in self.order:
            @pl.when(self.expected(place))
            def _():
                self.spread(chunk, place, place).wait_recv()
                self.total[chunk] += self.from_peer[chunk, place].astype(F32)

        total = self.total[chunk]
        return jnp.concatenate([total[: self.rows], total[self.rows :]], axis=1)

    def finish(self):
        for chunk in range(self.chunks):
            for place in range(self.size):
                self.over(chunk, place).wait_send()

                @pl.when(self.plain(place))
                def _():
                    self.spread(chunk, place, self.me).wait_send()

            for source, via, target in self.sides:
                @pl.when(self.me == source)
                def _():
                    self.by_way(chunk, via, target).wait_send()

                @pl.when(self.me == via)
                def _():
                    self.spread(chunk, target, self.me).wait_send()


class RowScatterer(Scatterer):
    def packed(self, tree, chunk, place, at):
        rows = self.rows
        first = rows * (place * self.chunks + chunk)
        low = first // 16 * 16
        high = -(-(first + rows) // 16) * 16
        parts = [
            self.terms[tree, low:high, pl.ds(side * self.half + at, CHUNK)].astype(F32)[
                first - low : first - low + rows
            ]
            for side in range(2)
        ]
        return jnp.concatenate(parts, axis=0)

    def prepare(self, terms):
        self.terms = terms
        for chunk in range(self.chunks):
            for place in range(self.size):
                def pack(at):
                    self.to_sib[chunk, place, :, pl.ds(at, CHUNK)] = self.packed(
                        self.sibling, chunk, place, at
                    ).astype(BF16)

                self.over_columns(pack)

    def start(self):
        for chunk in range(self.chunks):
            for place in range(self.size):
                self.over(chunk, place).start()

    def send_on(self):
        for chunk in range(self.chunks):
            self.absorb(chunk, lambda place, at: self.packed(self.core, chunk, place, at))


class Staged(Part):
    def __init__(self, ins, outs, scratch, helpers):
        self.in_names, self.out_names, self.scratch_names = list(ins), list(outs), list(scratch)
        self.ins, self.outs = list(ins.values()), list(outs.values())
        self.helpers = helpers
        self.scratch = list(scratch.values())
        for helper in helpers:
            self.scratch += helper.scratch

    def bind(self, ins, outs, scratch):
        scratch = list(scratch)
        names = self.in_names + self.out_names + self.scratch_names
        count = len(self.scratch_names)
        for name, ref in zip(names, list(ins) + list(outs) + scratch[:count]):
            setattr(self, name, ref)
        del scratch[:count]
        for helper in self.helpers:
            helper.bind(scratch[: len(helper.scratch)])
            del scratch[: len(helper.scratch)]

    def finish(self):
        for helper in self.helpers:
            helper.finish()


def vmem_f32(*shape):
    return (jax.ShapeDtypeStruct(shape, F32), VMEM)


def vmem_bf16(*shape):
    return (jax.ShapeDtypeStruct(shape, BF16), VMEM)


def rows_at(chunk, rows):
    return pl.ds(pl.multiple_of(chunk * rows, 8), rows)


class LastHub(Staged):
    def __init__(self, terms, values, gain, add, other):
        rows, depth = values.shape
        half = depth // 2
        self.rows_in = RowScatterer("tensor", rows, half)
        self.rows_out = Gatherer("tensor", rows, half)
        super().__init__(
            {
                "terms": (terms, VMEM), "values": (values, VMEM), "gain": (gain, VMEM),
                "add": (add, VMEM), "other": (other, VMEM),
            },
            {
                "gain_grad": vmem_f32(1, depth),
                "gathered": vmem_bf16(2, self.rows_out.size * rows, depth),
            },
            {},
            [self.rows_in, self.rows_out],
        )

    def prepare(self):
        self.rows_in.prepare(self.terms)

    def start(self):
        self.rows_in.start()

    def run(self):
        self.rows_in.send_on()
        self.gain_grad[...] = jnp.zeros_like(self.gain_grad)
        for chunk in range(self.rows_in.chunks):
            at = rows_at(chunk, self.rows_in.rows)
            result, gain_grad = norm_back(
                self.rows_in.collect(chunk), self.values[at], self.gain[...]
            )
            self.gain_grad[...] += gain_grad
            self.rows_out.begin(chunk, result + self.add[at])

    def late(self):
        self.rows_out.complete(self.gathered)

        @pl.when(lax.axis_index("section") == 1)
        def _():
            self.gathered[...] = self.other[...]


class RowsOut(Staged):
    def __init__(self, own, other=None):
        rows, depth = own.shape
        self.rows_out = Gatherer("tensor", rows, depth // 2)
        self.has_other = other is not None
        super().__init__(
            {"own": (own, VMEM)} | ({"other": (other, VMEM)} if self.has_other else {}),
            {"gathered": vmem_bf16(2, self.rows_out.size * rows, depth)},
            {},
            [self.rows_out],
        )

    def start(self):
        for chunk in range(self.rows_out.chunks):
            self.rows_out.begin(chunk, self.own[rows_at(chunk, self.rows_out.rows)])

    def late(self):
        self.rows_out.complete(self.gathered)
        if self.has_other:
            @pl.when(lax.axis_index("section") == 0)
            def _():
                self.gathered[...] = self.other[...]


class FeedForward(Staged):
    def __init__(self, terms, own, gain, weights, forward, backward, extra):
        rows, depth = own.shape
        half = depth // 2
        units = weights[0].shape[0]
        self.has_forward, self.has_backward, self.units = forward, backward, units
        self.depth = depth
        self.size = size = lax.axis_size("dp")
        self.rows_in = RowScatterer("tensor", rows, half)
        self.spread_in = Gatherer("dp", rows, half)
        self.chunks, self.rows = self.rows_in.chunks, self.rows_in.rows
        chunks, chunk_rows = self.chunks, 2 * size * self.rows
        helpers = [self.rows_in, self.spread_in]
        tensor_rows = lax.axis_size("tensor") * rows
        matrix = pltpu.VMEM((units, depth), BF16)
        ins = {"terms": (terms, VMEM), "own": (own, VMEM), "gain": (gain, VMEM)}
        ins |= {name: (w, HBM) for name, w in zip(("gate_hbm", "up_hbm", "down_hbm"), weights)}
        ins |= {name: (value, VMEM) for name, value in extra.items()}
        outs = {}
        scratch = {"w_gate": matrix, "w_up": matrix, "w_down": matrix, "load": SEM((3,))}
        kept = pltpu.VMEM((size, 2 * self.rows, half), F32)
        if forward:
            outs |= {
                "middle": vmem_f32(rows, depth),
                "mlp_in": vmem_bf16(chunks, chunk_rows, depth),
                "hidden": vmem_bf16(chunks, chunk_rows, units),
                "own_out": vmem_f32(rows, depth),
            }
            self.back = Scatterer("dp", rows, half)
            helpers += [self.back]
            scratch["kept"] = kept
        if forward and not backward:
            outs |= {
                "out": vmem_bf16(2, tensor_rows, depth),
                "gate": vmem_bf16(chunks, chunk_rows, units),
                "up": vmem_bf16(chunks, chunk_rows, units),
            }
            self.out_rows = Gatherer("tensor", rows, half)
            helpers += [self.out_rows]
        if forward and backward:
            outs["grad_mlp"] = vmem_bf16(chunks, chunk_rows, depth)
            self.grad_in = Gatherer("dp", rows, half)
            helpers += [self.grad_in]
            scratch |= {
                "gate": pltpu.VMEM((chunks, chunk_rows, units), F32),
                "up": pltpu.VMEM((chunks, chunk_rows, units), F32),
            }
        if backward:
            outs |= {
                "grad_gate": vmem_bf16(chunks, chunk_rows, units),
                "grad_up": vmem_bf16(chunks, chunk_rows, units),
                "grad_middle": vmem_f32(rows, depth),
                "mlp_gain_grad": vmem_f32(1, depth),
                "grad_attn": vmem_bf16(2, tensor_rows, depth),
            }
            self.grad_back = Scatterer("dp", rows, half)
            self.grad_rows = Gatherer("tensor", rows, half)
            helpers += [self.grad_back, self.grad_rows]
            scratch["grad_kept"] = kept
        if backward and not forward:
            outs |= {
                "gain_grad": vmem_f32(1, depth),
                "grad_own": vmem_f32(rows, depth),
                "grad_mlp": vmem_bf16(chunks, chunk_rows, depth),
            }
        super().__init__(ins, outs, scratch, helpers)

    def loads(self):
        pairs = [(self.gate_hbm, self.w_gate), (self.up_hbm, self.w_up), (self.down_hbm, self.w_down)]
        return [
            pltpu.make_async_copy(src, dst, self.load.at[i]) for i, (src, dst) in enumerate(pairs)
        ]

    def prepare(self):
        for copy in self.loads():
            copy.start()
        self.rows_in.prepare(self.terms)

    def start(self):
        self.rows_in.start()
        if self.has_forward and self.has_backward:
            for chunk in range(self.chunks):
                self.grad_in.begin(chunk, self.grad_own[rows_at(chunk, self.rows)])

    def run(self):
        self.rows_in.send_on()
        if self.has_backward:
            self.mlp_gain_grad[...] = jnp.zeros_like(self.mlp_gain_grad)
        if not self.has_forward:
            self.gain_grad[...] = jnp.zeros_like(self.gain_grad)
        for chunk in range(self.chunks):
            at = rows_at(chunk, self.rows)
            total = self.rows_in.collect(chunk)
            if self.has_forward:
                middle = self.own[at] + total
                self.middle[at] = middle
                mean_sq = jnp.mean(middle * middle, axis=1, keepdims=True)
                normed = middle * lax.rsqrt(mean_sq + EPSILON) * self.gain[...]
                self.spread_in.begin(chunk, normed)
            else:
                result, gain_grad = norm_back(total, self.own[at], self.gain[...])
                self.gain_grad[...] += gain_grad
                result = (result + self.add[at]).astype(BF16).astype(F32)
                self.grad_own[at] = result
                self.spread_in.begin(chunk, result)
        for copy in self.loads():
            copy.wait()

        self.spread_in.arrive(0)
        if self.has_forward and self.has_backward:
            self.grad_in.arrive(0)

        @pl.loop(0, self.chunks)
        def _(chunk):
            self.spread_in.arrive_over(chunk)
            if self.has_forward:
                self.spread_in.unpack_chunk(self.mlp_in, chunk)
                self.forward_chunk(chunk)
            else:
                self.spread_in.unpack_chunk(self.grad_mlp, chunk)
            if self.has_forward and self.has_backward:
                self.grad_in.arrive_over(chunk)
                self.grad_in.unpack_chunk(self.grad_mlp, chunk)
            if self.has_backward:
                self.backward_chunk(chunk)

            @pl.when(chunk + 1 < self.chunks)
            def _():
                self.spread_in.arrive(chunk + 1)
                if self.has_forward and self.has_backward:
                    self.grad_in.arrive(chunk + 1)

            if self.has_forward:
                self.back.absorb(chunk, lambda place, at: self.kept[place, :, pl.ds(at, CHUNK)])
            if self.has_backward:
                self.grad_back.absorb(
                    chunk, lambda place, at: self.grad_kept[place, :, pl.ds(at, CHUNK)]
                )

            @pl.when(chunk > 0)
            def _():
                self.hand_back(chunk - 1)

        self.hand_back(self.chunks - 1)
        if self.has_backward:
            self.grad_rows.complete(self.grad_attn)
        else:
            self.out_rows.complete(self.out)

    def hand_back(self, chunk):
        at = rows_at(chunk, self.rows)
        if self.has_backward:
            values = self.middle if self.has_forward else self.middle_in
            gain = self.gain if self.has_forward else self.mlp_gain
            result, gain_grad = norm_back(self.grad_back.collect(chunk), values[at], gain[...])
            self.mlp_gain_grad[...] += gain_grad
            result += self.grad_own[at]
            self.grad_middle[at] = result
            self.grad_rows.begin(chunk, result)
        if self.has_forward:
            output = (self.middle[at] + self.back.collect(chunk)).astype(BF16).astype(F32)
            self.own_out[at] = output
            if not self.has_backward:
                self.out_rows.begin(chunk, output)

    def unit_tiles(self, body):
        tile = 256

        @pl.loop(0, self.units // tile)
        def _(step):
            body(pl.ds(pl.multiple_of(step * tile, tile), tile))

    def forward_chunk(self, chunk):
        def tile(at):
            rows = self.mlp_in[chunk]
            gate = dot_inner(rows, self.w_gate[at, :])
            up = dot_inner(rows, self.w_up[at, :])
            self.gate[chunk, :, at] = gate.astype(self.gate.dtype)
            self.up[chunk, :, at] = up.astype(self.up.dtype)
            self.hidden[chunk, :, at] = (gate * jax.nn.sigmoid(gate) * up).astype(BF16)

        self.unit_tiles(tile)
        self.terms_out(
            chunk, self.back, self.kept, lambda at: dot(self.hidden[chunk], self.w_down[:, at])
        )

    def backward_chunk(self, chunk):
        def tile(at):
            grad_hidden = dot_inner(self.grad_mlp[chunk], self.w_down[at, :])
            gate, up = self.gate[chunk, :, at].astype(F32), self.up[chunk, :, at].astype(F32)
            share = jax.nn.sigmoid(gate)
            act = gate * share
            self.grad_up[chunk, :, at] = (grad_hidden * act).astype(BF16)
            self.grad_gate[chunk, :, at] = (
                grad_hidden * up * (share + act * (1.0 - share))
            ).astype(BF16)

        self.unit_tiles(tile)
        self.terms_out(
            chunk, self.grad_back, self.grad_kept,
            lambda at: dot(self.grad_gate[chunk], self.w_gate[:, at])
            + dot(self.grad_up[chunk], self.w_up[:, at]),
        )

    def terms_out(self, chunk, scatterer, kept, product):
        rows, half = self.rows, self.depth // 2
        first = lax.axis_index("section") == 0

        @pl.loop(0, half // CHUNK)
        def _(step):
            low = pl.multiple_of(step * CHUNK, CHUNK)
            at = pl.ds(low, CHUNK)
            sides = [product(pl.ds(side * half + low, CHUNK)) for side in range(2)]
            for place in range(self.size):
                trees = []
                for tree in range(2):
                    start = (2 * place + tree) * rows
                    trees.append(
                        jnp.concatenate([side[start : start + rows] for side in sides], axis=0)
                    )
                kept[place, :, at] = jnp.where(first, trees[0], trees[1])
                scatterer.to_sib[chunk, place, :, at] = jnp.where(
                    first, trees[1], trees[0]
                ).astype(BF16)

        for place in range(self.size):
            scatterer.over(chunk, place).start()


def finish_weights(first, second, attn_first, attn_second, arrived, widths, core, rows_out, tile=256):
    units, own_depth = first[0].shape
    q_width, k_width, _, _ = widths
    starts = [0, q_width, q_width + k_width, 0]
    steps = units // tile
    count = len(rows_out)

    def transposed(block):
        size = block.shape[1]
        rows = lax.broadcasted_iota(jnp.int32, (size, size), 0)
        identity = (rows == lax.broadcasted_iota(jnp.int32, rows.shape, 1)).astype(BF16)
        return dot_inner(identity, block)

    def kernel(core_ref, *refs):
        ins, passed_in = refs[:12], refs[12 : 12 + count]
        (gate, up, down), attn_outs = refs[12 + count : 15 + count], refs[15 + count : 19 + count]
        for src, dst in zip(passed_in, refs[19 + count :]):
            dst[...] = src[...]

        on_first = core_ref[0] == 0
        picked = [jnp.where(on_first, ins[i][...], ins[3 + i][...]) for i in range(3)]
        gate[...] = transposed(picked[0])
        up[...] = transposed(picked[1])
        down[...] = picked[2].astype(F32)

        @pl.when(pl.program_id(0) == 0)
        def _():
            for index, (out, start, width) in enumerate(zip(attn_outs, starts, widths)):
                at = pl.ds(start, width)
                mine, other, came = (ins[6 + 2 * i + index // 3][:, at] for i in range(3))
                halves = [jnp.where(on_first, mine, came), jnp.where(on_first, came, other)]
                for half, values in enumerate(halves):
                    if index == 3:
                        out[pl.ds(half * width, width)] = transposed(values)
                    else:
                        out[:, pl.ds(half * width, width)] = values.astype(F32)

    def whole(shape):
        return pl.BlockSpec(shape, lambda step: (0, 0))

    tall = pl.BlockSpec((tile, own_depth), lambda step: (step, 0))
    wide = pl.BlockSpec((own_depth, tile), lambda step: (0, step))
    attn_ins = [*attn_first, *attn_second, *arrived]
    flat_rows = [item.reshape(-1, item.shape[-1]) for item in rows_out]
    passed = [
        pl.BlockSpec((item.shape[0] // steps, item.shape[1]), lambda step: (step, 0))
        for item in flat_rows
    ]
    attn_shapes = [(own_depth, 2 * width) for width in widths[:3]] + [(2 * q_width, own_depth)]
    shapes = [(own_depth, units)] * 2 + [(units, own_depth)] + attn_shapes
    return pl.pallas_call(
        kernel,
        grid=(steps,),
        out_shape=[jax.ShapeDtypeStruct(shape, F32) for shape in shapes]
        + [jax.ShapeDtypeStruct(item.shape, item.dtype) for item in flat_rows],
        in_specs=[pl.BlockSpec(memory_space=pltpu.SMEM)]
        + [tall] * 6
        + [whole(item.shape) for item in attn_ins]
        + passed,
        out_specs=[wide, wide, tall] + [whole(shape) for shape in attn_shapes] + passed,
        cost_estimate=pl.CostEstimate(flops=0, bytes_accessed=25_000_000, transcendentals=0),
        compiler_params=pltpu.CompilerParams(vmem_limit_bytes=60 << 20),
    )(core.reshape(1), *first, *second, *attn_ins, *flat_rows)


def hub_plain(terms, own_args, body, own_outs, scatter, gathers):
    total = None
    if scatter:
        mine = lax.psum_scatter(terms, "section", scatter_dimension=0, tiled=True)
        mine = lax.psum_scatter(mine, scatter, scatter_dimension=1, tiled=True)[0]
        total = mine.astype(F32)

    class Cell:
        def __setitem__(self, _, value):
            self.value = value

    cells = [Cell() for _ in own_outs]
    result = body(total, own_args, cells).astype(BF16)
    gathered = [
        lax.all_gather(lax.all_gather(result, axis, axis=0, tiled=True), "section", axis=0)
        for axis in gathers
    ]
    return [cell.value for cell in cells] + gathered


def with_cargo(part, cargo, axes, collective_id, cost_us, vmem):
    outs = fused(cargo + [part], axes, bool(cargo), collective_id, cost_us, vmem)
    return outs[-1], outs[:-1]


def norm_back(total, values, gain):
    scale = lax.rsqrt(jnp.mean(values * values, axis=1, keepdims=True) + EPSILON)
    unit = values * scale
    gain_grad = jnp.sum(total * unit, axis=0, keepdims=True)
    scaled = total * gain
    along = jnp.mean(scaled * unit, axis=1, keepdims=True)
    return ((scaled - unit * along) * scale, gain_grad)


def norm_body(total, args, outs):
    middle = args[0] + total
    outs[0][...] = middle
    return rms_scale(middle, args[1])


def add_body(total, args, outs):
    result = args[0] + total
    outs[0][...] = result
    return result


def norm_back_body(total, args, outs):
    result, outs[1][...] = norm_back(total, args[0], args[1])
    result += args[2]
    outs[0][...] = result
    return result


def embed(q_pre, k_pre, q_scale, k_scale, cos_table, sine_table):
    queries = rms_scale(q_pre, q_scale)
    keys = rms_scale(k_pre, k_scale)
    return (
        rotate(queries, cos_table[:, :, None], sine_table[:, :, None]),
        rotate(keys, cos_table, sine_table),
    )


def attn_forward(hidden_in, weights, gains, slot, gather):
    attn_scale, _, q_scale, k_scale = gains
    w_qkv, w_out = weights[:2]
    allowed, cos_table, sine_table = slot
    trees, row_count, depth = hidden_in.shape
    q_width = w_out.shape[0]
    normed = rms_scale(hidden_in.astype(F32), attn_scale).astype(BF16).reshape(-1, depth)
    qkv = dot(normed, w_qkv).reshape(trees, row_count, -1)
    q_pre = qkv[:, :, :q_width].reshape(trees, row_count, -1, HD)
    k_pre = qkv[:, :, q_width : q_width + HD]
    value_bf = qkv[:, :, q_width + HD :].astype(BF16)
    queries, keys_rot = embed(q_pre, k_pre, q_scale, k_scale, cos_table, sine_table)
    query_bf = queries.astype(BF16)
    kv_all = gather(jnp.concatenate([keys_rot.astype(BF16), value_bf], axis=2))
    key_all = kv_all[:, :, :HD]
    value_all = kv_all[:, :, HD:]
    scores = masked_scores(query_bf, key_all, allowed)
    row_max = jnp.max(scores, axis=-1, keepdims=True)
    exp_scores = jnp.exp(scores - row_max)
    row_total = jnp.sum(exp_scores, axis=-1, keepdims=True)
    prob_bf = (exp_scores / row_total).astype(BF16)
    log_total = row_max + jnp.log(row_total)
    attended = jnp.einsum("bgrt,btd->brgd", prob_bf, value_all, preferred_element_type=F32)
    attended_bf = attended.reshape(trees * row_count, -1).astype(BF16)
    terms = dot(attended_bf, w_out).astype(BF16).reshape(trees, row_count, depth)
    saved = (normed, q_pre, k_pre, query_bf, key_all, value_all, log_total, attended_bf)
    return (terms, saved)


def attn_backward(grad_attn, saved, weights, gains, slot, scatter):
    _, _, q_scale, k_scale = gains
    w_qkv, w_out = weights[:2]
    allowed, cos_table, sine_table = slot
    normed, q_pre, k_pre, query_bf, key_all, value_all, log_total, attended_bf = saved
    trees, row_count = query_bf.shape[:2]
    depth = normed.shape[1]
    grad_attn = grad_attn.reshape(-1, depth)
    grad_heads = dot_inner(grad_attn, w_out).astype(BF16).reshape(query_bf.shape)
    scores = masked_scores(query_bf, key_all, allowed)
    prob_full = jnp.exp(scores - log_total)
    grad_prob = jnp.einsum("brgd,btd->bgrt", grad_heads, value_all, preferred_element_type=F32)
    row_dot = jnp.sum(prob_full * grad_prob, axis=-1, keepdims=True)
    grad_scores = (prob_full * (grad_prob - row_dot)).astype(BF16)
    scale_factor = HD ** (-0.5)
    grad_query = (
        jnp.einsum("bgrt,btd->brgd", grad_scores, key_all, preferred_element_type=F32)
        * scale_factor
    )
    grad_key_all = (
        jnp.einsum("bgrt,brgd->btd", grad_scores, query_bf, preferred_element_type=F32)
        * scale_factor
    )
    grad_value_all = jnp.einsum(
        "bgrt,brgd->btd", prob_full.astype(BF16), grad_heads, preferred_element_type=F32
    )
    grad_kv = scatter(jnp.concatenate([grad_key_all, grad_value_all], axis=2).astype(BF16))
    _, embedding_pull = jax.vjp(
        partial(embed, cos_table=cos_table, sine_table=sine_table), q_pre, k_pre, q_scale, k_scale
    )
    grad_q_pre, grad_k_pre, grad_q_scale, grad_k_scale = embedding_pull(
        (grad_query, grad_kv[:, :, :HD].astype(F32))
    )
    qkv_grad = jnp.concatenate(
        [
            grad_q_pre.astype(BF16).reshape(trees, row_count, -1),
            grad_k_pre.astype(BF16),
            grad_kv[:, :, HD:].astype(BF16),
        ],
        axis=2,
    ).reshape(trees * row_count, -1)
    terms = dot_inner(qkv_grad, w_qkv).astype(BF16).reshape(trees, row_count, depth)
    return (terms, [(normed, qkv_grad), (grad_attn, attended_bf)], [grad_q_scale, grad_k_scale])


def plain_layers(hidden, own_in, grad_own, weights, gains, slot, shared_kv):
    depth = own_in.shape[1]
    own_shape = own_in.shape

    def gather(own):
        return lax.all_gather(own, "dp", axis=1, tiled=True)

    def scatter(whole):
        total = lax.psum_scatter(whole, "dp", scatter_dimension=1, tiled=True)
        if shared_kv:
            total = lax.psum(total, "section")
            total = jnp.where(lax.axis_index("section") == 0, total, jnp.zeros_like(total))
        return total

    outputs, kept = [], []
    for layer in range(2):
        _, _, w_gate, w_up, w_down = weights[layer]
        terms, saved = attn_forward(hidden, weights[layer], gains[layer], slot, gather)
        mlp_scale = gains[layer][1][None]
        middle, mlp_in = hub_plain(
            terms, [own_in, mlp_scale], norm_body, [own_shape], "tensor", ["dp"]
        )
        mlp_in = mlp_in.reshape(-1, depth)
        gate, up = dot_inner(mlp_in, w_gate), dot_inner(mlp_in, w_up)
        hidden_bf = swiglu(gate, up).astype(BF16)
        terms = dot(hidden_bf, w_down).astype(BF16).reshape(2, -1, depth)
        kept.append((own_in, saved, middle, mlp_in, gate, up, hidden_bf))
        own_in, hidden = hub_plain(terms, [middle], add_body, [own_shape], "dp", ["tensor"])
        own_in = own_in.astype(BF16).astype(F32)
        outputs.append(hidden)

    own_outs = [own_shape, (1, depth)]
    grads, products, gain_grads = [None, None], [None, None], [None, None]
    (grad_mlp,) = hub_plain(None, [grad_own], lambda total, args, outs: args[0], [], None, ["dp"])
    for layer in (1, 0):
        _, _, w_gate, w_up, w_down = weights[layer]
        own_in, saved, middle, mlp_in, gate, up, hidden_bf = kept[layer]
        grad_mlp = grad_mlp.reshape(-1, depth)
        _, pull = jax.vjp(swiglu, gate, up)
        grad_gate, grad_up = (item.astype(BF16) for item in pull(dot_inner(grad_mlp, w_down)))
        terms = (dot(grad_gate, w_gate) + dot(grad_up, w_up)).astype(BF16).reshape(2, -1, depth)
        grad_middle, mlp_gain_grad, grad_attn = hub_plain(
            terms, [middle, gains[layer][1][None], grad_own], norm_back_body, own_outs, "dp",
            ["tensor"],
        )
        terms, pairs, head_grads = attn_backward(
            grad_attn, saved, weights[layer], gains[layer], slot, scatter
        )
        grad_own, gain_grad, grads[layer], grad_next = hub_plain(
            terms, [own_in, gains[layer][0][None], grad_middle], norm_back_body, own_outs, "tensor",
            ["tensor", "dp"],
        )
        grad_own = grad_own.astype(BF16).astype(F32)
        pairs += [(grad_gate, mlp_in), (grad_up, mlp_in), (hidden_bf, grad_mlp)]
        products[layer] = pairs
        gain_grads[layer] = jnp.concatenate([gain_grad[0], mlp_gain_grad[0], *head_grads])
        grad_mlp = grad_next
    return (outputs, grads, products, gain_grads)


def swap_cores(mine, other):
    core = lax.axis_index("section")
    arrived = lax.ppermute(other, "section", [(0, 1), (1, 0)])
    return (jnp.where(core == 0, mine, arrived), jnp.where(core == 0, arrived, mine))


def on_device(
    inputs, cotangent, seg_ids, parents, order, attn_gain, w_query, w_key, w_value, w_out,
    q_gain, k_gain, mlp_gain, w_gate, w_up, w_down,
):
    core = lax.axis_index("section")
    data_index = lax.axis_index("dp")
    tensor_index = lax.axis_index("tensor")
    dp_size = lax.axis_size("dp")
    tensor_size = lax.axis_size("tensor")
    trees, row_count, depth = inputs.shape
    own_rows = row_count // tensor_size
    row_start = data_index * row_count
    own_depth = w_query.shape[1]
    q_width = w_query.shape[2] // 2
    shared_kv = w_key.shape[2] == HD
    k_width = HD if shared_kv else w_key.shape[2] // 2
    own_units = w_gate.shape[2]
    share = own_units // (2 * dp_size)

    def pick(stacked, index):
        return lax.dynamic_index_in_dim(stacked, index, 0, keepdims=False)

    fast = (
        own_rows % 8 == 0
        and depth % (2 * CHUNK) == 0
        and row_count % 16 == 0
        and share % 16 == 0
        and own_depth % 128 == 0
        and not shared_kv
    )

    def halves(width, array):
        return [array[:, :width], array[:, array.shape[1] - width :]]

    unit_mats = [w_gate[0].T, w_up[0].T, w_down[0]]
    qkv_width = q_width + 2 * k_width
    gains_own = jnp.concatenate([attn_gain[0], mlp_gain[0], q_gain[0], k_gain[0]]).astype(F32)

    def spread_units(rows):
        return lax.all_gather(rows, "tensor", axis=0, tiled=True)

    def tied(value, *before):
        return lax.optimization_barrier((value, *before))[0]

    if fast:
        line = ["section", "dp"]
        everyone = ["section", "dp", "tensor"]
        (gate_rows, up_rows), (gains_all,) = fused(
            [UnitsOut(unit_mats[:2], 0), SharedRows(gains_own.reshape(-1, 128))], line, True, 1, 45, 60
        )
        shards = AttnShards(w_query[0], w_key[0], w_value[0], w_out[0])
        shards.arrays[0] = tied(shards.arrays[0], gate_rows)
        (w_qkv, w_heads), (down_rows,), (attn_shard,) = fused(
            [AttnOut(shards, 0), UnitsOut(unit_mats[2:], 0), HalfOver(shards)], line, True, 2, 80, 60
        )
        first_weights = [w_qkv, w_heads, spread_units(gate_rows), spread_units(up_rows)]
    else:
        gains_all = lax.all_gather(gains_own, ("section", "dp"))
        attn_halves = jnp.stack(
            [
                jnp.concatenate(parts, axis=1)
                for parts in zip(
                    halves(q_width, w_query[0]),
                    halves(k_width, w_key[0]),
                    halves(k_width, w_value[0]),
                    halves(q_width, w_out[0].T),
                )
            ]
        )
        attn_shards = swap_cores(pick(attn_halves, core), pick(attn_halves, 1 - core))
        unit_blocks = jnp.stack(unit_mats).reshape(3, 2, dp_size, share, own_depth)
        unit_blocks = unit_blocks.transpose(1, 2, 0, 3, 4)
        unit_shards = swap_cores(pick(unit_blocks, core), pick(unit_blocks, 1 - core))
        both_weights = []
        for layer in range(2):
            attn_all = lax.all_gather(attn_shards[layer], "dp", axis=0, tiled=True)
            pieces = exchange(unit_shards[layer], "dp")
            pieces = pieces.transpose(1, 2, 0, 3).reshape(3, share, depth)
            both_weights.append(
                (
                    attn_all[:, :qkv_width], attn_all[:, qkv_width:].T,
                    *(spread_units(pieces[i]) for i in range(3)),
                )
            )

    gains_all = gains_all.reshape(2, dp_size, -1)
    gains = [
        (
            gains_all[layer, :, :own_depth].reshape(depth),
            gains_all[layer, :, own_depth : 2 * own_depth].reshape(depth),
            gains_all[layer, 0, 2 * own_depth : 2 * own_depth + HD],
            gains_all[layer, 0, 2 * own_depth + HD :],
        )
        for layer in range(2)
    ]

    def slot_setup(slot_index):
        tree_id = pick(order, slot_index)
        allowed, row_positions = path_mask(
            pick(seg_ids, tree_id), pick(parents, tree_id), row_start, row_count
        )
        cos_table, sine_table = rope_tables(row_positions, HD)
        return (pick(inputs, tree_id), allowed, cos_table[:, 0], sine_table[:, 0])

    setups = [slot_setup(i) for i in range(trees)]
    hidden, *slot = (jnp.stack(item) for item in zip(*setups))

    def own_part(whole):
        return lax.dynamic_slice_in_dim(
            pick(whole, core), tensor_index * own_rows, own_rows, 0
        )

    own_in = own_part(hidden).astype(F32)
    grad_own = own_part(cotangent).astype(F32)

    def weight_products(pairs):
        return [dot_outer(left, right).astype(BF16) for left, right in pairs]

    def scatter_units(products):
        return [
            lax.psum_scatter(item, "tensor", scatter_dimension=0, tiled=True) for item in products
        ]

    def scatter_shards(products):
        return lax.psum_scatter(
            jnp.concatenate(products, axis=1), "dp", scatter_dimension=0, tiled=True
        )

    if fast:
        def units_on(*which):
            return [UnitsOut([unit_mats[i] for i in which], 1)]

        def kv_gather(own, cargo, collective_id, carried):
            (whole,), outs = with_cargo(GatherKV(own), cargo, everyone, collective_id, 40, 40)
            carried += outs
            return whole.reshape(trees, -1, 2 * HD)

        def kv_scatter(whole, cargo, collective_id, carried):
            part = ScatterKV(whole.reshape(trees, dp_size, row_count, 2 * HD))
            (total,), outs = with_cargo(part, cargo, everyone, collective_id, 30, 40)
            carried += outs
            return total

        def in_order(pairs):
            done = []
            for left, right in pairs:
                done += weight_products([(tied(left, *done[-1:]), right)])
            return done

        def flat(array):
            return array.reshape(-1, array.shape[-1])

        carried = []
        terms, saved_first = attn_forward(
            hidden, first_weights, gains[0], slot,
            lambda own: kv_gather(
                tied(own, *first_weights[2:]), [UnitsSpread(down_rows)] + units_on(0, 1, 2), 3, carried
            ),
        )
        (down_all,), (gate_rows, up_rows, down_rows) = carried
        first_weights.append(down_all)
        part = FeedForward(
            terms, own_in, gains[0][1][None], first_weights[2:], True, False, {}
        )
        outs, ((down_next,),) = with_cargo(part, [UnitsSpread(down_rows)], everyone, 4, 90, 60)
        middle_first, mlp_in_first, hidden_first, own_next, output_first, gate_first, up_first = outs
        attn_next = lax.all_gather(tied(attn_shard, gate_rows), "dp", axis=0)
        second_weights = [
            attn_next[:, :own_depth].reshape(depth, -1),
            attn_next[:, own_depth:].transpose(1, 0, 2).reshape(q_width, depth),
            spread_units(gate_rows), spread_units(up_rows),
        ]
        carried = []
        terms, saved_second = attn_forward(
            output_first, second_weights, gains[1], slot,
            lambda own: kv_gather(tied(own, second_weights[2]), [], 5, carried),
        )
        second_weights.append(down_next)
        part = FeedForward(
            terms, own_next, gains[1][1][None], second_weights[2:], True, True,
            {"grad_own": grad_own},
        )
        outs, _ = with_cargo(part, [], everyone, 6, 100, 60)
        (
            middle, mlp_in, hidden_bf, own_second, grad_mlp,
            grad_gate, grad_up, grad_middle, mlp_gain_second, grad_attn,
        ) = outs
        products = in_order([(flat(grad_gate), flat(mlp_in)), (flat(grad_up), flat(mlp_in))])
        unit_second = scatter_units(products)
        carried = []
        terms, pairs, head_second = attn_backward(
            grad_attn, saved_second, second_weights, gains[1], slot,
            lambda whole: kv_scatter(
                tied(whole, *products), [RowsOut(own_second, output_first)], 7, carried
            ),
        )
        ((layer_out,),) = carried
        unit_second += scatter_units(
            weight_products([(tied(flat(hidden_bf), layer_out), flat(grad_mlp))])
        )
        pairs = weight_products(pairs)
        attn_second = scatter_shards([tied(pairs[0], unit_second[1]), pairs[1]])
        terms = tied(terms, unit_second[0])
        part = FeedForward(
            terms, own_next, gains[1][0][None], first_weights[2:], False, True,
            {
                "add": grad_middle, "gate": gate_first, "up": up_first,
                "middle_in": middle_first, "mlp_gain": gains[0][1][None],
            },
        )
        outs, (home_second,) = with_cargo(
            part, [UnitsHome(unit_second[:1], 1)], everyone, 8, 90, 60
        )
        (
            grad_gate, grad_up, grad_middle, mlp_gain_first, grad_attn,
            attn_gain_second, own_incoming, grad_mlp,
        ) = outs
        products = in_order(
            [(flat(grad_gate), flat(mlp_in_first)), (flat(grad_up), flat(mlp_in_first))]
        )
        grad_attn = tied(grad_attn, *unit_second[1:], *products)
        unit_first = scatter_units([products[0], tied(products[1], attn_second)])
        carried = []
        terms, pairs, head_first = attn_backward(
            grad_attn, saved_first, first_weights, gains[0], slot,
            lambda whole: kv_scatter(
                whole, [UnitsHome(unit_second[1:], 1), RowsOut(own_incoming)], 9, carried
            ),
        )
        home_second += carried[0]
        (incoming_second,) = carried[1]
        unit_first += scatter_units(
            weight_products([(tied(flat(hidden_first), incoming_second), flat(grad_mlp))])
        )
        parts = [
            ScatterKV(item.reshape(dp_size, 4, own_depth // 4, -1), True, BF16, True)
            for item in weight_products(pairs)
        ]
        part = LastHub(terms, own_in, gains[0][0][None], grad_middle, incoming_second)
        (attn_gain_first, input_grad), (*attn_first, home_first) = with_cargo(
            part, parts + [UnitsHome(unit_first[:1], 0)], everyone, 10, 60, 60
        )
        attn_first = [item.reshape(own_depth, -1) for (item,) in attn_first]
        attn_second = [attn_second[:, :qkv_width], attn_second[:, qkv_width:]]
        gain_grads = [
            jnp.concatenate([attn_gain_first[0], mlp_gain_first[0], *head_first]),
            jnp.concatenate([attn_gain_second[0], mlp_gain_second[0], *head_second]),
        ]
    else:
        outputs, grads, products, gain_grads = plain_layers(
            hidden, own_in, grad_own, both_weights, gains, slot, shared_kv
        )
        layer_out = jnp.where(core == 0, *outputs)
        input_grad = jnp.where(core == 0, *grads)
        weight_grads = []
        for pairs in products:
            whole = weight_products(pairs)
            weight_grads.append((scatter_shards(whole[:2]), scatter_units(whole[2:])))

    gain_total = jnp.stack(gain_grads)
    if fast:
        others = [
            Swap(jnp.where(core == 0, second, first))
            for first, second in zip(attn_first, attn_second)
        ]
        (gain_total,), *arrived, down_home = fused(
            [TotalOverAll(gain_total.reshape(-1, 128)), *others, UnitsHome(unit_first[1:], 0)],
            everyone, True, 11, 60, 60,
        )
        grad_gate, grad_up, grad_down, *attn_grads, layer_out, input_grad = finish_weights(
            home_first + down_home, home_second, attn_first, attn_second,
            [item for (item,) in arrived], (q_width, k_width, k_width, q_width), core,
            (layer_out, input_grad),
        )
        layer_out = layer_out.reshape(trees, row_count, depth)
        input_grad = input_grad.reshape(trees, row_count, depth)
        gain_total = gain_total.reshape(2, -1)
    else:
        def bring_home(first, second):
            mine, other = jnp.where(core == 0, first, second), jnp.where(core == 0, second, first)
            arrived = lax.ppermute(other, "section", [(0, 1), (1, 0)])
            return (jnp.where(core == 0, mine, arrived), jnp.where(core == 0, arrived, mine))

        def pieces_of(grad):
            return exchange(
                jnp.stack(grad).reshape(3, share, dp_size, own_depth).transpose(2, 0, 1, 3), "dp"
            )

        attn_home = bring_home(weight_grads[0][0], weight_grads[1][0])
        unit_home = jnp.stack(bring_home(pieces_of(weight_grads[0][1]), pieces_of(weight_grads[1][1])))
        unit_home = unit_home.transpose(2, 0, 1, 3, 4).reshape(3, own_units, own_depth).astype(F32)
        grad_gate, grad_up, grad_down = unit_home[0].T, unit_home[1].T, unit_home[2]
        gain_total = lax.psum(gain_total, ("section", "dp", "tensor"))

        def joined(start, width):
            parts = [half[:, start : start + width] for half in attn_home]
            if shared_kv and start in (q_width, q_width + k_width):
                return parts[0].astype(F32)
            return jnp.concatenate(parts, axis=1).astype(F32)

        attn_grads = [
            joined(0, q_width), joined(q_width, k_width), joined(q_width + k_width, k_width),
            joined(qkv_width, q_width).T,
        ]

    gain_own = pick(gain_total, core)
    share_width = attn_gain.shape[1]
    attn_gain_grad = lax.dynamic_slice_in_dim(gain_own, data_index * share_width, share_width, 0)
    mlp_gain_grad = lax.dynamic_slice_in_dim(
        gain_own, depth + data_index * share_width, share_width, 0
    )
    return (
        layer_out[None],
        input_grad[None],
        attn_gain_grad[None],
        *(item[None] for item in attn_grads),
        gain_own[2 * depth : 2 * depth + HD][None],
        gain_own[2 * depth + HD :][None],
        mlp_gain_grad[None],
        grad_gate[None],
        grad_up[None],
        grad_down[None],
    )


def solution(mesh):
    rows = P(None, "dp", None)
    wide = P("section", "dp", "tensor")
    tall = P("section", "tensor", "dp")
    gain = P("section", "dp")
    head_gain = P("section", None)
    slots = P("section", None, "dp", None)
    in_specs = (
        rows, rows, P(), P(), P(), gain, wide, wide, wide, tall, head_gain, head_gain, gain,
        wide, wide, tall,
    )
    out_specs = (
        slots, slots, gain, wide, wide, wide, tall, head_gain, head_gain, gain, wide, wide, tall,
    )
    return jax.shard_map(
        on_device, mesh=mesh, in_specs=in_specs, out_specs=out_specs, check_vma=False
    )
```

```python
from functools import partial

import jax
import jax.numpy as jnp
from jax import lax
from jax.experimental import pallas as pl
from jax.experimental.pallas import tpu as pltpu
from jax.sharding import PartitionSpec as P

HD = 128
TRUNK = 512
BRANCH = 96
NB = 4
TREE = 1152
SEGS = 9


EPSILON = 1e-06
THETA = 1000000.0
MASKED = -1e30
F32 = jnp.float32
BF16 = jnp.bfloat16


def rms_scale(values, weight_gain):
    mean_sq = jnp.mean(values * values, axis=-1, keepdims=True)
    return values * lax.rsqrt(mean_sq + EPSILON) * weight_gain


def rotate(values, cos_table, sine_table):
    middle_at = values.shape[-1] // 2
    leading = values[..., :middle_at]
    trailing = values[..., middle_at:]
    return jnp.concatenate(
        [leading * cos_table - trailing * sine_table, trailing * cos_table + leading * sine_table],
        axis=-1,
    )


def rope_tables(positions, head_dim):
    half_steps = jnp.arange(head_dim // 2, dtype=F32)
    inverse = THETA ** (-2.0 * half_steps / head_dim)
    angles = positions.astype(F32)[:, None] * inverse[None, :]
    return (jnp.cos(angles)[:, None, :], jnp.sin(angles)[:, None, :])


def swiglu(gate_in, up_in):
    return jax.nn.silu(gate_in) * up_in


def embed_heads(q_pre, k_pre, q_scale, k_scale, cos_table, sine_table):
    row_count = q_pre.shape[0]
    queries = rms_scale(q_pre.reshape(row_count, -1, HD), q_scale)
    keys_part = rms_scale(k_pre.reshape(row_count, -1, HD), k_scale)
    return (rotate(queries, cos_table, sine_table), rotate(keys_part, cos_table, sine_table))


def tree_layout(seg_row, parent_row):
    labels = jnp.arange(SEGS, dtype=jnp.int32)
    places = jnp.arange(TREE, dtype=jnp.int32)
    member = seg_row[None, :] == labels[:, None]
    starts = jnp.min(jnp.where(member, places[None, :], TREE), axis=1)
    depth_base = jnp.where(labels == 0, 0, jnp.where(labels <= NB, TRUNK, TRUNK + BRANCH))
    shifts = depth_base - starts
    positions = places + jnp.sum(jnp.where(member, shifts[:, None], 0), axis=0)
    grandparent = jnp.sum(
        jnp.where(parent_row[:, None] == labels[None, :], parent_row[None, :], 0), axis=1
    )
    ancestor = (
        (labels[None, :] == labels[:, None])
        | (labels[None, :] == parent_row[:, None])
        | (labels[None, :] == grandparent[:, None])
    )
    return (positions, member.astype(F32), ancestor.astype(F32))


def path_mask(seg_row, parent_row, row_start, row_count):
    positions, member, ancestor = tree_layout(seg_row, parent_row)
    member_rows = lax.dynamic_slice_in_dim(member, row_start, row_count, 1)
    seg_rows = lax.dynamic_slice_in_dim(seg_row, row_start, row_count, 0)
    reach_table = jnp.dot(jnp.dot(member_rows.T, ancestor), member)
    places = jnp.arange(TREE, dtype=jnp.int32)
    row_places = row_start + jnp.arange(row_count, dtype=jnp.int32)
    same_seg = seg_rows[:, None] == seg_row[None, :]
    causal = places[None, :] <= row_places[:, None]
    allowed = (reach_table > 0.5) & (jnp.logical_not(same_seg) | causal)
    row_positions = lax.dynamic_slice_in_dim(positions, row_start, row_count, 0)
    return (allowed, row_positions)


OUTER = (((0,), (0,)), ((), ()))
INNER = (((1,), (1,)), ((), ()))


def dot(left, right):
    return jnp.dot(left, right, preferred_element_type=F32)


def dot_inner(left, right):
    return lax.dot_general(left, right, INNER, preferred_element_type=F32)


def dot_outer(left, right):
    return lax.dot_general(left, right, OUTER, preferred_element_type=F32)


def exchange(pieces, axis):
    size = lax.axis_size(axis)
    me = lax.axis_index(axis)
    got = jnp.zeros_like(pieces)
    own = lax.dynamic_index_in_dim(pieces, me, 0, keepdims=True)
    got = lax.dynamic_update_slice_in_dim(got, own, me, 0)
    for step in range(1, size):
        other = me ^ step
        piece = lax.dynamic_index_in_dim(pieces, other, 0, keepdims=True)
        arrived = lax.ppermute(piece, axis, [(i, i ^ step) for i in range(size)])
        got = lax.dynamic_update_slice_in_dim(got, arrived, other, 0)
    return got


def masked_scores(query_bf, key_all, allowed):
    raw_scores = jnp.einsum(
        "brgd,btd->bgrt", query_bf, key_all, preferred_element_type=F32
    ) * HD ** (-0.5)
    return jnp.where(allowed[:, None], raw_scores, MASKED)


MESH = pl.DeviceIdType.MESH
CHUNK = 512
SEM = pltpu.SemaphoreType.DMA
VMEM = pl.BlockSpec(memory_space=pltpu.VMEM)
HBM = pl.BlockSpec(memory_space=pl.ANY)


def remote(src, dst, send_sem, recv_sem, device_id):
    return pltpu.make_async_remote_copy(
        src_ref=src, dst_ref=dst, send_sem=send_sem, recv_sem=recv_sem,
        device_id=device_id, device_id_type=MESH,
    )


def greet(axes, across):
    barrier = pltpu.get_barrier_semaphore()
    count = 0
    for axis in axes:
        size = lax.axis_size(axis)
        me = lax.axis_index(axis)
        for step in range(1, size):
            pl.semaphore_signal(
                barrier, inc=1, device_id={axis: lax.rem(me + step, size)}, device_id_type=MESH
            )
        count += size - 1
    if across:
        size = lax.axis_size("dp")
        me = lax.axis_index("dp")
        sibling = 1 - lax.axis_index("section")
        for step in range(1, size):
            pl.semaphore_signal(
                barrier, inc=1, device_id={"section": sibling, "dp": lax.rem(me + step, size)},
                device_id_type=MESH,
            )
        count += size - 1
    pl.semaphore_wait(barrier, count)


class Part:
    ins, outs, scratch = (), (), ()

    def bind(self, ins, outs, scratch):
        self.in_refs, self.out_refs, self.refs = ins, outs, scratch

    def prepare(self):
        pass

    def start(self):
        pass

    def run(self):
        pass

    def pass_on(self):
        pass

    def late(self):
        pass

    def finish(self):
        pass


def fused(parts, axes, across, collective_id, cost_us, vmem):
    counts = [(len(part.ins), len(part.outs), len(part.scratch)) for part in parts]

    def kernel(*refs):
        refs = list(refs)
        groups = []
        for kind in range(3):
            groups.append([])
            for count in counts:
                groups[kind].append(refs[: count[kind]])
                del refs[: count[kind]]
        for part, ins, outs, scratch in zip(parts, *groups):
            part.bind(ins, outs, scratch)
        for part in parts:
            part.prepare()
        greet(axes, across)
        for part in parts:
            part.start()
        for part in reversed(parts):
            part.run()
        for part in reversed(parts):
            part.pass_on()
        for part in reversed(parts):
            part.late()
        for part in parts:
            part.finish()

    ins = [item for part in parts for item in part.ins]
    outs = [item for part in parts for item in part.outs]
    results = pl.pallas_call(
        kernel,
        out_shape=[item[0] for item in outs],
        in_specs=[item[1] for item in ins],
        out_specs=[item[1] for item in outs],
        scratch_shapes=[item for part in parts for item in part.scratch],
        cost_estimate=pl.CostEstimate(
            flops=0, bytes_accessed=cost_us * 3_000_000, transcendentals=0
        ),
        compiler_params=pltpu.CompilerParams(
            collective_id=collective_id, has_side_effects=True, vmem_limit_bytes=vmem << 20
        ),
    )(*[item[0] for item in ins])
    results = list(results)
    split = []
    for count in counts:
        split.append(results[: count[1]])
        del results[: count[1]]
    return split


def columns_of(place, width):
    return pl.ds(pl.multiple_of(place * width, width), width)


class UnitsOut(Part):
    def __init__(self, mats, layer):
        self.layer, self.count = layer, len(mats)
        self.size = lax.axis_size("dp")
        rows, self.width = mats[0].shape
        self.share = rows // (2 * self.size)
        self.ins = [(mat, HBM) for mat in mats]
        shape = jax.ShapeDtypeStruct((self.share, self.size * self.width), BF16)
        self.outs = [(shape, HBM)] * self.count
        self.scratch = [SEM((self.count,)), SEM((self.count, 2, self.size)), SEM((self.count, self.size))]

    def bind(self, ins, outs, scratch):
        self.src, self.dst = ins, outs
        self.keep, self.send, self.recv = scratch
        self.core, self.me = lax.axis_index("section"), lax.axis_index("dp")

    def piece(self, index, core, place):
        start = pl.multiple_of((core * self.size + place) * self.share, self.share)
        return self.src[index].at[pl.ds(start, self.share)]

    def lands(self, index, slot):
        return self.dst[index].at[:, columns_of(slot, self.width)]

    def copy(self, index, core, place, slot):
        return remote(
            self.piece(index, core, place), self.lands(index, slot),
            self.send.at[index, core, place], self.recv.at[index, slot],
            {"section": core, "dp": place},
        )

    def local(self, index):
        return pltpu.make_async_copy(
            self.piece(index, self.layer, self.me), self.lands(index, self.me), self.keep.at[index]
        )

    def targets(self):
        for index in range(self.count):
            for core in range(2):
                for place in range(self.size):
                    yield index, core, place, (place != self.me) | (core != self.layer)

    def start(self):
        @pl.when(self.core == self.layer)
        def _():
            for index, core, place, is_other in self.targets():
                @pl.when(is_other)
                def _():
                    self.copy(index, core, place, self.me).start()

            for index in range(self.count):
                self.local(index).start()

    def finish(self):
        for index in range(self.count):
            for place in range(self.size):
                @pl.when((self.core != self.layer) | (place != self.me))
                def _():
                    self.copy(index, 0, 0, place).wait_recv()

        @pl.when(self.core == self.layer)
        def _():
            for index, core, place, is_other in self.targets():
                @pl.when(is_other)
                def _():
                    self.copy(index, core, place, self.me).wait_send()

            for index in range(self.count):
                self.local(index).wait()


class UnitsHome(Part):
    def __init__(self, mats, layer):
        self.layer, self.count = layer, len(mats)
        self.size = lax.axis_size("dp")
        self.share, depth = mats[0].shape
        self.width = depth // self.size
        self.ins = [(mat, HBM) for mat in mats]
        shape = jax.ShapeDtypeStruct((2 * self.size * self.share, self.width), BF16)
        self.outs = [(shape, HBM)] * self.count
        self.scratch = [SEM((self.count,)), SEM((self.count, self.size)), SEM((self.count, 2, self.size))]

    def bind(self, ins, outs, scratch):
        self.src, self.dst = ins, outs
        self.keep, self.send, self.recv = scratch
        self.core, self.me = lax.axis_index("section"), lax.axis_index("dp")

    def lands(self, index, core, slot):
        start = pl.multiple_of((core * self.size + slot) * self.share, self.share)
        return self.dst[index].at[pl.ds(start, self.share)]

    def copy(self, index, place, core, slot):
        return remote(
            self.src[index].at[:, columns_of(place, self.width)], self.lands(index, core, slot),
            self.send.at[index, place], self.recv.at[index, core, slot],
            {"section": self.layer, "dp": place},
        )

    def local(self, index):
        return pltpu.make_async_copy(
            self.src[index].at[:, columns_of(self.me, self.width)],
            self.lands(index, self.layer, self.me), self.keep.at[index],
        )

    def start(self):
        for index in range(self.count):
            for place in range(self.size):
                @pl.when((self.core != self.layer) | (place != self.me))
                def _():
                    self.copy(index, place, self.core, self.me).start()

            @pl.when(self.core == self.layer)
            def _():
                self.local(index).start()

    def finish(self):
        for index in range(self.count):
            @pl.when(self.core == self.layer)
            def _():
                for core in range(2):
                    for place in range(self.size):
                        @pl.when((core != self.layer) | (place != self.me))
                        def _():
                            self.copy(index, 0, core, place).wait_recv()

                self.local(index).wait()

            for place in range(self.size):
                @pl.when((self.core != self.layer) | (place != self.me))
                def _():
                    self.copy(index, place, self.core, self.me).wait_send()


class UnitsSpread(Part):
    def __init__(self, rows):
        self.size = lax.axis_size("tensor")
        self.share, depth = rows.shape
        self.ins = [(rows, HBM)]
        self.outs = [(jax.ShapeDtypeStruct((self.size * self.share, depth), BF16), HBM)]
        self.scratch = [SEM, SEM((self.size,)), SEM((self.size,))]

    def bind(self, ins, outs, scratch):
        (self.src,), (self.dst,), (self.keep, self.send, self.recv) = ins, outs, scratch
        self.me = lax.axis_index("tensor")

    def lands(self, slot):
        return self.dst.at[pl.ds(pl.multiple_of(slot * self.share, self.share), self.share)]

    def copy(self, place, slot):
        return remote(
            self.src, self.lands(slot), self.send.at[place], self.recv.at[slot], {"tensor": place}
        )

    def start(self):
        for place in range(self.size):
            @pl.when(place != self.me)
            def _():
                self.copy(place, self.me).start()

        pltpu.make_async_copy(self.src, self.lands(self.me), self.keep).start()

    def finish(self):
        for place in range(self.size):
            @pl.when(place != self.me)
            def _():
                self.copy(place, place).wait_recv()
                self.copy(place, self.me).wait_send()

        pltpu.make_async_copy(self.src, self.lands(self.me), self.keep).wait()


class SharedRows(Part):
    def __init__(self, own):
        self.size = lax.axis_size("dp")
        self.ins = [(own, VMEM)]
        self.outs = [(jax.ShapeDtypeStruct((2, self.size) + own.shape, F32), VMEM)]
        self.scratch = [SEM((2, self.size)), SEM((2, self.size))]

    def copy(self, core, place, from_core, from_place):
        return remote(
            self.in_refs[0], self.out_refs[0].at[from_core, from_place],
            self.refs[0].at[core, place], self.refs[1].at[from_core, from_place],
            {"section": core, "dp": place},
        )

    def others(self):
        core, me = lax.axis_index("section"), lax.axis_index("dp")
        for other in range(2):
            for place in range(self.size):
                yield other, place, (other != core) | (place != me)

    def start(self):
        core, me = lax.axis_index("section"), lax.axis_index("dp")
        for other, place, is_other in self.others():
            @pl.when(is_other)
            def _():
                self.copy(other, place, core, me).start()

        self.out_refs[0][core, me] = self.in_refs[0][...]

    def finish(self):
        core, me = lax.axis_index("section"), lax.axis_index("dp")
        for other, place, is_other in self.others():
            @pl.when(is_other)
            def _():
                self.copy(other, place, other, place).wait_recv()
                self.copy(other, place, core, me).wait_send()


def passed_on(place, me):
    return ((place == 3) & (me <= 1)) | ((place == 0) & (me >= 2))


def line_relays(size):
    return [(2, 1, 3, 0), (2, 0, 3, 1), (1, 2, 0, 0), (1, 3, 0, 1)] if size == 4 else []


def line_order(size):
    return [1, 2, 0, 3] if size == 4 else list(range(size))


class AttnShards:
    def __init__(self, w_query, w_key, w_value, w_out):
        self.arrays = [w_query, w_key, w_value, w_out]
        self.depth = w_query.shape[0]
        self.q_width, self.k_width = w_query.shape[1] // 2, w_key.shape[1] // 2
        self.width = self.q_width + 2 * self.k_width
        half = self.depth // 2
        parts = self.q_width // 2
        self.items = [
            (0, lambda ref, core: ref.at[pl.ds(0, half), columns_of(core, self.q_width)]),
            (0, lambda ref, core: ref.at[pl.ds(half, half), columns_of(core, self.q_width)]),
            (1, lambda ref, core: ref.at[:, columns_of(core, self.k_width)]),
            (2, lambda ref, core: ref.at[:, columns_of(core, self.k_width)]),
            (3, lambda ref, core: ref.at[pl.ds(core * self.q_width, parts)]),
            (3, lambda ref, core: ref.at[pl.ds(core * self.q_width + parts, parts)]),
        ]
        q_width, k_width, depth = self.q_width, self.k_width, self.depth
        self.qkv_rows = [(0, half), (half, half), (0, depth), (0, depth)]
        self.qkv_columns = [
            (0, q_width), (0, q_width), (q_width, k_width), (q_width + k_width, k_width)
        ]
        self.out_rows = [(0, parts), (parts, parts)]

    def source(self, refs, index, core):
        array, cut = self.items[index]
        return cut(refs[array], core)

    def lands(self, qkv, out, index, slot):
        if index < 4:
            (start, rows), (left, columns) = self.qkv_rows[index], self.qkv_columns[index]
            at = pl.multiple_of(slot * self.depth + start, rows)
            return qkv.at[pl.ds(at, rows), pl.ds(left, columns)]
        start, rows = self.out_rows[index - 4]
        return out.at[pl.ds(start, rows), columns_of(slot, self.depth)]


class AttnOut(Part):
    def __init__(self, shards, layer):
        self.layer, self.shards = layer, shards
        self.size = lax.axis_size("dp")
        self.count = len(shards.items)
        depth = self.size * shards.depth
        self.ins = [(array, HBM) for array in shards.arrays]
        self.outs = [
            (jax.ShapeDtypeStruct((depth, shards.width), BF16), HBM),
            (jax.ShapeDtypeStruct((shards.q_width, depth), BF16), HBM),
        ]
        self.scratch = [
            SEM((self.count,)), SEM((2, self.size, self.count)), SEM((self.size, self.count)),
            SEM((self.count, 2)),
        ]

    def bind(self, ins, outs, scratch):
        self.src = ins
        self.qkv, self.out = outs
        self.keep, self.send, self.recv, self.relay_send = scratch
        self.core, self.me = lax.axis_index("section"), lax.axis_index("dp")

    def lands(self, index, slot):
        return self.shards.lands(self.qkv, self.out, index, slot)

    def copy(self, core, place, slot, index):
        return remote(
            self.shards.source(self.src, index, core), self.lands(index, slot),
            self.send.at[core, place, index], self.recv.at[slot, index],
            {"section": core, "dp": place},
        )

    def relay(self, source, target, turn, index):
        block = self.lands(index, source)
        return remote(
            block, block, self.relay_send.at[index, turn], self.recv.at[source, index],
            {"dp": target},
        )

    def local(self, index):
        return pltpu.make_async_copy(
            self.shards.source(self.src, index, self.layer), self.lands(index, self.me),
            self.keep.at[index],
        )

    def targets(self):
        for index in range(self.count):
            for core in range(2):
                for place in range(self.size):
                    sent = (place != self.me) | (core != self.layer)
                    if self.size == 4:
                        sent = sent & jnp.logical_not(passed_on(place, self.me))
                    yield core, place, index, sent

    def start(self):
        @pl.when(self.core == self.layer)
        def _():
            for core, place, index, sent in self.targets():
                @pl.when(sent)
                def _():
                    self.copy(core, place, self.me, index).start()

            for index in range(self.count):
                self.local(index).start()

    def run(self):
        for index in range(self.count):
            for place in line_order(self.size):
                @pl.when((self.core != self.layer) | (place != self.me))
                def _():
                    self.copy(0, 0, place, index).wait_recv()

                for via, source, target, turn in line_relays(self.size):
                    if source == place:
                        @pl.when(self.me == via)
                        def _():
                            self.relay(source, target, turn, index).start()

    def finish(self):
        @pl.when(self.core == self.layer)
        def _():
            for core, place, index, sent in self.targets():
                @pl.when(sent)
                def _():
                    self.copy(core, place, self.me, index).wait_send()

            for index in range(self.count):
                self.local(index).wait()

        for via, source, target, turn in line_relays(self.size):
            @pl.when(self.me == via)
            def _():
                for index in range(self.count):
                    self.relay(source, target, turn, index).wait_send()


class HalfOver(Part):
    def __init__(self, shards):
        self.shards = shards
        self.count = len(shards.items)
        rows = shards.depth + shards.q_width
        self.ins = [(array, HBM) for array in shards.arrays]
        self.outs = [(jax.ShapeDtypeStruct((rows, shards.depth), BF16), HBM)]
        self.scratch = [SEM((self.count,)), SEM((self.count,)), SEM((self.count,))]

    def lands(self, index):
        depth, q_width = self.shards.depth, self.shards.q_width
        packed = self.out_refs[0]
        return self.shards.lands(
            packed.at[pl.ds(0, depth)], packed.at[pl.ds(depth, q_width)], index, 0
        )

    def over(self, index):
        return remote(
            self.shards.source(self.in_refs, index, 0), self.lands(index), self.refs[0].at[index],
            self.refs[1].at[index], {"section": 0},
        )

    def keep(self, index):
        return pltpu.make_async_copy(
            self.shards.source(self.in_refs, index, 1), self.lands(index), self.refs[2].at[index]
        )

    def start(self):
        @pl.when(lax.axis_index("section") == 1)
        def _():
            for index in range(self.count):
                self.over(index).start()
                self.keep(index).start()

    def finish(self):
        @pl.when(lax.axis_index("section") == 1)
        def _():
            for index in range(self.count):
                self.over(index).wait_send()
                self.keep(index).wait()

        @pl.when(lax.axis_index("section") == 0)
        def _():
            for index in range(self.count):
                self.over(index).wait_recv()


class Swap(Part):
    def __init__(self, own):
        self.ins = [(own, HBM)]
        self.outs = [(jax.ShapeDtypeStruct(own.shape, own.dtype), HBM)]
        self.scratch = [SEM, SEM]

    def start(self):
        sibling = 1 - lax.axis_index("section")
        self.copy = remote(
            self.in_refs[0], self.out_refs[0], self.refs[0], self.refs[1], {"section": sibling}
        )
        self.copy.start()

    def finish(self):
        self.copy.wait()


class GatherKV(Part):
    def __init__(self, own):
        trees, rows, width = own.shape
        self.trees, self.size = trees, lax.axis_size("dp")
        self.ins = [(own, VMEM)]
        self.outs = [(jax.ShapeDtypeStruct((trees, self.size, rows, width), BF16), VMEM)]
        self.scratch = [SEM((self.size, trees)), SEM((self.size, trees)), SEM((trees, 2))]

    def bind(self, ins, outs, scratch):
        (self.own,), (self.out,) = ins, outs
        self.send, self.recv, self.relay_send = scratch
        self.me = lax.axis_index("dp")

    def copy(self, place, slot, tree):
        return remote(
            self.own.at[tree], self.out.at[tree, slot], self.send.at[place, tree],
            self.recv.at[slot, tree], {"dp": place},
        )

    def relay(self, source, target, turn, tree):
        return remote(
            self.out.at[tree, source], self.out.at[tree, source], self.relay_send.at[tree, turn],
            self.recv.at[source, tree], {"dp": target},
        )

    def targets(self):
        for tree in range(self.trees):
            for place in range(self.size):
                sent = place != self.me
                if self.size == 4:
                    sent = sent & jnp.logical_not(passed_on(place, self.me))
                yield place, tree, sent

    def start(self):
        for place, tree, sent in self.targets():
            @pl.when(sent)
            def _():
                self.copy(place, self.me, tree).start()

        self.out[:, self.me] = self.own[...]

    def run(self):
        for tree in range(self.trees):
            for place in line_order(self.size):
                @pl.when(place != self.me)
                def _():
                    self.copy(place, place, tree).wait_recv()

                for via, source, target, turn in line_relays(self.size):
                    if source == place:
                        @pl.when(self.me == via)
                        def _():
                            self.relay(source, target, turn, tree).start()

    def finish(self):
        for place, tree, sent in self.targets():
            @pl.when(sent)
            def _():
                self.copy(place, self.me, tree).wait_send()

        for via, source, target, turn in line_relays(self.size):
            @pl.when(self.me == via)
            def _():
                for tree in range(self.trees):
                    self.relay(source, target, turn, tree).wait_send()


class ScatterKV(Part):
    def __init__(self, whole, place_first=False, kept_as=F32, far_only=False):
        self.place_first = place_first
        trees, size, rows, width = whole.shape
        if place_first:
            trees, size = size, trees
        self.trees, self.size = trees, size
        self.sides = [(0, 1, 2, 0), (0, 1, 3, 1), (3, 2, 1, 0), (3, 2, 0, 1)] if size == 4 else []
        if far_only:
            self.sides = self.sides[1::2]
        self.ins = [(whole, VMEM)]
        self.outs = [(jax.ShapeDtypeStruct((trees, rows, width), kept_as), VMEM)]
        self.scratch = [
            pltpu.VMEM((rows, width), F32),
            pltpu.VMEM((size, trees, rows, width), BF16),
            pltpu.VMEM((2, trees, rows, width), BF16),
            SEM((size, trees)), SEM((size, trees)), SEM((2, trees)), SEM((2, trees)),
        ]

    def bind(self, ins, outs, scratch):
        (self.terms,), (self.out,) = ins, outs
        self.total, self.boxes, self.joint, self.send, self.recv, self.join_send, self.join_recv = scratch
        self.me = lax.axis_index("dp")

    def term(self, tree, place):
        return self.terms.at[place, tree] if self.place_first else self.terms.at[tree, place]

    def copy(self, place, slot, tree):
        return remote(
            self.term(tree, place), self.boxes.at[slot, tree], self.send.at[place, tree],
            self.recv.at[slot, tree], {"dp": place},
        )

    def by_way(self, via, target, turn, tree):
        return remote(
            self.term(tree, target), self.joint.at[turn, tree], self.join_send.at[turn, tree],
            self.join_recv.at[turn, tree], {"dp": via},
        )

    def joined(self, via, target, turn, tree):
        return remote(
            self.joint.at[turn, tree], self.boxes.at[via, tree], self.send.at[target, tree],
            self.recv.at[via, tree], {"dp": target},
        )

    def plain(self, place):
        ok = place != self.me
        for source, via, target, turn in self.sides:
            if place == target:
                ok = ok & (self.me != source) & (self.me != via)
        return ok

    def expected(self, place):
        ok = place != self.me
        for source, via, target, turn in self.sides:
            if place == source:
                ok = ok & (self.me != target)
        return ok

    def start(self):
        for tree in range(self.trees):
            for source, via, target, turn in self.sides:
                @pl.when(self.me == source)
                def _():
                    self.by_way(via, target, turn, tree).start()

            for place in range(self.size):
                @pl.when(self.plain(place))
                def _():
                    self.copy(place, self.me, tree).start()

    def pass_on(self):
        for tree in range(self.trees):
            for source, via, target, turn in self.sides:
                @pl.when(self.me == via)
                def _():
                    self.by_way(via, target, turn, tree).wait_recv()
                    both = self.joint[turn, tree].astype(F32)
                    both += self.term(tree, target)[...].astype(F32)
                    self.joint[turn, tree] = both.astype(BF16)
                    self.joined(via, target, turn, tree).start()

    def late(self):
        for tree in range(self.trees):
            self.total[...] = self.term(tree, self.me)[...].astype(F32)
            for place in line_order(self.size):
                @pl.when(self.expected(place))
                def _():
                    self.copy(place, place, tree).wait_recv()
                    self.total[...] += self.boxes[place, tree].astype(F32)

            self.out[tree] = self.total[...].astype(self.out.dtype)

    def finish(self):
        for tree in range(self.trees):
            for place in range(self.size):
                @pl.when(self.plain(place))
                def _():
                    self.copy(place, self.me, tree).wait_send()

            for source, via, target, turn in self.sides:
                @pl.when(self.me == source)
                def _():
                    self.by_way(via, target, turn, tree).wait_send()

                @pl.when(self.me == via)
                def _():
                    self.joined(via, target, turn, tree).wait_send()


class TotalOverAll(Part):
    axes = ("section", "tensor", "dp")

    def __init__(self, own):
        sizes = [lax.axis_size(axis) for axis in self.axes]
        self.ins = [(own, VMEM)]
        self.outs = [(jax.ShapeDtypeStruct(own.shape, F32), VMEM)]
        self.scratch = [pltpu.VMEM((size,) + own.shape, F32) for size in sizes]
        self.scratch += [SEM((size,)) for size in sizes] * 2

    def run(self):
        out = self.out_refs[0]
        out[...] = self.in_refs[0][...]
        for axis, box, send, recv in zip(self.axes, self.refs[:3], self.refs[3:6], self.refs[6:9]):
            size, me = lax.axis_size(axis), lax.axis_index(axis)
            box[me] = out[...]

            def spread(place, slot):
                return remote(box.at[me], box.at[slot], send.at[place], recv.at[slot], {axis: place})

            for place in range(size):
                @pl.when(place != me)
                def _():
                    spread(place, me).start()

            for place in range(size):
                @pl.when(place != me)
                def _():
                    spread(place, place).wait_recv()
                    spread(place, me).wait_send()

            total = box[0]
            for place in range(1, size):
                total += box[place]
            out[...] = total


def chunk_count(rows):
    return 3 if rows % 24 == 0 else 1


class Gatherer:
    def __init__(self, axis, rows, half):
        self.axis, self.half = axis, half
        self.size = size = lax.axis_size(axis)
        self.chunks = chunks = chunk_count(rows)
        self.rows = rows // chunks
        self.scratch = [pltpu.VMEM((2, chunks, size, 2 * self.rows, half), BF16)]
        self.scratch += [SEM((chunks, size))] * 4 + [SEM((chunks, 2))]

    def bind(self, refs):
        self.board, self.send, self.recv, self.sib_send, self.sib_recv, self.relay_send = refs
        self.core = lax.axis_index("section")
        self.sibling = 1 - self.core
        self.me = lax.axis_index(self.axis)
        self.relays = line_relays(self.size) if self.axis == "dp" else []
        self.order = line_order(self.size) if self.axis == "dp" else range(self.size)

    def direct(self, place):
        sent = place != self.me
        if self.relays:
            sent = sent & jnp.logical_not(passed_on(place, self.me))
        return sent

    def spread(self, chunk, place, slot):
        block = self.board.at[self.core, chunk, slot]
        return remote(
            block, block, self.send.at[chunk, place], self.recv.at[chunk, slot], {self.axis: place}
        )

    def passed(self, chunk, source, target, turn):
        block = self.board.at[self.core, chunk, source]
        return remote(
            block, block, self.relay_send.at[chunk, turn], self.recv.at[chunk, source],
            {self.axis: target},
        )

    def over(self, tree, chunk, slot):
        block = self.board.at[tree, chunk, slot]
        return remote(
            block, block, self.sib_send.at[chunk, slot], self.sib_recv.at[chunk, slot],
            {"section": self.sibling},
        )

    def begin(self, chunk, result):
        half = self.half
        piece = jnp.concatenate([result[:, :half], result[:, half:]], axis=0)
        self.board[self.core, chunk, self.me] = piece.astype(BF16)
        for place in range(self.size):
            @pl.when(self.direct(place))
            def _():
                self.spread(chunk, place, self.me).start()

        self.over(self.core, chunk, self.me).start()

    def arrive(self, chunk):
        for place in self.order:
            @pl.when(place != self.me)
            def _():
                self.spread(chunk, place, place).wait_recv()

            for via, source, target, turn in self.relays:
                if source == place:
                    @pl.when(self.me == via)
                    def _():
                        self.passed(chunk, source, target, turn).start()

            @pl.when(place != self.me)
            def _():
                self.over(self.core, chunk, place).start()

    def arrive_over(self, chunk):
        for place in range(self.size):
            self.over(self.sibling, chunk, place).wait_recv()

    def side_rows(self, block, side):
        return block[side * self.rows : (side + 1) * self.rows]

    def unpack(self, out, tree):
        @pl.loop(0, self.half // CHUNK)
        def _(step):
            at = pl.multiple_of(step * CHUNK, CHUNK)
            blocks = [
                self.board[tree, chunk, place, :, pl.ds(at, CHUNK)].astype(F32)
                for place in range(self.size)
                for chunk in range(self.chunks)
            ]
            for side in range(2):
                whole = [self.side_rows(block, side) for block in blocks]
                out[tree, :, pl.ds(side * self.half + at, CHUNK)] = jnp.concatenate(
                    whole, axis=0
                ).astype(BF16)

    def unpack_chunk(self, out, chunk):
        @pl.loop(0, self.half // CHUNK)
        def _(step):
            at = pl.multiple_of(step * CHUNK, CHUNK)
            blocks = [
                self.board[tree, chunk, place, :, pl.ds(at, CHUNK)].astype(F32)
                for place in range(self.size)
                for tree in range(2)
            ]
            for side in range(2):
                whole = [self.side_rows(block, side) for block in blocks]
                out[chunk, :, pl.ds(side * self.half + at, CHUNK)] = jnp.concatenate(
                    whole, axis=0
                ).astype(BF16)

    def complete(self, out):
        for chunk in range(self.chunks):
            self.arrive(chunk)
        self.unpack(out, self.core)
        for chunk in range(self.chunks):
            self.arrive_over(chunk)
        self.unpack(out, self.sibling)

    def finish(self):
        for chunk in range(self.chunks):
            for place in range(self.size):
                @pl.when(self.direct(place))
                def _():
                    self.spread(chunk, place, self.me).wait_send()

                self.over(self.core, chunk, place).wait_send()

            for via, source, target, turn in self.relays:
                @pl.when(self.me == via)
                def _():
                    self.passed(chunk, source, target, turn).wait_send()


class Scatterer:
    def __init__(self, axis, rows, half):
        self.axis, self.half = axis, half
        self.size = size = lax.axis_size(axis)
        self.chunks = chunks = chunk_count(rows)
        self.rows = rows // chunks
        block = (2 * self.rows, half)
        self.scratch = [pltpu.VMEM((chunks, size) + block, BF16)] * 4
        self.scratch += [pltpu.VMEM((chunks,) + block, F32), pltpu.VMEM((chunks,) + block, BF16)]
        self.scratch += [SEM((chunks, size))] * 4 + [SEM((chunks,))] * 2

    def bind(self, refs):
        self.to_sib, self.from_sib, self.to_peer, self.from_peer, self.total, self.joint = refs[:6]
        self.sib_send, self.sib_recv, self.peer_send, self.peer_recv = refs[6:10]
        self.join_send, self.join_recv = refs[10:]
        self.core = lax.axis_index("section")
        self.sibling = 1 - self.core
        self.me = lax.axis_index(self.axis)
        self.sides = [(0, 1, 3), (3, 2, 0)] if self.axis == "dp" and self.size == 4 else []
        self.order = [0, 3, 1, 2] if self.sides else range(self.size)

    def over(self, chunk, place):
        return remote(
            self.to_sib.at[chunk, place], self.from_sib.at[chunk, place],
            self.sib_send.at[chunk, place], self.sib_recv.at[chunk, place],
            {"section": self.sibling},
        )

    def spread(self, chunk, place, slot):
        return remote(
            self.to_peer.at[chunk, place], self.from_peer.at[chunk, slot],
            self.peer_send.at[chunk, place], self.peer_recv.at[chunk, slot], {self.axis: place},
        )

    def by_way(self, chunk, via, target):
        return remote(
            self.to_peer.at[chunk, target], self.joint.at[chunk], self.join_send.at[chunk],
            self.join_recv.at[chunk], {self.axis: via},
        )

    def plain(self, place):
        ok = place != self.me
        for source, via, target in self.sides:
            if place == target:
                ok = ok & (self.me != source) & (self.me != via)
        return ok

    def expected(self, place):
        ok = place != self.me
        for source, via, target in self.sides:
            if place == source:
                ok = ok & (self.me != target)
        return ok

    def over_columns(self, body):
        @pl.loop(0, self.half // CHUNK)
        def _(step):
            body(pl.multiple_of(step * CHUNK, CHUNK))

    def absorb(self, chunk, mine):
        for place in self.order:
            self.over(chunk, place).wait_recv()

            def add(at):
                both = mine(place, at)
                both += self.from_sib[chunk, place, :, pl.ds(at, CHUNK)].astype(F32)
                self.to_peer[chunk, place, :, pl.ds(at, CHUNK)] = both.astype(BF16)

                @pl.when(place == self.me)
                def _():
                    self.total[chunk, :, pl.ds(at, CHUNK)] = both

            self.over_columns(add)

            for source, via, target in self.sides:
                if place == target:
                    @pl.when(self.me == source)
                    def _():
                        self.by_way(chunk, via, target).start()

            @pl.when(self.plain(place))
            def _():
                self.spread(chunk, place, self.me).start()

        for source, via, target in self.sides:
            @pl.when(self.me == via)
            def _():
                self.by_way(chunk, via, target).wait_recv()

                def add(at):
                    at = pl.ds(at, CHUNK)
                    both = self.to_peer[chunk, target, :, at].astype(F32)
                    both += self.joint[chunk, :, at].astype(F32)
                    self.to_peer[chunk, target, :, at] = both.astype(BF16)

                self.over_columns(add)
                self.spread(chunk, target, self.me).start()

    def collect(self, chunk):
        for place in self.order:
            @pl.when(self.expected(place))
            def _():
                self.spread(chunk, place, place).wait_recv()
                self.total[chunk] += self.from_peer[chunk, place].astype(F32)

        total = self.total[chunk]
        return jnp.concatenate([total[: self.rows], total[self.rows :]], axis=1)

    def finish(self):
        for chunk in range(self.chunks):
            for place in range(self.size):
                self.over(chunk, place).wait_send()

                @pl.when(self.plain(place))
                def _():
                    self.spread(chunk, place, self.me).wait_send()

            for source, via, target in self.sides:
                @pl.when(self.me == source)
                def _():
                    self.by_way(chunk, via, target).wait_send()

                @pl.when(self.me == via)
                def _():
                    self.spread(chunk, target, self.me).wait_send()


class RowScatterer(Scatterer):
    def packed(self, tree, chunk, place, at):
        rows = self.rows
        first = rows * (place * self.chunks + chunk)
        low = first // 16 * 16
        high = -(-(first + rows) // 16) * 16
        parts = [
            self.terms[tree, low:high, pl.ds(side * self.half + at, CHUNK)].astype(F32)[
                first - low : first - low + rows
            ]
            for side in range(2)
        ]
        return jnp.concatenate(parts, axis=0)

    def prepare(self, terms):
        self.terms = terms
        for chunk in range(self.chunks):
            for place in range(self.size):
                def pack(at):
                    self.to_sib[chunk, place, :, pl.ds(at, CHUNK)] = self.packed(
                        self.sibling, chunk, place, at
                    ).astype(BF16)

                self.over_columns(pack)

    def start(self):
        for chunk in range(self.chunks):
            for place in range(self.size):
                self.over(chunk, place).start()

    def send_on(self):
        for chunk in range(self.chunks):
            self.absorb(chunk, lambda place, at: self.packed(self.core, chunk, place, at))


class Staged(Part):
    def __init__(self, ins, outs, scratch, helpers):
        self.in_names, self.out_names, self.scratch_names = list(ins), list(outs), list(scratch)
        self.ins, self.outs = list(ins.values()), list(outs.values())
        self.helpers = helpers
        self.scratch = list(scratch.values())
        for helper in helpers:
            self.scratch += helper.scratch

    def bind(self, ins, outs, scratch):
        scratch = list(scratch)
        names = self.in_names + self.out_names + self.scratch_names
        count = len(self.scratch_names)
        for name, ref in zip(names, list(ins) + list(outs) + scratch[:count]):
            setattr(self, name, ref)
        del scratch[:count]
        for helper in self.helpers:
            helper.bind(scratch[: len(helper.scratch)])
            del scratch[: len(helper.scratch)]

    def finish(self):
        for helper in self.helpers:
            helper.finish()


def vmem_f32(*shape):
    return (jax.ShapeDtypeStruct(shape, F32), VMEM)


def vmem_bf16(*shape):
    return (jax.ShapeDtypeStruct(shape, BF16), VMEM)


def rows_at(chunk, rows):
    return pl.ds(pl.multiple_of(chunk * rows, 8), rows)


class LastHub(Staged):
    def __init__(self, terms, values, gain, add, other):
        rows, depth = values.shape
        half = depth // 2
        self.rows_in = RowScatterer("tensor", rows, half)
        self.rows_out = Gatherer("tensor", rows, half)
        super().__init__(
            {
                "terms": (terms, VMEM), "values": (values, VMEM), "gain": (gain, VMEM),
                "add": (add, VMEM), "other": (other, VMEM),
            },
            {
                "gain_grad": vmem_f32(1, depth),
                "gathered": vmem_bf16(2, self.rows_out.size * rows, depth),
            },
            {},
            [self.rows_in, self.rows_out],
        )

    def prepare(self):
        self.rows_in.prepare(self.terms)

    def start(self):
        self.rows_in.start()

    def run(self):
        self.rows_in.send_on()
        self.gain_grad[...] = jnp.zeros_like(self.gain_grad)
        for chunk in range(self.rows_in.chunks):
            at = rows_at(chunk, self.rows_in.rows)
            result, gain_grad = norm_back(
                self.rows_in.collect(chunk), self.values[at], self.gain[...]
            )
            self.gain_grad[...] += gain_grad
            self.rows_out.begin(chunk, result + self.add[at])

    def late(self):
        self.rows_out.complete(self.gathered)

        @pl.when(lax.axis_index("section") == 1)
        def _():
            self.gathered[...] = self.other[...]


class RowsOut(Staged):
    def __init__(self, own, other=None):
        rows, depth = own.shape
        self.rows_out = Gatherer("tensor", rows, depth // 2)
        self.has_other = other is not None
        super().__init__(
            {"own": (own, VMEM)} | ({"other": (other, VMEM)} if self.has_other else {}),
            {"gathered": vmem_bf16(2, self.rows_out.size * rows, depth)},
            {},
            [self.rows_out],
        )

    def start(self):
        for chunk in range(self.rows_out.chunks):
            self.rows_out.begin(chunk, self.own[rows_at(chunk, self.rows_out.rows)])

    def late(self):
        self.rows_out.complete(self.gathered)
        if self.has_other:
            @pl.when(lax.axis_index("section") == 0)
            def _():
                self.gathered[...] = self.other[...]


class FeedForward(Staged):
    def __init__(self, terms, own, gain, weights, forward, backward, extra):
        rows, depth = own.shape
        half = depth // 2
        units = weights[0].shape[0]
        self.has_forward, self.has_backward, self.units = forward, backward, units
        self.depth = depth
        self.size = size = lax.axis_size("dp")
        self.rows_in = RowScatterer("tensor", rows, half)
        self.spread_in = Gatherer("dp", rows, half)
        self.chunks, self.rows = self.rows_in.chunks, self.rows_in.rows
        chunks, chunk_rows = self.chunks, 2 * size * self.rows
        helpers = [self.rows_in, self.spread_in]
        tensor_rows = lax.axis_size("tensor") * rows
        matrix = pltpu.VMEM((units, depth), BF16)
        ins = {"terms": (terms, VMEM), "own": (own, VMEM), "gain": (gain, VMEM)}
        ins |= {name: (w, HBM) for name, w in zip(("gate_hbm", "up_hbm", "down_hbm"), weights)}
        ins |= {name: (value, VMEM) for name, value in extra.items()}
        outs = {}
        scratch = {"w_gate": matrix, "w_up": matrix, "w_down": matrix, "load": SEM((3,))}
        kept = pltpu.VMEM((size, 2 * self.rows, half), F32)
        if forward:
            outs |= {
                "middle": vmem_f32(rows, depth),
                "mlp_in": vmem_bf16(chunks, chunk_rows, depth),
                "hidden": vmem_bf16(chunks, chunk_rows, units),
                "own_out": vmem_f32(rows, depth),
            }
            self.back = Scatterer("dp", rows, half)
            helpers += [self.back]
            scratch["kept"] = kept
        if forward and not backward:
            outs |= {
                "out": vmem_bf16(2, tensor_rows, depth),
                "gate": vmem_bf16(chunks, chunk_rows, units),
                "up": vmem_bf16(chunks, chunk_rows, units),
            }
            self.out_rows = Gatherer("tensor", rows, half)
            helpers += [self.out_rows]
        if forward and backward:
            outs["grad_mlp"] = vmem_bf16(chunks, chunk_rows, depth)
            self.grad_in = Gatherer("dp", rows, half)
            helpers += [self.grad_in]
            scratch |= {
                "gate": pltpu.VMEM((chunks, chunk_rows, units), F32),
                "up": pltpu.VMEM((chunks, chunk_rows, units), F32),
            }
        if backward:
            outs |= {
                "grad_gate": vmem_bf16(chunks, chunk_rows, units),
                "grad_up": vmem_bf16(chunks, chunk_rows, units),
                "grad_middle": vmem_f32(rows, depth),
                "mlp_gain_grad": vmem_f32(1, depth),
                "grad_attn": vmem_bf16(2, tensor_rows, depth),
            }
            self.grad_back = Scatterer("dp", rows, half)
            self.grad_rows = Gatherer("tensor", rows, half)
            helpers += [self.grad_back, self.grad_rows]
            scratch["grad_kept"] = kept
        if backward and not forward:
            outs |= {
                "gain_grad": vmem_f32(1, depth),
                "grad_own": vmem_f32(rows, depth),
                "grad_mlp": vmem_bf16(chunks, chunk_rows, depth),
            }
        super().__init__(ins, outs, scratch, helpers)

    def loads(self):
        pairs = [(self.gate_hbm, self.w_gate), (self.up_hbm, self.w_up), (self.down_hbm, self.w_down)]
        return [
            pltpu.make_async_copy(src, dst, self.load.at[i]) for i, (src, dst) in enumerate(pairs)
        ]

    def prepare(self):
        for copy in self.loads():
            copy.start()
        self.rows_in.prepare(self.terms)

    def start(self):
        self.rows_in.start()
        if self.has_forward and self.has_backward:
            for chunk in range(self.chunks):
                self.grad_in.begin(chunk, self.grad_own[rows_at(chunk, self.rows)])

    def run(self):
        self.rows_in.send_on()
        if self.has_backward:
            self.mlp_gain_grad[...] = jnp.zeros_like(self.mlp_gain_grad)
        if not self.has_forward:
            self.gain_grad[...] = jnp.zeros_like(self.gain_grad)
        for chunk in range(self.chunks):
            at = rows_at(chunk, self.rows)
            total = self.rows_in.collect(chunk)
            if self.has_forward:
                middle = self.own[at] + total
                self.middle[at] = middle
                mean_sq = jnp.mean(middle * middle, axis=1, keepdims=True)
                normed = middle * lax.rsqrt(mean_sq + EPSILON) * self.gain[...]
                self.spread_in.begin(chunk, normed)
            else:
                result, gain_grad = norm_back(total, self.own[at], self.gain[...])
                self.gain_grad[...] += gain_grad
                result = (result + self.add[at]).astype(BF16).astype(F32)
                self.grad_own[at] = result
                self.spread_in.begin(chunk, result)
        for copy in self.loads():
            copy.wait()

        self.spread_in.arrive(0)
        if self.has_forward and self.has_backward:
            self.grad_in.arrive(0)

        @pl.loop(0, self.chunks)
        def _(chunk):
            self.spread_in.arrive_over(chunk)
            if self.has_forward:
                self.spread_in.unpack_chunk(self.mlp_in, chunk)
                self.forward_chunk(chunk)
            else:
                self.spread_in.unpack_chunk(self.grad_mlp, chunk)
            if self.has_forward and self.has_backward:
                self.grad_in.arrive_over(chunk)
                self.grad_in.unpack_chunk(self.grad_mlp, chunk)
            if self.has_backward:
                self.backward_chunk(chunk)

            @pl.when(chunk + 1 < self.chunks)
            def _():
                self.spread_in.arrive(chunk + 1)
                if self.has_forward and self.has_backward:
                    self.grad_in.arrive(chunk + 1)

            if self.has_forward:
                self.back.absorb(chunk, lambda place, at: self.kept[place, :, pl.ds(at, CHUNK)])
            if self.has_backward:
                self.grad_back.absorb(
                    chunk, lambda place, at: self.grad_kept[place, :, pl.ds(at, CHUNK)]
                )

            @pl.when(chunk > 0)
            def _():
                self.hand_back(chunk - 1)

        self.hand_back(self.chunks - 1)
        if self.has_backward:
            self.grad_rows.complete(self.grad_attn)
        else:
            self.out_rows.complete(self.out)

    def hand_back(self, chunk):
        at = rows_at(chunk, self.rows)
        if self.has_backward:
            values = self.middle if self.has_forward else self.middle_in
            gain = self.gain if self.has_forward else self.mlp_gain
            result, gain_grad = norm_back(self.grad_back.collect(chunk), values[at], gain[...])
            self.mlp_gain_grad[...] += gain_grad
            result += self.grad_own[at]
            self.grad_middle[at] = result
            self.grad_rows.begin(chunk, result)
        if self.has_forward:
            output = (self.middle[at] + self.back.collect(chunk)).astype(BF16).astype(F32)
            self.own_out[at] = output
            if not self.has_backward:
                self.out_rows.begin(chunk, output)

    def unit_tiles(self, body):
        tile = 256

        @pl.loop(0, self.units // tile)
        def _(step):
            body(pl.ds(pl.multiple_of(step * tile, tile), tile))

    def forward_chunk(self, chunk):
        def tile(at):
            rows = self.mlp_in[chunk]
            gate = dot_inner(rows, self.w_gate[at, :])
            up = dot_inner(rows, self.w_up[at, :])
            self.gate[chunk, :, at] = gate.astype(self.gate.dtype)
            self.up[chunk, :, at] = up.astype(self.up.dtype)
            self.hidden[chunk, :, at] = (gate * jax.nn.sigmoid(gate) * up).astype(BF16)

        self.unit_tiles(tile)
        self.terms_out(
            chunk, self.back, self.kept, lambda at: dot(self.hidden[chunk], self.w_down[:, at])
        )

    def backward_chunk(self, chunk):
        def tile(at):
            grad_hidden = dot_inner(self.grad_mlp[chunk], self.w_down[at, :])
            gate, up = self.gate[chunk, :, at].astype(F32), self.up[chunk, :, at].astype(F32)
            share = jax.nn.sigmoid(gate)
            act = gate * share
            self.grad_up[chunk, :, at] = (grad_hidden * act).astype(BF16)
            self.grad_gate[chunk, :, at] = (
                grad_hidden * up * (share + act * (1.0 - share))
            ).astype(BF16)

        self.unit_tiles(tile)
        self.terms_out(
            chunk, self.grad_back, self.grad_kept,
            lambda at: dot(self.grad_gate[chunk], self.w_gate[:, at])
            + dot(self.grad_up[chunk], self.w_up[:, at]),
        )

    def terms_out(self, chunk, scatterer, kept, product):
        rows, half = self.rows, self.depth // 2
        first = lax.axis_index("section") == 0

        @pl.loop(0, half // CHUNK)
        def _(step):
            low = pl.multiple_of(step * CHUNK, CHUNK)
            at = pl.ds(low, CHUNK)
            sides = [product(pl.ds(side * half + low, CHUNK)) for side in range(2)]
            for place in range(self.size):
                trees = []
                for tree in range(2):
                    start = (2 * place + tree) * rows
                    trees.append(
                        jnp.concatenate([side[start : start + rows] for side in sides], axis=0)
                    )
                kept[place, :, at] = jnp.where(first, trees[0], trees[1])
                scatterer.to_sib[chunk, place, :, at] = jnp.where(
                    first, trees[1], trees[0]
                ).astype(BF16)

        for place in range(self.size):
            scatterer.over(chunk, place).start()


def finish_weights(first, second, attn_first, attn_second, arrived, widths, core, rows_out, tile=256):
    units, own_depth = first[0].shape
    q_width, k_width, _, _ = widths
    starts = [0, q_width, q_width + k_width, 0]
    steps = units // tile
    count = len(rows_out)

    def transposed(block):
        size = block.shape[1]
        rows = lax.broadcasted_iota(jnp.int32, (size, size), 0)
        identity = (rows == lax.broadcasted_iota(jnp.int32, rows.shape, 1)).astype(BF16)
        return dot_inner(identity, block)

    def kernel(core_ref, *refs):
        ins, passed_in = refs[:12], refs[12 : 12 + count]
        (gate, up, down), attn_outs = refs[12 + count : 15 + count], refs[15 + count : 19 + count]
        for src, dst in zip(passed_in, refs[19 + count :]):
            dst[...] = src[...]

        on_first = core_ref[0] == 0
        picked = [jnp.where(on_first, ins[i][...], ins[3 + i][...]) for i in range(3)]
        gate[...] = transposed(picked[0])
        up[...] = transposed(picked[1])
        down[...] = picked[2].astype(F32)

        @pl.when(pl.program_id(0) == 0)
        def _():
            for index, (out, start, width) in enumerate(zip(attn_outs, starts, widths)):
                at = pl.ds(start, width)
                mine, other, came = (ins[6 + 2 * i + index // 3][:, at] for i in range(3))
                halves = [jnp.where(on_first, mine, came), jnp.where(on_first, came, other)]
                for half, values in enumerate(halves):
                    if index == 3:
                        out[pl.ds(half * width, width)] = transposed(values)
                    else:
                        out[:, pl.ds(half * width, width)] = values.astype(F32)

    def whole(shape):
        return pl.BlockSpec(shape, lambda step: (0, 0))

    tall = pl.BlockSpec((tile, own_depth), lambda step: (step, 0))
    wide = pl.BlockSpec((own_depth, tile), lambda step: (0, step))
    attn_ins = [*attn_first, *attn_second, *arrived]
    flat_rows = [item.reshape(-1, item.shape[-1]) for item in rows_out]
    passed = [
        pl.BlockSpec((item.shape[0] // steps, item.shape[1]), lambda step: (step, 0))
        for item in flat_rows
    ]
    attn_shapes = [(own_depth, 2 * width) for width in widths[:3]] + [(2 * q_width, own_depth)]
    shapes = [(own_depth, units)] * 2 + [(units, own_depth)] + attn_shapes
    return pl.pallas_call(
        kernel,
        grid=(steps,),
        out_shape=[jax.ShapeDtypeStruct(shape, F32) for shape in shapes]
        + [jax.ShapeDtypeStruct(item.shape, item.dtype) for item in flat_rows],
        in_specs=[pl.BlockSpec(memory_space=pltpu.SMEM)]
        + [tall] * 6
        + [whole(item.shape) for item in attn_ins]
        + passed,
        out_specs=[wide, wide, tall] + [whole(shape) for shape in attn_shapes] + passed,
        cost_estimate=pl.CostEstimate(flops=0, bytes_accessed=25_000_000, transcendentals=0),
        compiler_params=pltpu.CompilerParams(vmem_limit_bytes=60 << 20),
    )(core.reshape(1), *first, *second, *attn_ins, *flat_rows)


def hub_plain(terms, own_args, body, own_outs, scatter, gathers):
    total = None
    if scatter:
        mine = lax.psum_scatter(terms, "section", scatter_dimension=0, tiled=True)
        mine = lax.psum_scatter(mine, scatter, scatter_dimension=1, tiled=True)[0]
        total = mine.astype(F32)

    class Cell:
        def __setitem__(self, _, value):
            self.value = value

    cells = [Cell() for _ in own_outs]
    result = body(total, own_args, cells).astype(BF16)
    gathered = [
        lax.all_gather(lax.all_gather(result, axis, axis=0, tiled=True), "section", axis=0)
        for axis in gathers
    ]
    return [cell.value for cell in cells] + gathered


def with_cargo(part, cargo, axes, collective_id, cost_us, vmem):
    outs = fused(cargo + [part], axes, bool(cargo), collective_id, cost_us, vmem)
    return outs[-1], outs[:-1]


def norm_back(total, values, gain):
    scale = lax.rsqrt(jnp.mean(values * values, axis=1, keepdims=True) + EPSILON)
    unit = values * scale
    gain_grad = jnp.sum(total * unit, axis=0, keepdims=True)
    scaled = total * gain
    along = jnp.mean(scaled * unit, axis=1, keepdims=True)
    return ((scaled - unit * along) * scale, gain_grad)


def norm_body(total, args, outs):
    middle = args[0] + total
    outs[0][...] = middle
    return rms_scale(middle, args[1])


def add_body(total, args, outs):
    result = args[0] + total
    outs[0][...] = result
    return result


def norm_back_body(total, args, outs):
    result, outs[1][...] = norm_back(total, args[0], args[1])
    result += args[2]
    outs[0][...] = result
    return result


def embed(q_pre, k_pre, q_scale, k_scale, cos_table, sine_table):
    queries = rms_scale(q_pre, q_scale)
    keys = rms_scale(k_pre, k_scale)
    return (
        rotate(queries, cos_table[:, :, None], sine_table[:, :, None]),
        rotate(keys, cos_table, sine_table),
    )


def attn_forward(hidden_in, weights, gains, slot, gather):
    attn_scale, _, q_scale, k_scale = gains
    w_qkv, w_out = weights[:2]
    allowed, cos_table, sine_table = slot
    trees, row_count, depth = hidden_in.shape
    q_width = w_out.shape[0]
    normed = rms_scale(hidden_in.astype(F32), attn_scale).astype(BF16).reshape(-1, depth)
    qkv = dot(normed, w_qkv).reshape(trees, row_count, -1)
    q_pre = qkv[:, :, :q_width].reshape(trees, row_count, -1, HD)
    k_pre = qkv[:, :, q_width : q_width + HD]
    value_bf = qkv[:, :, q_width + HD :].astype(BF16)
    queries, keys_rot = embed(q_pre, k_pre, q_scale, k_scale, cos_table, sine_table)
    query_bf = queries.astype(BF16)
    kv_all = gather(jnp.concatenate([keys_rot.astype(BF16), value_bf], axis=2))
    key_all = kv_all[:, :, :HD]
    value_all = kv_all[:, :, HD:]
    scores = masked_scores(query_bf, key_all, allowed)
    row_max = jnp.max(scores, axis=-1, keepdims=True)
    exp_scores = jnp.exp(scores - row_max)
    row_total = jnp.sum(exp_scores, axis=-1, keepdims=True)
    prob_bf = (exp_scores / row_total).astype(BF16)
    log_total = row_max + jnp.log(row_total)
    attended = jnp.einsum("bgrt,btd->brgd", prob_bf, value_all, preferred_element_type=F32)
    attended_bf = attended.reshape(trees * row_count, -1).astype(BF16)
    terms = dot(attended_bf, w_out).astype(BF16).reshape(trees, row_count, depth)
    saved = (normed, q_pre, k_pre, query_bf, key_all, value_all, log_total, attended_bf)
    return (terms, saved)


def attn_backward(grad_attn, saved, weights, gains, slot, scatter):
    _, _, q_scale, k_scale = gains
    w_qkv, w_out = weights[:2]
    allowed, cos_table, sine_table = slot
    normed, q_pre, k_pre, query_bf, key_all, value_all, log_total, attended_bf = saved
    trees, row_count = query_bf.shape[:2]
    depth = normed.shape[1]
    grad_attn = grad_attn.reshape(-1, depth)
    grad_heads = dot_inner(grad_attn, w_out).astype(BF16).reshape(query_bf.shape)
    scores = masked_scores(query_bf, key_all, allowed)
    prob_full = jnp.exp(scores - log_total)
    grad_prob = jnp.einsum("brgd,btd->bgrt", grad_heads, value_all, preferred_element_type=F32)
    row_dot = jnp.sum(prob_full * grad_prob, axis=-1, keepdims=True)
    grad_scores = (prob_full * (grad_prob - row_dot)).astype(BF16)
    scale_factor = HD ** (-0.5)
    grad_query = (
        jnp.einsum("bgrt,btd->brgd", grad_scores, key_all, preferred_element_type=F32)
        * scale_factor
    )
    grad_key_all = (
        jnp.einsum("bgrt,brgd->btd", grad_scores, query_bf, preferred_element_type=F32)
        * scale_factor
    )
    grad_value_all = jnp.einsum(
        "bgrt,brgd->btd", prob_full.astype(BF16), grad_heads, preferred_element_type=F32
    )
    grad_kv = scatter(jnp.concatenate([grad_key_all, grad_value_all], axis=2).astype(BF16))
    _, embedding_pull = jax.vjp(
        partial(embed, cos_table=cos_table, sine_table=sine_table), q_pre, k_pre, q_scale, k_scale
    )
    grad_q_pre, grad_k_pre, grad_q_scale, grad_k_scale = embedding_pull(
        (grad_query, grad_kv[:, :, :HD].astype(F32))
    )
    qkv_grad = jnp.concatenate(
        [
            grad_q_pre.astype(BF16).reshape(trees, row_count, -1),
            grad_k_pre.astype(BF16),
            grad_kv[:, :, HD:].astype(BF16),
        ],
        axis=2,
    ).reshape(trees * row_count, -1)
    terms = dot_inner(qkv_grad, w_qkv).astype(BF16).reshape(trees, row_count, depth)
    return (terms, [(normed, qkv_grad), (grad_attn, attended_bf)], [grad_q_scale, grad_k_scale])


def plain_layers(hidden, own_in, grad_own, weights, gains, slot, shared_kv):
    depth = own_in.shape[1]
    own_shape = own_in.shape

    def gather(own):
        return lax.all_gather(own, "dp", axis=1, tiled=True)

    def scatter(whole):
        total = lax.psum_scatter(whole, "dp", scatter_dimension=1, tiled=True)
        if shared_kv:
            total = lax.psum(total, "section")
            total = jnp.where(lax.axis_index("section") == 0, total, jnp.zeros_like(total))
        return total

    outputs, kept = [], []
    for layer in range(2):
        _, _, w_gate, w_up, w_down = weights[layer]
        terms, saved = attn_forward(hidden, weights[layer], gains[layer], slot, gather)
        mlp_scale = gains[layer][1][None]
        middle, mlp_in = hub_plain(
            terms, [own_in, mlp_scale], norm_body, [own_shape], "tensor", ["dp"]
        )
        mlp_in = mlp_in.reshape(-1, depth)
        gate, up = dot_inner(mlp_in, w_gate), dot_inner(mlp_in, w_up)
        hidden_bf = swiglu(gate, up).astype(BF16)
        terms = dot(hidden_bf, w_down).astype(BF16).reshape(2, -1, depth)
        kept.append((own_in, saved, middle, mlp_in, gate, up, hidden_bf))
        own_in, hidden = hub_plain(terms, [middle], add_body, [own_shape], "dp", ["tensor"])
        own_in = own_in.astype(BF16).astype(F32)
        outputs.append(hidden)

    own_outs = [own_shape, (1, depth)]
    grads, products, gain_grads = [None, None], [None, None], [None, None]
    (grad_mlp,) = hub_plain(None, [grad_own], lambda total, args, outs: args[0], [], None, ["dp"])
    for layer in (1, 0):
        _, _, w_gate, w_up, w_down = weights[layer]
        own_in, saved, middle, mlp_in, gate, up, hidden_bf = kept[layer]
        grad_mlp = grad_mlp.reshape(-1, depth)
        _, pull = jax.vjp(swiglu, gate, up)
        grad_gate, grad_up = (item.astype(BF16) for item in pull(dot_inner(grad_mlp, w_down)))
        terms = (dot(grad_gate, w_gate) + dot(grad_up, w_up)).astype(BF16).reshape(2, -1, depth)
        grad_middle, mlp_gain_grad, grad_attn = hub_plain(
            terms, [middle, gains[layer][1][None], grad_own], norm_back_body, own_outs, "dp",
            ["tensor"],
        )
        terms, pairs, head_grads = attn_backward(
            grad_attn, saved, weights[layer], gains[layer], slot, scatter
        )
        grad_own, gain_grad, grads[layer], grad_next = hub_plain(
            terms, [own_in, gains[layer][0][None], grad_middle], norm_back_body, own_outs, "tensor",
            ["tensor", "dp"],
        )
        grad_own = grad_own.astype(BF16).astype(F32)
        pairs += [(grad_gate, mlp_in), (grad_up, mlp_in), (hidden_bf, grad_mlp)]
        products[layer] = pairs
        gain_grads[layer] = jnp.concatenate([gain_grad[0], mlp_gain_grad[0], *head_grads])
        grad_mlp = grad_next
    return (outputs, grads, products, gain_grads)


def swap_cores(mine, other):
    core = lax.axis_index("section")
    arrived = lax.ppermute(other, "section", [(0, 1), (1, 0)])
    return (jnp.where(core == 0, mine, arrived), jnp.where(core == 0, arrived, mine))


def on_device(
    inputs, cotangent, seg_ids, parents, order, attn_gain, w_query, w_key, w_value, w_out,
    q_gain, k_gain, mlp_gain, w_gate, w_up, w_down,
):
    core = lax.axis_index("section")
    data_index = lax.axis_index("dp")
    tensor_index = lax.axis_index("tensor")
    dp_size = lax.axis_size("dp")
    tensor_size = lax.axis_size("tensor")
    trees, row_count, depth = inputs.shape
    own_rows = row_count // tensor_size
    row_start = data_index * row_count
    own_depth = w_query.shape[1]
    q_width = w_query.shape[2] // 2
    shared_kv = w_key.shape[2] == HD
    k_width = HD if shared_kv else w_key.shape[2] // 2
    own_units = w_gate.shape[2]
    share = own_units // (2 * dp_size)

    def pick(stacked, index):
        return lax.dynamic_index_in_dim(stacked, index, 0, keepdims=False)

    fast = (
        own_rows % 8 == 0
        and depth % (2 * CHUNK) == 0
        and row_count % 16 == 0
        and share % 16 == 0
        and own_depth % 128 == 0
        and not shared_kv
    )

    def halves(width, array):
        return [array[:, :width], array[:, array.shape[1] - width :]]

    unit_mats = [w_gate[0].T, w_up[0].T, w_down[0]]
    qkv_width = q_width + 2 * k_width
    gains_own = jnp.concatenate([attn_gain[0], mlp_gain[0], q_gain[0], k_gain[0]]).astype(F32)

    def spread_units(rows):
        return lax.all_gather(rows, "tensor", axis=0, tiled=True)

    def tied(value, *before):
        return lax.optimization_barrier((value, *before))[0]

    if fast:
        line = ["section", "dp"]
        everyone = ["section", "dp", "tensor"]
        (gate_rows, up_rows), (gains_all,) = fused(
            [UnitsOut(unit_mats[:2], 0), SharedRows(gains_own.reshape(-1, 128))], line, True, 1, 45, 60
        )
        shards = AttnShards(w_query[0], w_key[0], w_value[0], w_out[0])
        shards.arrays[0] = tied(shards.arrays[0], gate_rows)
        (w_qkv, w_heads), (down_rows,), (attn_shard,) = fused(
            [AttnOut(shards, 0), UnitsOut(unit_mats[2:], 0), HalfOver(shards)], line, True, 2, 80, 60
        )
        first_weights = [w_qkv, w_heads, spread_units(gate_rows), spread_units(up_rows)]
    else:
        gains_all = lax.all_gather(gains_own, ("section", "dp"))
        attn_halves = jnp.stack(
            [
                jnp.concatenate(parts, axis=1)
                for parts in zip(
                    halves(q_width, w_query[0]),
                    halves(k_width, w_key[0]),
                    halves(k_width, w_value[0]),
                    halves(q_width, w_out[0].T),
                )
            ]
        )
        attn_shards = swap_cores(pick(attn_halves, core), pick(attn_halves, 1 - core))
        unit_blocks = jnp.stack(unit_mats).reshape(3, 2, dp_size, share, own_depth)
        unit_blocks = unit_blocks.transpose(1, 2, 0, 3, 4)
        unit_shards = swap_cores(pick(unit_blocks, core), pick(unit_blocks, 1 - core))
        both_weights = []
        for layer in range(2):
            attn_all = lax.all_gather(attn_shards[layer], "dp", axis=0, tiled=True)
            pieces = exchange(unit_shards[layer], "dp")
            pieces = pieces.transpose(1, 2, 0, 3).reshape(3, share, depth)
            both_weights.append(
                (
                    attn_all[:, :qkv_width], attn_all[:, qkv_width:].T,
                    *(spread_units(pieces[i]) for i in range(3)),
                )
            )

    gains_all = gains_all.reshape(2, dp_size, -1)
    gains = [
        (
            gains_all[layer, :, :own_depth].reshape(depth),
            gains_all[layer, :, own_depth : 2 * own_depth].reshape(depth),
            gains_all[layer, 0, 2 * own_depth : 2 * own_depth + HD],
            gains_all[layer, 0, 2 * own_depth + HD :],
        )
        for layer in range(2)
    ]

    def slot_setup(slot_index):
        tree_id = pick(order, slot_index)
        allowed, row_positions = path_mask(
            pick(seg_ids, tree_id), pick(parents, tree_id), row_start, row_count
        )
        cos_table, sine_table = rope_tables(row_positions, HD)
        return (pick(inputs, tree_id), allowed, cos_table[:, 0], sine_table[:, 0])

    setups = [slot_setup(i) for i in range(trees)]
    hidden, *slot = (jnp.stack(item) for item in zip(*setups))

    def own_part(whole):
        return lax.dynamic_slice_in_dim(
            pick(whole, core), tensor_index * own_rows, own_rows, 0
        )

    own_in = own_part(hidden).astype(F32)
    grad_own = own_part(cotangent).astype(F32)

    def weight_products(pairs):
        return [dot_outer(left, right).astype(BF16) for left, right in pairs]

    def scatter_units(products):
        return [
            lax.psum_scatter(item, "tensor", scatter_dimension=0, tiled=True) for item in products
        ]

    def scatter_shards(products):
        return lax.psum_scatter(
            jnp.concatenate(products, axis=1), "dp", scatter_dimension=0, tiled=True
        )

    if fast:
        def units_on(*which):
            return [UnitsOut([unit_mats[i] for i in which], 1)]

        def kv_gather(own, cargo, collective_id, carried):
            (whole,), outs = with_cargo(GatherKV(own), cargo, everyone, collective_id, 40, 40)
            carried += outs
            return whole.reshape(trees, -1, 2 * HD)

        def kv_scatter(whole, cargo, collective_id, carried):
            part = ScatterKV(whole.reshape(trees, dp_size, row_count, 2 * HD))
            (total,), outs = with_cargo(part, cargo, everyone, collective_id, 30, 40)
            carried += outs
            return total

        def in_order(pairs):
            done = []
            for left, right in pairs:
                done += weight_products([(tied(left, *done[-1:]), right)])
            return done

        def flat(array):
            return array.reshape(-1, array.shape[-1])

        carried = []
        terms, saved_first = attn_forward(
            hidden, first_weights, gains[0], slot,
            lambda own: kv_gather(
                tied(own, *first_weights[2:]), [UnitsSpread(down_rows)] + units_on(0, 1, 2), 3, carried
            ),
        )
        (down_all,), (gate_rows, up_rows, down_rows) = carried
        first_weights.append(down_all)
        part = FeedForward(
            terms, own_in, gains[0][1][None], first_weights[2:], True, False, {}
        )
        outs, ((down_next,),) = with_cargo(part, [UnitsSpread(down_rows)], everyone, 4, 90, 60)
        middle_first, mlp_in_first, hidden_first, own_next, output_first, gate_first, up_first = outs
        attn_next = lax.all_gather(tied(attn_shard, gate_rows), "dp", axis=0)
        second_weights = [
            attn_next[:, :own_depth].reshape(depth, -1),
            attn_next[:, own_depth:].transpose(1, 0, 2).reshape(q_width, depth),
            spread_units(gate_rows), spread_units(up_rows),
        ]
        carried = []
        terms, saved_second = attn_forward(
            output_first, second_weights, gains[1], slot,
            lambda own: kv_gather(tied(own, second_weights[2]), [], 5, carried),
        )
        second_weights.append(down_next)
        part = FeedForward(
            terms, own_next, gains[1][1][None], second_weights[2:], True, True,
            {"grad_own": grad_own},
        )
        outs, _ = with_cargo(part, [], everyone, 6, 100, 60)
        (
            middle, mlp_in, hidden_bf, own_second, grad_mlp,
            grad_gate, grad_up, grad_middle, mlp_gain_second, grad_attn,
        ) = outs
        products = in_order([(flat(grad_gate), flat(mlp_in)), (flat(grad_up), flat(mlp_in))])
        unit_second = scatter_units(products)
        carried = []
        terms, pairs, head_second = attn_backward(
            grad_attn, saved_second, second_weights, gains[1], slot,
            lambda whole: kv_scatter(
                tied(whole, *products), [RowsOut(own_second, output_first)], 7, carried
            ),
        )
        ((layer_out,),) = carried
        unit_second += scatter_units(
            weight_products([(tied(flat(hidden_bf), layer_out), flat(grad_mlp))])
        )
        pairs = weight_products(pairs)
        attn_second = scatter_shards([tied(pairs[0], unit_second[1]), pairs[1]])
        terms = tied(terms, unit_second[0])
        part = FeedForward(
            terms, own_next, gains[1][0][None], first_weights[2:], False, True,
            {
                "add": grad_middle, "gate": gate_first, "up": up_first,
                "middle_in": middle_first, "mlp_gain": gains[0][1][None],
            },
        )
        outs, (home_second,) = with_cargo(
            part, [UnitsHome(unit_second[:1], 1)], everyone, 8, 90, 60
        )
        (
            grad_gate, grad_up, grad_middle, mlp_gain_first, grad_attn,
            attn_gain_second, own_incoming, grad_mlp,
        ) = outs
        products = in_order(
            [(flat(grad_gate), flat(mlp_in_first)), (flat(grad_up), flat(mlp_in_first))]
        )
        grad_attn = tied(grad_attn, *unit_second[1:], *products)
        unit_first = scatter_units([products[0], tied(products[1], attn_second)])
        carried = []
        terms, pairs, head_first = attn_backward(
            grad_attn, saved_first, first_weights, gains[0], slot,
            lambda whole: kv_scatter(
                whole, [UnitsHome(unit_second[1:], 1), RowsOut(own_incoming)], 9, carried
            ),
        )
        home_second += carried[0]
        (incoming_second,) = carried[1]
        unit_first += scatter_units(
            weight_products([(tied(flat(hidden_first), incoming_second), flat(grad_mlp))])
        )
        parts = [
            ScatterKV(item.reshape(dp_size, 4, own_depth // 4, -1), True, BF16, True)
            for item in weight_products(pairs)
        ]
        part = LastHub(terms, own_in, gains[0][0][None], grad_middle, incoming_second)
        (attn_gain_first, input_grad), (*attn_first, home_first) = with_cargo(
            part, parts + [UnitsHome(unit_first[:1], 0)], everyone, 10, 60, 60
        )
        attn_first = [item.reshape(own_depth, -1) for (item,) in attn_first]
        attn_second = [attn_second[:, :qkv_width], attn_second[:, qkv_width:]]
        gain_grads = [
            jnp.concatenate([attn_gain_first[0], mlp_gain_first[0], *head_first]),
            jnp.concatenate([attn_gain_second[0], mlp_gain_second[0], *head_second]),
        ]
    else:
        outputs, grads, products, gain_grads = plain_layers(
            hidden, own_in, grad_own, both_weights, gains, slot, shared_kv
        )
        layer_out = jnp.where(core == 0, *outputs)
        input_grad = jnp.where(core == 0, *grads)
        weight_grads = []
        for pairs in products:
            whole = weight_products(pairs)
            weight_grads.append((scatter_shards(whole[:2]), scatter_units(whole[2:])))

    gain_total = jnp.stack(gain_grads)
    if fast:
        others = [
            Swap(jnp.where(core == 0, second, first))
            for first, second in zip(attn_first, attn_second)
        ]
        (gain_total,), *arrived, down_home = fused(
            [TotalOverAll(gain_total.reshape(-1, 128)), *others, UnitsHome(unit_first[1:], 0)],
            everyone, True, 11, 60, 60,
        )
        grad_gate, grad_up, grad_down, *attn_grads, layer_out, input_grad = finish_weights(
            home_first + down_home, home_second, attn_first, attn_second,
            [item for (item,) in arrived], (q_width, k_width, k_width, q_width), core,
            (layer_out, input_grad),
        )
        layer_out = layer_out.reshape(trees, row_count, depth)
        input_grad = input_grad.reshape(trees, row_count, depth)
        gain_total = gain_total.reshape(2, -1)
    else:
        def bring_home(first, second):
            mine, other = jnp.where(core == 0, first, second), jnp.where(core == 0, second, first)
            arrived = lax.ppermute(other, "section", [(0, 1), (1, 0)])
            return (jnp.where(core == 0, mine, arrived), jnp.where(core == 0, arrived, mine))

        def pieces_of(grad):
            return exchange(
                jnp.stack(grad).reshape(3, share, dp_size, own_depth).transpose(2, 0, 1, 3), "dp"
            )

        attn_home = bring_home(weight_grads[0][0], weight_grads[1][0])
        unit_home = jnp.stack(bring_home(pieces_of(weight_grads[0][1]), pieces_of(weight_grads[1][1])))
        unit_home = unit_home.transpose(2, 0, 1, 3, 4).reshape(3, own_units, own_depth).astype(F32)
        grad_gate, grad_up, grad_down = unit_home[0].T, unit_home[1].T, unit_home[2]
        gain_total = lax.psum(gain_total, ("section", "dp", "tensor"))

        def joined(start, width):
            parts = [half[:, start : start + width] for half in attn_home]
            if shared_kv and start in (q_width, q_width + k_width):
                return parts[0].astype(F32)
            return jnp.concatenate(parts, axis=1).astype(F32)

        attn_grads = [
            joined(0, q_width), joined(q_width, k_width), joined(q_width + k_width, k_width),
            joined(qkv_width, q_width).T,
        ]

    gain_own = pick(gain_total, core)
    share_width = attn_gain.shape[1]
    attn_gain_grad = lax.dynamic_slice_in_dim(gain_own, data_index * share_width, share_width, 0)
    mlp_gain_grad = lax.dynamic_slice_in_dim(
        gain_own, depth + data_index * share_width, share_width, 0
    )
    return (
        layer_out[None],
        input_grad[None],
        attn_gain_grad[None],
        *(item[None] for item in attn_grads),
        gain_own[2 * depth : 2 * depth + HD][None],
        gain_own[2 * depth + HD :][None],
        mlp_gain_grad[None],
        grad_gate[None],
        grad_up[None],
        grad_down[None],
    )


def solution(mesh):
    rows = P(None, "dp", None)
    wide = P("section", "dp", "tensor")
    tall = P("section", "tensor", "dp")
    gain = P("section", "dp")
    head_gain = P("section", None)
    slots = P("section", None, "dp", None)
    in_specs = (
        rows, rows, P(), P(), P(), gain, wide, wide, wide, tall, head_gain, head_gain, gain,
        wide, wide, tall,
    )
    out_specs = (
        slots, slots, gain, wide, wide, wide, tall, head_gain, head_gain, gain, wide, wide, tall,
    )
    return jax.shard_map(
        on_device, mesh=mesh, in_specs=in_specs, out_specs=out_specs, check_vma=False
    )
```
